32 devices in a mesh: dp: 8 (over y, x, core), mp: 4 (over z).
Axes of the slice: x: 2, y: 2, z: 4, core: 2. Of those that a mesh axis runs over, the one named last changes fastest.
Arguments:
- tokens: bfloat16 [8192, 2048], P(('dp', 'mp')), may hold values from -6 to 6
- norm_gain: bfloat16 [2048], replicated, may hold values from 0.5 to 1.5
- norm_bias: bfloat16 [2048], replicated, may hold values from -4 to 4
- qkv_weight: bfloat16 [3, 2048, 2048], P(None, 'dp', 'mp'), may hold values from -0.125 to 0.125
- qkv_bias: bfloat16 [3, 2048], P(None, 'mp'), may hold values from -4 to 4
- dense_weight: bfloat16 [2048, 2048], P('mp', 'dp'), may hold values from -0.5 to 0.5
- dense_bias: bfloat16 [2048], replicated, may hold values from -4 to 4
- up_weight: bfloat16 [2048, 8192], P('dp', 'mp'), may hold values from -0.125 to 0.125
- up_bias: bfloat16 [8192], P('mp'), may hold values from -6 to 6
- down_weight: bfloat16 [8192, 2048], P('mp', 'dp'), may hold values from -0.0625 to 0.0625
- down_bias: bfloat16 [2048], replicated, may hold values from -4 to 4
- cotangent: bfloat16 [8192, 2048], P(('dp', 'mp')), may hold values from -6 to 6
Outputs:
- output: bfloat16 [8192, 2048], P(('dp', 'mp'))
- grad_tokens: bfloat16 [8192, 2048], P(('dp', 'mp'))
- grad_norm_gain: float32 [2048], replicated
- grad_norm_bias: float32 [2048], replicated
- grad_qkv_weight: float32 [3, 2048, 2048], P(None, 'dp', 'mp')
- grad_qkv_bias: float32 [3, 2048], P(None, 'mp')
- grad_dense_weight: float32 [2048, 2048], P('mp', 'dp')
- grad_dense_bias: float32 [2048], replicated
- grad_up_weight: float32 [2048, 8192], P('dp', 'mp')
- grad_up_bias: float32 [8192], P('mp')
- grad_down_weight: float32 [8192, 2048], P('mp', 'dp')
- grad_down_bias: float32 [2048], replicated
The draws below stay inside these ranges and needn't reach their ends.
All inputs are finite; a program needn't handle non-finite values.
Results may differ from the reference program's by a relative error of at most 0.013.
Values may be sent and summed in bfloat16 or wider, within the bound.
No kernel may reach another device: no remote copies, remote signals or barrier semaphores. Data moves between devices by JAX's collectives and lax.ppermute only.
A program may use at most 192 MiB of HBM per device.

```python
import jax
import jax.numpy as jnp
from jax import lax

D = 2048
FF = 8192
HEAD_DIM = 64
ROT = 32
BLOCK = 512
SEQ_LEN = 1024
TOKENS = 8192
N_DP = 8


def steps_of(key, extent, cuts, low, largest):
    gain = 1.0
    for position, parts in cuts:
        draws = jax.random.uniform(jax.random.fold_in(jax.random.fold_in(key, 6), position), (parts,), jnp.float32, low / len(cuts), largest / len(cuts))
        gain = gain * jnp.repeat(jnp.exp(draws), extent[position] // parts).reshape((-1,) + (1,) * (len(extent) - 1 - position))
    return gain


def normal_values(rng, extent, deviation, most, shards=(), held_as=jnp.bfloat16):
    entries = deviation * jax.random.normal(rng, extent, jnp.float32)
    if shards:
        entries = entries * steps_of(rng, extent, shards, -0.22, 0.18)
    return jnp.clip(entries, -most, most).astype(held_as)


def setup_inputs(seed: int = 0) -> dict:
    seeds = jax.random.split(jax.random.key(seed), 13)
    tokens = normal_values(seeds[0], (TOKENS, D), 1.0, 6.0, ((0, 32),))
    norm_gain = jnp.clip(1.0 + 0.1 * jax.random.normal(seeds[1], (D,), jnp.float32), 0.5, 1.5).astype(jnp.bfloat16)
    norm_bias = normal_values(seeds[2], (D,), 0.3, 4.0)
    qkv_weight = normal_values(seeds[3], (3, D, D), D ** -0.5, 0.125, ((1, 8), (2, 4)))
    qkv_bias = normal_values(seeds[4], (3, D), 0.3, 4.0, ((1, 4),))
    dense_weight = normal_values(seeds[5], (D, D), (D // 16) ** -0.5, 0.5, ((0, 4), (1, 8)))
    dense_bias = normal_values(seeds[6], (D,), 0.3, 4.0)
    up_weight = normal_values(seeds[7], (D, FF), D ** -0.5, 0.125, ((0, 8), (1, 4)))
    up_bias = normal_values(seeds[8], (FF,), 0.5, 6.0, ((0, 4),))
    down_weight = normal_values(seeds[9], (FF, D), FF ** -0.5, 0.0625, ((0, 4), (1, 8)))
    down_bias = normal_values(seeds[10], (D,), 0.3, 4.0)
    cotangent = normal_values(seeds[11], (TOKENS, D), 1.0, 6.0, ((0, 32),))
    return {"tokens": tokens, "norm_gain": norm_gain, "norm_bias": norm_bias, "qkv_weight": qkv_weight, "qkv_bias": qkv_bias, "dense_weight": dense_weight, "dense_bias": dense_bias, "up_weight": up_weight, "up_bias": up_bias, "down_weight": down_weight, "down_bias": down_bias, "cotangent": cotangent}


@jax.custom_vjp
def low(v):
    return lax.optimization_barrier(v.astype(jnp.bfloat16)).astype(jnp.float32)

@jax.custom_vjp
def low_back(v):
    return v

def low_keep(v):
    return (low(v), None)

def low_pass(kept, grad):
    return (grad,)

def back_keep(v):
    return (v, None)

def back_low(kept, grad):
    return (low(grad),)
low.defvjp(low_keep, low_pass)
low_back.defvjp(back_keep, back_low)
PRECISE = lax.Precision.HIGHEST
EPS = 1e-05

def rotary_tables(length):
    positions = jnp.arange(length).astype(jnp.float32)
    frequency = 10000.0 ** (-jnp.arange(ROT // 2).astype(jnp.float32) * 2.0 / ROT)
    angles = positions[:, None] * frequency[None, :]
    angles = jnp.concatenate([angles, angles], axis=1)
    return (jnp.cos(angles), jnp.sin(angles))

def rotate(tensor, cosine_table, sine_table):
    leading = tensor[..., :ROT]
    trailing = tensor[..., ROT:]
    turned = jnp.concatenate([-leading[..., ROT // 2:], leading[..., :ROT // 2]], axis=-1)
    rotated = leading * cosine_table + turned * sine_table
    return jnp.concatenate([rotated, trailing], axis=-1)

def attend(query, keys, values):
    heads, length, width = query.shape
    count = length // BLOCK
    scale = HEAD_DIM ** (-0.5)
    query_blocks = query.reshape(heads, count, BLOCK, width).transpose(1, 0, 2, 3)
    starts = jnp.arange(count).astype(jnp.int32) * BLOCK
    columns = jnp.arange(length).astype(jnp.int32)

    def one_block(pair):
        block_query, start = pair
        row_index = start + jnp.arange(BLOCK).astype(jnp.int32)
        scores = low_back(jnp.einsum('hqd,hkd->hqk', block_query, keys, precision=PRECISE) * scale)
        masked = jnp.where(columns[None, None, :] <= row_index[None, :, None], scores, -1e+30)
        weights = low(jax.nn.softmax(masked, axis=-1))
        return jnp.einsum('hqk,hkd->hqd', weights, values, precision=PRECISE)
    result = lax.map(jax.checkpoint(one_block), (query_blocks, starts))
    return result.transpose(1, 0, 2, 3).reshape(heads, length, width)

def layer(inputs, norm_gain, norm_bias, qkv_weight, qkv_bias, dense_weight, dense_bias, up_weight, up_bias, down_weight, down_bias):
    length = inputs.shape[0]
    row_mean = lax.optimization_barrier(jnp.mean(inputs, axis=1, keepdims=True))
    centered = inputs - row_mean
    row_var = lax.optimization_barrier(jnp.mean(centered * centered, axis=1, keepdims=True))
    normed = low(centered * lax.rsqrt(row_var + EPS) * norm_gain + norm_bias)
    proj = low_back(jnp.einsum('td,cde->cte', normed, qkv_weight, precision=PRECISE) + qkv_bias[:, None, :])
    split = proj.reshape(3, length, D // HEAD_DIM, HEAD_DIM).transpose(0, 2, 1, 3)
    cosine_table, sine_table = rotary_tables(length)
    query = low(rotate(split[0], cosine_table, sine_table))
    keys = low(rotate(split[1], cosine_table, sine_table))
    values = low(split[2])
    mixed = attend(query, keys, values).transpose(1, 0, 2).reshape(length, D)
    mixed = low(low_back(mixed))
    attention = jnp.dot(mixed, dense_weight, precision=PRECISE) + dense_bias
    pre_act = low_back(jnp.dot(normed, up_weight, precision=PRECISE) + up_bias)
    activ = low(jax.nn.gelu(pre_act, approximate=True))
    forward = jnp.dot(activ, down_weight, precision=PRECISE) + down_bias
    return inputs + attention + forward

def reference(tokens, norm_gain, norm_bias, qkv_weight, qkv_bias, dense_weight, dense_bias, up_weight, up_bias, down_weight, down_bias, cotangent):
    params = tuple((item.astype(jnp.float32) for item in (norm_gain, norm_bias, qkv_weight, qkv_bias, dense_weight, dense_bias, up_weight, up_bias, down_weight, down_bias)))
    seq_inputs = tokens.astype(jnp.float32).reshape(N_DP, SEQ_LEN, D)
    seq_grads = cotangent.astype(jnp.float32).reshape(N_DP, SEQ_LEN, D)

    def one_sequence(totals, pair):
        inputs, grad_out = pair
        result, pullback = jax.vjp(layer, inputs, *params)
        grads = pullback(grad_out)
        totals = tuple((total + grad for total, grad in zip(totals, grads[1:])))
        return (totals, (result.astype(jnp.bfloat16), grads[0].astype(jnp.bfloat16)))
    zeros = tuple((jnp.zeros(item.shape, jnp.float32) for item in params))
    totals, (results, grad_inputs) = lax.scan(one_sequence, zeros, (seq_inputs, seq_grads))
    return (results.reshape(TOKENS, D), grad_inputs.reshape(TOKENS, D), totals[0], totals[1], totals[2], totals[3], totals[4], totals[5], totals[6], totals[7], totals[8], totals[9])
```

```python
import functools

import jax
import jax.numpy as jnp
from jax import lax
from jax.experimental import pallas as pl
from jax.experimental.pallas import tpu as pltpu
from jax.sharding import PartitionSpec as P

HEAD_DIM = 64
ROT = 32
EPS = 1e-05
LANES = 128
VMEM_LIMIT = 56 << 20
F32 = jnp.float32
BF16 = jnp.bfloat16


def dot(lhs, rhs, lhs_dim, rhs_dim):
    return lax.dot_general(
        lhs, rhs, (((lhs_dim,), (rhs_dim,)), ((), ())), preferred_element_type=F32
    )


def params():
    return pltpu.CompilerParams(vmem_limit_bytes=VMEM_LIMIT)


def cost(flops, transcendentals=0, bytes_accessed=0):
    return pl.CostEstimate(
        flops=int(flops), transcendentals=int(transcendentals), bytes_accessed=int(bytes_accessed)
    )


def rotary_tables(length):
    positions = jnp.arange(length).astype(F32)
    frequency = 10000.0 ** (-jnp.arange(ROT // 2).astype(F32) * 2.0 / ROT)
    angles = positions[:, None] * frequency[None, :]
    cosine, sine = jnp.cos(angles), jnp.sin(angles)
    rest = HEAD_DIM - ROT
    none = jnp.zeros((length, ROT // 2), F32)
    ones, zeros = jnp.ones((length, rest), F32), jnp.zeros((length, rest), F32)
    straight = jnp.concatenate([cosine, cosine, ones], axis=1)
    left = jnp.concatenate([-sine, none, zeros], axis=1)
    right = jnp.concatenate([none, sine, zeros], axis=1)
    return [jnp.concatenate([t, t], axis=1) for t in (straight, left, right)]


def rotated(u, straight, left, right, sign):
    half = ROT // 2
    turned = pltpu.roll(u, LANES - half, 1) * left + pltpu.roll(u, half, 1) * right
    return u * straight + sign * turned


def load_blocks(blocks, place, sems):
    me = lax.axis_index("dp")
    copies = [
        pltpu.make_async_copy(block, place(lax.bitwise_xor(me, j)), sems.at[j])
        for j, block in enumerate(blocks)
    ]
    for copy in copies:
        copy.start()
    for copy in copies:
        copy.wait()


def rows_at(ref, size, lead=()):
    return lambda owner: ref.at[(*lead, pl.ds(pl.multiple_of(owner * size, size), size))]


def columns_at(ref, size):
    return lambda owner: ref.at[:, pl.ds(pl.multiple_of(owner * size, size), size)]


def qkv_kernel(count, x_ref, bias_ref, cos_ref, left_ref, right_ref, *rest):
    blocks, (out_ref, held, sems) = rest[:count], rest[count:]
    width = held.shape[2]

    @pl.when(pl.program_id(0) == 0)
    def _():
        load_blocks(blocks, rows_at(held, blocks[0].shape[1], (slice(None),)), sems)

    for c in range(3):
        y = dot(x_ref[...], held[c], 1, 0) + bias_ref[c : c + 1, :]
        for g in range(width // LANES):
            part = y[:, g * LANES : (g + 1) * LANES]
            if c < 2:
                part = rotated(part, cos_ref[...], left_ref[...], right_ref[...], 1.0)
            if c == 0:
                part = part * HEAD_DIM**-0.5
            start = c * width + g * LANES
            out_ref[:, start : start + LANES] = part.astype(BF16)


def project_qkv(rows, blocks, bias, tables, tile):
    length, model = rows.shape
    width = blocks[0].shape[2]
    count = len(blocks)
    table = pl.BlockSpec((tile, LANES), lambda i: (i, 0))
    return pl.pallas_call(
        functools.partial(qkv_kernel, count),
        grid=(length // tile,),
        in_specs=[
            pl.BlockSpec((tile, model), lambda i: (i, 0)),
            pl.BlockSpec(bias.shape, lambda i: (0, 0)),
            table,
            table,
            table,
        ]
        + [pl.BlockSpec(memory_space=pl.ANY)] * count,
        out_specs=pl.BlockSpec((tile, 3 * width), lambda i: (i, 0)),
        out_shape=jax.ShapeDtypeStruct((length, 3 * width), BF16),
        scratch_shapes=[
            pltpu.VMEM((3, model, width), BF16),
            pltpu.SemaphoreType.DMA((count,)),
        ],
        compiler_params=params(),
        cost_estimate=cost(2 * length * model * 3 * width, 0, 2 * model * (length + 3 * width)),
        name="project_qkv",
    )(rows, bias, *tables, *blocks)


def up_kernel(count, step, x_ref, bias_ref, *rest):
    blocks, (act_ref, slope_ref, held, sems) = rest[:count], rest[count:]

    @pl.when(pl.program_id(0) == 0)
    def _():
        load_blocks(blocks, rows_at(held, blocks[0].shape[0]), sems)

    root = 0.7978845608028654
    for start in range(0, held.shape[1], step):
        part = slice(start, start + step)
        pre = dot(x_ref[...], held[:, part], 1, 0) + bias_ref[:, part]
        square = pre * pre
        turn = jnp.tanh(root * pre * (1.0 + 0.044715 * square))
        half = 0.5 * (1.0 + turn)
        act_ref[:, part] = (pre * half).astype(BF16)
        slope_ref[:, part] = (
            half
            + 0.5 * pre * (1.0 - turn * turn) * (root + (3.0 * 0.044715 * root) * square)
        ).astype(BF16)


def project_up(rows, blocks, bias, tile):
    length, model = rows.shape
    width = blocks[0].shape[1]
    count = len(blocks)
    out = pl.BlockSpec((tile, width), lambda i: (i, 0))
    return pl.pallas_call(
        functools.partial(up_kernel, count, min(256, width)),
        grid=(length // tile,),
        in_specs=[
            pl.BlockSpec((tile, model), lambda i: (i, 0)),
            pl.BlockSpec(bias.shape, lambda i: (0, 0)),
        ]
        + [pl.BlockSpec(memory_space=pl.ANY)] * count,
        out_specs=[out, out],
        out_shape=[jax.ShapeDtypeStruct((length, width), BF16)] * 2,
        scratch_shapes=[pltpu.VMEM((model, width), BF16), pltpu.SemaphoreType.DMA((count,))],
        compiler_params=params(),
        cost_estimate=cost(2 * length * model * width, 0, 2 * model * (length + width)),
        name="project_up",
    )(rows, bias, *blocks)


def attend_kernel(block, q_ref, k_ref, v_ref, out_ref, lse_ref):
    length = q_ref.shape[0]
    lane = lax.broadcasted_iota(jnp.int32, (1, LANES), 1)
    key = lax.broadcasted_iota(jnp.int32, (block, block), 0)
    causal = key <= lax.broadcasted_iota(jnp.int32, (block, block), 1)
    for i in range(length // block):
        rows, before = pl.ds(i * block, block), pl.ds(0, i * block)
        results = []
        for h in range(2):
            mine = (lane < HEAD_DIM) if h == 0 else (lane >= HEAD_DIM)
            query = jnp.where(mine, q_ref[rows, :], 0)
            near = jnp.where(causal, dot(k_ref[rows, :], query, 1, 1), -1e30)
            highest = jnp.max(near, axis=0, keepdims=True)
            if i:
                far = dot(k_ref[before, :], query, 1, 1)
                highest = jnp.maximum(highest, jnp.max(far, axis=0, keepdims=True))
            near = jnp.exp(near - highest)
            total = jnp.sum(near, axis=0, keepdims=True)
            if i:
                far = jnp.exp(far - highest)
                total = total + jnp.sum(far, axis=0, keepdims=True)
            inverse = 1.0 / total
            result = dot((near * inverse).astype(BF16), v_ref[rows, :], 0, 0)
            if i:
                result = result + dot((far * inverse).astype(BF16), v_ref[before, :], 0, 0)
            results.append(result)
            lse_ref[0, h : h + 1, rows] = highest + jnp.log(total)
        out_ref[rows, :] = jnp.where(lane < HEAD_DIM, results[0], results[1]).astype(BF16)


def attend(qkv, block):
    length, width = qkv.shape[0], qkv.shape[1] // 3
    pairs = width // LANES
    at = lambda off: pl.BlockSpec((length, LANES), lambda p, off=off: (0, off * pairs + p))
    return pl.pallas_call(
        functools.partial(attend_kernel, block),
        grid=(pairs,),
        in_specs=[at(0), at(1), at(2)],
        out_specs=[at(0), pl.BlockSpec((1, 8, length), lambda p: (p, 0, 0))],
        out_shape=[
            jax.ShapeDtypeStruct((length, width), BF16),
            jax.ShapeDtypeStruct((pairs, 8, length), F32),
        ],
        compiler_params=params(),
        cost_estimate=cost(16 * length * length * width, pairs * 2 * length * length, 0),
        name="attend",
    )(qkv, qkv, qkv)


def attend_back_kernel(
    block,
    q_ref,
    k_ref,
    v_ref,
    grad_ref,
    mixed_ref,
    lse_ref,
    cos_ref,
    left_ref,
    right_ref,
    gq_ref,
    gk_ref,
    gv_ref,
    sum_ref,
    gk_sum,
    gv_sum,
):
    length = q_ref.shape[0]
    lane = lax.broadcasted_iota(jnp.int32, (1, LANES), 1)
    key = lax.broadcasted_iota(jnp.int32, (block, block), 0)
    causal = key <= lax.broadcasted_iota(jnp.int32, (block, block), 1)
    count = length // block
    sum_ref[...] = jnp.zeros_like(sum_ref)

    def put(ref, which, rows, value):
        value = value.astype(BF16)
        ref[rows, :] = value
        sum_ref[0, which : which + 1, :] += jnp.sum(value.astype(F32), axis=0, keepdims=True)

    def unrotated(value, rows):
        return rotated(value, cos_ref[rows, :], left_ref[rows, :], right_ref[rows, :], -1.0)

    for i in reversed(range(count)):
        rows = pl.ds(i * block, block)
        product = grad_ref[rows, :].astype(F32) * mixed_ref[rows, :].astype(F32)
        gq = None
        for h in range(2):
            mine = (lane < HEAD_DIM) if h == 0 else (lane >= HEAD_DIM)
            query = jnp.where(mine, q_ref[rows, :], 0)
            grad = jnp.where(mine, grad_ref[rows, :], 0)
            ones = jnp.where(mine, jnp.ones((8, LANES), F32), 0.0)
            delta = lax.dot_general(
                ones,
                product,
                (((1,), (1,)), ((), ())),
                precision=lax.Precision.HIGHEST,
                preferred_element_type=F32,
            )[0:1, :]
            lse = lse_ref[0, h : h + 1, rows]
            for j in range(i + 1):
                keys = pl.ds(j * block, block)
                key_rows = k_ref[keys, :]
                probs = jnp.exp(dot(key_rows, query, 1, 1) - lse)
                if j == i:
                    probs = jnp.where(causal, probs, 0.0)
                gprobs = dot(v_ref[keys, :], grad, 1, 1)
                gscores = (probs * (gprobs - delta)).astype(BF16)
                gv, gk = dot(probs.astype(BF16), grad, 1, 0), dot(gscores, query, 1, 0)
                if i == count - 1 and h == 0:
                    gv_sum[keys, :] = gv
                    gk_sum[keys, :] = gk
                else:
                    gv_sum[keys, :] += gv
                    gk_sum[keys, :] += gk
                part = dot(gscores, jnp.where(mine, key_rows, 0), 0, 0)
                gq = part if gq is None else gq + part
        put(gq_ref, 0, rows, unrotated(gq * HEAD_DIM**-0.5, rows))
    for i in range(count):
        rows = pl.ds(i * block, block)
        put(gk_ref, 1, rows, unrotated(gk_sum[rows, :], rows))
        put(gv_ref, 2, rows, gv_sum[rows, :])


def attend_back(qkv, grad, mixed, lse, tables, block):
    length, width = qkv.shape[0], qkv.shape[1] // 3
    pairs = width // LANES
    at = lambda off: pl.BlockSpec((length, LANES), lambda p, off=off: (0, off * pairs + p))
    table = pl.BlockSpec((length, LANES), lambda p: (0, 0))
    return pl.pallas_call(
        functools.partial(attend_back_kernel, block),
        grid=(pairs,),
        in_specs=[at(0), at(1), at(2), at(0), at(0)]
        + [pl.BlockSpec((1, 8, length), lambda p: (p, 0, 0)), table, table, table],
        out_specs=[at(0)] * 3 + [pl.BlockSpec((1, 8, LANES), lambda p: (p, 0, 0))],
        out_shape=[jax.ShapeDtypeStruct((length, width), BF16)] * 3
        + [jax.ShapeDtypeStruct((pairs, 8, LANES), F32)],
        scratch_shapes=[pltpu.VMEM((length, LANES), F32)] * 2,
        compiler_params=params(),
        cost_estimate=cost(40 * length * length * width, pairs * 2 * length * length, 0),
        name="attend_back",
    )(qkv, qkv, qkv, grad, mixed, lse, *tables)


def branch_kernel(count, parts, mixed_ref, act_ref, *rest):
    dense, down = rest[:count], rest[count : 2 * count]
    outs, (dense_held, down_held, sems) = rest[2 * count : 2 * count + parts], rest[-3:]

    @pl.when(pl.program_id(0) == 0)
    def _():
        size = dense[0].shape[1]
        load_blocks(dense, columns_at(dense_held, size), sems.at[0])
        load_blocks(down, columns_at(down_held, size), sems.at[1])

    result = dot(mixed_ref[...], dense_held[...], 1, 0) + dot(act_ref[...], down_held[...], 1, 0)
    for part, out_ref in enumerate(outs):

        @pl.when(pl.program_id(0) == part)
        def _(out_ref=out_ref):
            out_ref[...] = result.astype(BF16)


def quarter_specs(parts, rows, widths):
    return [pl.BlockSpec((rows, w), lambda k, at: ((at[0] + k) % parts, 0)) for w in widths]


def branch_sums(at, mixed, act, dense, down, parts):
    length, width = mixed.shape
    hidden = act.shape[1]
    count, rows = len(dense), length // parts
    model = count * dense[0].shape[1]
    return pl.pallas_call(
        lambda at_ref, *refs: branch_kernel(count, parts, *refs),
        grid_spec=pltpu.PrefetchScalarGridSpec(
            num_scalar_prefetch=1,
            grid=(parts,),
            in_specs=quarter_specs(parts, rows, (width, hidden))
            + [pl.BlockSpec(memory_space=pl.ANY)] * (2 * count),
            out_specs=[pl.BlockSpec((rows, model), lambda k, at: (0, 0))] * parts,
            scratch_shapes=[
                pltpu.VMEM((width, model), BF16),
                pltpu.VMEM((hidden, model), BF16),
                pltpu.SemaphoreType.DMA((2, count)),
            ],
        ),
        out_shape=[jax.ShapeDtypeStruct((rows, model), BF16)] * parts,
        compiler_params=params(),
        cost_estimate=cost(2 * length * model * (width + hidden), 0, 2 * length * model),
        name="branch_sums",
    )(at, mixed, act, *dense, *down)


def grad_in_kernel(count, step, dy_ref, slope_ref, *rest):
    dense, down = rest[:count], rest[count : 2 * count]
    gmixed_ref, gpre_ref, gsum_ref, dsum_ref, dense_held, down_held, sems = rest[2 * count :]

    @pl.when(pl.program_id(0) == 0)
    def _():
        size = dense[0].shape[1]
        load_blocks(dense, columns_at(dense_held, size), sems.at[0])
        load_blocks(down, columns_at(down_held, size), sems.at[1])
        gsum_ref[...] = jnp.zeros_like(gsum_ref)
        dsum_ref[...] = jnp.zeros_like(dsum_ref)

    gmixed_ref[...] = dot(dy_ref[...], dense_held[...], 1, 1).astype(BF16)
    for start in range(0, down_held.shape[0], step):
        part = slice(start, start + step)
        gact = dot(dy_ref[...], down_held[part, :], 1, 1)
        gpre = (gact * slope_ref[:, part].astype(F32)).astype(BF16)
        gpre_ref[:, part] = gpre
        gsum_ref[0:1, part] += jnp.sum(gpre.astype(F32), axis=0, keepdims=True)
    dsum_ref[0:1, :] += jnp.sum(dy_ref[...].astype(F32), axis=0, keepdims=True)


def grad_in(dy, slope, dense, down, tile):
    length, model = dy.shape
    hidden, width = slope.shape[1], dense[0].shape[0]
    count = len(dense)
    return pl.pallas_call(
        functools.partial(grad_in_kernel, count, min(256, hidden)),
        grid=(length // tile,),
        in_specs=[
            pl.BlockSpec((tile, model), lambda i: (i, 0)),
            pl.BlockSpec((tile, hidden), lambda i: (i, 0)),
        ]
        + [pl.BlockSpec(memory_space=pl.ANY)] * (2 * count),
        out_specs=[
            pl.BlockSpec((tile, width), lambda i: (i, 0)),
            pl.BlockSpec((tile, hidden), lambda i: (i, 0)),
            pl.BlockSpec((8, hidden), lambda i: (0, 0)),
            pl.BlockSpec((8, model), lambda i: (0, 0)),
        ],
        out_shape=[
            jax.ShapeDtypeStruct((length, width), BF16),
            jax.ShapeDtypeStruct((length, hidden), BF16),
            jax.ShapeDtypeStruct((8, hidden), F32),
            jax.ShapeDtypeStruct((8, model), F32),
        ],
        scratch_shapes=[
            pltpu.VMEM((width, model), BF16),
            pltpu.VMEM((hidden, model), BF16),
            pltpu.SemaphoreType.DMA((2, count)),
        ],
        compiler_params=params(),
        cost_estimate=cost(2 * length * model * (width + hidden), 0, 2 * length * model),
        name="grad_in",
    )(dy, slope, *dense, *down)


def grad_normed_kernel(count, parts, gq_ref, gk_ref, gv_ref, gpre_ref, *rest):
    qkv, up = rest[:count], rest[count : 2 * count]
    outs, (qkv_held, up_held, sems) = rest[2 * count : 2 * count + parts], rest[-3:]

    @pl.when(pl.program_id(0) == 0)
    def _():
        size = up[0].shape[0]
        load_blocks(qkv, rows_at(qkv_held, size, (slice(None),)), sems.at[0])
        load_blocks(up, rows_at(up_held, size), sems.at[1])

    result = dot(gpre_ref[...], up_held[...], 1, 1)
    for c, ref in enumerate((gq_ref, gk_ref, gv_ref)):
        result = result + dot(ref[...], qkv_held[c], 1, 1)
    for part, out_ref in enumerate(outs):

        @pl.when(pl.program_id(0) == part)
        def _(out_ref=out_ref):
            out_ref[...] = result.astype(BF16)


def grad_normed_sums(at, gqkv, gpre, qkv, up, parts):
    length, hidden = gpre.shape
    width = gqkv[0].shape[1]
    count, rows = len(up), length // parts
    model = count * up[0].shape[0]
    return pl.pallas_call(
        lambda at_ref, *refs: grad_normed_kernel(count, parts, *refs),
        grid_spec=pltpu.PrefetchScalarGridSpec(
            num_scalar_prefetch=1,
            grid=(parts,),
            in_specs=quarter_specs(parts, rows, (width, width, width, hidden))
            + [pl.BlockSpec(memory_space=pl.ANY)] * (2 * count),
            out_specs=[pl.BlockSpec((rows, model), lambda k, at: (0, 0))] * parts,
            scratch_shapes=[
                pltpu.VMEM((3, model, width), BF16),
                pltpu.VMEM((model, hidden), BF16),
                pltpu.SemaphoreType.DMA((2, count)),
            ],
        ),
        out_shape=[jax.ShapeDtypeStruct((rows, model), BF16)] * parts,
        compiler_params=params(),
        cost_estimate=cost(2 * length * model * (3 * width + hidden), 0, 2 * length * model),
        name="grad_normed_sums",
    )(at, *gqkv, gpre, *qkv, *up)


def row_block_kernel(count, terms, x0_ref, x1_ref, *rest):
    first, second, outs = rest[:terms], rest[terms : 2 * terms], rest[2 * terms :]
    for j, out_ref in enumerate(outs):

        @pl.when(pl.program_id(0) == j)
        def _(out_ref=out_ref):
            for c in range(terms):
                grad = dot(x0_ref[...], first[c][...], 0, 0) + dot(x1_ref[...], second[c][...], 0, 0)
                if terms == 1:
                    out_ref[...] = grad.astype(BF16)
                else:
                    out_ref[c] = grad.astype(BF16)


def row_block_grads(me, rows, grads, count):
    length, model = rows[0].shape
    terms, width, size = len(grads[0]), grads[0][0].shape[1], model // count
    shape = (size, width) if terms == 1 else (terms, size, width)
    x = pl.BlockSpec((length, size), lambda j, at: (0, lax.bitwise_xor(at[0], j)))
    whole = pl.BlockSpec((length, width), lambda j, at: (0, 0))
    return pl.pallas_call(
        lambda at_ref, *refs: row_block_kernel(count, terms, *refs),
        grid_spec=pltpu.PrefetchScalarGridSpec(
            num_scalar_prefetch=1,
            grid=(count,),
            in_specs=[x, x] + [whole] * (2 * terms),
            out_specs=[pl.BlockSpec(shape, lambda j, at: (0,) * len(shape))] * count,
        ),
        out_shape=[jax.ShapeDtypeStruct(shape, BF16)] * count,
        compiler_params=params(),
        cost_estimate=cost(4 * length * model * terms * width, 0, 4 * length * model),
        name="row_block_grads",
    )(me, *rows, *grads[0], *grads[1])


def column_block_kernel(x0_ref, x1_ref, g0_ref, g1_ref, *outs):
    for j, out_ref in enumerate(outs):

        @pl.when(pl.program_id(0) == j)
        def _(out_ref=out_ref):
            grad = dot(x0_ref[...], g0_ref[...], 0, 0) + dot(x1_ref[...], g1_ref[...], 0, 0)
            out_ref[...] = grad.astype(BF16)


def column_block_grads(me, inner, outer, count):
    length, width = inner[0].shape
    model = outer[0].shape[1]
    size = model // count
    whole = pl.BlockSpec((length, width), lambda j, at: (0, 0))
    g = pl.BlockSpec((length, size), lambda j, at: (0, lax.bitwise_xor(at[0], j)))
    return pl.pallas_call(
        lambda at_ref, *refs: column_block_kernel(*refs),
        grid_spec=pltpu.PrefetchScalarGridSpec(
            num_scalar_prefetch=1,
            grid=(count,),
            in_specs=[whole, whole, g, g],
            out_specs=[pl.BlockSpec((width, size), lambda j, at: (0, 0))] * count,
        ),
        out_shape=[jax.ShapeDtypeStruct((width, size), BF16)] * count,
        compiler_params=params(),
        cost_estimate=cost(4 * length * model * width, 0, 4 * length * model),
        name="column_block_grads",
    )(me, *inner, *outer)


def assemble_kernel(parts, *refs):
    own, below, above = refs[0], refs[1:parts], refs[parts : 2 * parts - 1]
    out_ref, sems = refs[-2:]
    rows = own.shape[0]
    z = lax.axis_index("mp")
    for wait in (False, True):
        for t in range(parts):
            target = out_ref.at[pl.ds(t * rows, rows)]
            sources = [(z == t, own)]
            sources += [(z == t + k, below[k - 1]) for k in range(1, parts - t)]
            sources += [(z == t - k, above[k - 1]) for k in range(1, t + 1)]
            for here, source in sources:

                @pl.when(here)
                def _(source=source, target=target, t=t):
                    copy = pltpu.make_async_copy(source, target, sems.at[t])
                    if wait:
                        copy.wait()
                    else:
                        copy.start()


def assemble(own, below, above):
    parts = len(below) + 1
    rows, width = own.shape
    return pl.pallas_call(
        functools.partial(assemble_kernel, parts),
        in_specs=[pl.BlockSpec(memory_space=pl.ANY)] * (2 * parts - 1),
        out_specs=pl.BlockSpec(memory_space=pl.ANY),
        out_shape=jax.ShapeDtypeStruct((parts * rows, width), own.dtype),
        scratch_shapes=[pltpu.SemaphoreType.DMA((parts,))],
        compiler_params=params(),
        cost_estimate=cost(0, 0, 4 * parts * rows * width),
        name="assemble",
    )(own, *below, *above)


def after(value, *earlier):
    return lax.optimization_barrier((value, *earlier))[0]


def across(value, bit, count):
    return lax.ppermute(value, "dp", [(i, i ^ bit) for i in range(count)])


def line_gather(own, parts):
    below, above, up, down = [], [], own, own
    for k in range(1, parts):
        up = lax.ppermute(up, "mp", [(i, i + 1) for i in range(k - 1, parts - 1)])
        down = lax.ppermute(down, "mp", [(i + 1, i) for i in range(parts - k)])
        below.append(up)
        above.append(down)
    return below, above


def line_scatter(sums):
    parts = len(sums)
    sums = [list(s) for s in sums]

    def total(k):
        if len(sums[k]) > 1:
            sums[k] = [sum(s.astype(F32) for s in sums[k]).astype(BF16)]
        return sums[k][0]

    for s in range(1, parts):
        up = lax.ppermute(total(parts - s), "mp", [(i, i + 1) for i in range(s)])
        down = lax.ppermute(total(s), "mp", [(i, i - 1) for i in range(parts - s, parts)])
        sums[(parts - s - 1) % parts].append(up)
        sums[(s + 1) % parts].append(down)
    return sums[0]


def chip_bits(count):
    bits, bit = [], 2
    while bit < count:
        bits.append(bit)
        bit *= 2
    return bits


def gather_blocks(own, sibling, count, gate):
    held = {0: own, 1: sibling}
    orders = (chip_bits(count), chip_bits(count)[::-1])
    first = None
    for s in range(len(orders[0])):
        moved = {}
        for half in range(2):
            bit = orders[half][s]
            for j in [j for j in held if j % 2 == half]:
                block = held[j] if s or gate is None else after(held[j], gate)
                moved[j ^ bit] = across(block, bit, count)
        held.update(moved)
        first = first if s else moved
    return [held[j] for j in range(count)], first


def scatter_blocks(blocks, count):
    held = {j: [b] for j, b in enumerate(blocks)}
    orders = (chip_bits(count)[::-1], chip_bits(count))

    def total(j):
        if len(held[j]) > 1:
            held[j] = [sum(b.astype(F32) for b in held[j]).astype(BF16)]
        return held[j][0]

    for s in range(len(orders[0])):
        moved = []
        for half in range(2):
            bit = orders[half][s]
            for j in [j for j in held if j % 2 == half and j & bit]:
                moved.append((j ^ bit, across(total(j), bit, count)))
                del held[j]
        for j, block in moved:
            held[j].append(block)
    mine = sum(b.astype(F32) for b in held[0])
    return mine, total(1)


def all_reduce_small(value, axis, count):
    parts = [value] + [
        lax.ppermute(value, axis, [(i, i ^ j) for i in range(count)]) for j in range(1, count)
    ]
    while len(parts) > 1:
        parts = [a + b for a, b in zip(parts[::2], parts[1::2])]
    return parts[0]


def on_device(
    tokens,
    norm_gain,
    norm_bias,
    qkv_weight,
    qkv_bias,
    dense_weight,
    dense_bias,
    up_weight,
    up_bias,
    down_weight,
    down_bias,
    cotangent,
    *,
    ndp,
    nmp,
):
    me, z = lax.axis_index("dp"), lax.axis_index("mp")
    core = me % 2
    at_dp, at_mp = me.astype(jnp.int32)[None], z.astype(jnp.int32)[None]
    length = tokens.shape[0] * nmp
    tile = min(256, length)
    block = min(512, length)
    width, hidden = qkv_weight.shape[2] // 2, up_weight.shape[1] // 2
    rank = lambda array, axis, which, size: lax.dynamic_slice_in_dim(
        array, which * size, size, axis
    )

    local_inputs = tokens.astype(F32)
    row_mean = jnp.mean(local_inputs, axis=1, keepdims=True)
    centered = local_inputs - row_mean
    row_var = jnp.mean(centered * centered, axis=1, keepdims=True)
    inverse_std = lax.rsqrt(row_var + EPS)
    normal_rows = centered * inverse_std
    gain_values = norm_gain.astype(F32)
    normed = (normal_rows * gain_values + norm_bias.astype(F32)).astype(BF16)

    def halves(weight, axis, size):
        own = rank(weight, axis, core, size)
        return own, across(rank(weight, axis, 1 - core, size), 1, ndp)

    pieces = {
        "qkv": halves(qkv_weight, 2, width),
        "up": halves(up_weight, 1, hidden),
        "dense": halves(dense_weight, 0, width),
        "down": halves(down_weight, 0, hidden),
    }
    gate, gathered = None, {}
    for name in ("qkv", "up", "dense", "down"):
        gathered[name], first = gather_blocks(*pieces[name], ndp, gate)
        gate = next(iter(first.values()))

    below, above = line_gather(normed, nmp)
    rows_own = assemble(normed, below, above)
    rows_other = across(rows_own, 1, ndp)
    late_cotangent = after(cotangent, below[-1], above[-1])
    grad_below, grad_above = line_gather(late_cotangent, nmp)
    dy_own = assemble(cotangent, grad_below, grad_above)
    dy_other = across(dy_own, 1, ndp)
    rows, dy = (rows_own, rows_other), (dy_own, dy_other)

    tables = rotary_tables(length)
    qkv_bias_here = rank(qkv_bias, 1, core, width).astype(F32)
    up_bias_here = rank(up_bias[None, :], 1, core, hidden).astype(F32)
    qkv = [project_qkv(r, gathered["qkv"], qkv_bias_here, tables, tile) for r in rows]
    act, slope = zip(*[project_up(r, gathered["up"], up_bias_here, tile) for r in rows])
    mixed, lse = zip(*[attend(p, block) for p in qkv])
    sums = [
        branch_sums(at_mp, m, a, gathered["dense"], gathered["down"], nmp)
        for m, a in zip(mixed, act)
    ]
    shares = [[mine, across(theirs, 1, ndp)] for mine, theirs in zip(*sums)]
    branches = sum(s.astype(F32) for s in line_scatter(shares))
    output = (local_inputs + branches + dense_bias.astype(F32) + down_bias.astype(F32)).astype(BF16)

    grad_down = column_block_grads(at_dp, act, dy, ndp)
    gmixed, gpre, gpre_sum, dy_sum = zip(
        *[grad_in(d, s, gathered["dense"], gathered["down"], tile) for d, s in zip(dy, slope)]
    )
    grad_up = row_block_grads(at_dp, rows, [[g] for g in gpre], ndp)
    back = [
        attend_back(p, g, m, e, tables, block) for p, g, m, e in zip(qkv, gmixed, mixed, lse)
    ]
    gqkv = [b[:3] for b in back]
    normed_sums = [
        grad_normed_sums(at_mp, g, p, gathered["qkv"], gathered["up"], nmp)
        for g, p in zip(gqkv, gpre)
    ]
    grad_dense = column_block_grads(at_dp, mixed, dy, ndp)
    grad_qkv = row_block_grads(at_dp, rows, gqkv, ndp)

    def owned(blocks, axis):
        mine, theirs = scatter_blocks(blocks, ndp)
        other = across(theirs, 1, ndp).astype(F32)
        return jnp.where(
            core == 0,
            jnp.concatenate([mine, other], axis=axis),
            jnp.concatenate([other, mine], axis=axis),
        )

    owned_down = owned(grad_down, 0)
    owned_up = owned(grad_up, 1)
    owned_dense = owned(grad_dense, 0)
    owned_qkv = owned(grad_qkv, 2)

    pairs = width // LANES
    qkv_sum = sum(b[3] for b in back)[:, :3, :].transpose(1, 0, 2).reshape(3 * width)
    small = jnp.concatenate(
        [sum(s[0] for s in gpre_sum), qkv_sum, sum(s[0] for s in dy_sum)]
    )
    for bit in chip_bits(ndp):
        small = small + across(small, bit, ndp)
    here, grad_out_bias = small[: hidden + 3 * width], small[hidden + 3 * width :]
    there = across(here, 1, ndp)
    even, odd = jnp.where(core == 0, here, there), jnp.where(core == 0, there, here)
    grad_up_bias = jnp.concatenate([even[:hidden], odd[:hidden]])
    grad_qkv_bias = jnp.concatenate(
        [even[hidden:].reshape(3, width), odd[hidden:].reshape(3, width)], axis=1
    )

    shares = [[mine, across(theirs, 1, ndp)] for mine, theirs in zip(*normed_sums)]
    grad_local = sum(s.astype(F32) for s in line_scatter(shares))
    scaled_grad = grad_local * gain_values
    first_mean = jnp.mean(scaled_grad, axis=1, keepdims=True)
    second_mean = jnp.mean(scaled_grad * normal_rows, axis=1, keepdims=True)
    grad_tokens = (
        cotangent.astype(F32)
        + (scaled_grad - first_mean - normal_rows * second_mean) * inverse_std
    ).astype(BF16)
    norm_sums = jnp.concatenate(
        [jnp.sum(grad_local * normal_rows, axis=0), jnp.sum(grad_local, axis=0)]
    )
    norm_sums = all_reduce_small(all_reduce_small(norm_sums, "dp", ndp), "mp", nmp)
    model = norm_gain.shape[0]
    return (
        output,
        grad_tokens,
        norm_sums[:model],
        norm_sums[model:],
        owned_qkv,
        grad_qkv_bias,
        owned_dense,
        grad_out_bias,
        owned_up,
        grad_up_bias,
        owned_down,
        grad_out_bias,
    )


def solution(mesh):
    return jax.shard_map(
        functools.partial(on_device, ndp=mesh.shape["dp"], nmp=mesh.shape["mp"]),
        mesh=mesh,
        in_specs=(
            P(("dp", "mp"), None),
            P(),
            P(),
            P(None, "dp", "mp"),
            P(None, "mp"),
            P("mp", "dp"),
            P(),
            P("dp", "mp"),
            P("mp"),
            P("mp", "dp"),
            P(),
            P(("dp", "mp"), None),
        ),
        out_specs=(
            P(("dp", "mp"), None),
            P(("dp", "mp"), None),
            P(),
            P(),
            P(None, "dp", "mp"),
            P(None, "mp"),
            P("mp", "dp"),
            P(),
            P("dp", "mp"),
            P("mp"),
            P("mp", "dp"),
            P(),
        ),
        check_vma=False,
    )
```

```python
import functools

import jax
import jax.numpy as jnp
from jax import lax
from jax.experimental import pallas as pl
from jax.experimental.pallas import tpu as pltpu
from jax.sharding import PartitionSpec as P

HEAD_DIM = 64
ROT = 32
EPS = 1e-05
LANES = 128
VMEM_LIMIT = 56 << 20
F32 = jnp.float32
BF16 = jnp.bfloat16
ANY = pl.BlockSpec(memory_space=pl.ANY)


def dot(lhs, rhs, lhs_dim, rhs_dim):
    return lax.dot_general(
        lhs, rhs, (((lhs_dim,), (rhs_dim,)), ((), ())), preferred_element_type=F32
    )


def call(kernel, name, operands, deps=(), scalars=(), **spec):
    deps, many, lead = tuple(deps), len(operands), len(scalars)

    def body(*refs):
        kernel(*refs[: lead + many], *refs[lead + many + len(deps) :])

    in_specs = list(spec.pop("in_specs")) + [ANY] * len(deps)
    out_shape, aliases = spec.pop("out_shape"), spec.pop("input_output_aliases", {})
    if scalars:
        grid_spec = pltpu.PrefetchScalarGridSpec(
            num_scalar_prefetch=lead, in_specs=in_specs, **spec
        )
        spec = {"grid_spec": grid_spec}
    else:
        spec["in_specs"] = in_specs
    return pl.pallas_call(
        body,
        out_shape=out_shape,
        input_output_aliases=aliases,
        compiler_params=pltpu.CompilerParams(vmem_limit_bytes=VMEM_LIMIT),
        cost_estimate=pl.CostEstimate(flops=0, transcendentals=0, bytes_accessed=0),
        name=name,
        **spec,
    )(*scalars, *operands, *deps)


def tie(value, *deps):
    return call(
        lambda *refs: None,
        "tie",
        [value],
        deps,
        in_specs=[ANY],
        out_specs=ANY,
        out_shape=jax.ShapeDtypeStruct(value.shape, value.dtype),
        input_output_aliases={0: 0},
    )


def rotary_tables(length):
    positions = jnp.arange(length).astype(F32)
    frequency = 10000.0 ** (-jnp.arange(ROT // 2).astype(F32) * 2.0 / ROT)
    angles = positions[:, None] * frequency[None, :]
    cosine, sine = jnp.cos(angles), jnp.sin(angles)
    rest = HEAD_DIM - ROT
    none = jnp.zeros((length, ROT // 2), F32)
    ones, zeros = jnp.ones((length, rest), F32), jnp.zeros((length, rest), F32)
    straight = jnp.concatenate([cosine, cosine, ones], axis=1)
    left = jnp.concatenate([-sine, none, zeros], axis=1)
    right = jnp.concatenate([none, sine, zeros], axis=1)
    return [jnp.concatenate([t, t], axis=1) for t in (straight, left, right)]


def rotated(u, straight, left, right, sign):
    half = ROT // 2
    turned = pltpu.roll(u, LANES - half, 1) * left + pltpu.roll(u, half, 1) * right
    return u * straight + sign * turned


def normalized(x):
    x = x.astype(F32)
    centered = x - jnp.mean(x, axis=1, keepdims=True)
    variance = jnp.mean(centered * centered, axis=1, keepdims=True)
    return centered * lax.rsqrt(variance + EPS)


def block_copies(blocks, place, sems):
    me = lax.axis_index("dp")
    return [
        pltpu.make_async_copy(block, place(lax.bitwise_xor(me, j)), sems.at[j])
        for j, block in enumerate(blocks)
    ]


def rows_at(ref, size):
    return lambda owner: ref.at[pl.ds(pl.multiple_of(owner * size, size), size)]


def columns_at(ref, size):
    return lambda owner: ref.at[:, pl.ds(pl.multiple_of(owner * size, size), size)]


class Chunks:
    def __init__(self, own, below, above):
        self.own, self.below, self.above = own, list(below), list(above)

    def flat(self):
        return [self.own, *self.below, *self.above]

    @staticmethod
    def of(refs):
        half = len(refs) // 2
        return Chunks(refs[0], refs[1 : 1 + half], refs[1 + half :])


def chunk_copies(chunks, places, parts, held, sems):
    z = lax.axis_index("mp")
    found = []
    for s, sequence in enumerate(chunks):
        for i, m in enumerate(places):
            slot = s * len(places) + i
            options = []
            if m == 0:
                options.append((None, sequence.own))
            else:
                moves = {(at ^ m) - at for at in range(parts)}
                for move in sorted(moves):
                    source = sequence.above[move - 1] if move > 0 else sequence.below[-move - 1]
                    options.append((lax.bitwise_xor(z, m) - z == move, source))
            found.append(
                [
                    (here, pltpu.make_async_copy(source, held.at[slot], sems.at[slot]))
                    for here, source in options
                ]
            )
    return found


def start_all(found):
    for options in found:
        for here, copy in options:
            if here is None:
                copy.start()
            else:
                pl.when(here)(copy.start)


def wait_for(options):
    options[0][1].wait()


def project_kernel(setup, at_ref, bias_ref, gain_ref, shift_ref, cos_ref, left_ref, right_ref, *rest):
    count, parts, places, width, hidden = setup
    refs = 2 * parts - 1
    chunks = [Chunks.of(rest[:refs]), Chunks.of(rest[refs : 2 * refs])]
    blocks, rest = rest[2 * refs : 2 * refs + count], rest[2 * refs + count :]
    qkv_ref, act_ref, slope_ref, normed_ref, tokens_ref, held, x_held, ready, sems, x_sems = rest
    step, steps = pl.program_id(0), 2 * len(places)
    found = chunk_copies(chunks, places, parts, x_held, x_sems)
    loads = block_copies(blocks, rows_at(held, blocks[0].shape[0]), sems)

    def norm(slot):
        return (normalized(x_held[slot]) * gain_ref[...] + shift_ref[...]).astype(BF16)

    @pl.when(step == 0)
    def _():
        for copy in loads:
            copy.start()
        start_all(found)
        wait_for(found[0])
        ready[0] = norm(0)
        for copy in loads:
            copy.wait()

    for slot in range(1, steps):

        @pl.when(step == slot - 1)
        def _(slot=slot):
            wait_for(found[slot])

    x = ready[step % 2]
    normed_ref[...] = x
    tokens_ref[...] = x_held[step]
    ready[(step + 1) % 2] = norm((step + 1) % steps)
    root = 0.7978845608028654
    for t in range((3 * width + hidden) // width):
        columns = slice(t * width, (t + 1) * width)
        y = dot(x, held[:, columns], 1, 0) + bias_ref[:, columns]
        if t < 3:
            for g in range(width // LANES):
                part = y[:, g * LANES : (g + 1) * LANES]
                if t < 2:
                    part = rotated(part, cos_ref[...], left_ref[...], right_ref[...], 1.0)
                if t == 0:
                    part = part * HEAD_DIM**-0.5
                start = t * width + g * LANES
                qkv_ref[:, start : start + LANES] = part.astype(BF16)
        else:
            columns = slice((t - 3) * width, (t - 2) * width)
            square = y * y
            turn = jnp.tanh(root * y * (1.0 + 0.044715 * square))
            half = 0.5 * (1.0 + turn)
            act_ref[:, columns] = (y * half).astype(BF16)
            slope = half * (1.0 + y * (1.0 - turn) * (root + (3.0 * 0.044715 * root) * square))
            slope_ref[:, columns] = slope.astype(BF16)


def project(at_mp, chunks, blocks, bias, gain, shift, tables, width, deps):
    parts, places = len(chunks[0].below) + 1, tuple(range(len(chunks[0].below) + 1))
    rows, model = chunks[0].own.shape
    total, hidden = blocks[0].shape[1], blocks[0].shape[1] - 3 * width
    count, length = len(blocks), 2 * parts * rows
    table = pl.BlockSpec((rows, LANES), lambda i, at: (at[0] ^ (i % parts), 0))
    out = lambda w: pl.BlockSpec((rows, w), lambda i, at: (i - i % parts + (at[0] ^ (i % parts)), 0))
    line = lambda a: pl.BlockSpec(a.shape, lambda i, at: (0, 0))
    widths = (3 * width, hidden, hidden, model, model)
    setup = (count, parts, places, width, hidden)
    return call(
        functools.partial(project_kernel, setup),
        "project",
        [bias, gain, shift, *tables, *chunks[0].flat(), *chunks[1].flat(), *blocks],
        deps,
        (at_mp,),
        grid=(2 * parts,),
        in_specs=[line(bias), line(gain), line(shift), table, table, table]
        + [ANY] * (2 * (2 * parts - 1) + count),
        out_specs=[out(w) for w in widths],
        out_shape=[jax.ShapeDtypeStruct((length, w), BF16) for w in widths],
        scratch_shapes=[
            pltpu.VMEM((model, total), BF16),
            pltpu.VMEM((2 * parts, rows, model), BF16),
            pltpu.VMEM((2, rows, model), BF16),
            pltpu.SemaphoreType.DMA((count,)),
            pltpu.SemaphoreType.DMA((2 * parts,)),
        ],
    )


def attend_kernel(block, q_ref, k_ref, v_ref, out_ref, lse_ref):
    length = q_ref.shape[0]
    lane = lax.broadcasted_iota(jnp.int32, (1, LANES), 1)
    key = lax.broadcasted_iota(jnp.int32, (block, block), 0)
    causal = key <= lax.broadcasted_iota(jnp.int32, (block, block), 1)
    for i in range(length // block):
        rows, before = pl.ds(i * block, block), pl.ds(0, i * block)
        results = []
        for h in range(2):
            mine = (lane < HEAD_DIM) if h == 0 else (lane >= HEAD_DIM)
            query = jnp.where(mine, q_ref[rows, :], 0)
            near = jnp.where(causal, dot(k_ref[rows, :], query, 1, 1), -1e30)
            highest = jnp.max(near, axis=0, keepdims=True)
            if i:
                far = dot(k_ref[before, :], query, 1, 1)
                highest = jnp.maximum(highest, jnp.max(far, axis=0, keepdims=True))
            near = jnp.exp(near - highest)
            total = jnp.sum(near, axis=0, keepdims=True)
            if i:
                far = jnp.exp(far - highest)
                total = total + jnp.sum(far, axis=0, keepdims=True)
            inverse = 1.0 / total
            result = dot((near * inverse).astype(BF16), v_ref[rows, :], 0, 0)
            if i:
                result = result + dot((far * inverse).astype(BF16), v_ref[before, :], 0, 0)
            results.append(result)
            lse_ref[0, h : h + 1, rows] = highest + jnp.log(total)
        out_ref[rows, :] = jnp.where(lane < HEAD_DIM, results[0], results[1]).astype(BF16)


def pair_specs(length, pairs):
    return lambda off: pl.BlockSpec(
        (length, LANES), lambda g: (g // pairs, off * pairs + g % pairs)
    )


def attend(qkv, length, block, deps):
    width, sequences = qkv.shape[1] // 3, qkv.shape[0] // length
    pairs = width // LANES
    at = pair_specs(length, pairs)
    return call(
        functools.partial(attend_kernel, block),
        "attend",
        [qkv, qkv, qkv],
        deps,
        grid=(sequences * pairs,),
        in_specs=[at(0), at(1), at(2)],
        out_specs=[at(0), pl.BlockSpec((1, 8, length), lambda g: (g, 0, 0))],
        out_shape=[
            jax.ShapeDtypeStruct((qkv.shape[0], width), BF16),
            jax.ShapeDtypeStruct((sequences * pairs, 8, length), F32),
        ],
    )


def attend_back_kernel(
    block,
    q_ref,
    k_ref,
    v_ref,
    grad_ref,
    mixed_ref,
    lse_ref,
    cos_ref,
    left_ref,
    right_ref,
    gq_ref,
    gk_ref,
    gv_ref,
    sum_ref,
    gk_sum,
    gv_sum,
):
    length = q_ref.shape[0]
    lane = lax.broadcasted_iota(jnp.int32, (1, LANES), 1)
    key = lax.broadcasted_iota(jnp.int32, (block, block), 0)
    causal = key <= lax.broadcasted_iota(jnp.int32, (block, block), 1)
    count = length // block
    sum_ref[...] = jnp.zeros_like(sum_ref)

    def put(ref, which, rows, value):
        value = value.astype(BF16)
        ref[rows, :] = value
        sum_ref[0, which : which + 1, :] += jnp.sum(value.astype(F32), axis=0, keepdims=True)

    def unrotated(value, rows):
        return rotated(value, cos_ref[rows, :], left_ref[rows, :], right_ref[rows, :], -1.0)

    for i in reversed(range(count)):
        rows = pl.ds(i * block, block)
        product = grad_ref[rows, :].astype(F32) * mixed_ref[rows, :].astype(F32)
        gq = None
        for h in range(2):
            mine = (lane < HEAD_DIM) if h == 0 else (lane >= HEAD_DIM)
            query = jnp.where(mine, q_ref[rows, :], 0)
            grad = jnp.where(mine, grad_ref[rows, :], 0)
            ones = jnp.where(mine, jnp.ones((8, LANES), F32), 0.0)
            delta = lax.dot_general(
                ones,
                product,
                (((1,), (1,)), ((), ())),
                precision=lax.Precision.HIGHEST,
                preferred_element_type=F32,
            )[0:1, :]
            lse = lse_ref[0, h : h + 1, rows]
            for j in range(i + 1):
                keys = pl.ds(j * block, block)
                key_rows = k_ref[keys, :]
                probs = jnp.exp(dot(key_rows, query, 1, 1) - lse)
                if j == i:
                    probs = jnp.where(causal, probs, 0.0)
                gprobs = dot(v_ref[keys, :], grad, 1, 1)
                gscores = (probs * (gprobs - delta)).astype(BF16)
                gv, gk = dot(probs.astype(BF16), grad, 1, 0), dot(gscores, query, 1, 0)
                if i == count - 1 and h == 0:
                    gv_sum[keys, :] = gv
                    gk_sum[keys, :] = gk
                else:
                    gv_sum[keys, :] += gv
                    gk_sum[keys, :] += gk
                part = dot(gscores, jnp.where(mine, key_rows, 0), 0, 0)
                gq = part if gq is None else gq + part
        put(gq_ref, 0, rows, unrotated(gq * HEAD_DIM**-0.5, rows))
    for i in range(count):
        rows = pl.ds(i * block, block)
        put(gk_ref, 1, rows, unrotated(gk_sum[rows, :], rows))
        put(gv_ref, 2, rows, gv_sum[rows, :])


def attend_back(qkv, grad, mixed, lse, tables, length, block, deps):
    width, sequences = qkv.shape[1] // 3, qkv.shape[0] // length
    pairs = width // LANES
    at = pair_specs(length, pairs)
    table = pl.BlockSpec((length, LANES), lambda g: (0, 0))
    small = pl.BlockSpec((1, 8, length), lambda g: (g, 0, 0))
    return call(
        functools.partial(attend_back_kernel, block),
        "attend_back",
        [qkv, qkv, qkv, grad, mixed, lse, *tables],
        deps,
        grid=(sequences * pairs,),
        in_specs=[at(0), at(1), at(2), at(0), at(0), small, table, table, table],
        out_specs=[at(0)] * 3 + [pl.BlockSpec((1, 8, LANES), lambda g: (g, 0, 0))],
        out_shape=[jax.ShapeDtypeStruct((qkv.shape[0], width), BF16)] * 3
        + [jax.ShapeDtypeStruct((sequences * pairs, 8, LANES), F32)],
        scratch_shapes=[pltpu.VMEM((length, LANES), F32)] * 2,
    )


def quarter_map(places, parts):
    turns = len(places)

    def rows_of(i, at):
        offset = jnp.int32(places[0])
        for n in range(1, turns):
            offset = jnp.where(i % turns == n, places[n], offset)
        return jnp.where(i < turns, parts, 0) + (at[0] + offset) % parts

    return rows_of


def split_outputs(step, turns, result, other_ref, own_ref):
    @pl.when(step < turns)
    def _():
        other_ref[0] = result

    @pl.when(step >= turns)
    def _():
        own_ref[0] = result


def split_specs(rows, model, turns):
    return [
        pl.BlockSpec((1, rows, model), lambda i, at: (jnp.minimum(i, turns - 1), 0, 0)),
        pl.BlockSpec((1, rows, model), lambda i, at: (jnp.maximum(i - turns, 0), 0, 0)),
    ]


def branch_kernel(count, turns, at_ref, mixed_ref, act_ref, *rest):
    blocks, (other_ref, own_ref, held, sems) = rest[:count], rest[count:]
    step = pl.program_id(0)

    @pl.when(step == 0)
    def _():
        loads = block_copies(blocks, columns_at(held, blocks[0].shape[1]), sems)
        for copy in loads:
            copy.start()
        for copy in loads:
            copy.wait()

    x = jnp.concatenate([mixed_ref[...], act_ref[...]], axis=1)
    split_outputs(step, turns, dot(x, held[...], 1, 0).astype(BF16), other_ref, own_ref)


def branch_sums(at_mp, mixed, act, blocks, parts, places, deps):
    rows, count, turns = mixed.shape[0] // (2 * parts), len(blocks), len(places)
    inner, model = blocks[0].shape[0], count * blocks[0].shape[1]
    where = quarter_map(places, parts)
    return call(
        functools.partial(branch_kernel, count, turns),
        "branch_sums",
        [mixed, act, *blocks],
        deps,
        (at_mp,),
        grid=(2 * turns,),
        in_specs=[
            pl.BlockSpec((rows, a.shape[1]), lambda i, at: (where(i, at), 0)) for a in (mixed, act)
        ]
        + [ANY] * count,
        out_specs=split_specs(rows, model, turns),
        out_shape=[jax.ShapeDtypeStruct((turns, rows, model), BF16)] * 2,
        scratch_shapes=[pltpu.VMEM((inner, model), BF16), pltpu.SemaphoreType.DMA((count,))],
    )


def grad_in_kernel(setup, at_ref, slope_ref, *rest):
    count, parts, places, width, hidden, many = setup
    refs = many // 2
    chunks = [Chunks.of(rest[:refs]), Chunks.of(rest[refs:many])]
    blocks, rest = rest[many : many + count], rest[many + count :]
    gmixed_ref, gpre_ref, dy_ref, gsum_ref, dsum_ref, held, dy_held, sems, dy_sems = rest[-9:]
    step, steps = pl.program_id(0), 2 * len(places)
    found = chunk_copies(chunks, places, parts, dy_held, dy_sems)
    loads = block_copies(blocks, columns_at(held, blocks[0].shape[1]), sems)

    @pl.when(step == 0)
    def _():
        for copy in loads:
            copy.start()
        start_all(found)
        gsum_ref[...] = jnp.zeros_like(gsum_ref)
        dsum_ref[...] = jnp.zeros_like(dsum_ref)
        for copy in loads:
            copy.wait()

    for slot in range(steps):

        @pl.when(step == slot)
        def _(slot=slot):
            wait_for(found[slot])

    dy = dy_held[step]
    dy_ref[...] = dy
    gmixed_ref[...] = dot(dy, held[:width, :], 1, 1).astype(BF16)
    for start in range(0, hidden, width):
        part = slice(start, start + width)
        gact = dot(dy, held[width + start : 2 * width + start, :], 1, 1)
        gpre = (gact * slope_ref[:, part].astype(F32)).astype(BF16)
        gpre_ref[:, part] = gpre
        gsum_ref[0:1, part] += jnp.sum(gpre.astype(F32), axis=0, keepdims=True)
    dsum_ref[0:1, :] += jnp.sum(dy.astype(F32), axis=0, keepdims=True)


def grad_in(at_mp, chunks, slope, blocks, width, parts, places, earlier, deps):
    rows, model = chunks[0].own.shape
    hidden, length = slope.shape[1], slope.shape[0]
    count, many = len(blocks), len(chunks[0].flat()) * 2
    turns = len(places)

    def where(i, at):
        m = jnp.int32(places[0])
        for n in range(1, turns):
            m = jnp.where(i % turns == n, places[n], m)
        return i // turns * parts + (at[0] ^ m)

    out = lambda w: pl.BlockSpec((rows, w), lambda i, at: (where(i, at), 0))
    total = lambda w: pl.BlockSpec((8, w), lambda i, at: (0, 0))
    setup = (count, parts, places, width, hidden, many)
    operands = [slope, *chunks[0].flat(), *chunks[1].flat(), *blocks]
    aliases = {1 + len(operands) + n: n for n in range(len(earlier))}
    return call(
        functools.partial(grad_in_kernel, setup),
        "grad_in",
        operands + list(earlier),
        deps,
        (at_mp,),
        grid=(2 * turns,),
        in_specs=[out(hidden)] + [ANY] * (many + count + len(earlier)),
        out_specs=[out(width), out(hidden), out(model), total(hidden), total(model)],
        out_shape=[jax.ShapeDtypeStruct((length, w), BF16) for w in (width, hidden, model)]
        + [jax.ShapeDtypeStruct((8, w), F32) for w in (hidden, model)],
        input_output_aliases=aliases,
        scratch_shapes=[
            pltpu.VMEM((width + hidden, model), BF16),
            pltpu.VMEM((2 * turns, rows, model), BF16),
            pltpu.SemaphoreType.DMA((count,)),
            pltpu.SemaphoreType.DMA((2 * turns,)),
        ],
    )


def grad_normed_kernel(
    count, turns, at_ref, gq_ref, gk_ref, gv_ref, gpre_ref, tokens_ref, *rest
):
    blocks, (other_ref, own_ref, sum_ref, held, sems) = rest[:count], rest[count:]
    step = pl.program_id(0)

    @pl.when(step == 0)
    def _():
        loads = block_copies(blocks, rows_at(held, blocks[0].shape[0]), sems)
        for copy in loads:
            copy.start()
        sum_ref[...] = jnp.zeros_like(sum_ref)
        for copy in loads:
            copy.wait()

    g = jnp.concatenate([gq_ref[...], gk_ref[...], gv_ref[...], gpre_ref[...]], axis=1)
    result = dot(g, held[...], 1, 1)
    sum_ref[0:1, :] += jnp.sum(result * normalized(tokens_ref[...]), axis=0, keepdims=True)
    sum_ref[1:2, :] += jnp.sum(result, axis=0, keepdims=True)
    split_outputs(step, turns, result.astype(BF16), other_ref, own_ref)


def grad_normed_sums(at_mp, gqkv, gpre, tokens, blocks, parts, places, deps):
    rows, count, turns = tokens.shape[0] // (2 * parts), len(blocks), len(places)
    model, total = tokens.shape[1], blocks[0].shape[1]
    where = quarter_map(places, parts)
    operands = [*gqkv, gpre, tokens]
    return call(
        functools.partial(grad_normed_kernel, count, turns),
        "grad_normed_sums",
        operands + list(blocks),
        deps,
        (at_mp,),
        grid=(2 * turns,),
        in_specs=[
            pl.BlockSpec((rows, a.shape[1]), lambda i, at: (where(i, at), 0)) for a in operands
        ]
        + [ANY] * count,
        out_specs=split_specs(rows, model, turns)
        + [pl.BlockSpec((8, model), lambda i, at: (0, 0))],
        out_shape=[jax.ShapeDtypeStruct((turns, rows, model), BF16)] * 2
        + [jax.ShapeDtypeStruct((8, model), F32)],
        scratch_shapes=[pltpu.VMEM((model, total), BF16), pltpu.SemaphoreType.DMA((count,))],
    )


def weight_grad_kernel(sizes, left, at_ref, *refs):
    ins, outs = refs[: len(refs) - len(sizes)], refs[len(refs) - len(sizes) :]
    if left:
        grad = jnp.concatenate([dot(ins[0][...], g[...], 0, 0) for g in ins[1:]], axis=1)
    else:
        grad = jnp.concatenate([dot(x[...], ins[-1][...], 0, 0) for x in ins[:-1]], axis=0)
    grad = grad.astype(BF16)
    first = 0
    for size, out_ref in zip(sizes, outs):

        @pl.when((pl.program_id(0) >= first) & (pl.program_id(0) < first + size))
        def _(out_ref=out_ref):
            out_ref[0] = grad

        first += size


def weight_grads(me, xs, gs, count, deps, left):
    plan = scatter_plan(count)
    sets = [(half, s) for s in range(len(plan[0])) for half in range(2)]
    sizes = [len(plan[half][s]) for half, s in sets]
    order = [j for half, s in sets for j in plan[half][s]]
    owners = lax.bitwise_xor(me, jnp.array(order, jnp.int32))
    length, (cut, whole) = xs[0].shape[0], ((xs, gs) if left else (gs, xs))
    size = cut[0].shape[1] // count
    cut_spec = pl.BlockSpec((length, size), lambda i, at: (0, at[i]))
    whole_specs = [pl.BlockSpec(a.shape, lambda i, at: (0, 0)) for a in whole]
    full = sum(a.shape[1] for a in whole)
    shape = (size, full) if left else (full, size)

    def out(first, many):
        return pl.BlockSpec(
            (1, *shape), lambda i, at: (jnp.clip(i - first, 0, many - 1), 0, 0)
        )

    firsts = [sum(sizes[:n]) for n in range(len(sizes))]
    outs = call(
        functools.partial(weight_grad_kernel, sizes, left),
        "weight_grads",
        [*xs, *gs],
        deps,
        (owners,),
        grid=(count,),
        in_specs=[cut_spec] + whole_specs if left else whole_specs + [cut_spec],
        out_specs=[out(first, many) for first, many in zip(firsts, sizes)],
        out_shape=[jax.ShapeDtypeStruct((many, *shape), BF16) for many in sizes],
    )
    return [[o for o, (half, _) in zip(outs, sets) if half == h] for h in range(2)]


def across(value, bit, count):
    return lax.ppermute(value, "dp", [(i, i ^ bit) for i in range(count)])


def line_step(below, above, k, parts):
    up = lax.ppermute(below, "mp", [(i, i + 1) for i in range(k - 1, parts - 1)])
    down = lax.ppermute(above, "mp", [(i + 1, i) for i in range(parts - k)])
    return up, down


class LineScatter:
    def __init__(self, sums):
        self.sums, self.parts = [list(s) for s in sums], len(sums)

    def total(self, k):
        if len(self.sums[k]) > 1:
            self.sums[k] = [sum(s.astype(F32) for s in self.sums[k]).astype(BF16)]
        return self.sums[k][0]

    def ready(self, s):
        return [self.total(k) for k in sorted({self.parts - s, s})]

    def step(self, s):
        parts = self.parts
        up = lax.ppermute(self.total(parts - s), "mp", [(i, i + 1) for i in range(s)])
        down = lax.ppermute(self.total(s), "mp", [(i, i - 1) for i in range(parts - s, parts)])
        self.sums[(parts - s - 1) % parts].append(up)
        self.sums[(s + 1) % parts].append(down)

    def result(self):
        return sum(s.astype(F32) for s in self.sums[0])


def chip_bits(count):
    bits, bit = [], 2
    while bit < count:
        bits.append(bit)
        bit *= 2
    return bits


def gather_blocks(own, sibling, count):
    held = {0: own, 1: sibling}
    orders = (chip_bits(count), chip_bits(count)[::-1])
    for s in range(len(orders[0])):
        moved = {}
        for half in range(2):
            bit = orders[half][s]
            for j in [j for j in held if j % 2 == half]:
                moved[j ^ bit] = across(held[j], bit, count)
        held.update(moved)
    return [held[j] for j in range(count)]


def scatter_orders(count):
    return (chip_bits(count)[::-1], chip_bits(count))


def scatter_plan(count):
    plan = []
    for half, order in enumerate(scatter_orders(count)):
        sets, rest = [[half]], [half]
        for bit in reversed(order):
            sets.insert(0, [j ^ bit for j in rest])
            rest = sets[0] + rest
        plan.append(sets)
    return plan


class BlockScatter:
    def __init__(self, halves, count):
        self.count, self.orders = count, scatter_orders(count)
        self.held = [[[a] for a in arrays] for arrays in halves]

    def total(self, half, s):
        addends = self.held[half][s]
        if len(addends) > 1:
            addends = [sum(a.astype(F32) for a in addends).astype(BF16)]
            self.held[half][s] = addends
        return addends[0]

    def ready(self, s):
        return [self.total(half, s) for half in range(2)]

    def step(self, s):
        for half in range(2):
            came = across(self.total(half, s), self.orders[half][s], self.count)
            first = 0
            for later in self.held[half][s + 1 :]:
                many = later[0].shape[0]
                later.append(came[first : first + many])
                first += many

    def finish(self):
        mine = sum(a[0].astype(F32) for a in self.held[0][-1])
        theirs = across(self.total(1, -1)[0], 1, self.count)
        return mine, theirs.astype(F32)


def on_device(
    tokens,
    norm_gain,
    norm_bias,
    qkv_weight,
    qkv_bias,
    dense_weight,
    dense_bias,
    up_weight,
    up_bias,
    down_weight,
    down_bias,
    cotangent,
    *,
    ndp,
    nmp,
):
    me, z = lax.axis_index("dp"), lax.axis_index("mp")
    core = me % 2
    at_mp = z.astype(jnp.int32)[None]
    length, model = tokens.shape[0] * nmp, tokens.shape[1]
    block = min(512, length)
    width, hidden = qkv_weight.shape[2] // 2, up_weight.shape[1] // 2
    chip_steps = len(chip_bits(ndp))
    rank = lambda array, axis, which, size: lax.dynamic_slice_in_dim(
        array, which * size, size, axis
    )

    def row_pack(which):
        qkv = rank(qkv_weight, 2, which, width)
        return jnp.concatenate([qkv[0], qkv[1], qkv[2], rank(up_weight, 1, which, hidden)], axis=1)

    def column_pack(which):
        return jnp.concatenate(
            [rank(dense_weight, 0, which, width), rank(down_weight, 0, which, hidden)], axis=0
        )

    below, above = [], []
    up, down = tokens, tokens
    for k in range(1, nmp):
        up, down = line_step(up, down, k, nmp)
        below.append(up)
        above.append(down)
    own = Chunks(tokens, below, above)
    other = Chunks.of([across(c, 1, ndp) for c in own.flat()])

    row_blocks = gather_blocks(row_pack(core), across(row_pack(1 - core), 1, ndp), ndp)
    late = tie(column_pack(core), row_blocks[2])
    late_other = tie(across(column_pack(1 - core), 1, ndp), row_blocks[2])
    column_blocks = gather_blocks(late, late_other, ndp)

    tables = rotary_tables(length)
    bias = jnp.concatenate(
        [
            rank(qkv_bias, 1, core, width).astype(F32).reshape(1, 3 * width),
            rank(up_bias[None, :], 1, core, hidden).astype(F32),
        ],
        axis=1,
    )
    gain, shift = norm_gain.astype(F32)[None, :], norm_bias.astype(F32)[None, :]
    cot = tie(cotangent, below[-1], above[-1])
    dy_below, dy_above = [], []
    up, down = line_step(cot, cot, 1, nmp)
    qkv, act, slope, normed, token_rows = project(
        at_mp, (own, other), row_blocks, bias, gain, shift, tables, width, [cot]
    )
    up, down = tie(up, qkv), tie(down, qkv)
    dy_below.append(up)
    dy_above.append(down)
    mixed, lse = attend(qkv, length, block, [up, down])
    anchor = mixed
    for k in range(2, nmp):
        up, down = line_step(up, down, k, nmp)
        if k < nmp - 1:
            up, down = tie(up, anchor), tie(down, anchor)
        dy_below.append(up)
        dy_above.append(down)
    places = list(range(nmp))
    other_sums, own_sums = branch_sums(
        at_mp, mixed, act, column_blocks, nmp, places, [dy_below[-2], dy_above[-2]]
    )
    came = across(other_sums, 1, ndp)
    branches = LineScatter([[own_sums[k], came[k]] for k in range(nmp)])

    dy_own = Chunks(cot, dy_below, dy_above)
    dy_other = Chunks.of([across(c, 1, ndp) for c in dy_own.flat()])
    near = lambda c: Chunks(c.own, c.below[:1], c.above[:1])
    first = grad_in(
        at_mp,
        (near(dy_own), near(dy_other)),
        slope,
        column_blocks,
        width,
        nmp,
        (0, 1),
        (),
        [other_sums],
    )
    second = grad_in(
        at_mp,
        (dy_own, dy_other),
        slope,
        column_blocks,
        width,
        nmp,
        tuple(range(2, nmp)),
        first[:3],
        branches.ready(1),
    )
    branches.step(1)
    gmixed, gpre, dy = second[:3]
    column_grads = BlockScatter(
        weight_grads(me, [mixed, act], [dy], ndp, [second[3]], left=False), ndp
    )
    column_grads.step(0)
    gq, gk, gv, qkv_sums = attend_back(
        qkv, gmixed, mixed, lse, tables, length, block, [column_grads.held[0][0][0], *branches.ready(2)]
    )
    for s in range(2, nmp - 1):
        branches.step(s)
    for s in range(1, chip_steps - 1):
        column_grads.step(s)
    early = [k for k in places if k % 2] if nmp > 2 else places
    late_places = [k for k in places if k not in early]
    grads_a = grad_normed_sums(
        at_mp,
        (gq, gk, gv),
        gpre,
        token_rows,
        row_blocks,
        nmp,
        early,
        [*branches.ready(nmp - 1), *column_grads.ready(chip_steps - 1)],
    )
    branches.step(nmp - 1)
    column_grads.step(chip_steps - 1)
    came_a = across(grads_a[0], 1, ndp)
    grads_b = grad_normed_sums(
        at_mp, (gq, gk, gv), gpre, token_rows, row_blocks, nmp, late_places, [grads_a[2]]
    )
    came_b = across(grads_b[0], 1, ndp)
    shares = {}
    for part, got, kept in ((early, came_a, grads_a[1]), (late_places, came_b, grads_b[1])):
        for n, k in enumerate(part):
            shares[k] = [kept[n], got[n]]
    grad_rows = LineScatter([shares[k] for k in places])
    up_grads = BlockScatter(
        weight_grads(me, [normed], [gpre], ndp, [grads_b[2], *grad_rows.ready(1)], left=True), ndp
    )
    grad_rows.step(1)
    up_grads.step(0)
    qkv_grads = BlockScatter(
        weight_grads(me, [normed], [gq, gk, gv], ndp, [up_grads.held[0][0][0]], left=True), ndp
    )
    for s in range(2, nmp):
        grad_rows.step(s)
    for s in range(1, chip_steps):
        up_grads.step(s)
    for s in range(chip_steps):
        qkv_grads.step(s)

    local_inputs = tokens.astype(F32)
    output = (
        local_inputs
        + branches.result()
        + (dense_bias.astype(F32) + down_bias.astype(F32))[None, :]
    ).astype(BF16)

    pairs = width // LANES
    qkv_sum = (
        qkv_sums.reshape(2, pairs, 8, LANES).sum(0)[:, :3, :].transpose(1, 0, 2).reshape(3 * width)
    )
    small = jnp.concatenate(
        [
            qkv_sum,
            first[3][0] + second[3][0],
            (grads_a[2][:2] + grads_b[2][:2]).reshape(2 * model),
            first[4][0] + second[4][0],
        ]
    )
    for bit in chip_bits(ndp):
        small = small + across(small, bit, ndp)
    inner = 3 * width + hidden
    here, grad_out_bias = small[: inner + 2 * model], small[inner + 2 * model :]
    there = across(here, 1, ndp)
    norm_sums = here[inner:] + there[inner:]
    sums = [norm_sums] + [
        lax.ppermute(norm_sums, "mp", [(i, i ^ j) for i in range(nmp)]) for j in range(1, nmp)
    ]
    while len(sums) > 1:
        sums = [a + b for a, b in zip(sums[::2], sums[1::2])]
    even, odd = jnp.where(core == 0, here, there), jnp.where(core == 0, there, here)
    grad_qkv_bias = jnp.concatenate(
        [even[: 3 * width].reshape(3, width), odd[: 3 * width].reshape(3, width)], axis=1
    )
    grad_up_bias = jnp.concatenate([even[3 * width : inner], odd[3 * width : inner]])

    def both(mine, theirs, axis):
        return jnp.where(
            core == 0,
            jnp.concatenate([mine, theirs], axis=axis),
            jnp.concatenate([theirs, mine], axis=axis),
        )

    mine, theirs = column_grads.finish()
    owned_dense = both(mine[:width], theirs[:width], 0)
    owned_down = both(mine[width:], theirs[width:], 0)
    owned_up = both(*up_grads.finish(), 1)
    mine, theirs = qkv_grads.finish()
    owned_qkv = jnp.stack(
        [
            both(mine[:, c * width : (c + 1) * width], theirs[:, c * width : (c + 1) * width], 1)
            for c in range(3)
        ]
    )

    row_mean = jnp.mean(local_inputs, axis=1, keepdims=True)
    centered = local_inputs - row_mean
    row_var = jnp.mean(centered * centered, axis=1, keepdims=True)
    inverse_std = lax.rsqrt(row_var + EPS)
    normal_rows = centered * inverse_std
    scaled_grad = grad_rows.result() * gain
    first_mean = jnp.mean(scaled_grad, axis=1, keepdims=True)
    second_mean = jnp.mean(scaled_grad * normal_rows, axis=1, keepdims=True)
    grad_tokens = (
        cotangent.astype(F32)
        + (scaled_grad - first_mean - normal_rows * second_mean) * inverse_std
    ).astype(BF16)
    return (
        output,
        grad_tokens,
        sums[0][:model],
        sums[0][model:],
        owned_qkv,
        grad_qkv_bias,
        owned_dense,
        grad_out_bias,
        owned_up,
        grad_up_bias,
        owned_down,
        grad_out_bias,
    )


def solution(mesh):
    return jax.shard_map(
        functools.partial(on_device, ndp=mesh.shape["dp"], nmp=mesh.shape["mp"]),
        mesh=mesh,
        in_specs=(
            P(("dp", "mp"), None),
            P(),
            P(),
            P(None, "dp", "mp"),
            P(None, "mp"),
            P("mp", "dp"),
            P(),
            P("dp", "mp"),
            P("mp"),
            P("mp", "dp"),
            P(),
            P(("dp", "mp"), None),
        ),
        out_specs=(
            P(("dp", "mp"), None),
            P(("dp", "mp"), None),
            P(),
            P(),
            P(None, "dp", "mp"),
            P(None, "mp"),
            P("mp", "dp"),
            P(),
            P("dp", "mp"),
            P("mp"),
            P("mp", "dp"),
            P(),
        ),
        check_vma=False,
    )
```

```python
import functools

import jax
import jax.numpy as jnp
import numpy as np
from jax import lax
from jax.experimental import pallas as pl
from jax.experimental.pallas import tpu as pltpu
from jax.sharding import PartitionSpec as P

HEAD_DIM = 64
ROT = 32
EPS = 1e-05
LANES = 128
VMEM_LIMIT = 56 << 20
F32 = jnp.float32
BF16 = jnp.bfloat16
ANY = pl.BlockSpec(memory_space=pl.ANY)


def dot(lhs, rhs, lhs_dim, rhs_dim):
    return lax.dot_general(
        lhs, rhs, (((lhs_dim,), (rhs_dim,)), ((), ())), preferred_element_type=F32
    )


def call(kernel, name, operands, deps=(), scalars=(), **spec):
    deps, many, lead = tuple(deps), len(operands), len(scalars)

    def body(*refs):
        kernel(*refs[: lead + many], *refs[lead + many + len(deps) :])

    in_specs = list(spec.pop("in_specs")) + [ANY] * len(deps)
    out_shape, aliases = spec.pop("out_shape"), spec.pop("input_output_aliases", {})
    if scalars:
        grid_spec = pltpu.PrefetchScalarGridSpec(
            num_scalar_prefetch=lead, in_specs=in_specs, **spec
        )
        spec = {"grid_spec": grid_spec}
    else:
        spec["in_specs"] = in_specs
    return pl.pallas_call(
        body,
        out_shape=out_shape,
        input_output_aliases=aliases,
        compiler_params=pltpu.CompilerParams(vmem_limit_bytes=VMEM_LIMIT),
        cost_estimate=pl.CostEstimate(flops=0, transcendentals=0, bytes_accessed=0),
        name=name,
        **spec,
    )(*scalars, *operands, *deps)


def fence(values, deps=()):
    return call(
        lambda *refs: None,
        "fence",
        values,
        deps,
        in_specs=[ANY] * len(values),
        out_specs=[ANY] * len(values),
        out_shape=[jax.ShapeDtypeStruct(v.shape, v.dtype) for v in values],
        input_output_aliases={n: n for n in range(len(values))},
    )


def rotary_tables(length):
    positions = np.arange(length, dtype=np.float32)
    frequency = 10000.0 ** (-np.arange(ROT // 2, dtype=np.float64) * 2.0 / ROT)
    angles = positions[:, None] * frequency.astype(np.float32)[None, :]
    cosine, sine = np.cos(angles.astype(np.float64)), np.sin(angles.astype(np.float64))
    rest = HEAD_DIM - ROT
    none = np.zeros((length, ROT // 2))
    ones, zeros = np.ones((length, rest)), np.zeros((length, rest))
    straight = np.concatenate([cosine, cosine, ones], axis=1)
    left = np.concatenate([-sine, none, zeros], axis=1)
    right = np.concatenate([none, sine, zeros], axis=1)
    return [
        jnp.asarray(np.concatenate([t, t], axis=1).astype(np.float32))
        for t in (straight, left, right)
    ]


def rotated(u, straight, left, right, sign):
    half = ROT // 2
    turned = pltpu.roll(u, LANES - half, 1) * left + pltpu.roll(u, half, 1) * right
    return u * straight + sign * turned


def normalized(x):
    x = x.astype(F32)
    centered = x - jnp.mean(x, axis=1, keepdims=True)
    variance = jnp.mean(centered * centered, axis=1, keepdims=True)
    return centered * lax.rsqrt(variance + EPS)


def block_copies(blocks, place, sems):
    me = lax.axis_index("dp")
    return [
        pltpu.make_async_copy(block, place(lax.bitwise_xor(me, j)), sems.at[j])
        for j, block in enumerate(blocks)
    ]


def rows_at(ref, size):
    return lambda owner: ref.at[pl.ds(pl.multiple_of(owner * size, size), size)]


def columns_at(ref, size):
    return lambda owner: ref.at[:, pl.ds(pl.multiple_of(owner * size, size), size)]


def flat(chunks):
    return [array for k in sorted(chunks) for array in chunks[k]]


def unflat(refs, shifts):
    refs, chunks = list(refs), {}
    for k, many in shifts:
        chunks[k], refs = refs[:many], refs[many:]
    return chunks


def chunk_copies(chunks, places, parts, held, sems):
    z = lax.axis_index("mp")
    found = []
    for s, sequence in enumerate(chunks):
        for i, m in enumerate(places):
            slot, options = s * len(places) + i, []
            for k in sorted({(at - (at ^ m)) % parts for at in range(parts)}):
                here = lax.rem(z - lax.bitwise_xor(z, m) + parts, parts) == k
                if len(sequence[k]) == 1:
                    options.append((None if k == 0 else here, sequence[k][0]))
                else:
                    options.append((here & (z >= parts // 2), sequence[k][0]))
                    options.append((here & (z < parts // 2), sequence[k][1]))
            found.append(
                [
                    (here, pltpu.make_async_copy(source, held.at[slot], sems.at[slot]))
                    for here, source in options
                ]
            )
    return found


def start_all(found):
    for options in found:
        for here, copy in options:
            if here is None:
                copy.start()
            else:
                pl.when(here)(copy.start)


def wait_for(options):
    options[0][1].wait()


def project_kernel(setup, at_ref, bias_ref, gain_ref, shift_ref, cos_ref, left_ref, right_ref, *rest):
    count, parts, places, width, hidden, shifts = setup
    refs = sum(many for _, many in shifts)
    chunks = [unflat(rest[:refs], shifts), unflat(rest[refs : 2 * refs], shifts)]
    blocks, rest = rest[2 * refs : 2 * refs + count], rest[2 * refs + count :]
    qkv_ref, act_ref, slope_ref, normed_ref, tokens_ref, held, x_held, ready, sems, x_sems = rest
    step, steps = pl.program_id(0), 2 * len(places)
    found = chunk_copies(chunks, places, parts, x_held, x_sems)
    loads = block_copies(blocks, rows_at(held, blocks[0].shape[0]), sems)

    def norm(slot):
        return (normalized(x_held[slot]) * gain_ref[...] + shift_ref[...]).astype(BF16)

    @pl.when(step == 0)
    def _():
        for copy in loads:
            copy.start()
        start_all(found)
        wait_for(found[0])
        ready[0] = norm(0)
        for copy in loads:
            copy.wait()

    for slot in range(1, steps):

        @pl.when(step == slot - 1)
        def _(slot=slot):
            wait_for(found[slot])

    x = ready[step % 2]
    normed_ref[...] = x
    tokens_ref[...] = x_held[step]
    ready[(step + 1) % 2] = norm((step + 1) % steps)
    root = 0.7978845608028654
    for t in range((3 * width + hidden) // width):
        columns = slice(t * width, (t + 1) * width)
        y = dot(x, held[:, columns], 1, 0) + bias_ref[:, columns]
        if t < 3:
            for g in range(width // LANES):
                part = y[:, g * LANES : (g + 1) * LANES]
                if t < 2:
                    part = rotated(part, cos_ref[...], left_ref[...], right_ref[...], 1.0)
                if t == 0:
                    part = part * HEAD_DIM**-0.5
                start = t * width + g * LANES
                qkv_ref[:, start : start + LANES] = part.astype(BF16)
        else:
            columns = slice((t - 3) * width, (t - 2) * width)
            square = y * y
            turn = jnp.tanh(root * y * (1.0 + 0.044715 * square))
            half = 0.5 * (1.0 + turn)
            act_ref[:, columns] = (y * half).astype(BF16)
            slope = half * (1.0 + y * (1.0 - turn) * (root + (3.0 * 0.044715 * root) * square))
            slope_ref[:, columns] = slope.astype(BF16)


def project(at_mp, chunks, blocks, bias, gain, shift, tables, width, parts, deps):
    places, shifts = tuple(range(parts)), [(k, len(chunks[0][k])) for k in sorted(chunks[0])]
    rows, model = chunks[0][0][0].shape
    total, hidden = blocks[0].shape[1], blocks[0].shape[1] - 3 * width
    count, length = len(blocks), 2 * parts * rows
    table = pl.BlockSpec((rows, LANES), lambda i, at: (at[0] ^ (i % parts), 0))
    out = lambda w: pl.BlockSpec((rows, w), lambda i, at: (i - i % parts + (at[0] ^ (i % parts)), 0))
    line = lambda a: pl.BlockSpec(a.shape, lambda i, at: (0, 0))
    widths = (3 * width, hidden, hidden, model, model)
    setup = (count, parts, places, width, hidden, shifts)
    return call(
        functools.partial(project_kernel, setup),
        "project",
        [bias, gain, shift, *tables, *flat(chunks[0]), *flat(chunks[1]), *blocks],
        deps,
        (at_mp,),
        grid=(2 * parts,),
        in_specs=[line(bias), line(gain), line(shift), table, table, table]
        + [ANY] * (2 * len(flat(chunks[0])) + count),
        out_specs=[out(w) for w in widths],
        out_shape=[jax.ShapeDtypeStruct((length, w), BF16) for w in widths],
        scratch_shapes=[
            pltpu.VMEM((model, total), BF16),
            pltpu.VMEM((2 * parts, rows, model), BF16),
            pltpu.VMEM((2, rows, model), BF16),
            pltpu.SemaphoreType.DMA((count,)),
            pltpu.SemaphoreType.DMA((2 * parts,)),
        ],
    )


def attend_kernel(block, q_ref, k_ref, v_ref, out_ref, lse_ref):
    length = q_ref.shape[0]
    lane = lax.broadcasted_iota(jnp.int32, (1, LANES), 1)
    key = lax.broadcasted_iota(jnp.int32, (block, block), 0)
    causal = key <= lax.broadcasted_iota(jnp.int32, (block, block), 1)
    for i in range(length // block):
        rows, before = pl.ds(i * block, block), pl.ds(0, i * block)
        results = []
        for h in range(2):
            mine = (lane < HEAD_DIM) if h == 0 else (lane >= HEAD_DIM)
            query = jnp.where(mine, q_ref[rows, :], 0)
            near = jnp.where(causal, dot(k_ref[rows, :], query, 1, 1), -1e30)
            highest = jnp.max(near, axis=0, keepdims=True)
            if i:
                far = dot(k_ref[before, :], query, 1, 1)
                highest = jnp.maximum(highest, jnp.max(far, axis=0, keepdims=True))
            near = jnp.exp(near - highest)
            total = jnp.sum(near, axis=0, keepdims=True)
            if i:
                far = jnp.exp(far - highest)
                total = total + jnp.sum(far, axis=0, keepdims=True)
            inverse = 1.0 / total
            result = dot((near * inverse).astype(BF16), v_ref[rows, :], 0, 0)
            if i:
                result = result + dot((far * inverse).astype(BF16), v_ref[before, :], 0, 0)
            results.append(result)
            lse_ref[0, h : h + 1, rows] = highest + jnp.log(total)
        out_ref[rows, :] = jnp.where(lane < HEAD_DIM, results[0], results[1]).astype(BF16)


def pair_specs(length, pairs):
    return lambda off: pl.BlockSpec(
        (length, LANES), lambda g: (g // pairs, off * pairs + g % pairs)
    )


def attend(qkv, length, block, deps):
    width, sequences = qkv.shape[1] // 3, qkv.shape[0] // length
    pairs = width // LANES
    at = pair_specs(length, pairs)
    return call(
        functools.partial(attend_kernel, block),
        "attend",
        [qkv, qkv, qkv],
        deps,
        grid=(sequences * pairs,),
        in_specs=[at(0), at(1), at(2)],
        out_specs=[at(0), pl.BlockSpec((1, 8, length), lambda g: (g, 0, 0))],
        out_shape=[
            jax.ShapeDtypeStruct((qkv.shape[0], width), BF16),
            jax.ShapeDtypeStruct((sequences * pairs, 8, length), F32),
        ],
    )


def attend_back_kernel(
    block,
    q_ref,
    k_ref,
    v_ref,
    grad_ref,
    mixed_ref,
    lse_ref,
    cos_ref,
    left_ref,
    right_ref,
    gq_ref,
    gk_ref,
    gv_ref,
    sum_ref,
    gk_sum,
    gv_sum,
):
    length = q_ref.shape[0]
    lane = lax.broadcasted_iota(jnp.int32, (1, LANES), 1)
    key = lax.broadcasted_iota(jnp.int32, (block, block), 0)
    causal = key <= lax.broadcasted_iota(jnp.int32, (block, block), 1)
    count = length // block
    sum_ref[...] = jnp.zeros_like(sum_ref)

    def put(ref, which, rows, value):
        value = value.astype(BF16)
        ref[rows, :] = value
        sum_ref[0, which : which + 1, :] += jnp.sum(value.astype(F32), axis=0, keepdims=True)

    def unrotated(value, rows):
        return rotated(value, cos_ref[rows, :], left_ref[rows, :], right_ref[rows, :], -1.0)

    for i in reversed(range(count)):
        rows = pl.ds(i * block, block)
        product = grad_ref[rows, :].astype(F32) * mixed_ref[rows, :].astype(F32)
        gq = None
        for h in range(2):
            mine = (lane < HEAD_DIM) if h == 0 else (lane >= HEAD_DIM)
            query = jnp.where(mine, q_ref[rows, :], 0)
            grad = jnp.where(mine, grad_ref[rows, :], 0)
            ones = jnp.where(mine, jnp.ones((8, LANES), F32), 0.0)
            delta = lax.dot_general(
                ones,
                product,
                (((1,), (1,)), ((), ())),
                precision=lax.Precision.HIGHEST,
                preferred_element_type=F32,
            )[0:1, :]
            lse = lse_ref[0, h : h + 1, rows]
            for j in range(i + 1):
                keys = pl.ds(j * block, block)
                key_rows = k_ref[keys, :]
                probs = jnp.exp(dot(key_rows, query, 1, 1) - lse)
                if j == i:
                    probs = jnp.where(causal, probs, 0.0)
                gprobs = dot(v_ref[keys, :], grad, 1, 1)
                gscores = (probs * (gprobs - delta)).astype(BF16)
                gv, gk = dot(probs.astype(BF16), grad, 1, 0), dot(gscores, query, 1, 0)
                if i == count - 1 and h == 0:
                    gv_sum[keys, :] = gv
                    gk_sum[keys, :] = gk
                else:
                    gv_sum[keys, :] += gv
                    gk_sum[keys, :] += gk
                part = dot(gscores, jnp.where(mine, key_rows, 0), 0, 0)
                gq = part if gq is None else gq + part
        put(gq_ref, 0, rows, unrotated(gq * HEAD_DIM**-0.5, rows))
    for i in range(count):
        rows = pl.ds(i * block, block)
        put(gk_ref, 1, rows, unrotated(gk_sum[rows, :], rows))
        put(gv_ref, 2, rows, gv_sum[rows, :])


def attend_back(qkv, grad, mixed, lse, tables, length, block, deps):
    width, sequences = qkv.shape[1] // 3, qkv.shape[0] // length
    pairs = width // LANES
    at = pair_specs(length, pairs)
    table = pl.BlockSpec((length, LANES), lambda g: (0, 0))
    small = pl.BlockSpec((1, 8, length), lambda g: (g, 0, 0))
    return call(
        functools.partial(attend_back_kernel, block),
        "attend_back",
        [qkv, qkv, qkv, grad, mixed, lse, *tables],
        deps,
        grid=(sequences * pairs,),
        in_specs=[at(0), at(1), at(2), at(0), at(0), small, table, table, table],
        out_specs=[at(0)] * 3 + [pl.BlockSpec((1, 8, LANES), lambda g: (g, 0, 0))],
        out_shape=[jax.ShapeDtypeStruct((qkv.shape[0], width), BF16)] * 3
        + [jax.ShapeDtypeStruct((sequences * pairs, 8, LANES), F32)],
        scratch_shapes=[pltpu.VMEM((length, LANES), F32)] * 2,
    )


def quarter_map(places, parts):
    turns = len(places)

    def rows_of(i, at):
        offset = jnp.int32(places[0])
        for n in range(1, turns):
            offset = jnp.where(i % turns == n, places[n], offset)
        return jnp.where(i < turns, parts, 0) + (at[0] + offset) % parts

    return rows_of


def split_outputs(step, turns, result, other_ref, own_ref):
    @pl.when(step < turns)
    def _():
        other_ref[0] = result

    @pl.when(step >= turns)
    def _():
        own_ref[0] = result


def split_specs(rows, model, turns):
    return [
        pl.BlockSpec((1, rows, model), lambda i, at: (jnp.minimum(i, turns - 1), 0, 0)),
        pl.BlockSpec((1, rows, model), lambda i, at: (jnp.maximum(i - turns, 0), 0, 0)),
    ]


def branch_kernel(count, turns, at_ref, mixed_ref, act_ref, *rest):
    blocks, (other_ref, own_ref, held, sems) = rest[:count], rest[count:]
    step = pl.program_id(0)

    @pl.when(step == 0)
    def _():
        loads = block_copies(blocks, columns_at(held, blocks[0].shape[1]), sems)
        for copy in loads:
            copy.start()
        for copy in loads:
            copy.wait()

    x = jnp.concatenate([mixed_ref[...], act_ref[...]], axis=1)
    split_outputs(step, turns, dot(x, held[...], 1, 0).astype(BF16), other_ref, own_ref)


def branch_sums(at_mp, mixed, act, blocks, parts, places, deps):
    rows, count, turns = mixed.shape[0] // (2 * parts), len(blocks), len(places)
    inner, model = blocks[0].shape[0], count * blocks[0].shape[1]
    where = quarter_map(places, parts)
    return call(
        functools.partial(branch_kernel, count, turns),
        "branch_sums",
        [mixed, act, *blocks],
        deps,
        (at_mp,),
        grid=(2 * turns,),
        in_specs=[
            pl.BlockSpec((rows, a.shape[1]), lambda i, at: (where(i, at), 0)) for a in (mixed, act)
        ]
        + [ANY] * count,
        out_specs=split_specs(rows, model, turns),
        out_shape=[jax.ShapeDtypeStruct((turns, rows, model), BF16)] * 2,
        scratch_shapes=[pltpu.VMEM((inner, model), BF16), pltpu.SemaphoreType.DMA((count,))],
    )


def grad_in_kernel(setup, at_ref, slope_ref, *rest):
    count, parts, places, width, hidden, shifts = setup
    refs = sum(many for _, many in shifts)
    many = 2 * refs
    chunks = [unflat(rest[:refs], shifts), unflat(rest[refs:many], shifts)]
    blocks, rest = rest[many : many + count], rest[many + count :]
    gmixed_ref, gpre_ref, dy_ref, gsum_ref, dsum_ref, held, dy_held, sems, dy_sems = rest[-9:]
    step, steps = pl.program_id(0), 2 * len(places)
    found = chunk_copies(chunks, places, parts, dy_held, dy_sems)
    loads = block_copies(blocks, columns_at(held, blocks[0].shape[1]), sems)

    @pl.when(step == 0)
    def _():
        for copy in loads:
            copy.start()
        start_all(found)
        gsum_ref[...] = jnp.zeros_like(gsum_ref)
        dsum_ref[...] = jnp.zeros_like(dsum_ref)
        for copy in loads:
            copy.wait()

    for slot in range(steps):

        @pl.when(step == slot)
        def _(slot=slot):
            wait_for(found[slot])

    dy = dy_held[step]
    dy_ref[...] = dy
    gmixed_ref[...] = dot(dy, held[:width, :], 1, 1).astype(BF16)
    for start in range(0, hidden, width):
        part = slice(start, start + width)
        gact = dot(dy, held[width + start : 2 * width + start, :], 1, 1)
        gpre = (gact * slope_ref[:, part].astype(F32)).astype(BF16)
        gpre_ref[:, part] = gpre
        gsum_ref[0:1, part] += jnp.sum(gpre.astype(F32), axis=0, keepdims=True)
    dsum_ref[0:1, :] += jnp.sum(dy.astype(F32), axis=0, keepdims=True)


def grad_in(at_mp, chunks, slope, blocks, width, parts, places, earlier, deps):
    rows, model = chunks[0][0][0].shape
    hidden, length = slope.shape[1], slope.shape[0]
    shifts = [(k, len(chunks[0][k])) for k in sorted(chunks[0])]
    count, many = len(blocks), len(flat(chunks[0])) * 2
    turns = len(places)

    def where(i, at):
        m = jnp.int32(places[0])
        for n in range(1, turns):
            m = jnp.where(i % turns == n, places[n], m)
        return i // turns * parts + (at[0] ^ m)

    out = lambda w: pl.BlockSpec((rows, w), lambda i, at: (where(i, at), 0))
    total = lambda w: pl.BlockSpec((8, w), lambda i, at: (0, 0))
    setup = (count, parts, places, width, hidden, shifts)
    operands = [slope, *flat(chunks[0]), *flat(chunks[1]), *blocks]
    aliases = {1 + len(operands) + n: n for n in range(len(earlier))}
    return call(
        functools.partial(grad_in_kernel, setup),
        "grad_in",
        operands + list(earlier),
        deps,
        (at_mp,),
        grid=(2 * turns,),
        in_specs=[out(hidden)] + [ANY] * (many + count + len(earlier)),
        out_specs=[out(width), out(hidden), out(model), total(hidden), total(model)],
        out_shape=[jax.ShapeDtypeStruct((length, w), BF16) for w in (width, hidden, model)]
        + [jax.ShapeDtypeStruct((8, w), F32) for w in (hidden, model)],
        input_output_aliases=aliases,
        scratch_shapes=[
            pltpu.VMEM((width + hidden, model), BF16),
            pltpu.VMEM((2 * turns, rows, model), BF16),
            pltpu.SemaphoreType.DMA((count,)),
            pltpu.SemaphoreType.DMA((2 * turns,)),
        ],
    )


def grad_normed_kernel(
    count, turns, at_ref, gq_ref, gk_ref, gv_ref, gpre_ref, tokens_ref, *rest
):
    blocks, (other_ref, own_ref, sum_ref, held, sems) = rest[:count], rest[count:]
    step = pl.program_id(0)

    @pl.when(step == 0)
    def _():
        loads = block_copies(blocks, rows_at(held, blocks[0].shape[0]), sems)
        for copy in loads:
            copy.start()
        sum_ref[...] = jnp.zeros_like(sum_ref)
        for copy in loads:
            copy.wait()

    g = jnp.concatenate([gq_ref[...], gk_ref[...], gv_ref[...], gpre_ref[...]], axis=1)
    result = dot(g, held[...], 1, 1)
    sum_ref[0:1, :] += jnp.sum(result * normalized(tokens_ref[...]), axis=0, keepdims=True)
    sum_ref[1:2, :] += jnp.sum(result, axis=0, keepdims=True)
    split_outputs(step, turns, result.astype(BF16), other_ref, own_ref)


def grad_normed_sums(at_mp, gqkv, gpre, tokens, blocks, parts, places, deps):
    rows, count, turns = tokens.shape[0] // (2 * parts), len(blocks), len(places)
    model, total = tokens.shape[1], blocks[0].shape[1]
    where = quarter_map(places, parts)
    operands = [*gqkv, gpre, tokens]
    return call(
        functools.partial(grad_normed_kernel, count, turns),
        "grad_normed_sums",
        operands + list(blocks),
        deps,
        (at_mp,),
        grid=(2 * turns,),
        in_specs=[
            pl.BlockSpec((rows, a.shape[1]), lambda i, at: (where(i, at), 0)) for a in operands
        ]
        + [ANY] * count,
        out_specs=split_specs(rows, model, turns)
        + [pl.BlockSpec((8, model), lambda i, at: (0, 0))],
        out_shape=[jax.ShapeDtypeStruct((turns, rows, model), BF16)] * 2
        + [jax.ShapeDtypeStruct((8, model), F32)],
        scratch_shapes=[pltpu.VMEM((model, total), BF16), pltpu.SemaphoreType.DMA((count,))],
    )


def weight_grad_kernel(sizes, left, at_ref, *refs):
    ins, outs = refs[: len(refs) - len(sizes)], refs[len(refs) - len(sizes) :]
    if left:
        grad = jnp.concatenate([dot(ins[0][...], g[...], 0, 0) for g in ins[1:]], axis=1)
    else:
        grad = jnp.concatenate([dot(x[...], ins[-1][...], 0, 0) for x in ins[:-1]], axis=0)
    grad = grad.astype(BF16)
    first = 0
    for size, out_ref in zip(sizes, outs):

        @pl.when((pl.program_id(0) >= first) & (pl.program_id(0) < first + size))
        def _(out_ref=out_ref):
            out_ref[0] = grad

        first += size


def weight_grads(me, xs, gs, count, deps, left):
    plan = scatter_plan(count)
    sets = [(half, s) for s in range(len(plan[0])) for half in range(2)]
    sizes = [len(plan[half][s]) for half, s in sets]
    order = [j for half, s in sets for j in plan[half][s]]
    owners = lax.bitwise_xor(me, jnp.array(order, jnp.int32))
    length, (cut, whole) = xs[0].shape[0], ((xs, gs) if left else (gs, xs))
    size = cut[0].shape[1] // count
    cut_spec = pl.BlockSpec((length, size), lambda i, at: (0, at[i]))
    whole_specs = [pl.BlockSpec(a.shape, lambda i, at: (0, 0)) for a in whole]
    full = sum(a.shape[1] for a in whole)
    shape = (size, full) if left else (full, size)

    def out(first, many):
        return pl.BlockSpec(
            (1, *shape), lambda i, at: (jnp.clip(i - first, 0, many - 1), 0, 0)
        )

    firsts = [sum(sizes[:n]) for n in range(len(sizes))]
    outs = call(
        functools.partial(weight_grad_kernel, sizes, left),
        "weight_grads",
        [*xs, *gs],
        deps,
        (owners,),
        grid=(count,),
        in_specs=[cut_spec] + whole_specs if left else whole_specs + [cut_spec],
        out_specs=[out(first, many) for first, many in zip(firsts, sizes)],
        out_shape=[jax.ShapeDtypeStruct((many, *shape), BF16) for many in sizes],
    )
    return [[o for o, (half, _) in zip(outs, sets) if half == h] for h in range(2)]


def across(value, bit, count):
    return lax.ppermute(value, "dp", [(i, i ^ bit) for i in range(count)])


def ring(value, k, parts):
    return lax.ppermute(value, "mp", [(i, (i + k) % parts) for i in range(parts)])


def gather_near(own, parts):
    shifts = (1, 3) if parts == 4 else range(1, parts)
    return {0: [own], **{k: [ring(own, k, parts)] for k in shifts}}


def gather_far(chunks, parts):
    if parts == 4:
        up = lax.ppermute(chunks[1][0], "mp", [(1, 2), (2, 3)])
        down = lax.ppermute(chunks[3][0], "mp", [(1, 0), (2, 1)])
        chunks = {**chunks, 2: [up, down]}
    return chunks


class LineScatter:
    def __init__(self, sums):
        self.sums, self.parts = [list(s) for s in sums], len(sums)

    def total(self, k):
        if len(self.sums[k]) > 1:
            self.sums[k] = [sum(s.astype(F32) for s in self.sums[k]).astype(BF16)]
        return self.sums[k][0]

    def far_ready(self):
        return [self.total(2)] if self.parts == 4 else []

    def far(self):
        if self.parts == 4:
            self.sums[1].append(lax.ppermute(self.total(2), "mp", [(0, 1), (1, 2)]))
            self.sums[3].append(lax.ppermute(self.total(2), "mp", [(3, 2), (2, 1)]))

    def shifts(self):
        return (1, 3) if self.parts == 4 else range(1, self.parts)

    def near_ready(self):
        return [self.total(k) for k in self.shifts()]

    def near(self):
        self.sums[0] += [ring(self.total(k), k, self.parts) for k in self.shifts()]

    def result(self):
        return sum(s.astype(F32) for s in self.sums[0])


def chip_bits(count):
    bits, bit = [], 2
    while bit < count:
        bits.append(bit)
        bit *= 2
    return bits


class BlockGather:
    def __init__(self, own, sibling, count):
        self.held, self.count = {0: own, 1: sibling}, count
        self.orders = (chip_bits(count), chip_bits(count)[::-1])

    def first(self):
        start, orders = dict(self.held), self.orders
        for s in range(min(2, len(orders[0]))):
            for half in range(2):
                bit = orders[half][s]
                self.held[half ^ bit] = across(start[half], bit, self.count)

    def second(self):
        for s in range(1, len(self.orders[0])):
            for half in range(2):
                order = self.orders[half]
                bit, done = order[s], order[:s]
                for j in [j for j in self.held if j % 2 == half and not j & bit]:
                    if j ^ bit not in self.held and not any(j & b for b in order[s:]):
                        self.held[j ^ bit] = across(self.held[j], bit, self.count)

    def fenced(self, deps=()):
        keys = sorted(self.held)
        self.held = dict(zip(keys, fence([self.held[j] for j in keys], deps)))

    def blocks(self):
        return [self.held[j] for j in range(self.count)]


def scatter_orders(count):
    return (chip_bits(count)[::-1], chip_bits(count))


def scatter_plan(count):
    plan = []
    for half, order in enumerate(scatter_orders(count)):
        sets, rest = [[half]], [half]
        for bit in reversed(order):
            sets.insert(0, [j ^ bit for j in rest])
            rest = sets[0] + rest
        plan.append(sets)
    return plan


class BlockScatter:
    def __init__(self, halves, count):
        self.count, self.orders = count, scatter_orders(count)
        self.held = [[[a] for a in arrays] for arrays in halves]

    def total(self, half, s):
        addends = self.held[half][s]
        if len(addends) > 1:
            addends = [sum(a.astype(F32) for a in addends).astype(BF16)]
            self.held[half][s] = addends
        return addends[0]

    def ready(self, s):
        return [self.total(half, s) for half in range(2)]

    def step(self, s):
        for half in range(2):
            came = across(self.total(half, s), self.orders[half][s], self.count)
            first = 0
            for later in self.held[half][s + 1 :]:
                many = later[0].shape[0]
                later.append(came[first : first + many])
                first += many

    def finish(self):
        mine = sum(a[0].astype(F32) for a in self.held[0][-1])
        theirs = across(self.total(1, -1)[0], 1, self.count)
        return mine, theirs.astype(F32)


def on_device(
    tokens,
    norm_gain,
    norm_bias,
    qkv_weight,
    qkv_bias,
    dense_weight,
    dense_bias,
    up_weight,
    up_bias,
    down_weight,
    down_bias,
    cotangent,
    *,
    ndp,
    nmp,
):
    me, z = lax.axis_index("dp"), lax.axis_index("mp")
    core = me % 2
    at_mp = z.astype(jnp.int32)[None]
    length, model = tokens.shape[0] * nmp, tokens.shape[1]
    block = min(512, length)
    width, hidden = qkv_weight.shape[2] // 2, up_weight.shape[1] // 2
    chip_steps = len(chip_bits(ndp))
    rank = lambda array, axis, which, size: lax.dynamic_slice_in_dim(
        array, which * size, size, axis
    )

    def row_pack(which):
        qkv = rank(qkv_weight, 2, which, width)
        return jnp.concatenate([qkv[0], qkv[1], qkv[2], rank(up_weight, 1, which, hidden)], axis=1)

    def column_pack(which):
        return jnp.concatenate(
            [rank(dense_weight, 0, which, width), rank(down_weight, 0, which, hidden)], axis=0
        )

    rows = BlockGather(row_pack(core), across(row_pack(1 - core), 1, ndp), ndp)
    columns = BlockGather(column_pack(core), across(column_pack(1 - core), 1, ndp), ndp)
    own = gather_near(tokens, nmp)
    rows.first()
    keys, moved = sorted(rows.held), [k for k in own if k]
    fenced = fence(
        [rows.held[j] for j in keys] + [own[k][0] for k in moved] + [cotangent],
        columns.held.values(),
    )
    rows.held = dict(zip(keys, fenced))
    own.update({k: [array] for k, array in zip(moved, fenced[len(keys) :])})
    cot = fenced[-1]
    other = {k: [across(own[k][0], 1, ndp)] for k in own}
    rows.second()
    own = gather_far(own, nmp)
    far = own.get(2, []) if nmp == 4 else []
    cot, *held = fence([cot, columns.held[0], columns.held[1]], [*far, *rows.blocks()])
    columns.held = dict(enumerate(held))
    if far:
        other[2] = [across(array, 1, ndp) for array in far]

    tables = rotary_tables(length)
    bias = jnp.concatenate(
        [
            rank(qkv_bias, 1, core, width).astype(F32).reshape(1, 3 * width),
            rank(up_bias[None, :], 1, core, hidden).astype(F32),
        ],
        axis=1,
    )
    gain, shift = norm_gain.astype(F32)[None, :], norm_bias.astype(F32)[None, :]
    dy_own = gather_near(cot, nmp)
    columns.first()
    qkv, act, slope, normed, token_rows = project(
        at_mp, (own, other), rows.blocks(), bias, gain, shift, tables, width, nmp, [cot]
    )
    columns.fenced([qkv])
    columns.second()
    mixed, lse = attend(qkv, length, block, [columns.held[0]])
    moved = [k for k in dy_own if k]
    dy_own.update(
        {k: [a] for k, a in zip(moved, fence([dy_own[k][0] for k in moved], [mixed]))}
    )
    dy_other = {k: [across(dy_own[k][0], 1, ndp)] for k in dy_own}
    dy_far = gather_far(dy_own, nmp)
    if nmp == 4:
        dy_other[2] = [across(array, 1, ndp) for array in dy_far[2]]
    places = list(range(nmp))
    other_sums, own_sums = branch_sums(
        at_mp, mixed, act, columns.blocks(), nmp, places, [dy_own[1][0]]
    )
    came = across(other_sums, 1, ndp)
    branches = LineScatter([[own_sums[k], came[k]] for k in range(nmp)])

    near = lambda chunks: {k: chunks[k] for k in (0, 1, nmp - 1)}
    first = grad_in(
        at_mp,
        (near(dy_own), near(dy_other)),
        slope,
        columns.blocks(),
        width,
        nmp,
        (0, 1),
        (),
        [other_sums],
    )
    second = grad_in(
        at_mp,
        (dy_far, dy_other),
        slope,
        columns.blocks(),
        width,
        nmp,
        tuple(range(2, nmp)),
        first[:3],
        branches.far_ready(),
    )
    branches.far()
    gmixed, gpre, dy = second[:3]
    column_grads = BlockScatter(
        weight_grads(me, [mixed, act], [dy], ndp, [second[3]], left=False), ndp
    )
    column_grads.step(0)
    gq, gk, gv, qkv_sums = attend_back(
        qkv,
        gmixed,
        mixed,
        lse,
        tables,
        length,
        block,
        [column_grads.held[0][0][0], *branches.near_ready()],
    )
    branches.near()
    for s in range(1, chip_steps - 1):
        column_grads.step(s)
    early = [2] if nmp == 4 else places[: nmp // 2]
    late = [k for k in places if k not in early]
    grads_a = grad_normed_sums(
        at_mp,
        (gq, gk, gv),
        gpre,
        token_rows,
        rows.blocks(),
        nmp,
        early,
        column_grads.ready(chip_steps - 1),
    )
    column_grads.step(chip_steps - 1)
    came_a = across(grads_a[0], 1, ndp)
    grads_b = grad_normed_sums(
        at_mp, (gq, gk, gv), gpre, token_rows, rows.blocks(), nmp, late, [grads_a[2]]
    )
    came_b = across(grads_b[0], 1, ndp)
    shares = {}
    for part, got, kept in ((early, came_a, grads_a[1]), (late, came_b, grads_b[1])):
        for n, k in enumerate(part):
            shares[k] = [kept[n], got[n]]
    grad_rows = LineScatter([shares[k] for k in places])
    up_grads = BlockScatter(
        weight_grads(
            me, [normed], [gpre], ndp, [grads_b[2], *grad_rows.far_ready()], left=True
        ),
        ndp,
    )
    grad_rows.far()
    up_grads.step(0)
    qkv_grads = BlockScatter(
        weight_grads(me, [normed], [gq, gk, gv], ndp, [up_grads.held[0][0][0]], left=True), ndp
    )
    grad_rows.near()
    for s in range(1, chip_steps):
        up_grads.step(s)
    for s in range(chip_steps):
        qkv_grads.step(s)

    local_inputs = tokens.astype(F32)
    output = (
        local_inputs
        + branches.result()
        + (dense_bias.astype(F32) + down_bias.astype(F32))[None, :]
    ).astype(BF16)

    pairs = width // LANES
    qkv_sum = (
        qkv_sums.reshape(2, pairs, 8, LANES).sum(0)[:, :3, :].transpose(1, 0, 2).reshape(3 * width)
    )
    small = jnp.concatenate(
        [
            qkv_sum,
            first[3][0] + second[3][0],
            (grads_a[2][:2] + grads_b[2][:2]).reshape(2 * model),
            first[4][0] + second[4][0],
        ]
    )
    for bit in chip_bits(ndp):
        small = small + across(small, bit, ndp)
    inner = 3 * width + hidden
    here, grad_out_bias = small[: inner + 2 * model], small[inner + 2 * model :]
    there = across(here, 1, ndp)
    norm_sums = here[inner:] + there[inner:]
    sums = [norm_sums] + [
        lax.ppermute(norm_sums, "mp", [(i, i ^ j) for i in range(nmp)]) for j in range(1, nmp)
    ]
    while len(sums) > 1:
        sums = [a + b for a, b in zip(sums[::2], sums[1::2])]
    even, odd = jnp.where(core == 0, here, there), jnp.where(core == 0, there, here)
    grad_qkv_bias = jnp.concatenate(
        [even[: 3 * width].reshape(3, width), odd[: 3 * width].reshape(3, width)], axis=1
    )
    grad_up_bias = jnp.concatenate([even[3 * width : inner], odd[3 * width : inner]])

    def both(mine, theirs, axis):
        return jnp.where(
            core == 0,
            jnp.concatenate([mine, theirs], axis=axis),
            jnp.concatenate([theirs, mine], axis=axis),
        )

    mine, theirs = column_grads.finish()
    owned_dense = both(mine[:width], theirs[:width], 0)
    owned_down = both(mine[width:], theirs[width:], 0)
    owned_up = both(*up_grads.finish(), 1)
    mine, theirs = qkv_grads.finish()
    owned_qkv = jnp.stack(
        [
            both(mine[:, c * width : (c + 1) * width], theirs[:, c * width : (c + 1) * width], 1)
            for c in range(3)
        ]
    )

    row_mean = jnp.mean(local_inputs, axis=1, keepdims=True)
    centered = local_inputs - row_mean
    row_var = jnp.mean(centered * centered, axis=1, keepdims=True)
    inverse_std = lax.rsqrt(row_var + EPS)
    normal_rows = centered * inverse_std
    scaled_grad = grad_rows.result() * gain
    first_mean = jnp.mean(scaled_grad, axis=1, keepdims=True)
    second_mean = jnp.mean(scaled_grad * normal_rows, axis=1, keepdims=True)
    grad_tokens = (
        cotangent.astype(F32)
        + (scaled_grad - first_mean - normal_rows * second_mean) * inverse_std
    ).astype(BF16)
    return (
        output,
        grad_tokens,
        sums[0][:model],
        sums[0][model:],
        owned_qkv,
        grad_qkv_bias,
        owned_dense,
        grad_out_bias,
        owned_up,
        grad_up_bias,
        owned_down,
        grad_out_bias,
    )


def solution(mesh):
    return jax.shard_map(
        functools.partial(on_device, ndp=mesh.shape["dp"], nmp=mesh.shape["mp"]),
        mesh=mesh,
        in_specs=(
            P(("dp", "mp"), None),
            P(),
            P(),
            P(None, "dp", "mp"),
            P(None, "mp"),
            P("mp", "dp"),
            P(),
            P("dp", "mp"),
            P("mp"),
            P("mp", "dp"),
            P(),
            P(("dp", "mp"), None),
        ),
        out_specs=(
            P(("dp", "mp"), None),
            P(("dp", "mp"), None),
            P(),
            P(),
            P(None, "dp", "mp"),
            P(None, "mp"),
            P("mp", "dp"),
            P(),
            P("dp", "mp"),
            P("mp"),
            P("mp", "dp"),
            P(),
        ),
        check_vma=False,
    )
```

```python
import functools

import jax
import jax.numpy as jnp
import numpy as np
from jax import lax
from jax.experimental import pallas as pl
from jax.experimental.pallas import tpu as pltpu
from jax.sharding import PartitionSpec as P

HEAD_DIM = 64
ROT = 32
EPS = 1e-05
LANES = 128
VMEM_LIMIT = 56 << 20
F32 = jnp.float32
BF16 = jnp.bfloat16
ANY = pl.BlockSpec(memory_space=pl.ANY)


def dot(lhs, rhs, lhs_dim, rhs_dim):
    return lax.dot_general(
        lhs, rhs, (((lhs_dim,), (rhs_dim,)), ((), ())), preferred_element_type=F32
    )


def call(kernel, name, operands, deps=(), scalars=(), **spec):
    deps, many, lead = tuple(deps), len(operands), len(scalars)

    def body(*refs):
        kernel(*refs[: lead + many], *refs[lead + many + len(deps) :])

    in_specs = list(spec.pop("in_specs")) + [ANY] * len(deps)
    out_shape, aliases = spec.pop("out_shape"), spec.pop("input_output_aliases", {})
    if scalars:
        grid_spec = pltpu.PrefetchScalarGridSpec(
            num_scalar_prefetch=lead, in_specs=in_specs, **spec
        )
        spec = {"grid_spec": grid_spec}
    else:
        spec["in_specs"] = in_specs
    return pl.pallas_call(
        body,
        out_shape=out_shape,
        input_output_aliases=aliases,
        compiler_params=pltpu.CompilerParams(vmem_limit_bytes=VMEM_LIMIT),
        cost_estimate=pl.CostEstimate(flops=0, transcendentals=0, bytes_accessed=0),
        name=name,
        **spec,
    )(*scalars, *operands, *deps)


def fence(values, deps=()):
    return call(
        lambda *refs: None,
        "fence",
        values,
        deps,
        in_specs=[ANY] * len(values),
        out_specs=[ANY] * len(values),
        out_shape=[jax.ShapeDtypeStruct(v.shape, v.dtype) for v in values],
        input_output_aliases={n: n for n in range(len(values))},
    )


def rotary_tables(length):
    positions = np.arange(length, dtype=np.float32)
    frequency = 10000.0 ** (-np.arange(ROT // 2, dtype=np.float64) * 2.0 / ROT)
    angles = positions[:, None] * frequency.astype(np.float32)[None, :]
    cosine, sine = np.cos(angles.astype(np.float64)), np.sin(angles.astype(np.float64))
    rest = HEAD_DIM - ROT
    none = np.zeros((length, ROT // 2))
    ones, zeros = np.ones((length, rest)), np.zeros((length, rest))
    straight = np.concatenate([cosine, cosine, ones], axis=1)
    left = np.concatenate([-sine, none, zeros], axis=1)
    right = np.concatenate([none, sine, zeros], axis=1)
    return [
        jnp.asarray(np.concatenate([t, t], axis=1).astype(np.float32))
        for t in (straight, left, right)
    ]


def rotated(u, straight, left, right, sign):
    half = ROT // 2
    turned = pltpu.roll(u, LANES - half, 1) * left + pltpu.roll(u, half, 1) * right
    return u * straight + sign * turned


def normalized(x):
    x = x.astype(F32)
    centered = x - jnp.mean(x, axis=1, keepdims=True)
    variance = jnp.mean(centered * centered, axis=1, keepdims=True)
    return centered * lax.rsqrt(variance + EPS)


def block_copies(blocks, place, sems):
    me = lax.axis_index("dp")
    return [
        pltpu.make_async_copy(block, place(lax.bitwise_xor(me, j)), sems.at[j])
        for j, block in enumerate(blocks)
    ]


def rows_at(ref, size):
    return lambda owner: ref.at[pl.ds(pl.multiple_of(owner * size, size), size)]


def columns_at(ref, size):
    return lambda owner: ref.at[:, pl.ds(pl.multiple_of(owner * size, size), size)]


def arrays_of(chunks):
    return [array for array, _ in chunks]


def shifts_of(chunks):
    return tuple(shifts for _, shifts in chunks)


def by_shift(refs, shifts):
    found = {}
    for ref, group in zip(refs, shifts):
        for n, k in enumerate(group):
            found[k] = ref if len(group) == 1 else ref.at[n]
    return found


def chunk_copies(chunks, places, parts, held, sems):
    z = lax.axis_index("mp")
    found = []
    for s, sequence in enumerate(chunks):
        for i, m in enumerate(places):
            slot, options = s * len(places) + i, []
            for k in sorted({(at - (at ^ m)) % parts for at in range(parts)}):
                here = lax.rem(z - lax.bitwise_xor(z, m) + parts, parts) == k
                options.append((here if k else None, sequence[k]))
            found.append(
                [
                    (here, pltpu.make_async_copy(source, held.at[slot], sems.at[slot]))
                    for here, source in options
                ]
            )
    return found


def start_all(found):
    for options in found:
        for here, copy in options:
            if here is None:
                copy.start()
            else:
                pl.when(here)(copy.start)


def wait_for(options):
    options[0][1].wait()


def project_kernel(setup, at_ref, bias_ref, gain_ref, shift_ref, cos_ref, left_ref, right_ref, *rest):
    count, parts, places, width, hidden, shifts = setup
    chunks = [by_shift(rest, shifts)]
    blocks = rest[len(shifts) : len(shifts) + count]
    qkv_ref, act_ref, slope_ref, normed_ref, tokens_ref, held, x_held, ready, sems, x_sems = rest[-10:]
    step, steps = pl.program_id(0), len(places)
    found = chunk_copies(chunks, places, parts, x_held, x_sems)
    loads = block_copies(blocks, rows_at(held, blocks[0].shape[0]), sems)

    def norm(slot):
        return (normalized(x_held[slot]) * gain_ref[...] + shift_ref[...]).astype(BF16)

    @pl.when(step == 0)
    def _():
        for copy in loads:
            copy.start()
        start_all(found)
        wait_for(found[0])
        ready[0] = norm(0)
        for copy in loads:
            copy.wait()

    for slot in range(1, steps):

        @pl.when(step == slot - 1)
        def _(slot=slot):
            wait_for(found[slot])

    x = ready[step % 2]
    normed_ref[...] = x
    tokens_ref[...] = x_held[step]
    ready[(step + 1) % 2] = norm((step + 1) % steps)
    root = 0.7978845608028654
    for t in range((3 * width + hidden) // width):
        columns = slice(t * width, (t + 1) * width)
        y = dot(x, held[:, columns], 1, 0) + bias_ref[:, columns]
        if t < 3:
            for g in range(width // LANES):
                part = y[:, g * LANES : (g + 1) * LANES]
                if t < 2:
                    part = rotated(part, cos_ref[...], left_ref[...], right_ref[...], 1.0)
                if t == 0:
                    part = part * HEAD_DIM**-0.5
                start = t * width + g * LANES
                qkv_ref[:, start : start + LANES] = part.astype(BF16)
        else:
            columns = slice((t - 3) * width, (t - 2) * width)
            square = y * y
            turn = jnp.tanh(root * y * (1.0 + 0.044715 * square))
            half = 0.5 * (1.0 + turn)
            act_ref[:, columns] = (y * half).astype(BF16)
            slope = half * (1.0 + y * (1.0 - turn) * (root + (3.0 * 0.044715 * root) * square))
            slope_ref[:, columns] = slope.astype(BF16)


def project(at_mp, sequence, chunks, blocks, bias, gain, shift, tables, width, parts, earlier, deps):
    places, total = tuple(range(parts)), blocks[0].shape[1]
    rows, model, count = tables[0].shape[0] // parts, gain.shape[1], len(blocks)
    hidden = total - 3 * width
    table = pl.BlockSpec((rows, LANES), lambda i, at: (at[0] ^ i, 0))
    out = lambda w: pl.BlockSpec((rows, w), lambda i, at: (sequence * parts + (at[0] ^ i), 0))
    line = lambda a: pl.BlockSpec(a.shape, lambda i, at: (0, 0))
    widths = (3 * width, hidden, hidden, model, model)
    setup = (count, parts, places, width, hidden, shifts_of(chunks))
    operands = [bias, gain, shift, *tables, *arrays_of(chunks), *blocks]
    return call(
        functools.partial(project_kernel, setup),
        "project",
        operands + list(earlier),
        deps,
        (at_mp,),
        grid=(parts,),
        in_specs=[line(bias), line(gain), line(shift), table, table, table]
        + [ANY] * (len(chunks) + count + len(earlier)),
        out_specs=[out(w) for w in widths],
        out_shape=[jax.ShapeDtypeStruct((2 * parts * rows, w), BF16) for w in widths],
        input_output_aliases={1 + len(operands) + n: n for n in range(len(earlier))},
        scratch_shapes=[
            pltpu.VMEM((model, total), BF16),
            pltpu.VMEM((parts, rows, model), BF16),
            pltpu.VMEM((2, rows, model), BF16),
            pltpu.SemaphoreType.DMA((count,)),
            pltpu.SemaphoreType.DMA((parts,)),
        ],
    )


def attend_kernel(block, q_ref, k_ref, v_ref, out_ref, lse_ref):
    length = q_ref.shape[0]
    lane = lax.broadcasted_iota(jnp.int32, (1, LANES), 1)
    key = lax.broadcasted_iota(jnp.int32, (block, block), 0)
    causal = key <= lax.broadcasted_iota(jnp.int32, (block, block), 1)
    for i in range(length // block):
        rows, before = pl.ds(i * block, block), pl.ds(0, i * block)
        results = []
        for h in range(2):
            mine = (lane < HEAD_DIM) if h == 0 else (lane >= HEAD_DIM)
            query = jnp.where(mine, q_ref[rows, :], 0)
            near = jnp.where(causal, dot(k_ref[rows, :], query, 1, 1), -1e30)
            highest = jnp.max(near, axis=0, keepdims=True)
            if i:
                far = dot(k_ref[before, :], query, 1, 1)
                highest = jnp.maximum(highest, jnp.max(far, axis=0, keepdims=True))
            near = jnp.exp(near - highest)
            total = jnp.sum(near, axis=0, keepdims=True)
            if i:
                far = jnp.exp(far - highest)
                total = total + jnp.sum(far, axis=0, keepdims=True)
            inverse = 1.0 / total
            result = dot((near * inverse).astype(BF16), v_ref[rows, :], 0, 0)
            if i:
                result = result + dot((far * inverse).astype(BF16), v_ref[before, :], 0, 0)
            results.append(result)
            lse_ref[0, h : h + 1, rows] = highest + jnp.log(total)
        out_ref[rows, :] = jnp.where(lane < HEAD_DIM, results[0], results[1]).astype(BF16)


def pair_specs(length, pairs):
    return lambda off: pl.BlockSpec(
        (length, LANES), lambda g: (g // pairs, off * pairs + g % pairs)
    )


def attend(qkv, length, block, deps):
    width, sequences = qkv.shape[1] // 3, qkv.shape[0] // length
    pairs = width // LANES
    at = pair_specs(length, pairs)
    return call(
        functools.partial(attend_kernel, block),
        "attend",
        [qkv, qkv, qkv],
        deps,
        grid=(sequences * pairs,),
        in_specs=[at(0), at(1), at(2)],
        out_specs=[at(0), pl.BlockSpec((1, 8, length), lambda g: (g, 0, 0))],
        out_shape=[
            jax.ShapeDtypeStruct((qkv.shape[0], width), BF16),
            jax.ShapeDtypeStruct((sequences * pairs, 8, length), F32),
        ],
    )


def attend_back_kernel(
    block,
    q_ref,
    k_ref,
    v_ref,
    grad_ref,
    mixed_ref,
    lse_ref,
    cos_ref,
    left_ref,
    right_ref,
    gq_ref,
    gk_ref,
    gv_ref,
    sum_ref,
    gk_sum,
    gv_sum,
):
    length = q_ref.shape[0]
    lane = lax.broadcasted_iota(jnp.int32, (1, LANES), 1)
    key = lax.broadcasted_iota(jnp.int32, (block, block), 0)
    causal = key <= lax.broadcasted_iota(jnp.int32, (block, block), 1)
    count = length // block
    sum_ref[...] = jnp.zeros_like(sum_ref)

    def put(ref, which, rows, value):
        value = value.astype(BF16)
        ref[rows, :] = value
        sum_ref[0, which : which + 1, :] += jnp.sum(value.astype(F32), axis=0, keepdims=True)

    def unrotated(value, rows):
        return rotated(value, cos_ref[rows, :], left_ref[rows, :], right_ref[rows, :], -1.0)

    for i in reversed(range(count)):
        rows = pl.ds(i * block, block)
        product = grad_ref[rows, :].astype(F32) * mixed_ref[rows, :].astype(F32)
        gq = None
        for h in range(2):
            mine = (lane < HEAD_DIM) if h == 0 else (lane >= HEAD_DIM)
            query = jnp.where(mine, q_ref[rows, :], 0)
            grad = jnp.where(mine, grad_ref[rows, :], 0)
            ones = jnp.where(mine, jnp.ones((8, LANES), F32), 0.0)
            delta = lax.dot_general(
                ones,
                product,
                (((1,), (1,)), ((), ())),
                precision=lax.Precision.HIGHEST,
                preferred_element_type=F32,
            )[0:1, :]
            lse = lse_ref[0, h : h + 1, rows]
            for j in range(i + 1):
                keys = pl.ds(j * block, block)
                key_rows = k_ref[keys, :]
                probs = jnp.exp(dot(key_rows, query, 1, 1) - lse)
                if j == i:
                    probs = jnp.where(causal, probs, 0.0)
                gprobs = dot(v_ref[keys, :], grad, 1, 1)
                gscores = (probs * (gprobs - delta)).astype(BF16)
                gv, gk = dot(probs.astype(BF16), grad, 1, 0), dot(gscores, query, 1, 0)
                if i == count - 1 and h == 0:
                    gv_sum[keys, :] = gv
                    gk_sum[keys, :] = gk
                else:
                    gv_sum[keys, :] += gv
                    gk_sum[keys, :] += gk
                part = dot(gscores, jnp.where(mine, key_rows, 0), 0, 0)
                gq = part if gq is None else gq + part
        put(gq_ref, 0, rows, unrotated(gq * HEAD_DIM**-0.5, rows))
    for i in range(count):
        rows = pl.ds(i * block, block)
        put(gk_ref, 1, rows, unrotated(gk_sum[rows, :], rows))
        put(gv_ref, 2, rows, gv_sum[rows, :])


def attend_back(qkv, grad, mixed, lse, tables, length, block, deps):
    width, sequences = qkv.shape[1] // 3, qkv.shape[0] // length
    pairs = width // LANES
    at = pair_specs(length, pairs)
    table = pl.BlockSpec((length, LANES), lambda g: (0, 0))
    small = pl.BlockSpec((1, 8, length), lambda g: (g, 0, 0))
    return call(
        functools.partial(attend_back_kernel, block),
        "attend_back",
        [qkv, qkv, qkv, grad, mixed, lse, *tables],
        deps,
        grid=(sequences * pairs,),
        in_specs=[at(0), at(1), at(2), at(0), at(0), small, table, table, table],
        out_specs=[at(0)] * 3 + [pl.BlockSpec((1, 8, LANES), lambda g: (g, 0, 0))],
        out_shape=[jax.ShapeDtypeStruct((qkv.shape[0], width), BF16)] * 3
        + [jax.ShapeDtypeStruct((sequences * pairs, 8, LANES), F32)],
        scratch_shapes=[pltpu.VMEM((length, LANES), F32)] * 2,
    )


def quarter_map(places, parts):
    turns = len(places)

    def rows_of(i, at):
        offset = jnp.int32(places[0])
        for n in range(1, turns):
            offset = jnp.where(i % turns == n, places[n], offset)
        return jnp.where(i < turns, parts, 0) + (at[0] + offset) % parts

    return rows_of


def split_outputs(step, turns, result, other_ref, own_ref):
    @pl.when(step < turns)
    def _():
        other_ref[0] = result

    @pl.when(step >= turns)
    def _():
        own_ref[0] = result


def split_specs(rows, model, turns):
    return [
        pl.BlockSpec((1, rows, model), lambda i, at: (jnp.minimum(i, turns - 1), 0, 0)),
        pl.BlockSpec((1, rows, model), lambda i, at: (jnp.maximum(i - turns, 0), 0, 0)),
    ]


def branch_kernel(count, turns, at_ref, mixed_ref, act_ref, *rest):
    blocks, (other_ref, own_ref, held, sems) = rest[:count], rest[count:]
    step = pl.program_id(0)

    @pl.when(step == 0)
    def _():
        loads = block_copies(blocks, columns_at(held, blocks[0].shape[1]), sems)
        for copy in loads:
            copy.start()
        for copy in loads:
            copy.wait()

    x = jnp.concatenate([mixed_ref[...], act_ref[...]], axis=1)
    split_outputs(step, turns, dot(x, held[...], 1, 0).astype(BF16), other_ref, own_ref)


def branch_sums(at_mp, mixed, act, blocks, parts, places, deps):
    rows, count, turns = mixed.shape[0] // (2 * parts), len(blocks), len(places)
    inner, model = blocks[0].shape[0], count * blocks[0].shape[1]
    where = quarter_map(places, parts)
    return call(
        functools.partial(branch_kernel, count, turns),
        "branch_sums",
        [mixed, act, *blocks],
        deps,
        (at_mp,),
        grid=(2 * turns,),
        in_specs=[
            pl.BlockSpec((rows, a.shape[1]), lambda i, at: (where(i, at), 0)) for a in (mixed, act)
        ]
        + [ANY] * count,
        out_specs=split_specs(rows, model, turns),
        out_shape=[jax.ShapeDtypeStruct((turns, rows, model), BF16)] * 2,
        scratch_shapes=[pltpu.VMEM((inner, model), BF16), pltpu.SemaphoreType.DMA((count,))],
    )


def grad_in_kernel(setup, at_ref, slope_ref, *rest):
    count, parts, places, width, hidden, groups = setup
    chunks, many = [], 0
    for shifts in groups:
        chunks.append(by_shift(rest[many:], shifts))
        many += len(shifts)
    blocks = rest[many : many + count]
    gmixed_ref, gpre_ref, dy_ref, gsum_ref, dsum_ref, held, dy_held, sems, dy_sems = rest[-9:]
    step, steps = pl.program_id(0), 2 * len(places)
    found = chunk_copies(chunks, places, parts, dy_held, dy_sems)
    loads = block_copies(blocks, columns_at(held, blocks[0].shape[1]), sems)

    @pl.when(step == 0)
    def _():
        for copy in loads:
            copy.start()
        start_all(found)
        gsum_ref[...] = jnp.zeros_like(gsum_ref)
        dsum_ref[...] = jnp.zeros_like(dsum_ref)
        for copy in loads:
            copy.wait()

    for slot in range(steps):

        @pl.when(step == slot)
        def _(slot=slot):
            wait_for(found[slot])

    dy = dy_held[step]
    dy_ref[...] = dy
    gmixed_ref[...] = dot(dy, held[:width, :], 1, 1).astype(BF16)
    for start in range(0, hidden, width):
        part = slice(start, start + width)
        gact = dot(dy, held[width + start : 2 * width + start, :], 1, 1)
        gpre = (gact * slope_ref[:, part].astype(F32)).astype(BF16)
        gpre_ref[:, part] = gpre
        gsum_ref[0:1, part] += jnp.sum(gpre.astype(F32), axis=0, keepdims=True)
    dsum_ref[0:1, :] += jnp.sum(dy.astype(F32), axis=0, keepdims=True)


def grad_in(at_mp, chunks, slope, blocks, width, parts, places, earlier, deps):
    model = len(blocks) * blocks[0].shape[1]
    hidden, length = slope.shape[1], slope.shape[0]
    rows, count, many = length // (2 * parts), len(blocks), sum(len(c) for c in chunks)
    turns = len(places)

    def where(i, at):
        m = jnp.int32(places[0])
        for n in range(1, turns):
            m = jnp.where(i % turns == n, places[n], m)
        return i // turns * parts + (at[0] ^ m)

    out = lambda w: pl.BlockSpec((rows, w), lambda i, at: (where(i, at), 0))
    total = lambda w: pl.BlockSpec((8, w), lambda i, at: (0, 0))
    setup = (count, parts, places, width, hidden, [shifts_of(c) for c in chunks])
    operands = [slope, *arrays_of(chunks[0]), *arrays_of(chunks[1]), *blocks]
    aliases = {1 + len(operands) + n: n for n in range(len(earlier))}
    return call(
        functools.partial(grad_in_kernel, setup),
        "grad_in",
        operands + list(earlier),
        deps,
        (at_mp,),
        grid=(2 * turns,),
        in_specs=[out(hidden)] + [ANY] * (many + count + len(earlier)),
        out_specs=[out(width), out(hidden), out(model), total(hidden), total(model)],
        out_shape=[jax.ShapeDtypeStruct((length, w), BF16) for w in (width, hidden, model)]
        + [jax.ShapeDtypeStruct((8, w), F32) for w in (hidden, model)],
        input_output_aliases=aliases,
        scratch_shapes=[
            pltpu.VMEM((width + hidden, model), BF16),
            pltpu.VMEM((2 * turns, rows, model), BF16),
            pltpu.SemaphoreType.DMA((count,)),
            pltpu.SemaphoreType.DMA((2 * turns,)),
        ],
    )


def grad_normed_kernel(
    count, turns, at_ref, gq_ref, gk_ref, gv_ref, gpre_ref, tokens_ref, *rest
):
    blocks, (other_ref, own_ref, sum_ref, held, sems) = rest[:count], rest[count:]
    step = pl.program_id(0)

    @pl.when(step == 0)
    def _():
        loads = block_copies(blocks, rows_at(held, blocks[0].shape[0]), sems)
        for copy in loads:
            copy.start()
        sum_ref[...] = jnp.zeros_like(sum_ref)
        for copy in loads:
            copy.wait()

    g = jnp.concatenate([gq_ref[...], gk_ref[...], gv_ref[...], gpre_ref[...]], axis=1)
    result = dot(g, held[...], 1, 1)
    sum_ref[0:1, :] += jnp.sum(result * normalized(tokens_ref[...]), axis=0, keepdims=True)
    sum_ref[1:2, :] += jnp.sum(result, axis=0, keepdims=True)
    split_outputs(step, turns, result.astype(BF16), other_ref, own_ref)


def grad_normed_sums(at_mp, gqkv, gpre, tokens, blocks, parts, places, deps):
    rows, count, turns = tokens.shape[0] // (2 * parts), len(blocks), len(places)
    model, total = tokens.shape[1], blocks[0].shape[1]
    where = quarter_map(places, parts)
    operands = [*gqkv, gpre, tokens]
    return call(
        functools.partial(grad_normed_kernel, count, turns),
        "grad_normed_sums",
        operands + list(blocks),
        deps,
        (at_mp,),
        grid=(2 * turns,),
        in_specs=[
            pl.BlockSpec((rows, a.shape[1]), lambda i, at: (where(i, at), 0)) for a in operands
        ]
        + [ANY] * count,
        out_specs=split_specs(rows, model, turns)
        + [pl.BlockSpec((8, model), lambda i, at: (0, 0))],
        out_shape=[jax.ShapeDtypeStruct((turns, rows, model), BF16)] * 2
        + [jax.ShapeDtypeStruct((8, model), F32)],
        scratch_shapes=[pltpu.VMEM((model, total), BF16), pltpu.SemaphoreType.DMA((count,))],
    )


def weight_grad_kernel(sizes, left, at_ref, *refs):
    ins, outs = refs[: len(refs) - len(sizes)], refs[len(refs) - len(sizes) :]
    if left:
        grad = jnp.concatenate([dot(ins[0][...], g[...], 0, 0) for g in ins[1:]], axis=1)
    else:
        grad = jnp.concatenate([dot(x[...], ins[-1][...], 0, 0) for x in ins[:-1]], axis=0)
    grad = grad.astype(BF16)
    first = 0
    for size, out_ref in zip(sizes, outs):

        @pl.when((pl.program_id(0) >= first) & (pl.program_id(0) < first + size))
        def _(out_ref=out_ref):
            out_ref[0] = grad

        first += size


def weight_grads(me, xs, gs, count, deps, left):
    plan = scatter_plan(count)
    sets = [(half, s) for s in range(len(plan[0])) for half in range(2)]
    sizes = [len(plan[half][s]) for half, s in sets]
    order = [j for half, s in sets for j in plan[half][s]]
    owners = lax.bitwise_xor(me, jnp.array(order, jnp.int32))
    length, (cut, whole) = xs[0].shape[0], ((xs, gs) if left else (gs, xs))
    size = cut[0].shape[1] // count
    cut_spec = pl.BlockSpec((length, size), lambda i, at: (0, at[i]))
    whole_specs = [pl.BlockSpec(a.shape, lambda i, at: (0, 0)) for a in whole]
    full = sum(a.shape[1] for a in whole)
    shape = (size, full) if left else (full, size)

    def out(first, many):
        return pl.BlockSpec(
            (1, *shape), lambda i, at: (jnp.clip(i - first, 0, many - 1), 0, 0)
        )

    firsts = [sum(sizes[:n]) for n in range(len(sizes))]
    outs = call(
        functools.partial(weight_grad_kernel, sizes, left),
        "weight_grads",
        [*xs, *gs],
        deps,
        (owners,),
        grid=(count,),
        in_specs=[cut_spec] + whole_specs if left else whole_specs + [cut_spec],
        out_specs=[out(first, many) for first, many in zip(firsts, sizes)],
        out_shape=[jax.ShapeDtypeStruct((many, *shape), BF16) for many in sizes],
    )
    return [[o for o, (half, _) in zip(outs, sets) if half == h] for h in range(2)]


def across(value, bit, count):
    return lax.ppermute(value, "dp", [(i, i ^ bit) for i in range(count)])


def ring(value, k, parts):
    return lax.ppermute(value, "mp", [(i, (i + k) % parts) for i in range(parts)])


def near_shifts(parts):
    return (1, 3) if parts == 4 else tuple(range(1, parts))


def gather_far(chunks, parts):
    if parts != 4:
        return None
    up = lax.ppermute(chunks[1], "mp", [(1, 2), (2, 3)])
    down = lax.ppermute(chunks[3], "mp", [(1, 0), (2, 1)])
    return up + down


def added(addends):
    return sum(a.astype(F32) for a in addends).astype(BF16)


def send_far(farthest):
    up = lax.ppermute(farthest, "mp", [(0, 1), (1, 2)])
    down = lax.ppermute(farthest, "mp", [(3, 2), (2, 1)])
    return [up, down]


def chip_bits(count):
    bits, bit = [], 2
    while bit < count:
        bits.append(bit)
        bit *= 2
    return bits


class BlockGather:
    def __init__(self, own, sibling, count):
        self.held, self.count = {0: own, 1: sibling}, count
        self.orders = (chip_bits(count), chip_bits(count)[::-1])

    def own_to(self, s):
        if s < len(self.orders[0]):
            for half in range(2):
                bit = self.orders[half][s]
                self.held[half ^ bit] = across(self.held[half], bit, self.count)

    def rest(self):
        for s in range(1, len(self.orders[0])):
            for half in range(2):
                order = self.orders[half]
                for j in [j for j in self.held if j % 2 == half]:
                    if j ^ order[s] not in self.held and not any(j & b for b in order[s:]):
                        self.held[j ^ order[s]] = across(self.held[j], order[s], self.count)

    def fenced(self, others=(), deps=()):
        keys = sorted(self.held)
        values = fence([self.held[j] for j in keys] + list(others), deps)
        self.held = dict(zip(keys, values))
        return values[len(keys) :]

    def blocks(self):
        return [self.held[j] for j in range(self.count)]


def scatter_orders(count):
    return (chip_bits(count)[::-1], chip_bits(count))


def scatter_plan(count):
    plan = []
    for half, order in enumerate(scatter_orders(count)):
        sets, rest = [[half]], [half]
        for bit in reversed(order):
            sets.insert(0, [j ^ bit for j in rest])
            rest = sets[0] + rest
        plan.append(sets)
    return plan


class BlockScatter:
    def __init__(self, halves, count):
        self.count, self.orders = count, scatter_orders(count)
        self.held = [[[a] for a in arrays] for arrays in halves]
        self.steps = len(self.orders[0])

    def total(self, half, s):
        if len(self.held[half][s]) > 1:
            self.held[half][s] = [added(self.held[half][s])]
        return self.held[half][s][0]

    def ready(self, s):
        return [self.total(half, s) for half in range(2)]

    def send(self, s):
        return [across(self.total(h, s), self.orders[h][s], self.count) for h in range(2)]

    def arrive(self, s, came):
        for half in range(2):
            first = 0
            for later in self.held[half][s + 1 :]:
                many = later[0].shape[0]
                later.append(came[half][first : first + many])
                first += many

    def between(self):
        for s in range(1, self.steps - 1):
            self.arrive(s, self.send(s))

    def last(self):
        return self.total(1, -1)[0]

    def finish(self, theirs):
        return sum(a[0].astype(F32) for a in self.held[0][-1]), theirs.astype(F32)


def on_device(
    tokens,
    norm_gain,
    norm_bias,
    qkv_weight,
    qkv_bias,
    dense_weight,
    dense_bias,
    up_weight,
    up_bias,
    down_weight,
    down_bias,
    cotangent,
    *,
    ndp,
    nmp,
):
    me, z = lax.axis_index("dp"), lax.axis_index("mp")
    core = me % 2
    at_mp = z.astype(jnp.int32)[None]
    length, model = tokens.shape[0] * nmp, tokens.shape[1]
    block = min(512, length)
    width, hidden = qkv_weight.shape[2] // 2, up_weight.shape[1] // 2
    chip_steps = len(chip_bits(ndp))
    rank = lambda array, axis, which, size: lax.dynamic_slice_in_dim(
        array, which * size, size, axis
    )

    def row_pack(which):
        qkv = rank(qkv_weight, 2, which, width)
        return jnp.concatenate([qkv[0], qkv[1], qkv[2], rank(up_weight, 1, which, hidden)], axis=1)

    def column_pack(which):
        return jnp.concatenate(
            [rank(dense_weight, 0, which, width), rank(down_weight, 0, which, hidden)], axis=0
        )

    def stage(*arrays):
        return jnp.stack(arrays), tuple([0, *near])

    near, places, pairs = near_shifts(nmp), list(range(nmp)), width // LANES
    rows = BlockGather(row_pack(core), across(row_pack(1 - core), 1, ndp), ndp)
    columns = BlockGather(column_pack(core), across(column_pack(1 - core), 1, ndp), ndp)
    head, tail = near[0], near[1:]
    came = {head: ring(tokens, head, nmp)}
    rows.own_to(0)
    came[head], begun = rows.fenced([came[head], tokens], columns.held.values())
    came.update({k: ring(begun, k, nmp) for k in tail})
    rows.own_to(1)
    *held, cot = rows.fenced([*came.values(), cotangent])
    came = dict(zip(near, held))
    own = [(tokens, (0,))] + [(came[k], (k,)) for k in near]
    packed, shifts = stage(tokens, *held)
    other = [(across(packed, 1, ndp), shifts)]
    far = gather_far(came, nmp)
    rows.rest()
    cot, *held = rows.fenced(
        [cot, columns.held[0], columns.held[1]] + ([far] if nmp == 4 else []), [other[0][0]]
    )
    columns.held = dict(enumerate(held[:2]))
    if nmp == 4:
        own.append((held[2], (2,)))
        other.append((across(held[2], 1, ndp), (2,)))

    tables = rotary_tables(length)
    bias = jnp.concatenate(
        [
            rank(qkv_bias, 1, core, width).astype(F32).reshape(1, 3 * width),
            rank(up_bias[None, :], 1, core, hidden).astype(F32),
        ],
        axis=1,
    )
    gain, shift = norm_gain.astype(F32)[None, :], norm_bias.astype(F32)[None, :]
    came = {head: ring(cot, head, nmp)}
    columns.own_to(0)
    common = (rows.blocks(), bias, gain, shift, tables, width, nmp)
    first = project(at_mp, 0, own, *common, (), [cot])
    cot, came[head] = columns.fenced([cot, came[head]], [first[0]])
    came.update({k: ring(cot, k, nmp) for k in tail})
    columns.own_to(1)
    qkv, act, slope, normed, token_rows = project(
        at_mp, 1, other, *common, first, [columns.held[0]]
    )
    columns.fenced(deps=[qkv])
    columns.rest()
    mixed, lse = attend(qkv, length, block, [columns.held[0]])
    held = columns.fenced(came.values(), [mixed])
    came = dict(zip(near, held))
    dy_own = [(cot, (0,))] + [(came[k], (k,)) for k in near]
    packed, shifts = stage(cot, *held)
    dy_packed = across(packed, 1, ndp)
    far = gather_far(came, nmp)
    other_sums, own_sums = branch_sums(
        at_mp, mixed, act, columns.blocks(), nmp, places, [packed]
    )
    dy_packed, other_sums, *far = fence(
        [dy_packed, other_sums] + ([far] if nmp == 4 else []), [own_sums]
    )
    theirs = across(other_sums, 1, ndp)

    dy_other = [(dy_packed, shifts)]
    grad_a = grad_in(
        at_mp, (dy_own, dy_other), slope, columns.blocks(), width, nmp, (0, 1), (), [other_sums]
    )
    far_other = [across(a, 1, ndp) for a in far]
    theirs, *far_other = fence([theirs, *far_other], [grad_a[3]])
    shares = [[own_sums[k], theirs[k]] for k in places]
    farthest = [added(shares[2])] if nmp == 4 else []
    moved = [a for f in farthest for a in send_far(f)]
    grad_b = grad_in(
        at_mp,
        (dy_own + [(a, (2,)) for a in far], dy_other + [(a, (2,)) for a in far_other]),
        slope,
        columns.blocks(),
        width,
        nmp,
        tuple(places[2:]),
        grad_a[:3],
        [grad_a[3], *farthest],
    )
    gmixed, gpre, dy = grad_b[:3]
    column_grads = BlockScatter(
        weight_grads(me, [mixed, act], [dy], ndp, [grad_b[3]], left=False), ndp
    )

    def with_far(shares, moved):
        if moved:
            shares[1], shares[3] = shares[1] + [moved[0]], shares[3] + [moved[1]]
        return {k: added(shares[k]) for k in near}

    if moved:
        moved = fence(moved, [column_grads.held[0][0][0]])
    sums = with_far(shares, moved)
    brought = [ring(sums[head], head, nmp)]
    column_came = column_grads.send(0)
    gq, gk, gv, qkv_sums = attend_back(
        qkv,
        gmixed,
        mixed,
        lse,
        tables,
        length,
        block,
        [column_grads.held[0][0][0], *sums.values()],
    )
    brought[0], *held = fence([brought[0], *(sums[k] for k in tail)], [gq])
    brought += [ring(a, k, nmp) for k, a in zip(tail, held)]

    def normed_part(part, deps):
        return grad_normed_sums(
            at_mp, (gq, gk, gv), gpre, token_rows, rows.blocks(), nmp, part, deps
        )

    thirds = ([2], [1, 3], [0]) if nmp == 4 else (places[1:2], places[2:], places[:1])
    other_a, own_a, sums_a = normed_part(thirds[0], [brought[0]])
    *column_came, other_a = fence([*column_came, other_a], [sums_a])
    column_grads.arrive(0, column_came)
    column_grads.between()
    column_came = column_grads.send(-1 + chip_steps)
    most = other_a.shape[1] // 2
    came_a = [across(p, 1, ndp) for p in (other_a[:, :most], other_a[:, most:])]
    other_b, own_b, sums_b = normed_part(
        thirds[1], [sums_a, *column_grads.ready(chip_steps - 1)]
    )
    brought[1:] = fence(brought[1:], [sums_b])
    c0, c1, a0, a1, other_b = fence([*column_came, *came_a, other_b], [brought[1]])
    column_grads.arrive(chip_steps - 1, [c0, c1])
    came_a = jnp.concatenate([a0, a1], axis=1)
    came_b = across(other_b, 1, ndp)
    shares = [[] for _ in places]
    for part, kept, got in ((thirds[0], own_a, came_a),):
        for n, k in enumerate(part):
            shares[k] = [kept[n], got[n]]
    farthest = [added(shares[2])] if nmp == 4 else []
    moved = [a for f in farthest for a in send_far(f)]
    up_grads = BlockScatter(
        weight_grads(
            me, [normed], [gpre], ndp, [sums_b, *farthest, column_grads.last()], left=True
        ),
        ndp,
    )
    up_came = up_grads.send(0)
    other_c, own_c, sums_c = normed_part(thirds[2], [up_grads.held[0][0][0]])
    qkv_sum = (
        qkv_sums.reshape(2, pairs, 8, LANES).sum(0)[:, :3, :].transpose(1, 0, 2).reshape(3 * width)
    )
    norm_sums = (sums_a + sums_b + sums_c)[:2].reshape(2 * model)
    small = jnp.concatenate(
        [norm_sums, qkv_sum, grad_a[3][0] + grad_b[3][0], grad_a[4][0] + grad_b[4][0]]
    )
    came_b, other_c, column_last, small, *moved = fence(
        [came_b, other_c, column_grads.last(), small, *moved], [sums_c]
    )
    for n, k in enumerate(thirds[1]):
        shares[k] = [own_b[n], came_b[n]]
    sums = with_far(shares, moved)
    came = {head: ring(sums[head], head, nmp)}
    column_theirs = across(column_last, 1, ndp)
    small = lax.all_gather(small, "dp")
    qkv_grads = BlockScatter(
        weight_grads(me, [normed], [gq, gk, gv], ndp, [sums_c, *sums.values()], left=True), ndp
    )
    *up_came, q0, q1, column_theirs, small = fence(
        [*up_came, qkv_grads.held[0][0][0], qkv_grads.held[1][0][0], column_theirs, small]
    )
    qkv_grads.held[0][0], qkv_grads.held[1][0] = [q0], [q1]
    up_grads.arrive(0, up_came)
    up_grads.between()
    up_came = up_grads.send(chip_steps - 1)
    qkv_came = qkv_grads.send(0)
    small = small.reshape(ndp // 2, 2, -1).sum(axis=0)
    norm_sums, small = small[:, : 2 * model].sum(axis=0), small[:, 2 * model :]
    came[head], other_c, norm_sums, *held = fence(
        [came[head], other_c, norm_sums, *(sums[k] for k in tail)], [q0]
    )
    half = held[0].shape[0] // 2
    early = [ring(a[:half], k, nmp) for k, a in zip(tail, held)]
    u0, u1, *qkv_came = fence([*up_came, *qkv_came], [came[head]])
    up_grads.arrive(chip_steps - 1, [u0, u1])
    up_theirs = across(up_grads.last(), 1, ndp)
    qkv_grads.arrive(0, qkv_came)
    qkv_grads.between()
    late = fence([*early, *(a[half:] for a in held)])
    early, late = late[: len(tail)], late[len(tail) :]
    late = [ring(a, k, nmp) for k, a in zip(tail, late)]
    came.update({k: jnp.concatenate(pair) for k, *pair in zip(tail, early, late)})
    came_c = across(other_c, 1, ndp)
    qkv_grads.arrive(chip_steps - 1, qkv_grads.send(chip_steps - 1))
    qkv_theirs = across(qkv_grads.last(), 1, ndp)
    norm_sums = lax.all_gather(norm_sums, "mp").sum(axis=0)

    local_inputs = tokens.astype(F32)
    output = (
        local_inputs
        + sum(a.astype(F32) for a in [own_sums[0], theirs[0], *brought])
        + (dense_bias.astype(F32) + down_bias.astype(F32))[None, :]
    ).astype(BF16)

    def both(mine, theirs, axis):
        return jnp.where(
            core == 0,
            jnp.concatenate([mine, theirs], axis=axis),
            jnp.concatenate([theirs, mine], axis=axis),
        )

    mine, theirs = column_grads.finish(column_theirs)
    owned_dense = both(mine[:width], theirs[:width], 0)
    owned_down = both(mine[width:], theirs[width:], 0)
    owned_up = both(*up_grads.finish(up_theirs), 1)
    mine, theirs = qkv_grads.finish(qkv_theirs)
    owned_qkv = jnp.stack(
        [
            both(mine[:, c * width : (c + 1) * width], theirs[:, c * width : (c + 1) * width], 1)
            for c in range(3)
        ]
    )

    inner = 3 * width + hidden
    grad_out_bias = small[0, inner:]
    grad_qkv_bias = jnp.concatenate(
        [small[h, : 3 * width].reshape(3, width) for h in range(2)], axis=1
    )
    grad_up_bias = small[:, 3 * width : inner].reshape(2 * hidden)

    centered = local_inputs - jnp.mean(local_inputs, axis=1, keepdims=True)
    inverse_std = lax.rsqrt(jnp.mean(centered * centered, axis=1, keepdims=True) + EPS)
    normal_rows = centered * inverse_std
    grad_rows = sum(a.astype(F32) for a in [own_c[0], came_c[0], *came.values()])
    scaled = grad_rows * gain
    first_mean = jnp.mean(scaled, axis=1, keepdims=True)
    second_mean = jnp.mean(scaled * normal_rows, axis=1, keepdims=True)
    grad_tokens = (
        cotangent.astype(F32) + (scaled - first_mean - normal_rows * second_mean) * inverse_std
    ).astype(BF16)
    return (
        output,
        grad_tokens,
        norm_sums[:model],
        norm_sums[model:],
        owned_qkv,
        grad_qkv_bias,
        owned_dense,
        grad_out_bias,
        owned_up,
        grad_up_bias,
        owned_down,
        grad_out_bias,
    )


def solution(mesh):
    return jax.shard_map(
        functools.partial(on_device, ndp=mesh.shape["dp"], nmp=mesh.shape["mp"]),
        mesh=mesh,
        in_specs=(
            P(("dp", "mp"), None),
            P(),
            P(),
            P(None, "dp", "mp"),
            P(None, "mp"),
            P("mp", "dp"),
            P(),
            P("dp", "mp"),
            P("mp"),
            P("mp", "dp"),
            P(),
            P(("dp", "mp"), None),
        ),
        out_specs=(
            P(("dp", "mp"), None),
            P(("dp", "mp"), None),
            P(),
            P(),
            P(None, "dp", "mp"),
            P(None, "mp"),
            P("mp", "dp"),
            P(),
            P("dp", "mp"),
            P("mp"),
            P("mp", "dp"),
            P(),
        ),
        check_vma=False,
    )
```

```python
import functools

import jax
import jax.numpy as jnp
import numpy as np
from jax import lax
from jax.experimental import pallas as pl
from jax.experimental.pallas import tpu as pltpu
from jax.sharding import PartitionSpec as P

HEAD_DIM = 64
ROT = 32
EPS = 1e-05
LANES = 128
F32 = jnp.float32
BF16 = jnp.bfloat16
ANY = pl.BlockSpec(memory_space=pl.ANY)


def dot(lhs, rhs, lhs_dim, rhs_dim):
    return lax.dot_general(
        lhs, rhs, (((lhs_dim,), (rhs_dim,)), ((), ())), preferred_element_type=F32
    )


def call(kernel, name, operands, deps=(), scalars=(), vmem=2, **spec):
    deps, many, lead = tuple(deps), len(operands), len(scalars)

    def body(*refs):
        kernel(*refs[: lead + many], *refs[lead + many + len(deps) :])

    in_specs = list(spec.pop("in_specs")) + [ANY] * len(deps)
    out_shape, aliases = spec.pop("out_shape"), spec.pop("input_output_aliases", {})
    if scalars:
        grid_spec = pltpu.PrefetchScalarGridSpec(
            num_scalar_prefetch=lead, in_specs=in_specs, **spec
        )
        spec = {"grid_spec": grid_spec}
    else:
        spec["in_specs"] = in_specs
    return pl.pallas_call(
        body,
        out_shape=out_shape,
        input_output_aliases=aliases,
        compiler_params=pltpu.CompilerParams(vmem_limit_bytes=vmem << 20),
        cost_estimate=pl.CostEstimate(flops=0, transcendentals=0, bytes_accessed=0),
        name=name,
        **spec,
    )(*scalars, *operands, *deps)


def fence(values, deps=()):
    return call(
        lambda *refs: None,
        "fence",
        values,
        deps,
        in_specs=[ANY] * len(values),
        out_specs=[ANY] * len(values),
        out_shape=[jax.ShapeDtypeStruct(v.shape, v.dtype) for v in values],
        input_output_aliases={n: n for n in range(len(values))},
    )


def rotary_tables(length):
    positions = np.arange(length, dtype=np.float32)
    frequency = 10000.0 ** (-np.arange(ROT // 2, dtype=np.float64) * 2.0 / ROT)
    angles = positions[:, None] * frequency.astype(np.float32)[None, :]
    cosine, sine = np.cos(angles.astype(np.float64)), np.sin(angles.astype(np.float64))
    rest = HEAD_DIM - ROT
    none = np.zeros((length, ROT // 2))
    ones, zeros = np.ones((length, rest)), np.zeros((length, rest))
    straight = np.concatenate([cosine, cosine, ones], axis=1)
    left = np.concatenate([-sine, none, zeros], axis=1)
    right = np.concatenate([none, sine, zeros], axis=1)
    return [
        jnp.asarray(np.concatenate([t, t], axis=1).astype(np.float32))
        for t in (straight, left, right)
    ]


def rotated(u, straight, left, right, sign):
    half = ROT // 2
    turned = pltpu.roll(u, LANES - half, 1) * left + pltpu.roll(u, half, 1) * right
    return u * straight + sign * turned


def normalized(x):
    x = x.astype(F32)
    centered = x - jnp.mean(x, axis=1, keepdims=True)
    variance = jnp.mean(centered * centered, axis=1, keepdims=True)
    return centered * lax.rsqrt(variance + EPS)


def block_copies(blocks, place, sems):
    me = lax.axis_index("dp")
    return [
        pltpu.make_async_copy(block, place(lax.bitwise_xor(me, j)), sems.at[j])
        for j, block in enumerate(blocks)
    ]


def rows_at(ref, size):
    return lambda owner: ref.at[pl.ds(pl.multiple_of(owner * size, size), size)]


def columns_at(ref, size):
    return lambda owner: ref.at[:, pl.ds(pl.multiple_of(owner * size, size), size)]


def arrays_of(chunks):
    return [array for array, _ in chunks]


def shifts_of(chunks):
    return tuple(shifts for _, shifts in chunks)


def by_shift(refs, shifts):
    found = {}
    for ref, group in zip(refs, shifts):
        for n, k in enumerate(group):
            found[k] = ref if len(group) == 1 else ref.at[n]
    return found


def chunk_copies(chunks, places, parts, held, sems):
    z = lax.axis_index("mp")
    found = []
    for s, sequence in enumerate(chunks):
        for i, m in enumerate(places):
            slot, options = s * len(places) + i, []
            for k in sorted({(at - (at ^ m)) % parts for at in range(parts)}):
                here = lax.rem(z - lax.bitwise_xor(z, m) + parts, parts) == k
                options.append((here if k else None, sequence[k]))
            found.append(
                [
                    (here, pltpu.make_async_copy(source, held.at[slot], sems.at[slot]))
                    for here, source in options
                ]
            )
    return found


def start_all(found):
    for options in found:
        for here, copy in options:
            if here is None:
                copy.start()
            else:
                pl.when(here)(copy.start)


def wait_for(options):
    options[0][1].wait()


def project_kernel(setup, at_ref, bias_ref, gain_ref, shift_ref, cos_ref, left_ref, right_ref, *rest):
    count, parts, places, width, hidden, shifts = setup
    chunks = [by_shift(rest, shifts)]
    blocks = rest[len(shifts) : len(shifts) + count]
    qkv_ref, act_ref, slope_ref, normed_ref, tokens_ref, held, x_held, ready, sems, x_sems = rest[-10:]
    step, steps = pl.program_id(0), len(places)
    found = chunk_copies(chunks, places, parts, x_held, x_sems)
    loads = block_copies(blocks, rows_at(held, blocks[0].shape[0]), sems)

    def norm(slot):
        return (normalized(x_held[slot]) * gain_ref[...] + shift_ref[...]).astype(BF16)

    @pl.when(step == 0)
    def _():
        for copy in loads:
            copy.start()
        start_all(found)
        wait_for(found[0])
        ready[0] = norm(0)
        for copy in loads:
            copy.wait()

    for slot in range(1, steps):

        @pl.when(step == slot - 1)
        def _(slot=slot):
            wait_for(found[slot])

    x = ready[step % 2]
    normed_ref[...] = x
    tokens_ref[...] = x_held[step]
    ready[(step + 1) % 2] = norm((step + 1) % steps)
    root = 0.7978845608028654
    for t in range((3 * width + hidden) // width):
        columns = slice(t * width, (t + 1) * width)
        y = dot(x, held[:, columns], 1, 0) + bias_ref[:, columns]
        if t < 3:
            for g in range(width // LANES):
                part = y[:, g * LANES : (g + 1) * LANES]
                if t < 2:
                    part = rotated(part, cos_ref[...], left_ref[...], right_ref[...], 1.0)
                if t == 0:
                    part = part * HEAD_DIM**-0.5
                start = t * width + g * LANES
                qkv_ref[:, start : start + LANES] = part.astype(BF16)
        else:
            columns = slice((t - 3) * width, (t - 2) * width)
            square = y * y
            turn = jnp.tanh(root * y * (1.0 + 0.044715 * square))
            half = 0.5 * (1.0 + turn)
            act_ref[:, columns] = (y * half).astype(BF16)
            slope = half * (1.0 + y * (1.0 - turn) * (root + (3.0 * 0.044715 * root) * square))
            slope_ref[:, columns] = slope.astype(BF16)


def project(at_mp, sequence, chunks, blocks, bias, gain, shift, tables, width, parts, earlier, deps):
    places, total = tuple(range(parts)), blocks[0].shape[1]
    rows, model, count = tables[0].shape[0] // parts, gain.shape[1], len(blocks)
    hidden = total - 3 * width
    table = pl.BlockSpec((rows, LANES), lambda i, at: (at[0] ^ i, 0))
    out = lambda w: pl.BlockSpec((rows, w), lambda i, at: (sequence * parts + (at[0] ^ i), 0))
    line = lambda a: pl.BlockSpec(a.shape, lambda i, at: (0, 0))
    widths = (3 * width, hidden, hidden, model, model)
    setup = (count, parts, places, width, hidden, shifts_of(chunks))
    operands = [bias, gain, shift, *tables, *arrays_of(chunks), *blocks]
    return call(
        functools.partial(project_kernel, setup),
        "project",
        operands + list(earlier),
        deps,
        (at_mp,),
        vmem=32,
        grid=(parts,),
        in_specs=[line(bias), line(gain), line(shift), table, table, table]
        + [ANY] * (len(chunks) + count + len(earlier)),
        out_specs=[out(w) for w in widths],
        out_shape=[jax.ShapeDtypeStruct((2 * parts * rows, w), BF16) for w in widths],
        input_output_aliases={1 + len(operands) + n: n for n in range(len(earlier))},
        scratch_shapes=[
            pltpu.VMEM((model, total), BF16),
            pltpu.VMEM((parts, rows, model), BF16),
            pltpu.VMEM((2, rows, model), BF16),
            pltpu.SemaphoreType.DMA((count,)),
            pltpu.SemaphoreType.DMA((parts,)),
        ],
    )


def attend_kernel(block, q_ref, k_ref, v_ref, out_ref, lse_ref):
    length = q_ref.shape[0]
    lane = lax.broadcasted_iota(jnp.int32, (1, LANES), 1)
    key = lax.broadcasted_iota(jnp.int32, (block, block), 0)
    causal = key <= lax.broadcasted_iota(jnp.int32, (block, block), 1)
    for i in range(length // block):
        rows, before = pl.ds(i * block, block), pl.ds(0, i * block)
        results = []
        for h in range(2):
            mine = (lane < HEAD_DIM) if h == 0 else (lane >= HEAD_DIM)
            query = jnp.where(mine, q_ref[rows, :], 0)
            near = jnp.where(causal, dot(k_ref[rows, :], query, 1, 1), -1e30)
            highest = jnp.max(near, axis=0, keepdims=True)
            if i:
                far = dot(k_ref[before, :], query, 1, 1)
                highest = jnp.maximum(highest, jnp.max(far, axis=0, keepdims=True))
            near = jnp.exp(near - highest)
            total = jnp.sum(near, axis=0, keepdims=True)
            if i:
                far = jnp.exp(far - highest)
                total = total + jnp.sum(far, axis=0, keepdims=True)
            inverse = 1.0 / total
            result = dot((near * inverse).astype(BF16), v_ref[rows, :], 0, 0)
            if i:
                result = result + dot((far * inverse).astype(BF16), v_ref[before, :], 0, 0)
            results.append(result)
            lse_ref[0, h : h + 1, rows] = highest + jnp.log(total)
        out_ref[rows, :] = jnp.where(lane < HEAD_DIM, results[0], results[1]).astype(BF16)


def pair_specs(length, pairs):
    return lambda off: pl.BlockSpec(
        (length, LANES), lambda g: (g // pairs, off * pairs + g % pairs)
    )


def attend(qkv, length, block, deps):
    width, sequences = qkv.shape[1] // 3, qkv.shape[0] // length
    pairs = width // LANES
    at = pair_specs(length, pairs)
    return call(
        functools.partial(attend_kernel, block),
        "attend",
        [qkv, qkv, qkv],
        deps,
        vmem=26,
        grid=(sequences * pairs,),
        in_specs=[at(0), at(1), at(2)],
        out_specs=[at(0), pl.BlockSpec((1, 8, length), lambda g: (g, 0, 0))],
        out_shape=[
            jax.ShapeDtypeStruct((qkv.shape[0], width), BF16),
            jax.ShapeDtypeStruct((sequences * pairs, 8, length), F32),
        ],
    )


def attend_back_kernel(
    block,
    q_ref,
    k_ref,
    v_ref,
    grad_ref,
    mixed_ref,
    lse_ref,
    cos_ref,
    left_ref,
    right_ref,
    gq_ref,
    gk_ref,
    gv_ref,
    sum_ref,
    gk_sum,
    gv_sum,
):
    length = q_ref.shape[0]
    lane = lax.broadcasted_iota(jnp.int32, (1, LANES), 1)
    key = lax.broadcasted_iota(jnp.int32, (block, block), 0)
    causal = key <= lax.broadcasted_iota(jnp.int32, (block, block), 1)
    count = length // block
    sum_ref[...] = jnp.zeros_like(sum_ref)

    def put(ref, which, rows, value):
        value = value.astype(BF16)
        ref[rows, :] = value
        sum_ref[0, which : which + 1, :] += jnp.sum(value.astype(F32), axis=0, keepdims=True)

    def unrotated(value, rows):
        return rotated(value, cos_ref[rows, :], left_ref[rows, :], right_ref[rows, :], -1.0)

    for i in reversed(range(count)):
        rows = pl.ds(i * block, block)
        product = grad_ref[rows, :].astype(F32) * mixed_ref[rows, :].astype(F32)
        gq = None
        for h in range(2):
            mine = (lane < HEAD_DIM) if h == 0 else (lane >= HEAD_DIM)
            query = jnp.where(mine, q_ref[rows, :], 0)
            grad = jnp.where(mine, grad_ref[rows, :], 0)
            ones = jnp.where(mine, jnp.ones((8, LANES), F32), 0.0)
            delta = lax.dot_general(
                ones,
                product,
                (((1,), (1,)), ((), ())),
                precision=lax.Precision.HIGHEST,
                preferred_element_type=F32,
            )[0:1, :]
            lse = lse_ref[0, h : h + 1, rows]
            for j in range(i + 1):
                keys = pl.ds(j * block, block)
                key_rows = k_ref[keys, :]
                probs = jnp.exp(dot(key_rows, query, 1, 1) - lse)
                if j == i:
                    probs = jnp.where(causal, probs, 0.0)
                gprobs = dot(v_ref[keys, :], grad, 1, 1)
                gscores = (probs * (gprobs - delta)).astype(BF16)
                gv, gk = dot(probs.astype(BF16), grad, 1, 0), dot(gscores, query, 1, 0)
                if i == count - 1 and h == 0:
                    gv_sum[keys, :] = gv
                    gk_sum[keys, :] = gk
                else:
                    gv_sum[keys, :] += gv
                    gk_sum[keys, :] += gk
                part = dot(gscores, jnp.where(mine, key_rows, 0), 0, 0)
                gq = part if gq is None else gq + part
        put(gq_ref, 0, rows, unrotated(gq * HEAD_DIM**-0.5, rows))
    for i in range(count):
        rows = pl.ds(i * block, block)
        put(gk_ref, 1, rows, unrotated(gk_sum[rows, :], rows))
        put(gv_ref, 2, rows, gv_sum[rows, :])


def attend_back(qkv, grad, mixed, lse, tables, length, block, deps):
    width, sequences = qkv.shape[1] // 3, qkv.shape[0] // length
    pairs = width // LANES
    at = pair_specs(length, pairs)
    table = pl.BlockSpec((length, LANES), lambda g: (0, 0))
    small = pl.BlockSpec((1, 8, length), lambda g: (g, 0, 0))
    return call(
        functools.partial(attend_back_kernel, block),
        "attend_back",
        [qkv, qkv, qkv, grad, mixed, lse, *tables],
        deps,
        vmem=26,
        grid=(sequences * pairs,),
        in_specs=[at(0), at(1), at(2), at(0), at(0), small, table, table, table],
        out_specs=[at(0)] * 3 + [pl.BlockSpec((1, 8, LANES), lambda g: (g, 0, 0))],
        out_shape=[jax.ShapeDtypeStruct((qkv.shape[0], width), BF16)] * 3
        + [jax.ShapeDtypeStruct((sequences * pairs, 8, LANES), F32)],
        scratch_shapes=[pltpu.VMEM((length, LANES), F32)] * 2,
    )


def quarter_map(places, parts):
    turns = len(places)

    def rows_of(i, at):
        offset = jnp.int32(places[0])
        for n in range(1, turns):
            offset = jnp.where(i % turns == n, places[n], offset)
        return jnp.where(i < turns, parts, 0) + (at[0] + offset) % parts

    return rows_of


def split_outputs(step, turns, result, other_ref, own_ref):
    @pl.when(step < turns)
    def _():
        other_ref[0] = result

    @pl.when(step >= turns)
    def _():
        own_ref[0] = result


def split_specs(rows, model, turns):
    return [
        pl.BlockSpec((1, rows, model), lambda i, at: (jnp.minimum(i, turns - 1), 0, 0)),
        pl.BlockSpec((1, rows, model), lambda i, at: (jnp.maximum(i - turns, 0), 0, 0)),
    ]


def branch_kernel(count, turns, at_ref, mixed_ref, act_ref, *rest):
    blocks, (other_ref, own_ref, held, sems) = rest[:count], rest[count:]
    step = pl.program_id(0)

    @pl.when(step == 0)
    def _():
        loads = block_copies(blocks, columns_at(held, blocks[0].shape[1]), sems)
        for copy in loads:
            copy.start()
        for copy in loads:
            copy.wait()

    x = jnp.concatenate([mixed_ref[...], act_ref[...]], axis=1)
    split_outputs(step, turns, dot(x, held[...], 1, 0).astype(BF16), other_ref, own_ref)


def branch_sums(at_mp, mixed, act, blocks, parts, places, deps):
    rows, count, turns = mixed.shape[0] // (2 * parts), len(blocks), len(places)
    inner, model = blocks[0].shape[0], count * blocks[0].shape[1]
    where = quarter_map(places, parts)
    return call(
        functools.partial(branch_kernel, count, turns),
        "branch_sums",
        [mixed, act, *blocks],
        deps,
        (at_mp,),
        vmem=22,
        grid=(2 * turns,),
        in_specs=[
            pl.BlockSpec((rows, a.shape[1]), lambda i, at: (where(i, at), 0)) for a in (mixed, act)
        ]
        + [ANY] * count,
        out_specs=split_specs(rows, model, turns),
        out_shape=[jax.ShapeDtypeStruct((turns, rows, model), BF16)] * 2,
        scratch_shapes=[pltpu.VMEM((inner, model), BF16), pltpu.SemaphoreType.DMA((count,))],
    )


def grad_in_kernel(setup, at_ref, slope_ref, *rest):
    count, parts, places, width, hidden, groups = setup
    chunks, many = [], 0
    for shifts in groups:
        chunks.append(by_shift(rest[many:], shifts))
        many += len(shifts)
    blocks = rest[many : many + count]
    gmixed_ref, gpre_ref, dy_ref, gsum_ref, dsum_ref, held, dy_held, sems, dy_sems = rest[-9:]
    step, steps = pl.program_id(0), 2 * len(places)
    found = chunk_copies(chunks, places, parts, dy_held, dy_sems)
    loads = block_copies(blocks, columns_at(held, blocks[0].shape[1]), sems)

    @pl.when(step == 0)
    def _():
        for copy in loads:
            copy.start()
        start_all(found)
        gsum_ref[...] = jnp.zeros_like(gsum_ref)
        dsum_ref[...] = jnp.zeros_like(dsum_ref)
        for copy in loads:
            copy.wait()

    for slot in range(steps):

        @pl.when(step == slot)
        def _(slot=slot):
            wait_for(found[slot])

    dy = dy_held[step]
    dy_ref[...] = dy
    gmixed_ref[...] = dot(dy, held[:width, :], 1, 1).astype(BF16)
    for start in range(0, hidden, width):
        part = slice(start, start + width)
        gact = dot(dy, held[width + start : 2 * width + start, :], 1, 1)
        gpre = (gact * slope_ref[:, part].astype(F32)).astype(BF16)
        gpre_ref[:, part] = gpre
        gsum_ref[0:1, part] += jnp.sum(gpre.astype(F32), axis=0, keepdims=True)
    dsum_ref[0:1, :] += jnp.sum(dy.astype(F32), axis=0, keepdims=True)


def grad_in(at_mp, chunks, slope, blocks, width, parts, places, earlier, deps):
    model = len(blocks) * blocks[0].shape[1]
    hidden, length = slope.shape[1], slope.shape[0]
    rows, count, many = length // (2 * parts), len(blocks), sum(len(c) for c in chunks)
    turns = len(places)

    def where(i, at):
        m = jnp.int32(places[0])
        for n in range(1, turns):
            m = jnp.where(i % turns == n, places[n], m)
        return i // turns * parts + (at[0] ^ m)

    out = lambda w: pl.BlockSpec((rows, w), lambda i, at: (where(i, at), 0))
    total = lambda w: pl.BlockSpec((8, w), lambda i, at: (0, 0))
    setup = (count, parts, places, width, hidden, [shifts_of(c) for c in chunks])
    operands = [slope, *arrays_of(chunks[0]), *arrays_of(chunks[1]), *blocks]
    aliases = {1 + len(operands) + n: n for n in range(len(earlier))}
    return call(
        functools.partial(grad_in_kernel, setup),
        "grad_in",
        operands + list(earlier),
        deps,
        (at_mp,),
        vmem=24,
        grid=(2 * turns,),
        in_specs=[out(hidden)] + [ANY] * (many + count + len(earlier)),
        out_specs=[out(width), out(hidden), out(model), total(hidden), total(model)],
        out_shape=[jax.ShapeDtypeStruct((length, w), BF16) for w in (width, hidden, model)]
        + [jax.ShapeDtypeStruct((8, w), F32) for w in (hidden, model)],
        input_output_aliases=aliases,
        scratch_shapes=[
            pltpu.VMEM((width + hidden, model), BF16),
            pltpu.VMEM((2 * turns, rows, model), BF16),
            pltpu.SemaphoreType.DMA((count,)),
            pltpu.SemaphoreType.DMA((2 * turns,)),
        ],
    )


def grad_normed_kernel(
    count, turns, at_ref, gq_ref, gk_ref, gv_ref, gpre_ref, tokens_ref, *rest
):
    blocks, (other_ref, own_ref, sum_ref, held, sems) = rest[:count], rest[count:]
    step = pl.program_id(0)

    @pl.when(step == 0)
    def _():
        loads = block_copies(blocks, rows_at(held, blocks[0].shape[0]), sems)
        for copy in loads:
            copy.start()
        sum_ref[...] = jnp.zeros_like(sum_ref)
        for copy in loads:
            copy.wait()

    g = jnp.concatenate([gq_ref[...], gk_ref[...], gv_ref[...], gpre_ref[...]], axis=1)
    result = dot(g, held[...], 1, 1)
    sum_ref[0:1, :] += jnp.sum(result * normalized(tokens_ref[...]), axis=0, keepdims=True)
    sum_ref[1:2, :] += jnp.sum(result, axis=0, keepdims=True)
    split_outputs(step, turns, result.astype(BF16), other_ref, own_ref)


def grad_normed_sums(at_mp, gqkv, gpre, tokens, blocks, parts, places, deps):
    rows, count, turns = tokens.shape[0] // (2 * parts), len(blocks), len(places)
    model, total = tokens.shape[1], blocks[0].shape[1]
    where = quarter_map(places, parts)
    operands = [*gqkv, gpre, tokens]
    return call(
        functools.partial(grad_normed_kernel, count, turns),
        "grad_normed_sums",
        operands + list(blocks),
        deps,
        (at_mp,),
        vmem=28,
        grid=(2 * turns,),
        in_specs=[
            pl.BlockSpec((rows, a.shape[1]), lambda i, at: (where(i, at), 0)) for a in operands
        ]
        + [ANY] * count,
        out_specs=split_specs(rows, model, turns)
        + [pl.BlockSpec((8, model), lambda i, at: (0, 0))],
        out_shape=[jax.ShapeDtypeStruct((turns, rows, model), BF16)] * 2
        + [jax.ShapeDtypeStruct((8, model), F32)],
        scratch_shapes=[pltpu.VMEM((model, total), BF16), pltpu.SemaphoreType.DMA((count,))],
    )


def weight_grad_kernel(sizes, left, at_ref, *refs):
    ins, outs = refs[: len(refs) - len(sizes)], refs[len(refs) - len(sizes) :]
    if left:
        grad = jnp.concatenate([dot(ins[0][...], g[...], 0, 0) for g in ins[1:]], axis=1)
    else:
        grad = jnp.concatenate([dot(x[...], ins[-1][...], 0, 0) for x in ins[:-1]], axis=0)
    grad = grad.astype(BF16)
    first = 0
    for size, out_ref in zip(sizes, outs):

        @pl.when((pl.program_id(0) >= first) & (pl.program_id(0) < first + size))
        def _(out_ref=out_ref):
            out_ref[0] = grad

        first += size


def weight_grads(me, xs, gs, count, deps, left):
    plan = scatter_plan(count)
    sets = [(half, s) for s in range(len(plan[0])) for half in range(2)]
    sizes = [len(plan[half][s]) for half, s in sets]
    order = [j for half, s in sets for j in plan[half][s]]
    owners = lax.bitwise_xor(me, jnp.array(order, jnp.int32))
    length, (cut, whole) = xs[0].shape[0], ((xs, gs) if left else (gs, xs))
    size = cut[0].shape[1] // count
    cut_spec = pl.BlockSpec((length, size), lambda i, at: (0, at[i]))
    whole_specs = [pl.BlockSpec(a.shape, lambda i, at: (0, 0)) for a in whole]
    full = sum(a.shape[1] for a in whole)
    shape = (size, full) if left else (full, size)

    def out(first, many):
        return pl.BlockSpec(
            (1, *shape), lambda i, at: (jnp.clip(i - first, 0, many - 1), 0, 0)
        )

    firsts = [sum(sizes[:n]) for n in range(len(sizes))]
    outs = call(
        functools.partial(weight_grad_kernel, sizes, left),
        "weight_grads",
        [*xs, *gs],
        deps,
        (owners,),
        vmem=32,
        grid=(count,),
        in_specs=[cut_spec] + whole_specs if left else whole_specs + [cut_spec],
        out_specs=[out(first, many) for first, many in zip(firsts, sizes)],
        out_shape=[jax.ShapeDtypeStruct((many, *shape), BF16) for many in sizes],
    )
    return [[o for o, (half, _) in zip(outs, sets) if half == h] for h in range(2)]


def across(value, bit, count):
    return lax.ppermute(value, "dp", [(i, i ^ bit) for i in range(count)])


def ring(value, k, parts):
    return lax.ppermute(value, "mp", [(i, (i + k) % parts) for i in range(parts)])


def near_shifts(parts):
    return (1, 3) if parts == 4 else tuple(range(1, parts))


def gather_far(chunks, parts):
    if parts != 4:
        return None
    up = lax.ppermute(chunks[1], "mp", [(1, 2), (2, 3)])
    down = lax.ppermute(chunks[3], "mp", [(1, 0), (2, 1)])
    return up + down


def added(addends):
    return sum(a.astype(F32) for a in addends).astype(BF16)


def send_far(farthest):
    up = lax.ppermute(farthest, "mp", [(0, 1), (1, 2)])
    down = lax.ppermute(farthest, "mp", [(3, 2), (2, 1)])
    return [up, down]


def chip_bits(count):
    bits, bit = [], 2
    while bit < count:
        bits.append(bit)
        bit *= 2
    return bits


class BlockGather:
    def __init__(self, own, sibling, count):
        self.held, self.count = {0: own, 1: sibling}, count
        self.orders = (chip_bits(count), chip_bits(count)[::-1])

    def own_to(self, s):
        if s < len(self.orders[0]):
            for half in range(2):
                bit = self.orders[half][s]
                self.held[half ^ bit] = across(self.held[half], bit, self.count)

    def rest(self):
        for s in range(1, len(self.orders[0])):
            for half in range(2):
                order = self.orders[half]
                for j in [j for j in self.held if j % 2 == half]:
                    if j ^ order[s] not in self.held and not any(j & b for b in order[s:]):
                        self.held[j ^ order[s]] = across(self.held[j], order[s], self.count)

    def fenced(self, others=(), deps=()):
        keys = sorted(self.held)
        values = fence([self.held[j] for j in keys] + list(others), deps)
        self.held = dict(zip(keys, values))
        return values[len(keys) :]

    def blocks(self):
        return [self.held[j] for j in range(self.count)]


def scatter_orders(count):
    return (chip_bits(count)[::-1], chip_bits(count))


def scatter_plan(count):
    plan = []
    for half, order in enumerate(scatter_orders(count)):
        sets, rest = [[half]], [half]
        for bit in reversed(order):
            sets.insert(0, [j ^ bit for j in rest])
            rest = sets[0] + rest
        plan.append(sets)
    return plan


class BlockScatter:
    def __init__(self, halves, count):
        self.count, self.orders = count, scatter_orders(count)
        self.held = [[[a] for a in arrays] for arrays in halves]
        self.steps = len(self.orders[0])

    def total(self, half, s):
        if len(self.held[half][s]) > 1:
            self.held[half][s] = [added(self.held[half][s])]
        return self.held[half][s][0]

    def ready(self, s):
        return [self.total(half, s) for half in range(2)]

    def send(self, s):
        return [across(self.total(h, s), self.orders[h][s], self.count) for h in range(2)]

    def arrive(self, s, came):
        for half in range(2):
            first = 0
            for later in self.held[half][s + 1 :]:
                many = later[0].shape[0]
                later.append(came[half][first : first + many])
                first += many

    def between(self):
        for s in range(1, self.steps - 1):
            self.arrive(s, self.send(s))

    def last(self):
        return self.total(1, -1)[0]

    def finish(self, theirs):
        return sum(a[0].astype(F32) for a in self.held[0][-1]), theirs.astype(F32)


def on_device(
    tokens,
    norm_gain,
    norm_bias,
    qkv_weight,
    qkv_bias,
    dense_weight,
    dense_bias,
    up_weight,
    up_bias,
    down_weight,
    down_bias,
    cotangent,
    *,
    ndp,
    nmp,
):
    me, z = lax.axis_index("dp"), lax.axis_index("mp")
    core = me % 2
    at_mp = z.astype(jnp.int32)[None]
    length, model = tokens.shape[0] * nmp, tokens.shape[1]
    block = min(512, length)
    width, hidden = qkv_weight.shape[2] // 2, up_weight.shape[1] // 2
    chip_steps = len(chip_bits(ndp))
    rank = lambda array, axis, which, size: lax.dynamic_slice_in_dim(
        array, which * size, size, axis
    )

    def row_pack(which):
        qkv = rank(qkv_weight, 2, which, width)
        return jnp.concatenate([qkv[0], qkv[1], qkv[2], rank(up_weight, 1, which, hidden)], axis=1)

    def column_pack(which):
        return jnp.concatenate(
            [rank(dense_weight, 0, which, width), rank(down_weight, 0, which, hidden)], axis=0
        )

    def stage(*arrays):
        return jnp.stack(arrays), tuple([0, *near])

    near, places, pairs = near_shifts(nmp), list(range(nmp)), width // LANES
    rows = BlockGather(row_pack(core), across(row_pack(1 - core), 1, ndp), ndp)
    columns = BlockGather(column_pack(core), across(column_pack(1 - core), 1, ndp), ndp)
    head, tail = near[0], near[1:]
    came = {head: ring(tokens, head, nmp)}
    rows.own_to(0)
    came[head], begun = rows.fenced([came[head], tokens], columns.held.values())
    came.update({k: ring(begun, k, nmp) for k in tail})
    rows.own_to(1)
    *held, cot = rows.fenced([*came.values(), cotangent])
    came = dict(zip(near, held))
    own = [(tokens, (0,))] + [(came[k], (k,)) for k in near]
    packed, shifts = stage(tokens, *held)
    other = [(across(packed, 1, ndp), shifts)]
    far = gather_far(came, nmp)
    rows.rest()
    cot, *held = rows.fenced(
        [cot, columns.held[0], columns.held[1]] + ([far] if nmp == 4 else []), [other[0][0]]
    )
    columns.held = dict(enumerate(held[:2]))
    if nmp == 4:
        own.append((held[2], (2,)))
        other.append((across(held[2], 1, ndp), (2,)))

    tables = rotary_tables(length)
    bias = jnp.concatenate(
        [
            rank(qkv_bias, 1, core, width).astype(F32).reshape(1, 3 * width),
            rank(up_bias[None, :], 1, core, hidden).astype(F32),
        ],
        axis=1,
    )
    gain, shift = norm_gain.astype(F32)[None, :], norm_bias.astype(F32)[None, :]
    came = {head: ring(cot, head, nmp)}
    columns.own_to(0)
    common = (rows.blocks(), bias, gain, shift, tables, width, nmp)
    first = project(at_mp, 0, own, *common, (), [cot])
    cot, came[head] = columns.fenced([cot, came[head]], [first[0]])
    came.update({k: ring(cot, k, nmp) for k in tail})
    columns.own_to(1)
    qkv, act, slope, normed, token_rows = project(
        at_mp, 1, other, *common, first, [columns.held[0]]
    )
    columns.fenced(deps=[qkv])
    columns.rest()
    mixed, lse = attend(qkv, length, block, [columns.held[0]])
    held = columns.fenced(came.values(), [mixed])
    came = dict(zip(near, held))
    dy_own = [(cot, (0,))] + [(came[k], (k,)) for k in near]
    packed, shifts = stage(cot, *held)
    dy_packed = across(packed, 1, ndp)
    far = gather_far(came, nmp)
    other_sums, own_sums = branch_sums(
        at_mp, mixed, act, columns.blocks(), nmp, places, [packed]
    )
    dy_packed, other_sums, *far = fence(
        [dy_packed, other_sums] + ([far] if nmp == 4 else []), [own_sums]
    )
    theirs = across(other_sums, 1, ndp)

    dy_other = [(dy_packed, shifts)]
    grad_a = grad_in(
        at_mp, (dy_own, dy_other), slope, columns.blocks(), width, nmp, (0, 1), (), [other_sums]
    )
    far_other = [across(a, 1, ndp) for a in far]
    theirs, *far_other = fence([theirs, *far_other], [grad_a[3]])
    shares = [[own_sums[k], theirs[k]] for k in places]
    farthest = [added(shares[2])] if nmp == 4 else []
    moved = [a for f in farthest for a in send_far(f)]
    grad_b = grad_in(
        at_mp,
        (dy_own + [(a, (2,)) for a in far], dy_other + [(a, (2,)) for a in far_other]),
        slope,
        columns.blocks(),
        width,
        nmp,
        tuple(places[2:]),
        grad_a[:3],
        [grad_a[3], *farthest],
    )
    gmixed, gpre, dy = grad_b[:3]
    column_grads = BlockScatter(
        weight_grads(me, [mixed, act], [dy], ndp, [grad_b[3]], left=False), ndp
    )

    def with_far(shares, moved):
        if moved:
            shares[1], shares[3] = shares[1] + [moved[0]], shares[3] + [moved[1]]
        return {k: added(shares[k]) for k in near}

    if moved:
        moved = fence(moved, [column_grads.held[0][0][0]])
    sums = with_far(shares, moved)
    brought = [ring(sums[head], head, nmp)]
    column_came = column_grads.send(0)
    gq, gk, gv, qkv_sums = attend_back(
        qkv,
        gmixed,
        mixed,
        lse,
        tables,
        length,
        block,
        [column_grads.held[0][0][0], *sums.values()],
    )
    brought[0], *held = fence([brought[0], *(sums[k] for k in tail)], [gq])
    brought += [ring(a, k, nmp) for k, a in zip(tail, held)]

    def normed_part(part, deps):
        return grad_normed_sums(
            at_mp, (gq, gk, gv), gpre, token_rows, rows.blocks(), nmp, part, deps
        )

    thirds = ([2], [1, 3], [0]) if nmp == 4 else (places[1:2], places[2:], places[:1])
    other_a, own_a, sums_a = normed_part(thirds[0], [brought[0]])
    *column_came, other_a = fence([*column_came, other_a], [sums_a])
    column_grads.arrive(0, column_came)
    column_grads.between()
    column_came = column_grads.send(-1 + chip_steps)
    most = other_a.shape[1] // 2
    came_a = [across(p, 1, ndp) for p in (other_a[:, :most], other_a[:, most:])]
    other_b, own_b, sums_b = normed_part(
        thirds[1], [sums_a, *column_grads.ready(chip_steps - 1)]
    )
    brought[1:] = fence(brought[1:], [sums_b])
    c0, c1, a0, a1, other_b = fence([*column_came, *came_a, other_b], [brought[1]])
    column_grads.arrive(chip_steps - 1, [c0, c1])
    came_a = jnp.concatenate([a0, a1], axis=1)
    came_b = across(other_b, 1, ndp)
    shares = [[] for _ in places]
    for part, kept, got in ((thirds[0], own_a, came_a),):
        for n, k in enumerate(part):
            shares[k] = [kept[n], got[n]]
    farthest = [added(shares[2])] if nmp == 4 else []
    moved = [a for f in farthest for a in send_far(f)]
    other_c, own_c, sums_c = normed_part(
        thirds[2], [sums_b, *farthest, column_grads.last()]
    )
    qkv_sum = (
        qkv_sums.reshape(2, pairs, 8, LANES).sum(0)[:, :3, :].transpose(1, 0, 2).reshape(3 * width)
    )
    norm_sums = (sums_a + sums_b + sums_c)[:2].reshape(2 * model)
    small = jnp.concatenate(
        [norm_sums, qkv_sum, grad_a[3][0] + grad_b[3][0], grad_a[4][0] + grad_b[4][0]]
    )
    bits = chip_bits(ndp)
    for bit in bits[:-2]:
        small = small + across(small, bit, ndp)
    small_came = across(small, bits[-2], ndp)
    up_grads = BlockScatter(
        weight_grads(me, [normed], [gpre], ndp, [sums_c, small], left=True), ndp
    )
    came_b, other_c, column_last, small_came, *moved = fence(
        [came_b, other_c, column_grads.last(), small_came, *moved], [up_grads.held[0][0][0]]
    )
    small = small + small_came
    small_came = across(small, bits[-1], ndp)
    up_came = up_grads.send(0)
    for n, k in enumerate(thirds[1]):
        shares[k] = [own_b[n], came_b[n]]
    sums = with_far(shares, moved)
    came = {head: ring(sums[head], head, nmp)}
    column_theirs = across(column_last, 1, ndp)
    qkv_grads = BlockScatter(
        weight_grads(me, [normed], [gq, gk, gv], ndp, [small, *sums.values()], left=True), ndp
    )
    *up_came, q0, q1, column_theirs, small_came = fence(
        [*up_came, qkv_grads.held[0][0][0], qkv_grads.held[1][0][0], column_theirs, small_came]
    )
    qkv_grads.held[0][0], qkv_grads.held[1][0] = [q0], [q1]
    up_grads.arrive(0, up_came)
    up_grads.between()
    up_came = up_grads.send(chip_steps - 1)
    qkv_came = qkv_grads.send(0)
    small = small + small_came
    came[head], other_c, small, *held = fence(
        [came[head], other_c, small, *(sums[k] for k in tail)], [q0]
    )
    half = held[0].shape[0] // 2
    early = [ring(a[:half], k, nmp) for k, a in zip(tail, held)]
    u0, u1, small, *qkv_came = fence([*up_came, small, *qkv_came], [came[head]])
    small_other = across(small, 1, ndp)
    up_grads.arrive(chip_steps - 1, [u0, u1])
    up_theirs = across(up_grads.last(), 1, ndp)
    qkv_grads.arrive(0, qkv_came)
    qkv_grads.between()
    late = fence([*early, *(a[half:] for a in held)])
    early, late = late[: len(tail)], late[len(tail) :]
    late = [ring(a, k, nmp) for k, a in zip(tail, late)]
    came.update({k: jnp.concatenate(pair) for k, *pair in zip(tail, early, late)})
    came_c = across(other_c, 1, ndp)
    qkv_grads.arrive(chip_steps - 1, qkv_grads.send(chip_steps - 1))
    qkv_theirs = across(qkv_grads.last(), 1, ndp)
    norm_sums = small[: 2 * model] + small_other[: 2 * model]
    norm_sums = [norm_sums] + [
        lax.ppermute(norm_sums, "mp", [(i, i ^ j) for i in range(nmp)]) for j in range(1, nmp)
    ]
    while len(norm_sums) > 1:
        norm_sums = [a + b for a, b in zip(norm_sums[::2], norm_sums[1::2])]
    norm_sums = norm_sums[0]

    local_inputs = tokens.astype(F32)
    output = (
        local_inputs
        + sum(a.astype(F32) for a in [own_sums[0], theirs[0], *brought])
        + (dense_bias.astype(F32) + down_bias.astype(F32))[None, :]
    ).astype(BF16)

    def both(mine, theirs, axis):
        return jnp.where(
            core == 0,
            jnp.concatenate([mine, theirs], axis=axis),
            jnp.concatenate([theirs, mine], axis=axis),
        )

    mine, theirs = column_grads.finish(column_theirs)
    owned_dense = both(mine[:width], theirs[:width], 0)
    owned_down = both(mine[width:], theirs[width:], 0)
    owned_up = both(*up_grads.finish(up_theirs), 1)
    mine, theirs = qkv_grads.finish(qkv_theirs)
    owned_qkv = jnp.stack(
        [
            both(mine[:, c * width : (c + 1) * width], theirs[:, c * width : (c + 1) * width], 1)
            for c in range(3)
        ]
    )

    inner = 3 * width + hidden
    grad_out_bias = small[2 * model + inner :]
    here, there = (a[2 * model : 2 * model + inner] for a in (small, small_other))
    even, odd = jnp.where(core == 0, here, there), jnp.where(core == 0, there, here)
    grad_qkv_bias = jnp.concatenate(
        [a[: 3 * width].reshape(3, width) for a in (even, odd)], axis=1
    )
    grad_up_bias = jnp.concatenate([even[3 * width :], odd[3 * width :]])

    centered = local_inputs - jnp.mean(local_inputs, axis=1, keepdims=True)
    inverse_std = lax.rsqrt(jnp.mean(centered * centered, axis=1, keepdims=True) + EPS)
    normal_rows = centered * inverse_std
    grad_rows = sum(a.astype(F32) for a in [own_c[0], came_c[0], *came.values()])
    scaled = grad_rows * gain
    first_mean = jnp.mean(scaled, axis=1, keepdims=True)
    second_mean = jnp.mean(scaled * normal_rows, axis=1, keepdims=True)
    grad_tokens = (
        cotangent.astype(F32) + (scaled - first_mean - normal_rows * second_mean) * inverse_std
    ).astype(BF16)
    return (
        output,
        grad_tokens,
        norm_sums[:model],
        norm_sums[model:],
        owned_qkv,
        grad_qkv_bias,
        owned_dense,
        grad_out_bias,
        owned_up,
        grad_up_bias,
        owned_down,
        grad_out_bias,
    )


def solution(mesh):
    return jax.shard_map(
        functools.partial(on_device, ndp=mesh.shape["dp"], nmp=mesh.shape["mp"]),
        mesh=mesh,
        in_specs=(
            P(("dp", "mp"), None),
            P(),
            P(),
            P(None, "dp", "mp"),
            P(None, "mp"),
            P("mp", "dp"),
            P(),
            P("dp", "mp"),
            P("mp"),
            P("mp", "dp"),
            P(),
            P(("dp", "mp"), None),
        ),
        out_specs=(
            P(("dp", "mp"), None),
            P(("dp", "mp"), None),
            P(),
            P(),
            P(None, "dp", "mp"),
            P(None, "mp"),
            P("mp", "dp"),
            P(),
            P("dp", "mp"),
            P("mp"),
            P("mp", "dp"),
            P(),
        ),
        check_vma=False,
    )
```

```python
import functools

import jax
import jax.numpy as jnp
import numpy as np
from jax import lax
from jax.experimental import pallas as pl
from jax.experimental.pallas import tpu as pltpu
from jax.sharding import PartitionSpec as P

HEAD_DIM = 64
ROT = 32
EPS = 1e-05
LANES = 128
F32 = jnp.float32
BF16 = jnp.bfloat16
HBM = pl.BlockSpec(memory_space=pltpu.HBM)


def dot(lhs, rhs, lhs_dim, rhs_dim):
    return lax.dot_general(
        lhs, rhs, (((lhs_dim,), (rhs_dim,)), ((), ())), preferred_element_type=F32
    )


def call(kernel, name, operands, deps=(), scalars=(), vmem=63, **spec):
    deps, many, lead = tuple(deps), len(operands), len(scalars)

    def body(*refs):
        kernel(*refs[: lead + many], *refs[lead + many + len(deps) :])

    in_specs = list(spec.pop("in_specs")) + [HBM] * len(deps)
    out_shape, aliases = spec.pop("out_shape"), spec.pop("input_output_aliases", {})
    if scalars:
        grid_spec = pltpu.PrefetchScalarGridSpec(
            num_scalar_prefetch=lead, in_specs=in_specs, **spec
        )
        spec = {"grid_spec": grid_spec}
    else:
        spec["in_specs"] = in_specs
    return pl.pallas_call(
        body,
        out_shape=out_shape,
        input_output_aliases=aliases,
        compiler_params=pltpu.CompilerParams(vmem_limit_bytes=vmem << 20),
        cost_estimate=pl.CostEstimate(flops=0, transcendentals=0, bytes_accessed=0),
        name=name,
        **spec,
    )(*scalars, *operands, *deps)


def fence(values, deps=()):
    return call(
        lambda *refs: None,
        "fence",
        values,
        deps,
        in_specs=[HBM] * len(values),
        out_specs=[HBM] * len(values),
        out_shape=[jax.ShapeDtypeStruct(v.shape, v.dtype) for v in values],
        input_output_aliases={n: n for n in range(len(values))},
    )


def rotary_tables(length):
    positions = np.arange(length, dtype=np.float32)
    frequency = 10000.0 ** (-np.arange(ROT // 2, dtype=np.float64) * 2.0 / ROT)
    angles = positions[:, None] * frequency.astype(np.float32)[None, :]
    cosine, sine = np.cos(angles.astype(np.float64)), np.sin(angles.astype(np.float64))
    rest = HEAD_DIM - ROT
    none = np.zeros((length, ROT // 2))
    ones, zeros = np.ones((length, rest)), np.zeros((length, rest))
    straight = np.concatenate([cosine, cosine, ones], axis=1)
    left = np.concatenate([-sine, none, zeros], axis=1)
    right = np.concatenate([none, sine, zeros], axis=1)
    return [
        jnp.asarray(np.concatenate([t, t], axis=1).astype(np.float32))
        for t in (straight, left, right)
    ]


def rotated(u, straight, left, right, sign):
    half = ROT // 2
    turned = pltpu.roll(u, LANES - half, 1) * left + pltpu.roll(u, half, 1) * right
    return u * straight + sign * turned


def normalized(x):
    x = x.astype(F32)
    centered = x - jnp.mean(x, axis=1, keepdims=True)
    variance = jnp.mean(centered * centered, axis=1, keepdims=True)
    return centered * lax.rsqrt(variance + EPS)


def block_copies(blocks, place, sems, pieces=None):
    me = lax.axis_index("dp")
    parts = []
    for j, block in enumerate(blocks):
        owner = lax.bitwise_xor(me, j)
        for n, (source, target) in enumerate(pieces(block, owner) if pieces else [(block, place(owner))]):
            if n == len(parts):
                parts.append([])
            parts[n].append(pltpu.make_async_copy(source, target, sems.at[n, j]))
    return parts


def start_copies(copies):
    for copy in copies:
        copy.start()


def wait_copies(copies):
    for copy in copies:
        copy.wait()


def span(owner, size):
    return pl.ds(pl.multiple_of(owner * size, size), size)


def arrays_of(chunks):
    return [array for array, _ in chunks]


def shifts_of(chunks):
    return tuple(shifts for _, shifts in chunks)


def by_shift(refs, shifts):
    found = {}
    for ref, group in zip(refs, shifts):
        for n, k in enumerate(group):
            found[k] = ref if len(group) == 1 else ref.at[n]
    return found


def chunk_copies(chunks, places, parts, held, sems):
    z = lax.axis_index("mp")
    found = []
    for s, sequence in enumerate(chunks):
        for i, m in enumerate(places):
            slot, options = s * len(places) + i, []
            for k in sorted({(at - (at ^ m)) % parts for at in range(parts)}):
                here = lax.rem(z - lax.bitwise_xor(z, m) + parts, parts) == k
                options.append((here if k else None, sequence[k]))
            found.append(
                [
                    (here, pltpu.make_async_copy(source, held.at[slot], sems.at[slot]))
                    for here, source in options
                ]
            )
    return found


def start_all(found):
    for options in found:
        for here, copy in options:
            if here is None:
                copy.start()
            else:
                pl.when(here)(copy.start)


def wait_for(options):
    options[0][1].wait()


def project_kernel(setup, at_ref, bias_ref, gain_ref, shift_ref, cos_ref, left_ref, right_ref, *rest):
    count, parts, places, width, hidden, shifts = setup
    chunks = [by_shift(rest, shifts)]
    blocks = rest[len(shifts) : len(shifts) + count]
    qkv_ref, act_ref, slope_ref, normed_ref, tokens_ref, held, x_held, ready, sems, x_sems = rest[-10:]
    step, steps = pl.program_id(0), len(places)
    found = chunk_copies(chunks, places, parts, x_held, x_sems)
    size, tiles = blocks[0].shape[0], (3 * width + hidden) // width
    column = lambda t: slice(t * width, (t + 1) * width)
    loads = block_copies(
        blocks,
        None,
        sems,
        lambda block, owner: [
            (block.at[:, column(t)], held.at[span(owner, size), column(t)]) for t in range(tiles)
        ],
    )

    def norm(slot):
        return (normalized(x_held[slot]) * gain_ref[...] + shift_ref[...]).astype(BF16)

    @pl.when(step == 0)
    def _():
        start_all(found)
        for copies in loads:
            start_copies(copies)
        wait_for(found[0])
        ready[0] = norm(0)

    for slot in range(1, steps):

        @pl.when(step == slot - 1)
        def _(slot=slot):
            wait_for(found[slot])

    x = ready[step % 2]
    normed_ref[...] = x
    tokens_ref[...] = x_held[step]
    ready[(step + 1) % 2] = norm((step + 1) % steps)
    root = 0.7978845608028654
    for t in range(tiles):
        columns = column(t)
        pl.when(step == 0)(functools.partial(wait_copies, loads[t]))
        y = dot(x, held[:, columns], 1, 0) + bias_ref[:, columns]
        if t < 3:
            for g in range(width // LANES):
                part = y[:, g * LANES : (g + 1) * LANES]
                if t < 2:
                    part = rotated(part, cos_ref[...], left_ref[...], right_ref[...], 1.0)
                if t == 0:
                    part = part * HEAD_DIM**-0.5
                start = t * width + g * LANES
                qkv_ref[:, start : start + LANES] = part.astype(BF16)
        else:
            columns = slice((t - 3) * width, (t - 2) * width)
            square = y * y
            turn = jnp.tanh(root * y * (1.0 + 0.044715 * square))
            half = 0.5 * (1.0 + turn)
            act_ref[:, columns] = (y * half).astype(BF16)
            slope = half * (1.0 + y * (1.0 - turn) * (root + (3.0 * 0.044715 * root) * square))
            slope_ref[:, columns] = slope.astype(BF16)


def project(at_mp, sequence, chunks, blocks, bias, gain, shift, tables, width, parts, earlier, deps):
    places, total = tuple(range(parts)), blocks[0].shape[1]
    rows, model, count = tables[0].shape[0] // parts, gain.shape[1], len(blocks)
    hidden = total - 3 * width
    table = pl.BlockSpec((rows, LANES), lambda i, at: (at[0] ^ i, 0))
    out = lambda w: pl.BlockSpec((rows, w), lambda i, at: (sequence * parts + (at[0] ^ i), 0))
    line = lambda a: pl.BlockSpec(a.shape, lambda i, at: (0, 0))
    widths = (3 * width, hidden, hidden, model, model)
    setup = (count, parts, places, width, hidden, shifts_of(chunks))
    operands = [bias, gain, shift, *tables, *arrays_of(chunks), *blocks]
    return call(
        functools.partial(project_kernel, setup),
        "project",
        operands + list(earlier),
        deps,
        (at_mp,),
        grid=(parts,),
        in_specs=[line(bias), line(gain), line(shift), table, table, table]
        + [HBM] * (len(chunks) + count + len(earlier)),
        out_specs=[out(w) for w in widths],
        out_shape=[jax.ShapeDtypeStruct((2 * parts * rows, w), BF16) for w in widths],
        input_output_aliases={1 + len(operands) + n: n for n in range(len(earlier))},
        scratch_shapes=[
            pltpu.VMEM((model, total), BF16),
            pltpu.VMEM((parts, rows, model), BF16),
            pltpu.VMEM((2, rows, model), BF16),
            pltpu.SemaphoreType.DMA((total // width, count)),
            pltpu.SemaphoreType.DMA((parts,)),
        ],
    )


def attend_kernel(block, q_ref, k_ref, v_ref, out_ref, lse_ref):
    length = q_ref.shape[0]
    lane = lax.broadcasted_iota(jnp.int32, (1, LANES), 1)
    key = lax.broadcasted_iota(jnp.int32, (block, block), 0)
    causal = key <= lax.broadcasted_iota(jnp.int32, (block, block), 1)
    for i in range(length // block):
        rows, before = pl.ds(i * block, block), pl.ds(0, i * block)
        results = []
        for h in range(2):
            mine = (lane < HEAD_DIM) if h == 0 else (lane >= HEAD_DIM)
            query = jnp.where(mine, q_ref[rows, :], 0)
            near = jnp.where(causal, dot(k_ref[rows, :], query, 1, 1), -1e30)
            highest = jnp.max(near, axis=0, keepdims=True)
            if i:
                far = dot(k_ref[before, :], query, 1, 1)
                highest = jnp.maximum(highest, jnp.max(far, axis=0, keepdims=True))
            near = jnp.exp(near - highest)
            total = jnp.sum(near, axis=0, keepdims=True)
            if i:
                far = jnp.exp(far - highest)
                total = total + jnp.sum(far, axis=0, keepdims=True)
            inverse = 1.0 / total
            result = dot((near * inverse).astype(BF16), v_ref[rows, :], 0, 0)
            if i:
                result = result + dot((far * inverse).astype(BF16), v_ref[before, :], 0, 0)
            results.append(result)
            lse_ref[0, h : h + 1, rows] = highest + jnp.log(total)
        out_ref[rows, :] = jnp.where(lane < HEAD_DIM, results[0], results[1]).astype(BF16)


def pair_specs(length, pairs):
    return lambda off: pl.BlockSpec(
        (length, LANES), lambda g: (g // pairs, off * pairs + g % pairs)
    )


def attend(qkv, length, block, deps):
    width, sequences = qkv.shape[1] // 3, qkv.shape[0] // length
    pairs = width // LANES
    at = pair_specs(length, pairs)
    return call(
        functools.partial(attend_kernel, block),
        "attend",
        [qkv, qkv, qkv],
        deps,
        grid=(sequences * pairs,),
        in_specs=[at(0), at(1), at(2)],
        out_specs=[at(0), pl.BlockSpec((1, 8, length), lambda g: (g, 0, 0))],
        out_shape=[
            jax.ShapeDtypeStruct((qkv.shape[0], width), BF16),
            jax.ShapeDtypeStruct((sequences * pairs, 8, length), F32),
        ],
    )


def attend_back_kernel(
    block,
    q_ref,
    k_ref,
    v_ref,
    grad_ref,
    mixed_ref,
    lse_ref,
    cos_ref,
    left_ref,
    right_ref,
    gq_ref,
    gk_ref,
    gv_ref,
    sum_ref,
    gk_sum,
    gv_sum,
):
    length = q_ref.shape[0]
    lane = lax.broadcasted_iota(jnp.int32, (1, LANES), 1)
    key = lax.broadcasted_iota(jnp.int32, (block, block), 0)
    causal = key <= lax.broadcasted_iota(jnp.int32, (block, block), 1)
    count = length // block
    sum_ref[...] = jnp.zeros_like(sum_ref)

    def put(ref, which, rows, value):
        value = value.astype(BF16)
        ref[rows, :] = value
        sum_ref[0, which : which + 1, :] += jnp.sum(value.astype(F32), axis=0, keepdims=True)

    def unrotated(value, rows):
        return rotated(value, cos_ref[rows, :], left_ref[rows, :], right_ref[rows, :], -1.0)

    for i in reversed(range(count)):
        rows = pl.ds(i * block, block)
        product = grad_ref[rows, :].astype(F32) * mixed_ref[rows, :].astype(F32)
        gq = None
        for h in range(2):
            mine = (lane < HEAD_DIM) if h == 0 else (lane >= HEAD_DIM)
            query = jnp.where(mine, q_ref[rows, :], 0)
            grad = jnp.where(mine, grad_ref[rows, :], 0)
            ones = jnp.where(mine, jnp.ones((8, LANES), F32), 0.0)
            delta = lax.dot_general(
                ones,
                product,
                (((1,), (1,)), ((), ())),
                precision=lax.Precision.HIGHEST,
                preferred_element_type=F32,
            )[0:1, :]
            lse = lse_ref[0, h : h + 1, rows]
            for j in range(i + 1):
                keys = pl.ds(j * block, block)
                key_rows = k_ref[keys, :]
                probs = jnp.exp(dot(key_rows, query, 1, 1) - lse)
                if j == i:
                    probs = jnp.where(causal, probs, 0.0)
                gprobs = dot(v_ref[keys, :], grad, 1, 1)
                gscores = (probs * (gprobs - delta)).astype(BF16)
                gv, gk = dot(probs.astype(BF16), grad, 1, 0), dot(gscores, query, 1, 0)
                if i == count - 1 and h == 0:
                    gv_sum[keys, :] = gv
                    gk_sum[keys, :] = gk
                else:
                    gv_sum[keys, :] += gv
                    gk_sum[keys, :] += gk
                part = dot(gscores, jnp.where(mine, key_rows, 0), 0, 0)
                gq = part if gq is None else gq + part
        put(gq_ref, 0, rows, unrotated(gq * HEAD_DIM**-0.5, rows))
    for i in range(count):
        rows = pl.ds(i * block, block)
        put(gk_ref, 1, rows, unrotated(gk_sum[rows, :], rows))
        put(gv_ref, 2, rows, gv_sum[rows, :])


def attend_back(qkv, grad, mixed, lse, tables, length, block, deps):
    width, sequences = qkv.shape[1] // 3, qkv.shape[0] // length
    pairs = width // LANES
    at = pair_specs(length, pairs)
    table = pl.BlockSpec((length, LANES), lambda g: (0, 0))
    small = pl.BlockSpec((1, 8, length), lambda g: (g, 0, 0))
    return call(
        functools.partial(attend_back_kernel, block),
        "attend_back",
        [qkv, qkv, qkv, grad, mixed, lse, *tables],
        deps,
        grid=(sequences * pairs,),
        in_specs=[at(0), at(1), at(2), at(0), at(0), small, table, table, table],
        out_specs=[at(0)] * 3 + [pl.BlockSpec((1, 8, LANES), lambda g: (g, 0, 0))],
        out_shape=[jax.ShapeDtypeStruct((qkv.shape[0], width), BF16)] * 3
        + [jax.ShapeDtypeStruct((sequences * pairs, 8, LANES), F32)],
        scratch_shapes=[pltpu.VMEM((length, LANES), F32)] * 2,
    )


def quarter_map(places, parts):
    turns = len(places)

    def rows_of(i, at):
        offset = jnp.int32(places[0])
        for n in range(1, turns):
            offset = jnp.where(i % turns == n, places[n], offset)
        return jnp.where(i < turns, parts, 0) + (at[0] + offset) % parts

    return rows_of


def split_specs(rows, model, turns):
    return [
        pl.BlockSpec((1, rows, model), lambda i, at: (jnp.minimum(i, turns - 1), 0, 0)),
        pl.BlockSpec((1, rows, model), lambda i, at: (jnp.maximum(i - turns, 0), 0, 0)),
    ]


def branch_kernel(count, turns, at_ref, mixed_ref, act_ref, *rest):
    blocks, (other_ref, own_ref, held, sems) = rest[:count], rest[count:]
    step, size, me = pl.program_id(0), blocks[0].shape[1], lax.axis_index("dp")
    (loads,) = block_copies(blocks, lambda owner: held.at[:, span(owner, size)], sems)

    def rows():
        return jnp.concatenate([mixed_ref[...], act_ref[...]], axis=1)

    @pl.when(step == 0)
    def _():
        start_copies(loads)
        x = rows()
        for j, copy in enumerate(loads):
            copy.wait()
            columns = span(lax.bitwise_xor(me, j), size)
            other_ref[0, :, columns] = dot(x, held[:, columns], 1, 0).astype(BF16)

    @pl.when((step > 0) & (step < turns))
    def _():
        other_ref[0] = dot(rows(), held[...], 1, 0).astype(BF16)

    @pl.when(step >= turns)
    def _():
        own_ref[0] = dot(rows(), held[...], 1, 0).astype(BF16)


def branch_sums(at_mp, mixed, act, blocks, parts, places, deps):
    rows, count, turns = mixed.shape[0] // (2 * parts), len(blocks), len(places)
    inner, model = blocks[0].shape[0], count * blocks[0].shape[1]
    where = quarter_map(places, parts)
    return call(
        functools.partial(branch_kernel, count, turns),
        "branch_sums",
        [mixed, act, *blocks],
        deps,
        (at_mp,),
        grid=(2 * turns,),
        in_specs=[
            pl.BlockSpec((rows, a.shape[1]), lambda i, at: (where(i, at), 0)) for a in (mixed, act)
        ]
        + [HBM] * count,
        out_specs=split_specs(rows, model, turns),
        out_shape=[jax.ShapeDtypeStruct((turns, rows, model), BF16)] * 2,
        scratch_shapes=[pltpu.VMEM((inner, model), BF16), pltpu.SemaphoreType.DMA((1, count))],
    )


def grad_in_kernel(setup, at_ref, slope_ref, *rest):
    count, parts, places, width, hidden, groups = setup
    chunks, many = [], 0
    for shifts in groups:
        chunks.append(by_shift(rest[many:], shifts))
        many += len(shifts)
    blocks = rest[many : many + count]
    gmixed_ref, gpre_ref, dy_ref, gsum_ref, dsum_ref, held, dy_held, sems, dy_sems = rest[-9:]
    step, steps = pl.program_id(0), 2 * len(places)
    found = chunk_copies(chunks, places, parts, dy_held, dy_sems)
    size, tiles = blocks[0].shape[1], (width + hidden) // width
    row = lambda t: slice(t * width, (t + 1) * width)
    loads = block_copies(
        blocks,
        None,
        sems,
        lambda block, owner: [
            (block.at[row(t)], held.at[row(t), span(owner, size)]) for t in range(tiles)
        ],
    )

    @pl.when(step == 0)
    def _():
        start_all(found)
        for copies in loads:
            start_copies(copies)
        gsum_ref[...] = jnp.zeros_like(gsum_ref)
        dsum_ref[...] = jnp.zeros_like(dsum_ref)

    for slot in range(steps):

        @pl.when(step == slot)
        def _(slot=slot):
            wait_for(found[slot])

    dy = dy_held[step]
    dy_ref[...] = dy
    dsum_ref[0:1, :] += jnp.sum(dy.astype(F32), axis=0, keepdims=True)
    pl.when(step == 0)(functools.partial(wait_copies, loads[0]))
    gmixed_ref[...] = dot(dy, held[:width, :], 1, 1).astype(BF16)
    for t in range(1, tiles):
        part = row(t - 1)
        pl.when(step == 0)(functools.partial(wait_copies, loads[t]))
        gact = dot(dy, held[row(t), :], 1, 1)
        gpre = (gact * slope_ref[:, part].astype(F32)).astype(BF16)
        gpre_ref[:, part] = gpre
        gsum_ref[0:1, part] += jnp.sum(gpre.astype(F32), axis=0, keepdims=True)


def grad_in(at_mp, chunks, slope, blocks, width, parts, places, earlier, deps):
    model = len(blocks) * blocks[0].shape[1]
    hidden, length = slope.shape[1], slope.shape[0]
    rows, count, many = length // (2 * parts), len(blocks), sum(len(c) for c in chunks)
    turns = len(places)

    def where(i, at):
        m = jnp.int32(places[0])
        for n in range(1, turns):
            m = jnp.where(i % turns == n, places[n], m)
        return i // turns * parts + (at[0] ^ m)

    out = lambda w: pl.BlockSpec((rows, w), lambda i, at: (where(i, at), 0))
    total = lambda w: pl.BlockSpec((8, w), lambda i, at: (0, 0))
    setup = (count, parts, places, width, hidden, [shifts_of(c) for c in chunks])
    operands = [slope, *arrays_of(chunks[0]), *arrays_of(chunks[1]), *blocks]
    aliases = {1 + len(operands) + n: n for n in range(len(earlier))}
    return call(
        functools.partial(grad_in_kernel, setup),
        "grad_in",
        operands + list(earlier),
        deps,
        (at_mp,),
        grid=(2 * turns,),
        in_specs=[out(hidden)] + [HBM] * (many + count + len(earlier)),
        out_specs=[out(width), out(hidden), out(model), total(hidden), total(model)],
        out_shape=[jax.ShapeDtypeStruct((length, w), BF16) for w in (width, hidden, model)]
        + [jax.ShapeDtypeStruct((8, w), F32) for w in (hidden, model)],
        input_output_aliases=aliases,
        scratch_shapes=[
            pltpu.VMEM((width + hidden, model), BF16),
            pltpu.VMEM((2 * turns, rows, model), BF16),
            pltpu.SemaphoreType.DMA(((width + hidden) // width, count)),
            pltpu.SemaphoreType.DMA((2 * turns,)),
        ],
    )


def grad_normed_kernel(
    count, turns, at_ref, gq_ref, gk_ref, gv_ref, gpre_ref, tokens_ref, *rest
):
    blocks, (other_ref, own_ref, sum_ref, held, result, sems) = rest[:count], rest[count:]
    step, size, me = pl.program_id(0), blocks[0].shape[0], lax.axis_index("dp")
    (loads,) = block_copies(blocks, lambda owner: held.at[span(owner, size)], sems)

    def grads():
        return jnp.concatenate([gq_ref[...], gk_ref[...], gv_ref[...], gpre_ref[...]], axis=1)

    @pl.when(step == 0)
    def _():
        start_copies(loads)
        sum_ref[...] = jnp.zeros_like(sum_ref)
        g = grads()
        for j, copy in enumerate(loads):
            copy.wait()
            there = span(lax.bitwise_xor(me, j), size)
            result[:, there] = dot(g, held[there, :], 1, 1)

    @pl.when(step > 0)
    def _():
        result[...] = dot(grads(), held[...], 1, 1)

    sum_ref[0:1, :] += jnp.sum(result[...] * normalized(tokens_ref[...]), axis=0, keepdims=True)
    sum_ref[1:2, :] += jnp.sum(result[...], axis=0, keepdims=True)

    @pl.when(step < turns)
    def _():
        other_ref[0] = result[...].astype(BF16)

    @pl.when(step >= turns)
    def _():
        own_ref[0] = result[...].astype(BF16)


def grad_normed_sums(at_mp, gqkv, gpre, tokens, blocks, parts, places, deps):
    rows, count, turns = tokens.shape[0] // (2 * parts), len(blocks), len(places)
    model, total = tokens.shape[1], blocks[0].shape[1]
    where = quarter_map(places, parts)
    operands = [*gqkv, gpre, tokens]
    return call(
        functools.partial(grad_normed_kernel, count, turns),
        "grad_normed_sums",
        operands + list(blocks),
        deps,
        (at_mp,),
        grid=(2 * turns,),
        in_specs=[
            pl.BlockSpec((rows, a.shape[1]), lambda i, at: (where(i, at), 0)) for a in operands
        ]
        + [HBM] * count,
        out_specs=split_specs(rows, model, turns)
        + [pl.BlockSpec((8, model), lambda i, at: (0, 0))],
        out_shape=[jax.ShapeDtypeStruct((turns, rows, model), BF16)] * 2
        + [jax.ShapeDtypeStruct((8, model), F32)],
        scratch_shapes=[
            pltpu.VMEM((model, total), BF16),
            pltpu.VMEM((rows, model), F32),
            pltpu.SemaphoreType.DMA((1, count)),
        ],
    )


def weight_grad_kernel(sizes, left, tile, at_ref, cut_ref, *refs):
    *refs, held, grad, sems = refs
    whole, outs = refs[: len(refs) - len(sizes)], refs[len(refs) - len(sizes) :]
    step = pl.program_id(0)
    starts = [(ref, start) for ref in whole for start in range(0, ref.shape[1], tile)]
    place = lambda n: slice(n * tile, (n + 1) * tile)
    loads = [
        pltpu.make_async_copy(ref.at[:, start : start + tile], held.at[:, place(n)], sems.at[n])
        for n, (ref, start) in enumerate(starts)
    ]

    @pl.when(step == 0)
    def _():
        start_copies(loads)
        for n, copy in enumerate(loads):
            copy.wait()
            if left:
                grad[:, place(n)] = dot(cut_ref[...], held[:, place(n)], 0, 0).astype(BF16)
            else:
                grad[place(n), :] = dot(held[:, place(n)], cut_ref[...], 0, 0).astype(BF16)

    @pl.when(step > 0)
    def _():
        pair = (cut_ref[...], held[...]) if left else (held[...], cut_ref[...])
        grad[...] = dot(*pair, 0, 0).astype(BF16)

    first = 0
    for size, out_ref in zip(sizes, outs):

        @pl.when((step >= first) & (step < first + size))
        def _(out_ref=out_ref):
            out_ref[0] = grad[...]

        first += size


def weight_grads(me, xs, gs, count, deps, left):
    plan = scatter_plan(count)
    sets = [(half, s) for s in range(len(plan[0])) for half in range(2)]
    sizes = [len(plan[half][s]) for half, s in sets]
    order = [j for half, s in sets for j in plan[half][s]]
    owners = lax.bitwise_xor(me, jnp.array(order, jnp.int32))
    length, (cut, whole) = xs[0].shape[0], ((xs, gs) if left else (gs, xs))
    size = cut[0].shape[1] // count
    cut_spec = pl.BlockSpec((length, size), lambda i, at: (0, at[i]))
    full, tile = sum(a.shape[1] for a in whole), min(a.shape[1] for a in whole)
    shape = (size, full) if left else (full, size)

    def out(first, many):
        return pl.BlockSpec(
            (1, *shape), lambda i, at: (jnp.clip(i - first, 0, many - 1), 0, 0)
        )

    firsts = [sum(sizes[:n]) for n in range(len(sizes))]
    outs = call(
        functools.partial(weight_grad_kernel, sizes, left, min(tile, 256)),
        "weight_grads",
        [*cut, *whole],
        deps,
        (owners,),
        grid=(count,),
        in_specs=[cut_spec] + [HBM] * len(whole),
        out_specs=[out(first, many) for first, many in zip(firsts, sizes)],
        out_shape=[jax.ShapeDtypeStruct((many, *shape), BF16) for many in sizes],
        scratch_shapes=[
            pltpu.VMEM((length, full), BF16),
            pltpu.VMEM(shape, BF16),
            pltpu.SemaphoreType.DMA((full // min(tile, 256),)),
        ],
    )
    return [[o for o, (half, _) in zip(outs, sets) if half == h] for h in range(2)]


def across(value, bit, count):
    return lax.ppermute(value, "dp", [(i, i ^ bit) for i in range(count)])


def ring(value, k, parts):
    return lax.ppermute(value, "mp", [(i, (i + k) % parts) for i in range(parts)])


def near_shifts(parts):
    return (1, 3) if parts == 4 else tuple(range(1, parts))


def gather_far(chunks, parts):
    if parts != 4:
        return None
    up = lax.ppermute(chunks[1], "mp", [(1, 2), (2, 3)])
    down = lax.ppermute(chunks[3], "mp", [(1, 0), (2, 1)])
    return up + down


def added(addends):
    return sum(a.astype(F32) for a in addends).astype(BF16)


def send_far(farthest):
    up = lax.ppermute(farthest, "mp", [(0, 1), (1, 2)])
    down = lax.ppermute(farthest, "mp", [(3, 2), (2, 1)])
    return [up, down]


def chip_bits(count):
    bits, bit = [], 2
    while bit < count:
        bits.append(bit)
        bit *= 2
    return bits


class BlockGather:
    def __init__(self, own, sibling, count):
        self.held, self.count = {0: own, 1: sibling}, count
        self.orders = (chip_bits(count), chip_bits(count)[::-1])

    def own_to(self, s):
        if s < len(self.orders[0]):
            for half in range(2):
                bit = self.orders[half][s]
                self.held[half ^ bit] = across(self.held[half], bit, self.count)

    def rest(self):
        for s in range(1, len(self.orders[0])):
            for half in range(2):
                order = self.orders[half]
                for j in [j for j in self.held if j % 2 == half]:
                    if j ^ order[s] not in self.held and not any(j & b for b in order[s:]):
                        self.held[j ^ order[s]] = across(self.held[j], order[s], self.count)

    def fenced(self, others=(), deps=()):
        keys = sorted(self.held)
        values = fence([self.held[j] for j in keys] + list(others), deps)
        self.held = dict(zip(keys, values))
        return values[len(keys) :]

    def blocks(self):
        return [self.held[j] for j in range(self.count)]


def scatter_orders(count):
    return (chip_bits(count)[::-1], chip_bits(count))


def scatter_plan(count):
    plan = []
    for half, order in enumerate(scatter_orders(count)):
        sets, rest = [[half]], [half]
        for bit in reversed(order):
            sets.insert(0, [j ^ bit for j in rest])
            rest = sets[0] + rest
        plan.append(sets)
    return plan


class BlockScatter:
    def __init__(self, halves, count):
        self.count, self.orders = count, scatter_orders(count)
        self.held = [[[a] for a in arrays] for arrays in halves]
        self.steps = len(self.orders[0])

    def total(self, half, s):
        if len(self.held[half][s]) > 1:
            self.held[half][s] = [added(self.held[half][s])]
        return self.held[half][s][0]

    def ready(self, s):
        return [self.total(half, s) for half in range(2)]

    def send(self, s):
        return [across(self.total(h, s), self.orders[h][s], self.count) for h in range(2)]

    def arrive(self, s, came):
        for half in range(2):
            first = 0
            for later in self.held[half][s + 1 :]:
                many = later[0].shape[0]
                later.append(came[half][first : first + many])
                first += many

    def between(self):
        for s in range(1, self.steps - 1):
            self.arrive(s, self.send(s))

    def last(self):
        return self.total(1, -1)[0]

    def finish(self, theirs):
        return sum(a[0].astype(F32) for a in self.held[0][-1]), theirs.astype(F32)


def on_device(
    tokens,
    norm_gain,
    norm_bias,
    qkv_weight,
    qkv_bias,
    dense_weight,
    dense_bias,
    up_weight,
    up_bias,
    down_weight,
    down_bias,
    cotangent,
    *,
    ndp,
    nmp,
):
    me, z = lax.axis_index("dp"), lax.axis_index("mp")
    core = me % 2
    at_mp = z.astype(jnp.int32)[None]
    length, model = tokens.shape[0] * nmp, tokens.shape[1]
    block = min(512, length)
    width, hidden = qkv_weight.shape[2] // 2, up_weight.shape[1] // 2
    chip_steps = len(chip_bits(ndp))
    rank = lambda array, axis, which, size: lax.dynamic_slice_in_dim(
        array, which * size, size, axis
    )

    def row_pack(which):
        qkv = rank(qkv_weight, 2, which, width)
        return jnp.concatenate([qkv[0], qkv[1], qkv[2], rank(up_weight, 1, which, hidden)], axis=1)

    def column_pack(which):
        return jnp.concatenate(
            [rank(dense_weight, 0, which, width), rank(down_weight, 0, which, hidden)], axis=0
        )

    def stage(*arrays):
        return jnp.stack(arrays), tuple([0, *near])

    near, places, pairs = near_shifts(nmp), list(range(nmp)), width // LANES
    rows = BlockGather(row_pack(core), across(row_pack(1 - core), 1, ndp), ndp)
    columns = BlockGather(column_pack(core), across(column_pack(1 - core), 1, ndp), ndp)
    head, tail = near[0], near[1:]
    came = {head: ring(tokens, head, nmp)}
    rows.own_to(0)
    came[head], begun = rows.fenced([came[head], tokens], columns.held.values())
    came.update({k: ring(begun, k, nmp) for k in tail})
    rows.own_to(1)
    *held, cot = rows.fenced([*came.values(), cotangent])
    came = dict(zip(near, held))
    own = [(tokens, (0,))] + [(came[k], (k,)) for k in near]
    packed, shifts = stage(tokens, *held)
    other = [(across(packed, 1, ndp), shifts)]
    far = gather_far(came, nmp)
    rows.rest()
    cot, *held = rows.fenced(
        [cot, columns.held[0], columns.held[1]] + ([far] if nmp == 4 else []), [other[0][0]]
    )
    columns.held = dict(enumerate(held[:2]))
    if nmp == 4:
        own.append((held[2], (2,)))
        other.append((across(held[2], 1, ndp), (2,)))

    tables = rotary_tables(length)
    bias = jnp.concatenate(
        [
            rank(qkv_bias, 1, core, width).astype(F32).reshape(1, 3 * width),
            rank(up_bias[None, :], 1, core, hidden).astype(F32),
        ],
        axis=1,
    )
    gain, shift = norm_gain.astype(F32)[None, :], norm_bias.astype(F32)[None, :]
    came = {head: ring(cot, head, nmp)}
    columns.own_to(0)
    common = (rows.blocks(), bias, gain, shift, tables, width, nmp)
    first = project(at_mp, 0, own, *common, (), [cot])
    cot, came[head] = columns.fenced([cot, came[head]], [first[0]])
    came.update({k: ring(cot, k, nmp) for k in tail})
    columns.own_to(1)
    qkv, act, slope, normed, token_rows = project(
        at_mp, 1, other, *common, first, [columns.held[0]]
    )
    columns.fenced(deps=[qkv])
    columns.rest()
    mixed, lse = attend(qkv, length, block, [columns.held[0]])
    held = columns.fenced(came.values(), [mixed])
    came = dict(zip(near, held))
    dy_own = [(cot, (0,))] + [(came[k], (k,)) for k in near]
    packed, shifts = stage(cot, *held)
    dy_packed = across(packed, 1, ndp)
    far = gather_far(came, nmp)
    other_sums, own_sums = branch_sums(
        at_mp, mixed, act, columns.blocks(), nmp, places, [packed]
    )
    dy_packed, other_sums, *far = fence(
        [dy_packed, other_sums] + ([far] if nmp == 4 else []), [own_sums]
    )
    theirs = across(other_sums, 1, ndp)

    dy_other = [(dy_packed, shifts)]
    grad_a = grad_in(
        at_mp, (dy_own, dy_other), slope, columns.blocks(), width, nmp, (0, 1), (), [other_sums]
    )
    far_other = [across(a, 1, ndp) for a in far]
    theirs, *far_other = fence([theirs, *far_other], [grad_a[3]])
    shares = [[own_sums[k], theirs[k]] for k in places]
    farthest = [added(shares[2])] if nmp == 4 else []
    moved = [a for f in farthest for a in send_far(f)]
    grad_b = grad_in(
        at_mp,
        (dy_own + [(a, (2,)) for a in far], dy_other + [(a, (2,)) for a in far_other]),
        slope,
        columns.blocks(),
        width,
        nmp,
        tuple(places[2:]),
        grad_a[:3],
        [grad_a[3], *farthest],
    )
    gmixed, gpre, dy = grad_b[:3]
    column_grads = BlockScatter(
        weight_grads(me, [mixed, act], [dy], ndp, [grad_b[3]], left=False), ndp
    )

    def with_far(shares, moved):
        if moved:
            shares[1], shares[3] = shares[1] + [moved[0]], shares[3] + [moved[1]]
        return {k: added(shares[k]) for k in near}

    if moved:
        moved = fence(moved, [column_grads.held[0][0][0]])
    sums = with_far(shares, moved)
    brought = [ring(sums[head], head, nmp)]
    column_came = column_grads.send(0)
    gq, gk, gv, qkv_sums = attend_back(
        qkv,
        gmixed,
        mixed,
        lse,
        tables,
        length,
        block,
        [column_grads.held[0][0][0], *sums.values()],
    )
    brought[0], *held = fence([brought[0], *(sums[k] for k in tail)], [gq])
    brought += [ring(a, k, nmp) for k, a in zip(tail, held)]

    def normed_part(part, deps):
        return grad_normed_sums(
            at_mp, (gq, gk, gv), gpre, token_rows, rows.blocks(), nmp, part, deps
        )

    thirds = ([2], [1, 3], [0]) if nmp == 4 else (places[1:2], places[2:], places[:1])
    other_a, own_a, sums_a = normed_part(thirds[0], [brought[0]])
    *column_came, other_a = fence([*column_came, other_a], [sums_a])
    column_grads.arrive(0, column_came)
    column_grads.between()
    column_came = column_grads.send(-1 + chip_steps)
    most = other_a.shape[1] // 2
    came_a = [across(p, 1, ndp) for p in (other_a[:, :most], other_a[:, most:])]
    other_b, own_b, sums_b = normed_part(
        thirds[1], [sums_a, *column_grads.ready(chip_steps - 1)]
    )
    brought[1:] = fence(brought[1:], [sums_b])
    c0, c1, a0, a1, other_b = fence([*column_came, *came_a, other_b], [brought[1]])
    column_grads.arrive(chip_steps - 1, [c0, c1])
    came_a = jnp.concatenate([a0, a1], axis=1)
    came_b = across(other_b, 1, ndp)
    shares = [[] for _ in places]
    for part, kept, got in ((thirds[0], own_a, came_a),):
        for n, k in enumerate(part):
            shares[k] = [kept[n], got[n]]
    farthest = [added(shares[2])] if nmp == 4 else []
    moved = [a for f in farthest for a in send_far(f)]
    other_c, own_c, sums_c = normed_part(
        thirds[2], [sums_b, *farthest, column_grads.last()]
    )
    qkv_sum = (
        qkv_sums.reshape(2, pairs, 8, LANES).sum(0)[:, :3, :].transpose(1, 0, 2).reshape(3 * width)
    )
    norm_sums = (sums_a + sums_b + sums_c)[:2].reshape(2 * model)
    small = jnp.concatenate(
        [norm_sums, qkv_sum, grad_a[3][0] + grad_b[3][0], grad_a[4][0] + grad_b[4][0]]
    )
    bits = chip_bits(ndp)
    for bit in bits[:-2]:
        small = small + across(small, bit, ndp)
    small_came = across(small, bits[-2], ndp)
    up_grads = BlockScatter(
        weight_grads(me, [normed], [gpre], ndp, [sums_c, small], left=True), ndp
    )
    came_b, other_c, column_last, small_came, *moved = fence(
        [came_b, other_c, column_grads.last(), small_came, *moved], [up_grads.held[0][0][0]]
    )
    small = small + small_came
    small_came = across(small, bits[-1], ndp)
    up_came = up_grads.send(0)
    for n, k in enumerate(thirds[1]):
        shares[k] = [own_b[n], came_b[n]]
    sums = with_far(shares, moved)
    came = {head: ring(sums[head], head, nmp)}
    column_theirs = across(column_last, 1, ndp)
    qkv_grads = BlockScatter(
        weight_grads(me, [normed], [gq, gk, gv], ndp, [small, *sums.values()], left=True), ndp
    )
    *up_came, q0, q1, column_theirs, small_came = fence(
        [*up_came, qkv_grads.held[0][0][0], qkv_grads.held[1][0][0], column_theirs, small_came]
    )
    qkv_grads.held[0][0], qkv_grads.held[1][0] = [q0], [q1]
    up_grads.arrive(0, up_came)
    up_grads.between()
    up_came = up_grads.send(chip_steps - 1)
    qkv_came = qkv_grads.send(0)
    small = small + small_came
    came[head], other_c, small, *held = fence(
        [came[head], other_c, small, *(sums[k] for k in tail)], [q0]
    )
    half = held[0].shape[0] // 2
    early = [ring(a[:half], k, nmp) for k, a in zip(tail, held)]
    u0, u1, small, *qkv_came = fence([*up_came, small, *qkv_came], [came[head]])
    small_other = across(small, 1, ndp)
    up_grads.arrive(chip_steps - 1, [u0, u1])
    up_theirs = across(up_grads.last(), 1, ndp)
    qkv_grads.arrive(0, qkv_came)
    qkv_grads.between()
    late = fence([*early, *(a[half:] for a in held)])
    early, late = late[: len(tail)], late[len(tail) :]
    late = [ring(a, k, nmp) for k, a in zip(tail, late)]
    came.update({k: jnp.concatenate(pair) for k, *pair in zip(tail, early, late)})
    came_c = across(other_c, 1, ndp)
    qkv_grads.arrive(chip_steps - 1, qkv_grads.send(chip_steps - 1))
    qkv_theirs = across(qkv_grads.last(), 1, ndp)
    norm_sums = small[: 2 * model] + small_other[: 2 * model]
    norm_sums = [norm_sums] + [
        lax.ppermute(norm_sums, "mp", [(i, i ^ j) for i in range(nmp)]) for j in range(1, nmp)
    ]
    while len(norm_sums) > 1:
        norm_sums = [a + b for a, b in zip(norm_sums[::2], norm_sums[1::2])]
    norm_sums = norm_sums[0]

    local_inputs = tokens.astype(F32)
    output = (
        local_inputs
        + sum(a.astype(F32) for a in [own_sums[0], theirs[0], *brought])
        + (dense_bias.astype(F32) + down_bias.astype(F32))[None, :]
    ).astype(BF16)

    def both(mine, theirs, axis):
        return jnp.where(
            core == 0,
            jnp.concatenate([mine, theirs], axis=axis),
            jnp.concatenate([theirs, mine], axis=axis),
        )

    mine, theirs = column_grads.finish(column_theirs)
    owned_dense = both(mine[:width], theirs[:width], 0)
    owned_down = both(mine[width:], theirs[width:], 0)
    owned_up = both(*up_grads.finish(up_theirs), 1)
    mine, theirs = qkv_grads.finish(qkv_theirs)
    owned_qkv = jnp.stack(
        [
            both(mine[:, c * width : (c + 1) * width], theirs[:, c * width : (c + 1) * width], 1)
            for c in range(3)
        ]
    )

    inner = 3 * width + hidden
    grad_out_bias = small[2 * model + inner :]
    here, there = (a[2 * model : 2 * model + inner] for a in (small, small_other))
    even, odd = jnp.where(core == 0, here, there), jnp.where(core == 0, there, here)
    grad_qkv_bias = jnp.concatenate(
        [a[: 3 * width].reshape(3, width) for a in (even, odd)], axis=1
    )
    grad_up_bias = jnp.concatenate([even[3 * width :], odd[3 * width :]])

    centered = local_inputs - jnp.mean(local_inputs, axis=1, keepdims=True)
    inverse_std = lax.rsqrt(jnp.mean(centered * centered, axis=1, keepdims=True) + EPS)
    normal_rows = centered * inverse_std
    grad_rows = sum(a.astype(F32) for a in [own_c[0], came_c[0], *came.values()])
    scaled = grad_rows * gain
    first_mean = jnp.mean(scaled, axis=1, keepdims=True)
    second_mean = jnp.mean(scaled * normal_rows, axis=1, keepdims=True)
    grad_tokens = (
        cotangent.astype(F32) + (scaled - first_mean - normal_rows * second_mean) * inverse_std
    ).astype(BF16)
    return (
        output,
        grad_tokens,
        norm_sums[:model],
        norm_sums[model:],
        owned_qkv,
        grad_qkv_bias,
        owned_dense,
        grad_out_bias,
        owned_up,
        grad_up_bias,
        owned_down,
        grad_out_bias,
    )


def solution(mesh):
    return jax.shard_map(
        functools.partial(on_device, ndp=mesh.shape["dp"], nmp=mesh.shape["mp"]),
        mesh=mesh,
        in_specs=(
            P(("dp", "mp"), None),
            P(),
            P(),
            P(None, "dp", "mp"),
            P(None, "mp"),
            P("mp", "dp"),
            P(),
            P("dp", "mp"),
            P("mp"),
            P("mp", "dp"),
            P(),
            P(("dp", "mp"), None),
        ),
        out_specs=(
            P(("dp", "mp"), None),
            P(("dp", "mp"), None),
            P(),
            P(),
            P(None, "dp", "mp"),
            P(None, "mp"),
            P("mp", "dp"),
            P(),
            P("dp", "mp"),
            P("mp"),
            P("mp", "dp"),
            P(),
        ),
        check_vma=False,
    )
```

```python
import functools

import jax
import jax.numpy as jnp
import numpy as np
from jax import lax
from jax.experimental import pallas as pl
from jax.experimental.pallas import tpu as pltpu
from jax.sharding import PartitionSpec as P

HEAD_DIM = 64
ROT = 32
EPS = 1e-05
LANES = 128
F32 = jnp.float32
BF16 = jnp.bfloat16
ANY = pl.BlockSpec(memory_space=pl.ANY)


def dot(lhs, rhs, lhs_dim, rhs_dim):
    return lax.dot_general(
        lhs, rhs, (((lhs_dim,), (rhs_dim,)), ((), ())), preferred_element_type=F32
    )


def call(kernel, name, operands, deps=(), scalars=(), vmem=63, **spec):
    deps, many, lead = tuple(deps), len(operands), len(scalars)

    def body(*refs):
        kernel(*refs[: lead + many], *refs[lead + many + len(deps) :])

    in_specs = list(spec.pop("in_specs")) + [ANY] * len(deps)
    out_shape, aliases = spec.pop("out_shape"), spec.pop("input_output_aliases", {})
    if scalars:
        grid_spec = pltpu.PrefetchScalarGridSpec(
            num_scalar_prefetch=lead, in_specs=in_specs, **spec
        )
        spec = {"grid_spec": grid_spec}
    else:
        spec["in_specs"] = in_specs
    return pl.pallas_call(
        body,
        out_shape=out_shape,
        input_output_aliases=aliases,
        compiler_params=pltpu.CompilerParams(vmem_limit_bytes=vmem << 20),
        cost_estimate=pl.CostEstimate(flops=0, transcendentals=0, bytes_accessed=0),
        name=name,
        **spec,
    )(*scalars, *operands, *deps)


def fence(values, deps=()):
    return call(
        lambda *refs: None,
        "fence",
        values,
        deps,
        vmem=2,
        in_specs=[ANY] * len(values),
        out_specs=[ANY] * len(values),
        out_shape=[jax.ShapeDtypeStruct(v.shape, v.dtype) for v in values],
        input_output_aliases={n: n for n in range(len(values))},
    )


def rotary_tables(length):
    positions = np.arange(length, dtype=np.float32)
    frequency = 10000.0 ** (-np.arange(ROT // 2, dtype=np.float64) * 2.0 / ROT)
    angles = positions[:, None] * frequency.astype(np.float32)[None, :]
    cosine, sine = np.cos(angles.astype(np.float64)), np.sin(angles.astype(np.float64))
    rest = HEAD_DIM - ROT
    none = np.zeros((length, ROT // 2))
    ones, zeros = np.ones((length, rest)), np.zeros((length, rest))
    straight = np.concatenate([cosine, cosine, ones], axis=1)
    left = np.concatenate([-sine, none, zeros], axis=1)
    right = np.concatenate([none, sine, zeros], axis=1)
    return [
        jnp.asarray(np.concatenate([t, t], axis=1).astype(np.float32))
        for t in (straight, left, right)
    ]


def rotated(u, straight, left, right, sign):
    half = ROT // 2
    turned = pltpu.roll(u, LANES - half, 1) * left + pltpu.roll(u, half, 1) * right
    return u * straight + sign * turned


def normalized(x):
    x = x.astype(F32)
    centered = x - jnp.mean(x, axis=1, keepdims=True)
    variance = jnp.mean(centered * centered, axis=1, keepdims=True)
    return centered * lax.rsqrt(variance + EPS)


def block_copies(blocks, place, sems):
    me = lax.axis_index("dp")
    return [
        pltpu.make_async_copy(block, place(lax.bitwise_xor(me, j)), sems.at[j])
        for j, block in enumerate(blocks)
    ]


def span(owner, size):
    return pl.ds(pl.multiple_of(owner * size, size), size)


def rows_at(ref, size):
    return lambda owner: ref.at[pl.ds(pl.multiple_of(owner * size, size), size)]


def columns_at(ref, size):
    return lambda owner: ref.at[:, pl.ds(pl.multiple_of(owner * size, size), size)]


def arrays_of(chunks):
    return [array for array, _ in chunks]


def shifts_of(chunks):
    return tuple(shifts for _, shifts in chunks)


def by_shift(refs, shifts):
    found = {}
    for ref, group in zip(refs, shifts):
        for n, k in enumerate(group):
            found[k] = ref if len(group) == 1 else ref.at[n]
    return found


def chunk_copies(chunks, places, parts, held, sems):
    z = lax.axis_index("mp")
    found = []
    for s, sequence in enumerate(chunks):
        for i, m in enumerate(places):
            slot, options = s * len(places) + i, []
            for k in sorted({(at - (at ^ m)) % parts for at in range(parts)}):
                here = lax.rem(z - lax.bitwise_xor(z, m) + parts, parts) == k
                options.append((here if k else None, sequence[k]))
            found.append(
                [
                    (here, pltpu.make_async_copy(source, held.at[slot], sems.at[slot]))
                    for here, source in options
                ]
            )
    return found


def start_all(found):
    for options in found:
        for here, copy in options:
            if here is None:
                copy.start()
            else:
                pl.when(here)(copy.start)


def wait_for(options):
    options[0][1].wait()


def project_kernel(setup, at_ref, bias_ref, gain_ref, shift_ref, cos_ref, left_ref, right_ref, *rest):
    count, parts, places, width, hidden, shifts = setup
    chunks = [by_shift(rest, shifts)]
    blocks = rest[len(shifts) : len(shifts) + count]
    qkv_ref, act_ref, slope_ref, normed_ref, tokens_ref, held, x_held, ready, sems, x_sems = rest[-10:]
    step, steps = pl.program_id(0), len(places)
    found = chunk_copies(chunks, places, parts, x_held, x_sems)
    loads = block_copies(blocks, rows_at(held, blocks[0].shape[0]), sems)

    def norm(slot):
        return (normalized(x_held[slot]) * gain_ref[...] + shift_ref[...]).astype(BF16)

    @pl.when(step == 0)
    def _():
        for copy in loads:
            copy.start()
        start_all(found)
        wait_for(found[0])
        ready[0] = norm(0)
        for copy in loads:
            copy.wait()

    for slot in range(1, steps):

        @pl.when(step == slot - 1)
        def _(slot=slot):
            wait_for(found[slot])

    x = ready[step % 2]
    normed_ref[...] = x
    tokens_ref[...] = x_held[step]
    ready[(step + 1) % 2] = norm((step + 1) % steps)
    root = 0.7978845608028654
    for t in range((3 * width + hidden) // width):
        columns = slice(t * width, (t + 1) * width)
        y = dot(x, held[:, columns], 1, 0) + bias_ref[:, columns]
        if t < 3:
            for g in range(width // LANES):
                part = y[:, g * LANES : (g + 1) * LANES]
                if t < 2:
                    part = rotated(part, cos_ref[...], left_ref[...], right_ref[...], 1.0)
                if t == 0:
                    part = part * HEAD_DIM**-0.5
                start = t * width + g * LANES
                qkv_ref[:, start : start + LANES] = part.astype(BF16)
        else:
            columns = slice((t - 3) * width, (t - 2) * width)
            square = y * y
            turn = jnp.tanh(root * y * (1.0 + 0.044715 * square))
            half = 0.5 * (1.0 + turn)
            act_ref[:, columns] = (y * half).astype(BF16)
            slope = half * (1.0 + y * (1.0 - turn) * (root + (3.0 * 0.044715 * root) * square))
            slope_ref[:, columns] = slope.astype(BF16)


def project(at_mp, sequence, chunks, blocks, bias, gain, shift, tables, width, parts, earlier, deps):
    places, total = tuple(range(parts)), blocks[0].shape[1]
    rows, model, count = tables[0].shape[0] // parts, gain.shape[1], len(blocks)
    hidden = total - 3 * width
    table = pl.BlockSpec((rows, LANES), lambda i, at: (at[0] ^ i, 0))
    out = lambda w: pl.BlockSpec((rows, w), lambda i, at: (sequence * parts + (at[0] ^ i), 0))
    line = lambda a: pl.BlockSpec(a.shape, lambda i, at: (0, 0))
    widths = (3 * width, hidden, hidden, model, model)
    setup = (count, parts, places, width, hidden, shifts_of(chunks))
    operands = [bias, gain, shift, *tables, *arrays_of(chunks), *blocks]
    return call(
        functools.partial(project_kernel, setup),
        "project",
        operands + list(earlier),
        deps,
        (at_mp,),
        grid=(parts,),
        in_specs=[line(bias), line(gain), line(shift), table, table, table]
        + [ANY] * (len(chunks) + count + len(earlier)),
        out_specs=[out(w) for w in widths],
        out_shape=[jax.ShapeDtypeStruct((2 * parts * rows, w), BF16) for w in widths],
        input_output_aliases={1 + len(operands) + n: n for n in range(len(earlier))},
        scratch_shapes=[
            pltpu.VMEM((model, total), BF16),
            pltpu.VMEM((parts, rows, model), BF16),
            pltpu.VMEM((2, rows, model), BF16),
            pltpu.SemaphoreType.DMA((count,)),
            pltpu.SemaphoreType.DMA((parts,)),
        ],
    )


def attend_kernel(block, q_ref, k_ref, v_ref, out_ref, lse_ref):
    length = q_ref.shape[0]
    lane = lax.broadcasted_iota(jnp.int32, (1, LANES), 1)
    key = lax.broadcasted_iota(jnp.int32, (block, block), 0)
    causal = key <= lax.broadcasted_iota(jnp.int32, (block, block), 1)
    for i in range(length // block):
        rows, before = pl.ds(i * block, block), pl.ds(0, i * block)
        results = []
        for h in range(2):
            mine = (lane < HEAD_DIM) if h == 0 else (lane >= HEAD_DIM)
            query = jnp.where(mine, q_ref[rows, :], 0)
            near = jnp.where(causal, dot(k_ref[rows, :], query, 1, 1), -1e30)
            highest = jnp.max(near, axis=0, keepdims=True)
            if i:
                far = dot(k_ref[before, :], query, 1, 1)
                highest = jnp.maximum(highest, jnp.max(far, axis=0, keepdims=True))
            near = jnp.exp(near - highest)
            total = jnp.sum(near, axis=0, keepdims=True)
            if i:
                far = jnp.exp(far - highest)
                total = total + jnp.sum(far, axis=0, keepdims=True)
            inverse = 1.0 / total
            result = dot((near * inverse).astype(BF16), v_ref[rows, :], 0, 0)
            if i:
                result = result + dot((far * inverse).astype(BF16), v_ref[before, :], 0, 0)
            results.append(result)
            lse_ref[0, h : h + 1, rows] = highest + jnp.log(total)
        out_ref[rows, :] = jnp.where(lane < HEAD_DIM, results[0], results[1]).astype(BF16)


def pair_specs(length, pairs):
    return lambda off: pl.BlockSpec(
        (length, LANES), lambda g: (g // pairs, off * pairs + g % pairs)
    )


def attend(qkv, length, block, deps):
    width, sequences = qkv.shape[1] // 3, qkv.shape[0] // length
    pairs = width // LANES
    at = pair_specs(length, pairs)
    return call(
        functools.partial(attend_kernel, block),
        "attend",
        [qkv, qkv, qkv],
        deps,
        grid=(sequences * pairs,),
        in_specs=[at(0), at(1), at(2)],
        out_specs=[at(0), pl.BlockSpec((1, 8, length), lambda g: (g, 0, 0))],
        out_shape=[
            jax.ShapeDtypeStruct((qkv.shape[0], width), BF16),
            jax.ShapeDtypeStruct((sequences * pairs, 8, length), F32),
        ],
    )


def attend_back_kernel(
    block,
    q_ref,
    k_ref,
    v_ref,
    grad_ref,
    mixed_ref,
    lse_ref,
    cos_ref,
    left_ref,
    right_ref,
    gq_ref,
    gk_ref,
    gv_ref,
    sum_ref,
    gk_sum,
    gv_sum,
):
    length = q_ref.shape[0]
    lane = lax.broadcasted_iota(jnp.int32, (1, LANES), 1)
    key = lax.broadcasted_iota(jnp.int32, (block, block), 0)
    causal = key <= lax.broadcasted_iota(jnp.int32, (block, block), 1)
    count = length // block
    sum_ref[...] = jnp.zeros_like(sum_ref)

    def put(ref, which, rows, value):
        value = value.astype(BF16)
        ref[rows, :] = value
        sum_ref[0, which : which + 1, :] += jnp.sum(value.astype(F32), axis=0, keepdims=True)

    def unrotated(value, rows):
        return rotated(value, cos_ref[rows, :], left_ref[rows, :], right_ref[rows, :], -1.0)

    for i in reversed(range(count)):
        rows = pl.ds(i * block, block)
        product = grad_ref[rows, :].astype(F32) * mixed_ref[rows, :].astype(F32)
        gq = None
        for h in range(2):
            mine = (lane < HEAD_DIM) if h == 0 else (lane >= HEAD_DIM)
            query = jnp.where(mine, q_ref[rows, :], 0)
            grad = jnp.where(mine, grad_ref[rows, :], 0)
            ones = jnp.where(mine, jnp.ones((8, LANES), F32), 0.0)
            delta = lax.dot_general(
                ones,
                product,
                (((1,), (1,)), ((), ())),
                precision=lax.Precision.HIGHEST,
                preferred_element_type=F32,
            )[0:1, :]
            lse = lse_ref[0, h : h + 1, rows]
            for j in range(i + 1):
                keys = pl.ds(j * block, block)
                key_rows = k_ref[keys, :]
                probs = jnp.exp(dot(key_rows, query, 1, 1) - lse)
                if j == i:
                    probs = jnp.where(causal, probs, 0.0)
                gprobs = dot(v_ref[keys, :], grad, 1, 1)
                gscores = (probs * (gprobs - delta)).astype(BF16)
                gv, gk = dot(probs.astype(BF16), grad, 1, 0), dot(gscores, query, 1, 0)
                if i == count - 1 and h == 0:
                    gv_sum[keys, :] = gv
                    gk_sum[keys, :] = gk
                else:
                    gv_sum[keys, :] += gv
                    gk_sum[keys, :] += gk
                part = dot(gscores, jnp.where(mine, key_rows, 0), 0, 0)
                gq = part if gq is None else gq + part
        put(gq_ref, 0, rows, unrotated(gq * HEAD_DIM**-0.5, rows))
    for i in range(count):
        rows = pl.ds(i * block, block)
        put(gk_ref, 1, rows, unrotated(gk_sum[rows, :], rows))
        put(gv_ref, 2, rows, gv_sum[rows, :])


def attend_back(qkv, grad, mixed, lse, tables, length, block, deps):
    width, sequences = qkv.shape[1] // 3, qkv.shape[0] // length
    pairs = width // LANES
    at = pair_specs(length, pairs)
    table = pl.BlockSpec((length, LANES), lambda g: (0, 0))
    small = pl.BlockSpec((1, 8, length), lambda g: (g, 0, 0))
    return call(
        functools.partial(attend_back_kernel, block),
        "attend_back",
        [qkv, qkv, qkv, grad, mixed, lse, *tables],
        deps,
        grid=(sequences * pairs,),
        in_specs=[at(0), at(1), at(2), at(0), at(0), small, table, table, table],
        out_specs=[at(0)] * 3 + [pl.BlockSpec((1, 8, LANES), lambda g: (g, 0, 0))],
        out_shape=[jax.ShapeDtypeStruct((qkv.shape[0], width), BF16)] * 3
        + [jax.ShapeDtypeStruct((sequences * pairs, 8, LANES), F32)],
        scratch_shapes=[pltpu.VMEM((length, LANES), F32)] * 2,
    )


def quarter_map(places, parts):
    turns = len(places)

    def rows_of(i, at):
        offset = jnp.int32(places[0])
        for n in range(1, turns):
            offset = jnp.where(i % turns == n, places[n], offset)
        return jnp.where(i < turns, parts, 0) + (at[0] + offset) % parts

    return rows_of


def split_outputs(step, turns, result, other_ref, own_ref):
    @pl.when(step < turns)
    def _():
        other_ref[0] = result

    @pl.when(step >= turns)
    def _():
        own_ref[0] = result


def split_specs(rows, model, turns):
    return [
        pl.BlockSpec((1, rows, model), lambda i, at: (jnp.minimum(i, turns - 1), 0, 0)),
        pl.BlockSpec((1, rows, model), lambda i, at: (jnp.maximum(i - turns, 0), 0, 0)),
    ]


def branch_kernel(count, turns, at_ref, mixed_ref, act_ref, *rest):
    blocks, (other_ref, own_ref, held, sems) = rest[:count], rest[count:]
    step = pl.program_id(0)

    @pl.when(step == 0)
    def _():
        loads = block_copies(blocks, columns_at(held, blocks[0].shape[1]), sems)
        for copy in loads:
            copy.start()
        for copy in loads:
            copy.wait()

    x = jnp.concatenate([mixed_ref[...], act_ref[...]], axis=1)
    split_outputs(step, turns, dot(x, held[...], 1, 0).astype(BF16), other_ref, own_ref)


def branch_sums(at_mp, mixed, act, blocks, parts, places, deps):
    rows, count, turns = mixed.shape[0] // (2 * parts), len(blocks), len(places)
    inner, model = blocks[0].shape[0], count * blocks[0].shape[1]
    where = quarter_map(places, parts)
    return call(
        functools.partial(branch_kernel, count, turns),
        "branch_sums",
        [mixed, act, *blocks],
        deps,
        (at_mp,),
        grid=(2 * turns,),
        in_specs=[
            pl.BlockSpec((rows, a.shape[1]), lambda i, at: (where(i, at), 0)) for a in (mixed, act)
        ]
        + [ANY] * count,
        out_specs=split_specs(rows, model, turns),
        out_shape=[jax.ShapeDtypeStruct((turns, rows, model), BF16)] * 2,
        scratch_shapes=[pltpu.VMEM((inner, model), BF16), pltpu.SemaphoreType.DMA((count,))],
    )


def grad_in_kernel(setup, at_ref, slope_ref, *rest):
    count, parts, places, width, hidden, groups = setup
    chunks, many = [], 0
    for shifts in groups:
        chunks.append(by_shift(rest[many:], shifts))
        many += len(shifts)
    blocks = rest[many : many + count]
    gmixed_ref, gpre_ref, dy_ref, gsum_ref, dsum_ref, held, dy_held, sems, dy_sems = rest[-9:]
    step, steps = pl.program_id(0), 2 * len(places)
    found = chunk_copies(chunks, places, parts, dy_held, dy_sems)
    loads = block_copies(blocks, columns_at(held, blocks[0].shape[1]), sems)

    @pl.when(step == 0)
    def _():
        for copy in loads:
            copy.start()
        start_all(found)
        gsum_ref[...] = jnp.zeros_like(gsum_ref)
        dsum_ref[...] = jnp.zeros_like(dsum_ref)
        for copy in loads:
            copy.wait()

    for slot in range(steps):

        @pl.when(step == slot)
        def _(slot=slot):
            wait_for(found[slot])

    dy = dy_held[step]
    dy_ref[...] = dy
    gmixed_ref[...] = dot(dy, held[:width, :], 1, 1).astype(BF16)
    for start in range(0, hidden, width):
        part = slice(start, start + width)
        gact = dot(dy, held[width + start : 2 * width + start, :], 1, 1)
        gpre = (gact * slope_ref[:, part].astype(F32)).astype(BF16)
        gpre_ref[:, part] = gpre
        gsum_ref[0:1, part] += jnp.sum(gpre.astype(F32), axis=0, keepdims=True)
    dsum_ref[0:1, :] += jnp.sum(dy.astype(F32), axis=0, keepdims=True)


def grad_in(at_mp, chunks, slope, blocks, width, parts, places, earlier, deps):
    model = len(blocks) * blocks[0].shape[1]
    hidden, length = slope.shape[1], slope.shape[0]
    rows, count, many = length // (2 * parts), len(blocks), sum(len(c) for c in chunks)
    turns = len(places)

    def where(i, at):
        m = jnp.int32(places[0])
        for n in range(1, turns):
            m = jnp.where(i % turns == n, places[n], m)
        return i // turns * parts + (at[0] ^ m)

    out = lambda w: pl.BlockSpec((rows, w), lambda i, at: (where(i, at), 0))
    total = lambda w: pl.BlockSpec((8, w), lambda i, at: (0, 0))
    setup = (count, parts, places, width, hidden, [shifts_of(c) for c in chunks])
    operands = [slope, *arrays_of(chunks[0]), *arrays_of(chunks[1]), *blocks]
    aliases = {1 + len(operands) + n: n for n in range(len(earlier))}
    return call(
        functools.partial(grad_in_kernel, setup),
        "grad_in",
        operands + list(earlier),
        deps,
        (at_mp,),
        grid=(2 * turns,),
        in_specs=[out(hidden)] + [ANY] * (many + count + len(earlier)),
        out_specs=[out(width), out(hidden), out(model), total(hidden), total(model)],
        out_shape=[jax.ShapeDtypeStruct((length, w), BF16) for w in (width, hidden, model)]
        + [jax.ShapeDtypeStruct((8, w), F32) for w in (hidden, model)],
        input_output_aliases=aliases,
        scratch_shapes=[
            pltpu.VMEM((width + hidden, model), BF16),
            pltpu.VMEM((2 * turns, rows, model), BF16),
            pltpu.SemaphoreType.DMA((count,)),
            pltpu.SemaphoreType.DMA((2 * turns,)),
        ],
    )


def grad_normed_kernel(
    count, turns, at_ref, gq_ref, gk_ref, gv_ref, gpre_ref, tokens_ref, *rest
):
    blocks, others, rest = rest[:count], rest[count : count + turns], rest[count + turns :]
    own_ref, sum_ref, held, sems = rest
    step = pl.program_id(0)

    @pl.when(step == 0)
    def _():
        loads = block_copies(blocks, rows_at(held, blocks[0].shape[0]), sems)
        for copy in loads:
            copy.start()
        sum_ref[...] = jnp.zeros_like(sum_ref)
        for copy in loads:
            copy.wait()

    g = jnp.concatenate([gq_ref[...], gk_ref[...], gv_ref[...], gpre_ref[...]], axis=1)
    result = dot(g, held[...], 1, 1)
    sum_ref[0:1, :] += jnp.sum(result * normalized(tokens_ref[...]), axis=0, keepdims=True)
    sum_ref[1:2, :] += jnp.sum(result, axis=0, keepdims=True)
    result = result.astype(BF16)
    for n, other_ref in enumerate(others):

        @pl.when(step == n)
        def _(other_ref=other_ref):
            other_ref[...] = result

    @pl.when(step >= turns)
    def _():
        own_ref[0] = result


def grad_normed_sums(at_mp, gqkv, gpre, tokens, blocks, parts, places, deps):
    rows, count, turns = tokens.shape[0] // (2 * parts), len(blocks), len(places)
    model, total = tokens.shape[1], blocks[0].shape[1]
    where = quarter_map(places, parts)
    operands = [*gqkv, gpre, tokens]
    return call(
        functools.partial(grad_normed_kernel, count, turns),
        "grad_normed_sums",
        operands + list(blocks),
        deps,
        (at_mp,),
        grid=(2 * turns,),
        in_specs=[
            pl.BlockSpec((rows, a.shape[1]), lambda i, at: (where(i, at), 0)) for a in operands
        ]
        + [ANY] * count,
        out_specs=[pl.BlockSpec((rows, model), lambda i, at: (0, 0))] * turns
        + split_specs(rows, model, turns)[1:]
        + [pl.BlockSpec((8, model), lambda i, at: (0, 0))],
        out_shape=[jax.ShapeDtypeStruct((rows, model), BF16)] * turns
        + [
            jax.ShapeDtypeStruct((turns, rows, model), BF16),
            jax.ShapeDtypeStruct((8, model), F32),
        ],
        scratch_shapes=[pltpu.VMEM((model, total), BF16), pltpu.SemaphoreType.DMA((count,))],
    )


def weight_grad_kernel(writes, left, rows, at_ref, cut_ref, *refs):
    *refs, held, grad, sems = refs
    whole, outs = refs[: len(refs) - len(writes)], refs[len(refs) - len(writes) :]
    step, core, loads, first = pl.program_id(0), lax.rem(lax.axis_index("dp"), 2), [], 0
    for ref in whole:
        columns = pl.ds(first, ref.shape[1])
        first += ref.shape[1]
        for start in range(0, ref.shape[0], rows):
            part = pl.ds(start, rows)
            loads.append((ref.at[part], held.at[part, columns]))
    loads = [pltpu.make_async_copy(*pair, sems.at[n]) for n, pair in enumerate(loads)]

    @pl.when(step == 0)
    def _():
        for copy in loads:
            copy.start()
        for copy in loads:
            copy.wait()

    pair = (cut_ref[...], held[...]) if left else (held[...], cut_ref[...])
    grad[...] = dot(*pair, 0, 0).astype(BF16)
    size = cut_ref.shape[1] // 2
    for half, steps, out_ref in writes_of(writes, outs):
        here = functools.reduce(jnp.logical_or, [step == s for s in steps])

        @pl.when(here)
        def _(half=half, out_ref=out_ref):
            mine = span(core if half == 0 else 1 - core, size)
            out_ref[0] = grad[mine, :] if left else grad[:, mine]


def writes_of(writes, outs):
    return [(half, steps, out) for (half, steps), out in zip(writes, outs)]


def weight_grads(me, xs, gs, count, deps, left):
    plan, chips = scatter_plan(count), count // 2
    order = [j // 2 for s in plan[0] for j in s]
    sets = [(half, s) for s in range(len(plan[0])) for half in range(2)]
    writes = [(half, [order.index(j // 2) for j in plan[half][s]]) for half, s in sets]
    table = []
    for _, steps in writes:
        for i in range(chips):
            later = [w for w in steps if w >= i]
            table.append(steps.index(min(later) if later else max(steps)))
    owners = lax.bitwise_xor(me // 2, jnp.array(order, jnp.int32))
    at = jnp.concatenate([owners, jnp.array(table, jnp.int32)])
    length, (cut, whole) = xs[0].shape[0], ((xs, gs) if left else (gs, xs))
    size, full = cut[0].shape[1] // count, sum(a.shape[1] for a in whole)
    shape = (size, full) if left else (full, size)
    pieces = 8 // len(whole)

    def out(n):
        return pl.BlockSpec((1, *shape), lambda i, at: (at[chips * (n + 1) + i], 0, 0))

    outs = call(
        functools.partial(weight_grad_kernel, writes, left, length // pieces),
        "weight_grads",
        [*cut, *whole],
        deps,
        (at,),
        grid=(chips,),
        in_specs=[pl.BlockSpec((length, 2 * size), lambda i, at: (0, at[i]))]
        + [ANY] * len(whole),
        out_specs=[out(n) for n in range(len(sets))],
        out_shape=[
            jax.ShapeDtypeStruct((len(plan[half][s]), *shape), BF16) for half, s in sets
        ],
        scratch_shapes=[
            pltpu.VMEM((length, full), BF16),
            pltpu.VMEM((2 * size, full) if left else (full, 2 * size), BF16),
            pltpu.SemaphoreType.DMA((pieces * len(whole),)),
        ],
    )
    return [[o for o, (half, _) in zip(outs, sets) if half == h] for h in range(2)]


def norm_back_kernel(many, tokens_ref, dy_ref, gain_ref, *rest):
    addends, out_ref = rest[:many], rest[many]
    x = tokens_ref[...].astype(F32)
    centered = x - jnp.mean(x, axis=1, keepdims=True)
    inverse_std = lax.rsqrt(jnp.mean(centered * centered, axis=1, keepdims=True) + EPS)
    normal = centered * inverse_std
    scaled = sum(a[...].astype(F32) for a in addends) * gain_ref[...]
    first_mean = jnp.mean(scaled, axis=1, keepdims=True)
    second_mean = jnp.mean(scaled * normal, axis=1, keepdims=True)
    back = (scaled - first_mean - normal * second_mean) * inverse_std
    out_ref[...] = (dy_ref[...].astype(F32) + back).astype(BF16)


def norm_back(tokens, dy, gain, addends, deps):
    rows, model = tokens.shape
    tile = min(64, rows)
    part = pl.BlockSpec((tile, model), lambda i: (i, 0))
    return call(
        functools.partial(norm_back_kernel, len(addends)),
        "norm_back",
        [tokens, dy, gain, *addends],
        deps,
        grid=(rows // tile,),
        in_specs=[part, part, pl.BlockSpec((1, model), lambda i: (0, 0))] + [part] * len(addends),
        out_specs=part,
        out_shape=jax.ShapeDtypeStruct((rows, model), BF16),
    )


def across(value, bit, count):
    return lax.ppermute(value, "dp", [(i, i ^ bit) for i in range(count)])


def ring(value, k, parts):
    return lax.ppermute(value, "mp", [(i, (i + k) % parts) for i in range(parts)])


def near_shifts(parts):
    return (1, 3) if parts == 4 else tuple(range(1, parts))


def gather_far(chunks, parts):
    if parts != 4:
        return None
    up = lax.ppermute(chunks[1], "mp", [(1, 2), (2, 3)])
    down = lax.ppermute(chunks[3], "mp", [(1, 0), (2, 1)])
    return up + down


def added(addends):
    return sum(a.astype(F32) for a in addends).astype(BF16)


def send_far(farthest):
    up = lax.ppermute(farthest, "mp", [(0, 1), (1, 2)])
    down = lax.ppermute(farthest, "mp", [(3, 2), (2, 1)])
    return [up, down]


def chip_bits(count):
    bits, bit = [], 2
    while bit < count:
        bits.append(bit)
        bit *= 2
    return bits


class BlockGather:
    def __init__(self, own, sibling, count):
        self.held, self.count = {0: own, 1: sibling}, count
        self.orders = (chip_bits(count), chip_bits(count)[::-1])

    def own_to(self, s):
        if s < len(self.orders[0]):
            for half in range(2):
                bit = self.orders[half][s]
                self.held[half ^ bit] = across(self.held[half], bit, self.count)

    def rest(self):
        for s in range(1, len(self.orders[0])):
            for half in range(2):
                order = self.orders[half]
                for j in [j for j in self.held if j % 2 == half]:
                    if j ^ order[s] not in self.held and not any(j & b for b in order[s:]):
                        self.held[j ^ order[s]] = across(self.held[j], order[s], self.count)

    def fenced(self, others=(), deps=()):
        keys = sorted(self.held)
        values = fence([self.held[j] for j in keys] + list(others), deps)
        self.held = dict(zip(keys, values))
        return values[len(keys) :]

    def blocks(self):
        return [self.held[j] for j in range(self.count)]


def scatter_orders(count):
    return (chip_bits(count)[::-1], chip_bits(count))


def scatter_plan(count):
    plan = []
    for half, order in enumerate(scatter_orders(count)):
        sets, rest = [[half]], [half]
        for bit in reversed(order):
            sets.insert(0, [j ^ bit for j in rest])
            rest = sets[0] + rest
        plan.append(sets)
    return plan


class BlockScatter:
    def __init__(self, halves, count):
        self.count, self.orders = count, scatter_orders(count)
        self.held = [[[a] for a in arrays] for arrays in halves]
        self.steps = len(self.orders[0])

    def total(self, half, s):
        if len(self.held[half][s]) > 1:
            self.held[half][s] = [added(self.held[half][s])]
        return self.held[half][s][0]

    def ready(self, s):
        return [self.total(half, s) for half in range(2)]

    def send(self, s):
        return [across(self.total(h, s), self.orders[h][s], self.count) for h in range(2)]

    def arrive(self, s, came):
        for half in range(2):
            first = 0
            for later in self.held[half][s + 1 :]:
                many = later[0].shape[0]
                later.append(came[half][first : first + many])
                first += many

    def between(self):
        for s in range(1, self.steps - 1):
            self.arrive(s, self.send(s))

    def last(self):
        return self.total(1, -1)[0]

    def finish(self, theirs):
        return sum(a[0].astype(F32) for a in self.held[0][-1]), theirs.astype(F32)


def on_device(
    tokens,
    norm_gain,
    norm_bias,
    qkv_weight,
    qkv_bias,
    dense_weight,
    dense_bias,
    up_weight,
    up_bias,
    down_weight,
    down_bias,
    cotangent,
    *,
    ndp,
    nmp,
):
    me, z = lax.axis_index("dp"), lax.axis_index("mp")
    core = me % 2
    at_mp = z.astype(jnp.int32)[None]
    length, model = tokens.shape[0] * nmp, tokens.shape[1]
    block = min(512, length)
    width, hidden = qkv_weight.shape[2] // 2, up_weight.shape[1] // 2
    chip_steps = len(chip_bits(ndp))
    rank = lambda array, axis, which, size: lax.dynamic_slice_in_dim(
        array, which * size, size, axis
    )

    def row_pack(which):
        qkv = rank(qkv_weight, 2, which, width)
        return jnp.concatenate([qkv[0], qkv[1], qkv[2], rank(up_weight, 1, which, hidden)], axis=1)

    def column_pack(which):
        return jnp.concatenate(
            [rank(dense_weight, 0, which, width), rank(down_weight, 0, which, hidden)], axis=0
        )

    near, places, pairs = near_shifts(nmp), list(range(nmp)), width // LANES
    head, tail = near[0], near[1:]
    swap = lambda array: across(array, 1, ndp)
    rows = BlockGather(row_pack(core), swap(row_pack(1 - core)), ndp)
    columns = BlockGather(column_pack(core), swap(column_pack(1 - core)), ndp)
    came = {head: ring(tokens, head, nmp)}
    other = [(swap(tokens), (0,))]
    rows.own_to(0)
    came[head], begun = rows.fenced([came[head], tokens], [*columns.held.values(), other[0][0]])
    came.update({k: ring(begun, k, nmp) for k in tail})
    other.append((swap(came[head]), (head,)))
    rows.own_to(1)
    *held, cot = rows.fenced([*came.values(), cotangent], [other[1][0]])
    came = dict(zip(near, held))
    own = [(tokens, (0,))] + [(came[k], (k,)) for k in near]
    other += [(swap(came[k]), (k,)) for k in tail]
    far = gather_far(came, nmp)
    rows.rest()
    cot, *held = rows.fenced(
        [cot, columns.held[0], columns.held[1]] + ([far] if nmp == 4 else []),
        [array for array, _ in other[2:]],
    )
    columns.held = dict(enumerate(held[:2]))
    if nmp == 4:
        own.append((held[2], (2,)))
        other.append((swap(held[2]), (2,)))

    tables = rotary_tables(length)
    bias = jnp.concatenate(
        [
            rank(qkv_bias, 1, core, width).astype(F32).reshape(1, 3 * width),
            rank(up_bias[None, :], 1, core, hidden).astype(F32),
        ],
        axis=1,
    )
    gain, shift = norm_gain.astype(F32)[None, :], norm_bias.astype(F32)[None, :]
    came = {head: ring(cot, head, nmp)}
    dy_other = [(swap(cot), (0,))]
    columns.own_to(0)
    common = (rows.blocks(), bias, gain, shift, tables, width, nmp)
    first = project(at_mp, 0, own, *common, (), [cot])
    cot, came[head], begun = columns.fenced([cot, came[head], dy_other[0][0]], [first[0]])
    dy_other = [(begun, (0,)), (swap(came[head]), (head,))]
    came.update({k: ring(cot, k, nmp) for k in tail})
    columns.own_to(1)
    qkv, act, slope, normed, token_rows = project(
        at_mp, 1, other, *common, first, [columns.held[0]]
    )
    begun, *held = columns.fenced([dy_other[1][0], *came.values()], [qkv])
    dy_other[1] = (begun, (head,))
    came = dict(zip(near, held))
    dy_own = [(cot, (0,))] + [(came[k], (k,)) for k in near]
    dy_other += [(swap(came[k]), (k,)) for k in tail]
    far = gather_far(came, nmp)
    columns.rest()
    mixed, lse = attend(qkv, length, block, [columns.held[0]])
    begun = columns.fenced([array for array, _ in dy_other[2:]], [mixed])
    dy_other[2:] = [(array, (k,)) for array, k in zip(begun, tail)]
    other_sums, own_sums = branch_sums(
        at_mp, mixed, act, columns.blocks(), nmp, places, [begun[0]]
    )
    other_sums, *far = fence([other_sums] + ([far] if nmp == 4 else []), [own_sums])
    theirs = swap(other_sums)

    grad_a = grad_in(
        at_mp,
        ([c for c in dy_own if c[1][0] in (0, 1, nmp - 1)], [c for c in dy_other if c[1][0] in (0, 1, nmp - 1)]),
        slope,
        columns.blocks(),
        width,
        nmp,
        (0, 1),
        (),
        far,
    )
    far_other = [swap(a) for a in far]
    theirs, *far_other = fence([theirs, *far_other], [grad_a[3]])
    shares = [[own_sums[k], theirs[k]] for k in places]
    farthest = [added(shares[2])] if nmp == 4 else []
    moved = [a for f in farthest for a in send_far(f)]
    grad_b = grad_in(
        at_mp,
        (dy_own + [(a, (2,)) for a in far], dy_other + [(a, (2,)) for a in far_other]),
        slope,
        columns.blocks(),
        width,
        nmp,
        tuple(places[2:]),
        grad_a[:3],
        [grad_a[3], *farthest],
    )
    gmixed, gpre, dy = grad_b[:3]
    column_grads = BlockScatter(
        weight_grads(me, [mixed, act], [dy], ndp, [grad_b[3]], left=False), ndp
    )

    def with_far(shares, moved, shifts):
        if moved:
            shares[1], shares[3] = shares[1] + [moved[0]], shares[3] + [moved[1]]
        return {k: added(shares[k]) for k in shifts}

    if moved:
        moved = fence(moved, [column_grads.held[0][0][0]])
    sums = with_far(shares, moved, near)
    brought = [ring(sums[head], head, nmp)]
    column_came = column_grads.send(0)
    gq, gk, gv, qkv_sums = attend_back(
        qkv,
        gmixed,
        mixed,
        lse,
        tables,
        length,
        block,
        [column_grads.held[0][0][0], *sums.values()],
    )
    brought[0], *held = fence([brought[0], *(sums[k] for k in tail)], [gq])
    brought += [ring(a, k, nmp) for k, a in zip(tail, held)]

    def normed_part(part, deps):
        *other_part, own_part, sums = grad_normed_sums(
            at_mp, (gq, gk, gv), gpre, token_rows, rows.blocks(), nmp, part, deps
        )
        return other_part, own_part, sums

    thirds = ([2], [1, 3], [0]) if nmp == 4 else (places[1:2], places[2:], places[:1])
    other_a, own_a, sums_a = normed_part(thirds[0], [brought[0]])
    *column_came, other_a = fence([*column_came, *other_a], [sums_a])
    column_grads.arrive(0, column_came)
    column_grads.between()
    column_came = column_grads.send(chip_steps - 1)
    most = other_a.shape[0] // 2
    came_a = [swap(p) for p in (other_a[:most], other_a[most:])]
    up_grads = BlockScatter(
        weight_grads(
            me,
            [normed],
            [gpre],
            ndp,
            [sums_a, *column_grads.ready(chip_steps - 1)],
            left=True,
        ),
        ndp,
    )
    brought[1:] = fence(brought[1:], [up_grads.held[0][0][0]])
    c0, c1, a0, a1 = fence([*column_came, *came_a], [brought[1]])
    column_grads.arrive(chip_steps - 1, [c0, c1])
    shares = [[] for _ in places]
    shares[thirds[0][0]] = [own_a[0], jnp.concatenate([a0, a1])]
    farthest = [added(shares[2])] if nmp == 4 else []
    moved = [a for f in farthest for a in send_far(f)]
    up_came = up_grads.send(0)
    column_theirs = swap(column_grads.last())
    other_b, own_b, sums_b = normed_part(
        thirds[1], [sums_a, *farthest, up_grads.held[0][0][0], column_grads.last()]
    )
    column_theirs, *other_b = fence([column_theirs, *other_b], [sums_b])
    came_b = [swap(other_b[0])]
    other_c, own_c, sums_c = normed_part(thirds[2], [sums_b, column_theirs])
    qkv_sum = (
        qkv_sums.reshape(2, pairs, 8, LANES).sum(0)[:, :3, :].transpose(1, 0, 2).reshape(3 * width)
    )
    norm_sums = (sums_a + sums_b + sums_c)[:2].reshape(2 * model)
    small = jnp.concatenate(
        [norm_sums, qkv_sum, grad_a[3][0] + grad_b[3][0], grad_a[4][0] + grad_b[4][0]]
    )
    bits = chip_bits(ndp)
    for bit in bits[:-2]:
        small = small + across(small, bit, ndp)
    (other_c,) = other_c
    u0, u1, *moved = fence([*up_came, *moved], [sums_c])
    u0, u1 = fence([u0, u1])
    up_grads.arrive(0, [u0, u1])
    up_grads.between()
    came_b0, small, other_c, *other_b[1:] = fence(
        [came_b[0], small, other_c, *other_b[1:]], [u0]
    )
    came_b = [came_b0] + [swap(a) for a in other_b[1:]]
    for n, k in enumerate(thirds[1]):
        shares[k] = [own_b[n], came_b[n]]
    if moved:
        shares[1], shares[3] = shares[1] + [moved[0]], shares[3] + [moved[1]]
    first_sum = added(shares[head])
    came = {head: ring(first_sum, head, nmp)}
    up_came = up_grads.send(chip_steps - 1)
    small_came = across(small, bits[-2], ndp)
    qkv_grads = BlockScatter(
        weight_grads(
            me,
            [normed],
            [gq, gk, gv],
            ndp,
            [sums_c, first_sum, *up_grads.ready(chip_steps - 1)],
            left=True,
        ),
        ndp,
    )
    u0, u1, small_came, q0, q1, other_c, *held = fence(
        [
            *up_came,
            small_came,
            qkv_grads.held[0][0][0],
            qkv_grads.held[1][0][0],
            other_c,
            *came_b[1:],
        ]
    )
    for n, k in enumerate(thirds[1][1:]):
        shares[k][1] = held[n]
    up_grads.arrive(chip_steps - 1, [u0, u1])
    qkv_grads.held[0][0], qkv_grads.held[1][0] = [q0], [q1]
    qkv_came = qkv_grads.send(0)
    small = small + small_came
    small_came = across(small, bits[-1], ndp)
    came_c = swap(other_c)
    sums = {k: added(shares[k]) for k in tail}
    came[head], up_last, *held = fence(
        [came[head], up_grads.last(), *(sums[k] for k in tail)], [q0]
    )
    came.update({k: ring(a, k, nmp) for k, a in zip(tail, held)})
    q0, q1, small_came, came_c, up_last = fence(
        [*qkv_came, small_came, came_c, up_last], [came[head]]
    )
    qkv_grads.arrive(0, [q0, q1])
    qkv_grads.between()
    small = small + small_came
    up_theirs = swap(up_last)
    q0, q1, small = fence([*qkv_grads.send(chip_steps - 1), small])
    qkv_grads.arrive(chip_steps - 1, [q0, q1])
    small_other = swap(small)
    qkv_theirs = swap(qkv_grads.last())
    norm_sums = small[: 2 * model] + small_other[: 2 * model]
    norm_sums = [norm_sums] + [
        lax.ppermute(norm_sums, "mp", [(i, i ^ j) for i in range(nmp)]) for j in range(1, nmp)
    ]
    while len(norm_sums) > 1:
        norm_sums = [a + b for a, b in zip(norm_sums[::2], norm_sums[1::2])]
    norm_sums = norm_sums[0]

    local_inputs = tokens.astype(F32)
    output = (
        local_inputs
        + sum(a.astype(F32) for a in [own_sums[0], theirs[0], *brought])
        + (dense_bias.astype(F32) + down_bias.astype(F32))[None, :]
    ).astype(BF16)

    def both(mine, theirs, axis):
        return jnp.where(
            core == 0,
            jnp.concatenate([mine, theirs], axis=axis),
            jnp.concatenate([theirs, mine], axis=axis),
        )

    mine, theirs = column_grads.finish(column_theirs)
    owned_dense = both(mine[:width], theirs[:width], 0)
    owned_down = both(mine[width:], theirs[width:], 0)
    owned_up = both(*up_grads.finish(up_theirs), 1)
    mine, theirs = qkv_grads.finish(qkv_theirs)
    owned_qkv = jnp.stack(
        [
            both(mine[:, c * width : (c + 1) * width], theirs[:, c * width : (c + 1) * width], 1)
            for c in range(3)
        ]
    )

    inner = 3 * width + hidden
    grad_out_bias = small[2 * model + inner :]
    here, there = (a[2 * model : 2 * model + inner] for a in (small, small_other))
    even, odd = jnp.where(core == 0, here, there), jnp.where(core == 0, there, here)
    grad_qkv_bias = jnp.concatenate(
        [a[: 3 * width].reshape(3, width) for a in (even, odd)], axis=1
    )
    grad_up_bias = jnp.concatenate([even[3 * width :], odd[3 * width :]])

    grad_tokens = norm_back(
        tokens, cotangent, gain, [own_c[0], came_c, *came.values()], [qkv_theirs, small_other]
    )
    return (
        output,
        grad_tokens,
        norm_sums[:model],
        norm_sums[model:],
        owned_qkv,
        grad_qkv_bias,
        owned_dense,
        grad_out_bias,
        owned_up,
        grad_up_bias,
        owned_down,
        grad_out_bias,
    )


def solution(mesh):
    return jax.shard_map(
        functools.partial(on_device, ndp=mesh.shape["dp"], nmp=mesh.shape["mp"]),
        mesh=mesh,
        in_specs=(
            P(("dp", "mp"), None),
            P(),
            P(),
            P(None, "dp", "mp"),
            P(None, "mp"),
            P("mp", "dp"),
            P(),
            P("dp", "mp"),
            P("mp"),
            P("mp", "dp"),
            P(),
            P(("dp", "mp"), None),
        ),
        out_specs=(
            P(("dp", "mp"), None),
            P(("dp", "mp"), None),
            P(),
            P(),
            P(None, "dp", "mp"),
            P(None, "mp"),
            P("mp", "dp"),
            P(),
            P("dp", "mp"),
            P("mp"),
            P("mp", "dp"),
            P(),
        ),
        check_vma=False,
    )
```

```python
import functools

import jax
import jax.numpy as jnp
import numpy as np
from jax import lax
from jax.experimental import pallas as pl
from jax.experimental.pallas import tpu as pltpu
from jax.sharding import PartitionSpec as P

HEAD_DIM = 64
ROT = 32
EPS = 1e-05
LANES = 128
F32 = jnp.float32
BF16 = jnp.bfloat16
HBM = pl.BlockSpec(memory_space=pltpu.HBM)


def dot(lhs, rhs, lhs_dim, rhs_dim):
    return lax.dot_general(
        lhs, rhs, (((lhs_dim,), (rhs_dim,)), ((), ())), preferred_element_type=F32
    )


def call(kernel, name, operands, deps=(), scalars=(), vmem=63, **spec):
    deps, many, lead = tuple(deps), len(operands), len(scalars)

    def body(*refs):
        kernel(*refs[: lead + many], *refs[lead + many + len(deps) :])

    in_specs = list(spec.pop("in_specs")) + [HBM] * len(deps)
    out_shape, aliases = spec.pop("out_shape"), spec.pop("input_output_aliases", {})
    if scalars:
        grid_spec = pltpu.PrefetchScalarGridSpec(
            num_scalar_prefetch=lead, in_specs=in_specs, **spec
        )
        spec = {"grid_spec": grid_spec}
    else:
        spec["in_specs"] = in_specs
    return pl.pallas_call(
        body,
        out_shape=out_shape,
        input_output_aliases=aliases,
        compiler_params=pltpu.CompilerParams(vmem_limit_bytes=vmem << 20),
        cost_estimate=pl.CostEstimate(flops=0, transcendentals=0, bytes_accessed=0),
        name=name,
        **spec,
    )(*scalars, *operands, *deps)


def fence(values, deps=()):
    return call(
        lambda *refs: None,
        "fence",
        values,
        deps,
        in_specs=[HBM] * len(values),
        out_specs=[HBM] * len(values),
        out_shape=[jax.ShapeDtypeStruct(v.shape, v.dtype) for v in values],
        input_output_aliases={n: n for n in range(len(values))},
    )


def rotary_tables(length):
    positions = np.arange(length, dtype=np.float32)
    frequency = 10000.0 ** (-np.arange(ROT // 2, dtype=np.float64) * 2.0 / ROT)
    angles = positions[:, None] * frequency.astype(np.float32)[None, :]
    cosine, sine = np.cos(angles.astype(np.float64)), np.sin(angles.astype(np.float64))
    rest = HEAD_DIM - ROT
    none = np.zeros((length, ROT // 2))
    ones, zeros = np.ones((length, rest)), np.zeros((length, rest))
    straight = np.concatenate([cosine, cosine, ones], axis=1)
    left = np.concatenate([-sine, none, zeros], axis=1)
    right = np.concatenate([none, sine, zeros], axis=1)
    return [
        jnp.asarray(np.concatenate([t, t], axis=1).astype(np.float32))
        for t in (straight, left, right)
    ]


def rotated(u, straight, left, right, sign):
    half = ROT // 2
    turned = pltpu.roll(u, LANES - half, 1) * left + pltpu.roll(u, half, 1) * right
    return u * straight + sign * turned


def normalized(x):
    x = x.astype(F32)
    centered = x - jnp.mean(x, axis=1, keepdims=True)
    variance = jnp.mean(centered * centered, axis=1, keepdims=True)
    return centered * lax.rsqrt(variance + EPS)


def block_copies(blocks, place, sems):
    me = lax.axis_index("dp")
    return [
        pltpu.make_async_copy(block, place(lax.bitwise_xor(me, j)), sems.at[j])
        for j, block in enumerate(blocks)
    ]


def span(owner, size):
    return pl.ds(pl.multiple_of(owner * size, size), size)


def rows_at(ref, size):
    return lambda owner: ref.at[pl.ds(pl.multiple_of(owner * size, size), size)]


def columns_at(ref, size):
    return lambda owner: ref.at[:, pl.ds(pl.multiple_of(owner * size, size), size)]


def project_kernel(setup, x_ref, bias_ref, gain_ref, shift_ref, cos_ref, left_ref, right_ref, *rest):
    count, width, hidden = setup
    blocks = rest[:count]
    qkv_ref, act_ref, slope_ref, normed_ref, held, sems = rest[-6:]

    @pl.when(pl.program_id(0) == 0)
    def _():
        loads = block_copies(blocks, rows_at(held, blocks[0].shape[0]), sems)
        for copy in loads:
            copy.start()
        for copy in loads:
            copy.wait()

    x = (normalized(x_ref[...]) * gain_ref[...] + shift_ref[...]).astype(BF16)
    normed_ref[...] = x
    root = 0.7978845608028654
    for t in range((3 * width + hidden) // width):
        columns = slice(t * width, (t + 1) * width)
        y = dot(x, held[:, columns], 1, 0) + bias_ref[:, columns]
        if t < 3:
            for g in range(width // LANES):
                part = y[:, g * LANES : (g + 1) * LANES]
                if t < 2:
                    part = rotated(part, cos_ref[...], left_ref[...], right_ref[...], 1.0)
                if t == 0:
                    part = part * HEAD_DIM**-0.5
                start = t * width + g * LANES
                qkv_ref[:, start : start + LANES] = part.astype(BF16)
        else:
            columns = slice((t - 3) * width, (t - 2) * width)
            square = y * y
            turn = jnp.tanh(root * y * (1.0 + 0.044715 * square))
            half = 0.5 * (1.0 + turn)
            act_ref[:, columns] = (y * half).astype(BF16)
            slope = half * (1.0 + y * (1.0 - turn) * (root + (3.0 * 0.044715 * root) * square))
            slope_ref[:, columns] = slope.astype(BF16)


def project(sequence, x, blocks, bias, gain, shift, tables, width, tile, earlier, deps):
    (length, model), total, count = x.shape, blocks[0].shape[1], len(blocks)
    hidden, steps = total - 3 * width, length // tile
    rows = lambda w: pl.BlockSpec((tile, w), lambda i: (i, 0))
    out = lambda w: pl.BlockSpec((tile, w), lambda i: (sequence * steps + i, 0))
    line = lambda a: pl.BlockSpec(a.shape, lambda i: (0, 0))
    widths = (3 * width, hidden, hidden, model)
    operands = [x, bias, gain, shift, *tables, *blocks]
    return call(
        functools.partial(project_kernel, (count, width, hidden)),
        "project",
        operands + list(earlier),
        deps,
        grid=(steps,),
        in_specs=[rows(model), line(bias), line(gain), line(shift)]
        + [rows(LANES)] * 3
        + [HBM] * (count + len(earlier)),
        out_specs=[out(w) for w in widths],
        out_shape=[jax.ShapeDtypeStruct((2 * length, w), BF16) for w in widths],
        input_output_aliases={len(operands) + n: n for n in range(len(earlier))},
        scratch_shapes=[pltpu.VMEM((model, total), BF16), pltpu.SemaphoreType.DMA((count,))],
    )


def attend_kernel(block, q_ref, k_ref, v_ref, out_ref, lse_ref):
    length = q_ref.shape[0]
    lane = lax.broadcasted_iota(jnp.int32, (1, LANES), 1)
    key = lax.broadcasted_iota(jnp.int32, (block, block), 0)
    causal = key <= lax.broadcasted_iota(jnp.int32, (block, block), 1)
    for i in range(length // block):
        rows, before = pl.ds(i * block, block), pl.ds(0, i * block)
        results = []
        for h in range(2):
            mine = (lane < HEAD_DIM) if h == 0 else (lane >= HEAD_DIM)
            query = jnp.where(mine, q_ref[rows, :], 0)
            near = jnp.where(causal, dot(k_ref[rows, :], query, 1, 1), -1e30)
            highest = jnp.max(near, axis=0, keepdims=True)
            if i:
                far = dot(k_ref[before, :], query, 1, 1)
                highest = jnp.maximum(highest, jnp.max(far, axis=0, keepdims=True))
            near = jnp.exp(near - highest)
            total = jnp.sum(near, axis=0, keepdims=True)
            if i:
                far = jnp.exp(far - highest)
                total = total + jnp.sum(far, axis=0, keepdims=True)
            inverse = 1.0 / total
            result = dot((near * inverse).astype(BF16), v_ref[rows, :], 0, 0)
            if i:
                result = result + dot((far * inverse).astype(BF16), v_ref[before, :], 0, 0)
            results.append(result)
            lse_ref[0, h : h + 1, rows] = highest + jnp.log(total)
        out_ref[rows, :] = jnp.where(lane < HEAD_DIM, results[0], results[1]).astype(BF16)


def pair_specs(length, pairs):
    return lambda off: pl.BlockSpec(
        (length, LANES), lambda g: (g // pairs, off * pairs + g % pairs)
    )


def attend(qkv, length, block, deps):
    width, sequences = qkv.shape[1] // 3, qkv.shape[0] // length
    pairs = width // LANES
    at = pair_specs(length, pairs)
    return call(
        functools.partial(attend_kernel, block),
        "attend",
        [qkv, qkv, qkv],
        deps,
        grid=(sequences * pairs,),
        in_specs=[at(0), at(1), at(2)],
        out_specs=[at(0), pl.BlockSpec((1, 8, length), lambda g: (g, 0, 0))],
        out_shape=[
            jax.ShapeDtypeStruct((qkv.shape[0], width), BF16),
            jax.ShapeDtypeStruct((sequences * pairs, 8, length), F32),
        ],
    )


def attend_back_kernel(
    block,
    q_ref,
    k_ref,
    v_ref,
    grad_ref,
    mixed_ref,
    lse_ref,
    cos_ref,
    left_ref,
    right_ref,
    gq_ref,
    gk_ref,
    gv_ref,
    sum_ref,
    gk_sum,
    gv_sum,
):
    length = q_ref.shape[0]
    lane = lax.broadcasted_iota(jnp.int32, (1, LANES), 1)
    key = lax.broadcasted_iota(jnp.int32, (block, block), 0)
    causal = key <= lax.broadcasted_iota(jnp.int32, (block, block), 1)
    count = length // block
    sum_ref[...] = jnp.zeros_like(sum_ref)

    def put(ref, which, rows, value):
        value = value.astype(BF16)
        ref[rows, :] = value
        sum_ref[0, which : which + 1, :] += jnp.sum(value.astype(F32), axis=0, keepdims=True)

    def unrotated(value, rows):
        return rotated(value, cos_ref[rows, :], left_ref[rows, :], right_ref[rows, :], -1.0)

    for i in reversed(range(count)):
        rows = pl.ds(i * block, block)
        product = grad_ref[rows, :].astype(F32) * mixed_ref[rows, :].astype(F32)
        gq = None
        for h in range(2):
            mine = (lane < HEAD_DIM) if h == 0 else (lane >= HEAD_DIM)
            query = jnp.where(mine, q_ref[rows, :], 0)
            grad = jnp.where(mine, grad_ref[rows, :], 0)
            ones = jnp.where(mine, jnp.ones((8, LANES), F32), 0.0)
            delta = lax.dot_general(
                ones,
                product,
                (((1,), (1,)), ((), ())),
                precision=lax.Precision.HIGHEST,
                preferred_element_type=F32,
            )[0:1, :]
            lse = lse_ref[0, h : h + 1, rows]
            for j in range(i + 1):
                keys = pl.ds(j * block, block)
                key_rows = k_ref[keys, :]
                probs = jnp.exp(dot(key_rows, query, 1, 1) - lse)
                if j == i:
                    probs = jnp.where(causal, probs, 0.0)
                gprobs = dot(v_ref[keys, :], grad, 1, 1)
                gscores = (probs * (gprobs - delta)).astype(BF16)
                gv, gk = dot(probs.astype(BF16), grad, 1, 0), dot(gscores, query, 1, 0)
                if i == count - 1 and h == 0:
                    gv_sum[keys, :] = gv
                    gk_sum[keys, :] = gk
                else:
                    gv_sum[keys, :] += gv
                    gk_sum[keys, :] += gk
                part = dot(gscores, jnp.where(mine, key_rows, 0), 0, 0)
                gq = part if gq is None else gq + part
        put(gq_ref, 0, rows, unrotated(gq * HEAD_DIM**-0.5, rows))
    for i in range(count):
        rows = pl.ds(i * block, block)
        put(gk_ref, 1, rows, unrotated(gk_sum[rows, :], rows))
        put(gv_ref, 2, rows, gv_sum[rows, :])


def attend_back(qkv, grad, mixed, lse, tables, length, block, deps):
    width, sequences = qkv.shape[1] // 3, qkv.shape[0] // length
    pairs = width // LANES
    at = pair_specs(length, pairs)
    table = pl.BlockSpec((length, LANES), lambda g: (0, 0))
    small = pl.BlockSpec((1, 8, length), lambda g: (g, 0, 0))
    return call(
        functools.partial(attend_back_kernel, block),
        "attend_back",
        [qkv, qkv, qkv, grad, mixed, lse, *tables],
        deps,
        grid=(sequences * pairs,),
        in_specs=[at(0), at(1), at(2), at(0), at(0), small, table, table, table],
        out_specs=[at(0)] * 3 + [pl.BlockSpec((1, 8, LANES), lambda g: (g, 0, 0))],
        out_shape=[jax.ShapeDtypeStruct((qkv.shape[0], width), BF16)] * 3
        + [jax.ShapeDtypeStruct((sequences * pairs, 8, LANES), F32)],
        scratch_shapes=[pltpu.VMEM((length, LANES), F32)] * 2,
    )


def by_sequence(tile, width, steps):
    return [
        pl.BlockSpec((tile, width), lambda i: (jnp.minimum(i, steps - 1), 0)),
        pl.BlockSpec((tile, width), lambda i: (jnp.maximum(i - steps, 0), 0)),
    ]


def other_first(tile, width, steps):
    return pl.BlockSpec((tile, width), lambda i: ((i + steps) % (2 * steps), 0))


def put_by_sequence(step, steps, value, other_ref, own_ref):
    @pl.when(step < steps)
    def _():
        other_ref[...] = value

    @pl.when(step >= steps)
    def _():
        own_ref[...] = value


def branch_kernel(count, steps, mixed_ref, act_ref, *rest):
    blocks, (other_ref, own_ref, held, sems) = rest[:count], rest[count:]
    step = pl.program_id(0)

    @pl.when(step == 0)
    def _():
        loads = block_copies(blocks, columns_at(held, blocks[0].shape[1]), sems)
        for copy in loads:
            copy.start()
        for copy in loads:
            copy.wait()

    x = jnp.concatenate([mixed_ref[...], act_ref[...]], axis=1)
    put_by_sequence(step, steps, dot(x, held[...], 1, 0).astype(BF16), other_ref, own_ref)


def branch_sums(mixed, act, blocks, tile, deps):
    length, count = mixed.shape[0] // 2, len(blocks)
    inner, model, steps = blocks[0].shape[0], count * blocks[0].shape[1], length // tile
    return call(
        functools.partial(branch_kernel, count, steps),
        "branch_sums",
        [mixed, act, *blocks],
        deps,
        grid=(2 * steps,),
        in_specs=[other_first(tile, a.shape[1], steps) for a in (mixed, act)] + [HBM] * count,
        out_specs=by_sequence(tile, model, steps),
        out_shape=[jax.ShapeDtypeStruct((length, model), BF16)] * 2,
        scratch_shapes=[pltpu.VMEM((inner, model), BF16), pltpu.SemaphoreType.DMA((count,))],
    )


def grad_in_kernel(setup, dy_ref, slope_ref, *rest):
    count, width, hidden = setup
    blocks = rest[:count]
    gmixed_ref, gpre_ref, gsum_ref, dsum_ref, held, sems = rest[-6:]

    @pl.when(pl.program_id(0) == 0)
    def _():
        loads = block_copies(blocks, columns_at(held, blocks[0].shape[1]), sems)
        for copy in loads:
            copy.start()
        gsum_ref[...] = jnp.zeros_like(gsum_ref)
        dsum_ref[...] = jnp.zeros_like(dsum_ref)
        for copy in loads:
            copy.wait()

    dy = dy_ref[...]
    gmixed_ref[...] = dot(dy, held[:width, :], 1, 1).astype(BF16)
    for start in range(0, hidden, width):
        part = slice(start, start + width)
        gact = dot(dy, held[width + start : 2 * width + start, :], 1, 1)
        gpre = (gact * slope_ref[:, part].astype(F32)).astype(BF16)
        gpre_ref[:, part] = gpre
        gsum_ref[0:1, part] += jnp.sum(gpre.astype(F32), axis=0, keepdims=True)
    dsum_ref[0:1, :] += jnp.sum(dy.astype(F32), axis=0, keepdims=True)


def grad_in(sequence, dy, slope, blocks, width, tile, earlier, deps):
    (length, model), hidden, count = dy.shape, slope.shape[1], len(blocks)
    steps = length // tile
    out = lambda w: pl.BlockSpec((tile, w), lambda i: (sequence * steps + i, 0))
    total = lambda w: pl.BlockSpec((8, w), lambda i: (0, 0))
    operands = [dy, slope, *blocks]
    return call(
        functools.partial(grad_in_kernel, (count, width, hidden)),
        "grad_in",
        operands + list(earlier),
        deps,
        grid=(steps,),
        in_specs=[pl.BlockSpec((tile, model), lambda i: (i, 0)), out(hidden)]
        + [HBM] * (count + len(earlier)),
        out_specs=[out(width), out(hidden), total(hidden), total(model)],
        out_shape=[jax.ShapeDtypeStruct((2 * length, w), BF16) for w in (width, hidden)]
        + [jax.ShapeDtypeStruct((8, w), F32) for w in (hidden, model)],
        input_output_aliases={len(operands) + n: n for n in range(len(earlier))},
        scratch_shapes=[
            pltpu.VMEM((width + hidden, model), BF16),
            pltpu.SemaphoreType.DMA((count,)),
        ],
    )


def grad_normed_kernel(
    count, steps, half, gq_ref, gk_ref, gv_ref, gpre_ref, x_other_ref, x_own_ref, *rest
):
    blocks, (early_ref, late_ref, own_ref, sum_ref, held, normal, sems) = rest[:count], rest[count:]
    step, size, few = pl.program_id(0), blocks[0].shape[0], count // 2
    me = lax.axis_index("dp")

    @pl.when(step == 0)
    def _():
        for start in (True, False):
            for j, block in enumerate(blocks):
                owner = lax.bitwise_xor(me, j) - half * few

                @pl.when((owner >= 0) & (owner < few))
                def _(start=start, j=j, block=block, owner=owner):
                    copy = pltpu.make_async_copy(block, held.at[span(owner, size)], sems.at[j])
                    if start:
                        copy.start()
                    else:
                        copy.wait()

        sum_ref[...] = jnp.zeros_like(sum_ref)

    columns = slice(half * few * size, (half + 1) * few * size)

    @pl.when(step < steps)
    def _():
        normal[...] = normalized(x_other_ref[...])[:, columns]

    @pl.when(step >= steps)
    def _():
        normal[...] = normalized(x_own_ref[...])[:, columns]

    g = jnp.concatenate([gq_ref[...], gk_ref[...], gv_ref[...], gpre_ref[...]], axis=1)
    result = dot(g, held[...], 1, 1)
    sum_ref[0:1, :] += jnp.sum(result * normal[...], axis=0, keepdims=True)
    sum_ref[1:2, :] += jnp.sum(result, axis=0, keepdims=True)
    result = result.astype(BF16)
    for n, ref in enumerate((early_ref, late_ref)):

        @pl.when(step // (steps // 2) == n)
        def _(ref=ref):
            ref[...] = result

    @pl.when(step >= steps)
    def _():
        own_ref[...] = result


def grad_normed_sums(half, gqkv, gpre, x_own, x_other, blocks, tile, deps):
    (length, model), count, total = x_own.shape, len(blocks), blocks[0].shape[1]
    steps, part = length // tile, model // 2
    few = steps // 2
    operands = [*gqkv, gpre]
    return call(
        functools.partial(grad_normed_kernel, count, steps, half),
        "grad_normed_sums",
        operands + [x_other, x_own, *blocks],
        deps,
        grid=(2 * steps,),
        in_specs=[other_first(tile, a.shape[1], steps) for a in operands]
        + by_sequence(tile, model, steps)
        + [HBM] * count,
        out_specs=[
            pl.BlockSpec((tile, part), lambda i: (jnp.minimum(i, few - 1), 0)),
            pl.BlockSpec((tile, part), lambda i: (jnp.clip(i - few, 0, few - 1), 0)),
        ]
        + by_sequence(tile, part, steps)[1:]
        + [pl.BlockSpec((8, part), lambda i: (0, 0))],
        out_shape=[jax.ShapeDtypeStruct((length // 2, part), BF16)] * 2
        + [jax.ShapeDtypeStruct((length, part), BF16), jax.ShapeDtypeStruct((8, part), F32)],
        scratch_shapes=[
            pltpu.VMEM((part, total), BF16),
            pltpu.VMEM((tile, part), F32),
            pltpu.SemaphoreType.DMA((count,)),
        ],
    )


def weight_grad_kernel(writes, left, rows, many, at_ref, *refs):
    cuts, (*refs, held, grad, sems) = refs[:many], refs[many:]
    whole, outs = refs[: len(refs) - len(writes)], refs[len(refs) - len(writes) :]
    step, core, loads, first = pl.program_id(0), lax.rem(lax.axis_index("dp"), 2), [], 0
    for ref in whole:
        columns = pl.ds(first, ref.shape[1])
        first += ref.shape[1]
        for start in range(0, ref.shape[0], rows):
            part = pl.ds(start, rows)
            loads.append((ref.at[part], held.at[part, columns]))
    loads = [pltpu.make_async_copy(*pair, sems.at[n]) for n, pair in enumerate(loads)]

    @pl.when(step == 0)
    def _():
        for copy in loads:
            copy.start()
        for copy in loads:
            copy.wait()

    cut = jnp.concatenate([ref[...] for ref in cuts], axis=0)
    pair = (cut, held[...]) if left else (held[...], cut)
    grad[...] = dot(*pair, 0, 0).astype(BF16)
    size = cut.shape[1] // 2
    for half, steps, out_ref in writes_of(writes, outs):
        here = functools.reduce(jnp.logical_or, [step == s for s in steps])

        @pl.when(here)
        def _(half=half, out_ref=out_ref):
            mine = span(core if half == 0 else 1 - core, size)
            out_ref[0] = grad[mine, :] if left else grad[:, mine]


def writes_of(writes, outs):
    return [(half, steps, out) for (half, steps), out in zip(writes, outs)]


def weight_grads(me, xs, gs, count, deps, left):
    plan, chips = scatter_plan(count), count // 2
    order = [j // 2 for s in plan[0] for j in s]
    sets = [(half, s) for s in range(len(plan[0])) for half in range(2)]
    writes = [(half, [order.index(j // 2) for j in plan[half][s]]) for half, s in sets]
    table = []
    for _, steps in writes:
        for i in range(chips):
            later = [w for w in steps if w >= i]
            table.append(steps.index(min(later) if later else max(steps)))
    owners = lax.bitwise_xor(me // 2, jnp.array(order, jnp.int32))
    at = jnp.concatenate([owners, jnp.array(table, jnp.int32)])
    cut, whole = (xs, gs) if left else (gs, xs)
    length = whole[0].shape[0]
    size, full = cut[0].shape[1] // count, sum(a.shape[1] for a in whole)
    shape = (size, full) if left else (full, size)
    pieces = 8 // len(whole)

    def out(n):
        return pl.BlockSpec((1, *shape), lambda i, at: (at[chips * (n + 1) + i], 0, 0))

    outs = call(
        functools.partial(weight_grad_kernel, writes, left, length // pieces, len(cut)),
        "weight_grads",
        [*cut, *whole],
        deps,
        (at,),
        grid=(chips,),
        in_specs=[pl.BlockSpec((a.shape[0], 2 * size), lambda i, at: (0, at[i])) for a in cut]
        + [HBM] * len(whole),
        out_specs=[out(n) for n in range(len(sets))],
        out_shape=[
            jax.ShapeDtypeStruct((len(plan[half][s]), *shape), BF16) for half, s in sets
        ],
        scratch_shapes=[
            pltpu.VMEM((length, full), BF16),
            pltpu.VMEM((2 * size, full) if left else (full, 2 * size), BF16),
            pltpu.SemaphoreType.DMA((pieces * len(whole),)),
        ],
    )
    return [[o for o, (half, _) in zip(outs, sets) if half == h] for h in range(2)]


def norm_back_kernel(tokens_ref, dy_ref, gain_ref, left_ref, right_ref, out_ref):
    x = tokens_ref[...].astype(F32)
    centered = x - jnp.mean(x, axis=1, keepdims=True)
    inverse_std = lax.rsqrt(jnp.mean(centered * centered, axis=1, keepdims=True) + EPS)
    normal = centered * inverse_std
    grad = jnp.concatenate([left_ref[...], right_ref[...]], axis=1).astype(F32)
    scaled = grad * gain_ref[...]
    first_mean = jnp.mean(scaled, axis=1, keepdims=True)
    second_mean = jnp.mean(scaled * normal, axis=1, keepdims=True)
    back = (scaled - first_mean - normal * second_mean) * inverse_std
    out_ref[...] = (dy_ref[...].astype(F32) + back).astype(BF16)


def norm_back(tokens, dy, gain, halves, deps):
    rows, model = tokens.shape
    tile = min(64, rows)
    part = lambda w: pl.BlockSpec((tile, w), lambda i: (i, 0))
    return call(
        norm_back_kernel,
        "norm_back",
        [tokens, dy, gain, *halves],
        deps,
        grid=(rows // tile,),
        in_specs=[part(model), part(model), pl.BlockSpec((1, model), lambda i: (0, 0))]
        + [part(model // 2)] * 2,
        out_specs=part(model),
        out_shape=jax.ShapeDtypeStruct((rows, model), BF16),
    )


def across(value, bit, count):
    return lax.ppermute(value, "dp", [(i, i ^ bit) for i in range(count)])


def added(addends):
    return sum(a.astype(F32) for a in addends).astype(BF16)


def chip_bits(count):
    bits, bit = [], 2
    while bit < count:
        bits.append(bit)
        bit *= 2
    return bits


class BlockGather:
    def __init__(self, own, sibling, count):
        self.held, self.count = {0: own, 1: sibling}, count
        self.orders = (chip_bits(count), chip_bits(count)[::-1])

    def own_to(self, s):
        if s < len(self.orders[0]):
            for half in range(2):
                bit = self.orders[half][s]
                self.held[half ^ bit] = across(self.held[half], bit, self.count)

    def rest(self):
        for s in range(1, len(self.orders[0])):
            for half in range(2):
                order = self.orders[half]
                for j in [j for j in self.held if j % 2 == half]:
                    if j ^ order[s] not in self.held and not any(j & b for b in order[s:]):
                        self.held[j ^ order[s]] = across(self.held[j], order[s], self.count)

    def fenced(self, others=(), deps=()):
        keys = sorted(self.held)
        values = fence([self.held[j] for j in keys] + list(others), deps)
        self.held = dict(zip(keys, values))
        return values[len(keys) :]

    def blocks(self):
        return [self.held[j] for j in range(self.count)]


def scatter_orders(count):
    return (chip_bits(count)[::-1], chip_bits(count))


def scatter_plan(count):
    plan = []
    for half, order in enumerate(scatter_orders(count)):
        sets, rest = [[half]], [half]
        for bit in reversed(order):
            sets.insert(0, [j ^ bit for j in rest])
            rest = sets[0] + rest
        plan.append(sets)
    return plan


class BlockScatter:
    def __init__(self, halves, count):
        self.count, self.orders = count, scatter_orders(count)
        self.held = [[[a] for a in arrays] for arrays in halves]
        self.steps = len(self.orders[0])

    def total(self, half, s):
        if len(self.held[half][s]) > 1:
            self.held[half][s] = [added(self.held[half][s])]
        return self.held[half][s][0]

    def ready(self, s):
        return [self.total(half, s) for half in range(2)]

    def send(self, s):
        return [across(self.total(h, s), self.orders[h][s], self.count) for h in range(2)]

    def arrive(self, s, came):
        for half in range(2):
            first = 0
            for later in self.held[half][s + 1 :]:
                many = later[0].shape[0]
                later.append(came[half][first : first + many])
                first += many

    def between(self):
        for s in range(1, self.steps - 1):
            self.arrive(s, self.send(s))

    def last(self):
        return self.total(1, -1)[0]

    def finish(self, theirs):
        return sum(a[0].astype(F32) for a in self.held[0][-1]), theirs.astype(F32)


def on_device(
    tokens,
    norm_gain,
    norm_bias,
    qkv_weight,
    qkv_bias,
    dense_weight,
    dense_bias,
    up_weight,
    up_bias,
    down_weight,
    down_bias,
    cotangent,
    *,
    ndp,
    nmp,
):
    me = lax.axis_index("dp")
    core = me % 2
    length, model = tokens.shape[0] * nmp, tokens.shape[1]
    tile, block = min(256, length), min(512, length)
    width, hidden = qkv_weight.shape[2] // 2, up_weight.shape[1] // 2
    chip_steps = len(chip_bits(ndp))
    rank = lambda array, axis, which, size: lax.dynamic_slice_in_dim(
        array, which * size, size, axis
    )

    def row_pack(which):
        qkv = rank(qkv_weight, 2, which, width)
        return jnp.concatenate([qkv[0], qkv[1], qkv[2], rank(up_weight, 1, which, hidden)], axis=1)

    def column_pack(which):
        return jnp.concatenate(
            [rank(dense_weight, 0, which, width), rank(down_weight, 0, which, hidden)], axis=0
        )

    pairs = width // LANES
    swap = lambda array: across(array, 1, ndp)
    line_gather = lambda array: lax.all_gather(array, "mp", axis=0, tiled=True)
    line_scatter = lambda array: lax.psum_scatter(array, "mp", scatter_dimension=0, tiled=True)
    x_own, dy_own = line_gather(tokens), line_gather(cotangent)
    rows = BlockGather(row_pack(core), swap(row_pack(1 - core)), ndp)
    columns = BlockGather(column_pack(core), swap(column_pack(1 - core)), ndp)
    rows.own_to(0)
    rows.fenced(deps=columns.held.values())
    rows.own_to(1)
    rows.fenced()
    rows.rest()
    x_own, *held = fence([x_own, columns.held[0], columns.held[1]], rows.blocks())
    columns.held = dict(enumerate(held))

    tables = rotary_tables(length)
    bias = jnp.concatenate(
        [
            rank(qkv_bias, 1, core, width).astype(F32).reshape(1, 3 * width),
            rank(up_bias[None, :], 1, core, hidden).astype(F32),
        ],
        axis=1,
    )
    gain, shift = norm_gain.astype(F32)[None, :], norm_bias.astype(F32)[None, :]
    x_other = swap(x_own)
    columns.own_to(0)
    common = (rows.blocks(), bias, gain, shift, tables, width, tile)
    first = project(0, x_own, *common, (), [columns.held[0]])
    (x_other,) = columns.fenced([x_other], [first[0]])
    columns.own_to(1)
    qkv, act, slope, normed = project(1, x_other, *common, first, [columns.held[0]])
    columns.fenced(deps=[qkv])
    columns.rest()
    mixed, lse = attend(qkv, length, block, [columns.held[0]])
    columns.fenced(deps=[mixed])
    other_sums, own_sums = branch_sums(mixed, act, columns.blocks(), tile, [])
    other_sums, dy_own = fence([other_sums, dy_own], [own_sums])
    theirs = swap(other_sums)
    dy_other = swap(dy_own)

    grads = (slope, columns.blocks(), width, tile)
    grad_a = grad_in(0, dy_own, *grads, (), [own_sums])
    theirs, dy_other = fence([theirs, dy_other], [grad_a[2]])
    total = added([own_sums, theirs])
    branches = line_scatter(total)
    gmixed, gpre, *grad_b = grad_in(1, dy_other, *grads, grad_a[:2], [total])
    column_grads = BlockScatter(
        weight_grads(me, [mixed, act], [dy_own, dy_other], ndp, [grad_b[0]], left=False), ndp
    )
    column_came = column_grads.send(0)
    gq, gk, gv, qkv_sums = attend_back(
        qkv, gmixed, mixed, lse, tables, length, block, [column_grads.held[0][0][0]]
    )

    def normed_half(half, deps):
        *other, own, sums = grad_normed_sums(
            half, (gq, gk, gv), gpre, x_own, x_other, rows.blocks(), tile, deps
        )
        return other, own, sums

    other_a, own_a, sums_a = normed_half(0, [column_grads.held[0][0][0]])
    c0, c1, *other_a = fence([*column_came, *other_a], [sums_a])
    column_came = [c0, c1]
    column_grads.arrive(0, column_came)
    column_grads.between()
    column_came = column_grads.send(chip_steps - 1)
    theirs_a = [swap(a) for a in other_a]
    up_grads = BlockScatter(
        weight_grads(
            me, [normed], [gpre], ndp, [sums_a, *column_grads.ready(chip_steps - 1)], left=True
        ),
        ndp,
    )
    c0, c1, branches, u0, u1, *theirs_a = fence(
        [*column_came, branches, *(up_grads.held[h][0][0] for h in range(2)), *theirs_a]
    )
    up_grads.held[0][0], up_grads.held[1][0] = [u0], [u1]
    column_grads.arrive(chip_steps - 1, [c0, c1])
    total_a = added([own_a, jnp.concatenate(theirs_a)])
    half_a = line_scatter(total_a)
    up_came = up_grads.send(0)
    column_theirs = swap(column_grads.last())
    other_b, own_b, sums_b = normed_half(1, [u0, total_a, column_grads.last()])
    *other_b, column_theirs = fence([*other_b, column_theirs], [sums_b])
    theirs_b = [swap(a) for a in other_b]
    qkv_sum = (
        qkv_sums.reshape(2, pairs, 8, LANES).sum(0)[:, :3, :].transpose(1, 0, 2).reshape(3 * width)
    )
    norm_sums = jnp.concatenate([sums_a[:2], sums_b[:2]], axis=1).reshape(2 * model)
    small = jnp.concatenate(
        [norm_sums, qkv_sum, grad_a[2][0] + grad_b[0][0], grad_a[3][0] + grad_b[1][0]]
    )
    bits = chip_bits(ndp)
    for bit in bits[:-2]:
        small = small + across(small, bit, ndp)
    small_came = across(small, bits[-2], ndp)
    qkv_grads = BlockScatter(
        weight_grads(me, [normed], [gq, gk, gv], ndp, [small, other_b[0]], left=True), ndp
    )
    u0, u1 = fence(up_came, [qkv_grads.held[0][0][0]])
    for _ in range(3):
        u0, u1 = fence([u0, u1])
    small_came, q0, q1, *theirs_b = fence(
        [small_came, *(qkv_grads.held[h][0][0] for h in range(2)), *theirs_b], [u0]
    )
    half_b = line_scatter(added([own_b, jnp.concatenate(theirs_b)]))
    up_grads.arrive(0, [u0, u1])
    up_grads.between()
    qkv_grads.held[0][0], qkv_grads.held[1][0] = [q0], [q1]
    up_came = up_grads.send(chip_steps - 1)
    qkv_came = qkv_grads.send(0)
    small = small + small_came
    small_came = across(small, bits[-1], ndp)
    u0, u1, q0, q1, small_came, column_theirs, branches, half_a = fence(
        [*up_came, *qkv_came, small_came, column_theirs, branches, half_a]
    )
    up_grads.arrive(chip_steps - 1, [u0, u1])
    up_theirs = swap(up_grads.last())
    qkv_grads.arrive(0, [q0, q1])
    qkv_grads.between()
    small = small + small_came
    q0, q1, small = fence([*qkv_grads.send(chip_steps - 1), small])
    qkv_grads.arrive(chip_steps - 1, [q0, q1])
    small_other = swap(small)
    qkv_theirs = swap(qkv_grads.last())
    norm_sums = small[: 2 * model] + small_other[: 2 * model]
    norm_sums = [norm_sums] + [
        lax.ppermute(norm_sums, "mp", [(i, i ^ j) for i in range(nmp)]) for j in range(1, nmp)
    ]
    while len(norm_sums) > 1:
        norm_sums = [a + b for a, b in zip(norm_sums[::2], norm_sums[1::2])]
    norm_sums = norm_sums[0]

    output = (
        tokens.astype(F32)
        + branches.astype(F32)
        + (dense_bias.astype(F32) + down_bias.astype(F32))[None, :]
    ).astype(BF16)

    def both(mine, theirs, axis):
        return jnp.where(
            core == 0,
            jnp.concatenate([mine, theirs], axis=axis),
            jnp.concatenate([theirs, mine], axis=axis),
        )

    mine, theirs = column_grads.finish(column_theirs)
    owned_dense = both(mine[:width], theirs[:width], 0)
    owned_down = both(mine[width:], theirs[width:], 0)
    owned_up = both(*up_grads.finish(up_theirs), 1)
    mine, theirs = qkv_grads.finish(qkv_theirs)
    owned_qkv = jnp.stack(
        [
            both(mine[:, c * width : (c + 1) * width], theirs[:, c * width : (c + 1) * width], 1)
            for c in range(3)
        ]
    )

    inner = 3 * width + hidden
    grad_out_bias = small[2 * model + inner :]
    here, there = (a[2 * model : 2 * model + inner] for a in (small, small_other))
    even, odd = jnp.where(core == 0, here, there), jnp.where(core == 0, there, here)
    grad_qkv_bias = jnp.concatenate(
        [a[: 3 * width].reshape(3, width) for a in (even, odd)], axis=1
    )
    grad_up_bias = jnp.concatenate([even[3 * width :], odd[3 * width :]])

    grad_tokens = norm_back(tokens, cotangent, gain, [half_a, half_b], [qkv_theirs, small_other])
    return (
        output,
        grad_tokens,
        norm_sums[:model],
        norm_sums[model:],
        owned_qkv,
        grad_qkv_bias,
        owned_dense,
        grad_out_bias,
        owned_up,
        grad_up_bias,
        owned_down,
        grad_out_bias,
    )


def solution(mesh):
    return jax.shard_map(
        functools.partial(on_device, ndp=mesh.shape["dp"], nmp=mesh.shape["mp"]),
        mesh=mesh,
        in_specs=(
            P(("dp", "mp"), None),
            P(),
            P(),
            P(None, "dp", "mp"),
            P(None, "mp"),
            P("mp", "dp"),
            P(),
            P("dp", "mp"),
            P("mp"),
            P("mp", "dp"),
            P(),
            P(("dp", "mp"), None),
        ),
        out_specs=(
            P(("dp", "mp"), None),
            P(("dp", "mp"), None),
            P(),
            P(),
            P(None, "dp", "mp"),
            P(None, "mp"),
            P("mp", "dp"),
            P(),
            P("dp", "mp"),
            P("mp"),
            P("mp", "dp"),
            P(),
        ),
        check_vma=False,
    )
```

```python
import functools

import jax
import jax.numpy as jnp
import numpy as np
from jax import lax
from jax.experimental import pallas as pl
from jax.experimental.pallas import tpu as pltpu
from jax.sharding import PartitionSpec as P

HEAD_DIM = 64
ROT = 32
EPS = 1e-05
LANES = 128
F32 = jnp.float32
BF16 = jnp.bfloat16
HBM = pl.BlockSpec(memory_space=pltpu.HBM)


def dot(lhs, rhs, lhs_dim, rhs_dim):
    return lax.dot_general(
        lhs, rhs, (((lhs_dim,), (rhs_dim,)), ((), ())), preferred_element_type=F32
    )


def call(kernel, name, operands, deps=(), scalars=(), adds=(), vmem=63, **spec):
    deps, out_shape = tuple(deps), spec.pop("out_shape")
    single = not isinstance(out_shape, list)
    out_shape = [out_shape] if single else out_shape
    out_specs = spec.pop("out_specs")
    out_specs = [out_specs] if single else list(out_specs)
    extra, extra_specs, sizes = [], [], []
    steps = spec["grid"][0] if adds else 1
    for many, addends in adds:
        _, rows, columns = addends[0][0].shape
        block = (many, rows // steps, columns)
        for array, first in addends:
            extra.append(array)
            extra_specs.append(
                pl.BlockSpec(block, lambda i, *at, first=first, many=many: (first // many, i, 0))
            )
        out_shape = out_shape + [jax.ShapeDtypeStruct((many, rows, columns), BF16)]
        out_specs = out_specs + [pl.BlockSpec(block, lambda i, *at: (0, i, 0))]
        sizes.append(len(addends))
    lead, outs = len(scalars) + len(operands), len(out_shape) - len(adds)

    def body(*refs):
        first = lead + len(extra) + len(deps)
        kernel(*refs[:lead], *refs[first : first + outs], *refs[first + outs + len(adds) :])
        sources = refs[lead : lead + len(extra)]
        for n, out in zip(sizes, refs[first + outs : first + outs + len(adds)]):
            out[...] = sum(ref[...].astype(F32) for ref in sources[:n]).astype(BF16)
            sources = sources[n:]

    in_specs = list(spec.pop("in_specs")) + extra_specs + [HBM] * len(deps)
    aliases = spec.pop("input_output_aliases", {})
    if scalars:
        grid_spec = pltpu.PrefetchScalarGridSpec(
            num_scalar_prefetch=len(scalars), in_specs=in_specs, out_specs=out_specs, **spec
        )
        spec = {"grid_spec": grid_spec}
    else:
        spec.update(in_specs=in_specs, out_specs=out_specs)
    results = pl.pallas_call(
        body,
        out_shape=out_shape,
        input_output_aliases=aliases,
        compiler_params=pltpu.CompilerParams(vmem_limit_bytes=vmem << 20),
        cost_estimate=pl.CostEstimate(flops=0, transcendentals=0, bytes_accessed=0),
        name=name,
        **spec,
    )(*scalars, *operands, *extra, *deps)
    return results[0] if single and not adds else results


def fence(values, deps=()):
    return call(
        lambda *refs: None,
        "fence",
        values,
        deps,
        in_specs=[HBM] * len(values),
        out_specs=[HBM] * len(values),
        out_shape=[jax.ShapeDtypeStruct(v.shape, v.dtype) for v in values],
        input_output_aliases={n: n for n in range(len(values))},
    )


def rotary_tables(length):
    positions = np.arange(length, dtype=np.float32)
    frequency = 10000.0 ** (-np.arange(ROT // 2, dtype=np.float64) * 2.0 / ROT)
    angles = positions[:, None] * frequency.astype(np.float32)[None, :]
    cosine, sine = np.cos(angles.astype(np.float64)), np.sin(angles.astype(np.float64))
    rest = HEAD_DIM - ROT
    none = np.zeros((length, ROT // 2))
    ones, zeros = np.ones((length, rest)), np.zeros((length, rest))
    straight = np.concatenate([cosine, cosine, ones], axis=1)
    left = np.concatenate([-sine, none, zeros], axis=1)
    right = np.concatenate([none, sine, zeros], axis=1)
    return [
        jnp.asarray(np.concatenate([t, t], axis=1).astype(np.float32))
        for t in (straight, left, right)
    ]


def rotated(u, straight, left, right, sign):
    half = ROT // 2
    turned = pltpu.roll(u, LANES - half, 1) * left + pltpu.roll(u, half, 1) * right
    return u * straight + sign * turned


def normalized(x):
    x = x.astype(F32)
    centered = x - jnp.mean(x, axis=1, keepdims=True)
    variance = jnp.mean(centered * centered, axis=1, keepdims=True)
    return centered * lax.rsqrt(variance + EPS)


def block_copies(blocks, place, sems):
    me = lax.axis_index("dp")
    return [
        pltpu.make_async_copy(block, place(lax.bitwise_xor(me, j)), sems.at[j])
        for j, block in enumerate(blocks)
    ]


def span(owner, size):
    return pl.ds(pl.multiple_of(owner * size, size), size)


def rows_at(ref, size):
    return lambda owner: ref.at[pl.ds(pl.multiple_of(owner * size, size), size)]


def columns_at(ref, size):
    return lambda owner: ref.at[:, pl.ds(pl.multiple_of(owner * size, size), size)]


def project_kernel(setup, x_ref, bias_ref, gain_ref, shift_ref, cos_ref, left_ref, right_ref, *rest):
    count, width, hidden = setup
    blocks = rest[:count]
    qkv_ref, act_ref, slope_ref, normed_ref, held, sems = rest[-6:]

    @pl.when(pl.program_id(0) == 0)
    def _():
        loads = block_copies(blocks, rows_at(held, blocks[0].shape[0]), sems)
        for copy in loads:
            copy.start()
        for copy in loads:
            copy.wait()

    x = (normalized(x_ref[...]) * gain_ref[...] + shift_ref[...]).astype(BF16)
    normed_ref[...] = x
    root = 0.7978845608028654
    for t in range((3 * width + hidden) // width):
        columns = slice(t * width, (t + 1) * width)
        y = dot(x, held[:, columns], 1, 0) + bias_ref[:, columns]
        if t < 3:
            for g in range(width // LANES):
                part = y[:, g * LANES : (g + 1) * LANES]
                if t < 2:
                    part = rotated(part, cos_ref[...], left_ref[...], right_ref[...], 1.0)
                if t == 0:
                    part = part * HEAD_DIM**-0.5
                start = t * width + g * LANES
                qkv_ref[:, start : start + LANES] = part.astype(BF16)
        else:
            columns = slice((t - 3) * width, (t - 2) * width)
            square = y * y
            turn = jnp.tanh(root * y * (1.0 + 0.044715 * square))
            half = 0.5 * (1.0 + turn)
            act_ref[:, columns] = (y * half).astype(BF16)
            slope = half * (1.0 + y * (1.0 - turn) * (root + (3.0 * 0.044715 * root) * square))
            slope_ref[:, columns] = slope.astype(BF16)


def project(sequence, x, blocks, bias, gain, shift, tables, width, tile, earlier, deps):
    (length, model), total, count = x.shape, blocks[0].shape[1], len(blocks)
    hidden, steps = total - 3 * width, length // tile
    rows = lambda w: pl.BlockSpec((tile, w), lambda i: (i, 0))
    out = lambda w: pl.BlockSpec((tile, w), lambda i: (sequence * steps + i, 0))
    line = lambda a: pl.BlockSpec(a.shape, lambda i: (0, 0))
    widths = (3 * width, hidden, hidden, model)
    operands = [x, bias, gain, shift, *tables, *blocks]
    return call(
        functools.partial(project_kernel, (count, width, hidden)),
        "project",
        operands + list(earlier),
        deps,
        grid=(steps,),
        in_specs=[rows(model), line(bias), line(gain), line(shift)]
        + [rows(LANES)] * 3
        + [HBM] * (count + len(earlier)),
        out_specs=[out(w) for w in widths],
        out_shape=[jax.ShapeDtypeStruct((2 * length, w), BF16) for w in widths],
        input_output_aliases={len(operands) + n: n for n in range(len(earlier))},
        scratch_shapes=[pltpu.VMEM((model, total), BF16), pltpu.SemaphoreType.DMA((count,))],
    )


def attend_kernel(block, q_ref, k_ref, v_ref, out_ref, lse_ref):
    length = q_ref.shape[0]
    lane = lax.broadcasted_iota(jnp.int32, (1, LANES), 1)
    key = lax.broadcasted_iota(jnp.int32, (block, block), 0)
    causal = key <= lax.broadcasted_iota(jnp.int32, (block, block), 1)
    for i in range(length // block):
        rows, before = pl.ds(i * block, block), pl.ds(0, i * block)
        results = []
        for h in range(2):
            mine = (lane < HEAD_DIM) if h == 0 else (lane >= HEAD_DIM)
            query = jnp.where(mine, q_ref[rows, :], 0)
            near = jnp.where(causal, dot(k_ref[rows, :], query, 1, 1), -1e30)
            highest = jnp.max(near, axis=0, keepdims=True)
            if i:
                far = dot(k_ref[before, :], query, 1, 1)
                highest = jnp.maximum(highest, jnp.max(far, axis=0, keepdims=True))
            near = jnp.exp(near - highest)
            total = jnp.sum(near, axis=0, keepdims=True)
            if i:
                far = jnp.exp(far - highest)
                total = total + jnp.sum(far, axis=0, keepdims=True)
            inverse = 1.0 / total
            result = dot((near * inverse).astype(BF16), v_ref[rows, :], 0, 0)
            if i:
                result = result + dot((far * inverse).astype(BF16), v_ref[before, :], 0, 0)
            results.append(result)
            lse_ref[0, h : h + 1, rows] = highest + jnp.log(total)
        out_ref[rows, :] = jnp.where(lane < HEAD_DIM, results[0], results[1]).astype(BF16)


def pair_specs(length, pairs):
    return lambda off: pl.BlockSpec(
        (length, LANES), lambda g: (g // pairs, off * pairs + g % pairs)
    )


def attend(qkv, length, block, deps):
    width, sequences = qkv.shape[1] // 3, qkv.shape[0] // length
    pairs = width // LANES
    at = pair_specs(length, pairs)
    return call(
        functools.partial(attend_kernel, block),
        "attend",
        [qkv, qkv, qkv],
        deps,
        grid=(sequences * pairs,),
        in_specs=[at(0), at(1), at(2)],
        out_specs=[at(0), pl.BlockSpec((1, 8, length), lambda g: (g, 0, 0))],
        out_shape=[
            jax.ShapeDtypeStruct((qkv.shape[0], width), BF16),
            jax.ShapeDtypeStruct((sequences * pairs, 8, length), F32),
        ],
    )


def attend_back_kernel(
    block,
    q_ref,
    k_ref,
    v_ref,
    grad_ref,
    mixed_ref,
    lse_ref,
    cos_ref,
    left_ref,
    right_ref,
    gq_ref,
    gk_ref,
    gv_ref,
    sum_ref,
    gk_sum,
    gv_sum,
):
    length = q_ref.shape[0]
    lane = lax.broadcasted_iota(jnp.int32, (1, LANES), 1)
    key = lax.broadcasted_iota(jnp.int32, (block, block), 0)
    causal = key <= lax.broadcasted_iota(jnp.int32, (block, block), 1)
    count = length // block
    sum_ref[...] = jnp.zeros_like(sum_ref)

    def put(ref, which, rows, value):
        value = value.astype(BF16)
        ref[rows, :] = value
        sum_ref[0, which : which + 1, :] += jnp.sum(value.astype(F32), axis=0, keepdims=True)

    def unrotated(value, rows):
        return rotated(value, cos_ref[rows, :], left_ref[rows, :], right_ref[rows, :], -1.0)

    for i in reversed(range(count)):
        rows = pl.ds(i * block, block)
        product = grad_ref[rows, :].astype(F32) * mixed_ref[rows, :].astype(F32)
        gq = None
        for h in range(2):
            mine = (lane < HEAD_DIM) if h == 0 else (lane >= HEAD_DIM)
            query = jnp.where(mine, q_ref[rows, :], 0)
            grad = jnp.where(mine, grad_ref[rows, :], 0)
            ones = jnp.where(mine, jnp.ones((8, LANES), F32), 0.0)
            delta = lax.dot_general(
                ones,
                product,
                (((1,), (1,)), ((), ())),
                precision=lax.Precision.HIGHEST,
                preferred_element_type=F32,
            )[0:1, :]
            lse = lse_ref[0, h : h + 1, rows]
            for j in range(i + 1):
                keys = pl.ds(j * block, block)
                key_rows = k_ref[keys, :]
                probs = jnp.exp(dot(key_rows, query, 1, 1) - lse)
                if j == i:
                    probs = jnp.where(causal, probs, 0.0)
                gprobs = dot(v_ref[keys, :], grad, 1, 1)
                gscores = (probs * (gprobs - delta)).astype(BF16)
                gv, gk = dot(probs.astype(BF16), grad, 1, 0), dot(gscores, query, 1, 0)
                if i == count - 1 and h == 0:
                    gv_sum[keys, :] = gv
                    gk_sum[keys, :] = gk
                else:
                    gv_sum[keys, :] += gv
                    gk_sum[keys, :] += gk
                part = dot(gscores, jnp.where(mine, key_rows, 0), 0, 0)
                gq = part if gq is None else gq + part
        put(gq_ref, 0, rows, unrotated(gq * HEAD_DIM**-0.5, rows))
    for i in range(count):
        rows = pl.ds(i * block, block)
        put(gk_ref, 1, rows, unrotated(gk_sum[rows, :], rows))
        put(gv_ref, 2, rows, gv_sum[rows, :])


def attend_back(qkv, grad, mixed, lse, tables, length, block, deps):
    width, sequences = qkv.shape[1] // 3, qkv.shape[0] // length
    pairs = width // LANES
    at = pair_specs(length, pairs)
    table = pl.BlockSpec((length, LANES), lambda g: (0, 0))
    small = pl.BlockSpec((1, 8, length), lambda g: (g, 0, 0))
    return call(
        functools.partial(attend_back_kernel, block),
        "attend_back",
        [qkv, qkv, qkv, grad, mixed, lse, *tables],
        deps,
        grid=(sequences * pairs,),
        in_specs=[at(0), at(1), at(2), at(0), at(0), small, table, table, table],
        out_specs=[at(0)] * 3 + [pl.BlockSpec((1, 8, LANES), lambda g: (g, 0, 0))],
        out_shape=[jax.ShapeDtypeStruct((qkv.shape[0], width), BF16)] * 3
        + [jax.ShapeDtypeStruct((sequences * pairs, 8, LANES), F32)],
        scratch_shapes=[pltpu.VMEM((length, LANES), F32)] * 2,
    )


def by_sequence(tile, width, steps):
    return [
        pl.BlockSpec((tile, width), lambda i: (jnp.minimum(i, steps - 1), 0)),
        pl.BlockSpec((tile, width), lambda i: (jnp.maximum(i - steps, 0), 0)),
    ]


def other_first(tile, width, steps):
    return pl.BlockSpec((tile, width), lambda i: ((i + steps) % (2 * steps), 0))


def put_by_sequence(step, steps, value, other_ref, own_ref):
    @pl.when(step < steps)
    def _():
        other_ref[...] = value

    @pl.when(step >= steps)
    def _():
        own_ref[...] = value


def branch_kernel(count, steps, mixed_ref, act_ref, *rest):
    blocks, (other_ref, own_ref, held, sems) = rest[:count], rest[count:]
    step = pl.program_id(0)

    @pl.when(step == 0)
    def _():
        loads = block_copies(blocks, columns_at(held, blocks[0].shape[1]), sems)
        for copy in loads:
            copy.start()
        for copy in loads:
            copy.wait()

    x = jnp.concatenate([mixed_ref[...], act_ref[...]], axis=1)
    put_by_sequence(step, steps, dot(x, held[...], 1, 0).astype(BF16), other_ref, own_ref)


def branch_sums(mixed, act, blocks, tile, deps):
    length, count = mixed.shape[0] // 2, len(blocks)
    inner, model, steps = blocks[0].shape[0], count * blocks[0].shape[1], length // tile
    return call(
        functools.partial(branch_kernel, count, steps),
        "branch_sums",
        [mixed, act, *blocks],
        deps,
        grid=(2 * steps,),
        in_specs=[other_first(tile, a.shape[1], steps) for a in (mixed, act)] + [HBM] * count,
        out_specs=by_sequence(tile, model, steps),
        out_shape=[jax.ShapeDtypeStruct((length, model), BF16)] * 2,
        scratch_shapes=[pltpu.VMEM((inner, model), BF16), pltpu.SemaphoreType.DMA((count,))],
    )


def grad_in_kernel(setup, dy_ref, slope_ref, *rest):
    count, width, hidden = setup
    blocks = rest[:count]
    gmixed_ref, gpre_ref, gsum_ref, dsum_ref, held, sems = rest[-6:]

    @pl.when(pl.program_id(0) == 0)
    def _():
        loads = block_copies(blocks, columns_at(held, blocks[0].shape[1]), sems)
        for copy in loads:
            copy.start()
        gsum_ref[...] = jnp.zeros_like(gsum_ref)
        dsum_ref[...] = jnp.zeros_like(dsum_ref)
        for copy in loads:
            copy.wait()

    dy = dy_ref[...]
    gmixed_ref[...] = dot(dy, held[:width, :], 1, 1).astype(BF16)
    for start in range(0, hidden, width):
        part = slice(start, start + width)
        gact = dot(dy, held[width + start : 2 * width + start, :], 1, 1)
        gpre = (gact * slope_ref[:, part].astype(F32)).astype(BF16)
        gpre_ref[:, part] = gpre
        gsum_ref[0:1, part] += jnp.sum(gpre.astype(F32), axis=0, keepdims=True)
    dsum_ref[0:1, :] += jnp.sum(dy.astype(F32), axis=0, keepdims=True)


def grad_in(sequence, dy, slope, blocks, width, tile, earlier, deps, adds=()):
    (length, model), hidden, count = dy.shape, slope.shape[1], len(blocks)
    steps = length // tile
    out = lambda w: pl.BlockSpec((tile, w), lambda i: (sequence * steps + i, 0))
    total = lambda w: pl.BlockSpec((8, w), lambda i: (0, 0))
    operands = [dy, slope, *blocks]
    return call(
        functools.partial(grad_in_kernel, (count, width, hidden)),
        "grad_in",
        operands + list(earlier),
        deps,
        adds=adds,
        grid=(steps,),
        in_specs=[pl.BlockSpec((tile, model), lambda i: (i, 0)), out(hidden)]
        + [HBM] * (count + len(earlier)),
        out_specs=[out(width), out(hidden), total(hidden), total(model)],
        out_shape=[jax.ShapeDtypeStruct((2 * length, w), BF16) for w in (width, hidden)]
        + [jax.ShapeDtypeStruct((8, w), F32) for w in (hidden, model)],
        input_output_aliases={len(operands) + n: n for n in range(len(earlier))},
        scratch_shapes=[
            pltpu.VMEM((width + hidden, model), BF16),
            pltpu.SemaphoreType.DMA((count,)),
        ],
    )


def grad_normed_kernel(count, half, many, gq_ref, gk_ref, gv_ref, gpre_ref, x_ref, *rest):
    blocks, theirs, rest = rest[:count], rest[count : count + many], rest[count + many :]
    *outs, sum_ref, held, sems = rest
    step, turns = pl.program_id(0), pl.num_programs(0) // 2
    size, few, me = blocks[0].shape[0], count // 2, lax.axis_index("dp")

    @pl.when(pl.program_id(0) == 0)
    def _():
        for start in (True, False):
            for j, block in enumerate(blocks):
                owner = lax.bitwise_xor(me, j) - half * few

                @pl.when((owner >= 0) & (owner < few))
                def _(start=start, j=j, block=block, owner=owner):
                    copy = pltpu.make_async_copy(block, held.at[span(owner, size)], sems.at[j])
                    if start:
                        copy.start()
                    else:
                        copy.wait()

        sum_ref[...] = jnp.zeros_like(sum_ref)

    columns = slice(half * few * size, (half + 1) * few * size)
    normal = normalized(x_ref[...])[:, columns]
    g = jnp.concatenate([gq_ref[...], gk_ref[...], gv_ref[...], gpre_ref[...]], axis=1)
    result = dot(g, held[...], 1, 1)
    sum_ref[0:1, :] += jnp.sum(result * normal, axis=0, keepdims=True)
    sum_ref[1:2, :] += jnp.sum(result, axis=0, keepdims=True)
    if theirs:
        result = result + jnp.where(step < turns, theirs[0][...], theirs[1][...]).astype(F32)
        outs[0][...] = result.astype(BF16)
    else:
        result = result.astype(BF16)
        for n, out_ref in enumerate(outs):

            @pl.when(step // turns == n)
            def _(out_ref=out_ref):
                out_ref[...] = result


def grad_normed_sums(sequence, half, gqkv, gpre, x, blocks, theirs, tile, deps, adds=()):
    (length, model), count, total = x.shape, len(blocks), blocks[0].shape[1]
    steps, part = length // tile, model // 2
    operands = [*gqkv, gpre]
    rows, few = pl.BlockSpec((tile, part), lambda i: (i, 0)), steps // 2
    parts = [
        pl.BlockSpec((tile, part), lambda i: (jnp.minimum(i, few - 1), 0)),
        pl.BlockSpec((tile, part), lambda i: (jnp.maximum(i - few, 0), 0)),
    ]
    outs = [length] if theirs else [length // 2] * 2
    return call(
        functools.partial(grad_normed_kernel, count, half, len(theirs)),
        "grad_normed_sums",
        operands + [x, *blocks, *theirs],
        deps,
        adds=adds,
        grid=(steps,),
        in_specs=[
            pl.BlockSpec((tile, a.shape[1]), lambda i: (sequence * steps + i, 0)) for a in operands
        ]
        + [pl.BlockSpec((tile, model), lambda i: (i, 0))]
        + [HBM] * count
        + (parts if theirs else []),
        out_specs=([rows] if theirs else parts) + [pl.BlockSpec((8, part), lambda i: (0, 0))],
        out_shape=[jax.ShapeDtypeStruct((n, part), BF16) for n in outs]
        + [jax.ShapeDtypeStruct((8, part), F32)],
        scratch_shapes=[pltpu.VMEM((part, total), BF16), pltpu.SemaphoreType.DMA((count,))],
    )


def weight_grad_kernel(writes, left, rows, many, at_ref, *refs):
    cuts, (*refs, held, grad, sems) = refs[:many], refs[many:]
    whole, outs = refs[: len(refs) - len(writes)], refs[len(refs) - len(writes) :]
    step, core, loads, first = pl.program_id(0), lax.rem(lax.axis_index("dp"), 2), [], 0
    for ref in whole:
        columns = pl.ds(first, ref.shape[1])
        first += ref.shape[1]
        for start in range(0, ref.shape[0], rows):
            part = pl.ds(start, rows)
            loads.append((ref.at[part], held.at[part, columns]))
    loads = [pltpu.make_async_copy(*pair, sems.at[n]) for n, pair in enumerate(loads)]

    @pl.when(step == 0)
    def _():
        for copy in loads:
            copy.start()
        for copy in loads:
            copy.wait()

    cut = jnp.concatenate([ref[...] for ref in cuts], axis=0)
    pair = (cut, held[...]) if left else (held[...], cut)
    grad[...] = dot(*pair, 0, 0).astype(BF16)
    size = cut.shape[1] // 2
    for half, steps, out_ref in writes_of(writes, outs):
        here = functools.reduce(jnp.logical_or, [step == s for s in steps])

        @pl.when(here)
        def _(half=half, out_ref=out_ref):
            mine = span(core if half == 0 else 1 - core, size)
            out_ref[0] = grad[mine, :] if left else grad[:, mine]


def writes_of(writes, outs):
    return [(half, steps, out) for (half, steps), out in zip(writes, outs)]


def weight_grads(me, xs, gs, count, deps, left):
    plan, chips = scatter_plan(count), count // 2
    order = [j // 2 for s in plan[0] for j in s]
    sets = [(half, s) for s in range(len(plan[0])) for half in range(2)]
    writes = [(half, [order.index(j // 2) for j in plan[half][s]]) for half, s in sets]
    table = []
    for _, steps in writes:
        for i in range(chips):
            later = [w for w in steps if w >= i]
            table.append(steps.index(min(later) if later else max(steps)))
    owners = lax.bitwise_xor(me // 2, jnp.array(order, jnp.int32))
    at = jnp.concatenate([owners, jnp.array(table, jnp.int32)])
    cut, whole = (xs, gs) if left else (gs, xs)
    length = whole[0].shape[0]
    size, full = cut[0].shape[1] // count, sum(a.shape[1] for a in whole)
    shape = (size, full) if left else (full, size)
    pieces = 8 // len(whole)

    def out(n):
        return pl.BlockSpec((1, *shape), lambda i, at: (at[chips * (n + 1) + i], 0, 0))

    outs = call(
        functools.partial(weight_grad_kernel, writes, left, length // pieces, len(cut)),
        "weight_grads",
        [*cut, *whole],
        deps,
        (at,),
        grid=(chips,),
        in_specs=[pl.BlockSpec((a.shape[0], 2 * size), lambda i, at: (0, at[i])) for a in cut]
        + [HBM] * len(whole),
        out_specs=[out(n) for n in range(len(sets))],
        out_shape=[
            jax.ShapeDtypeStruct((len(plan[half][s]), *shape), BF16) for half, s in sets
        ],
        scratch_shapes=[
            pltpu.VMEM((length, full), BF16),
            pltpu.VMEM((2 * size, full) if left else (full, 2 * size), BF16),
            pltpu.SemaphoreType.DMA((pieces * len(whole),)),
        ],
    )
    return [[o for o, (half, _) in zip(outs, sets) if half == h] for h in range(2)]


def norm_back_kernel(tokens_ref, dy_ref, gain_ref, left_ref, right_ref, out_ref):
    x = tokens_ref[...].astype(F32)
    centered = x - jnp.mean(x, axis=1, keepdims=True)
    inverse_std = lax.rsqrt(jnp.mean(centered * centered, axis=1, keepdims=True) + EPS)
    normal = centered * inverse_std
    grad = jnp.concatenate([left_ref[...], right_ref[...]], axis=1).astype(F32)
    scaled = grad * gain_ref[...]
    first_mean = jnp.mean(scaled, axis=1, keepdims=True)
    second_mean = jnp.mean(scaled * normal, axis=1, keepdims=True)
    back = (scaled - first_mean - normal * second_mean) * inverse_std
    out_ref[...] = (dy_ref[...].astype(F32) + back).astype(BF16)


def norm_back(tokens, dy, gain, halves, deps):
    rows, model = tokens.shape
    tile = min(64, rows)
    part = lambda w: pl.BlockSpec((tile, w), lambda i: (i, 0))
    return call(
        norm_back_kernel,
        "norm_back",
        [tokens, dy, gain, *halves],
        deps,
        grid=(rows // tile,),
        in_specs=[part(model), part(model), pl.BlockSpec((1, model), lambda i: (0, 0))]
        + [part(model // 2)] * 2,
        out_specs=part(model),
        out_shape=jax.ShapeDtypeStruct((rows, model), BF16),
    )


def across(value, bit, count):
    return lax.ppermute(value, "dp", [(i, i ^ bit) for i in range(count)])


def added(addends):
    return sum(a.astype(F32) for a in addends).astype(BF16)


def chip_bits(count):
    bits, bit = [], 2
    while bit < count:
        bits.append(bit)
        bit *= 2
    return bits


class BlockGather:
    def __init__(self, own, sibling, count):
        self.held, self.count = {0: own, 1: sibling}, count
        self.orders = (chip_bits(count), chip_bits(count)[::-1])

    def own_to(self, s):
        if s < len(self.orders[0]):
            for half in range(2):
                bit = self.orders[half][s]
                self.held[half ^ bit] = across(self.held[half], bit, self.count)

    def rest(self):
        for s in range(1, len(self.orders[0])):
            for half in range(2):
                order = self.orders[half]
                for j in [j for j in self.held if j % 2 == half]:
                    if j ^ order[s] not in self.held and not any(j & b for b in order[s:]):
                        self.held[j ^ order[s]] = across(self.held[j], order[s], self.count)

    def fenced(self, others=(), deps=()):
        keys = sorted(self.held)
        values = fence([self.held[j] for j in keys] + list(others), deps)
        self.held = dict(zip(keys, values))
        return values[len(keys) :]

    def blocks(self):
        return [self.held[j] for j in range(self.count)]


def scatter_orders(count):
    return (chip_bits(count)[::-1], chip_bits(count))


def scatter_plan(count):
    plan = []
    for half, order in enumerate(scatter_orders(count)):
        sets, rest = [[half]], [half]
        for bit in reversed(order):
            sets.insert(0, [j ^ bit for j in rest])
            rest = sets[0] + rest
        plan.append(sets)
    return plan


class BlockScatter:
    def __init__(self, halves, count):
        self.count, self.orders, self.plan = count, scatter_orders(count), scatter_plan(count)
        self.held = [[[(a, 0)] for a in arrays] for arrays in halves]
        self.steps = len(self.orders[0])

    def parts(self, half, s):
        many = len(self.plan[half][s])
        return [a[first : first + many] for a, first in self.held[half][s]]

    def total(self, half, s):
        if len(self.held[half][s]) > 1:
            self.held[half][s] = [(added(self.parts(half, s)), 0)]
        return self.parts(half, s)[0]

    def ready(self, s):
        return [self.total(half, s) for half in range(2)]

    def adds(self, s):
        return [(len(self.plan[half][s]), self.held[half][s]) for half in range(2)]

    def settle(self, s, sums):
        for half in range(2):
            self.held[half][s] = [(sums[half], 0)]

    def send(self, s):
        return [across(self.total(h, s), self.orders[h][s], self.count) for h in range(2)]

    def arrive(self, s, came):
        for half in range(2):
            first = 0
            for t in range(s + 1, len(self.plan[half])):
                self.held[half][t].append((came[half], first))
                first += len(self.plan[half][t])

    def between(self):
        for s in range(1, self.steps - 1):
            self.arrive(s, self.send(s))

    def last(self):
        return self.total(1, -1)[0]

    def finish(self, theirs):
        return sum(a[0].astype(F32) for a in self.parts(0, -1)), theirs.astype(F32)


def on_device(
    tokens,
    norm_gain,
    norm_bias,
    qkv_weight,
    qkv_bias,
    dense_weight,
    dense_bias,
    up_weight,
    up_bias,
    down_weight,
    down_bias,
    cotangent,
    *,
    ndp,
    nmp,
):
    me = lax.axis_index("dp")
    core = me % 2
    length, model = tokens.shape[0] * nmp, tokens.shape[1]
    tile, block = min(256, length), min(512, length)
    width, hidden = qkv_weight.shape[2] // 2, up_weight.shape[1] // 2
    chip_steps = len(chip_bits(ndp))
    rank = lambda array, axis, which, size: lax.dynamic_slice_in_dim(
        array, which * size, size, axis
    )

    def row_pack(which):
        qkv = rank(qkv_weight, 2, which, width)
        return jnp.concatenate([qkv[0], qkv[1], qkv[2], rank(up_weight, 1, which, hidden)], axis=1)

    def column_pack(which):
        return jnp.concatenate(
            [rank(dense_weight, 0, which, width), rank(down_weight, 0, which, hidden)], axis=0
        )

    pairs = width // LANES
    swap = lambda array: across(array, 1, ndp)
    line_gather = lambda array: lax.all_gather(array, "mp", axis=0, tiled=True)
    line_scatter = lambda array: lax.psum_scatter(array, "mp", scatter_dimension=0, tiled=True)
    x_own, dy_own = line_gather(tokens), line_gather(cotangent)
    rows = BlockGather(row_pack(core), swap(row_pack(1 - core)), ndp)
    columns = BlockGather(column_pack(core), swap(column_pack(1 - core)), ndp)
    rows.own_to(0)
    rows.fenced(deps=columns.held.values())
    rows.own_to(1)
    rows.fenced()
    rows.rest()
    x_own, *held = fence([x_own, columns.held[0], columns.held[1]], rows.blocks())
    columns.held = dict(enumerate(held))

    tables = rotary_tables(length)
    bias = jnp.concatenate(
        [
            rank(qkv_bias, 1, core, width).astype(F32).reshape(1, 3 * width),
            rank(up_bias[None, :], 1, core, hidden).astype(F32),
        ],
        axis=1,
    )
    gain, shift = norm_gain.astype(F32)[None, :], norm_bias.astype(F32)[None, :]
    x_other = swap(x_own)
    columns.own_to(0)
    common = (rows.blocks(), bias, gain, shift, tables, width, tile)
    first = project(0, x_own, *common, (), [columns.held[0]])
    (x_other,) = columns.fenced([x_other], [first[0]])
    columns.own_to(1)
    qkv, act, slope, normed = project(1, x_other, *common, first, [columns.held[0]])
    columns.fenced(deps=[qkv])
    columns.rest()
    mixed, lse = attend(qkv, length, block, [columns.held[0]])
    columns.fenced(deps=[mixed])
    other_sums, own_sums = branch_sums(mixed, act, columns.blocks(), tile, [])
    other_sums, dy_own = fence([other_sums, dy_own], [own_sums])
    theirs = swap(other_sums)
    dy_other = swap(dy_own)

    grads = (slope, columns.blocks(), width, tile)
    grad_a = grad_in(0, dy_own, *grads, (), [own_sums])
    theirs, dy_other = fence([theirs, dy_other], [grad_a[2]])
    gmixed, gpre, *grad_b, total = grad_in(
        1, dy_other, *grads, grad_a[:2], [], [(1, [(own_sums[None], 0), (theirs[None], 0)])]
    )
    branches = line_scatter(total[0])
    column_grads = BlockScatter(
        weight_grads(me, [mixed, act], [dy_own, dy_other], ndp, [grad_b[0]], left=False), ndp
    )
    column_came = column_grads.send(0)
    gq, gk, gv, qkv_sums = attend_back(
        qkv, gmixed, mixed, lse, tables, length, block, [column_grads.held[0][0][0][0]]
    )

    def normed_part(sequence, half, theirs, deps, adds=()):
        x = x_other if sequence else x_own
        return grad_normed_sums(
            sequence, half, (gq, gk, gv), gpre, x, rows.blocks(), theirs, tile, deps, adds
        )

    *other_a, sums_a = normed_part(1, 0, [], [column_grads.held[0][0][0][0]])
    theirs_a = [swap(a) for a in other_a]
    column_came = fence(column_came, [sums_a])
    *other_b, sums_b = normed_part(1, 1, [], [sums_a, column_came[0]])
    moved = fence([*other_b, *theirs_a], [sums_b])
    other_b, theirs_a = moved[:2], moved[2:]
    theirs_b = [swap(a) for a in other_b]
    column_grads.arrive(0, column_came)
    column_grads.between()
    total_a, more_a, *settled = normed_part(
        0, 0, theirs_a, [other_b[0]], column_grads.adds(chip_steps - 1)
    )
    column_grads.settle(chip_steps - 1, settled)
    half_a = line_scatter(total_a)
    column_came = column_grads.send(chip_steps - 1)
    up_grads = BlockScatter(
        weight_grads(me, [normed], [gpre], ndp, [more_a], left=True), ndp
    )
    c0, c1, branches, u0, u1, *theirs_b = fence(
        [*column_came, branches, *(up_grads.held[h][0][0][0] for h in range(2)), *theirs_b]
    )
    up_grads.held[0][0], up_grads.held[1][0] = [(u0, 0)], [(u1, 0)]
    up_came = up_grads.send(0)
    column_grads.arrive(chip_steps - 1, [c0, c1])
    total_b, more_b, column_last = normed_part(
        0, 1, theirs_b, [u0], [column_grads.adds(len(column_grads.plan[1]) - 1)[1]]
    )
    half_b = line_scatter(total_b)
    column_theirs = swap(column_last[0])
    qkv_sum = (
        qkv_sums.reshape(2, pairs, 8, LANES).sum(0)[:, :3, :].transpose(1, 0, 2).reshape(3 * width)
    )
    norm_sums = jnp.concatenate([(sums_a + more_a)[:2], (sums_b + more_b)[:2]], axis=1)
    small = jnp.concatenate(
        [
            norm_sums.reshape(2 * model),
            qkv_sum,
            grad_a[2][0] + grad_b[0][0],
            grad_a[3][0] + grad_b[1][0],
        ]
    )
    bits = chip_bits(ndp)
    for bit in bits[:-2]:
        small = small + across(small, bit, ndp)
    small_came = across(small, bits[-2], ndp)
    qkv_grads = BlockScatter(
        weight_grads(me, [normed], [gq, gk, gv], ndp, [small], left=True), ndp
    )
    half_a, q0, q1, small_came, column_theirs, u0, u1 = fence(
        [
            half_a,
            *(qkv_grads.held[h][0][0][0] for h in range(2)),
            small_came,
            column_theirs,
            *up_came,
        ]
    )
    up_grads.arrive(0, [u0, u1])
    up_grads.between()
    qkv_grads.held[0][0], qkv_grads.held[1][0] = [(q0, 0)], [(q1, 0)]
    qkv_came = qkv_grads.send(0)
    up_came = up_grads.send(chip_steps - 1)
    small = small + small_came
    small_came = across(small, bits[-1], ndp)
    u0, u1, q0, q1, small_came, column_theirs, branches = fence(
        [*up_came, *qkv_came, small_came, column_theirs, branches]
    )
    up_grads.arrive(chip_steps - 1, [u0, u1])
    up_theirs = swap(up_grads.last())
    qkv_grads.arrive(0, [q0, q1])
    qkv_grads.between()
    small = small + small_came
    q0, q1, small = fence([*qkv_grads.send(chip_steps - 1), small])
    qkv_grads.arrive(chip_steps - 1, [q0, q1])
    small_other = swap(small)
    qkv_theirs = swap(qkv_grads.last())
    norm_sums, half_b = fence([small[: 2 * model] + small_other[: 2 * model], half_b])
    norm_sums = [norm_sums] + [
        lax.ppermute(norm_sums, "mp", [(i, i ^ j) for i in range(nmp)]) for j in range(1, nmp)
    ]
    while len(norm_sums) > 1:
        norm_sums = [a + b for a, b in zip(norm_sums[::2], norm_sums[1::2])]
    norm_sums = norm_sums[0]

    output = (
        tokens.astype(F32)
        + branches.astype(F32)
        + (dense_bias.astype(F32) + down_bias.astype(F32))[None, :]
    ).astype(BF16)

    def both(mine, theirs, axis):
        return jnp.where(
            core == 0,
            jnp.concatenate([mine, theirs], axis=axis),
            jnp.concatenate([theirs, mine], axis=axis),
        )

    mine, theirs = column_grads.finish(column_theirs)
    owned_dense = both(mine[:width], theirs[:width], 0)
    owned_down = both(mine[width:], theirs[width:], 0)
    owned_up = both(*up_grads.finish(up_theirs), 1)
    mine, theirs = qkv_grads.finish(qkv_theirs)
    owned_qkv = jnp.stack(
        [
            both(mine[:, c * width : (c + 1) * width], theirs[:, c * width : (c + 1) * width], 1)
            for c in range(3)
        ]
    )

    inner = 3 * width + hidden
    grad_out_bias = small[2 * model + inner :]
    here, there = (a[2 * model : 2 * model + inner] for a in (small, small_other))
    even, odd = jnp.where(core == 0, here, there), jnp.where(core == 0, there, here)
    grad_qkv_bias = jnp.concatenate(
        [a[: 3 * width].reshape(3, width) for a in (even, odd)], axis=1
    )
    grad_up_bias = jnp.concatenate([even[3 * width :], odd[3 * width :]])

    grad_tokens = norm_back(tokens, cotangent, gain, [half_a, half_b], [])
    return (
        output,
        grad_tokens,
        norm_sums[:model],
        norm_sums[model:],
        owned_qkv,
        grad_qkv_bias,
        owned_dense,
        grad_out_bias,
        owned_up,
        grad_up_bias,
        owned_down,
        grad_out_bias,
    )


def solution(mesh):
    return jax.shard_map(
        functools.partial(on_device, ndp=mesh.shape["dp"], nmp=mesh.shape["mp"]),
        mesh=mesh,
        in_specs=(
            P(("dp", "mp"), None),
            P(),
            P(),
            P(None, "dp", "mp"),
            P(None, "mp"),
            P("mp", "dp"),
            P(),
            P("dp", "mp"),
            P("mp"),
            P("mp", "dp"),
            P(),
            P(("dp", "mp"), None),
        ),
        out_specs=(
            P(("dp", "mp"), None),
            P(("dp", "mp"), None),
            P(),
            P(),
            P(None, "dp", "mp"),
            P(None, "mp"),
            P("mp", "dp"),
            P(),
            P("dp", "mp"),
            P("mp"),
            P("mp", "dp"),
            P(),
        ),
        check_vma=False,
    )
```

```python
import functools

import jax
import jax.numpy as jnp
import numpy as np
from jax import lax
from jax.experimental import pallas as pl
from jax.experimental.pallas import tpu as pltpu
from jax.sharding import PartitionSpec as P

HEAD_DIM = 64
ROT = 32
EPS = 1e-05
LANES = 128
F32 = jnp.float32
BF16 = jnp.bfloat16
HBM = pl.BlockSpec(memory_space=pltpu.HBM)


def dot(lhs, rhs, lhs_dim, rhs_dim):
    return lax.dot_general(
        lhs, rhs, (((lhs_dim,), (rhs_dim,)), ((), ())), preferred_element_type=F32
    )


def call(kernel, name, operands, deps=(), scalars=(), adds=(), vmem=63, **spec):
    deps, out_shape = tuple(deps), spec.pop("out_shape")
    single = not isinstance(out_shape, list)
    out_shape = [out_shape] if single else out_shape
    out_specs = spec.pop("out_specs")
    out_specs = [out_specs] if single else list(out_specs)
    extra, extra_specs, sizes = [], [], []
    steps = spec["grid"][0] if adds else 1
    for many, addends in adds:
        _, rows, columns = addends[0][0].shape
        block = (many, rows // steps, columns)
        for array, first in addends:
            extra.append(array)
            extra_specs.append(
                pl.BlockSpec(block, lambda i, *at, first=first, many=many: (first // many, i, 0))
            )
        out_shape = out_shape + [jax.ShapeDtypeStruct((many, rows, columns), BF16)]
        out_specs = out_specs + [pl.BlockSpec(block, lambda i, *at: (0, i, 0))]
        sizes.append(len(addends))
    lead, outs = len(scalars) + len(operands), len(out_shape) - len(adds)

    def body(*refs):
        first = lead + len(extra) + len(deps)
        kernel(*refs[:lead], *refs[first : first + outs], *refs[first + outs + len(adds) :])
        sources = refs[lead : lead + len(extra)]
        for n, out in zip(sizes, refs[first + outs : first + outs + len(adds)]):
            out[...] = sum(ref[...].astype(F32) for ref in sources[:n]).astype(BF16)
            sources = sources[n:]

    in_specs = list(spec.pop("in_specs")) + extra_specs + [HBM] * len(deps)
    aliases = spec.pop("input_output_aliases", {})
    if scalars:
        grid_spec = pltpu.PrefetchScalarGridSpec(
            num_scalar_prefetch=len(scalars), in_specs=in_specs, out_specs=out_specs, **spec
        )
        spec = {"grid_spec": grid_spec}
    else:
        spec.update(in_specs=in_specs, out_specs=out_specs)
    results = pl.pallas_call(
        body,
        out_shape=out_shape,
        input_output_aliases=aliases,
        compiler_params=pltpu.CompilerParams(vmem_limit_bytes=vmem << 20),
        cost_estimate=pl.CostEstimate(flops=0, transcendentals=0, bytes_accessed=0),
        name=name,
        **spec,
    )(*scalars, *operands, *extra, *deps)
    return results[0] if single and not adds else results


def fence(values, deps=()):
    return list(
        call(
            lambda *refs: None,
            "fence",
            values,
            deps,
            in_specs=[HBM] * len(values),
            out_specs=[HBM] * len(values),
            out_shape=[jax.ShapeDtypeStruct(v.shape, v.dtype) for v in values],
            input_output_aliases={n: n for n in range(len(values))},
        )
    )


def rotary_tables(length):
    positions = np.arange(length, dtype=np.float32)
    frequency = 10000.0 ** (-np.arange(ROT // 2, dtype=np.float64) * 2.0 / ROT)
    angles = positions[:, None] * frequency.astype(np.float32)[None, :]
    cosine, sine = np.cos(angles.astype(np.float64)), np.sin(angles.astype(np.float64))
    rest = HEAD_DIM - ROT
    none = np.zeros((length, ROT // 2))
    ones, zeros = np.ones((length, rest)), np.zeros((length, rest))
    straight = np.concatenate([cosine, cosine, ones], axis=1)
    left = np.concatenate([-sine, none, zeros], axis=1)
    right = np.concatenate([none, sine, zeros], axis=1)
    return [
        jnp.asarray(np.concatenate([t, t], axis=1).astype(np.float32))
        for t in (straight, left, right)
    ]


def rotated(u, straight, left, right, sign):
    half = ROT // 2
    turned = pltpu.roll(u, LANES - half, 1) * left + pltpu.roll(u, half, 1) * right
    return u * straight + sign * turned


def normalized(x):
    x = x.astype(F32)
    centered = x - jnp.mean(x, axis=1, keepdims=True)
    variance = jnp.mean(centered * centered, axis=1, keepdims=True)
    return centered * lax.rsqrt(variance + EPS)


def block_copies(blocks, place, sems):
    me = lax.axis_index("dp")
    return [
        pltpu.make_async_copy(block, place(lax.bitwise_xor(me, j)), sems.at[j])
        for j, block in enumerate(blocks)
    ]


def span(owner, size):
    return pl.ds(pl.multiple_of(owner * size, size), size)


def rows_at(ref, size):
    return lambda owner: ref.at[pl.ds(pl.multiple_of(owner * size, size), size)]


def columns_at(ref, size):
    return lambda owner: ref.at[:, pl.ds(pl.multiple_of(owner * size, size), size)]


def project_kernel(setup, x_ref, bias_ref, gain_ref, shift_ref, cos_ref, left_ref, right_ref, *rest):
    count, width, hidden = setup
    blocks = rest[:count]
    qkv_ref, act_ref, slope_ref, normed_ref, held, sems = rest[-6:]

    @pl.when(pl.program_id(0) == 0)
    def _():
        loads = block_copies(blocks, rows_at(held, blocks[0].shape[0]), sems)
        for copy in loads:
            copy.start()
        for copy in loads:
            copy.wait()

    x = (normalized(x_ref[...]) * gain_ref[...] + shift_ref[...]).astype(BF16)
    normed_ref[...] = x
    root = 0.7978845608028654
    for t in range((3 * width + hidden) // width):
        columns = slice(t * width, (t + 1) * width)
        y = dot(x, held[:, columns], 1, 0) + bias_ref[:, columns]
        if t < 3:
            for g in range(width // LANES):
                part = y[:, g * LANES : (g + 1) * LANES]
                if t < 2:
                    part = rotated(part, cos_ref[...], left_ref[...], right_ref[...], 1.0)
                if t == 0:
                    part = part * HEAD_DIM**-0.5
                start = t * width + g * LANES
                qkv_ref[:, start : start + LANES] = part.astype(BF16)
        else:
            columns = slice((t - 3) * width, (t - 2) * width)
            square = y * y
            turn = jnp.tanh(root * y * (1.0 + 0.044715 * square))
            half = 0.5 * (1.0 + turn)
            act_ref[:, columns] = (y * half).astype(BF16)
            slope = half * (1.0 + y * (1.0 - turn) * (root + (3.0 * 0.044715 * root) * square))
            slope_ref[:, columns] = slope.astype(BF16)


def project(sequence, x, blocks, bias, gain, shift, tables, width, tile, earlier, deps):
    (length, model), total, count = x.shape, blocks[0].shape[1], len(blocks)
    hidden, steps = total - 3 * width, length // tile
    rows = lambda w: pl.BlockSpec((tile, w), lambda i: (i, 0))
    out = lambda w: pl.BlockSpec((tile, w), lambda i: (sequence * steps + i, 0))
    line = lambda a: pl.BlockSpec(a.shape, lambda i: (0, 0))
    widths = (3 * width, hidden, hidden, model)
    operands = [x, bias, gain, shift, *tables, *blocks]
    return call(
        functools.partial(project_kernel, (count, width, hidden)),
        "project",
        operands + list(earlier),
        deps,
        grid=(steps,),
        in_specs=[rows(model), line(bias), line(gain), line(shift)]
        + [rows(LANES)] * 3
        + [HBM] * (count + len(earlier)),
        out_specs=[out(w) for w in widths],
        out_shape=[jax.ShapeDtypeStruct((2 * length, w), BF16) for w in widths],
        input_output_aliases={len(operands) + n: n for n in range(len(earlier))},
        scratch_shapes=[pltpu.VMEM((model, total), BF16), pltpu.SemaphoreType.DMA((count,))],
    )


def attend_kernel(block, q_ref, k_ref, v_ref, out_ref, lse_ref):
    length = q_ref.shape[0]
    lane = lax.broadcasted_iota(jnp.int32, (1, LANES), 1)
    key = lax.broadcasted_iota(jnp.int32, (block, block), 0)
    causal = key <= lax.broadcasted_iota(jnp.int32, (block, block), 1)
    for i in range(length // block):
        rows, before = pl.ds(i * block, block), pl.ds(0, i * block)
        results = []
        for h in range(2):
            mine = (lane < HEAD_DIM) if h == 0 else (lane >= HEAD_DIM)
            query = jnp.where(mine, q_ref[rows, :], 0)
            near = jnp.where(causal, dot(k_ref[rows, :], query, 1, 1), -1e30)
            highest = jnp.max(near, axis=0, keepdims=True)
            if i:
                far = dot(k_ref[before, :], query, 1, 1)
                highest = jnp.maximum(highest, jnp.max(far, axis=0, keepdims=True))
            near = jnp.exp(near - highest)
            total = jnp.sum(near, axis=0, keepdims=True)
            if i:
                far = jnp.exp(far - highest)
                total = total + jnp.sum(far, axis=0, keepdims=True)
            inverse = 1.0 / total
            result = dot((near * inverse).astype(BF16), v_ref[rows, :], 0, 0)
            if i:
                result = result + dot((far * inverse).astype(BF16), v_ref[before, :], 0, 0)
            results.append(result)
            lse_ref[0, h : h + 1, rows] = highest + jnp.log(total)
        out_ref[rows, :] = jnp.where(lane < HEAD_DIM, results[0], results[1]).astype(BF16)


def pair_specs(length, pairs):
    return lambda off: pl.BlockSpec(
        (length, LANES), lambda g: (g // pairs, off * pairs + g % pairs)
    )


def attend(qkv, length, block, deps):
    width, sequences = qkv.shape[1] // 3, qkv.shape[0] // length
    pairs = width // LANES
    at = pair_specs(length, pairs)
    return call(
        functools.partial(attend_kernel, block),
        "attend",
        [qkv, qkv, qkv],
        deps,
        grid=(sequences * pairs,),
        in_specs=[at(0), at(1), at(2)],
        out_specs=[at(0), pl.BlockSpec((1, 8, length), lambda g: (g, 0, 0))],
        out_shape=[
            jax.ShapeDtypeStruct((qkv.shape[0], width), BF16),
            jax.ShapeDtypeStruct((sequences * pairs, 8, length), F32),
        ],
    )


def attend_back_kernel(
    block,
    q_ref,
    k_ref,
    v_ref,
    grad_ref,
    mixed_ref,
    lse_ref,
    cos_ref,
    left_ref,
    right_ref,
    gq_ref,
    gk_ref,
    gv_ref,
    sum_ref,
    gk_sum,
    gv_sum,
):
    length = q_ref.shape[0]
    lane = lax.broadcasted_iota(jnp.int32, (1, LANES), 1)
    key = lax.broadcasted_iota(jnp.int32, (block, block), 0)
    causal = key <= lax.broadcasted_iota(jnp.int32, (block, block), 1)
    count = length // block
    sum_ref[...] = jnp.zeros_like(sum_ref)

    def put(ref, which, rows, value):
        value = value.astype(BF16)
        ref[rows, :] = value
        sum_ref[0, which : which + 1, :] += jnp.sum(value.astype(F32), axis=0, keepdims=True)

    def unrotated(value, rows):
        return rotated(value, cos_ref[rows, :], left_ref[rows, :], right_ref[rows, :], -1.0)

    for i in reversed(range(count)):
        rows = pl.ds(i * block, block)
        product = grad_ref[rows, :].astype(F32) * mixed_ref[rows, :].astype(F32)
        gq = None
        for h in range(2):
            mine = (lane < HEAD_DIM) if h == 0 else (lane >= HEAD_DIM)
            query = jnp.where(mine, q_ref[rows, :], 0)
            grad = jnp.where(mine, grad_ref[rows, :], 0)
            ones = jnp.where(mine, jnp.ones((8, LANES), F32), 0.0)
            delta = lax.dot_general(
                ones,
                product,
                (((1,), (1,)), ((), ())),
                precision=lax.Precision.HIGHEST,
                preferred_element_type=F32,
            )[0:1, :]
            lse = lse_ref[0, h : h + 1, rows]
            for j in range(i + 1):
                keys = pl.ds(j * block, block)
                key_rows = k_ref[keys, :]
                probs = jnp.exp(dot(key_rows, query, 1, 1) - lse)
                if j == i:
                    probs = jnp.where(causal, probs, 0.0)
                gprobs = dot(v_ref[keys, :], grad, 1, 1)
                gscores = (probs * (gprobs - delta)).astype(BF16)
                gv, gk = dot(probs.astype(BF16), grad, 1, 0), dot(gscores, query, 1, 0)
                if i == count - 1 and h == 0:
                    gv_sum[keys, :] = gv
                    gk_sum[keys, :] = gk
                else:
                    gv_sum[keys, :] += gv
                    gk_sum[keys, :] += gk
                part = dot(gscores, jnp.where(mine, key_rows, 0), 0, 0)
                gq = part if gq is None else gq + part
        put(gq_ref, 0, rows, unrotated(gq * HEAD_DIM**-0.5, rows))
    for i in range(count):
        rows = pl.ds(i * block, block)
        put(gk_ref, 1, rows, unrotated(gk_sum[rows, :], rows))
        put(gv_ref, 2, rows, gv_sum[rows, :])


def attend_back(sequence, qkv, grad, mixed, lse, tables, length, block, deps):
    width = qkv.shape[1] // 3
    pairs = width // LANES
    at = lambda off: pl.BlockSpec((length, LANES), lambda g: (sequence, off * pairs + g))
    out = pl.BlockSpec((length, LANES), lambda g: (0, g))
    table = pl.BlockSpec((length, LANES), lambda g: (0, 0))
    small = pl.BlockSpec((1, 8, length), lambda g: (sequence * pairs + g, 0, 0))
    return call(
        functools.partial(attend_back_kernel, block),
        "attend_back",
        [qkv, qkv, qkv, grad, mixed, lse, *tables],
        deps,
        grid=(pairs,),
        in_specs=[at(0), at(1), at(2), at(0), at(0), small, table, table, table],
        out_specs=[out] * 3 + [pl.BlockSpec((1, 8, LANES), lambda g: (g, 0, 0))],
        out_shape=[jax.ShapeDtypeStruct((length, width), BF16)] * 3
        + [jax.ShapeDtypeStruct((pairs, 8, LANES), F32)],
        scratch_shapes=[pltpu.VMEM((length, LANES), F32)] * 2,
    )


def by_sequence(tile, width, steps):
    return [
        pl.BlockSpec((tile, width), lambda i: (jnp.minimum(i, steps - 1), 0)),
        pl.BlockSpec((tile, width), lambda i: (jnp.maximum(i - steps, 0), 0)),
    ]


def other_first(tile, width, steps):
    return pl.BlockSpec((tile, width), lambda i: ((i + steps) % (2 * steps), 0))


def put_by_sequence(step, steps, value, other_ref, own_ref):
    @pl.when(step < steps)
    def _():
        other_ref[...] = value

    @pl.when(step >= steps)
    def _():
        own_ref[...] = value


def branch_kernel(count, steps, mixed_ref, act_ref, *rest):
    blocks, (other_ref, own_ref, held, sems) = rest[:count], rest[count:]
    step = pl.program_id(0)

    @pl.when(step == 0)
    def _():
        loads = block_copies(blocks, columns_at(held, blocks[0].shape[1]), sems)
        for copy in loads:
            copy.start()
        for copy in loads:
            copy.wait()

    x = jnp.concatenate([mixed_ref[...], act_ref[...]], axis=1)
    put_by_sequence(step, steps, dot(x, held[...], 1, 0).astype(BF16), other_ref, own_ref)


def branch_sums(mixed, act, blocks, tile, deps):
    length, count = mixed.shape[0] // 2, len(blocks)
    inner, model, steps = blocks[0].shape[0], count * blocks[0].shape[1], length // tile
    return call(
        functools.partial(branch_kernel, count, steps),
        "branch_sums",
        [mixed, act, *blocks],
        deps,
        grid=(2 * steps,),
        in_specs=[other_first(tile, a.shape[1], steps) for a in (mixed, act)] + [HBM] * count,
        out_specs=by_sequence(tile, model, steps),
        out_shape=[jax.ShapeDtypeStruct((length, model), BF16)] * 2,
        scratch_shapes=[pltpu.VMEM((inner, model), BF16), pltpu.SemaphoreType.DMA((count,))],
    )


def grad_in_kernel(setup, dy_ref, slope_ref, *rest):
    count, width, hidden = setup
    blocks = rest[:count]
    gmixed_ref, gpre_ref, gsum_ref, dsum_ref, held, sems = rest[-6:]

    @pl.when(pl.program_id(0) == 0)
    def _():
        loads = block_copies(blocks, columns_at(held, blocks[0].shape[1]), sems)
        for copy in loads:
            copy.start()
        gsum_ref[...] = jnp.zeros_like(gsum_ref)
        dsum_ref[...] = jnp.zeros_like(dsum_ref)
        for copy in loads:
            copy.wait()

    dy = dy_ref[...]
    gmixed_ref[...] = dot(dy, held[:width, :], 1, 1).astype(BF16)
    for start in range(0, hidden, width):
        part = slice(start, start + width)
        gact = dot(dy, held[width + start : 2 * width + start, :], 1, 1)
        gpre = (gact * slope_ref[:, part].astype(F32)).astype(BF16)
        gpre_ref[:, part] = gpre
        gsum_ref[0:1, part] += jnp.sum(gpre.astype(F32), axis=0, keepdims=True)
    dsum_ref[0:1, :] += jnp.sum(dy.astype(F32), axis=0, keepdims=True)


def grad_in(sequence, dy, slope, blocks, width, tile, earlier, deps):
    (length, model), hidden, count = dy.shape, slope.shape[1], len(blocks)
    steps = length // tile
    at = lambda w: pl.BlockSpec((tile, w), lambda i: (sequence * steps + i, 0))
    total = lambda w: pl.BlockSpec((8, w), lambda i: (0, 0))
    operands = [dy, slope, *blocks]
    return call(
        functools.partial(grad_in_kernel, (count, width, hidden)),
        "grad_in",
        operands + list(earlier),
        deps,
        grid=(steps,),
        in_specs=[pl.BlockSpec((tile, model), lambda i: (i, 0)), at(hidden)]
        + [HBM] * (count + len(earlier)),
        out_specs=[
            at(width),
            pl.BlockSpec((tile, hidden), lambda i: (i, 0)),
            total(hidden),
            total(model),
        ],
        out_shape=[
            jax.ShapeDtypeStruct((2 * length, width), BF16),
            jax.ShapeDtypeStruct((length, hidden), BF16),
            jax.ShapeDtypeStruct((8, hidden), F32),
            jax.ShapeDtypeStruct((8, model), F32),
        ],
        input_output_aliases={len(operands) + n: n for n in range(len(earlier))},
        scratch_shapes=[
            pltpu.VMEM((width + hidden, model), BF16),
            pltpu.SemaphoreType.DMA((count,)),
        ],
    )


def add_kernel(a_ref, b_ref, out_ref):
    out_ref[...] = (a_ref[...].astype(F32) + b_ref[...].astype(F32)).astype(BF16)


def add_rows(a, b):
    rows = pl.BlockSpec((a.shape[0] // 8, a.shape[1]), lambda i: (i, 0))
    return call(
        add_kernel,
        "add_rows",
        [a, b],
        grid=(8,),
        in_specs=[rows, rows],
        out_specs=rows,
        out_shape=jax.ShapeDtypeStruct(a.shape, BF16),
    )


def grad_normed_kernel(count, half, x_ref, *rest):
    grads, blocks, (out_ref, sum_ref, held, sems) = rest[:8], rest[8 : 8 + 2 * count], rest[-4:]
    (size, total), few, me = blocks[0].shape, count // 2, lax.axis_index("dp")

    @pl.when(pl.program_id(0) == 0)
    def _():
        for start in (True, False):
            for n, block in enumerate(blocks):
                core, j = n // count, n % count
                owner = lax.bitwise_xor(me, j ^ core) - half * few
                columns = slice(core * total, (core + 1) * total)

                @pl.when((owner >= 0) & (owner < few))
                def _(start=start, n=n, block=block, owner=owner, columns=columns):
                    target = held.at[span(owner, size), columns]
                    copy = pltpu.make_async_copy(block, target, sems.at[n])
                    if start:
                        copy.start()
                    else:
                        copy.wait()

        sum_ref[...] = jnp.zeros_like(sum_ref)

    columns = slice(half * few * size, (half + 1) * few * size)
    normal = normalized(x_ref[...])[:, columns]
    g = jnp.concatenate([ref[...] for ref in grads], axis=1)
    result = dot(g, held[...], 1, 1)
    sum_ref[0:1, :] += jnp.sum(result * normal, axis=0, keepdims=True)
    sum_ref[1:2, :] += jnp.sum(result, axis=0, keepdims=True)
    out_ref[...] = result.astype(BF16)


def grad_normed_sums(half, grads, x, blocks, tile, deps, adds=()):
    (length, model), count, total = x.shape, len(blocks) // 2, blocks[0].shape[1]
    part = model // 2
    rows = lambda w: pl.BlockSpec((tile, w), lambda i: (i, 0))
    return call(
        functools.partial(grad_normed_kernel, count, half),
        "grad_normed_sums",
        [x, *grads, *blocks],
        deps,
        adds=adds,
        grid=(length // tile,),
        in_specs=[rows(model)] + [rows(g.shape[1]) for g in grads] + [HBM] * (2 * count),
        out_specs=[rows(part), pl.BlockSpec((8, part), lambda i: (0, 0))],
        out_shape=[
            jax.ShapeDtypeStruct((length, part), BF16),
            jax.ShapeDtypeStruct((8, part), F32),
        ],
        scratch_shapes=[
            pltpu.VMEM((part, 2 * total), BF16),
            pltpu.SemaphoreType.DMA((2 * count,)),
        ],
    )


def weight_grad_kernel(writes, left, rows, many, groups, at_ref, *refs):
    cuts, (*refs, held, grad, sems) = refs[:many], refs[many:]
    whole, outs = refs[: len(refs) - len(writes)], refs[len(refs) - len(writes) :]
    step, core, loads, first = pl.program_id(0), lax.rem(lax.axis_index("dp"), 2), [], 0
    for group in groups:
        below = 0
        for ref in whole[:group]:
            columns = pl.ds(first, ref.shape[1])
            for start in range(0, ref.shape[0], rows):
                target = held.at[pl.ds(below + start, rows), columns]
                loads.append((ref.at[pl.ds(start, rows)], target))
            below += ref.shape[0]
        first += whole[0].shape[1]
        whole = whole[group:]
    loads = [pltpu.make_async_copy(*pair, sems.at[n]) for n, pair in enumerate(loads)]

    @pl.when(step == 0)
    def _():
        for copy in loads:
            copy.start()
        for copy in loads:
            copy.wait()

    cut = jnp.concatenate([ref[...] for ref in cuts], axis=0)
    pair = (cut, held[...]) if left else (held[...], cut)
    grad[...] = dot(*pair, 0, 0).astype(BF16)
    size = cut.shape[1] // 2
    for half, steps, out_ref in writes_of(writes, outs):
        here = functools.reduce(jnp.logical_or, [step == s for s in steps])

        @pl.when(here)
        def _(half=half, out_ref=out_ref):
            mine = span(core if half == 0 else 1 - core, size)
            out_ref[0] = grad[mine, :] if left else grad[:, mine]


def writes_of(writes, outs):
    return [(half, steps, out) for (half, steps), out in zip(writes, outs)]


def weight_grads(me, xs, gs, count, deps, left):
    plan, chips = scatter_plan(count), count // 2
    order = [j // 2 for s in plan[0] for j in s]
    sets = [(half, s) for s in range(len(plan[0])) for half in range(2)]
    writes = [(half, [order.index(j // 2) for j in plan[half][s]]) for half, s in sets]
    table = []
    for _, steps in writes:
        for i in range(chips):
            later = [w for w in steps if w >= i]
            table.append(steps.index(min(later) if later else max(steps)))
    owners = lax.bitwise_xor(me // 2, jnp.array(order, jnp.int32))
    at = jnp.concatenate([owners, jnp.array(table, jnp.int32)])
    cut, whole = (xs, gs) if left else (gs, xs)
    groups, length = [len(g) for g in whole], sum(a.shape[0] for a in whole[0])
    size, full = cut[0].shape[1] // count, sum(g[0].shape[1] for g in whole)
    shape, whole = (size, full) if left else (full, size), [a for g in whole for a in g]
    rows = length // 4
    pieces = 4 * len(groups)

    def out(n):
        return pl.BlockSpec((1, *shape), lambda i, at: (at[chips * (n + 1) + i], 0, 0))

    outs = call(
        functools.partial(weight_grad_kernel, writes, left, rows, len(cut), groups),
        "weight_grads",
        [*cut, *whole],
        deps,
        (at,),
        grid=(chips,),
        in_specs=[pl.BlockSpec((a.shape[0], 2 * size), lambda i, at: (0, at[i])) for a in cut]
        + [HBM] * len(whole),
        out_specs=[out(n) for n in range(len(sets))],
        out_shape=[
            jax.ShapeDtypeStruct((len(plan[half][s]), *shape), BF16) for half, s in sets
        ],
        scratch_shapes=[
            pltpu.VMEM((length, full), BF16),
            pltpu.VMEM((2 * size, full) if left else (full, 2 * size), BF16),
            pltpu.SemaphoreType.DMA((pieces,)),
        ],
    )
    return [[o for o, (half, _) in zip(outs, sets) if half == h] for h in range(2)]


def norm_back_kernel(tokens_ref, dy_ref, gain_ref, left_ref, right_ref, out_ref):
    x = tokens_ref[...].astype(F32)
    centered = x - jnp.mean(x, axis=1, keepdims=True)
    inverse_std = lax.rsqrt(jnp.mean(centered * centered, axis=1, keepdims=True) + EPS)
    normal = centered * inverse_std
    grad = jnp.concatenate([left_ref[...], right_ref[...]], axis=1).astype(F32)
    scaled = grad * gain_ref[...]
    first_mean = jnp.mean(scaled, axis=1, keepdims=True)
    second_mean = jnp.mean(scaled * normal, axis=1, keepdims=True)
    back = (scaled - first_mean - normal * second_mean) * inverse_std
    out_ref[...] = (dy_ref[...].astype(F32) + back).astype(BF16)


def norm_back(tokens, dy, gain, halves, deps):
    rows, model = tokens.shape
    tile = min(64, rows)
    part = lambda w: pl.BlockSpec((tile, w), lambda i: (i, 0))
    return call(
        norm_back_kernel,
        "norm_back",
        [tokens, dy, gain, *halves],
        deps,
        grid=(rows // tile,),
        in_specs=[part(model), part(model), pl.BlockSpec((1, model), lambda i: (0, 0))]
        + [part(model // 2)] * 2,
        out_specs=part(model),
        out_shape=jax.ShapeDtypeStruct((rows, model), BF16),
    )


def across(value, bit, count):
    return lax.ppermute(value, "dp", [(i, i ^ bit) for i in range(count)])


def added(addends):
    return sum(a.astype(F32) for a in addends).astype(BF16)


def chip_bits(count):
    bits, bit = [], 2
    while bit < count:
        bits.append(bit)
        bit *= 2
    return bits


class BlockGather:
    def __init__(self, own, sibling, count):
        self.held, self.count = {0: own, 1: sibling}, count
        self.orders = (chip_bits(count), chip_bits(count)[::-1])

    def own_to(self, s):
        if s < len(self.orders[0]):
            for half in range(2):
                bit = self.orders[half][s]
                self.held[half ^ bit] = across(self.held[half], bit, self.count)

    def rest(self):
        for s in range(1, len(self.orders[0])):
            for half in range(2):
                order = self.orders[half]
                for j in [j for j in self.held if j % 2 == half]:
                    if j ^ order[s] not in self.held and not any(j & b for b in order[s:]):
                        self.held[j ^ order[s]] = across(self.held[j], order[s], self.count)

    def fenced(self, others=(), deps=()):
        keys = sorted(self.held)
        values = fence([self.held[j] for j in keys] + list(others), deps)
        self.held = dict(zip(keys, values))
        return values[len(keys) :]

    def blocks(self):
        return [self.held[j] for j in range(self.count)]


def scatter_orders(count):
    return (chip_bits(count)[::-1], chip_bits(count))


def scatter_plan(count):
    plan = []
    for half, order in enumerate(scatter_orders(count)):
        sets, rest = [[half]], [half]
        for bit in reversed(order):
            sets.insert(0, [j ^ bit for j in rest])
            rest = sets[0] + rest
        plan.append(sets)
    return plan


class BlockScatter:
    def __init__(self, halves, count):
        self.count, self.orders, self.plan = count, scatter_orders(count), scatter_plan(count)
        self.held = [[[(a, 0)] for a in arrays] for arrays in halves]
        self.steps = len(self.orders[0])

    def parts(self, half, s):
        many = len(self.plan[half][s])
        return [a[first : first + many] for a, first in self.held[half][s]]

    def total(self, half, s):
        if len(self.held[half][s]) > 1:
            self.held[half][s] = [(added(self.parts(half, s)), 0)]
        return self.parts(half, s)[0]

    def ready(self, s):
        return [self.total(half, s) for half in range(2)]

    def adds(self, s):
        return [(len(self.plan[half][s]), self.held[half][s]) for half in range(2)]

    def settle(self, s, sums):
        for half in range(2):
            self.held[half][s] = [(sums[half], 0)]

    def send(self, s):
        return [across(self.total(h, s), self.orders[h][s], self.count) for h in range(2)]

    def arrive(self, s, came):
        for half in range(2):
            first = 0
            for t in range(s + 1, len(self.plan[half])):
                self.held[half][t].append((came[half], first))
                first += len(self.plan[half][t])

    def between(self):
        for s in range(1, self.steps - 1):
            self.arrive(s, self.send(s))

    def last(self):
        return self.total(1, -1)[0]

    def finish(self, theirs):
        return sum(a[0].astype(F32) for a in self.parts(0, -1)), theirs.astype(F32)


def on_device(
    tokens,
    norm_gain,
    norm_bias,
    qkv_weight,
    qkv_bias,
    dense_weight,
    dense_bias,
    up_weight,
    up_bias,
    down_weight,
    down_bias,
    cotangent,
    *,
    ndp,
    nmp,
):
    me = lax.axis_index("dp")
    core = me % 2
    length, model = tokens.shape[0] * nmp, tokens.shape[1]
    tile, block = min(256, length), min(512, length)
    width, hidden = qkv_weight.shape[2] // 2, up_weight.shape[1] // 2
    chip_steps = len(chip_bits(ndp))
    rank = lambda array, axis, which, size: lax.dynamic_slice_in_dim(
        array, which * size, size, axis
    )

    def row_pack(which):
        qkv = rank(qkv_weight, 2, which, width)
        return jnp.concatenate([qkv[0], qkv[1], qkv[2], rank(up_weight, 1, which, hidden)], axis=1)

    def column_pack(which):
        return jnp.concatenate(
            [rank(dense_weight, 0, which, width), rank(down_weight, 0, which, hidden)], axis=0
        )

    pairs = width // LANES
    swap = lambda array: across(array, 1, ndp)
    line_gather = lambda array: lax.all_gather(array, "mp", axis=0, tiled=True)
    line_scatter = lambda array: lax.psum_scatter(array, "mp", scatter_dimension=0, tiled=True)
    x_own, dy_own = line_gather(tokens), line_gather(cotangent)
    rows = BlockGather(row_pack(core), swap(row_pack(1 - core)), ndp)
    columns = BlockGather(column_pack(core), swap(column_pack(1 - core)), ndp)
    rows.own_to(0)
    rows.fenced(deps=columns.held.values())
    rows.own_to(1)
    rows.fenced()
    rows.rest()
    x_own, *held = fence([x_own, columns.held[0], columns.held[1]], rows.blocks())
    columns.held = dict(enumerate(held))

    tables = rotary_tables(length)
    bias = jnp.concatenate(
        [
            rank(qkv_bias, 1, core, width).astype(F32).reshape(1, 3 * width),
            rank(up_bias[None, :], 1, core, hidden).astype(F32),
        ],
        axis=1,
    )
    gain, shift = norm_gain.astype(F32)[None, :], norm_bias.astype(F32)[None, :]
    x_other = swap(x_own)
    columns.own_to(0)
    common = (rows.blocks(), bias, gain, shift, tables, width, tile)
    first = project(0, x_own, *common, (), [columns.held[0]])
    (x_other,) = columns.fenced([x_other], [first[0]])
    columns.own_to(1)
    qkv, act, slope, normed = project(1, x_other, *common, first, [columns.held[0]])
    held = columns.fenced(rows.blocks(), [qkv])
    columns.rest()
    row_blocks, row_others = held, [swap(a) for a in held[:3]]
    mixed, lse = attend(qkv, length, block, [columns.held[0]])
    row_others = columns.fenced(row_others, [mixed])
    row_blocks[3:] = fence(row_blocks[3:], [row_others[0]])
    row_others += [swap(a) for a in row_blocks[3:]]
    other_sums, own_sums = branch_sums(mixed, act, columns.blocks(), tile, [row_blocks[3]])
    other_sums, dy_own, *row_others[3:] = fence([other_sums, dy_own, *row_others[3:]], [own_sums])
    theirs = swap(other_sums)
    dy_other = swap(dy_own)

    grads = (slope, columns.blocks(), width, tile)
    gmixed, gpre_own, *grad_a = grad_in(0, dy_own, *grads, (), [own_sums])
    theirs, dy_other = fence([theirs, dy_other], [grad_a[0]])
    total = add_rows(own_sums, theirs)
    branches = line_scatter(total)
    gmixed, gpre_other, *grad_b = grad_in(1, dy_other, *grads, [gmixed], [total])
    (gpre_sent,) = fence([gpre_other])
    gpre_came = swap(gpre_sent)
    column_grads = BlockScatter(
        weight_grads(me, [[mixed], [act]], [dy_own, dy_other], ndp, [gpre_sent], left=False), ndp
    )
    (gpre_came,) = fence([gpre_came], [column_grads.held[0][0][0][0]])
    column_came = column_grads.send(0)
    back = lambda sequence, deps: attend_back(
        sequence, qkv, gmixed, mixed, lse, tables, length, block, deps
    )
    *other, qkv_sums_b = back(1, [gpre_came])
    came = [swap(a) for a in other]
    *own, qkv_sums_a = back(0, [other[0]])
    came = fence([*came, *column_came], [own[0]])
    column_came, came = came[3:], came[:3]
    column_grads.arrive(0, column_came)
    column_grads.between()
    all_grads = [*own, gpre_own, *came, gpre_came]

    def normed_half(half, deps, adds=()):
        return grad_normed_sums(
            half, all_grads, x_own, [*row_blocks, *row_others], tile, deps, adds
        )

    total_a, sums_a, *settled = normed_half(0, [], column_grads.adds(chip_steps - 1))
    column_grads.settle(chip_steps - 1, settled)
    half_a = line_scatter(total_a)
    column_came = column_grads.send(chip_steps - 1)
    up_grads = BlockScatter(
        weight_grads(me, [normed], [[gpre_own, gpre_sent]], ndp, [sums_a], left=True), ndp
    )
    c0, c1, branches, u0, u1 = fence(
        [*column_came, branches, *(up_grads.held[h][0][0][0] for h in range(2))]
    )
    up_grads.held[0][0], up_grads.held[1][0] = [(u0, 0)], [(u1, 0)]
    up_came = up_grads.send(0)
    column_grads.arrive(chip_steps - 1, [c0, c1])
    total_b, sums_b, column_last = normed_half(
        1, [u0], [column_grads.adds(len(column_grads.plan[1]) - 1)[1]]
    )
    half_b = line_scatter(total_b)
    column_theirs = swap(column_last[0])
    qkv_sum = (
        (qkv_sums_a + qkv_sums_b)[:, :3, :].transpose(1, 0, 2).reshape(3 * width)
    )
    norm_sums = jnp.concatenate([sums_a[:2], sums_b[:2]], axis=1)
    small = jnp.concatenate(
        [
            norm_sums.reshape(2 * model),
            qkv_sum,
            grad_a[0][0] + grad_b[0][0],
            grad_a[1][0] + grad_b[1][0],
        ]
    )
    bits = chip_bits(ndp)
    for bit in bits[:-2]:
        small = small + across(small, bit, ndp)
    small_came = across(small, bits[-2], ndp)
    qkv_grads = BlockScatter(
        weight_grads(
            me, [normed], [[a, b] for a, b in zip(own, other)], ndp, [small], left=True
        ),
        ndp,
    )
    u0, u1 = fence(up_came, [qkv_grads.held[0][0][0][0]])
    half_a, q0, q1, small_came, column_theirs = fence(
        [
            half_a,
            *(qkv_grads.held[h][0][0][0] for h in range(2)),
            small_came,
            column_theirs,
        ],
        [u0],
    )
    up_grads.arrive(0, [u0, u1])
    up_grads.between()
    qkv_grads.held[0][0], qkv_grads.held[1][0] = [(q0, 0)], [(q1, 0)]
    qkv_came = qkv_grads.send(0)
    up_came = up_grads.send(chip_steps - 1)
    small = small + small_came
    small_came = across(small, bits[-1], ndp)
    u0, u1, q0, q1, small_came, column_theirs, branches, half_b = fence(
        [*up_came, *qkv_came, small_came, column_theirs, branches, half_b]
    )
    up_grads.arrive(chip_steps - 1, [u0, u1])
    up_theirs = swap(up_grads.last())
    qkv_grads.arrive(0, [q0, q1])
    qkv_grads.between()
    small = small + small_came
    q0, q1, small = fence([*qkv_grads.send(chip_steps - 1), small])
    qkv_grads.arrive(chip_steps - 1, [q0, q1])
    small_other = swap(small)
    qkv_theirs = swap(qkv_grads.last())
    norm_sums = small[: 2 * model] + small_other[: 2 * model]
    norm_sums = [norm_sums] + [
        lax.ppermute(norm_sums, "mp", [(i, i ^ j) for i in range(nmp)]) for j in range(1, nmp)
    ]
    while len(norm_sums) > 1:
        norm_sums = [a + b for a, b in zip(norm_sums[::2], norm_sums[1::2])]
    norm_sums = norm_sums[0]

    output = (
        tokens.astype(F32)
        + branches.astype(F32)
        + (dense_bias.astype(F32) + down_bias.astype(F32))[None, :]
    ).astype(BF16)

    def both(mine, theirs, axis):
        return jnp.where(
            core == 0,
            jnp.concatenate([mine, theirs], axis=axis),
            jnp.concatenate([theirs, mine], axis=axis),
        )

    mine, theirs = column_grads.finish(column_theirs)
    owned_dense = both(mine[:width], theirs[:width], 0)
    owned_down = both(mine[width:], theirs[width:], 0)
    owned_up = both(*up_grads.finish(up_theirs), 1)
    mine, theirs = qkv_grads.finish(qkv_theirs)
    owned_qkv = jnp.stack(
        [
            both(mine[:, c * width : (c + 1) * width], theirs[:, c * width : (c + 1) * width], 1)
            for c in range(3)
        ]
    )

    inner = 3 * width + hidden
    grad_out_bias = small[2 * model + inner :]
    here, there = (a[2 * model : 2 * model + inner] for a in (small, small_other))
    even, odd = jnp.where(core == 0, here, there), jnp.where(core == 0, there, here)
    grad_qkv_bias = jnp.concatenate(
        [a[: 3 * width].reshape(3, width) for a in (even, odd)], axis=1
    )
    grad_up_bias = jnp.concatenate([even[3 * width :], odd[3 * width :]])

    grad_tokens = norm_back(tokens, cotangent, gain, [half_a, half_b], [])
    return (
        output,
        grad_tokens,
        norm_sums[:model],
        norm_sums[model:],
        owned_qkv,
        grad_qkv_bias,
        owned_dense,
        grad_out_bias,
        owned_up,
        grad_up_bias,
        owned_down,
        grad_out_bias,
    )


def solution(mesh):
    return jax.shard_map(
        functools.partial(on_device, ndp=mesh.shape["dp"], nmp=mesh.shape["mp"]),
        mesh=mesh,
        in_specs=(
            P(("dp", "mp"), None),
            P(),
            P(),
            P(None, "dp", "mp"),
            P(None, "mp"),
            P("mp", "dp"),
            P(),
            P("dp", "mp"),
            P("mp"),
            P("mp", "dp"),
            P(),
            P(("dp", "mp"), None),
        ),
        out_specs=(
            P(("dp", "mp"), None),
            P(("dp", "mp"), None),
            P(),
            P(),
            P(None, "dp", "mp"),
            P(None, "mp"),
            P("mp", "dp"),
            P(),
            P("dp", "mp"),
            P("mp"),
            P("mp", "dp"),
            P(),
        ),
        check_vma=False,
    )
```

```python
import functools

import jax
import jax.numpy as jnp
import numpy as np
from jax import lax
from jax.experimental import pallas as pl
from jax.experimental.pallas import tpu as pltpu
from jax.sharding import PartitionSpec as P

HEAD_DIM = 64
ROT = 32
EPS = 1e-05
LANES = 128
F32 = jnp.float32
BF16 = jnp.bfloat16
HBM = pl.BlockSpec(memory_space=pltpu.HBM)


def dot(lhs, rhs, lhs_dim, rhs_dim):
    return lax.dot_general(
        lhs, rhs, (((lhs_dim,), (rhs_dim,)), ((), ())), preferred_element_type=F32
    )


def call(kernel, name, operands, deps=(), scalars=(), adds=(), vmem=63, **spec):
    deps, out_shape = tuple(deps), spec.pop("out_shape")
    single = not isinstance(out_shape, list)
    out_shape = [out_shape] if single else out_shape
    out_specs = spec.pop("out_specs")
    out_specs = [out_specs] if single else list(out_specs)
    extra, extra_specs, sizes = [], [], []
    steps = spec["grid"][0] if adds else 1
    for many, addends in adds:
        _, rows, columns = addends[0][0].shape
        block = (many, rows // steps, columns)
        for array, first in addends:
            extra.append(array)
            extra_specs.append(
                pl.BlockSpec(block, lambda i, *at, first=first, many=many: (first // many, i, 0))
            )
        out_shape = out_shape + [jax.ShapeDtypeStruct((many, rows, columns), BF16)]
        out_specs = out_specs + [pl.BlockSpec(block, lambda i, *at: (0, i, 0))]
        sizes.append(len(addends))
    lead, outs = len(scalars) + len(operands), len(out_shape) - len(adds)

    def body(*refs):
        first = lead + len(extra) + len(deps)
        kernel(*refs[:lead], *refs[first : first + outs], *refs[first + outs + len(adds) :])
        sources = refs[lead : lead + len(extra)]
        for n, out in zip(sizes, refs[first + outs : first + outs + len(adds)]):
            out[...] = sum(ref[...].astype(F32) for ref in sources[:n]).astype(BF16)
            sources = sources[n:]

    in_specs = list(spec.pop("in_specs")) + extra_specs + [HBM] * len(deps)
    aliases = spec.pop("input_output_aliases", {})
    if scalars:
        grid_spec = pltpu.PrefetchScalarGridSpec(
            num_scalar_prefetch=len(scalars), in_specs=in_specs, out_specs=out_specs, **spec
        )
        spec = {"grid_spec": grid_spec}
    else:
        spec.update(in_specs=in_specs, out_specs=out_specs)
    results = pl.pallas_call(
        body,
        out_shape=out_shape,
        input_output_aliases=aliases,
        compiler_params=pltpu.CompilerParams(vmem_limit_bytes=vmem << 20),
        cost_estimate=pl.CostEstimate(flops=0, transcendentals=0, bytes_accessed=0),
        name=name,
        **spec,
    )(*scalars, *operands, *extra, *deps)
    return results[0] if single and not adds else results


def fence(values, deps=()):
    return list(
        call(
            lambda *refs: None,
            "fence",
            values,
            deps,
            in_specs=[HBM] * len(values),
            out_specs=[HBM] * len(values),
            out_shape=[jax.ShapeDtypeStruct(v.shape, v.dtype) for v in values],
            input_output_aliases={n: n for n in range(len(values))},
        )
    )


def rotary_tables(length):
    positions = np.arange(length, dtype=np.float32)
    frequency = 10000.0 ** (-np.arange(ROT // 2, dtype=np.float64) * 2.0 / ROT)
    angles = positions[:, None] * frequency.astype(np.float32)[None, :]
    cosine, sine = np.cos(angles.astype(np.float64)), np.sin(angles.astype(np.float64))
    rest = HEAD_DIM - ROT
    none = np.zeros((length, ROT // 2))
    ones, zeros = np.ones((length, rest)), np.zeros((length, rest))
    straight = np.concatenate([cosine, cosine, ones], axis=1)
    left = np.concatenate([-sine, none, zeros], axis=1)
    right = np.concatenate([none, sine, zeros], axis=1)
    return [
        jnp.asarray(np.concatenate([t, t], axis=1).astype(np.float32))
        for t in (straight, left, right)
    ]


def rotated(u, straight, left, right, sign):
    half = ROT // 2
    turned = pltpu.roll(u, LANES - half, 1) * left + pltpu.roll(u, half, 1) * right
    return u * straight + sign * turned


def normalized(x):
    x = x.astype(F32)
    centered = x - jnp.mean(x, axis=1, keepdims=True)
    variance = jnp.mean(centered * centered, axis=1, keepdims=True)
    return centered * lax.rsqrt(variance + EPS)


def block_copies(blocks, place, sems):
    me = lax.axis_index("dp")
    return [
        pltpu.make_async_copy(block, place(lax.bitwise_xor(me, j)), sems.at[j])
        for j, block in enumerate(blocks)
    ]


def span(owner, size):
    return pl.ds(pl.multiple_of(owner * size, size), size)


def rows_at(ref, size):
    return lambda owner: ref.at[pl.ds(pl.multiple_of(owner * size, size), size)]


def columns_at(ref, size):
    return lambda owner: ref.at[:, pl.ds(pl.multiple_of(owner * size, size), size)]


def project_kernel(setup, x_ref, bias_ref, gain_ref, shift_ref, cos_ref, left_ref, right_ref, *rest):
    count, width, hidden = setup
    blocks = rest[:count]
    qkv_ref, act_ref, slope_ref, normed_ref, held, sems = rest[-6:]

    @pl.when(pl.program_id(0) == 0)
    def _():
        loads = block_copies(blocks, rows_at(held, blocks[0].shape[0]), sems)
        for copy in loads:
            copy.start()
        for copy in loads:
            copy.wait()

    x = (normalized(x_ref[...]) * gain_ref[...] + shift_ref[...]).astype(BF16)
    normed_ref[...] = x
    root = 0.7978845608028654
    for t in range((3 * width + hidden) // width):
        columns = slice(t * width, (t + 1) * width)
        y = dot(x, held[:, columns], 1, 0) + bias_ref[:, columns]
        if t < 3:
            for g in range(width // LANES):
                part = y[:, g * LANES : (g + 1) * LANES]
                if t < 2:
                    part = rotated(part, cos_ref[...], left_ref[...], right_ref[...], 1.0)
                if t == 0:
                    part = part * HEAD_DIM**-0.5
                start = t * width + g * LANES
                qkv_ref[:, start : start + LANES] = part.astype(BF16)
        else:
            columns = slice((t - 3) * width, (t - 2) * width)
            square = y * y
            turn = jnp.tanh(root * y * (1.0 + 0.044715 * square))
            half = 0.5 * (1.0 + turn)
            act_ref[:, columns] = (y * half).astype(BF16)
            slope = half * (1.0 + y * (1.0 - turn) * (root + (3.0 * 0.044715 * root) * square))
            slope_ref[:, columns] = slope.astype(BF16)


def project(sequence, x, blocks, bias, gain, shift, tables, width, tile, earlier, deps):
    (length, model), total, count = x.shape, blocks[0].shape[1], len(blocks)
    hidden, steps = total - 3 * width, length // tile
    rows = lambda w: pl.BlockSpec((tile, w), lambda i: (i, 0))
    out = lambda w: pl.BlockSpec((tile, w), lambda i: (sequence * steps + i, 0))
    line = lambda a: pl.BlockSpec(a.shape, lambda i: (0, 0))
    widths = (3 * width, hidden, hidden, model)
    operands = [x, bias, gain, shift, *tables, *blocks]
    return call(
        functools.partial(project_kernel, (count, width, hidden)),
        "project",
        operands + list(earlier),
        deps,
        grid=(steps,),
        in_specs=[rows(model), line(bias), line(gain), line(shift)]
        + [rows(LANES)] * 3
        + [HBM] * (count + len(earlier)),
        out_specs=[out(w) for w in widths],
        out_shape=[jax.ShapeDtypeStruct((2 * length, w), BF16) for w in widths],
        input_output_aliases={len(operands) + n: n for n in range(len(earlier))},
        scratch_shapes=[pltpu.VMEM((model, total), BF16), pltpu.SemaphoreType.DMA((count,))],
    )


def attend_kernel(block, q_ref, k_ref, v_ref, out_ref, lse_ref):
    length = q_ref.shape[0]
    lane = lax.broadcasted_iota(jnp.int32, (1, LANES), 1)
    key = lax.broadcasted_iota(jnp.int32, (block, block), 0)
    causal = key <= lax.broadcasted_iota(jnp.int32, (block, block), 1)
    for i in range(length // block):
        rows, before = pl.ds(i * block, block), pl.ds(0, i * block)
        results = []
        for h in range(2):
            mine = (lane < HEAD_DIM) if h == 0 else (lane >= HEAD_DIM)
            query = jnp.where(mine, q_ref[rows, :], 0)
            near = jnp.where(causal, dot(k_ref[rows, :], query, 1, 1), -1e30)
            highest = jnp.max(near, axis=0, keepdims=True)
            if i:
                far = dot(k_ref[before, :], query, 1, 1)
                highest = jnp.maximum(highest, jnp.max(far, axis=0, keepdims=True))
            near = jnp.exp(near - highest)
            total = jnp.sum(near, axis=0, keepdims=True)
            if i:
                far = jnp.exp(far - highest)
                total = total + jnp.sum(far, axis=0, keepdims=True)
            inverse = 1.0 / total
            result = dot((near * inverse).astype(BF16), v_ref[rows, :], 0, 0)
            if i:
                result = result + dot((far * inverse).astype(BF16), v_ref[before, :], 0, 0)
            results.append(result)
            lse_ref[0, h : h + 1, rows] = highest + jnp.log(total)
        out_ref[rows, :] = jnp.where(lane < HEAD_DIM, results[0], results[1]).astype(BF16)


def pair_specs(length, pairs):
    return lambda off: pl.BlockSpec(
        (length, LANES), lambda g: (g // pairs, off * pairs + g % pairs)
    )


def attend(qkv, length, block, deps):
    width, sequences = qkv.shape[1] // 3, qkv.shape[0] // length
    pairs = width // LANES
    at = pair_specs(length, pairs)
    return call(
        functools.partial(attend_kernel, block),
        "attend",
        [qkv, qkv, qkv],
        deps,
        grid=(sequences * pairs,),
        in_specs=[at(0), at(1), at(2)],
        out_specs=[at(0), pl.BlockSpec((1, 8, length), lambda g: (g, 0, 0))],
        out_shape=[
            jax.ShapeDtypeStruct((qkv.shape[0], width), BF16),
            jax.ShapeDtypeStruct((sequences * pairs, 8, length), F32),
        ],
    )


def attend_back_kernel(
    block,
    q_ref,
    k_ref,
    v_ref,
    grad_ref,
    mixed_ref,
    lse_ref,
    cos_ref,
    left_ref,
    right_ref,
    gq_ref,
    gk_ref,
    gv_ref,
    sum_ref,
    gk_sum,
    gv_sum,
):
    length = q_ref.shape[0]
    lane = lax.broadcasted_iota(jnp.int32, (1, LANES), 1)
    key = lax.broadcasted_iota(jnp.int32, (block, block), 0)
    causal = key <= lax.broadcasted_iota(jnp.int32, (block, block), 1)
    count = length // block
    sum_ref[...] = jnp.zeros_like(sum_ref)

    def put(ref, which, rows, value):
        value = value.astype(BF16)
        ref[rows, :] = value
        sum_ref[0, which : which + 1, :] += jnp.sum(value.astype(F32), axis=0, keepdims=True)

    def unrotated(value, rows):
        return rotated(value, cos_ref[rows, :], left_ref[rows, :], right_ref[rows, :], -1.0)

    for i in reversed(range(count)):
        rows = pl.ds(i * block, block)
        product = grad_ref[rows, :].astype(F32) * mixed_ref[rows, :].astype(F32)
        gq = None
        for h in range(2):
            mine = (lane < HEAD_DIM) if h == 0 else (lane >= HEAD_DIM)
            query = jnp.where(mine, q_ref[rows, :], 0)
            grad = jnp.where(mine, grad_ref[rows, :], 0)
            ones = jnp.where(mine, jnp.ones((8, LANES), F32), 0.0)
            delta = lax.dot_general(
                ones,
                product,
                (((1,), (1,)), ((), ())),
                precision=lax.Precision.HIGHEST,
                preferred_element_type=F32,
            )[0:1, :]
            lse = lse_ref[0, h : h + 1, rows]
            for j in range(i + 1):
                keys = pl.ds(j * block, block)
                key_rows = k_ref[keys, :]
                probs = jnp.exp(dot(key_rows, query, 1, 1) - lse)
                if j == i:
                    probs = jnp.where(causal, probs, 0.0)
                gprobs = dot(v_ref[keys, :], grad, 1, 1)
                gscores = (probs * (gprobs - delta)).astype(BF16)
                gv, gk = dot(probs.astype(BF16), grad, 1, 0), dot(gscores, query, 1, 0)
                if i == count - 1 and h == 0:
                    gv_sum[keys, :] = gv
                    gk_sum[keys, :] = gk
                else:
                    gv_sum[keys, :] += gv
                    gk_sum[keys, :] += gk
                part = dot(gscores, jnp.where(mine, key_rows, 0), 0, 0)
                gq = part if gq is None else gq + part
        put(gq_ref, 0, rows, unrotated(gq * HEAD_DIM**-0.5, rows))
    for i in range(count):
        rows = pl.ds(i * block, block)
        put(gk_ref, 1, rows, unrotated(gk_sum[rows, :], rows))
        put(gv_ref, 2, rows, gv_sum[rows, :])


def attend_back(sequence, qkv, grad, mixed, lse, tables, length, block, deps):
    width = qkv.shape[1] // 3
    pairs = width // LANES
    at = lambda off: pl.BlockSpec((length, LANES), lambda g: (sequence, off * pairs + g))
    out = pl.BlockSpec((length, LANES), lambda g: (0, g))
    table = pl.BlockSpec((length, LANES), lambda g: (0, 0))
    small = pl.BlockSpec((1, 8, length), lambda g: (sequence * pairs + g, 0, 0))
    return call(
        functools.partial(attend_back_kernel, block),
        "attend_back",
        [qkv, qkv, qkv, grad, mixed, lse, *tables],
        deps,
        grid=(pairs,),
        in_specs=[at(0), at(1), at(2), at(0), at(0), small, table, table, table],
        out_specs=[out] * 3 + [pl.BlockSpec((1, 8, LANES), lambda g: (g, 0, 0))],
        out_shape=[jax.ShapeDtypeStruct((length, width), BF16)] * 3
        + [jax.ShapeDtypeStruct((pairs, 8, LANES), F32)],
        scratch_shapes=[pltpu.VMEM((length, LANES), F32)] * 2,
    )


def by_sequence(tile, width, steps):
    return [
        pl.BlockSpec((tile, width), lambda i: (jnp.minimum(i, steps - 1), 0)),
        pl.BlockSpec((tile, width), lambda i: (jnp.maximum(i - steps, 0), 0)),
    ]


def other_first(tile, width, steps):
    return pl.BlockSpec((tile, width), lambda i: ((i + steps) % (2 * steps), 0))


def put_by_sequence(step, steps, value, other_ref, own_ref):
    @pl.when(step < steps)
    def _():
        other_ref[...] = value

    @pl.when(step >= steps)
    def _():
        own_ref[...] = value


def branch_kernel(count, steps, mixed_ref, act_ref, *rest):
    blocks, (other_ref, own_ref, held, sems) = rest[:count], rest[count:]
    step = pl.program_id(0)

    @pl.when(step == 0)
    def _():
        loads = block_copies(blocks, columns_at(held, blocks[0].shape[1]), sems)
        for copy in loads:
            copy.start()
        for copy in loads:
            copy.wait()

    x = jnp.concatenate([mixed_ref[...], act_ref[...]], axis=1)
    put_by_sequence(step, steps, dot(x, held[...], 1, 0).astype(BF16), other_ref, own_ref)


def branch_sums(mixed, act, blocks, tile, deps):
    length, count = mixed.shape[0] // 2, len(blocks)
    inner, model, steps = blocks[0].shape[0], count * blocks[0].shape[1], length // tile
    return call(
        functools.partial(branch_kernel, count, steps),
        "branch_sums",
        [mixed, act, *blocks],
        deps,
        grid=(2 * steps,),
        in_specs=[other_first(tile, a.shape[1], steps) for a in (mixed, act)] + [HBM] * count,
        out_specs=by_sequence(tile, model, steps),
        out_shape=[jax.ShapeDtypeStruct((length, model), BF16)] * 2,
        scratch_shapes=[pltpu.VMEM((inner, model), BF16), pltpu.SemaphoreType.DMA((count,))],
    )


def grad_in_kernel(setup, dy_ref, slope_ref, *rest):
    count, width, hidden = setup
    blocks = rest[:count]
    gmixed_ref, gpre_ref, gsum_ref, dsum_ref, held, sems = rest[-6:]

    @pl.when(pl.program_id(0) == 0)
    def _():
        loads = block_copies(blocks, columns_at(held, blocks[0].shape[1]), sems)
        for copy in loads:
            copy.start()
        gsum_ref[...] = jnp.zeros_like(gsum_ref)
        dsum_ref[...] = jnp.zeros_like(dsum_ref)
        for copy in loads:
            copy.wait()

    dy = dy_ref[...]
    gmixed_ref[...] = dot(dy, held[:width, :], 1, 1).astype(BF16)
    for start in range(0, hidden, width):
        part = slice(start, start + width)
        gact = dot(dy, held[width + start : 2 * width + start, :], 1, 1)
        gpre = (gact * slope_ref[:, part].astype(F32)).astype(BF16)
        gpre_ref[:, part] = gpre
        gsum_ref[0:1, part] += jnp.sum(gpre.astype(F32), axis=0, keepdims=True)
    dsum_ref[0:1, :] += jnp.sum(dy.astype(F32), axis=0, keepdims=True)


def grad_in(sequence, dy, slope, blocks, width, tile, earlier, deps):
    (length, model), hidden, count = dy.shape, slope.shape[1], len(blocks)
    steps = length // tile
    at = lambda w: pl.BlockSpec((tile, w), lambda i: (sequence * steps + i, 0))
    total = lambda w: pl.BlockSpec((8, w), lambda i: (0, 0))
    operands = [dy, slope, *blocks]
    return call(
        functools.partial(grad_in_kernel, (count, width, hidden)),
        "grad_in",
        operands + list(earlier),
        deps,
        grid=(steps,),
        in_specs=[pl.BlockSpec((tile, model), lambda i: (i, 0)), at(hidden)]
        + [HBM] * (count + len(earlier)),
        out_specs=[
            at(width),
            pl.BlockSpec((tile, hidden), lambda i: (i, 0)),
            total(hidden),
            total(model),
        ],
        out_shape=[
            jax.ShapeDtypeStruct((2 * length, width), BF16),
            jax.ShapeDtypeStruct((length, hidden), BF16),
            jax.ShapeDtypeStruct((8, hidden), F32),
            jax.ShapeDtypeStruct((8, model), F32),
        ],
        input_output_aliases={len(operands) + n: n for n in range(len(earlier))},
        scratch_shapes=[
            pltpu.VMEM((width + hidden, model), BF16),
            pltpu.SemaphoreType.DMA((count,)),
        ],
    )


def add_kernel(a_ref, b_ref, out_ref):
    out_ref[...] = (a_ref[...].astype(F32) + b_ref[...].astype(F32)).astype(BF16)


def add_rows(a, b):
    rows = pl.BlockSpec((a.shape[0] // 8, a.shape[1]), lambda i: (i, 0))
    return call(
        add_kernel,
        "add_rows",
        [a, b],
        grid=(8,),
        in_specs=[rows, rows],
        out_specs=rows,
        out_shape=jax.ShapeDtypeStruct(a.shape, BF16),
    )


def grad_normed_kernel(count, half, x_ref, *rest):
    grads, blocks, (out_ref, sum_ref, held, sems) = rest[:8], rest[8 : 8 + 2 * count], rest[-4:]
    (size, total), few, me = blocks[0].shape, count // 2, lax.axis_index("dp")

    @pl.when(pl.program_id(0) == 0)
    def _():
        for start in (True, False):
            for n, block in enumerate(blocks):
                core, j = n // count, n % count
                owner = lax.bitwise_xor(me, j ^ core) - half * few
                columns = slice(core * total, (core + 1) * total)

                @pl.when((owner >= 0) & (owner < few))
                def _(start=start, n=n, block=block, owner=owner, columns=columns):
                    target = held.at[span(owner, size), columns]
                    copy = pltpu.make_async_copy(block, target, sems.at[n])
                    if start:
                        copy.start()
                    else:
                        copy.wait()

        sum_ref[...] = jnp.zeros_like(sum_ref)

    columns = slice(half * few * size, (half + 1) * few * size)
    normal = normalized(x_ref[...])[:, columns]
    g = jnp.concatenate([ref[...] for ref in grads], axis=1)
    result = dot(g, held[...], 1, 1)
    sum_ref[0:1, :] += jnp.sum(result * normal, axis=0, keepdims=True)
    sum_ref[1:2, :] += jnp.sum(result, axis=0, keepdims=True)
    out_ref[...] = result.astype(BF16)


def grad_normed_sums(half, grads, x, blocks, tile, deps, adds=()):
    (length, model), count, total = x.shape, len(blocks) // 2, blocks[0].shape[1]
    part = model // 2
    rows = lambda w: pl.BlockSpec((tile, w), lambda i: (i, 0))
    return call(
        functools.partial(grad_normed_kernel, count, half),
        "grad_normed_sums",
        [x, *grads, *blocks],
        deps,
        adds=adds,
        grid=(length // tile,),
        in_specs=[rows(model)] + [rows(g.shape[1]) for g in grads] + [HBM] * (2 * count),
        out_specs=[rows(part), pl.BlockSpec((8, part), lambda i: (0, 0))],
        out_shape=[
            jax.ShapeDtypeStruct((length, part), BF16),
            jax.ShapeDtypeStruct((8, part), F32),
        ],
        scratch_shapes=[
            pltpu.VMEM((part, 2 * total), BF16),
            pltpu.SemaphoreType.DMA((2 * count,)),
        ],
    )


def weight_grad_kernel(writes, left, rows, many, groups, at_ref, *refs):
    cuts, (*refs, held, grad, sems) = refs[:many], refs[many:]
    whole, outs = refs[: len(refs) - len(writes)], refs[len(refs) - len(writes) :]
    step, core, loads, first = pl.program_id(0), lax.rem(lax.axis_index("dp"), 2), [], 0
    for group in groups:
        below = 0
        for ref in whole[:group]:
            columns = pl.ds(first, ref.shape[1])
            for start in range(0, ref.shape[0], rows):
                target = held.at[pl.ds(below + start, rows), columns]
                loads.append((ref.at[pl.ds(start, rows)], target))
            below += ref.shape[0]
        first += whole[0].shape[1]
        whole = whole[group:]
    loads = [pltpu.make_async_copy(*pair, sems.at[n]) for n, pair in enumerate(loads)]

    @pl.when(step == 0)
    def _():
        for copy in loads:
            copy.start()
        for copy in loads:
            copy.wait()

    cut = jnp.concatenate([ref[...] for ref in cuts], axis=0)
    pair = (cut, held[...]) if left else (held[...], cut)
    grad[...] = dot(*pair, 0, 0).astype(BF16)
    size = cut.shape[1] // 2
    for half, steps, out_ref in writes_of(writes, outs):
        here = functools.reduce(jnp.logical_or, [step == s for s in steps])

        @pl.when(here)
        def _(half=half, out_ref=out_ref):
            mine = span(core if half == 0 else 1 - core, size)
            out_ref[0] = grad[mine, :] if left else grad[:, mine]


def writes_of(writes, outs):
    return [(half, steps, out) for (half, steps), out in zip(writes, outs)]


def weight_grads(me, xs, gs, count, deps, left, adds=()):
    plan, chips = scatter_plan(count), count // 2
    order = [j // 2 for s in plan[0] for j in s]
    sets = [(half, s) for s in range(len(plan[0])) for half in range(2)]
    writes = [(half, [order.index(j // 2) for j in plan[half][s]]) for half, s in sets]
    table = []
    for _, steps in writes:
        for i in range(chips):
            later = [w for w in steps if w >= i]
            table.append(steps.index(min(later) if later else max(steps)))
    owners = lax.bitwise_xor(me // 2, jnp.array(order, jnp.int32))
    at = jnp.concatenate([owners, jnp.array(table, jnp.int32)])
    cut, whole = (xs, gs) if left else (gs, xs)
    groups, length = [len(g) for g in whole], sum(a.shape[0] for a in whole[0])
    size, full = cut[0].shape[1] // count, sum(g[0].shape[1] for g in whole)
    shape, whole = (size, full) if left else (full, size), [a for g in whole for a in g]
    rows = length // 4
    pieces = 4 * len(groups)

    def out(n):
        return pl.BlockSpec((1, *shape), lambda i, at: (at[chips * (n + 1) + i], 0, 0))

    outs = call(
        functools.partial(weight_grad_kernel, writes, left, rows, len(cut), groups),
        "weight_grads",
        [*cut, *whole],
        deps,
        (at,),
        adds,
        grid=(chips,),
        in_specs=[pl.BlockSpec((a.shape[0], 2 * size), lambda i, at: (0, at[i])) for a in cut]
        + [HBM] * len(whole),
        out_specs=[out(n) for n in range(len(sets))],
        out_shape=[
            jax.ShapeDtypeStruct((len(plan[half][s]), *shape), BF16) for half, s in sets
        ],
        scratch_shapes=[
            pltpu.VMEM((length, full), BF16),
            pltpu.VMEM((2 * size, full) if left else (full, 2 * size), BF16),
            pltpu.SemaphoreType.DMA((pieces,)),
        ],
    )
    blocks = [[o for o, (half, _) in zip(outs, sets) if half == h] for h in range(2)]
    return (blocks, *outs[len(sets) :]) if adds else blocks


def norm_back_kernel(tokens_ref, dy_ref, gain_ref, left_ref, right_ref, out_ref):
    x = tokens_ref[...].astype(F32)
    centered = x - jnp.mean(x, axis=1, keepdims=True)
    inverse_std = lax.rsqrt(jnp.mean(centered * centered, axis=1, keepdims=True) + EPS)
    normal = centered * inverse_std
    grad = jnp.concatenate([left_ref[...], right_ref[...]], axis=1).astype(F32)
    scaled = grad * gain_ref[...]
    first_mean = jnp.mean(scaled, axis=1, keepdims=True)
    second_mean = jnp.mean(scaled * normal, axis=1, keepdims=True)
    back = (scaled - first_mean - normal * second_mean) * inverse_std
    out_ref[...] = (dy_ref[...].astype(F32) + back).astype(BF16)


def norm_back(tokens, dy, gain, halves, deps):
    rows, model = tokens.shape
    tile = min(64, rows)
    part = lambda w: pl.BlockSpec((tile, w), lambda i: (i, 0))
    return call(
        norm_back_kernel,
        "norm_back",
        [tokens, dy, gain, *halves],
        deps,
        grid=(rows // tile,),
        in_specs=[part(model), part(model), pl.BlockSpec((1, model), lambda i: (0, 0))]
        + [part(model // 2)] * 2,
        out_specs=part(model),
        out_shape=jax.ShapeDtypeStruct((rows, model), BF16),
    )


def across(value, bit, count):
    return lax.ppermute(value, "dp", [(i, i ^ bit) for i in range(count)])


def added(addends):
    return sum(a.astype(F32) for a in addends).astype(BF16)


def chip_bits(count):
    bits, bit = [], 2
    while bit < count:
        bits.append(bit)
        bit *= 2
    return bits


class BlockGather:
    def __init__(self, own, sibling, count):
        self.held, self.count = {0: own, 1: sibling}, count
        self.orders = (chip_bits(count), chip_bits(count)[::-1])

    def own_to(self, s):
        if s < len(self.orders[0]):
            for half in range(2):
                bit = self.orders[half][s]
                self.held[half ^ bit] = across(self.held[half], bit, self.count)

    def rest(self):
        for s in range(1, len(self.orders[0])):
            for half in range(2):
                order = self.orders[half]
                for j in [j for j in self.held if j % 2 == half]:
                    if j ^ order[s] not in self.held and not any(j & b for b in order[s:]):
                        self.held[j ^ order[s]] = across(self.held[j], order[s], self.count)

    def fenced(self, others=(), deps=()):
        keys = sorted(self.held)
        values = fence([self.held[j] for j in keys] + list(others), deps)
        self.held = dict(zip(keys, values))
        return values[len(keys) :]

    def blocks(self):
        return [self.held[j] for j in range(self.count)]


def scatter_orders(count):
    return (chip_bits(count)[::-1], chip_bits(count))


def scatter_plan(count):
    plan = []
    for half, order in enumerate(scatter_orders(count)):
        sets, rest = [[half]], [half]
        for bit in reversed(order):
            sets.insert(0, [j ^ bit for j in rest])
            rest = sets[0] + rest
        plan.append(sets)
    return plan


class BlockScatter:
    def __init__(self, halves, count):
        self.count, self.orders, self.plan = count, scatter_orders(count), scatter_plan(count)
        self.held = [[[(a, 0)] for a in arrays] for arrays in halves]
        self.steps = len(self.orders[0])

    def parts(self, half, s):
        many = len(self.plan[half][s])
        return [a[first : first + many] for a, first in self.held[half][s]]

    def total(self, half, s):
        if len(self.held[half][s]) > 1:
            self.held[half][s] = [(added(self.parts(half, s)), 0)]
        return self.parts(half, s)[0]

    def ready(self, s):
        return [self.total(half, s) for half in range(2)]

    def adds(self, s):
        return [(len(self.plan[half][s]), self.held[half][s]) for half in range(2)]

    def settle(self, s, sums):
        for half in range(2):
            self.held[half][s] = [(sums[half], 0)]

    def send(self, s):
        return [across(self.total(h, s), self.orders[h][s], self.count) for h in range(2)]

    def arrive(self, s, came):
        for half in range(2):
            first = 0
            for t in range(s + 1, len(self.plan[half])):
                self.held[half][t].append((came[half], first))
                first += len(self.plan[half][t])

    def between(self):
        for s in range(1, self.steps - 1):
            self.arrive(s, self.send(s))

    def last(self):
        return self.total(1, -1)[0]

    def finish(self, theirs):
        return sum(a[0].astype(F32) for a in self.parts(0, -1)), theirs.astype(F32)


def on_device(
    tokens,
    norm_gain,
    norm_bias,
    qkv_weight,
    qkv_bias,
    dense_weight,
    dense_bias,
    up_weight,
    up_bias,
    down_weight,
    down_bias,
    cotangent,
    *,
    ndp,
    nmp,
):
    me = lax.axis_index("dp")
    core = me % 2
    length, model = tokens.shape[0] * nmp, tokens.shape[1]
    tile, block = min(256, length), min(512, length)
    width, hidden = qkv_weight.shape[2] // 2, up_weight.shape[1] // 2
    chip_steps = len(chip_bits(ndp))
    rank = lambda array, axis, which, size: lax.dynamic_slice_in_dim(
        array, which * size, size, axis
    )

    def row_pack(which):
        qkv = rank(qkv_weight, 2, which, width)
        return jnp.concatenate([qkv[0], qkv[1], qkv[2], rank(up_weight, 1, which, hidden)], axis=1)

    def column_pack(which):
        return jnp.concatenate(
            [rank(dense_weight, 0, which, width), rank(down_weight, 0, which, hidden)], axis=0
        )

    pairs = width // LANES
    swap = lambda array: across(array, 1, ndp)
    line_gather = lambda array: lax.all_gather(array, "mp", axis=0, tiled=True)
    line_scatter = lambda array: lax.psum_scatter(array, "mp", scatter_dimension=0, tiled=True)
    x_own, dy_own = line_gather(tokens), line_gather(cotangent)
    rows = BlockGather(row_pack(core), swap(row_pack(1 - core)), ndp)
    columns = BlockGather(column_pack(core), swap(column_pack(1 - core)), ndp)
    rows.own_to(0)
    rows.fenced(deps=columns.held.values())
    rows.own_to(1)
    rows.fenced()
    rows.rest()
    x_own, *held = fence([x_own, columns.held[0], columns.held[1]], rows.blocks())
    columns.held = dict(enumerate(held))

    tables = rotary_tables(length)
    bias = jnp.concatenate(
        [
            rank(qkv_bias, 1, core, width).astype(F32).reshape(1, 3 * width),
            rank(up_bias[None, :], 1, core, hidden).astype(F32),
        ],
        axis=1,
    )
    gain, shift = norm_gain.astype(F32)[None, :], norm_bias.astype(F32)[None, :]
    x_other = swap(x_own)
    columns.own_to(0)
    common = (rows.blocks(), bias, gain, shift, tables, width, tile)
    first = project(0, x_own, *common, (), [columns.held[0]])
    (x_other,) = columns.fenced([x_other], [first[0]])
    columns.own_to(1)
    qkv, act, slope, normed = project(1, x_other, *common, first, [columns.held[0]])
    held = columns.fenced(rows.blocks(), [qkv])
    columns.rest()
    row_blocks, row_others = held, [swap(a) for a in held[:3]]
    mixed, lse = attend(qkv, length, block, [columns.held[0]])
    row_others = columns.fenced(row_others, [mixed])
    row_blocks[3:] = fence(row_blocks[3:], [row_others[0]])
    row_others += [swap(a) for a in row_blocks[3:]]
    other_sums, own_sums = branch_sums(mixed, act, columns.blocks(), tile, [row_blocks[3]])
    other_sums, dy_own, *row_others[3:] = fence([other_sums, dy_own, *row_others[3:]], [own_sums])
    theirs = swap(other_sums)
    dy_other = swap(dy_own)

    grads = (slope, columns.blocks(), width, tile)
    gmixed, gpre_own, *grad_a = grad_in(0, dy_own, *grads, (), [own_sums])
    theirs, dy_other = fence([theirs, dy_other], [grad_a[0]])
    total = add_rows(own_sums, theirs)
    branches = line_scatter(total)
    gmixed, gpre_other, *grad_b = grad_in(1, dy_other, *grads, [gmixed], [total])
    (gpre_sent,) = fence([gpre_other])
    gpre_came = swap(gpre_sent)
    column_grads = BlockScatter(
        weight_grads(me, [[mixed], [act]], [dy_own, dy_other], ndp, [gpre_sent], left=False), ndp
    )
    (gpre_came,) = fence([gpre_came], [column_grads.held[0][0][0][0]])
    column_came = column_grads.send(0)
    back = lambda sequence, deps: attend_back(
        sequence, qkv, gmixed, mixed, lse, tables, length, block, deps
    )
    *other, qkv_sums_b = back(1, [gpre_came])
    came = [swap(a) for a in other]
    *own, qkv_sums_a = back(0, [other[0]])
    came = fence([*came, *column_came], [own[0]])
    column_came, came = came[3:], came[:3]
    column_grads.arrive(0, column_came)
    column_grads.between()
    all_grads = [*own, gpre_own, *came, gpre_came]

    def normed_half(half, deps, adds=()):
        return grad_normed_sums(
            half, all_grads, x_own, [*row_blocks, *row_others], tile, deps, adds
        )

    total_a, sums_a, *settled = normed_half(0, [], column_grads.adds(chip_steps - 1))
    column_grads.settle(chip_steps - 1, settled)
    half_a = line_scatter(total_a)
    column_came = column_grads.send(chip_steps - 1)
    up_grads = BlockScatter(
        weight_grads(me, [normed], [[gpre_own, gpre_sent]], ndp, [sums_a], left=True), ndp
    )
    up_came = up_grads.send(0)
    c0, c1, branches = fence([*column_came, branches], [up_grads.held[0][0][0][0]])
    column_grads.arrive(chip_steps - 1, [c0, c1])
    blocks, column_last = weight_grads(
        me,
        [normed],
        [[a, b] for a, b in zip(own, other)],
        ndp,
        [c0],
        True,
        [column_grads.adds(len(column_grads.plan[1]) - 1)[1]],
    )
    qkv_grads = BlockScatter(blocks, ndp)
    qkv_came = qkv_grads.send(0)
    column_theirs = swap(column_last[0])
    total_b, sums_b = normed_half(1, [qkv_grads.held[0][0][0][0]])
    half_b = line_scatter(total_b)
    u0, u1, q0, q1, half_a, column_theirs = fence(
        [*up_came, *qkv_came, half_a, column_theirs], [sums_b]
    )
    up_grads.arrive(0, [u0, u1])
    qkv_grads.arrive(0, [q0, q1])
    up_grads.between()
    qkv_grads.between()
    up_came, qkv_came = up_grads.send(chip_steps - 1), qkv_grads.send(chip_steps - 1)
    u0, u1, q0, q1, branches, sums_b = fence([*up_came, *qkv_came, branches, sums_b])
    up_grads.arrive(chip_steps - 1, [u0, u1])
    qkv_grads.arrive(chip_steps - 1, [q0, q1])
    up_theirs = swap(up_grads.last())
    qkv_theirs = swap(qkv_grads.last())
    qkv_sum = (qkv_sums_a + qkv_sums_b)[:, :3, :].transpose(1, 0, 2).reshape(3 * width)
    norm_sums = jnp.concatenate([sums_a[:2], sums_b[:2]], axis=1)
    small = jnp.concatenate(
        [
            norm_sums.reshape(2 * model),
            qkv_sum,
            grad_a[0][0] + grad_b[0][0],
            grad_a[1][0] + grad_b[1][0],
        ]
    )
    for bit in chip_bits(ndp):
        small = small + across(small, bit, ndp)
    small_other = swap(small)
    norm_sums = small[: 2 * model] + small_other[: 2 * model]
    norm_sums = [norm_sums] + [
        lax.ppermute(norm_sums, "mp", [(i, i ^ j) for i in range(nmp)]) for j in range(1, nmp)
    ]
    while len(norm_sums) > 1:
        norm_sums = [a + b for a, b in zip(norm_sums[::2], norm_sums[1::2])]
    norm_sums = norm_sums[0]

    output = (
        tokens.astype(F32)
        + branches.astype(F32)
        + (dense_bias.astype(F32) + down_bias.astype(F32))[None, :]
    ).astype(BF16)

    def both(mine, theirs, axis):
        return jnp.where(
            core == 0,
            jnp.concatenate([mine, theirs], axis=axis),
            jnp.concatenate([theirs, mine], axis=axis),
        )

    mine, theirs = column_grads.finish(column_theirs)
    owned_dense = both(mine[:width], theirs[:width], 0)
    owned_down = both(mine[width:], theirs[width:], 0)
    owned_up = both(*up_grads.finish(up_theirs), 1)
    mine, theirs = qkv_grads.finish(qkv_theirs)
    owned_qkv = jnp.stack(
        [
            both(mine[:, c * width : (c + 1) * width], theirs[:, c * width : (c + 1) * width], 1)
            for c in range(3)
        ]
    )

    inner = 3 * width + hidden
    grad_out_bias = small[2 * model + inner :]
    here, there = (a[2 * model : 2 * model + inner] for a in (small, small_other))
    even, odd = jnp.where(core == 0, here, there), jnp.where(core == 0, there, here)
    grad_qkv_bias = jnp.concatenate(
        [a[: 3 * width].reshape(3, width) for a in (even, odd)], axis=1
    )
    grad_up_bias = jnp.concatenate([even[3 * width :], odd[3 * width :]])

    grad_tokens = norm_back(tokens, cotangent, gain, [half_a, half_b], [qkv_theirs])
    return (
        output,
        grad_tokens,
        norm_sums[:model],
        norm_sums[model:],
        owned_qkv,
        grad_qkv_bias,
        owned_dense,
        grad_out_bias,
        owned_up,
        grad_up_bias,
        owned_down,
        grad_out_bias,
    )


def solution(mesh):
    return jax.shard_map(
        functools.partial(on_device, ndp=mesh.shape["dp"], nmp=mesh.shape["mp"]),
        mesh=mesh,
        in_specs=(
            P(("dp", "mp"), None),
            P(),
            P(),
            P(None, "dp", "mp"),
            P(None, "mp"),
            P("mp", "dp"),
            P(),
            P("dp", "mp"),
            P("mp"),
            P("mp", "dp"),
            P(),
            P(("dp", "mp"), None),
        ),
        out_specs=(
            P(("dp", "mp"), None),
            P(("dp", "mp"), None),
            P(),
            P(),
            P(None, "dp", "mp"),
            P(None, "mp"),
            P("mp", "dp"),
            P(),
            P("dp", "mp"),
            P("mp"),
            P("mp", "dp"),
            P(),
        ),
        check_vma=False,
    )
```

```python
import functools

import jax
import jax.numpy as jnp
import numpy as np
from jax import lax
from jax.experimental import pallas as pl
from jax.experimental.pallas import tpu as pltpu
from jax.sharding import PartitionSpec as P

HEAD_DIM = 64
ROT = 32
EPS = 1e-05
LANES = 128
F32 = jnp.float32
BF16 = jnp.bfloat16
HBM = pl.BlockSpec(memory_space=pltpu.HBM)


def dot(lhs, rhs, lhs_dim, rhs_dim):
    return lax.dot_general(
        lhs, rhs, (((lhs_dim,), (rhs_dim,)), ((), ())), preferred_element_type=F32
    )


def call(kernel, name, operands, deps=(), scalars=(), adds=(), vmem=64, **spec):
    deps, out_shape = tuple(deps), spec.pop("out_shape")
    single = not isinstance(out_shape, list)
    out_shape = [out_shape] if single else out_shape
    out_specs = spec.pop("out_specs")
    out_specs = [out_specs] if single else list(out_specs)
    extra, extra_specs, sizes = [], [], []
    steps = spec["grid"][0] if adds else 1
    for many, addends in adds:
        _, rows, columns = addends[0][0].shape
        block = (many, rows // steps, columns)
        for array, first in addends:
            extra.append(array)
            extra_specs.append(
                pl.BlockSpec(block, lambda i, *at, first=first, many=many: (first // many, i, 0))
            )
        out_shape = out_shape + [jax.ShapeDtypeStruct((many, rows, columns), BF16)]
        out_specs = out_specs + [pl.BlockSpec(block, lambda i, *at: (0, i, 0))]
        sizes.append(len(addends))
    lead, outs = len(scalars) + len(operands), len(out_shape) - len(adds)

    def body(*refs):
        first = lead + len(extra) + len(deps)
        kernel(*refs[:lead], *refs[first : first + outs], *refs[first + outs + len(adds) :])
        sources = refs[lead : lead + len(extra)]
        for n, out in zip(sizes, refs[first + outs : first + outs + len(adds)]):
            out[...] = sum(ref[...].astype(F32) for ref in sources[:n]).astype(BF16)
            sources = sources[n:]

    in_specs = list(spec.pop("in_specs")) + extra_specs + [HBM] * len(deps)
    aliases = spec.pop("input_output_aliases", {})
    if scalars:
        grid_spec = pltpu.PrefetchScalarGridSpec(
            num_scalar_prefetch=len(scalars), in_specs=in_specs, out_specs=out_specs, **spec
        )
        spec = {"grid_spec": grid_spec}
    else:
        spec.update(in_specs=in_specs, out_specs=out_specs)
    results = pl.pallas_call(
        body,
        out_shape=out_shape,
        input_output_aliases=aliases,
        compiler_params=pltpu.CompilerParams(vmem_limit_bytes=vmem << 20),
        cost_estimate=pl.CostEstimate(flops=0, transcendentals=0, bytes_accessed=0),
        name=name,
        **spec,
    )(*scalars, *operands, *extra, *deps)
    return results[0] if single and not adds else results


def fence(values, deps=()):
    return list(
        call(
            lambda *refs: None,
            "fence",
            values,
            deps,
            in_specs=[HBM] * len(values),
            out_specs=[HBM] * len(values),
            out_shape=[jax.ShapeDtypeStruct(v.shape, v.dtype) for v in values],
            input_output_aliases={n: n for n in range(len(values))},
        )
    )


def rotary_tables(length):
    positions = np.arange(length, dtype=np.float32)
    frequency = 10000.0 ** (-np.arange(ROT // 2, dtype=np.float64) * 2.0 / ROT)
    angles = positions[:, None] * frequency.astype(np.float32)[None, :]
    cosine, sine = np.cos(angles.astype(np.float64)), np.sin(angles.astype(np.float64))
    rest = HEAD_DIM - ROT
    none = np.zeros((length, ROT // 2))
    ones, zeros = np.ones((length, rest)), np.zeros((length, rest))
    straight = np.concatenate([cosine, cosine, ones], axis=1)
    left = np.concatenate([-sine, none, zeros], axis=1)
    right = np.concatenate([none, sine, zeros], axis=1)
    return [
        jnp.asarray(np.concatenate([t, t], axis=1).astype(np.float32))
        for t in (straight, left, right)
    ]


def rotated(u, straight, left, right, sign):
    half = ROT // 2
    turned = pltpu.roll(u, LANES - half, 1) * left + pltpu.roll(u, half, 1) * right
    return u * straight + sign * turned


def normalized(x):
    x = x.astype(F32)
    centered = x - jnp.mean(x, axis=1, keepdims=True)
    variance = jnp.mean(centered * centered, axis=1, keepdims=True)
    return centered * lax.rsqrt(variance + EPS)


def block_copies(blocks, place, sems):
    me = lax.axis_index("dp")
    return [
        pltpu.make_async_copy(block, place(lax.bitwise_xor(me, j)), sems.at[j])
        for j, block in enumerate(blocks)
    ]


def span(owner, size):
    return pl.ds(pl.multiple_of(owner * size, size), size)


def rows_at(ref, size):
    return lambda owner: ref.at[pl.ds(pl.multiple_of(owner * size, size), size)]


def columns_at(ref, size):
    return lambda owner: ref.at[:, pl.ds(pl.multiple_of(owner * size, size), size)]


def project_kernel(setup, x_ref, bias_ref, gain_ref, shift_ref, cos_ref, left_ref, right_ref, *rest):
    count, width, hidden = setup
    blocks = rest[:count]
    qkv_ref, act_ref, slope_ref, normed_ref, held, sems = rest[-6:]

    @pl.when(pl.program_id(0) == 0)
    def _():
        loads = block_copies(blocks, rows_at(held, blocks[0].shape[0]), sems)
        for copy in loads:
            copy.start()
        for copy in loads:
            copy.wait()

    x = (normalized(x_ref[...]) * gain_ref[...] + shift_ref[...]).astype(BF16)
    normed_ref[...] = x
    root = 0.7978845608028654
    for t in range((3 * width + hidden) // width):
        columns = slice(t * width, (t + 1) * width)
        y = dot(x, held[:, columns], 1, 0) + bias_ref[:, columns]
        if t < 3:
            for g in range(width // LANES):
                part = y[:, g * LANES : (g + 1) * LANES]
                if t < 2:
                    part = rotated(part, cos_ref[...], left_ref[...], right_ref[...], 1.0)
                if t == 0:
                    part = part * HEAD_DIM**-0.5
                start = t * width + g * LANES
                qkv_ref[:, start : start + LANES] = part.astype(BF16)
        else:
            columns = slice((t - 3) * width, (t - 2) * width)
            square = y * y
            turn = jnp.tanh(root * y * (1.0 + 0.044715 * square))
            half = 0.5 * (1.0 + turn)
            act_ref[:, columns] = (y * half).astype(BF16)
            slope = half * (1.0 + y * (1.0 - turn) * (root + (3.0 * 0.044715 * root) * square))
            slope_ref[:, columns] = slope.astype(BF16)


def project(sequence, x, blocks, bias, gain, shift, tables, width, tile, earlier, deps):
    (length, model), total, count = x.shape, blocks[0].shape[1], len(blocks)
    hidden, steps = total - 3 * width, length // tile
    rows = lambda w: pl.BlockSpec((tile, w), lambda i: (i, 0))
    out = lambda w: pl.BlockSpec((tile, w), lambda i: (sequence * steps + i, 0))
    line = lambda a: pl.BlockSpec(a.shape, lambda i: (0, 0))
    widths = (3 * width, hidden, hidden, model)
    operands = [x, bias, gain, shift, *tables, *blocks]
    return call(
        functools.partial(project_kernel, (count, width, hidden)),
        "project",
        operands + list(earlier),
        deps,
        grid=(steps,),
        in_specs=[rows(model), line(bias), line(gain), line(shift)]
        + [rows(LANES)] * 3
        + [HBM] * (count + len(earlier)),
        out_specs=[out(w) for w in widths],
        out_shape=[jax.ShapeDtypeStruct((2 * length, w), BF16) for w in widths],
        input_output_aliases={len(operands) + n: n for n in range(len(earlier))},
        scratch_shapes=[pltpu.VMEM((model, total), BF16), pltpu.SemaphoreType.DMA((count,))],
    )


def attend_kernel(block, q_ref, k_ref, v_ref, out_ref, lse_ref):
    length = q_ref.shape[0]
    lane = lax.broadcasted_iota(jnp.int32, (1, LANES), 1)
    key = lax.broadcasted_iota(jnp.int32, (block, block), 0)
    causal = key <= lax.broadcasted_iota(jnp.int32, (block, block), 1)
    for i in range(length // block):
        rows, before = pl.ds(i * block, block), pl.ds(0, i * block)
        results = []
        for h in range(2):
            mine = (lane < HEAD_DIM) if h == 0 else (lane >= HEAD_DIM)
            query = jnp.where(mine, q_ref[rows, :], 0)
            near = jnp.where(causal, dot(k_ref[rows, :], query, 1, 1), -1e30)
            highest = jnp.max(near, axis=0, keepdims=True)
            if i:
                far = dot(k_ref[before, :], query, 1, 1)
                highest = jnp.maximum(highest, jnp.max(far, axis=0, keepdims=True))
            near = jnp.exp(near - highest)
            total = jnp.sum(near, axis=0, keepdims=True)
            if i:
                far = jnp.exp(far - highest)
                total = total + jnp.sum(far, axis=0, keepdims=True)
            inverse = 1.0 / total
            result = dot((near * inverse).astype(BF16), v_ref[rows, :], 0, 0)
            if i:
                result = result + dot((far * inverse).astype(BF16), v_ref[before, :], 0, 0)
            results.append(result)
            lse_ref[0, h : h + 1, rows] = highest + jnp.log(total)
        out_ref[rows, :] = jnp.where(lane < HEAD_DIM, results[0], results[1]).astype(BF16)


def pair_specs(length, pairs):
    return lambda off: pl.BlockSpec(
        (length, LANES), lambda g: (g // pairs, off * pairs + g % pairs)
    )


def attend(qkv, length, block, deps):
    width, sequences = qkv.shape[1] // 3, qkv.shape[0] // length
    pairs = width // LANES
    at = pair_specs(length, pairs)
    return call(
        functools.partial(attend_kernel, block),
        "attend",
        [qkv, qkv, qkv],
        deps,
        grid=(sequences * pairs,),
        in_specs=[at(0), at(1), at(2)],
        out_specs=[at(0), pl.BlockSpec((1, 8, length), lambda g: (g, 0, 0))],
        out_shape=[
            jax.ShapeDtypeStruct((qkv.shape[0], width), BF16),
            jax.ShapeDtypeStruct((sequences * pairs, 8, length), F32),
        ],
    )


def attend_back_kernel(
    block,
    q_ref,
    k_ref,
    v_ref,
    grad_ref,
    mixed_ref,
    lse_ref,
    cos_ref,
    left_ref,
    right_ref,
    gq_ref,
    gk_ref,
    gv_ref,
    sum_ref,
    gk_sum,
    gv_sum,
):
    length = q_ref.shape[0]
    lane = lax.broadcasted_iota(jnp.int32, (1, LANES), 1)
    key = lax.broadcasted_iota(jnp.int32, (block, block), 0)
    causal = key <= lax.broadcasted_iota(jnp.int32, (block, block), 1)
    count = length // block
    sum_ref[...] = jnp.zeros_like(sum_ref)

    def put(ref, which, rows, value):
        value = value.astype(BF16)
        ref[rows, :] = value
        sum_ref[0, which : which + 1, :] += jnp.sum(value.astype(F32), axis=0, keepdims=True)

    def unrotated(value, rows):
        return rotated(value, cos_ref[rows, :], left_ref[rows, :], right_ref[rows, :], -1.0)

    for i in reversed(range(count)):
        rows = pl.ds(i * block, block)
        product = grad_ref[rows, :].astype(F32) * mixed_ref[rows, :].astype(F32)
        gq = None
        for h in range(2):
            mine = (lane < HEAD_DIM) if h == 0 else (lane >= HEAD_DIM)
            query = jnp.where(mine, q_ref[rows, :], 0)
            grad = jnp.where(mine, grad_ref[rows, :], 0)
            ones = jnp.where(mine, jnp.ones((8, LANES), F32), 0.0)
            delta = lax.dot_general(
                ones,
                product,
                (((1,), (1,)), ((), ())),
                precision=lax.Precision.HIGHEST,
                preferred_element_type=F32,
            )[0:1, :]
            lse = lse_ref[0, h : h + 1, rows]
            for j in range(i + 1):
                keys = pl.ds(j * block, block)
                key_rows = k_ref[keys, :]
                probs = jnp.exp(dot(key_rows, query, 1, 1) - lse)
                if j == i:
                    probs = jnp.where(causal, probs, 0.0)
                gprobs = dot(v_ref[keys, :], grad, 1, 1)
                gscores = (probs * (gprobs - delta)).astype(BF16)
                gv, gk = dot(probs.astype(BF16), grad, 1, 0), dot(gscores, query, 1, 0)
                if i == count - 1 and h == 0:
                    gv_sum[keys, :] = gv
                    gk_sum[keys, :] = gk
                else:
                    gv_sum[keys, :] += gv
                    gk_sum[keys, :] += gk
                part = dot(gscores, jnp.where(mine, key_rows, 0), 0, 0)
                gq = part if gq is None else gq + part
        put(gq_ref, 0, rows, unrotated(gq * HEAD_DIM**-0.5, rows))
    for i in range(count):
        rows = pl.ds(i * block, block)
        put(gk_ref, 1, rows, unrotated(gk_sum[rows, :], rows))
        put(gv_ref, 2, rows, gv_sum[rows, :])


def attend_back(sequence, qkv, grad, mixed, lse, tables, length, block, deps):
    width = qkv.shape[1] // 3
    pairs = width // LANES
    at = lambda off: pl.BlockSpec((length, LANES), lambda g: (sequence, off * pairs + g))
    out = pl.BlockSpec((length, LANES), lambda g: (0, g))
    table = pl.BlockSpec((length, LANES), lambda g: (0, 0))
    small = pl.BlockSpec((1, 8, length), lambda g: (sequence * pairs + g, 0, 0))
    return call(
        functools.partial(attend_back_kernel, block),
        "attend_back",
        [qkv, qkv, qkv, grad, mixed, lse, *tables],
        deps,
        grid=(pairs,),
        in_specs=[at(0), at(1), at(2), at(0), at(0), small, table, table, table],
        out_specs=[out] * 3 + [pl.BlockSpec((1, 8, LANES), lambda g: (g, 0, 0))],
        out_shape=[jax.ShapeDtypeStruct((length, width), BF16)] * 3
        + [jax.ShapeDtypeStruct((pairs, 8, LANES), F32)],
        scratch_shapes=[pltpu.VMEM((length, LANES), F32)] * 2,
    )


def by_sequence(tile, width, steps):
    return [
        pl.BlockSpec((tile, width), lambda i: (jnp.minimum(i, steps - 1), 0)),
        pl.BlockSpec((tile, width), lambda i: (jnp.maximum(i - steps, 0), 0)),
    ]


def other_first(tile, width, steps):
    return pl.BlockSpec((tile, width), lambda i: ((i + steps) % (2 * steps), 0))


def put_by_sequence(step, steps, value, other_ref, own_ref):
    @pl.when(step < steps)
    def _():
        other_ref[...] = value

    @pl.when(step >= steps)
    def _():
        own_ref[...] = value


def branch_kernel(count, steps, mixed_ref, act_ref, *rest):
    blocks, (other_ref, own_ref, held, sems) = rest[:count], rest[count:]
    step = pl.program_id(0)

    @pl.when(step == 0)
    def _():
        loads = block_copies(blocks, columns_at(held, blocks[0].shape[1]), sems)
        for copy in loads:
            copy.start()
        for copy in loads:
            copy.wait()

    x = jnp.concatenate([mixed_ref[...], act_ref[...]], axis=1)
    put_by_sequence(step, steps, dot(x, held[...], 1, 0).astype(BF16), other_ref, own_ref)


def branch_sums(mixed, act, blocks, tile, deps):
    length, count = mixed.shape[0] // 2, len(blocks)
    inner, model, steps = blocks[0].shape[0], count * blocks[0].shape[1], length // tile
    return call(
        functools.partial(branch_kernel, count, steps),
        "branch_sums",
        [mixed, act, *blocks],
        deps,
        grid=(2 * steps,),
        in_specs=[other_first(tile, a.shape[1], steps) for a in (mixed, act)] + [HBM] * count,
        out_specs=by_sequence(tile, model, steps),
        out_shape=[jax.ShapeDtypeStruct((length, model), BF16)] * 2,
        scratch_shapes=[pltpu.VMEM((inner, model), BF16), pltpu.SemaphoreType.DMA((count,))],
    )


def grad_in_kernel(setup, dy_ref, slope_ref, *rest):
    count, width, hidden = setup
    blocks = rest[:count]
    gmixed_ref, gpre_ref, gsum_ref, dsum_ref, held, sems = rest[-6:]

    @pl.when(pl.program_id(0) == 0)
    def _():
        loads = block_copies(blocks, columns_at(held, blocks[0].shape[1]), sems)
        for copy in loads:
            copy.start()
        gsum_ref[...] = jnp.zeros_like(gsum_ref)
        dsum_ref[...] = jnp.zeros_like(dsum_ref)
        for copy in loads:
            copy.wait()

    dy = dy_ref[...]
    gmixed_ref[...] = dot(dy, held[:width, :], 1, 1).astype(BF16)
    for start in range(0, hidden, width):
        part = slice(start, start + width)
        gact = dot(dy, held[width + start : 2 * width + start, :], 1, 1)
        gpre = (gact * slope_ref[:, part].astype(F32)).astype(BF16)
        gpre_ref[:, part] = gpre
        gsum_ref[0:1, part] += jnp.sum(gpre.astype(F32), axis=0, keepdims=True)
    dsum_ref[0:1, :] += jnp.sum(dy.astype(F32), axis=0, keepdims=True)


def grad_in(sequence, dy, slope, blocks, width, tile, earlier, deps):
    (length, model), hidden, count = dy.shape, slope.shape[1], len(blocks)
    steps = length // tile
    at = lambda w: pl.BlockSpec((tile, w), lambda i: (sequence * steps + i, 0))
    total = lambda w: pl.BlockSpec((8, w), lambda i: (0, 0))
    operands = [dy, slope, *blocks]
    return call(
        functools.partial(grad_in_kernel, (count, width, hidden)),
        "grad_in",
        operands + list(earlier),
        deps,
        grid=(steps,),
        in_specs=[pl.BlockSpec((tile, model), lambda i: (i, 0)), at(hidden)]
        + [HBM] * (count + len(earlier)),
        out_specs=[
            at(width),
            pl.BlockSpec((tile, hidden), lambda i: (i, 0)),
            total(hidden),
            total(model),
        ],
        out_shape=[
            jax.ShapeDtypeStruct((2 * length, width), BF16),
            jax.ShapeDtypeStruct((length, hidden), BF16),
            jax.ShapeDtypeStruct((8, hidden), F32),
            jax.ShapeDtypeStruct((8, model), F32),
        ],
        input_output_aliases={len(operands) + n: n for n in range(len(earlier))},
        scratch_shapes=[
            pltpu.VMEM((width + hidden, model), BF16),
            pltpu.SemaphoreType.DMA((count,)),
        ],
    )


def add_kernel(a_ref, b_ref, out_ref):
    out_ref[...] = (a_ref[...].astype(F32) + b_ref[...].astype(F32)).astype(BF16)


def add_rows(a, b):
    rows = pl.BlockSpec((a.shape[0] // 8, a.shape[1]), lambda i: (i, 0))
    return call(
        add_kernel,
        "add_rows",
        [a, b],
        grid=(8,),
        in_specs=[rows, rows],
        out_specs=rows,
        out_shape=jax.ShapeDtypeStruct(a.shape, BF16),
    )


def grad_normed_kernel(count, half, x_ref, *rest):
    grads, blocks, (out_ref, sum_ref, held, sems) = rest[:8], rest[8 : 8 + 2 * count], rest[-4:]
    (size, total), few, me = blocks[0].shape, count // 2, lax.axis_index("dp")

    @pl.when(pl.program_id(0) == 0)
    def _():
        for start in (True, False):
            for n, block in enumerate(blocks):
                core, j = n // count, n % count
                owner = lax.bitwise_xor(me, j ^ core) - half * few
                columns = slice(core * total, (core + 1) * total)

                @pl.when((owner >= 0) & (owner < few))
                def _(start=start, n=n, block=block, owner=owner, columns=columns):
                    target = held.at[span(owner, size), columns]
                    copy = pltpu.make_async_copy(block, target, sems.at[n])
                    if start:
                        copy.start()
                    else:
                        copy.wait()

        sum_ref[...] = jnp.zeros_like(sum_ref)

    columns = slice(half * few * size, (half + 1) * few * size)
    normal = normalized(x_ref[...])[:, columns]
    g = jnp.concatenate([ref[...] for ref in grads], axis=1)
    result = dot(g, held[...], 1, 1)
    sum_ref[0:1, :] += jnp.sum(result * normal, axis=0, keepdims=True)
    sum_ref[1:2, :] += jnp.sum(result, axis=0, keepdims=True)
    out_ref[...] = result.astype(BF16)


def grad_normed_sums(half, grads, x, blocks, tile, deps, adds=()):
    (length, model), count, total = x.shape, len(blocks) // 2, blocks[0].shape[1]
    part = model // 2
    rows = lambda w: pl.BlockSpec((tile, w), lambda i: (i, 0))
    return call(
        functools.partial(grad_normed_kernel, count, half),
        "grad_normed_sums",
        [x, *grads, *blocks],
        deps,
        adds=adds,
        grid=(length // tile,),
        in_specs=[rows(model)] + [rows(g.shape[1]) for g in grads] + [HBM] * (2 * count),
        out_specs=[rows(part), pl.BlockSpec((8, part), lambda i: (0, 0))],
        out_shape=[
            jax.ShapeDtypeStruct((length, part), BF16),
            jax.ShapeDtypeStruct((8, part), F32),
        ],
        scratch_shapes=[
            pltpu.VMEM((part, 2 * total), BF16),
            pltpu.SemaphoreType.DMA((2 * count,)),
        ],
    )


def weight_grad_kernel(writes, left, rows, many, groups, at_ref, *refs):
    cuts, (*refs, held, grad, sems) = refs[:many], refs[many:]
    whole, outs = refs[: len(refs) - len(writes)], refs[len(refs) - len(writes) :]
    step, core, loads, first = pl.program_id(0), lax.rem(lax.axis_index("dp"), 2), [], 0
    for group in groups:
        below = 0
        for ref in whole[:group]:
            columns = pl.ds(first, ref.shape[1])
            for start in range(0, ref.shape[0], rows):
                target = held.at[pl.ds(below + start, rows), columns]
                loads.append((ref.at[pl.ds(start, rows)], target))
            below += ref.shape[0]
        first += whole[0].shape[1]
        whole = whole[group:]
    loads = [pltpu.make_async_copy(*pair, sems.at[n]) for n, pair in enumerate(loads)]

    @pl.when(step == 0)
    def _():
        for copy in loads:
            copy.start()
        for copy in loads:
            copy.wait()

    cut = jnp.concatenate([ref[...] for ref in cuts], axis=0)
    pair = (cut, held[...]) if left else (held[...], cut)
    grad[...] = dot(*pair, 0, 0).astype(BF16)
    size = cut.shape[1] // 2
    for half, steps, out_ref in writes_of(writes, outs):
        here = functools.reduce(jnp.logical_or, [step == s for s in steps])

        @pl.when(here)
        def _(half=half, out_ref=out_ref):
            mine = span(core if half == 0 else 1 - core, size)
            out_ref[0] = grad[mine, :] if left else grad[:, mine]


def writes_of(writes, outs):
    return [(half, steps, out) for (half, steps), out in zip(writes, outs)]


def weight_grads(me, xs, gs, count, deps, left, adds=()):
    plan, chips = scatter_plan(count), count // 2
    order = [j // 2 for s in plan[0] for j in s]
    sets = [(half, s) for s in range(len(plan[0])) for half in range(2)]
    writes = [(half, [order.index(j // 2) for j in plan[half][s]]) for half, s in sets]
    table = []
    for _, steps in writes:
        for i in range(chips):
            later = [w for w in steps if w >= i]
            table.append(steps.index(min(later) if later else max(steps)))
    owners = lax.bitwise_xor(me // 2, jnp.array(order, jnp.int32))
    at = jnp.concatenate([owners, jnp.array(table, jnp.int32)])
    cut, whole = (xs, gs) if left else (gs, xs)
    groups, length = [len(g) for g in whole], sum(a.shape[0] for a in whole[0])
    size, full = cut[0].shape[1] // count, sum(g[0].shape[1] for g in whole)
    shape, whole = (size, full) if left else (full, size), [a for g in whole for a in g]
    rows = length // 4
    pieces = 4 * len(groups)

    def out(n):
        return pl.BlockSpec((1, *shape), lambda i, at: (at[chips * (n + 1) + i], 0, 0))

    outs = call(
        functools.partial(weight_grad_kernel, writes, left, rows, len(cut), groups),
        "weight_grads",
        [*cut, *whole],
        deps,
        (at,),
        adds,
        grid=(chips,),
        in_specs=[pl.BlockSpec((a.shape[0], 2 * size), lambda i, at: (0, at[i])) for a in cut]
        + [HBM] * len(whole),
        out_specs=[out(n) for n in range(len(sets))],
        out_shape=[
            jax.ShapeDtypeStruct((len(plan[half][s]), *shape), BF16) for half, s in sets
        ],
        scratch_shapes=[
            pltpu.VMEM((length, full), BF16),
            pltpu.VMEM((2 * size, full) if left else (full, 2 * size), BF16),
            pltpu.SemaphoreType.DMA((pieces,)),
        ],
    )
    blocks = [[o for o, (half, _) in zip(outs, sets) if half == h] for h in range(2)]
    return (blocks, *outs[len(sets) :]) if adds else blocks


def norm_back_kernel(tokens_ref, dy_ref, gain_ref, left_ref, right_ref, out_ref):
    x = tokens_ref[...].astype(F32)
    centered = x - jnp.mean(x, axis=1, keepdims=True)
    inverse_std = lax.rsqrt(jnp.mean(centered * centered, axis=1, keepdims=True) + EPS)
    normal = centered * inverse_std
    grad = jnp.concatenate([left_ref[...], right_ref[...]], axis=1).astype(F32)
    scaled = grad * gain_ref[...]
    first_mean = jnp.mean(scaled, axis=1, keepdims=True)
    second_mean = jnp.mean(scaled * normal, axis=1, keepdims=True)
    back = (scaled - first_mean - normal * second_mean) * inverse_std
    out_ref[...] = (dy_ref[...].astype(F32) + back).astype(BF16)


def norm_back(tokens, dy, gain, halves, deps):
    rows, model = tokens.shape
    tile = min(64, rows)
    part = lambda w: pl.BlockSpec((tile, w), lambda i: (i, 0))
    return call(
        norm_back_kernel,
        "norm_back",
        [tokens, dy, gain, *halves],
        deps,
        grid=(rows // tile,),
        in_specs=[part(model), part(model), pl.BlockSpec((1, model), lambda i: (0, 0))]
        + [part(model // 2)] * 2,
        out_specs=part(model),
        out_shape=jax.ShapeDtypeStruct((rows, model), BF16),
    )


def across(value, bit, count):
    return lax.ppermute(value, "dp", [(i, i ^ bit) for i in range(count)])


def added(addends):
    return sum(a.astype(F32) for a in addends).astype(BF16)


def pair_sum(parts):
    while len(parts) > 1:
        parts = [a + b for a, b in zip(parts[::2], parts[1::2])]
    return parts[0]


def chip_bits(count):
    bits, bit = [], 2
    while bit < count:
        bits.append(bit)
        bit *= 2
    return bits


class BlockGather:
    def __init__(self, own, sibling, count):
        self.held, self.count = {0: own, 1: sibling}, count
        self.orders = (chip_bits(count), chip_bits(count)[::-1])

    def own_to(self, s):
        if s < len(self.orders[0]):
            for half in range(2):
                bit = self.orders[half][s]
                self.held[half ^ bit] = across(self.held[half], bit, self.count)

    def rest(self):
        for s in range(1, len(self.orders[0])):
            for half in range(2):
                order = self.orders[half]
                for j in [j for j in self.held if j % 2 == half]:
                    if j ^ order[s] not in self.held and not any(j & b for b in order[s:]):
                        self.held[j ^ order[s]] = across(self.held[j], order[s], self.count)

    def fenced(self, others=(), deps=()):
        keys = sorted(self.held)
        values = fence([self.held[j] for j in keys] + list(others), deps)
        self.held = dict(zip(keys, values))
        return values[len(keys) :]

    def blocks(self):
        return [self.held[j] for j in range(self.count)]


def scatter_orders(count):
    return (chip_bits(count)[::-1], chip_bits(count))


def scatter_plan(count):
    plan = []
    for half, order in enumerate(scatter_orders(count)):
        sets, rest = [[half]], [half]
        for bit in reversed(order):
            sets.insert(0, [j ^ bit for j in rest])
            rest = sets[0] + rest
        plan.append(sets)
    return plan


class BlockScatter:
    def __init__(self, halves, count):
        self.count, self.orders, self.plan = count, scatter_orders(count), scatter_plan(count)
        self.held = [[[(a, 0)] for a in arrays] for arrays in halves]
        self.steps = len(self.orders[0])

    def parts(self, half, s):
        many = len(self.plan[half][s])
        return [a[first : first + many] for a, first in self.held[half][s]]

    def total(self, half, s):
        if len(self.held[half][s]) > 1:
            self.held[half][s] = [(added(self.parts(half, s)), 0)]
        return self.parts(half, s)[0]

    def ready(self, s):
        return [self.total(half, s) for half in range(2)]

    def adds(self, s):
        return [(len(self.plan[half][s]), self.held[half][s]) for half in range(2)]

    def settle(self, s, sums):
        for half in range(2):
            self.held[half][s] = [(sums[half], 0)]

    def send(self, s):
        return [across(self.total(h, s), self.orders[h][s], self.count) for h in range(2)]

    def arrive(self, s, came):
        for half in range(2):
            first = 0
            for t in range(s + 1, len(self.plan[half])):
                self.held[half][t].append((came[half], first))
                first += len(self.plan[half][t])

    def between(self):
        for s in range(1, self.steps - 1):
            self.arrive(s, self.send(s))

    def last(self):
        return self.total(1, -1)[0]

    def finish(self, theirs):
        return sum(a[0].astype(F32) for a in self.parts(0, -1)), theirs.astype(F32)


def on_device(
    tokens,
    norm_gain,
    norm_bias,
    qkv_weight,
    qkv_bias,
    dense_weight,
    dense_bias,
    up_weight,
    up_bias,
    down_weight,
    down_bias,
    cotangent,
    *,
    ndp,
    nmp,
):
    me = lax.axis_index("dp")
    core = me % 2
    length, model = tokens.shape[0] * nmp, tokens.shape[1]
    tile, block = min(256, length), min(512, length)
    width, hidden = qkv_weight.shape[2] // 2, up_weight.shape[1] // 2
    chip_steps = len(chip_bits(ndp))
    rank = lambda array, axis, which, size: lax.dynamic_slice_in_dim(
        array, which * size, size, axis
    )

    def row_pack(which):
        qkv = rank(qkv_weight, 2, which, width)
        return jnp.concatenate([qkv[0], qkv[1], qkv[2], rank(up_weight, 1, which, hidden)], axis=1)

    def column_pack(which):
        return jnp.concatenate(
            [rank(dense_weight, 0, which, width), rank(down_weight, 0, which, hidden)], axis=0
        )

    pairs = width // LANES
    swap = lambda array: across(array, 1, ndp)
    line_gather = lambda array: lax.all_gather(array, "mp", axis=0, tiled=True)
    line_scatter = lambda array: lax.psum_scatter(array, "mp", scatter_dimension=0, tiled=True)
    x_own, dy_own = line_gather(tokens), line_gather(cotangent)
    rows = BlockGather(row_pack(core), swap(row_pack(1 - core)), ndp)
    columns = BlockGather(column_pack(core), swap(column_pack(1 - core)), ndp)
    rows.own_to(0)
    rows.fenced(deps=columns.held.values())
    rows.own_to(1)
    rows.fenced()
    rows.rest()
    x_own, *held = fence([x_own, columns.held[0], columns.held[1]], rows.blocks())
    columns.held = dict(enumerate(held))

    tables = rotary_tables(length)
    bias = jnp.concatenate(
        [
            rank(qkv_bias, 1, core, width).astype(F32).reshape(1, 3 * width),
            rank(up_bias[None, :], 1, core, hidden).astype(F32),
        ],
        axis=1,
    )
    gain, shift = norm_gain.astype(F32)[None, :], norm_bias.astype(F32)[None, :]
    x_other = swap(x_own)
    columns.own_to(0)
    common = (rows.blocks(), bias, gain, shift, tables, width, tile)
    first = project(0, x_own, *common, (), [columns.held[0]])
    (x_other,) = columns.fenced([x_other], [first[0]])
    columns.own_to(1)
    qkv, act, slope, normed = project(1, x_other, *common, first, [columns.held[0]])
    held = columns.fenced(rows.blocks(), [qkv])
    columns.rest()
    row_blocks, row_others = held, [swap(a) for a in held[:3]]
    mixed, lse = attend(qkv, length, block, [columns.held[0]])
    row_others = columns.fenced(row_others, [mixed])
    row_blocks[3:] = fence(row_blocks[3:], [row_others[0]])
    row_others += [swap(a) for a in row_blocks[3:]]
    other_sums, own_sums = branch_sums(mixed, act, columns.blocks(), tile, [row_blocks[3]])
    other_sums, dy_own, *row_others[3:] = fence([other_sums, dy_own, *row_others[3:]], [own_sums])
    theirs = swap(other_sums)
    dy_other = swap(dy_own)

    grads = (slope, columns.blocks(), width, tile)
    gmixed, gpre_own, *grad_a = grad_in(0, dy_own, *grads, (), [own_sums])
    theirs, dy_other = fence([theirs, dy_other], [grad_a[0]])
    total = add_rows(own_sums, theirs)
    branches = line_scatter(total)
    gmixed, gpre_other, *grad_b = grad_in(1, dy_other, *grads, [gmixed], [total])
    (gpre_sent,) = fence([gpre_other])
    gpre_came = swap(gpre_sent)
    column_grads = BlockScatter(
        weight_grads(me, [[mixed], [act]], [dy_own, dy_other], ndp, [gpre_sent], left=False), ndp
    )
    (gpre_came,) = fence([gpre_came], [column_grads.held[0][0][0][0]])
    column_came = column_grads.send(0)
    back = lambda sequence, deps: attend_back(
        sequence, qkv, gmixed, mixed, lse, tables, length, block, deps
    )
    *other, qkv_sums_b = back(1, [gpre_came])
    came = [swap(a) for a in other]
    *own, qkv_sums_a = back(0, [other[0]])
    came = fence([*came, *column_came], [own[0]])
    column_came, came = came[3:], came[:3]
    column_grads.arrive(0, column_came)
    column_grads.between()
    all_grads = [*own, gpre_own, *came, gpre_came]

    def normed_half(half, deps, adds=()):
        return grad_normed_sums(
            half, all_grads, x_own, [*row_blocks, *row_others], tile, deps, adds
        )

    total_a, sums_a, *settled = normed_half(0, [], column_grads.adds(chip_steps - 1))
    column_grads.settle(chip_steps - 1, settled)
    half_a = line_scatter(total_a)
    column_came = column_grads.send(chip_steps - 1)
    up_grads = BlockScatter(
        weight_grads(me, [normed], [[gpre_own, gpre_sent]], ndp, [sums_a], left=True), ndp
    )
    up_came = up_grads.send(0)
    qkv_grads = BlockScatter(
        weight_grads(
            me,
            [normed],
            [[a, b] for a, b in zip(own, other)],
            ndp,
            [up_grads.held[0][0][0][0]],
            left=True,
        ),
        ndp,
    )
    qkv_came = qkv_grads.send(0)
    c0, c1, branches = fence([*column_came, branches], [qkv_grads.held[0][0][0][0]])
    column_grads.arrive(chip_steps - 1, [c0, c1])
    total_b, sums_b, column_last = normed_half(
        1, [c0], [column_grads.adds(len(column_grads.plan[1]) - 1)[1]]
    )
    half_b = line_scatter(total_b)
    u0, u1, q0, q1, half_a, column_last = fence(
        [*up_came, *qkv_came, half_a, column_last], [sums_b]
    )
    column_theirs = swap(column_last[0])
    up_grads.arrive(0, [u0, u1])
    qkv_grads.arrive(0, [q0, q1])
    up_grads.between()
    qkv_grads.between()
    up_came, qkv_came = up_grads.send(chip_steps - 1), qkv_grads.send(chip_steps - 1)
    u0, u1, q0, q1, branches, sums_b, column_theirs = fence(
        [*up_came, *qkv_came, branches, sums_b, column_theirs]
    )
    up_grads.arrive(chip_steps - 1, [u0, u1])
    qkv_grads.arrive(chip_steps - 1, [q0, q1])
    up_theirs = swap(up_grads.last())
    qkv_theirs = swap(qkv_grads.last())
    qkv_sum = (qkv_sums_a + qkv_sums_b)[:, :3, :].transpose(1, 0, 2).reshape(3 * width)
    norm_sums = jnp.concatenate([sums_a[:2], sums_b[:2]], axis=1)
    small = jnp.concatenate(
        [
            norm_sums.reshape(2 * model),
            qkv_sum,
            grad_a[0][0] + grad_b[0][0],
            grad_a[1][0] + grad_b[1][0],
        ]
    )
    for bit in chip_bits(ndp):
        small = small + across(small, bit, ndp)
    small_other = swap(small)
    grad_tokens = norm_back(tokens, cotangent, gain, [half_a, half_b], [small])
    (norm_sums,) = fence([small[: 2 * model] + small_other[: 2 * model]], [grad_tokens])
    norm_sums = pair_sum(
        [norm_sums]
        + [
            lax.ppermute(norm_sums, "mp", [(i, i ^ j) for i in range(nmp)])
            for j in range(1, nmp)
        ]
    )

    output = (
        tokens.astype(F32)
        + branches.astype(F32)
        + (dense_bias.astype(F32) + down_bias.astype(F32))[None, :]
    ).astype(BF16)

    def both(mine, theirs, axis):
        return jnp.where(
            core == 0,
            jnp.concatenate([mine, theirs], axis=axis),
            jnp.concatenate([theirs, mine], axis=axis),
        )

    mine, theirs = column_grads.finish(column_theirs)
    owned_dense = both(mine[:width], theirs[:width], 0)
    owned_down = both(mine[width:], theirs[width:], 0)
    owned_up = both(*up_grads.finish(up_theirs), 1)
    mine, theirs = qkv_grads.finish(qkv_theirs)
    owned_qkv = jnp.stack(
        [
            both(mine[:, c * width : (c + 1) * width], theirs[:, c * width : (c + 1) * width], 1)
            for c in range(3)
        ]
    )

    inner = 3 * width + hidden
    grad_out_bias = small[2 * model + inner :]
    here, there = (a[2 * model : 2 * model + inner] for a in (small, small_other))
    even, odd = jnp.where(core == 0, here, there), jnp.where(core == 0, there, here)
    grad_qkv_bias = jnp.concatenate(
        [a[: 3 * width].reshape(3, width) for a in (even, odd)], axis=1
    )
    grad_up_bias = jnp.concatenate([even[3 * width :], odd[3 * width :]])

    return (
        output,
        grad_tokens,
        norm_sums[:model],
        norm_sums[model:],
        owned_qkv,
        grad_qkv_bias,
        owned_dense,
        grad_out_bias,
        owned_up,
        grad_up_bias,
        owned_down,
        grad_out_bias,
    )


def solution(mesh):
    return jax.shard_map(
        functools.partial(on_device, ndp=mesh.shape["dp"], nmp=mesh.shape["mp"]),
        mesh=mesh,
        in_specs=(
            P(("dp", "mp"), None),
            P(),
            P(),
            P(None, "dp", "mp"),
            P(None, "mp"),
            P("mp", "dp"),
            P(),
            P("dp", "mp"),
            P("mp"),
            P("mp", "dp"),
            P(),
            P(("dp", "mp"), None),
        ),
        out_specs=(
            P(("dp", "mp"), None),
            P(("dp", "mp"), None),
            P(),
            P(),
            P(None, "dp", "mp"),
            P(None, "mp"),
            P("mp", "dp"),
            P(),
            P("dp", "mp"),
            P("mp"),
            P("mp", "dp"),
            P(),
        ),
        check_vma=False,
    )
```

```python
import functools

import jax
import jax.numpy as jnp
import numpy as np
from jax import lax
from jax.experimental import pallas as pl
from jax.experimental.pallas import tpu as pltpu
from jax.sharding import PartitionSpec as P

HEAD_DIM = 64
ROT = 32
EPS = 1e-05
LANES = 128
F32 = jnp.float32
BF16 = jnp.bfloat16
HBM = pl.BlockSpec(memory_space=pltpu.HBM)


def dot(lhs, rhs, lhs_dim, rhs_dim):
    return lax.dot_general(
        lhs, rhs, (((lhs_dim,), (rhs_dim,)), ((), ())), preferred_element_type=F32
    )


def call(kernel, name, operands, deps=(), scalars=(), adds=(), vmem=64, **spec):
    deps, out_shape = tuple(deps), spec.pop("out_shape")
    single = not isinstance(out_shape, list)
    out_shape = [out_shape] if single else out_shape
    out_specs = spec.pop("out_specs")
    out_specs = [out_specs] if single else list(out_specs)
    extra, extra_specs, sizes = [], [], []
    steps = spec["grid"][0] if adds else 1
    for many, addends in adds:
        _, rows, columns = addends[0][0].shape
        block = (many, rows // steps, columns)
        for array, first in addends:
            extra.append(array)
            extra_specs.append(
                pl.BlockSpec(block, lambda i, *at, first=first, many=many: (first // many, i, 0))
            )
        out_shape = out_shape + [jax.ShapeDtypeStruct((many, rows, columns), BF16)]
        out_specs = out_specs + [pl.BlockSpec(block, lambda i, *at: (0, i, 0))]
        sizes.append(len(addends))
    lead, outs = len(scalars) + len(operands), len(out_shape) - len(adds)

    def body(*refs):
        first = lead + len(extra) + len(deps)
        kernel(*refs[:lead], *refs[first : first + outs], *refs[first + outs + len(adds) :])
        sources = refs[lead : lead + len(extra)]
        for n, out in zip(sizes, refs[first + outs : first + outs + len(adds)]):
            out[...] = sum(ref[...].astype(F32) for ref in sources[:n]).astype(BF16)
            sources = sources[n:]

    in_specs = list(spec.pop("in_specs")) + extra_specs + [HBM] * len(deps)
    aliases = spec.pop("input_output_aliases", {})
    if scalars:
        grid_spec = pltpu.PrefetchScalarGridSpec(
            num_scalar_prefetch=len(scalars), in_specs=in_specs, out_specs=out_specs, **spec
        )
        spec = {"grid_spec": grid_spec}
    else:
        spec.update(in_specs=in_specs, out_specs=out_specs)
    results = pl.pallas_call(
        body,
        out_shape=out_shape,
        input_output_aliases=aliases,
        compiler_params=pltpu.CompilerParams(vmem_limit_bytes=vmem << 20),
        cost_estimate=pl.CostEstimate(flops=0, transcendentals=0, bytes_accessed=0),
        name=name,
        **spec,
    )(*scalars, *operands, *extra, *deps)
    return results[0] if single and not adds else results


def fence(values, deps=()):
    return list(
        call(
            lambda *refs: None,
            "fence",
            values,
            deps,
            in_specs=[HBM] * len(values),
            out_specs=[HBM] * len(values),
            out_shape=[jax.ShapeDtypeStruct(v.shape, v.dtype) for v in values],
            input_output_aliases={n: n for n in range(len(values))},
        )
    )


def rotary_tables(length):
    positions = np.arange(length, dtype=np.float32)
    frequency = 10000.0 ** (-np.arange(ROT // 2, dtype=np.float64) * 2.0 / ROT)
    angles = positions[:, None] * frequency.astype(np.float32)[None, :]
    cosine, sine = np.cos(angles.astype(np.float64)), np.sin(angles.astype(np.float64))
    rest = HEAD_DIM - ROT
    none = np.zeros((length, ROT // 2))
    ones, zeros = np.ones((length, rest)), np.zeros((length, rest))
    straight = np.concatenate([cosine, cosine, ones], axis=1)
    left = np.concatenate([-sine, none, zeros], axis=1)
    right = np.concatenate([none, sine, zeros], axis=1)
    return [
        jnp.asarray(np.concatenate([t, t], axis=1).astype(np.float32))
        for t in (straight, left, right)
    ]


def rotated(u, straight, left, right, sign):
    half = ROT // 2
    turned = pltpu.roll(u, LANES - half, 1) * left + pltpu.roll(u, half, 1) * right
    return u * straight + sign * turned


def normalized(x):
    x = x.astype(F32)
    centered = x - jnp.mean(x, axis=1, keepdims=True)
    variance = jnp.mean(centered * centered, axis=1, keepdims=True)
    return centered * lax.rsqrt(variance + EPS)


def block_copies(blocks, place, sems):
    me = lax.axis_index("dp")
    return [
        pltpu.make_async_copy(block, place(lax.bitwise_xor(me, j)), sems.at[j])
        for j, block in enumerate(blocks)
    ]


def span(owner, size):
    return pl.ds(pl.multiple_of(owner * size, size), size)


def rows_at(ref, size):
    return lambda owner: ref.at[pl.ds(pl.multiple_of(owner * size, size), size)]


def columns_at(ref, size):
    return lambda owner: ref.at[:, pl.ds(pl.multiple_of(owner * size, size), size)]


def project_kernel(setup, x_ref, bias_ref, gain_ref, shift_ref, cos_ref, left_ref, right_ref, *rest):
    count, width, hidden = setup
    blocks = rest[:count]
    qkv_ref, act_ref, slope_ref, normed_ref, held, sems = rest[-6:]

    @pl.when(pl.program_id(0) == 0)
    def _():
        loads = block_copies(blocks, rows_at(held, blocks[0].shape[0]), sems)
        for copy in loads:
            copy.start()
        for copy in loads:
            copy.wait()

    x = (normalized(x_ref[...]) * gain_ref[...] + shift_ref[...]).astype(BF16)
    normed_ref[...] = x
    root = 0.7978845608028654
    for t in range((3 * width + hidden) // width):
        columns = slice(t * width, (t + 1) * width)
        y = dot(x, held[:, columns], 1, 0) + bias_ref[:, columns]
        if t < 3:
            for g in range(width // LANES):
                part = y[:, g * LANES : (g + 1) * LANES]
                if t < 2:
                    part = rotated(part, cos_ref[...], left_ref[...], right_ref[...], 1.0)
                if t == 0:
                    part = part * HEAD_DIM**-0.5
                start = t * width + g * LANES
                qkv_ref[:, start : start + LANES] = part.astype(BF16)
        else:
            columns = slice((t - 3) * width, (t - 2) * width)
            square = y * y
            turn = jnp.tanh(root * y * (1.0 + 0.044715 * square))
            half = 0.5 * (1.0 + turn)
            act_ref[:, columns] = (y * half).astype(BF16)
            slope = half * (1.0 + y * (1.0 - turn) * (root + (3.0 * 0.044715 * root) * square))
            slope_ref[:, columns] = slope.astype(BF16)


def project(sequence, x, blocks, bias, gain, shift, tables, width, tile, earlier, deps):
    (length, model), total, count = x.shape, blocks[0].shape[1], len(blocks)
    hidden, steps = total - 3 * width, length // tile
    rows = lambda w: pl.BlockSpec((tile, w), lambda i: (i, 0))
    out = lambda w: pl.BlockSpec((tile, w), lambda i: (sequence * steps + i, 0))
    line = lambda a: pl.BlockSpec(a.shape, lambda i: (0, 0))
    widths = (3 * width, hidden, hidden, model)
    operands = [x, bias, gain, shift, *tables, *blocks]
    return call(
        functools.partial(project_kernel, (count, width, hidden)),
        "project",
        operands + list(earlier),
        deps,
        grid=(steps,),
        in_specs=[rows(model), line(bias), line(gain), line(shift)]
        + [rows(LANES)] * 3
        + [HBM] * (count + len(earlier)),
        out_specs=[out(w) for w in widths],
        out_shape=[jax.ShapeDtypeStruct((2 * length, w), BF16) for w in widths],
        input_output_aliases={len(operands) + n: n for n in range(len(earlier))},
        scratch_shapes=[pltpu.VMEM((model, total), BF16), pltpu.SemaphoreType.DMA((count,))],
    )


def attend_kernel(block, q_ref, k_ref, v_ref, out_ref, lse_ref):
    length = q_ref.shape[0]
    lane = lax.broadcasted_iota(jnp.int32, (1, LANES), 1)
    key = lax.broadcasted_iota(jnp.int32, (block, block), 0)
    causal = key <= lax.broadcasted_iota(jnp.int32, (block, block), 1)
    for i in range(length // block):
        rows, before = pl.ds(i * block, block), pl.ds(0, i * block)
        results = []
        for h in range(2):
            mine = (lane < HEAD_DIM) if h == 0 else (lane >= HEAD_DIM)
            query = jnp.where(mine, q_ref[rows, :], 0)
            near = jnp.where(causal, dot(k_ref[rows, :], query, 1, 1), -1e30)
            highest = jnp.max(near, axis=0, keepdims=True)
            if i:
                far = dot(k_ref[before, :], query, 1, 1)
                highest = jnp.maximum(highest, jnp.max(far, axis=0, keepdims=True))
            near = jnp.exp(near - highest)
            total = jnp.sum(near, axis=0, keepdims=True)
            if i:
                far = jnp.exp(far - highest)
                total = total + jnp.sum(far, axis=0, keepdims=True)
            inverse = 1.0 / total
            result = dot((near * inverse).astype(BF16), v_ref[rows, :], 0, 0)
            if i:
                result = result + dot((far * inverse).astype(BF16), v_ref[before, :], 0, 0)
            results.append(result)
            lse_ref[0, h : h + 1, rows] = highest + jnp.log(total)
        out_ref[rows, :] = jnp.where(lane < HEAD_DIM, results[0], results[1]).astype(BF16)


def pair_specs(length, pairs):
    return lambda off: pl.BlockSpec(
        (length, LANES), lambda g: (g // pairs, off * pairs + g % pairs)
    )


def attend(qkv, length, block, deps):
    width, sequences = qkv.shape[1] // 3, qkv.shape[0] // length
    pairs = width // LANES
    at = pair_specs(length, pairs)
    return call(
        functools.partial(attend_kernel, block),
        "attend",
        [qkv, qkv, qkv],
        deps,
        grid=(sequences * pairs,),
        in_specs=[at(0), at(1), at(2)],
        out_specs=[at(0), pl.BlockSpec((1, 8, length), lambda g: (g, 0, 0))],
        out_shape=[
            jax.ShapeDtypeStruct((qkv.shape[0], width), BF16),
            jax.ShapeDtypeStruct((sequences * pairs, 8, length), F32),
        ],
    )


def attend_back_kernel(
    block,
    q_ref,
    k_ref,
    v_ref,
    grad_ref,
    mixed_ref,
    lse_ref,
    cos_ref,
    left_ref,
    right_ref,
    gq_ref,
    gk_ref,
    gv_ref,
    sum_ref,
    gk_sum,
    gv_sum,
):
    length = q_ref.shape[0]
    lane = lax.broadcasted_iota(jnp.int32, (1, LANES), 1)
    key = lax.broadcasted_iota(jnp.int32, (block, block), 0)
    causal = key <= lax.broadcasted_iota(jnp.int32, (block, block), 1)
    count = length // block
    sum_ref[...] = jnp.zeros_like(sum_ref)

    def put(ref, which, rows, value):
        value = value.astype(BF16)
        ref[rows, :] = value
        sum_ref[0, which : which + 1, :] += jnp.sum(value.astype(F32), axis=0, keepdims=True)

    def unrotated(value, rows):
        return rotated(value, cos_ref[rows, :], left_ref[rows, :], right_ref[rows, :], -1.0)

    for i in reversed(range(count)):
        rows = pl.ds(i * block, block)
        product = grad_ref[rows, :].astype(F32) * mixed_ref[rows, :].astype(F32)
        gq = None
        for h in range(2):
            mine = (lane < HEAD_DIM) if h == 0 else (lane >= HEAD_DIM)
            query = jnp.where(mine, q_ref[rows, :], 0)
            grad = jnp.where(mine, grad_ref[rows, :], 0)
            ones = jnp.where(mine, jnp.ones((8, LANES), F32), 0.0)
            delta = lax.dot_general(
                ones,
                product,
                (((1,), (1,)), ((), ())),
                precision=lax.Precision.HIGHEST,
                preferred_element_type=F32,
            )[0:1, :]
            lse = lse_ref[0, h : h + 1, rows]
            for j in range(i + 1):
                keys = pl.ds(j * block, block)
                key_rows = k_ref[keys, :]
                probs = jnp.exp(dot(key_rows, query, 1, 1) - lse)
                if j == i:
                    probs = jnp.where(causal, probs, 0.0)
                gprobs = dot(v_ref[keys, :], grad, 1, 1)
                gscores = (probs * (gprobs - delta)).astype(BF16)
                gv, gk = dot(probs.astype(BF16), grad, 1, 0), dot(gscores, query, 1, 0)
                if i == count - 1 and h == 0:
                    gv_sum[keys, :] = gv
                    gk_sum[keys, :] = gk
                else:
                    gv_sum[keys, :] += gv
                    gk_sum[keys, :] += gk
                part = dot(gscores, jnp.where(mine, key_rows, 0), 0, 0)
                gq = part if gq is None else gq + part
        put(gq_ref, 0, rows, unrotated(gq * HEAD_DIM**-0.5, rows))
    for i in range(count):
        rows = pl.ds(i * block, block)
        put(gk_ref, 1, rows, unrotated(gk_sum[rows, :], rows))
        put(gv_ref, 2, rows, gv_sum[rows, :])


def attend_back(sequence, qkv, grad, mixed, lse, tables, length, block, deps):
    width = qkv.shape[1] // 3
    pairs = width // LANES
    at = lambda off: pl.BlockSpec((length, LANES), lambda g: (sequence, off * pairs + g))
    out = pl.BlockSpec((length, LANES), lambda g: (0, g))
    table = pl.BlockSpec((length, LANES), lambda g: (0, 0))
    small = pl.BlockSpec((1, 8, length), lambda g: (sequence * pairs + g, 0, 0))
    return call(
        functools.partial(attend_back_kernel, block),
        "attend_back",
        [qkv, qkv, qkv, grad, mixed, lse, *tables],
        deps,
        grid=(pairs,),
        in_specs=[at(0), at(1), at(2), at(0), at(0), small, table, table, table],
        out_specs=[out] * 3 + [pl.BlockSpec((1, 8, LANES), lambda g: (g, 0, 0))],
        out_shape=[jax.ShapeDtypeStruct((length, width), BF16)] * 3
        + [jax.ShapeDtypeStruct((pairs, 8, LANES), F32)],
        scratch_shapes=[pltpu.VMEM((length, LANES), F32)] * 2,
    )


def by_sequence(tile, width, steps):
    return [
        pl.BlockSpec((tile, width), lambda i: (jnp.minimum(i, steps - 1), 0)),
        pl.BlockSpec((tile, width), lambda i: (jnp.maximum(i - steps, 0), 0)),
    ]


def other_first(tile, width, steps):
    return pl.BlockSpec((tile, width), lambda i: ((i + steps) % (2 * steps), 0))


def put_by_sequence(step, steps, value, other_ref, own_ref):
    @pl.when(step < steps)
    def _():
        other_ref[...] = value

    @pl.when(step >= steps)
    def _():
        own_ref[...] = value


def branch_kernel(count, steps, mixed_ref, act_ref, *rest):
    blocks, (other_ref, own_ref, held, sems) = rest[:count], rest[count:]
    step = pl.program_id(0)

    @pl.when(step == 0)
    def _():
        loads = block_copies(blocks, columns_at(held, blocks[0].shape[1]), sems)
        for copy in loads:
            copy.start()
        for copy in loads:
            copy.wait()

    x = jnp.concatenate([mixed_ref[...], act_ref[...]], axis=1)
    put_by_sequence(step, steps, dot(x, held[...], 1, 0).astype(BF16), other_ref, own_ref)


def branch_sums(mixed, act, blocks, tile, deps):
    length, count = mixed.shape[0] // 2, len(blocks)
    inner, model, steps = blocks[0].shape[0], count * blocks[0].shape[1], length // tile
    return call(
        functools.partial(branch_kernel, count, steps),
        "branch_sums",
        [mixed, act, *blocks],
        deps,
        grid=(2 * steps,),
        in_specs=[other_first(tile, a.shape[1], steps) for a in (mixed, act)] + [HBM] * count,
        out_specs=by_sequence(tile, model, steps),
        out_shape=[jax.ShapeDtypeStruct((length, model), BF16)] * 2,
        scratch_shapes=[pltpu.VMEM((inner, model), BF16), pltpu.SemaphoreType.DMA((count,))],
    )


def grad_in_kernel(setup, dy_ref, slope_ref, *rest):
    count, width, hidden = setup
    blocks = rest[:count]
    gmixed_ref, gpre_ref, gsum_ref, dsum_ref, held, sems = rest[-6:]

    @pl.when(pl.program_id(0) == 0)
    def _():
        loads = block_copies(blocks, columns_at(held, blocks[0].shape[1]), sems)
        for copy in loads:
            copy.start()
        gsum_ref[...] = jnp.zeros_like(gsum_ref)
        dsum_ref[...] = jnp.zeros_like(dsum_ref)
        for copy in loads:
            copy.wait()

    dy = dy_ref[...]
    gmixed_ref[...] = dot(dy, held[:width, :], 1, 1).astype(BF16)
    for start in range(0, hidden, width):
        part = slice(start, start + width)
        gact = dot(dy, held[width + start : 2 * width + start, :], 1, 1)
        gpre = (gact * slope_ref[:, part].astype(F32)).astype(BF16)
        gpre_ref[:, part] = gpre
        gsum_ref[0:1, part] += jnp.sum(gpre.astype(F32), axis=0, keepdims=True)
    dsum_ref[0:1, :] += jnp.sum(dy.astype(F32), axis=0, keepdims=True)


def grad_in(sequence, dy, slope, blocks, width, tile, earlier, deps):
    (length, model), hidden, count = dy.shape, slope.shape[1], len(blocks)
    steps = length // tile
    at = lambda w: pl.BlockSpec((tile, w), lambda i: (sequence * steps + i, 0))
    total = lambda w: pl.BlockSpec((8, w), lambda i: (0, 0))
    operands = [dy, slope, *blocks]
    return call(
        functools.partial(grad_in_kernel, (count, width, hidden)),
        "grad_in",
        operands + list(earlier),
        deps,
        grid=(steps,),
        in_specs=[pl.BlockSpec((tile, model), lambda i: (i, 0)), at(hidden)]
        + [HBM] * (count + len(earlier)),
        out_specs=[
            at(width),
            pl.BlockSpec((tile, hidden), lambda i: (i, 0)),
            total(hidden),
            total(model),
        ],
        out_shape=[
            jax.ShapeDtypeStruct((2 * length, width), BF16),
            jax.ShapeDtypeStruct((length, hidden), BF16),
            jax.ShapeDtypeStruct((8, hidden), F32),
            jax.ShapeDtypeStruct((8, model), F32),
        ],
        input_output_aliases={len(operands) + n: n for n in range(len(earlier))},
        scratch_shapes=[
            pltpu.VMEM((width + hidden, model), BF16),
            pltpu.SemaphoreType.DMA((count,)),
        ],
    )


def add_kernel(a_ref, b_ref, out_ref):
    out_ref[...] = (a_ref[...].astype(F32) + b_ref[...].astype(F32)).astype(BF16)


def add_rows(a, b):
    rows = pl.BlockSpec((a.shape[0] // 8, a.shape[1]), lambda i: (i, 0))
    return call(
        add_kernel,
        "add_rows",
        [a, b],
        grid=(8,),
        in_specs=[rows, rows],
        out_specs=rows,
        out_shape=jax.ShapeDtypeStruct(a.shape, BF16),
    )


def grad_normed_kernel(count, half, x_ref, *rest):
    grads, blocks, (out_ref, sum_ref, held, sems) = rest[:8], rest[8 : 8 + 2 * count], rest[-4:]
    (size, total), few, me = blocks[0].shape, count // 2, lax.axis_index("dp")

    @pl.when(pl.program_id(0) == 0)
    def _():
        for start in (True, False):
            for n, block in enumerate(blocks):
                core, j = n // count, n % count
                owner = lax.bitwise_xor(me, j ^ core) - half * few
                columns = slice(core * total, (core + 1) * total)

                @pl.when((owner >= 0) & (owner < few))
                def _(start=start, n=n, block=block, owner=owner, columns=columns):
                    target = held.at[span(owner, size), columns]
                    copy = pltpu.make_async_copy(block, target, sems.at[n])
                    if start:
                        copy.start()
                    else:
                        copy.wait()

        sum_ref[...] = jnp.zeros_like(sum_ref)

    columns = slice(half * few * size, (half + 1) * few * size)
    normal = normalized(x_ref[...])[:, columns]
    g = jnp.concatenate([ref[...] for ref in grads], axis=1)
    result = dot(g, held[...], 1, 1)
    sum_ref[0:1, :] += jnp.sum(result * normal, axis=0, keepdims=True)
    sum_ref[1:2, :] += jnp.sum(result, axis=0, keepdims=True)
    out_ref[...] = result.astype(BF16)


def grad_normed_sums(half, grads, x, blocks, tile, deps, adds=()):
    (length, model), count, total = x.shape, len(blocks) // 2, blocks[0].shape[1]
    part = model // 2
    rows = lambda w: pl.BlockSpec((tile, w), lambda i: (i, 0))
    return call(
        functools.partial(grad_normed_kernel, count, half),
        "grad_normed_sums",
        [x, *grads, *blocks],
        deps,
        adds=adds,
        grid=(length // tile,),
        in_specs=[rows(model)] + [rows(g.shape[1]) for g in grads] + [HBM] * (2 * count),
        out_specs=[rows(part), pl.BlockSpec((8, part), lambda i: (0, 0))],
        out_shape=[
            jax.ShapeDtypeStruct((length, part), BF16),
            jax.ShapeDtypeStruct((8, part), F32),
        ],
        scratch_shapes=[
            pltpu.VMEM((part, 2 * total), BF16),
            pltpu.SemaphoreType.DMA((2 * count,)),
        ],
    )


def weight_grad_kernel(writes, left, rows, many, groups, at_ref, *refs):
    cuts, (*refs, held, grad, sems) = refs[:many], refs[many:]
    whole, outs = refs[: len(refs) - len(writes)], refs[len(refs) - len(writes) :]
    step, core, loads, first = pl.program_id(0), lax.rem(lax.axis_index("dp"), 2), [], 0
    for group in groups:
        below = 0
        for ref in whole[:group]:
            columns = pl.ds(first, ref.shape[1])
            for start in range(0, ref.shape[0], rows):
                target = held.at[pl.ds(below + start, rows), columns]
                loads.append((ref.at[pl.ds(start, rows)], target))
            below += ref.shape[0]
        first += whole[0].shape[1]
        whole = whole[group:]
    loads = [pltpu.make_async_copy(*pair, sems.at[n]) for n, pair in enumerate(loads)]

    @pl.when(step == 0)
    def _():
        for copy in loads:
            copy.start()
        for copy in loads:
            copy.wait()

    cut = jnp.concatenate([ref[...] for ref in cuts], axis=0)
    pair = (cut, held[...]) if left else (held[...], cut)
    grad[...] = dot(*pair, 0, 0).astype(BF16)
    size = cut.shape[1] // 2
    for half, steps, out_ref in writes_of(writes, outs):
        here = functools.reduce(jnp.logical_or, [step == s for s in steps])

        @pl.when(here)
        def _(half=half, out_ref=out_ref):
            mine = span(core if half == 0 else 1 - core, size)
            out_ref[0] = grad[mine, :] if left else grad[:, mine]


def writes_of(writes, outs):
    return [(half, steps, out) for (half, steps), out in zip(writes, outs)]


def weight_grads(me, xs, gs, count, deps, left, adds=()):
    plan, chips = scatter_plan(count), count // 2
    order = [j // 2 for s in plan[0] for j in s]
    sets = [(half, s) for s in range(len(plan[0])) for half in range(2)]
    writes = [(half, [order.index(j // 2) for j in plan[half][s]]) for half, s in sets]
    table = []
    for _, steps in writes:
        for i in range(chips):
            later = [w for w in steps if w >= i]
            table.append(steps.index(min(later) if later else max(steps)))
    owners = lax.bitwise_xor(me // 2, jnp.array(order, jnp.int32))
    at = jnp.concatenate([owners, jnp.array(table, jnp.int32)])
    cut, whole = (xs, gs) if left else (gs, xs)
    groups, length = [len(g) for g in whole], sum(a.shape[0] for a in whole[0])
    size, full = cut[0].shape[1] // count, sum(g[0].shape[1] for g in whole)
    shape, whole = (size, full) if left else (full, size), [a for g in whole for a in g]
    rows = length // 4
    pieces = 4 * len(groups)

    def out(n):
        return pl.BlockSpec((1, *shape), lambda i, at: (at[chips * (n + 1) + i], 0, 0))

    outs = call(
        functools.partial(weight_grad_kernel, writes, left, rows, len(cut), groups),
        "weight_grads",
        [*cut, *whole],
        deps,
        (at,),
        adds,
        grid=(chips,),
        in_specs=[pl.BlockSpec((a.shape[0], 2 * size), lambda i, at: (0, at[i])) for a in cut]
        + [HBM] * len(whole),
        out_specs=[out(n) for n in range(len(sets))],
        out_shape=[
            jax.ShapeDtypeStruct((len(plan[half][s]), *shape), BF16) for half, s in sets
        ],
        scratch_shapes=[
            pltpu.VMEM((length, full), BF16),
            pltpu.VMEM((2 * size, full) if left else (full, 2 * size), BF16),
            pltpu.SemaphoreType.DMA((pieces,)),
        ],
    )
    blocks = [[o for o, (half, _) in zip(outs, sets) if half == h] for h in range(2)]
    return (blocks, *outs[len(sets) :]) if adds else blocks


def norm_back_kernel(tokens_ref, dy_ref, gain_ref, left_ref, right_ref, out_ref):
    x = tokens_ref[...].astype(F32)
    centered = x - jnp.mean(x, axis=1, keepdims=True)
    inverse_std = lax.rsqrt(jnp.mean(centered * centered, axis=1, keepdims=True) + EPS)
    normal = centered * inverse_std
    grad = jnp.concatenate([left_ref[...], right_ref[...]], axis=1).astype(F32)
    scaled = grad * gain_ref[...]
    first_mean = jnp.mean(scaled, axis=1, keepdims=True)
    second_mean = jnp.mean(scaled * normal, axis=1, keepdims=True)
    back = (scaled - first_mean - normal * second_mean) * inverse_std
    out_ref[...] = (dy_ref[...].astype(F32) + back).astype(BF16)


def norm_back(tokens, dy, gain, halves, deps):
    rows, model = tokens.shape
    tile = min(64, rows)
    part = lambda w: pl.BlockSpec((tile, w), lambda i: (i, 0))
    return call(
        norm_back_kernel,
        "norm_back",
        [tokens, dy, gain, *halves],
        deps,
        grid=(rows // tile,),
        in_specs=[part(model), part(model), pl.BlockSpec((1, model), lambda i: (0, 0))]
        + [part(model // 2)] * 2,
        out_specs=part(model),
        out_shape=jax.ShapeDtypeStruct((rows, model), BF16),
    )


def across(value, bit, count):
    return lax.ppermute(value, "dp", [(i, i ^ bit) for i in range(count)])


def added(addends):
    return sum(a.astype(F32) for a in addends).astype(BF16)


def chip_bits(count):
    bits, bit = [], 2
    while bit < count:
        bits.append(bit)
        bit *= 2
    return bits


class BlockGather:
    def __init__(self, own, sibling, count):
        self.held, self.count = {0: own, 1: sibling}, count
        self.orders = (chip_bits(count), chip_bits(count)[::-1])

    def own_to(self, s):
        if s < len(self.orders[0]):
            for half in range(2):
                bit = self.orders[half][s]
                self.held[half ^ bit] = across(self.held[half], bit, self.count)

    def rest(self):
        for s in range(1, len(self.orders[0])):
            for half in range(2):
                order = self.orders[half]
                for j in [j for j in self.held if j % 2 == half]:
                    if j ^ order[s] not in self.held and not any(j & b for b in order[s:]):
                        self.held[j ^ order[s]] = across(self.held[j], order[s], self.count)

    def fenced(self, others=(), deps=()):
        keys = sorted(self.held)
        values = fence([self.held[j] for j in keys] + list(others), deps)
        self.held = dict(zip(keys, values))
        return values[len(keys) :]

    def blocks(self):
        return [self.held[j] for j in range(self.count)]


def scatter_orders(count):
    return (chip_bits(count)[::-1], chip_bits(count))


def scatter_plan(count):
    plan = []
    for half, order in enumerate(scatter_orders(count)):
        sets, rest = [[half]], [half]
        for bit in reversed(order):
            sets.insert(0, [j ^ bit for j in rest])
            rest = sets[0] + rest
        plan.append(sets)
    return plan


class BlockScatter:
    def __init__(self, halves, count):
        self.count, self.orders, self.plan = count, scatter_orders(count), scatter_plan(count)
        self.held = [[[(a, 0)] for a in arrays] for arrays in halves]
        self.steps = len(self.orders[0])

    def parts(self, half, s):
        many = len(self.plan[half][s])
        return [a[first : first + many] for a, first in self.held[half][s]]

    def total(self, half, s):
        if len(self.held[half][s]) > 1:
            self.held[half][s] = [(added(self.parts(half, s)), 0)]
        return self.parts(half, s)[0]

    def ready(self, s):
        return [self.total(half, s) for half in range(2)]

    def adds(self, s):
        return [(len(self.plan[half][s]), self.held[half][s]) for half in range(2)]

    def settle(self, s, sums):
        for half in range(2):
            self.held[half][s] = [(sums[half], 0)]

    def send(self, s):
        return [across(self.total(h, s), self.orders[h][s], self.count) for h in range(2)]

    def arrive(self, s, came):
        for half in range(2):
            first = 0
            for t in range(s + 1, len(self.plan[half])):
                self.held[half][t].append((came[half], first))
                first += len(self.plan[half][t])

    def between(self):
        for s in range(1, self.steps - 1):
            self.arrive(s, self.send(s))

    def last(self):
        return self.total(1, -1)[0]

    def finish(self, theirs):
        return sum(a[0].astype(F32) for a in self.parts(0, -1)), theirs.astype(F32)


def on_device(
    tokens,
    norm_gain,
    norm_bias,
    qkv_weight,
    qkv_bias,
    dense_weight,
    dense_bias,
    up_weight,
    up_bias,
    down_weight,
    down_bias,
    cotangent,
    *,
    ndp,
    nmp,
):
    me = lax.axis_index("dp")
    core = me % 2
    length, model = tokens.shape[0] * nmp, tokens.shape[1]
    tile, block = min(256, length), min(512, length)
    width, hidden = qkv_weight.shape[2] // 2, up_weight.shape[1] // 2
    chip_steps = len(chip_bits(ndp))
    rank = lambda array, axis, which, size: lax.dynamic_slice_in_dim(
        array, which * size, size, axis
    )

    def row_pack(which):
        qkv = rank(qkv_weight, 2, which, width)
        return jnp.concatenate([qkv[0], qkv[1], qkv[2], rank(up_weight, 1, which, hidden)], axis=1)

    def column_pack(which):
        return jnp.concatenate(
            [rank(dense_weight, 0, which, width), rank(down_weight, 0, which, hidden)], axis=0
        )

    pairs = width // LANES
    swap = lambda array: across(array, 1, ndp)
    line_gather = lambda array: lax.all_gather(array, "mp", axis=0, tiled=True)
    line_scatter = lambda array: lax.psum_scatter(array, "mp", scatter_dimension=0, tiled=True)
    x_own, dy_own = line_gather(tokens), line_gather(cotangent)
    rows = BlockGather(row_pack(core), swap(row_pack(1 - core)), ndp)
    columns = BlockGather(column_pack(core), swap(column_pack(1 - core)), ndp)
    rows.own_to(0)
    rows.fenced(deps=columns.held.values())
    rows.own_to(1)
    rows.fenced()
    rows.rest()
    x_own, *held = fence([x_own, columns.held[0], columns.held[1]], rows.blocks())
    columns.held = dict(enumerate(held))

    tables = rotary_tables(length)
    bias = jnp.concatenate(
        [
            rank(qkv_bias, 1, core, width).astype(F32).reshape(1, 3 * width),
            rank(up_bias[None, :], 1, core, hidden).astype(F32),
        ],
        axis=1,
    )
    gain, shift = norm_gain.astype(F32)[None, :], norm_bias.astype(F32)[None, :]
    x_other = swap(x_own)
    columns.own_to(0)
    common = (rows.blocks(), bias, gain, shift, tables, width, tile)
    first = project(0, x_own, *common, (), [columns.held[0]])
    (x_other,) = columns.fenced([x_other], [first[0]])
    columns.own_to(1)
    qkv, act, slope, normed = project(1, x_other, *common, first, [columns.held[0]])
    held = columns.fenced(rows.blocks(), [qkv])
    columns.rest()
    row_blocks, row_others = held, [swap(a) for a in held[:3]]
    mixed, lse = attend(qkv, length, block, [columns.held[0]])
    row_others = columns.fenced(row_others, [mixed])
    row_blocks[3:] = fence(row_blocks[3:], [row_others[0]])
    row_others += [swap(a) for a in row_blocks[3:]]
    other_sums, own_sums = branch_sums(mixed, act, columns.blocks(), tile, [row_blocks[3]])
    other_sums, dy_own, *row_others[3:] = fence([other_sums, dy_own, *row_others[3:]], [own_sums])
    theirs = swap(other_sums)
    dy_other = swap(dy_own)

    grads = (slope, columns.blocks(), width, tile)
    gmixed, gpre_own, *grad_a = grad_in(0, dy_own, *grads, (), [own_sums])
    theirs, dy_other = fence([theirs, dy_other], [grad_a[0]])
    total = add_rows(own_sums, theirs)
    branches = line_scatter(total)
    gmixed, gpre_other, *grad_b = grad_in(1, dy_other, *grads, [gmixed], [total])
    (gpre_sent,) = fence([gpre_other])
    gpre_came = swap(gpre_sent)
    column_grads = BlockScatter(
        weight_grads(me, [[mixed], [act]], [dy_own, dy_other], ndp, [gpre_sent], left=False), ndp
    )
    (gpre_came,) = fence([gpre_came], [column_grads.held[0][0][0][0]])
    column_came = column_grads.send(0)
    back = lambda sequence, deps: attend_back(
        sequence, qkv, gmixed, mixed, lse, tables, length, block, deps
    )
    *other, qkv_sums_b = back(1, [gpre_came])
    came = [swap(a) for a in other]
    *own, qkv_sums_a = back(0, [other[0]])
    came = fence([*came, *column_came], [own[0]])
    column_came, came = came[3:], came[:3]
    column_grads.arrive(0, column_came)
    column_grads.between()
    all_grads = [*own, gpre_own, *came, gpre_came]

    def normed_half(half, deps, adds=()):
        return grad_normed_sums(
            half, all_grads, x_own, [*row_blocks, *row_others], tile, deps, adds
        )

    total_a, sums_a, *settled = normed_half(0, [], column_grads.adds(chip_steps - 1))
    column_grads.settle(chip_steps - 1, settled)
    half_a = line_scatter(total_a)
    column_came = column_grads.send(chip_steps - 1)
    up_grads = BlockScatter(
        weight_grads(me, [normed], [[gpre_own, gpre_sent]], ndp, [sums_a], left=True), ndp
    )
    c0, c1, branches, u0, u1 = fence(
        [*column_came, branches, *(up_grads.held[h][0][0][0] for h in range(2))]
    )
    up_grads.held[0][0], up_grads.held[1][0] = [(u0, 0)], [(u1, 0)]
    up_came = up_grads.send(0)
    column_grads.arrive(chip_steps - 1, [c0, c1])
    blocks, column_last = weight_grads(
        me,
        [normed],
        [[a, b] for a, b in zip(own, other)],
        ndp,
        [c0],
        True,
        [column_grads.adds(len(column_grads.plan[1]) - 1)[1]],
    )
    qkv_grads = BlockScatter(blocks, ndp)
    qkv_came = qkv_grads.send(0)
    column_theirs = swap(column_last[0])
    total_b, sums_b = normed_half(1, [qkv_grads.held[0][0][0][0]])
    half_b = line_scatter(total_b)
    u0, u1, q0, q1, half_a = fence([*up_came, *qkv_came, half_a], [sums_b, column_theirs])
    up_grads.arrive(0, [u0, u1])
    qkv_grads.arrive(0, [q0, q1])
    up_grads.between()
    qkv_grads.between()
    up_came, qkv_came = up_grads.send(chip_steps - 1), qkv_grads.send(chip_steps - 1)
    u0, u1, q0, q1, branches, sums_b, column_theirs = fence(
        [*up_came, *qkv_came, branches, sums_b, column_theirs]
    )
    up_grads.arrive(chip_steps - 1, [u0, u1])
    qkv_grads.arrive(chip_steps - 1, [q0, q1])
    up_theirs = swap(up_grads.last())
    qkv_theirs = swap(qkv_grads.last())
    qkv_sum = (qkv_sums_a + qkv_sums_b)[:, :3, :].transpose(1, 0, 2).reshape(3 * width)
    norm_sums = jnp.concatenate([sums_a[:2], sums_b[:2]], axis=1)
    small = jnp.concatenate(
        [
            norm_sums.reshape(2 * model),
            qkv_sum,
            grad_a[0][0] + grad_b[0][0],
            grad_a[1][0] + grad_b[1][0],
        ]
    )
    for bit in chip_bits(ndp):
        small = small + across(small, bit, ndp)
    small_other = swap(small)
    norm_sums = small[: 2 * model] + small_other[: 2 * model]
    norm_sums = [norm_sums] + [
        lax.ppermute(norm_sums, "mp", [(i, i ^ j) for i in range(nmp)]) for j in range(1, nmp)
    ]
    while len(norm_sums) > 1:
        norm_sums = [a + b for a, b in zip(norm_sums[::2], norm_sums[1::2])]
    norm_sums = norm_sums[0]

    output = (
        tokens.astype(F32)
        + branches.astype(F32)
        + (dense_bias.astype(F32) + down_bias.astype(F32))[None, :]
    ).astype(BF16)

    def both(mine, theirs, axis):
        return jnp.where(
            core == 0,
            jnp.concatenate([mine, theirs], axis=axis),
            jnp.concatenate([theirs, mine], axis=axis),
        )

    mine, theirs = column_grads.finish(column_theirs)
    owned_dense = both(mine[:width], theirs[:width], 0)
    owned_down = both(mine[width:], theirs[width:], 0)
    owned_up = both(*up_grads.finish(up_theirs), 1)
    mine, theirs = qkv_grads.finish(qkv_theirs)
    owned_qkv = jnp.stack(
        [
            both(mine[:, c * width : (c + 1) * width], theirs[:, c * width : (c + 1) * width], 1)
            for c in range(3)
        ]
    )

    inner = 3 * width + hidden
    grad_out_bias = small[2 * model + inner :]
    here, there = (a[2 * model : 2 * model + inner] for a in (small, small_other))
    even, odd = jnp.where(core == 0, here, there), jnp.where(core == 0, there, here)
    grad_qkv_bias = jnp.concatenate(
        [a[: 3 * width].reshape(3, width) for a in (even, odd)], axis=1
    )
    grad_up_bias = jnp.concatenate([even[3 * width :], odd[3 * width :]])

    grad_tokens = norm_back(tokens, cotangent, gain, [half_a, half_b], [qkv_theirs])
    return (
        output,
        grad_tokens,
        norm_sums[:model],
        norm_sums[model:],
        owned_qkv,
        grad_qkv_bias,
        owned_dense,
        grad_out_bias,
        owned_up,
        grad_up_bias,
        owned_down,
        grad_out_bias,
    )


def solution(mesh):
    return jax.shard_map(
        functools.partial(on_device, ndp=mesh.shape["dp"], nmp=mesh.shape["mp"]),
        mesh=mesh,
        in_specs=(
            P(("dp", "mp"), None),
            P(),
            P(),
            P(None, "dp", "mp"),
            P(None, "mp"),
            P("mp", "dp"),
            P(),
            P("dp", "mp"),
            P("mp"),
            P("mp", "dp"),
            P(),
            P(("dp", "mp"), None),
        ),
        out_specs=(
            P(("dp", "mp"), None),
            P(("dp", "mp"), None),
            P(),
            P(),
            P(None, "dp", "mp"),
            P(None, "mp"),
            P("mp", "dp"),
            P(),
            P("dp", "mp"),
            P("mp"),
            P("mp", "dp"),
            P(),
        ),
        check_vma=False,
    )
```

```python
import functools

import jax
import jax.numpy as jnp
import numpy as np
from jax import lax
from jax.experimental import pallas as pl
from jax.experimental.pallas import tpu as pltpu
from jax.sharding import PartitionSpec as P

HEAD_DIM = 64
ROT = 32
EPS = 1e-05
LANES = 128
F32 = jnp.float32
BF16 = jnp.bfloat16
HBM = pl.BlockSpec(memory_space=pltpu.HBM)


def dot(lhs, rhs, lhs_dim, rhs_dim):
    return lax.dot_general(
        lhs, rhs, (((lhs_dim,), (rhs_dim,)), ((), ())), preferred_element_type=F32
    )


def call(kernel, name, operands, deps=(), scalars=(), adds=(), vmem=64, **spec):
    deps, out_shape = tuple(deps), spec.pop("out_shape")
    single = not isinstance(out_shape, list)
    out_shape = [out_shape] if single else out_shape
    out_specs = spec.pop("out_specs")
    out_specs = [out_specs] if single else list(out_specs)
    extra, extra_specs, sizes = [], [], []
    steps = spec["grid"][0] if adds else 1
    for many, addends in adds:
        _, rows, columns = addends[0][0].shape
        block = (many, rows // steps, columns)
        for array, first in addends:
            extra.append(array)
            extra_specs.append(
                pl.BlockSpec(block, lambda i, *at, first=first, many=many: (first // many, i, 0))
            )
        out_shape = out_shape + [jax.ShapeDtypeStruct((many, rows, columns), BF16)]
        out_specs = out_specs + [pl.BlockSpec(block, lambda i, *at: (0, i, 0))]
        sizes.append(len(addends))
    lead, outs = len(scalars) + len(operands), len(out_shape) - len(adds)

    def body(*refs):
        first = lead + len(extra) + len(deps)
        kernel(*refs[:lead], *refs[first : first + outs], *refs[first + outs + len(adds) :])
        sources = refs[lead : lead + len(extra)]
        for n, out in zip(sizes, refs[first + outs : first + outs + len(adds)]):
            out[...] = sum(ref[...].astype(F32) for ref in sources[:n]).astype(BF16)
            sources = sources[n:]

    in_specs = list(spec.pop("in_specs")) + extra_specs + [HBM] * len(deps)
    aliases = spec.pop("input_output_aliases", {})
    if scalars:
        grid_spec = pltpu.PrefetchScalarGridSpec(
            num_scalar_prefetch=len(scalars), in_specs=in_specs, out_specs=out_specs, **spec
        )
        spec = {"grid_spec": grid_spec}
    else:
        spec.update(in_specs=in_specs, out_specs=out_specs)
    results = pl.pallas_call(
        body,
        out_shape=out_shape,
        input_output_aliases=aliases,
        compiler_params=pltpu.CompilerParams(vmem_limit_bytes=vmem << 20),
        cost_estimate=pl.CostEstimate(flops=0, transcendentals=0, bytes_accessed=0),
        name=name,
        **spec,
    )(*scalars, *operands, *extra, *deps)
    return results[0] if single and not adds else results


def fence(values, deps=()):
    return list(
        call(
            lambda *refs: None,
            "fence",
            values,
            deps,
            in_specs=[HBM] * len(values),
            out_specs=[HBM] * len(values),
            out_shape=[jax.ShapeDtypeStruct(v.shape, v.dtype) for v in values],
            input_output_aliases={n: n for n in range(len(values))},
        )
    )


def rotary_tables(length):
    positions = np.arange(length, dtype=np.float32)
    frequency = 10000.0 ** (-np.arange(ROT // 2, dtype=np.float64) * 2.0 / ROT)
    angles = positions[:, None] * frequency.astype(np.float32)[None, :]
    cosine, sine = np.cos(angles.astype(np.float64)), np.sin(angles.astype(np.float64))
    rest = HEAD_DIM - ROT
    none = np.zeros((length, ROT // 2))
    ones, zeros = np.ones((length, rest)), np.zeros((length, rest))
    straight = np.concatenate([cosine, cosine, ones], axis=1)
    left = np.concatenate([-sine, none, zeros], axis=1)
    right = np.concatenate([none, sine, zeros], axis=1)
    return [
        jnp.asarray(np.concatenate([t, t], axis=1).astype(np.float32))
        for t in (straight, left, right)
    ]


def rotated(u, straight, left, right, sign):
    half = ROT // 2
    turned = pltpu.roll(u, LANES - half, 1) * left + pltpu.roll(u, half, 1) * right
    return u * straight + sign * turned


def normalized(x):
    x = x.astype(F32)
    centered = x - jnp.mean(x, axis=1, keepdims=True)
    variance = jnp.mean(centered * centered, axis=1, keepdims=True)
    return centered * lax.rsqrt(variance + EPS)


def block_copies(blocks, place, sems):
    me = lax.axis_index("dp")
    return [
        pltpu.make_async_copy(block, place(lax.bitwise_xor(me, j)), sems.at[j])
        for j, block in enumerate(blocks)
    ]


def span(owner, size):
    return pl.ds(pl.multiple_of(owner * size, size), size)


def rows_at(ref, size):
    return lambda owner: ref.at[pl.ds(pl.multiple_of(owner * size, size), size)]


def columns_at(ref, size):
    return lambda owner: ref.at[:, pl.ds(pl.multiple_of(owner * size, size), size)]


def project_kernel(setup, x_ref, bias_ref, gain_ref, shift_ref, cos_ref, left_ref, right_ref, *rest):
    count, width, hidden = setup
    blocks = rest[:count]
    qkv_ref, act_ref, slope_ref, normed_ref, held, sems = rest[-6:]

    @pl.when(pl.program_id(0) == 0)
    def _():
        loads = block_copies(blocks, rows_at(held, blocks[0].shape[0]), sems)
        for copy in loads:
            copy.start()
        for copy in loads:
            copy.wait()

    x = (normalized(x_ref[...]) * gain_ref[...] + shift_ref[...]).astype(BF16)
    normed_ref[...] = x
    root = 0.7978845608028654
    for t in range((3 * width + hidden) // width):
        columns = slice(t * width, (t + 1) * width)
        y = dot(x, held[:, columns], 1, 0) + bias_ref[:, columns]
        if t < 3:
            for g in range(width // LANES):
                part = y[:, g * LANES : (g + 1) * LANES]
                if t < 2:
                    part = rotated(part, cos_ref[...], left_ref[...], right_ref[...], 1.0)
                if t == 0:
                    part = part * HEAD_DIM**-0.5
                start = t * width + g * LANES
                qkv_ref[:, start : start + LANES] = part.astype(BF16)
        else:
            columns = slice((t - 3) * width, (t - 2) * width)
            square = y * y
            turn = jnp.tanh(root * y * (1.0 + 0.044715 * square))
            half = 0.5 * (1.0 + turn)
            act_ref[:, columns] = (y * half).astype(BF16)
            slope = half * (1.0 + y * (1.0 - turn) * (root + (3.0 * 0.044715 * root) * square))
            slope_ref[:, columns] = slope.astype(BF16)


def project(sequence, x, blocks, bias, gain, shift, tables, width, tile, earlier, deps):
    (length, model), total, count = x.shape, blocks[0].shape[1], len(blocks)
    hidden, steps = total - 3 * width, length // tile
    rows = lambda w: pl.BlockSpec((tile, w), lambda i: (i, 0))
    out = lambda w: pl.BlockSpec((tile, w), lambda i: (sequence * steps + i, 0))
    line = lambda a: pl.BlockSpec(a.shape, lambda i: (0, 0))
    widths = (3 * width, hidden, hidden, model)
    operands = [x, bias, gain, shift, *tables, *blocks]
    return call(
        functools.partial(project_kernel, (count, width, hidden)),
        "project",
        operands + list(earlier),
        deps,
        grid=(steps,),
        in_specs=[rows(model), line(bias), line(gain), line(shift)]
        + [rows(LANES)] * 3
        + [HBM] * (count + len(earlier)),
        out_specs=[out(w) for w in widths],
        out_shape=[jax.ShapeDtypeStruct((2 * length, w), BF16) for w in widths],
        input_output_aliases={len(operands) + n: n for n in range(len(earlier))},
        scratch_shapes=[pltpu.VMEM((model, total), BF16), pltpu.SemaphoreType.DMA((count,))],
    )


def attend_kernel(block, q_ref, k_ref, v_ref, out_ref, lse_ref):
    length = q_ref.shape[0]
    lane = lax.broadcasted_iota(jnp.int32, (1, LANES), 1)
    key = lax.broadcasted_iota(jnp.int32, (block, block), 0)
    causal = key <= lax.broadcasted_iota(jnp.int32, (block, block), 1)
    for i in range(length // block):
        rows, before = pl.ds(i * block, block), pl.ds(0, i * block)
        results = []
        for h in range(2):
            mine = (lane < HEAD_DIM) if h == 0 else (lane >= HEAD_DIM)
            query = jnp.where(mine, q_ref[rows, :], 0)
            near = jnp.where(causal, dot(k_ref[rows, :], query, 1, 1), -1e30)
            highest = jnp.max(near, axis=0, keepdims=True)
            if i:
                far = dot(k_ref[before, :], query, 1, 1)
                highest = jnp.maximum(highest, jnp.max(far, axis=0, keepdims=True))
            near = jnp.exp(near - highest)
            total = jnp.sum(near, axis=0, keepdims=True)
            if i:
                far = jnp.exp(far - highest)
                total = total + jnp.sum(far, axis=0, keepdims=True)
            inverse = 1.0 / total
            result = dot((near * inverse).astype(BF16), v_ref[rows, :], 0, 0)
            if i:
                result = result + dot((far * inverse).astype(BF16), v_ref[before, :], 0, 0)
            results.append(result)
            lse_ref[0, h : h + 1, rows] = highest + jnp.log(total)
        out_ref[rows, :] = jnp.where(lane < HEAD_DIM, results[0], results[1]).astype(BF16)


def pair_specs(length, pairs):
    return lambda off: pl.BlockSpec(
        (length, LANES), lambda g: (g // pairs, off * pairs + g % pairs)
    )


def attend(qkv, length, block, deps):
    width, sequences = qkv.shape[1] // 3, qkv.shape[0] // length
    pairs = width // LANES
    at = pair_specs(length, pairs)
    return call(
        functools.partial(attend_kernel, block),
        "attend",
        [qkv, qkv, qkv],
        deps,
        grid=(sequences * pairs,),
        in_specs=[at(0), at(1), at(2)],
        out_specs=[at(0), pl.BlockSpec((1, 8, length), lambda g: (g, 0, 0))],
        out_shape=[
            jax.ShapeDtypeStruct((qkv.shape[0], width), BF16),
            jax.ShapeDtypeStruct((sequences * pairs, 8, length), F32),
        ],
    )


def attend_back_kernel(
    block,
    q_ref,
    k_ref,
    v_ref,
    grad_ref,
    mixed_ref,
    lse_ref,
    cos_ref,
    left_ref,
    right_ref,
    gq_ref,
    gk_ref,
    gv_ref,
    sum_ref,
    gk_sum,
    gv_sum,
):
    length = q_ref.shape[0]
    lane = lax.broadcasted_iota(jnp.int32, (1, LANES), 1)
    key = lax.broadcasted_iota(jnp.int32, (block, block), 0)
    causal = key <= lax.broadcasted_iota(jnp.int32, (block, block), 1)
    count = length // block
    sum_ref[...] = jnp.zeros_like(sum_ref)

    def put(ref, which, rows, value):
        value = value.astype(BF16)
        ref[rows, :] = value
        sum_ref[0, which : which + 1, :] += jnp.sum(value.astype(F32), axis=0, keepdims=True)

    def unrotated(value, rows):
        return rotated(value, cos_ref[rows, :], left_ref[rows, :], right_ref[rows, :], -1.0)

    for i in reversed(range(count)):
        rows = pl.ds(i * block, block)
        product = grad_ref[rows, :].astype(F32) * mixed_ref[rows, :].astype(F32)
        gq = None
        for h in range(2):
            mine = (lane < HEAD_DIM) if h == 0 else (lane >= HEAD_DIM)
            query = jnp.where(mine, q_ref[rows, :], 0)
            grad = jnp.where(mine, grad_ref[rows, :], 0)
            ones = jnp.where(mine, jnp.ones((8, LANES), F32), 0.0)
            delta = lax.dot_general(
                ones,
                product,
                (((1,), (1,)), ((), ())),
                precision=lax.Precision.HIGHEST,
                preferred_element_type=F32,
            )[0:1, :]
            lse = lse_ref[0, h : h + 1, rows]
            for j in range(i + 1):
                keys = pl.ds(j * block, block)
                key_rows = k_ref[keys, :]
                probs = jnp.exp(dot(key_rows, query, 1, 1) - lse)
                if j == i:
                    probs = jnp.where(causal, probs, 0.0)
                gprobs = dot(v_ref[keys, :], grad, 1, 1)
                gscores = (probs * (gprobs - delta)).astype(BF16)
                gv, gk = dot(probs.astype(BF16), grad, 1, 0), dot(gscores, query, 1, 0)
                if i == count - 1 and h == 0:
                    gv_sum[keys, :] = gv
                    gk_sum[keys, :] = gk
                else:
                    gv_sum[keys, :] += gv
                    gk_sum[keys, :] += gk
                part = dot(gscores, jnp.where(mine, key_rows, 0), 0, 0)
                gq = part if gq is None else gq + part
        put(gq_ref, 0, rows, unrotated(gq * HEAD_DIM**-0.5, rows))
    for i in range(count):
        rows = pl.ds(i * block, block)
        put(gk_ref, 1, rows, unrotated(gk_sum[rows, :], rows))
        put(gv_ref, 2, rows, gv_sum[rows, :])


def attend_back(sequence, qkv, grad, mixed, lse, tables, length, block, deps):
    width = qkv.shape[1] // 3
    pairs = width // LANES
    at = lambda off: pl.BlockSpec((length, LANES), lambda g: (sequence, off * pairs + g))
    out = pl.BlockSpec((length, LANES), lambda g: (0, g))
    table = pl.BlockSpec((length, LANES), lambda g: (0, 0))
    small = pl.BlockSpec((1, 8, length), lambda g: (sequence * pairs + g, 0, 0))
    return call(
        functools.partial(attend_back_kernel, block),
        "attend_back",
        [qkv, qkv, qkv, grad, mixed, lse, *tables],
        deps,
        grid=(pairs,),
        in_specs=[at(0), at(1), at(2), at(0), at(0), small, table, table, table],
        out_specs=[out] * 3 + [pl.BlockSpec((1, 8, LANES), lambda g: (g, 0, 0))],
        out_shape=[jax.ShapeDtypeStruct((length, width), BF16)] * 3
        + [jax.ShapeDtypeStruct((pairs, 8, LANES), F32)],
        scratch_shapes=[pltpu.VMEM((length, LANES), F32)] * 2,
    )


def by_sequence(tile, width, steps):
    return [
        pl.BlockSpec((tile, width), lambda i: (jnp.minimum(i, steps - 1), 0)),
        pl.BlockSpec((tile, width), lambda i: (jnp.maximum(i - steps, 0), 0)),
    ]


def other_first(tile, width, steps):
    return pl.BlockSpec((tile, width), lambda i: ((i + steps) % (2 * steps), 0))


def put_by_sequence(step, steps, value, other_ref, own_ref):
    @pl.when(step < steps)
    def _():
        other_ref[...] = value

    @pl.when(step >= steps)
    def _():
        own_ref[...] = value


def branch_kernel(count, steps, mixed_ref, act_ref, *rest):
    blocks, (other_ref, own_ref, held, sems) = rest[:count], rest[count:]
    step = pl.program_id(0)

    @pl.when(step == 0)
    def _():
        loads = block_copies(blocks, columns_at(held, blocks[0].shape[1]), sems)
        for copy in loads:
            copy.start()
        for copy in loads:
            copy.wait()

    x = jnp.concatenate([mixed_ref[...], act_ref[...]], axis=1)
    put_by_sequence(step, steps, dot(x, held[...], 1, 0).astype(BF16), other_ref, own_ref)


def branch_sums(mixed, act, blocks, tile, deps):
    length, count = mixed.shape[0] // 2, len(blocks)
    inner, model, steps = blocks[0].shape[0], count * blocks[0].shape[1], length // tile
    return call(
        functools.partial(branch_kernel, count, steps),
        "branch_sums",
        [mixed, act, *blocks],
        deps,
        grid=(2 * steps,),
        in_specs=[other_first(tile, a.shape[1], steps) for a in (mixed, act)] + [HBM] * count,
        out_specs=by_sequence(tile, model, steps),
        out_shape=[jax.ShapeDtypeStruct((length, model), BF16)] * 2,
        scratch_shapes=[pltpu.VMEM((inner, model), BF16), pltpu.SemaphoreType.DMA((count,))],
    )


def grad_in_kernel(setup, dy_ref, slope_ref, *rest):
    count, width, hidden = setup
    blocks = rest[:count]
    gmixed_ref, gpre_ref, gsum_ref, dsum_ref, held, sems = rest[-6:]

    @pl.when(pl.program_id(0) == 0)
    def _():
        loads = block_copies(blocks, columns_at(held, blocks[0].shape[1]), sems)
        for copy in loads:
            copy.start()
        gsum_ref[...] = jnp.zeros_like(gsum_ref)
        dsum_ref[...] = jnp.zeros_like(dsum_ref)
        for copy in loads:
            copy.wait()

    dy = dy_ref[...]
    gmixed_ref[...] = dot(dy, held[:width, :], 1, 1).astype(BF16)
    for start in range(0, hidden, width):
        part = slice(start, start + width)
        gact = dot(dy, held[width + start : 2 * width + start, :], 1, 1)
        gpre = (gact * slope_ref[:, part].astype(F32)).astype(BF16)
        gpre_ref[:, part] = gpre
        gsum_ref[0:1, part] += jnp.sum(gpre.astype(F32), axis=0, keepdims=True)
    dsum_ref[0:1, :] += jnp.sum(dy.astype(F32), axis=0, keepdims=True)


def grad_in(sequence, dy, slope, blocks, width, tile, earlier, deps):
    (length, model), hidden, count = dy.shape, slope.shape[1], len(blocks)
    steps = length // tile
    at = lambda w: pl.BlockSpec((tile, w), lambda i: (sequence * steps + i, 0))
    total = lambda w: pl.BlockSpec((8, w), lambda i: (0, 0))
    operands = [dy, slope, *blocks]
    return call(
        functools.partial(grad_in_kernel, (count, width, hidden)),
        "grad_in",
        operands + list(earlier),
        deps,
        grid=(steps,),
        in_specs=[pl.BlockSpec((tile, model), lambda i: (i, 0)), at(hidden)]
        + [HBM] * (count + len(earlier)),
        out_specs=[
            at(width),
            pl.BlockSpec((tile, hidden), lambda i: (i, 0)),
            total(hidden),
            total(model),
        ],
        out_shape=[
            jax.ShapeDtypeStruct((2 * length, width), BF16),
            jax.ShapeDtypeStruct((length, hidden), BF16),
            jax.ShapeDtypeStruct((8, hidden), F32),
            jax.ShapeDtypeStruct((8, model), F32),
        ],
        input_output_aliases={len(operands) + n: n for n in range(len(earlier))},
        scratch_shapes=[
            pltpu.VMEM((width + hidden, model), BF16),
            pltpu.SemaphoreType.DMA((count,)),
        ],
    )


def add_kernel(a_ref, b_ref, out_ref):
    out_ref[...] = (a_ref[...].astype(F32) + b_ref[...].astype(F32)).astype(BF16)


def add_rows(a, b):
    rows = pl.BlockSpec((a.shape[0] // 8, a.shape[1]), lambda i: (i, 0))
    return call(
        add_kernel,
        "add_rows",
        [a, b],
        grid=(8,),
        in_specs=[rows, rows],
        out_specs=rows,
        out_shape=jax.ShapeDtypeStruct(a.shape, BF16),
    )


def grad_normed_kernel(count, half, x_ref, *rest):
    grads, blocks, (out_ref, sum_ref, held, sems) = rest[:8], rest[8 : 8 + 2 * count], rest[-4:]
    (size, total), few, me = blocks[0].shape, count // 2, lax.axis_index("dp")

    @pl.when(pl.program_id(0) == 0)
    def _():
        for start in (True, False):
            for n, block in enumerate(blocks):
                core, j = n // count, n % count
                owner = lax.bitwise_xor(me, j ^ core) - half * few
                columns = slice(core * total, (core + 1) * total)

                @pl.when((owner >= 0) & (owner < few))
                def _(start=start, n=n, block=block, owner=owner, columns=columns):
                    target = held.at[span(owner, size), columns]
                    copy = pltpu.make_async_copy(block, target, sems.at[n])
                    if start:
                        copy.start()
                    else:
                        copy.wait()

        sum_ref[...] = jnp.zeros_like(sum_ref)

    columns = slice(half * few * size, (half + 1) * few * size)
    normal = normalized(x_ref[...])[:, columns]
    g = jnp.concatenate([ref[...] for ref in grads], axis=1)
    result = dot(g, held[...], 1, 1)
    sum_ref[0:1, :] += jnp.sum(result * normal, axis=0, keepdims=True)
    sum_ref[1:2, :] += jnp.sum(result, axis=0, keepdims=True)
    out_ref[...] = result.astype(BF16)


def grad_normed_sums(half, grads, x, blocks, tile, deps, adds=()):
    (length, model), count, total = x.shape, len(blocks) // 2, blocks[0].shape[1]
    part = model // 2
    rows = lambda w: pl.BlockSpec((tile, w), lambda i: (i, 0))
    return call(
        functools.partial(grad_normed_kernel, count, half),
        "grad_normed_sums",
        [x, *grads, *blocks],
        deps,
        adds=adds,
        grid=(length // tile,),
        in_specs=[rows(model)] + [rows(g.shape[1]) for g in grads] + [HBM] * (2 * count),
        out_specs=[rows(part), pl.BlockSpec((8, part), lambda i: (0, 0))],
        out_shape=[
            jax.ShapeDtypeStruct((length, part), BF16),
            jax.ShapeDtypeStruct((8, part), F32),
        ],
        scratch_shapes=[
            pltpu.VMEM((part, 2 * total), BF16),
            pltpu.SemaphoreType.DMA((2 * count,)),
        ],
    )


def weight_grad_kernel(writes, left, rows, many, groups, at_ref, *refs):
    cuts, (*refs, held, grad, sems) = refs[:many], refs[many:]
    whole, outs = refs[: len(refs) - len(writes)], refs[len(refs) - len(writes) :]
    step, core, loads, first = pl.program_id(0), lax.rem(lax.axis_index("dp"), 2), [], 0
    for group in groups:
        below = 0
        for ref in whole[:group]:
            columns = pl.ds(first, ref.shape[1])
            for start in range(0, ref.shape[0], rows):
                target = held.at[pl.ds(below + start, rows), columns]
                loads.append((ref.at[pl.ds(start, rows)], target))
            below += ref.shape[0]
        first += whole[0].shape[1]
        whole = whole[group:]
    loads = [pltpu.make_async_copy(*pair, sems.at[n]) for n, pair in enumerate(loads)]

    @pl.when(step == 0)
    def _():
        for copy in loads:
            copy.start()
        for copy in loads:
            copy.wait()

    cut = jnp.concatenate([ref[...] for ref in cuts], axis=0)
    pair = (cut, held[...]) if left else (held[...], cut)
    grad[...] = dot(*pair, 0, 0).astype(BF16)
    size = cut.shape[1] // 2
    for half, steps, out_ref in writes_of(writes, outs):
        here = functools.reduce(jnp.logical_or, [step == s for s in steps])

        @pl.when(here)
        def _(half=half, out_ref=out_ref):
            mine = span(core if half == 0 else 1 - core, size)
            out_ref[0] = grad[mine, :] if left else grad[:, mine]


def writes_of(writes, outs):
    return [(half, steps, out) for (half, steps), out in zip(writes, outs)]


def weight_grads(me, xs, gs, count, deps, left, adds=()):
    plan, chips = scatter_plan(count), count // 2
    order = [j // 2 for s in plan[0] for j in s]
    sets = [(half, s) for s in range(len(plan[0])) for half in range(2)]
    writes = [(half, [order.index(j // 2) for j in plan[half][s]]) for half, s in sets]
    table = []
    for _, steps in writes:
        for i in range(chips):
            later = [w for w in steps if w >= i]
            table.append(steps.index(min(later) if later else max(steps)))
    owners = lax.bitwise_xor(me // 2, jnp.array(order, jnp.int32))
    at = jnp.concatenate([owners, jnp.array(table, jnp.int32)])
    cut, whole = (xs, gs) if left else (gs, xs)
    groups, length = [len(g) for g in whole], sum(a.shape[0] for a in whole[0])
    size, full = cut[0].shape[1] // count, sum(g[0].shape[1] for g in whole)
    shape, whole = (size, full) if left else (full, size), [a for g in whole for a in g]
    rows = length // 4
    pieces = 4 * len(groups)

    def out(n):
        return pl.BlockSpec((1, *shape), lambda i, at: (at[chips * (n + 1) + i], 0, 0))

    outs = call(
        functools.partial(weight_grad_kernel, writes, left, rows, len(cut), groups),
        "weight_grads",
        [*cut, *whole],
        deps,
        (at,),
        adds,
        grid=(chips,),
        in_specs=[pl.BlockSpec((a.shape[0], 2 * size), lambda i, at: (0, at[i])) for a in cut]
        + [HBM] * len(whole),
        out_specs=[out(n) for n in range(len(sets))],
        out_shape=[
            jax.ShapeDtypeStruct((len(plan[half][s]), *shape), BF16) for half, s in sets
        ],
        scratch_shapes=[
            pltpu.VMEM((length, full), BF16),
            pltpu.VMEM((2 * size, full) if left else (full, 2 * size), BF16),
            pltpu.SemaphoreType.DMA((pieces,)),
        ],
    )
    blocks = [[o for o, (half, _) in zip(outs, sets) if half == h] for h in range(2)]
    return (blocks, *outs[len(sets) :]) if adds else blocks


def norm_back_kernel(tokens_ref, dy_ref, gain_ref, left_ref, right_ref, out_ref):
    x = tokens_ref[...].astype(F32)
    centered = x - jnp.mean(x, axis=1, keepdims=True)
    inverse_std = lax.rsqrt(jnp.mean(centered * centered, axis=1, keepdims=True) + EPS)
    normal = centered * inverse_std
    grad = jnp.concatenate([left_ref[...], right_ref[...]], axis=1).astype(F32)
    scaled = grad * gain_ref[...]
    first_mean = jnp.mean(scaled, axis=1, keepdims=True)
    second_mean = jnp.mean(scaled * normal, axis=1, keepdims=True)
    back = (scaled - first_mean - normal * second_mean) * inverse_std
    out_ref[...] = (dy_ref[...].astype(F32) + back).astype(BF16)


def norm_back(tokens, dy, gain, halves, deps):
    rows, model = tokens.shape
    tile = min(64, rows)
    part = lambda w: pl.BlockSpec((tile, w), lambda i: (i, 0))
    return call(
        norm_back_kernel,
        "norm_back",
        [tokens, dy, gain, *halves],
        deps,
        grid=(rows // tile,),
        in_specs=[part(model), part(model), pl.BlockSpec((1, model), lambda i: (0, 0))]
        + [part(model // 2)] * 2,
        out_specs=part(model),
        out_shape=jax.ShapeDtypeStruct((rows, model), BF16),
    )


def across(value, bit, count):
    return lax.ppermute(value, "dp", [(i, i ^ bit) for i in range(count)])


def added(addends):
    return sum(a.astype(F32) for a in addends).astype(BF16)


def pair_sum(parts):
    while len(parts) > 1:
        parts = [a + b for a, b in zip(parts[::2], parts[1::2])]
    return parts[0]


def chip_bits(count):
    bits, bit = [], 2
    while bit < count:
        bits.append(bit)
        bit *= 2
    return bits


class BlockGather:
    def __init__(self, own, sibling, count):
        self.held, self.count = {0: own, 1: sibling}, count
        self.orders = (chip_bits(count), chip_bits(count)[::-1])

    def own_to(self, s):
        if s < len(self.orders[0]):
            for half in range(2):
                bit = self.orders[half][s]
                self.held[half ^ bit] = across(self.held[half], bit, self.count)

    def rest(self):
        for s in range(1, len(self.orders[0])):
            for half in range(2):
                order = self.orders[half]
                for j in [j for j in self.held if j % 2 == half]:
                    if j ^ order[s] not in self.held and not any(j & b for b in order[s:]):
                        self.held[j ^ order[s]] = across(self.held[j], order[s], self.count)

    def fenced(self, others=(), deps=()):
        keys = sorted(self.held)
        values = fence([self.held[j] for j in keys] + list(others), deps)
        self.held = dict(zip(keys, values))
        return values[len(keys) :]

    def blocks(self):
        return [self.held[j] for j in range(self.count)]


def scatter_orders(count):
    return (chip_bits(count)[::-1], chip_bits(count))


def scatter_plan(count):
    plan = []
    for half, order in enumerate(scatter_orders(count)):
        sets, rest = [[half]], [half]
        for bit in reversed(order):
            sets.insert(0, [j ^ bit for j in rest])
            rest = sets[0] + rest
        plan.append(sets)
    return plan


class BlockScatter:
    def __init__(self, halves, count):
        self.count, self.orders, self.plan = count, scatter_orders(count), scatter_plan(count)
        self.held = [[[(a, 0)] for a in arrays] for arrays in halves]
        self.steps = len(self.orders[0])

    def parts(self, half, s):
        many = len(self.plan[half][s])
        return [a[first : first + many] for a, first in self.held[half][s]]

    def total(self, half, s):
        if len(self.held[half][s]) > 1:
            self.held[half][s] = [(added(self.parts(half, s)), 0)]
        return self.parts(half, s)[0]

    def ready(self, s):
        return [self.total(half, s) for half in range(2)]

    def adds(self, s):
        return [(len(self.plan[half][s]), self.held[half][s]) for half in range(2)]

    def settle(self, s, sums):
        for half in range(2):
            self.held[half][s] = [(sums[half], 0)]

    def send(self, s):
        return [across(self.total(h, s), self.orders[h][s], self.count) for h in range(2)]

    def arrive(self, s, came):
        for half in range(2):
            first = 0
            for t in range(s + 1, len(self.plan[half])):
                self.held[half][t].append((came[half], first))
                first += len(self.plan[half][t])

    def between(self):
        for s in range(1, self.steps - 1):
            self.arrive(s, self.send(s))

    def last(self):
        return self.total(1, -1)[0]

    def finish(self, theirs):
        return sum(a[0].astype(F32) for a in self.parts(0, -1)), theirs.astype(F32)


def on_device(
    tokens,
    norm_gain,
    norm_bias,
    qkv_weight,
    qkv_bias,
    dense_weight,
    dense_bias,
    up_weight,
    up_bias,
    down_weight,
    down_bias,
    cotangent,
    *,
    ndp,
    nmp,
):
    me = lax.axis_index("dp")
    core = me % 2
    length, model = tokens.shape[0] * nmp, tokens.shape[1]
    tile, block = min(256, length), min(512, length)
    width, hidden = qkv_weight.shape[2] // 2, up_weight.shape[1] // 2
    chip_steps = len(chip_bits(ndp))
    rank = lambda array, axis, which, size: lax.dynamic_slice_in_dim(
        array, which * size, size, axis
    )

    def row_pack(which):
        qkv = rank(qkv_weight, 2, which, width)
        return jnp.concatenate([qkv[0], qkv[1], qkv[2], rank(up_weight, 1, which, hidden)], axis=1)

    def column_pack(which):
        return jnp.concatenate(
            [rank(dense_weight, 0, which, width), rank(down_weight, 0, which, hidden)], axis=0
        )

    pairs = width // LANES
    swap = lambda array: across(array, 1, ndp)
    line_gather = lambda array: lax.all_gather(array, "mp", axis=0, tiled=True)
    line_scatter = lambda array: lax.psum_scatter(array, "mp", scatter_dimension=0, tiled=True)
    x_own, dy_own = line_gather(tokens), line_gather(cotangent)
    rows = BlockGather(row_pack(core), swap(row_pack(1 - core)), ndp)
    columns = BlockGather(column_pack(core), swap(column_pack(1 - core)), ndp)
    rows.own_to(0)
    rows.fenced(deps=columns.held.values())
    rows.own_to(1)
    rows.fenced()
    rows.rest()
    x_own, *held = fence([x_own, columns.held[0], columns.held[1]], rows.blocks())
    columns.held = dict(enumerate(held))

    tables = rotary_tables(length)
    bias = jnp.concatenate(
        [
            rank(qkv_bias, 1, core, width).astype(F32).reshape(1, 3 * width),
            rank(up_bias[None, :], 1, core, hidden).astype(F32),
        ],
        axis=1,
    )
    gain, shift = norm_gain.astype(F32)[None, :], norm_bias.astype(F32)[None, :]
    x_other = swap(x_own)
    columns.own_to(0)
    common = (rows.blocks(), bias, gain, shift, tables, width, tile)
    first = project(0, x_own, *common, (), [columns.held[0]])
    (x_other,) = columns.fenced([x_other], [first[0]])
    columns.own_to(1)
    qkv, act, slope, normed = project(1, x_other, *common, first, [columns.held[0]])
    held = columns.fenced(rows.blocks(), [qkv])
    columns.rest()
    row_blocks, row_others = held, [swap(a) for a in held[:3]]
    mixed, lse = attend(qkv, length, block, [columns.held[0]])
    row_others = columns.fenced(row_others, [mixed])
    row_blocks[3:] = fence(row_blocks[3:], [row_others[0]])
    row_others += [swap(a) for a in row_blocks[3:]]
    other_sums, own_sums = branch_sums(mixed, act, columns.blocks(), tile, [row_blocks[3]])
    other_sums, dy_own, *row_others[3:] = fence([other_sums, dy_own, *row_others[3:]], [own_sums])
    theirs = swap(other_sums)
    dy_other = swap(dy_own)

    grads = (slope, columns.blocks(), width, tile)
    gmixed, gpre_own, *grad_a = grad_in(0, dy_own, *grads, (), [own_sums])
    theirs, dy_other = fence([theirs, dy_other], [grad_a[0]])
    total = add_rows(own_sums, theirs)
    branches = line_scatter(total)
    gmixed, gpre_other, *grad_b = grad_in(1, dy_other, *grads, [gmixed], [total])
    (gpre_sent,) = fence([gpre_other])
    gpre_came = swap(gpre_sent)
    column_grads = BlockScatter(
        weight_grads(me, [[mixed], [act]], [dy_own, dy_other], ndp, [gpre_sent], left=False), ndp
    )
    (gpre_came,) = fence([gpre_came], [column_grads.held[0][0][0][0]])
    column_came = column_grads.send(0)
    back = lambda sequence, deps: attend_back(
        sequence, qkv, gmixed, mixed, lse, tables, length, block, deps
    )
    *other, qkv_sums_b = back(1, [gpre_came])
    came = [swap(a) for a in other]
    *own, qkv_sums_a = back(0, [other[0]])
    came = fence([*came, *column_came], [own[0]])
    column_came, came = came[3:], came[:3]
    column_grads.arrive(0, column_came)
    column_grads.between()
    all_grads = [*own, gpre_own, *came, gpre_came]

    def normed_half(half, deps, adds=()):
        return grad_normed_sums(
            half, all_grads, x_own, [*row_blocks, *row_others], tile, deps, adds
        )

    total_a, sums_a, *settled = normed_half(0, [], column_grads.adds(chip_steps - 1))
    column_grads.settle(chip_steps - 1, settled)
    half_a = line_scatter(total_a)
    column_came = column_grads.send(chip_steps - 1)
    up_grads = BlockScatter(
        weight_grads(me, [normed], [[gpre_own, gpre_sent]], ndp, [sums_a], left=True), ndp
    )
    c0, c1, branches, u0, u1 = fence(
        [*column_came, branches, *(up_grads.held[h][0][0][0] for h in range(2))]
    )
    up_grads.held[0][0], up_grads.held[1][0] = [(u0, 0)], [(u1, 0)]
    up_came = up_grads.send(0)
    column_grads.arrive(chip_steps - 1, [c0, c1])
    blocks, column_last = weight_grads(
        me,
        [normed],
        [[a, b] for a, b in zip(own, other)],
        ndp,
        [c0],
        True,
        [column_grads.adds(len(column_grads.plan[1]) - 1)[1]],
    )
    qkv_grads = BlockScatter(blocks, ndp)
    qkv_came = qkv_grads.send(0)
    column_theirs = swap(column_last[0])
    total_b, sums_b = normed_half(1, [qkv_grads.held[0][0][0][0]])
    half_b = line_scatter(total_b)
    u0, u1, q0, q1, half_a = fence([*up_came, *qkv_came, half_a], [sums_b, column_theirs])
    up_grads.arrive(0, [u0, u1])
    qkv_grads.arrive(0, [q0, q1])
    up_grads.between()
    qkv_grads.between()
    up_came, qkv_came = up_grads.send(chip_steps - 1), qkv_grads.send(chip_steps - 1)
    u0, u1, q0, q1, branches, sums_b, column_theirs = fence(
        [*up_came, *qkv_came, branches, sums_b, column_theirs]
    )
    up_grads.arrive(chip_steps - 1, [u0, u1])
    qkv_grads.arrive(chip_steps - 1, [q0, q1])
    up_theirs = swap(up_grads.last())
    qkv_theirs = swap(qkv_grads.last())
    qkv_sum = (qkv_sums_a + qkv_sums_b)[:, :3, :].transpose(1, 0, 2).reshape(3 * width)
    norm_sums = jnp.concatenate([sums_a[:2], sums_b[:2]], axis=1)
    small = jnp.concatenate(
        [
            norm_sums.reshape(2 * model),
            qkv_sum,
            grad_a[0][0] + grad_b[0][0],
            grad_a[1][0] + grad_b[1][0],
        ]
    )
    small = pair_sum([small] + [across(small, j, ndp) for j in range(2, ndp, 2)])
    small_other = swap(small)
    grad_tokens = norm_back(tokens, cotangent, gain, [half_a, half_b], [small_other])
    (norm_sums,) = fence([small[: 2 * model] + small_other[: 2 * model]], [grad_tokens])
    norm_sums = [norm_sums] + [
        lax.ppermute(norm_sums, "mp", [(i, i ^ j) for i in range(nmp)]) for j in range(1, nmp)
    ]
    while len(norm_sums) > 1:
        norm_sums = [a + b for a, b in zip(norm_sums[::2], norm_sums[1::2])]
    norm_sums = norm_sums[0]

    output = (
        tokens.astype(F32)
        + branches.astype(F32)
        + (dense_bias.astype(F32) + down_bias.astype(F32))[None, :]
    ).astype(BF16)

    def both(mine, theirs, axis):
        return jnp.where(
            core == 0,
            jnp.concatenate([mine, theirs], axis=axis),
            jnp.concatenate([theirs, mine], axis=axis),
        )

    mine, theirs = column_grads.finish(column_theirs)
    owned_dense = both(mine[:width], theirs[:width], 0)
    owned_down = both(mine[width:], theirs[width:], 0)
    owned_up = both(*up_grads.finish(up_theirs), 1)
    mine, theirs = qkv_grads.finish(qkv_theirs)
    owned_qkv = jnp.stack(
        [
            both(mine[:, c * width : (c + 1) * width], theirs[:, c * width : (c + 1) * width], 1)
            for c in range(3)
        ]
    )

    inner = 3 * width + hidden
    grad_out_bias = small[2 * model + inner :]
    here, there = (a[2 * model : 2 * model + inner] for a in (small, small_other))
    even, odd = jnp.where(core == 0, here, there), jnp.where(core == 0, there, here)
    grad_qkv_bias = jnp.concatenate(
        [a[: 3 * width].reshape(3, width) for a in (even, odd)], axis=1
    )
    grad_up_bias = jnp.concatenate([even[3 * width :], odd[3 * width :]])

    return (
        output,
        grad_tokens,
        norm_sums[:model],
        norm_sums[model:],
        owned_qkv,
        grad_qkv_bias,
        owned_dense,
        grad_out_bias,
        owned_up,
        grad_up_bias,
        owned_down,
        grad_out_bias,
    )


def solution(mesh):
    return jax.shard_map(
        functools.partial(on_device, ndp=mesh.shape["dp"], nmp=mesh.shape["mp"]),
        mesh=mesh,
        in_specs=(
            P(("dp", "mp"), None),
            P(),
            P(),
            P(None, "dp", "mp"),
            P(None, "mp"),
            P("mp", "dp"),
            P(),
            P("dp", "mp"),
            P("mp"),
            P("mp", "dp"),
            P(),
            P(("dp", "mp"), None),
        ),
        out_specs=(
            P(("dp", "mp"), None),
            P(("dp", "mp"), None),
            P(),
            P(),
            P(None, "dp", "mp"),
            P(None, "mp"),
            P("mp", "dp"),
            P(),
            P("dp", "mp"),
            P("mp"),
            P("mp", "dp"),
            P(),
        ),
        check_vma=False,
    )
```

```python
import functools

import jax
import jax.numpy as jnp
import numpy as np
from jax import lax
from jax.experimental import pallas as pl
from jax.experimental.pallas import tpu as pltpu
from jax.sharding import PartitionSpec as P

HEAD_DIM = 64
ROT = 32
EPS = 1e-05
LANES = 128
F32 = jnp.float32
BF16 = jnp.bfloat16
HBM = pl.BlockSpec(memory_space=pltpu.HBM)


def dot(lhs, rhs, lhs_dim, rhs_dim):
    return lax.dot_general(
        lhs, rhs, (((lhs_dim,), (rhs_dim,)), ((), ())), preferred_element_type=F32
    )


def call(kernel, name, operands, deps=(), scalars=(), adds=(), vmem=64, **spec):
    deps, out_shape = tuple(deps), spec.pop("out_shape")
    single = not isinstance(out_shape, list)
    out_shape = [out_shape] if single else out_shape
    out_specs = spec.pop("out_specs")
    out_specs = [out_specs] if single else list(out_specs)
    extra, extra_specs, sizes = [], [], []
    steps = spec["grid"][0] if adds else 1
    for many, addends in adds:
        _, rows, columns = addends[0][0].shape
        block = (many, rows // steps, columns)
        for array, first in addends:
            extra.append(array)
            extra_specs.append(
                pl.BlockSpec(block, lambda i, *at, first=first, many=many: (first // many, i, 0))
            )
        out_shape = out_shape + [jax.ShapeDtypeStruct((many, rows, columns), BF16)]
        out_specs = out_specs + [pl.BlockSpec(block, lambda i, *at: (0, i, 0))]
        sizes.append(len(addends))
    lead, outs = len(scalars) + len(operands), len(out_shape) - len(adds)

    def body(*refs):
        first = lead + len(extra) + len(deps)
        kernel(*refs[:lead], *refs[first : first + outs], *refs[first + outs + len(adds) :])
        sources = refs[lead : lead + len(extra)]
        for n, out in zip(sizes, refs[first + outs : first + outs + len(adds)]):
            out[...] = sum(ref[...].astype(F32) for ref in sources[:n]).astype(BF16)
            sources = sources[n:]

    in_specs = list(spec.pop("in_specs")) + extra_specs + [HBM] * len(deps)
    aliases = spec.pop("input_output_aliases", {})
    if scalars:
        grid_spec = pltpu.PrefetchScalarGridSpec(
            num_scalar_prefetch=len(scalars), in_specs=in_specs, out_specs=out_specs, **spec
        )
        spec = {"grid_spec": grid_spec}
    else:
        spec.update(in_specs=in_specs, out_specs=out_specs)
    results = pl.pallas_call(
        body,
        out_shape=out_shape,
        input_output_aliases=aliases,
        compiler_params=pltpu.CompilerParams(vmem_limit_bytes=vmem << 20),
        cost_estimate=pl.CostEstimate(flops=0, transcendentals=0, bytes_accessed=0),
        name=name,
        **spec,
    )(*scalars, *operands, *extra, *deps)
    return results[0] if single and not adds else results


def fence(values, deps=()):
    return list(
        call(
            lambda *refs: None,
            "fence",
            values,
            deps,
            in_specs=[HBM] * len(values),
            out_specs=[HBM] * len(values),
            out_shape=[jax.ShapeDtypeStruct(v.shape, v.dtype) for v in values],
            input_output_aliases={n: n for n in range(len(values))},
        )
    )


def rotary_tables(length):
    positions = np.arange(length, dtype=np.float32)
    frequency = 10000.0 ** (-np.arange(ROT // 2, dtype=np.float64) * 2.0 / ROT)
    angles = positions[:, None] * frequency.astype(np.float32)[None, :]
    cosine, sine = np.cos(angles.astype(np.float64)), np.sin(angles.astype(np.float64))
    rest = HEAD_DIM - ROT
    none = np.zeros((length, ROT // 2))
    ones, zeros = np.ones((length, rest)), np.zeros((length, rest))
    straight = np.concatenate([cosine, cosine, ones], axis=1)
    left = np.concatenate([-sine, none, zeros], axis=1)
    right = np.concatenate([none, sine, zeros], axis=1)
    return [
        jnp.asarray(np.concatenate([t, t], axis=1).astype(np.float32))
        for t in (straight, left, right)
    ]


def rotated(u, straight, left, right, sign):
    half = ROT // 2
    turned = pltpu.roll(u, LANES - half, 1) * left + pltpu.roll(u, half, 1) * right
    return u * straight + sign * turned


def normalized(x):
    x = x.astype(F32)
    centered = x - jnp.mean(x, axis=1, keepdims=True)
    variance = jnp.mean(centered * centered, axis=1, keepdims=True)
    return centered * lax.rsqrt(variance + EPS)


def block_copies(blocks, place, sems):
    me = lax.axis_index("dp")
    return [
        pltpu.make_async_copy(block, place(lax.bitwise_xor(me, j)), sems.at[j])
        for j, block in enumerate(blocks)
    ]


def span(owner, size):
    return pl.ds(pl.multiple_of(owner * size, size), size)


def rows_at(ref, size):
    return lambda owner: ref.at[pl.ds(pl.multiple_of(owner * size, size), size)]


def columns_at(ref, size):
    return lambda owner: ref.at[:, pl.ds(pl.multiple_of(owner * size, size), size)]


def project_kernel(setup, x_ref, bias_ref, gain_ref, shift_ref, cos_ref, left_ref, right_ref, *rest):
    count, width, hidden = setup
    blocks = rest[:count]
    qkv_ref, act_ref, slope_ref, normed_ref, held, sems = rest[-6:]

    @pl.when(pl.program_id(0) == 0)
    def _():
        loads = block_copies(blocks, rows_at(held, blocks[0].shape[0]), sems)
        for copy in loads:
            copy.start()
        for copy in loads:
            copy.wait()

    x = (normalized(x_ref[...]) * gain_ref[...] + shift_ref[...]).astype(BF16)
    normed_ref[...] = x
    root = 0.7978845608028654
    for t in range((3 * width + hidden) // width):
        columns = slice(t * width, (t + 1) * width)
        y = dot(x, held[:, columns], 1, 0) + bias_ref[:, columns]
        if t < 3:
            for g in range(width // LANES):
                part = y[:, g * LANES : (g + 1) * LANES]
                if t < 2:
                    part = rotated(part, cos_ref[...], left_ref[...], right_ref[...], 1.0)
                if t == 0:
                    part = part * HEAD_DIM**-0.5
                start = t * width + g * LANES
                qkv_ref[:, start : start + LANES] = part.astype(BF16)
        else:
            columns = slice((t - 3) * width, (t - 2) * width)
            square = y * y
            turn = jnp.tanh(root * y * (1.0 + 0.044715 * square))
            half = 0.5 * (1.0 + turn)
            act_ref[:, columns] = (y * half).astype(BF16)
            slope = half * (1.0 + y * (1.0 - turn) * (root + (3.0 * 0.044715 * root) * square))
            slope_ref[:, columns] = slope.astype(BF16)


def project(sequence, x, blocks, bias, gain, shift, tables, width, tile, earlier, deps):
    (length, model), total, count = x.shape, blocks[0].shape[1], len(blocks)
    hidden, steps = total - 3 * width, length // tile
    rows = lambda w: pl.BlockSpec((tile, w), lambda i: (i, 0))
    out = lambda w: pl.BlockSpec((tile, w), lambda i: (sequence * steps + i, 0))
    line = lambda a: pl.BlockSpec(a.shape, lambda i: (0, 0))
    widths = (3 * width, hidden, hidden, model)
    operands = [x, bias, gain, shift, *tables, *blocks]
    return call(
        functools.partial(project_kernel, (count, width, hidden)),
        "project",
        operands + list(earlier),
        deps,
        grid=(steps,),
        in_specs=[rows(model), line(bias), line(gain), line(shift)]
        + [rows(LANES)] * 3
        + [HBM] * (count + len(earlier)),
        out_specs=[out(w) for w in widths],
        out_shape=[jax.ShapeDtypeStruct((2 * length, w), BF16) for w in widths],
        input_output_aliases={len(operands) + n: n for n in range(len(earlier))},
        scratch_shapes=[pltpu.VMEM((model, total), BF16), pltpu.SemaphoreType.DMA((count,))],
    )


def attend_kernel(block, q_ref, k_ref, v_ref, out_ref, lse_ref):
    length = q_ref.shape[0]
    lane = lax.broadcasted_iota(jnp.int32, (1, LANES), 1)
    key = lax.broadcasted_iota(jnp.int32, (block, block), 0)
    causal = key <= lax.broadcasted_iota(jnp.int32, (block, block), 1)
    for i in range(length // block):
        rows, before = pl.ds(i * block, block), pl.ds(0, i * block)
        results = []
        for h in range(2):
            mine = (lane < HEAD_DIM) if h == 0 else (lane >= HEAD_DIM)
            query = jnp.where(mine, q_ref[rows, :], 0)
            near = jnp.where(causal, dot(k_ref[rows, :], query, 1, 1), -1e30)
            highest = jnp.max(near, axis=0, keepdims=True)
            if i:
                far = dot(k_ref[before, :], query, 1, 1)
                highest = jnp.maximum(highest, jnp.max(far, axis=0, keepdims=True))
            near = jnp.exp(near - highest)
            total = jnp.sum(near, axis=0, keepdims=True)
            if i:
                far = jnp.exp(far - highest)
                total = total + jnp.sum(far, axis=0, keepdims=True)
            inverse = 1.0 / total
            result = dot((near * inverse).astype(BF16), v_ref[rows, :], 0, 0)
            if i:
                result = result + dot((far * inverse).astype(BF16), v_ref[before, :], 0, 0)
            results.append(result)
            lse_ref[0, h : h + 1, rows] = highest + jnp.log(total)
        out_ref[rows, :] = jnp.where(lane < HEAD_DIM, results[0], results[1]).astype(BF16)


def pair_specs(length, pairs):
    return lambda off: pl.BlockSpec(
        (length, LANES), lambda g: (g // pairs, off * pairs + g % pairs)
    )


def attend(qkv, length, block, deps):
    width, sequences = qkv.shape[1] // 3, qkv.shape[0] // length
    pairs = width // LANES
    at = pair_specs(length, pairs)
    return call(
        functools.partial(attend_kernel, block),
        "attend",
        [qkv, qkv, qkv],
        deps,
        grid=(sequences * pairs,),
        in_specs=[at(0), at(1), at(2)],
        out_specs=[at(0), pl.BlockSpec((1, 8, length), lambda g: (g, 0, 0))],
        out_shape=[
            jax.ShapeDtypeStruct((qkv.shape[0], width), BF16),
            jax.ShapeDtypeStruct((sequences * pairs, 8, length), F32),
        ],
    )


def attend_back_kernel(
    block,
    q_ref,
    k_ref,
    v_ref,
    grad_ref,
    mixed_ref,
    lse_ref,
    cos_ref,
    left_ref,
    right_ref,
    gq_ref,
    gk_ref,
    gv_ref,
    sum_ref,
    gk_sum,
    gv_sum,
):
    length = q_ref.shape[0]
    lane = lax.broadcasted_iota(jnp.int32, (1, LANES), 1)
    key = lax.broadcasted_iota(jnp.int32, (block, block), 0)
    causal = key <= lax.broadcasted_iota(jnp.int32, (block, block), 1)
    count = length // block
    sum_ref[...] = jnp.zeros_like(sum_ref)

    def put(ref, which, rows, value):
        value = value.astype(BF16)
        ref[rows, :] = value
        sum_ref[0, which : which + 1, :] += jnp.sum(value.astype(F32), axis=0, keepdims=True)

    def unrotated(value, rows):
        return rotated(value, cos_ref[rows, :], left_ref[rows, :], right_ref[rows, :], -1.0)

    for i in reversed(range(count)):
        rows = pl.ds(i * block, block)
        product = grad_ref[rows, :].astype(F32) * mixed_ref[rows, :].astype(F32)
        gq = None
        for h in range(2):
            mine = (lane < HEAD_DIM) if h == 0 else (lane >= HEAD_DIM)
            query = jnp.where(mine, q_ref[rows, :], 0)
            grad = jnp.where(mine, grad_ref[rows, :], 0)
            ones = jnp.where(mine, jnp.ones((8, LANES), F32), 0.0)
            delta = lax.dot_general(
                ones,
                product,
                (((1,), (1,)), ((), ())),
                precision=lax.Precision.HIGHEST,
                preferred_element_type=F32,
            )[0:1, :]
            lse = lse_ref[0, h : h + 1, rows]
            for j in range(i + 1):
                keys = pl.ds(j * block, block)
                key_rows = k_ref[keys, :]
                probs = jnp.exp(dot(key_rows, query, 1, 1) - lse)
                if j == i:
                    probs = jnp.where(causal, probs, 0.0)
                gprobs = dot(v_ref[keys, :], grad, 1, 1)
                gscores = (probs * (gprobs - delta)).astype(BF16)
                gv, gk = dot(probs.astype(BF16), grad, 1, 0), dot(gscores, query, 1, 0)
                if i == count - 1 and h == 0:
                    gv_sum[keys, :] = gv
                    gk_sum[keys, :] = gk
                else:
                    gv_sum[keys, :] += gv
                    gk_sum[keys, :] += gk
                part = dot(gscores, jnp.where(mine, key_rows, 0), 0, 0)
                gq = part if gq is None else gq + part
        put(gq_ref, 0, rows, unrotated(gq * HEAD_DIM**-0.5, rows))
    for i in range(count):
        rows = pl.ds(i * block, block)
        put(gk_ref, 1, rows, unrotated(gk_sum[rows, :], rows))
        put(gv_ref, 2, rows, gv_sum[rows, :])


def attend_back(sequence, qkv, grad, mixed, lse, tables, length, block, deps):
    width = qkv.shape[1] // 3
    pairs = width // LANES
    at = lambda off: pl.BlockSpec((length, LANES), lambda g: (sequence, off * pairs + g))
    out = pl.BlockSpec((length, LANES), lambda g: (0, g))
    table = pl.BlockSpec((length, LANES), lambda g: (0, 0))
    small = pl.BlockSpec((1, 8, length), lambda g: (sequence * pairs + g, 0, 0))
    return call(
        functools.partial(attend_back_kernel, block),
        "attend_back",
        [qkv, qkv, qkv, grad, mixed, lse, *tables],
        deps,
        grid=(pairs,),
        in_specs=[at(0), at(1), at(2), at(0), at(0), small, table, table, table],
        out_specs=[out] * 3 + [pl.BlockSpec((1, 8, LANES), lambda g: (g, 0, 0))],
        out_shape=[jax.ShapeDtypeStruct((length, width), BF16)] * 3
        + [jax.ShapeDtypeStruct((pairs, 8, LANES), F32)],
        scratch_shapes=[pltpu.VMEM((length, LANES), F32)] * 2,
    )


def by_sequence(tile, width, steps):
    return [
        pl.BlockSpec((tile, width), lambda i: (jnp.minimum(i, steps - 1), 0)),
        pl.BlockSpec((tile, width), lambda i: (jnp.maximum(i - steps, 0), 0)),
    ]


def other_first(tile, width, steps):
    return pl.BlockSpec((tile, width), lambda i: ((i + steps) % (2 * steps), 0))


def put_by_sequence(step, steps, value, other_ref, own_ref):
    @pl.when(step < steps)
    def _():
        other_ref[...] = value

    @pl.when(step >= steps)
    def _():
        own_ref[...] = value


def branch_kernel(count, steps, mixed_ref, act_ref, *rest):
    blocks, (other_ref, own_ref, held, sems) = rest[:count], rest[count:]
    step = pl.program_id(0)

    @pl.when(step == 0)
    def _():
        loads = block_copies(blocks, columns_at(held, blocks[0].shape[1]), sems)
        for copy in loads:
            copy.start()
        for copy in loads:
            copy.wait()

    x = jnp.concatenate([mixed_ref[...], act_ref[...]], axis=1)
    put_by_sequence(step, steps, dot(x, held[...], 1, 0).astype(BF16), other_ref, own_ref)


def branch_sums(mixed, act, blocks, tile, deps):
    length, count = mixed.shape[0] // 2, len(blocks)
    inner, model, steps = blocks[0].shape[0], count * blocks[0].shape[1], length // tile
    return call(
        functools.partial(branch_kernel, count, steps),
        "branch_sums",
        [mixed, act, *blocks],
        deps,
        grid=(2 * steps,),
        in_specs=[other_first(tile, a.shape[1], steps) for a in (mixed, act)] + [HBM] * count,
        out_specs=by_sequence(tile, model, steps),
        out_shape=[jax.ShapeDtypeStruct((length, model), BF16)] * 2,
        scratch_shapes=[pltpu.VMEM((inner, model), BF16), pltpu.SemaphoreType.DMA((count,))],
    )


def grad_in_kernel(setup, dy_ref, slope_ref, *rest):
    count, width, hidden = setup
    blocks = rest[:count]
    gmixed_ref, gpre_ref, gsum_ref, dsum_ref, held, sems = rest[-6:]

    @pl.when(pl.program_id(0) == 0)
    def _():
        loads = block_copies(blocks, columns_at(held, blocks[0].shape[1]), sems)
        for copy in loads:
            copy.start()
        gsum_ref[...] = jnp.zeros_like(gsum_ref)
        dsum_ref[...] = jnp.zeros_like(dsum_ref)
        for copy in loads:
            copy.wait()

    dy = dy_ref[...]
    gmixed_ref[...] = dot(dy, held[:width, :], 1, 1).astype(BF16)
    for start in range(0, hidden, width):
        part = slice(start, start + width)
        gact = dot(dy, held[width + start : 2 * width + start, :], 1, 1)
        gpre = (gact * slope_ref[:, part].astype(F32)).astype(BF16)
        gpre_ref[:, part] = gpre
        gsum_ref[0:1, part] += jnp.sum(gpre.astype(F32), axis=0, keepdims=True)
    dsum_ref[0:1, :] += jnp.sum(dy.astype(F32), axis=0, keepdims=True)


def grad_in(sequence, dy, slope, blocks, width, tile, earlier, deps):
    (length, model), hidden, count = dy.shape, slope.shape[1], len(blocks)
    steps = length // tile
    at = lambda w: pl.BlockSpec((tile, w), lambda i: (sequence * steps + i, 0))
    total = lambda w: pl.BlockSpec((8, w), lambda i: (0, 0))
    operands = [dy, slope, *blocks]
    return call(
        functools.partial(grad_in_kernel, (count, width, hidden)),
        "grad_in",
        operands + list(earlier),
        deps,
        grid=(steps,),
        in_specs=[pl.BlockSpec((tile, model), lambda i: (i, 0)), at(hidden)]
        + [HBM] * (count + len(earlier)),
        out_specs=[
            at(width),
            pl.BlockSpec((tile, hidden), lambda i: (i, 0)),
            total(hidden),
            total(model),
        ],
        out_shape=[
            jax.ShapeDtypeStruct((2 * length, width), BF16),
            jax.ShapeDtypeStruct((length, hidden), BF16),
            jax.ShapeDtypeStruct((8, hidden), F32),
            jax.ShapeDtypeStruct((8, model), F32),
        ],
        input_output_aliases={len(operands) + n: n for n in range(len(earlier))},
        scratch_shapes=[
            pltpu.VMEM((width + hidden, model), BF16),
            pltpu.SemaphoreType.DMA((count,)),
        ],
    )


def add_kernel(a_ref, b_ref, out_ref):
    out_ref[...] = (a_ref[...].astype(F32) + b_ref[...].astype(F32)).astype(BF16)


def add_rows(a, b):
    rows = pl.BlockSpec((a.shape[0] // 2, a.shape[1]), lambda i: (i, 0))
    return call(
        add_kernel,
        "add_rows",
        [a, b],
        grid=(2,),
        in_specs=[rows, rows],
        out_specs=rows,
        out_shape=jax.ShapeDtypeStruct(a.shape, BF16),
    )


def grad_normed_kernel(count, half, x_ref, *rest):
    grads, blocks, (out_ref, sum_ref, held, sems) = rest[:8], rest[8 : 8 + 2 * count], rest[-4:]
    (size, total), few, me = blocks[0].shape, count // 2, lax.axis_index("dp")

    @pl.when(pl.program_id(0) == 0)
    def _():
        for start in (True, False):
            for n, block in enumerate(blocks):
                core, j = n // count, n % count
                owner = lax.bitwise_xor(me, j ^ core) - half * few
                columns = slice(core * total, (core + 1) * total)

                @pl.when((owner >= 0) & (owner < few))
                def _(start=start, n=n, block=block, owner=owner, columns=columns):
                    target = held.at[span(owner, size), columns]
                    copy = pltpu.make_async_copy(block, target, sems.at[n])
                    if start:
                        copy.start()
                    else:
                        copy.wait()

        sum_ref[...] = jnp.zeros_like(sum_ref)

    columns = slice(half * few * size, (half + 1) * few * size)
    normal = normalized(x_ref[...])[:, columns]
    g = jnp.concatenate([ref[...] for ref in grads], axis=1)
    result = dot(g, held[...], 1, 1)
    sum_ref[0:1, :] += jnp.sum(result * normal, axis=0, keepdims=True)
    sum_ref[1:2, :] += jnp.sum(result, axis=0, keepdims=True)
    out_ref[...] = result.astype(BF16)


def grad_normed_sums(half, grads, x, blocks, tile, deps, adds=()):
    (length, model), count, total = x.shape, len(blocks) // 2, blocks[0].shape[1]
    part = model // 2
    rows = lambda w: pl.BlockSpec((tile, w), lambda i: (i, 0))
    return call(
        functools.partial(grad_normed_kernel, count, half),
        "grad_normed_sums",
        [x, *grads, *blocks],
        deps,
        adds=adds,
        grid=(length // tile,),
        in_specs=[rows(model)] + [rows(g.shape[1]) for g in grads] + [HBM] * (2 * count),
        out_specs=[rows(part), pl.BlockSpec((8, part), lambda i: (0, 0))],
        out_shape=[
            jax.ShapeDtypeStruct((length, part), BF16),
            jax.ShapeDtypeStruct((8, part), F32),
        ],
        scratch_shapes=[
            pltpu.VMEM((part, 2 * total), BF16),
            pltpu.SemaphoreType.DMA((2 * count,)),
        ],
    )


def weight_grad_kernel(writes, left, rows, many, groups, at_ref, *refs):
    cuts, (*refs, held, grad, sems) = refs[:many], refs[many:]
    whole, outs = refs[: len(refs) - len(writes)], refs[len(refs) - len(writes) :]
    step, core, loads, first = pl.program_id(0), lax.rem(lax.axis_index("dp"), 2), [], 0
    for group in groups:
        below = 0
        for ref in whole[:group]:
            columns = pl.ds(first, ref.shape[1])
            for start in range(0, ref.shape[0], rows):
                target = held.at[pl.ds(below + start, rows), columns]
                loads.append((ref.at[pl.ds(start, rows)], target))
            below += ref.shape[0]
        first += whole[0].shape[1]
        whole = whole[group:]
    loads = [pltpu.make_async_copy(*pair, sems.at[n]) for n, pair in enumerate(loads)]

    @pl.when(step == 0)
    def _():
        for copy in loads:
            copy.start()
        for copy in loads:
            copy.wait()

    cut = jnp.concatenate([ref[...] for ref in cuts], axis=0)
    pair = (cut, held[...]) if left else (held[...], cut)
    grad[...] = dot(*pair, 0, 0).astype(BF16)
    size = cut.shape[1] // 2
    for half, steps, out_ref in writes_of(writes, outs):
        here = functools.reduce(jnp.logical_or, [step == s for s in steps])

        @pl.when(here)
        def _(half=half, out_ref=out_ref):
            mine = span(core if half == 0 else 1 - core, size)
            out_ref[0] = grad[mine, :] if left else grad[:, mine]


def writes_of(writes, outs):
    return [(half, steps, out) for (half, steps), out in zip(writes, outs)]


def weight_grads(me, xs, gs, count, deps, left, adds=()):
    plan, chips = scatter_plan(count), count // 2
    order = [j // 2 for s in plan[0] for j in s]
    sets = [(half, s) for s in range(len(plan[0])) for half in range(2)]
    writes = [(half, [order.index(j // 2) for j in plan[half][s]]) for half, s in sets]
    table = []
    for _, steps in writes:
        for i in range(chips):
            later = [w for w in steps if w >= i]
            table.append(steps.index(min(later) if later else max(steps)))
    owners = lax.bitwise_xor(me // 2, jnp.array(order, jnp.int32))
    at = jnp.concatenate([owners, jnp.array(table, jnp.int32)])
    cut, whole = (xs, gs) if left else (gs, xs)
    groups, length = [len(g) for g in whole], sum(a.shape[0] for a in whole[0])
    size, full = cut[0].shape[1] // count, sum(g[0].shape[1] for g in whole)
    shape, whole = (size, full) if left else (full, size), [a for g in whole for a in g]
    rows = length // 4
    pieces = 4 * len(groups)

    def out(n):
        return pl.BlockSpec((1, *shape), lambda i, at: (at[chips * (n + 1) + i], 0, 0))

    outs = call(
        functools.partial(weight_grad_kernel, writes, left, rows, len(cut), groups),
        "weight_grads",
        [*cut, *whole],
        deps,
        (at,),
        adds,
        grid=(chips,),
        in_specs=[pl.BlockSpec((a.shape[0], 2 * size), lambda i, at: (0, at[i])) for a in cut]
        + [HBM] * len(whole),
        out_specs=[out(n) for n in range(len(sets))],
        out_shape=[
            jax.ShapeDtypeStruct((len(plan[half][s]), *shape), BF16) for half, s in sets
        ],
        scratch_shapes=[
            pltpu.VMEM((length, full), BF16),
            pltpu.VMEM((2 * size, full) if left else (full, 2 * size), BF16),
            pltpu.SemaphoreType.DMA((pieces,)),
        ],
    )
    blocks = [[o for o, (half, _) in zip(outs, sets) if half == h] for h in range(2)]
    return (blocks, *outs[len(sets) :]) if adds else blocks


def norm_back_kernel(tokens_ref, dy_ref, gain_ref, left_ref, right_ref, out_ref):
    x = tokens_ref[...].astype(F32)
    centered = x - jnp.mean(x, axis=1, keepdims=True)
    inverse_std = lax.rsqrt(jnp.mean(centered * centered, axis=1, keepdims=True) + EPS)
    normal = centered * inverse_std
    grad = jnp.concatenate([left_ref[...], right_ref[...]], axis=1).astype(F32)
    scaled = grad * gain_ref[...]
    first_mean = jnp.mean(scaled, axis=1, keepdims=True)
    second_mean = jnp.mean(scaled * normal, axis=1, keepdims=True)
    back = (scaled - first_mean - normal * second_mean) * inverse_std
    out_ref[...] = (dy_ref[...].astype(F32) + back).astype(BF16)


def norm_back(tokens, dy, gain, halves, deps):
    rows, model = tokens.shape
    tile = min(128, rows)
    part = lambda w: pl.BlockSpec((tile, w), lambda i: (i, 0))
    return call(
        norm_back_kernel,
        "norm_back",
        [tokens, dy, gain, *halves],
        deps,
        grid=(rows // tile,),
        in_specs=[part(model), part(model), pl.BlockSpec((1, model), lambda i: (0, 0))]
        + [part(model // 2)] * 2,
        out_specs=part(model),
        out_shape=jax.ShapeDtypeStruct((rows, model), BF16),
    )


def across(value, bit, count):
    return lax.ppermute(value, "dp", [(i, i ^ bit) for i in range(count)])


def added(addends):
    return sum(a.astype(F32) for a in addends).astype(BF16)


def pair_sum(parts):
    while len(parts) > 1:
        parts = [a + b for a, b in zip(parts[::2], parts[1::2])]
    return parts[0]


def chip_bits(count):
    bits, bit = [], 2
    while bit < count:
        bits.append(bit)
        bit *= 2
    return bits


class BlockGather:
    def __init__(self, own, sibling, count):
        self.held, self.count = {0: own, 1: sibling}, count
        self.orders = (chip_bits(count), chip_bits(count)[::-1])

    def own_to(self, s):
        if s < len(self.orders[0]):
            for half in range(2):
                bit = self.orders[half][s]
                self.held[half ^ bit] = across(self.held[half], bit, self.count)

    def rest(self):
        for s in range(1, len(self.orders[0])):
            for half in range(2):
                order = self.orders[half]
                for j in [j for j in self.held if j % 2 == half]:
                    if j ^ order[s] not in self.held and not any(j & b for b in order[s:]):
                        self.held[j ^ order[s]] = across(self.held[j], order[s], self.count)

    def fenced(self, others=(), deps=()):
        keys = sorted(self.held)
        values = fence([self.held[j] for j in keys] + list(others), deps)
        self.held = dict(zip(keys, values))
        return values[len(keys) :]

    def blocks(self):
        return [self.held[j] for j in range(self.count)]


def scatter_orders(count):
    return (chip_bits(count)[::-1], chip_bits(count))


def scatter_plan(count):
    plan = []
    for half, order in enumerate(scatter_orders(count)):
        sets, rest = [[half]], [half]
        for bit in reversed(order):
            sets.insert(0, [j ^ bit for j in rest])
            rest = sets[0] + rest
        plan.append(sets)
    return plan


class BlockScatter:
    def __init__(self, halves, count):
        self.count, self.orders, self.plan = count, scatter_orders(count), scatter_plan(count)
        self.held = [[[(a, 0)] for a in arrays] for arrays in halves]
        self.steps = len(self.orders[0])

    def parts(self, half, s):
        many = len(self.plan[half][s])
        return [a[first : first + many] for a, first in self.held[half][s]]

    def total(self, half, s):
        if len(self.held[half][s]) > 1:
            self.held[half][s] = [(added(self.parts(half, s)), 0)]
        return self.parts(half, s)[0]

    def ready(self, s):
        return [self.total(half, s) for half in range(2)]

    def adds(self, s):
        return [(len(self.plan[half][s]), self.held[half][s]) for half in range(2)]

    def settle(self, s, sums):
        for half in range(2):
            self.held[half][s] = [(sums[half], 0)]

    def send(self, s):
        return [across(self.total(h, s), self.orders[h][s], self.count) for h in range(2)]

    def arrive(self, s, came):
        for half in range(2):
            first = 0
            for t in range(s + 1, len(self.plan[half])):
                self.held[half][t].append((came[half], first))
                first += len(self.plan[half][t])

    def between(self):
        for s in range(1, self.steps - 1):
            self.arrive(s, self.send(s))

    def last(self):
        return self.total(1, -1)[0]

    def finish(self, theirs):
        return sum(a[0].astype(F32) for a in self.parts(0, -1)), theirs.astype(F32)


def on_device(
    tokens,
    norm_gain,
    norm_bias,
    qkv_weight,
    qkv_bias,
    dense_weight,
    dense_bias,
    up_weight,
    up_bias,
    down_weight,
    down_bias,
    cotangent,
    *,
    ndp,
    nmp,
):
    me = lax.axis_index("dp")
    core = me % 2
    length, model = tokens.shape[0] * nmp, tokens.shape[1]
    tile, block = min(512, length), min(512, length)
    width, hidden = qkv_weight.shape[2] // 2, up_weight.shape[1] // 2
    chip_steps = len(chip_bits(ndp))
    rank = lambda array, axis, which, size: lax.dynamic_slice_in_dim(
        array, which * size, size, axis
    )

    def row_pack(which):
        qkv = rank(qkv_weight, 2, which, width)
        return jnp.concatenate([qkv[0], qkv[1], qkv[2], rank(up_weight, 1, which, hidden)], axis=1)

    def column_pack(which):
        return jnp.concatenate(
            [rank(dense_weight, 0, which, width), rank(down_weight, 0, which, hidden)], axis=0
        )

    pairs = width // LANES
    swap = lambda array: across(array, 1, ndp)
    line_gather = lambda array: lax.all_gather(array, "mp", axis=0, tiled=True)
    line_scatter = lambda array: lax.psum_scatter(array, "mp", scatter_dimension=0, tiled=True)
    x_own, dy_own = line_gather(tokens), line_gather(cotangent)
    rows = BlockGather(row_pack(core), swap(row_pack(1 - core)), ndp)
    columns = BlockGather(column_pack(core), swap(column_pack(1 - core)), ndp)
    rows.own_to(0)
    rows.fenced(deps=columns.held.values())
    rows.own_to(1)
    rows.fenced()
    rows.rest()
    x_own, *held = fence([x_own, columns.held[0], columns.held[1]], rows.blocks())
    columns.held = dict(enumerate(held))

    tables = rotary_tables(length)
    bias = jnp.concatenate(
        [
            rank(qkv_bias, 1, core, width).astype(F32).reshape(1, 3 * width),
            rank(up_bias[None, :], 1, core, hidden).astype(F32),
        ],
        axis=1,
    )
    gain, shift = norm_gain.astype(F32)[None, :], norm_bias.astype(F32)[None, :]
    x_other = swap(x_own)
    columns.own_to(0)
    common = (rows.blocks(), bias, gain, shift, tables, width, tile)
    first = project(0, x_own, *common, (), [columns.held[0]])
    (x_other,) = columns.fenced([x_other], [first[0]])
    columns.own_to(1)
    qkv, act, slope, normed = project(1, x_other, *common, first, [columns.held[0]])
    held = columns.fenced(rows.blocks(), [qkv])
    columns.rest()
    row_blocks, row_others = held, [swap(a) for a in held[:3]]
    mixed, lse = attend(qkv, length, block, [columns.held[0]])
    row_others = columns.fenced(row_others, [mixed])
    row_blocks[3:] = fence(row_blocks[3:], [row_others[0]])
    row_others += [swap(a) for a in row_blocks[3:]]
    other_sums, own_sums = branch_sums(mixed, act, columns.blocks(), tile, [row_blocks[3]])
    other_sums, dy_own, *row_others[3:] = fence([other_sums, dy_own, *row_others[3:]], [own_sums])
    theirs = swap(other_sums)
    dy_other = swap(dy_own)

    grads = (slope, columns.blocks(), width, tile)
    gmixed, gpre_own, *grad_a = grad_in(0, dy_own, *grads, (), [own_sums])
    theirs, dy_other = fence([theirs, dy_other], [grad_a[0]])
    total = add_rows(own_sums, theirs)
    branches = line_scatter(total)
    gmixed, gpre_other, *grad_b = grad_in(1, dy_other, *grads, [gmixed], [total])
    (gpre_sent,) = fence([gpre_other])
    gpre_came = swap(gpre_sent)
    column_grads = BlockScatter(
        weight_grads(me, [[mixed], [act]], [dy_own, dy_other], ndp, [gpre_sent], left=False), ndp
    )
    (gpre_came,) = fence([gpre_came], [column_grads.held[0][0][0][0]])
    column_came = column_grads.send(0)
    back = lambda sequence, deps: attend_back(
        sequence, qkv, gmixed, mixed, lse, tables, length, block, deps
    )
    *other, qkv_sums_b = back(1, [gpre_came])
    came = [swap(a) for a in other]
    *own, qkv_sums_a = back(0, [other[0]])
    came = fence([*came, *column_came], [own[0]])
    column_came, came = came[3:], came[:3]
    column_grads.arrive(0, column_came)
    column_grads.between()
    all_grads = [*own, gpre_own, *came, gpre_came]

    def normed_half(half, deps, adds=()):
        return grad_normed_sums(
            half, all_grads, x_own, [*row_blocks, *row_others], tile, deps, adds
        )

    total_a, sums_a, *settled = normed_half(0, [], column_grads.adds(chip_steps - 1))
    column_grads.settle(chip_steps - 1, settled)
    half_a = line_scatter(total_a)
    column_came = column_grads.send(chip_steps - 1)
    up_grads = BlockScatter(
        weight_grads(me, [normed], [[gpre_own, gpre_sent]], ndp, [sums_a], left=True), ndp
    )
    c0, c1, branches, u0, u1 = fence(
        [*column_came, branches, *(up_grads.held[h][0][0][0] for h in range(2))]
    )
    up_grads.held[0][0], up_grads.held[1][0] = [(u0, 0)], [(u1, 0)]
    up_came = up_grads.send(0)
    column_grads.arrive(chip_steps - 1, [c0, c1])
    blocks, column_last = weight_grads(
        me,
        [normed],
        [[a, b] for a, b in zip(own, other)],
        ndp,
        [c0],
        True,
        [column_grads.adds(len(column_grads.plan[1]) - 1)[1]],
    )
    qkv_grads = BlockScatter(blocks, ndp)
    qkv_came = qkv_grads.send(0)
    column_theirs = swap(column_last[0])
    total_b, sums_b = normed_half(1, [qkv_grads.held[0][0][0][0]])
    half_b = line_scatter(total_b)
    u0, u1, q0, q1, half_a = fence([*up_came, *qkv_came, half_a], [sums_b, column_theirs])
    up_grads.arrive(0, [u0, u1])
    qkv_grads.arrive(0, [q0, q1])
    up_grads.between()
    qkv_grads.between()
    up_came, qkv_came = up_grads.send(chip_steps - 1), qkv_grads.send(chip_steps - 1)
    u0, u1, q0, q1, branches, sums_b, column_theirs = fence(
        [*up_came, *qkv_came, branches, sums_b, column_theirs]
    )
    up_grads.arrive(chip_steps - 1, [u0, u1])
    qkv_grads.arrive(chip_steps - 1, [q0, q1])
    up_theirs = swap(up_grads.last())
    qkv_theirs = swap(qkv_grads.last())
    qkv_sum = (qkv_sums_a + qkv_sums_b)[:, :3, :].transpose(1, 0, 2).reshape(3 * width)
    norm_sums = jnp.concatenate([sums_a[:2], sums_b[:2]], axis=1)
    small = jnp.concatenate(
        [
            norm_sums.reshape(2 * model),
            qkv_sum,
            grad_a[0][0] + grad_b[0][0],
            grad_a[1][0] + grad_b[1][0],
        ]
    )
    small = pair_sum([small] + [across(small, j, ndp) for j in range(2, ndp, 2)])
    small_other = swap(small)
    grad_tokens = norm_back(tokens, cotangent, gain, [half_a, half_b], [small_other])
    (norm_sums,) = fence([small[: 2 * model] + small_other[: 2 * model]], [grad_tokens])
    norm_sums = [norm_sums] + [
        lax.ppermute(norm_sums, "mp", [(i, i ^ j) for i in range(nmp)]) for j in range(1, nmp)
    ]
    while len(norm_sums) > 1:
        norm_sums = [a + b for a, b in zip(norm_sums[::2], norm_sums[1::2])]
    norm_sums = norm_sums[0]

    output = (
        tokens.astype(F32)
        + branches.astype(F32)
        + (dense_bias.astype(F32) + down_bias.astype(F32))[None, :]
    ).astype(BF16)

    def both(mine, theirs, axis):
        return jnp.where(
            core == 0,
            jnp.concatenate([mine, theirs], axis=axis),
            jnp.concatenate([theirs, mine], axis=axis),
        )

    mine, theirs = column_grads.finish(column_theirs)
    owned_dense = both(mine[:width], theirs[:width], 0)
    owned_down = both(mine[width:], theirs[width:], 0)
    owned_up = both(*up_grads.finish(up_theirs), 1)
    mine, theirs = qkv_grads.finish(qkv_theirs)
    owned_qkv = jnp.stack(
        [
            both(mine[:, c * width : (c + 1) * width], theirs[:, c * width : (c + 1) * width], 1)
            for c in range(3)
        ]
    )

    inner = 3 * width + hidden
    grad_out_bias = small[2 * model + inner :]
    here, there = (a[2 * model : 2 * model + inner] for a in (small, small_other))
    even, odd = jnp.where(core == 0, here, there), jnp.where(core == 0, there, here)
    grad_qkv_bias = jnp.concatenate(
        [a[: 3 * width].reshape(3, width) for a in (even, odd)], axis=1
    )
    grad_up_bias = jnp.concatenate([even[3 * width :], odd[3 * width :]])

    return (
        output,
        grad_tokens,
        norm_sums[:model],
        norm_sums[model:],
        owned_qkv,
        grad_qkv_bias,
        owned_dense,
        grad_out_bias,
        owned_up,
        grad_up_bias,
        owned_down,
        grad_out_bias,
    )


def solution(mesh):
    return jax.shard_map(
        functools.partial(on_device, ndp=mesh.shape["dp"], nmp=mesh.shape["mp"]),
        mesh=mesh,
        in_specs=(
            P(("dp", "mp"), None),
            P(),
            P(),
            P(None, "dp", "mp"),
            P(None, "mp"),
            P("mp", "dp"),
            P(),
            P("dp", "mp"),
            P("mp"),
            P("mp", "dp"),
            P(),
            P(("dp", "mp"), None),
        ),
        out_specs=(
            P(("dp", "mp"), None),
            P(("dp", "mp"), None),
            P(),
            P(),
            P(None, "dp", "mp"),
            P(None, "mp"),
            P("mp", "dp"),
            P(),
            P("dp", "mp"),
            P("mp"),
            P("mp", "dp"),
            P(),
        ),
        check_vma=False,
    )
```

```python
import functools

import jax
import jax.numpy as jnp
import numpy as np
from jax import lax
from jax.experimental import pallas as pl
from jax.experimental.pallas import tpu as pltpu
from jax.sharding import PartitionSpec as P

HEAD_DIM = 64
ROT = 32
EPS = 1e-05
LANES = 128
F32 = jnp.float32
BF16 = jnp.bfloat16
HBM = pl.BlockSpec(memory_space=pltpu.HBM)


def dot(lhs, rhs, lhs_dim, rhs_dim):
    return lax.dot_general(
        lhs, rhs, (((lhs_dim,), (rhs_dim,)), ((), ())), preferred_element_type=F32
    )


def call(kernel, name, operands, deps=(), scalars=(), adds=(), vmem=64, **spec):
    deps, out_shape = tuple(deps), spec.pop("out_shape")
    single = not isinstance(out_shape, list)
    out_shape = [out_shape] if single else out_shape
    out_specs = spec.pop("out_specs")
    out_specs = [out_specs] if single else list(out_specs)
    extra, extra_specs, sizes = [], [], []
    steps = spec["grid"][0] if adds else 1
    for many, addends in adds:
        _, rows, columns = addends[0][0].shape
        block = (many, rows // steps, columns)
        for array, first in addends:
            extra.append(array)
            extra_specs.append(
                pl.BlockSpec(block, lambda i, *at, first=first, many=many: (first // many, i, 0))
            )
        out_shape = out_shape + [jax.ShapeDtypeStruct((many, rows, columns), BF16)]
        out_specs = out_specs + [pl.BlockSpec(block, lambda i, *at: (0, i, 0))]
        sizes.append(len(addends))
    lead, outs = len(scalars) + len(operands), len(out_shape) - len(adds)

    def body(*refs):
        first = lead + len(extra) + len(deps)
        kernel(*refs[:lead], *refs[first : first + outs], *refs[first + outs + len(adds) :])
        sources = refs[lead : lead + len(extra)]
        for n, out in zip(sizes, refs[first + outs : first + outs + len(adds)]):
            out[...] = sum(ref[...].astype(F32) for ref in sources[:n]).astype(BF16)
            sources = sources[n:]

    in_specs = list(spec.pop("in_specs")) + extra_specs + [HBM] * len(deps)
    aliases = spec.pop("input_output_aliases", {})
    if scalars:
        grid_spec = pltpu.PrefetchScalarGridSpec(
            num_scalar_prefetch=len(scalars), in_specs=in_specs, out_specs=out_specs, **spec
        )
        spec = {"grid_spec": grid_spec}
    else:
        spec.update(in_specs=in_specs, out_specs=out_specs)
    results = pl.pallas_call(
        body,
        out_shape=out_shape,
        input_output_aliases=aliases,
        compiler_params=pltpu.CompilerParams(vmem_limit_bytes=vmem << 20),
        cost_estimate=pl.CostEstimate(flops=0, transcendentals=0, bytes_accessed=0),
        name=name,
        **spec,
    )(*scalars, *operands, *extra, *deps)
    return results[0] if single and not adds else results


def fence(values, deps=()):
    return list(
        call(
            lambda *refs: None,
            "fence",
            values,
            deps,
            in_specs=[HBM] * len(values),
            out_specs=[HBM] * len(values),
            out_shape=[jax.ShapeDtypeStruct(v.shape, v.dtype) for v in values],
            input_output_aliases={n: n for n in range(len(values))},
        )
    )


def rotary_tables(length):
    positions = np.arange(length, dtype=np.float32)
    frequency = 10000.0 ** (-np.arange(ROT // 2, dtype=np.float64) * 2.0 / ROT)
    angles = positions[:, None] * frequency.astype(np.float32)[None, :]
    cosine, sine = np.cos(angles.astype(np.float64)), np.sin(angles.astype(np.float64))
    rest = HEAD_DIM - ROT
    none = np.zeros((length, ROT // 2))
    ones, zeros = np.ones((length, rest)), np.zeros((length, rest))
    straight = np.concatenate([cosine, cosine, ones], axis=1)
    left = np.concatenate([-sine, none, zeros], axis=1)
    right = np.concatenate([none, sine, zeros], axis=1)
    return [
        jnp.asarray(np.concatenate([t, t], axis=1).astype(np.float32))
        for t in (straight, left, right)
    ]


def rotated(u, straight, left, right, sign):
    half = ROT // 2
    turned = pltpu.roll(u, LANES - half, 1) * left + pltpu.roll(u, half, 1) * right
    return u * straight + sign * turned


def normalized(x):
    x = x.astype(F32)
    centered = x - jnp.mean(x, axis=1, keepdims=True)
    variance = jnp.mean(centered * centered, axis=1, keepdims=True)
    return centered * lax.rsqrt(variance + EPS)


def block_copies(blocks, place, sems):
    me = lax.axis_index("dp")
    return [
        pltpu.make_async_copy(block, place(lax.bitwise_xor(me, j)), sems.at[j])
        for j, block in enumerate(blocks)
    ]


def span(owner, size):
    return pl.ds(pl.multiple_of(owner * size, size), size)


def rows_at(ref, size):
    return lambda owner: ref.at[pl.ds(pl.multiple_of(owner * size, size), size)]


def columns_at(ref, size):
    return lambda owner: ref.at[:, pl.ds(pl.multiple_of(owner * size, size), size)]


def project_kernel(setup, x_ref, bias_ref, gain_ref, shift_ref, cos_ref, left_ref, right_ref, *rest):
    count, width, hidden = setup
    blocks = rest[:count]
    qkv_ref, act_ref, slope_ref, normed_ref, held, sems = rest[-6:]

    @pl.when(pl.program_id(0) == 0)
    def _():
        loads = block_copies(blocks, rows_at(held, blocks[0].shape[0]), sems)
        for copy in loads:
            copy.start()
        for copy in loads:
            copy.wait()

    x = (normalized(x_ref[...]) * gain_ref[...] + shift_ref[...]).astype(BF16)
    normed_ref[...] = x
    root = 0.7978845608028654
    for t in range((3 * width + hidden) // width):
        columns = slice(t * width, (t + 1) * width)
        y = dot(x, held[:, columns], 1, 0) + bias_ref[:, columns]
        if t < 3:
            for g in range(width // LANES):
                part = y[:, g * LANES : (g + 1) * LANES]
                if t < 2:
                    part = rotated(part, cos_ref[...], left_ref[...], right_ref[...], 1.0)
                if t == 0:
                    part = part * HEAD_DIM**-0.5
                start = t * width + g * LANES
                qkv_ref[:, start : start + LANES] = part.astype(BF16)
        else:
            columns = slice((t - 3) * width, (t - 2) * width)
            square = y * y
            turn = jnp.tanh(root * y * (1.0 + 0.044715 * square))
            half = 0.5 * (1.0 + turn)
            act_ref[:, columns] = (y * half).astype(BF16)
            slope = half * (1.0 + y * (1.0 - turn) * (root + (3.0 * 0.044715 * root) * square))
            slope_ref[:, columns] = slope.astype(BF16)


def project(sequence, x, blocks, bias, gain, shift, tables, width, tile, earlier, deps):
    (length, model), total, count = x.shape, blocks[0].shape[1], len(blocks)
    hidden, steps = total - 3 * width, length // tile
    rows = lambda w: pl.BlockSpec((tile, w), lambda i: (i, 0))
    out = lambda w: pl.BlockSpec((tile, w), lambda i: (sequence * steps + i, 0))
    line = lambda a: pl.BlockSpec(a.shape, lambda i: (0, 0))
    widths = (3 * width, hidden, hidden, model)
    operands = [x, bias, gain, shift, *tables, *blocks]
    return call(
        functools.partial(project_kernel, (count, width, hidden)),
        "project",
        operands + list(earlier),
        deps,
        grid=(steps,),
        in_specs=[rows(model), line(bias), line(gain), line(shift)]
        + [rows(LANES)] * 3
        + [HBM] * (count + len(earlier)),
        out_specs=[out(w) for w in widths],
        out_shape=[jax.ShapeDtypeStruct((2 * length, w), BF16) for w in widths],
        input_output_aliases={len(operands) + n: n for n in range(len(earlier))},
        scratch_shapes=[pltpu.VMEM((model, total), BF16), pltpu.SemaphoreType.DMA((count,))],
    )


def attend_kernel(block, q_ref, k_ref, v_ref, out_ref, lse_ref):
    length = q_ref.shape[0]
    lane = lax.broadcasted_iota(jnp.int32, (1, LANES), 1)
    key = lax.broadcasted_iota(jnp.int32, (block, block), 0)
    causal = key <= lax.broadcasted_iota(jnp.int32, (block, block), 1)
    for i in range(length // block):
        rows, before = pl.ds(i * block, block), pl.ds(0, i * block)
        results = []
        for h in range(2):
            mine = (lane < HEAD_DIM) if h == 0 else (lane >= HEAD_DIM)
            query = jnp.where(mine, q_ref[rows, :], 0)
            near = jnp.where(causal, dot(k_ref[rows, :], query, 1, 1), -1e30)
            highest = jnp.max(near, axis=0, keepdims=True)
            if i:
                far = dot(k_ref[before, :], query, 1, 1)
                highest = jnp.maximum(highest, jnp.max(far, axis=0, keepdims=True))
            near = jnp.exp(near - highest)
            total = jnp.sum(near, axis=0, keepdims=True)
            if i:
                far = jnp.exp(far - highest)
                total = total + jnp.sum(far, axis=0, keepdims=True)
            inverse = 1.0 / total
            result = dot((near * inverse).astype(BF16), v_ref[rows, :], 0, 0)
            if i:
                result = result + dot((far * inverse).astype(BF16), v_ref[before, :], 0, 0)
            results.append(result)
            lse_ref[0, h : h + 1, rows] = highest + jnp.log(total)
        out_ref[rows, :] = jnp.where(lane < HEAD_DIM, results[0], results[1]).astype(BF16)


def pair_specs(length, pairs):
    return lambda off: pl.BlockSpec(
        (length, LANES), lambda g: (g // pairs, off * pairs + g % pairs)
    )


def attend(qkv, length, block, deps):
    width, sequences = qkv.shape[1] // 3, qkv.shape[0] // length
    pairs = width // LANES
    at = pair_specs(length, pairs)
    return call(
        functools.partial(attend_kernel, block),
        "attend",
        [qkv, qkv, qkv],
        deps,
        grid=(sequences * pairs,),
        in_specs=[at(0), at(1), at(2)],
        out_specs=[at(0), pl.BlockSpec((1, 8, length), lambda g: (g, 0, 0))],
        out_shape=[
            jax.ShapeDtypeStruct((qkv.shape[0], width), BF16),
            jax.ShapeDtypeStruct((sequences * pairs, 8, length), F32),
        ],
    )


def attend_back_kernel(
    block,
    q_ref,
    k_ref,
    v_ref,
    grad_ref,
    mixed_ref,
    lse_ref,
    cos_ref,
    left_ref,
    right_ref,
    gq_ref,
    gk_ref,
    gv_ref,
    sum_ref,
    gk_sum,
    gv_sum,
):
    length = q_ref.shape[0]
    lane = lax.broadcasted_iota(jnp.int32, (1, LANES), 1)
    key = lax.broadcasted_iota(jnp.int32, (block, block), 0)
    causal = key <= lax.broadcasted_iota(jnp.int32, (block, block), 1)
    count = length // block
    sum_ref[...] = jnp.zeros_like(sum_ref)

    def put(ref, which, rows, value):
        value = value.astype(BF16)
        ref[rows, :] = value
        sum_ref[0, which : which + 1, :] += jnp.sum(value.astype(F32), axis=0, keepdims=True)

    def unrotated(value, rows):
        return rotated(value, cos_ref[rows, :], left_ref[rows, :], right_ref[rows, :], -1.0)

    for i in reversed(range(count)):
        rows = pl.ds(i * block, block)
        product = grad_ref[rows, :].astype(F32) * mixed_ref[rows, :].astype(F32)
        gq = None
        for h in range(2):
            mine = (lane < HEAD_DIM) if h == 0 else (lane >= HEAD_DIM)
            query = jnp.where(mine, q_ref[rows, :], 0)
            grad = jnp.where(mine, grad_ref[rows, :], 0)
            ones = jnp.where(mine, jnp.ones((8, LANES), F32), 0.0)
            delta = lax.dot_general(
                ones,
                product,
                (((1,), (1,)), ((), ())),
                precision=lax.Precision.HIGHEST,
                preferred_element_type=F32,
            )[0:1, :]
            lse = lse_ref[0, h : h + 1, rows]
            for j in range(i + 1):
                keys = pl.ds(j * block, block)
                key_rows = k_ref[keys, :]
                probs = jnp.exp(dot(key_rows, query, 1, 1) - lse)
                if j == i:
                    probs = jnp.where(causal, probs, 0.0)
                gprobs = dot(v_ref[keys, :], grad, 1, 1)
                gscores = (probs * (gprobs - delta)).astype(BF16)
                gv, gk = dot(probs.astype(BF16), grad, 1, 0), dot(gscores, query, 1, 0)
                if i == count - 1 and h == 0:
                    gv_sum[keys, :] = gv
                    gk_sum[keys, :] = gk
                else:
                    gv_sum[keys, :] += gv
                    gk_sum[keys, :] += gk
                part = dot(gscores, jnp.where(mine, key_rows, 0), 0, 0)
                gq = part if gq is None else gq + part
        put(gq_ref, 0, rows, unrotated(gq * HEAD_DIM**-0.5, rows))
    for i in range(count):
        rows = pl.ds(i * block, block)
        put(gk_ref, 1, rows, unrotated(gk_sum[rows, :], rows))
        put(gv_ref, 2, rows, gv_sum[rows, :])


def attend_back(sequence, qkv, grad, mixed, lse, tables, length, block, deps):
    width = qkv.shape[1] // 3
    pairs = width // LANES
    at = lambda off: pl.BlockSpec((length, LANES), lambda g: (sequence, off * pairs + g))
    out = pl.BlockSpec((length, LANES), lambda g: (0, g))
    table = pl.BlockSpec((length, LANES), lambda g: (0, 0))
    small = pl.BlockSpec((1, 8, length), lambda g: (sequence * pairs + g, 0, 0))
    return call(
        functools.partial(attend_back_kernel, block),
        "attend_back",
        [qkv, qkv, qkv, grad, mixed, lse, *tables],
        deps,
        grid=(pairs,),
        in_specs=[at(0), at(1), at(2), at(0), at(0), small, table, table, table],
        out_specs=[out] * 3 + [pl.BlockSpec((1, 8, LANES), lambda g: (g, 0, 0))],
        out_shape=[jax.ShapeDtypeStruct((length, width), BF16)] * 3
        + [jax.ShapeDtypeStruct((pairs, 8, LANES), F32)],
        scratch_shapes=[pltpu.VMEM((length, LANES), F32)] * 2,
    )


def by_sequence(tile, width, steps):
    return [
        pl.BlockSpec((tile, width), lambda i: (jnp.minimum(i, steps - 1), 0)),
        pl.BlockSpec((tile, width), lambda i: (jnp.maximum(i - steps, 0), 0)),
    ]


def other_first(tile, width, steps):
    return pl.BlockSpec((tile, width), lambda i: ((i + steps) % (2 * steps), 0))


def put_by_sequence(step, steps, value, other_ref, own_ref):
    @pl.when(step < steps)
    def _():
        other_ref[...] = value

    @pl.when(step >= steps)
    def _():
        own_ref[...] = value


def branch_kernel(count, steps, mixed_ref, act_ref, *rest):
    blocks, (other_ref, own_ref, held, sems) = rest[:count], rest[count:]
    step = pl.program_id(0)

    @pl.when(step == 0)
    def _():
        loads = block_copies(blocks, columns_at(held, blocks[0].shape[1]), sems)
        for copy in loads:
            copy.start()
        for copy in loads:
            copy.wait()

    x = jnp.concatenate([mixed_ref[...], act_ref[...]], axis=1)
    put_by_sequence(step, steps, dot(x, held[...], 1, 0).astype(BF16), other_ref, own_ref)


def branch_sums(mixed, act, blocks, tile, deps):
    length, count = mixed.shape[0] // 2, len(blocks)
    inner, model, steps = blocks[0].shape[0], count * blocks[0].shape[1], length // tile
    return call(
        functools.partial(branch_kernel, count, steps),
        "branch_sums",
        [mixed, act, *blocks],
        deps,
        grid=(2 * steps,),
        in_specs=[other_first(tile, a.shape[1], steps) for a in (mixed, act)] + [HBM] * count,
        out_specs=by_sequence(tile, model, steps),
        out_shape=[jax.ShapeDtypeStruct((length, model), BF16)] * 2,
        scratch_shapes=[pltpu.VMEM((inner, model), BF16), pltpu.SemaphoreType.DMA((count,))],
    )


def grad_in_kernel(setup, dy_ref, slope_ref, *rest):
    count, width, hidden = setup
    blocks = rest[:count]
    gmixed_ref, gpre_ref, gsum_ref, dsum_ref, held, sems = rest[-6:]

    @pl.when(pl.program_id(0) == 0)
    def _():
        loads = block_copies(blocks, columns_at(held, blocks[0].shape[1]), sems)
        for copy in loads:
            copy.start()
        gsum_ref[...] = jnp.zeros_like(gsum_ref)
        dsum_ref[...] = jnp.zeros_like(dsum_ref)
        for copy in loads:
            copy.wait()

    dy = dy_ref[...]
    gmixed_ref[...] = dot(dy, held[:width, :], 1, 1).astype(BF16)
    for start in range(0, hidden, width):
        part = slice(start, start + width)
        gact = dot(dy, held[width + start : 2 * width + start, :], 1, 1)
        gpre = (gact * slope_ref[:, part].astype(F32)).astype(BF16)
        gpre_ref[:, part] = gpre
        gsum_ref[0:1, part] += jnp.sum(gpre.astype(F32), axis=0, keepdims=True)
    dsum_ref[0:1, :] += jnp.sum(dy.astype(F32), axis=0, keepdims=True)


def grad_in(sequence, dy, slope, blocks, width, tile, earlier, deps):
    (length, model), hidden, count = dy.shape, slope.shape[1], len(blocks)
    steps = length // tile
    at = lambda w: pl.BlockSpec((tile, w), lambda i: (sequence * steps + i, 0))
    total = lambda w: pl.BlockSpec((8, w), lambda i: (0, 0))
    operands = [dy, slope, *blocks]
    return call(
        functools.partial(grad_in_kernel, (count, width, hidden)),
        "grad_in",
        operands + list(earlier),
        deps,
        grid=(steps,),
        in_specs=[pl.BlockSpec((tile, model), lambda i: (i, 0)), at(hidden)]
        + [HBM] * (count + len(earlier)),
        out_specs=[
            at(width),
            pl.BlockSpec((tile, hidden), lambda i: (i, 0)),
            total(hidden),
            total(model),
        ],
        out_shape=[
            jax.ShapeDtypeStruct((2 * length, width), BF16),
            jax.ShapeDtypeStruct((length, hidden), BF16),
            jax.ShapeDtypeStruct((8, hidden), F32),
            jax.ShapeDtypeStruct((8, model), F32),
        ],
        input_output_aliases={len(operands) + n: n for n in range(len(earlier))},
        scratch_shapes=[
            pltpu.VMEM((width + hidden, model), BF16),
            pltpu.SemaphoreType.DMA((count,)),
        ],
    )


def add_kernel(a_ref, b_ref, out_ref):
    out_ref[...] = (a_ref[...].astype(F32) + b_ref[...].astype(F32)).astype(BF16)


def add_rows(a, b):
    rows = pl.BlockSpec((a.shape[0] // 2, a.shape[1]), lambda i: (i, 0))
    return call(
        add_kernel,
        "add_rows",
        [a, b],
        grid=(2,),
        in_specs=[rows, rows],
        out_specs=rows,
        out_shape=jax.ShapeDtypeStruct(a.shape, BF16),
    )


def grad_normed_kernel(count, half, x_ref, *rest):
    grads, blocks, (out_ref, sum_ref, held, sems) = rest[:8], rest[8 : 8 + 2 * count], rest[-4:]
    (size, total), few, me = blocks[0].shape, count // 2, lax.axis_index("dp")

    @pl.when(pl.program_id(0) == 0)
    def _():
        for start in (True, False):
            for n, block in enumerate(blocks):
                core, j = n // count, n % count
                owner = lax.bitwise_xor(me, j ^ core) - half * few
                columns = slice(core * total, (core + 1) * total)

                @pl.when((owner >= 0) & (owner < few))
                def _(start=start, n=n, block=block, owner=owner, columns=columns):
                    target = held.at[span(owner, size), columns]
                    copy = pltpu.make_async_copy(block, target, sems.at[n])
                    if start:
                        copy.start()
                    else:
                        copy.wait()

        sum_ref[...] = jnp.zeros_like(sum_ref)

    columns = slice(half * few * size, (half + 1) * few * size)
    normal = normalized(x_ref[...])[:, columns]
    g = jnp.concatenate([ref[...] for ref in grads], axis=1)
    result = dot(g, held[...], 1, 1)
    sum_ref[0:1, :] += jnp.sum(result * normal, axis=0, keepdims=True)
    sum_ref[1:2, :] += jnp.sum(result, axis=0, keepdims=True)
    out_ref[...] = result.astype(BF16)


def grad_normed_sums(half, grads, x, blocks, tile, deps, adds=()):
    (length, model), count, total = x.shape, len(blocks) // 2, blocks[0].shape[1]
    part = model // 2
    rows = lambda w: pl.BlockSpec((tile, w), lambda i: (i, 0))
    return call(
        functools.partial(grad_normed_kernel, count, half),
        "grad_normed_sums",
        [x, *grads, *blocks],
        deps,
        adds=adds,
        grid=(length // tile,),
        in_specs=[rows(model)] + [rows(g.shape[1]) for g in grads] + [HBM] * (2 * count),
        out_specs=[rows(part), pl.BlockSpec((8, part), lambda i: (0, 0))],
        out_shape=[
            jax.ShapeDtypeStruct((length, part), BF16),
            jax.ShapeDtypeStruct((8, part), F32),
        ],
        scratch_shapes=[
            pltpu.VMEM((part, 2 * total), BF16),
            pltpu.SemaphoreType.DMA((2 * count,)),
        ],
    )


def weight_grad_kernel(writes, left, rows, many, groups, at_ref, *refs):
    cuts, (*refs, held, grad, sems) = refs[:many], refs[many:]
    whole, outs = refs[: len(refs) - len(writes)], refs[len(refs) - len(writes) :]
    step, core, loads, first = pl.program_id(0), lax.rem(lax.axis_index("dp"), 2), [], 0
    for group in groups:
        below = 0
        for ref in whole[:group]:
            columns = pl.ds(first, ref.shape[1])
            for start in range(0, ref.shape[0], rows):
                target = held.at[pl.ds(below + start, rows), columns]
                loads.append((ref.at[pl.ds(start, rows)], target))
            below += ref.shape[0]
        first += whole[0].shape[1]
        whole = whole[group:]
    loads = [pltpu.make_async_copy(*pair, sems.at[n]) for n, pair in enumerate(loads)]

    @pl.when(step == 0)
    def _():
        for copy in loads:
            copy.start()
        for copy in loads:
            copy.wait()

    cut = jnp.concatenate([ref[...] for ref in cuts], axis=0)
    pair = (cut, held[...]) if left else (held[...], cut)
    grad[...] = dot(*pair, 0, 0).astype(BF16)
    size = cut.shape[1] // 2
    for half, steps, out_ref in writes_of(writes, outs):
        here = functools.reduce(jnp.logical_or, [step == s for s in steps])

        @pl.when(here)
        def _(half=half, out_ref=out_ref):
            mine = span(core if half == 0 else 1 - core, size)
            out_ref[0] = grad[mine, :] if left else grad[:, mine]


def writes_of(writes, outs):
    return [(half, steps, out) for (half, steps), out in zip(writes, outs)]


def weight_grads(me, xs, gs, count, deps, left, adds=()):
    plan, chips = scatter_plan(count), count // 2
    order = [j // 2 for s in plan[0] for j in s]
    sets = [(half, s) for s in range(len(plan[0])) for half in range(2)]
    writes = [(half, [order.index(j // 2) for j in plan[half][s]]) for half, s in sets]
    table = []
    for _, steps in writes:
        for i in range(chips):
            later = [w for w in steps if w >= i]
            table.append(steps.index(min(later) if later else max(steps)))
    owners = lax.bitwise_xor(me // 2, jnp.array(order, jnp.int32))
    at = jnp.concatenate([owners, jnp.array(table, jnp.int32)])
    cut, whole = (xs, gs) if left else (gs, xs)
    groups, length = [len(g) for g in whole], sum(a.shape[0] for a in whole[0])
    size, full = cut[0].shape[1] // count, sum(g[0].shape[1] for g in whole)
    shape, whole = (size, full) if left else (full, size), [a for g in whole for a in g]
    rows = length // 4
    pieces = 4 * len(groups)

    def out(n):
        return pl.BlockSpec((1, *shape), lambda i, at: (at[chips * (n + 1) + i], 0, 0))

    outs = call(
        functools.partial(weight_grad_kernel, writes, left, rows, len(cut), groups),
        "weight_grads",
        [*cut, *whole],
        deps,
        (at,),
        adds,
        grid=(chips,),
        in_specs=[pl.BlockSpec((a.shape[0], 2 * size), lambda i, at: (0, at[i])) for a in cut]
        + [HBM] * len(whole),
        out_specs=[out(n) for n in range(len(sets))],
        out_shape=[
            jax.ShapeDtypeStruct((len(plan[half][s]), *shape), BF16) for half, s in sets
        ],
        scratch_shapes=[
            pltpu.VMEM((length, full), BF16),
            pltpu.VMEM((2 * size, full) if left else (full, 2 * size), BF16),
            pltpu.SemaphoreType.DMA((pieces,)),
        ],
    )
    blocks = [[o for o, (half, _) in zip(outs, sets) if half == h] for h in range(2)]
    return (blocks, *outs[len(sets) :]) if adds else blocks


def finish_kernel(sizes, width, *refs):
    ins, (up_ref, qkv_ref, dense_ref, down_ref) = refs[:-4], refs[-4:]
    core = lax.rem(lax.axis_index("dp"), 2)
    pairs = []
    for size in sizes:
        mine = sum(ref[0].astype(F32) for ref in ins[: size - 1])
        pairs.append(((core, mine), (1 - core, ins[size - 1][0].astype(F32))))
        ins = ins[size:]
    for where, value in pairs[0]:
        up_ref[:, span(where, value.shape[1])] = value
    for where, value in pairs[1]:
        for c in range(3):
            qkv_ref[c, :, span(where, width)] = value[:, c * width : (c + 1) * width]
    for out_ref, pair in ((dense_ref, pairs[2]), (down_ref, pairs[3])):
        for where, value in pair:
            out_ref[where] = value


def finish(up, qkv, columns):
    (size, hidden), width = up[1].shape, qkv[1].shape[1] // 3
    steps = hidden // width
    operands, specs, sizes = [], [], []

    def take(parts, rows, base):
        addends, theirs = parts
        for array, first in [*addends, (theirs[None], 0)]:
            operands.append(array)
            specs.append(
                pl.BlockSpec(
                    (1, rows, array.shape[2]), lambda i, first=first: (first, base + i, 0)
                )
            )
        sizes.append(len(addends) + 1)

    take(up, size // steps, 0)
    take(qkv, size // steps, 0)
    take(columns, width // steps, 0)
    take(columns, width, 1)
    owned_up, owned_qkv, owned_dense, owned_down = call(
        lambda *refs: finish_kernel(sizes, width, *refs),
        "finish",
        operands,
        grid=(steps,),
        in_specs=specs,
        out_specs=[
            pl.BlockSpec((size // steps, 2 * hidden), lambda i: (i, 0)),
            pl.BlockSpec((3, size // steps, 2 * width), lambda i: (0, i, 0)),
            pl.BlockSpec((2, width // steps, size), lambda i: (0, i, 0)),
            pl.BlockSpec((2, width, size), lambda i: (0, i, 0)),
        ],
        out_shape=[
            jax.ShapeDtypeStruct((size, 2 * hidden), F32),
            jax.ShapeDtypeStruct((3, size, 2 * width), F32),
            jax.ShapeDtypeStruct((2, width, size), F32),
            jax.ShapeDtypeStruct((2, hidden, size), F32),
        ],
    )
    return (
        owned_up,
        owned_qkv,
        owned_dense.reshape(2 * width, size),
        owned_down.reshape(2 * hidden, size),
    )


def norm_back_kernel(tokens_ref, dy_ref, gain_ref, left_ref, right_ref, out_ref):
    x = tokens_ref[...].astype(F32)
    centered = x - jnp.mean(x, axis=1, keepdims=True)
    inverse_std = lax.rsqrt(jnp.mean(centered * centered, axis=1, keepdims=True) + EPS)
    normal = centered * inverse_std
    grad = jnp.concatenate([left_ref[...], right_ref[...]], axis=1).astype(F32)
    scaled = grad * gain_ref[...]
    first_mean = jnp.mean(scaled, axis=1, keepdims=True)
    second_mean = jnp.mean(scaled * normal, axis=1, keepdims=True)
    back = (scaled - first_mean - normal * second_mean) * inverse_std
    out_ref[...] = (dy_ref[...].astype(F32) + back).astype(BF16)


def norm_back(tokens, dy, gain, halves, deps):
    rows, model = tokens.shape
    tile = min(128, rows)
    part = lambda w: pl.BlockSpec((tile, w), lambda i: (i, 0))
    return call(
        norm_back_kernel,
        "norm_back",
        [tokens, dy, gain, *halves],
        deps,
        grid=(rows // tile,),
        in_specs=[part(model), part(model), pl.BlockSpec((1, model), lambda i: (0, 0))]
        + [part(model // 2)] * 2,
        out_specs=part(model),
        out_shape=jax.ShapeDtypeStruct((rows, model), BF16),
    )


def across(value, bit, count):
    return lax.ppermute(value, "dp", [(i, i ^ bit) for i in range(count)])


def added(addends):
    return sum(a.astype(F32) for a in addends).astype(BF16)


def pair_sum(parts):
    while len(parts) > 1:
        parts = [a + b for a, b in zip(parts[::2], parts[1::2])]
    return parts[0]


def chip_bits(count):
    bits, bit = [], 2
    while bit < count:
        bits.append(bit)
        bit *= 2
    return bits


class BlockGather:
    def __init__(self, own, sibling, count):
        self.held, self.count = {0: own, 1: sibling}, count
        self.orders = (chip_bits(count), chip_bits(count)[::-1])

    def own_to(self, s):
        if s < len(self.orders[0]):
            for half in range(2):
                bit = self.orders[half][s]
                self.held[half ^ bit] = across(self.held[half], bit, self.count)

    def rest(self):
        for s in range(1, len(self.orders[0])):
            for half in range(2):
                order = self.orders[half]
                for j in [j for j in self.held if j % 2 == half]:
                    if j ^ order[s] not in self.held and not any(j & b for b in order[s:]):
                        self.held[j ^ order[s]] = across(self.held[j], order[s], self.count)

    def fenced(self, others=(), deps=()):
        keys = sorted(self.held)
        values = fence([self.held[j] for j in keys] + list(others), deps)
        self.held = dict(zip(keys, values))
        return values[len(keys) :]

    def blocks(self):
        return [self.held[j] for j in range(self.count)]


def scatter_orders(count):
    return (chip_bits(count)[::-1], chip_bits(count))


def scatter_plan(count):
    plan = []
    for half, order in enumerate(scatter_orders(count)):
        sets, rest = [[half]], [half]
        for bit in reversed(order):
            sets.insert(0, [j ^ bit for j in rest])
            rest = sets[0] + rest
        plan.append(sets)
    return plan


class BlockScatter:
    def __init__(self, halves, count):
        self.count, self.orders, self.plan = count, scatter_orders(count), scatter_plan(count)
        self.held = [[[(a, 0)] for a in arrays] for arrays in halves]
        self.steps = len(self.orders[0])

    def parts(self, half, s):
        many = len(self.plan[half][s])
        return [a[first : first + many] for a, first in self.held[half][s]]

    def total(self, half, s):
        if len(self.held[half][s]) > 1:
            self.held[half][s] = [(added(self.parts(half, s)), 0)]
        return self.parts(half, s)[0]

    def ready(self, s):
        return [self.total(half, s) for half in range(2)]

    def adds(self, s):
        return [(len(self.plan[half][s]), self.held[half][s]) for half in range(2)]

    def settle(self, s, sums):
        for half in range(2):
            self.held[half][s] = [(sums[half], 0)]

    def send(self, s):
        return [across(self.total(h, s), self.orders[h][s], self.count) for h in range(2)]

    def arrive(self, s, came):
        for half in range(2):
            first = 0
            for t in range(s + 1, len(self.plan[half])):
                self.held[half][t].append((came[half], first))
                first += len(self.plan[half][t])

    def between(self):
        for s in range(1, self.steps - 1):
            self.arrive(s, self.send(s))

    def last(self):
        return self.total(1, -1)[0]

    def kept(self):
        return self.held[0][-1]


def on_device(
    tokens,
    norm_gain,
    norm_bias,
    qkv_weight,
    qkv_bias,
    dense_weight,
    dense_bias,
    up_weight,
    up_bias,
    down_weight,
    down_bias,
    cotangent,
    *,
    ndp,
    nmp,
):
    me = lax.axis_index("dp")
    core = me % 2
    length, model = tokens.shape[0] * nmp, tokens.shape[1]
    tile, block = min(256, length), min(512, length)
    width, hidden = qkv_weight.shape[2] // 2, up_weight.shape[1] // 2
    chip_steps = len(chip_bits(ndp))
    rank = lambda array, axis, which, size: lax.dynamic_slice_in_dim(
        array, which * size, size, axis
    )

    def row_pack(which):
        qkv = rank(qkv_weight, 2, which, width)
        return jnp.concatenate([qkv[0], qkv[1], qkv[2], rank(up_weight, 1, which, hidden)], axis=1)

    def column_pack(which):
        return jnp.concatenate(
            [rank(dense_weight, 0, which, width), rank(down_weight, 0, which, hidden)], axis=0
        )

    pairs = width // LANES
    swap = lambda array: across(array, 1, ndp)
    line_gather = lambda array: lax.all_gather(array, "mp", axis=0, tiled=True)
    line_scatter = lambda array: lax.psum_scatter(array, "mp", scatter_dimension=0, tiled=True)
    x_own, dy_own = line_gather(tokens), line_gather(cotangent)
    rows = BlockGather(row_pack(core), swap(row_pack(1 - core)), ndp)
    columns = BlockGather(column_pack(core), swap(column_pack(1 - core)), ndp)
    rows.own_to(0)
    rows.fenced(deps=columns.held.values())
    rows.own_to(1)
    rows.fenced()
    rows.rest()
    x_own, *held = fence([x_own, columns.held[0], columns.held[1]], rows.blocks())
    columns.held = dict(enumerate(held))

    tables = rotary_tables(length)
    bias = jnp.concatenate(
        [
            rank(qkv_bias, 1, core, width).astype(F32).reshape(1, 3 * width),
            rank(up_bias[None, :], 1, core, hidden).astype(F32),
        ],
        axis=1,
    )
    gain, shift = norm_gain.astype(F32)[None, :], norm_bias.astype(F32)[None, :]
    x_other = swap(x_own)
    columns.own_to(0)
    common = (rows.blocks(), bias, gain, shift, tables, width, tile)
    first = project(0, x_own, *common, (), [columns.held[0]])
    (x_other,) = columns.fenced([x_other], [first[0]])
    columns.own_to(1)
    qkv, act, slope, normed = project(1, x_other, *common, first, [columns.held[0]])
    held = columns.fenced(rows.blocks(), [qkv])
    columns.rest()
    row_blocks, row_others = held, [swap(a) for a in held[:3]]
    mixed, lse = attend(qkv, length, block, [columns.held[0]])
    row_others = columns.fenced(row_others, [mixed])
    row_blocks[3:] = fence(row_blocks[3:], [row_others[0]])
    row_others += [swap(a) for a in row_blocks[3:]]
    other_sums, own_sums = branch_sums(mixed, act, columns.blocks(), tile, [row_blocks[3]])
    other_sums, dy_own, *row_others[3:] = fence([other_sums, dy_own, *row_others[3:]], [own_sums])
    theirs = swap(other_sums)
    dy_other = swap(dy_own)

    grads = (slope, columns.blocks(), width, tile)
    gmixed, gpre_own, *grad_a = grad_in(0, dy_own, *grads, (), [own_sums])
    theirs, dy_other = fence([theirs, dy_other], [grad_a[0]])
    total = add_rows(own_sums, theirs)
    branches = line_scatter(total)
    gmixed, gpre_other, *grad_b = grad_in(1, dy_other, *grads, [gmixed], [total])
    (gpre_sent,) = fence([gpre_other])
    gpre_came = swap(gpre_sent)
    column_grads = BlockScatter(
        weight_grads(me, [[mixed], [act]], [dy_own, dy_other], ndp, [gpre_sent], left=False), ndp
    )
    (gpre_came,) = fence([gpre_came], [column_grads.held[0][0][0][0]])
    column_came = column_grads.send(0)
    back = lambda sequence, deps: attend_back(
        sequence, qkv, gmixed, mixed, lse, tables, length, block, deps
    )
    *other, qkv_sums_b = back(1, [gpre_came])
    came = [swap(a) for a in other]
    *own, qkv_sums_a = back(0, [other[0]])
    came = fence([*came, *column_came], [own[0]])
    column_came, came = came[3:], came[:3]
    column_grads.arrive(0, column_came)
    column_grads.between()
    all_grads = [*own, gpre_own, *came, gpre_came]

    def normed_half(half, deps, adds=()):
        return grad_normed_sums(
            half, all_grads, x_own, [*row_blocks, *row_others], tile, deps, adds
        )

    total_a, sums_a, *settled = normed_half(0, [], column_grads.adds(chip_steps - 1))
    column_grads.settle(chip_steps - 1, settled)
    half_a = line_scatter(total_a)
    column_came = column_grads.send(chip_steps - 1)
    up_grads = BlockScatter(
        weight_grads(me, [normed], [[gpre_own, gpre_sent]], ndp, [sums_a], left=True), ndp
    )
    c0, c1, branches, u0, u1 = fence(
        [*column_came, branches, *(up_grads.held[h][0][0][0] for h in range(2))]
    )
    up_grads.held[0][0], up_grads.held[1][0] = [(u0, 0)], [(u1, 0)]
    up_came = up_grads.send(0)
    column_grads.arrive(chip_steps - 1, [c0, c1])
    blocks, column_last = weight_grads(
        me,
        [normed],
        [[a, b] for a, b in zip(own, other)],
        ndp,
        [c0],
        True,
        [column_grads.adds(len(column_grads.plan[1]) - 1)[1]],
    )
    qkv_grads = BlockScatter(blocks, ndp)
    qkv_came = qkv_grads.send(0)
    column_theirs = swap(column_last[0])
    total_b, sums_b = normed_half(1, [qkv_grads.held[0][0][0][0]])
    half_b = line_scatter(total_b)
    u0, u1, q0, q1, half_a = fence([*up_came, *qkv_came, half_a], [sums_b, column_theirs])
    up_grads.arrive(0, [u0, u1])
    qkv_grads.arrive(0, [q0, q1])
    up_grads.between()
    qkv_grads.between()
    up_came, qkv_came = up_grads.send(chip_steps - 1), qkv_grads.send(chip_steps - 1)
    u0, u1, q0, q1, branches, sums_b, column_theirs = fence(
        [*up_came, *qkv_came, branches, sums_b, column_theirs]
    )
    up_grads.arrive(chip_steps - 1, [u0, u1])
    qkv_grads.arrive(chip_steps - 1, [q0, q1])
    up_theirs = swap(up_grads.last())
    qkv_theirs = swap(qkv_grads.last())
    qkv_sum = (qkv_sums_a + qkv_sums_b)[:, :3, :].transpose(1, 0, 2).reshape(3 * width)
    norm_sums = jnp.concatenate([sums_a[:2], sums_b[:2]], axis=1)
    small = jnp.concatenate(
        [
            norm_sums.reshape(2 * model),
            qkv_sum,
            grad_a[0][0] + grad_b[0][0],
            grad_a[1][0] + grad_b[1][0],
        ]
    )
    small = pair_sum([small] + [across(small, j, ndp) for j in range(2, ndp, 2)])
    owned_up, owned_qkv, owned_dense, owned_down = finish(
        (up_grads.kept(), up_theirs),
        (qkv_grads.kept(), qkv_theirs),
        (column_grads.kept(), column_theirs),
    )
    small, half_b = fence([small, half_b], [owned_up])
    small_other = swap(small)
    grad_tokens = norm_back(tokens, cotangent, gain, [half_a, half_b], [small_other])
    norm_sums = small[: 2 * model] + small_other[: 2 * model]
    norm_sums = [norm_sums] + [
        lax.ppermute(norm_sums, "mp", [(i, i ^ j) for i in range(nmp)]) for j in range(1, nmp)
    ]
    while len(norm_sums) > 1:
        norm_sums = [a + b for a, b in zip(norm_sums[::2], norm_sums[1::2])]
    norm_sums = norm_sums[0]

    output = (
        tokens.astype(F32)
        + branches.astype(F32)
        + (dense_bias.astype(F32) + down_bias.astype(F32))[None, :]
    ).astype(BF16)

    inner = 3 * width + hidden
    grad_out_bias = small[2 * model + inner :]
    here, there = (a[2 * model : 2 * model + inner] for a in (small, small_other))
    even, odd = jnp.where(core == 0, here, there), jnp.where(core == 0, there, here)
    grad_qkv_bias = jnp.concatenate(
        [a[: 3 * width].reshape(3, width) for a in (even, odd)], axis=1
    )
    grad_up_bias = jnp.concatenate([even[3 * width :], odd[3 * width :]])

    return (
        output,
        grad_tokens,
        norm_sums[:model],
        norm_sums[model:],
        owned_qkv,
        grad_qkv_bias,
        owned_dense,
        grad_out_bias,
        owned_up,
        grad_up_bias,
        owned_down,
        grad_out_bias,
    )


def solution(mesh):
    return jax.shard_map(
        functools.partial(on_device, ndp=mesh.shape["dp"], nmp=mesh.shape["mp"]),
        mesh=mesh,
        in_specs=(
            P(("dp", "mp"), None),
            P(),
            P(),
            P(None, "dp", "mp"),
            P(None, "mp"),
            P("mp", "dp"),
            P(),
            P("dp", "mp"),
            P("mp"),
            P("mp", "dp"),
            P(),
            P(("dp", "mp"), None),
        ),
        out_specs=(
            P(("dp", "mp"), None),
            P(("dp", "mp"), None),
            P(),
            P(),
            P(None, "dp", "mp"),
            P(None, "mp"),
            P("mp", "dp"),
            P(),
            P("dp", "mp"),
            P("mp"),
            P("mp", "dp"),
            P(),
        ),
        check_vma=False,
    )
```

```python
import functools

import jax
import jax.numpy as jnp
import numpy as np
from jax import lax
from jax.experimental import pallas as pl
from jax.experimental.pallas import tpu as pltpu
from jax.sharding import PartitionSpec as P

HEAD_DIM = 64
ROT = 32
EPS = 1e-05
LANES = 128
F32 = jnp.float32
BF16 = jnp.bfloat16
HBM = pl.BlockSpec(memory_space=pltpu.HBM)


def dot(lhs, rhs, lhs_dim, rhs_dim):
    return lax.dot_general(
        lhs, rhs, (((lhs_dim,), (rhs_dim,)), ((), ())), preferred_element_type=F32
    )


def call(kernel, name, operands, deps=(), scalars=(), adds=(), vmem=64, **spec):
    deps, out_shape = tuple(deps), spec.pop("out_shape")
    single = not isinstance(out_shape, list)
    out_shape = [out_shape] if single else out_shape
    out_specs = spec.pop("out_specs")
    out_specs = [out_specs] if single else list(out_specs)
    extra, extra_specs, sizes = [], [], []
    steps = spec["grid"][0] if adds else 1
    for many, addends in adds:
        _, rows, columns = addends[0][0].shape
        block = (many, rows // steps, columns)
        for array, first in addends:
            extra.append(array)
            extra_specs.append(
                pl.BlockSpec(block, lambda i, *at, first=first, many=many: (first // many, i, 0))
            )
        out_shape = out_shape + [jax.ShapeDtypeStruct((many, rows, columns), BF16)]
        out_specs = out_specs + [pl.BlockSpec(block, lambda i, *at: (0, i, 0))]
        sizes.append(len(addends))
    lead, outs = len(scalars) + len(operands), len(out_shape) - len(adds)

    def body(*refs):
        first = lead + len(extra) + len(deps)
        kernel(*refs[:lead], *refs[first : first + outs], *refs[first + outs + len(adds) :])
        sources = refs[lead : lead + len(extra)]
        for n, out in zip(sizes, refs[first + outs : first + outs + len(adds)]):
            out[...] = sum(ref[...].astype(F32) for ref in sources[:n]).astype(BF16)
            sources = sources[n:]

    in_specs = list(spec.pop("in_specs")) + extra_specs + [HBM] * len(deps)
    aliases = spec.pop("input_output_aliases", {})
    if scalars:
        grid_spec = pltpu.PrefetchScalarGridSpec(
            num_scalar_prefetch=len(scalars), in_specs=in_specs, out_specs=out_specs, **spec
        )
        spec = {"grid_spec": grid_spec}
    else:
        spec.update(in_specs=in_specs, out_specs=out_specs)
    results = pl.pallas_call(
        body,
        out_shape=out_shape,
        input_output_aliases=aliases,
        compiler_params=pltpu.CompilerParams(vmem_limit_bytes=vmem << 20),
        cost_estimate=pl.CostEstimate(flops=0, transcendentals=0, bytes_accessed=0),
        name=name,
        **spec,
    )(*scalars, *operands, *extra, *deps)
    return results[0] if single and not adds else results


def fence(values, deps=()):
    return list(
        call(
            lambda *refs: None,
            "fence",
            values,
            deps,
            in_specs=[HBM] * len(values),
            out_specs=[HBM] * len(values),
            out_shape=[jax.ShapeDtypeStruct(v.shape, v.dtype) for v in values],
            input_output_aliases={n: n for n in range(len(values))},
        )
    )


def rotary_tables(length):
    positions = np.arange(length, dtype=np.float32)
    frequency = 10000.0 ** (-np.arange(ROT // 2, dtype=np.float64) * 2.0 / ROT)
    angles = positions[:, None] * frequency.astype(np.float32)[None, :]
    cosine, sine = np.cos(angles.astype(np.float64)), np.sin(angles.astype(np.float64))
    rest = HEAD_DIM - ROT
    none = np.zeros((length, ROT // 2))
    ones, zeros = np.ones((length, rest)), np.zeros((length, rest))
    straight = np.concatenate([cosine, cosine, ones], axis=1)
    left = np.concatenate([-sine, none, zeros], axis=1)
    right = np.concatenate([none, sine, zeros], axis=1)
    return [
        jnp.asarray(np.concatenate([t, t], axis=1).astype(np.float32))
        for t in (straight, left, right)
    ]


def rotated(u, straight, left, right, sign):
    half = ROT // 2
    turned = pltpu.roll(u, LANES - half, 1) * left + pltpu.roll(u, half, 1) * right
    return u * straight + sign * turned


def normalized(x):
    x = x.astype(F32)
    centered = x - jnp.mean(x, axis=1, keepdims=True)
    variance = jnp.mean(centered * centered, axis=1, keepdims=True)
    return centered * lax.rsqrt(variance + EPS)


def block_copies(blocks, place, sems):
    me = lax.axis_index("dp")
    return [
        pltpu.make_async_copy(block, place(lax.bitwise_xor(me, j)), sems.at[j])
        for j, block in enumerate(blocks)
    ]


def span(owner, size):
    return pl.ds(pl.multiple_of(owner * size, size), size)


def rows_at(ref, size):
    return lambda owner: ref.at[pl.ds(pl.multiple_of(owner * size, size), size)]


def columns_at(ref, size):
    return lambda owner: ref.at[:, pl.ds(pl.multiple_of(owner * size, size), size)]


def project_kernel(setup, x_ref, bias_ref, gain_ref, shift_ref, cos_ref, left_ref, right_ref, *rest):
    count, width, hidden = setup
    blocks = rest[:count]
    qkv_ref, act_ref, slope_ref, normed_ref, held, sems = rest[-6:]

    @pl.when(pl.program_id(0) == 0)
    def _():
        loads = block_copies(blocks, rows_at(held, blocks[0].shape[0]), sems)
        for copy in loads:
            copy.start()
        for copy in loads:
            copy.wait()

    x = (normalized(x_ref[...]) * gain_ref[...] + shift_ref[...]).astype(BF16)
    normed_ref[...] = x
    root = 0.7978845608028654
    for t in range((3 * width + hidden) // width):
        columns = slice(t * width, (t + 1) * width)
        y = dot(x, held[:, columns], 1, 0) + bias_ref[:, columns]
        if t < 3:
            for g in range(width // LANES):
                part = y[:, g * LANES : (g + 1) * LANES]
                if t < 2:
                    part = rotated(part, cos_ref[...], left_ref[...], right_ref[...], 1.0)
                if t == 0:
                    part = part * HEAD_DIM**-0.5
                start = t * width + g * LANES
                qkv_ref[:, start : start + LANES] = part.astype(BF16)
        else:
            columns = slice((t - 3) * width, (t - 2) * width)
            square = y * y
            turn = jnp.tanh(root * y * (1.0 + 0.044715 * square))
            half = 0.5 * (1.0 + turn)
            act_ref[:, columns] = (y * half).astype(BF16)
            slope = half * (1.0 + y * (1.0 - turn) * (root + (3.0 * 0.044715 * root) * square))
            slope_ref[:, columns] = slope.astype(BF16)


def project(sequence, x, blocks, bias, gain, shift, tables, width, tile, earlier, deps):
    (length, model), total, count = x.shape, blocks[0].shape[1], len(blocks)
    hidden, steps = total - 3 * width, length // tile
    rows = lambda w: pl.BlockSpec((tile, w), lambda i: (i, 0))
    out = lambda w: pl.BlockSpec((tile, w), lambda i: (sequence * steps + i, 0))
    line = lambda a: pl.BlockSpec(a.shape, lambda i: (0, 0))
    widths = (3 * width, hidden, hidden, model)
    operands = [x, bias, gain, shift, *tables, *blocks]
    return call(
        functools.partial(project_kernel, (count, width, hidden)),
        "project",
        operands + list(earlier),
        deps,
        grid=(steps,),
        in_specs=[rows(model), line(bias), line(gain), line(shift)]
        + [rows(LANES)] * 3
        + [HBM] * (count + len(earlier)),
        out_specs=[out(w) for w in widths],
        out_shape=[jax.ShapeDtypeStruct((2 * length, w), BF16) for w in widths],
        input_output_aliases={len(operands) + n: n for n in range(len(earlier))},
        scratch_shapes=[pltpu.VMEM((model, total), BF16), pltpu.SemaphoreType.DMA((count,))],
    )


def attend_kernel(block, q_ref, k_ref, v_ref, out_ref, lse_ref):
    length = q_ref.shape[0]
    lane = lax.broadcasted_iota(jnp.int32, (1, LANES), 1)
    key = lax.broadcasted_iota(jnp.int32, (block, block), 0)
    causal = key <= lax.broadcasted_iota(jnp.int32, (block, block), 1)
    for i in range(length // block):
        rows, before = pl.ds(i * block, block), pl.ds(0, i * block)
        results = []
        for h in range(2):
            mine = (lane < HEAD_DIM) if h == 0 else (lane >= HEAD_DIM)
            query = jnp.where(mine, q_ref[rows, :], 0)
            near = jnp.where(causal, dot(k_ref[rows, :], query, 1, 1), -1e30)
            highest = jnp.max(near, axis=0, keepdims=True)
            if i:
                far = dot(k_ref[before, :], query, 1, 1)
                highest = jnp.maximum(highest, jnp.max(far, axis=0, keepdims=True))
            near = jnp.exp(near - highest)
            total = jnp.sum(near, axis=0, keepdims=True)
            if i:
                far = jnp.exp(far - highest)
                total = total + jnp.sum(far, axis=0, keepdims=True)
            inverse = 1.0 / total
            result = dot((near * inverse).astype(BF16), v_ref[rows, :], 0, 0)
            if i:
                result = result + dot((far * inverse).astype(BF16), v_ref[before, :], 0, 0)
            results.append(result)
            lse_ref[0, h : h + 1, rows] = highest + jnp.log(total)
        out_ref[rows, :] = jnp.where(lane < HEAD_DIM, results[0], results[1]).astype(BF16)


def pair_specs(length, pairs):
    return lambda off: pl.BlockSpec(
        (length, LANES), lambda g: (g // pairs, off * pairs + g % pairs)
    )


def attend(qkv, length, block, deps):
    width, sequences = qkv.shape[1] // 3, qkv.shape[0] // length
    pairs = width // LANES
    at = pair_specs(length, pairs)
    return call(
        functools.partial(attend_kernel, block),
        "attend",
        [qkv, qkv, qkv],
        deps,
        grid=(sequences * pairs,),
        in_specs=[at(0), at(1), at(2)],
        out_specs=[at(0), pl.BlockSpec((1, 8, length), lambda g: (g, 0, 0))],
        out_shape=[
            jax.ShapeDtypeStruct((qkv.shape[0], width), BF16),
            jax.ShapeDtypeStruct((sequences * pairs, 8, length), F32),
        ],
    )


def attend_back_kernel(
    block,
    q_ref,
    k_ref,
    v_ref,
    grad_ref,
    mixed_ref,
    lse_ref,
    cos_ref,
    left_ref,
    right_ref,
    gq_ref,
    gk_ref,
    gv_ref,
    sum_ref,
    gk_sum,
    gv_sum,
):
    length = q_ref.shape[0]
    lane = lax.broadcasted_iota(jnp.int32, (1, LANES), 1)
    key = lax.broadcasted_iota(jnp.int32, (block, block), 0)
    causal = key <= lax.broadcasted_iota(jnp.int32, (block, block), 1)
    count = length // block
    sum_ref[...] = jnp.zeros_like(sum_ref)

    def put(ref, which, rows, value):
        value = value.astype(BF16)
        ref[rows, :] = value
        sum_ref[0, which : which + 1, :] += jnp.sum(value.astype(F32), axis=0, keepdims=True)

    def unrotated(value, rows):
        return rotated(value, cos_ref[rows, :], left_ref[rows, :], right_ref[rows, :], -1.0)

    for i in reversed(range(count)):
        rows = pl.ds(i * block, block)
        product = grad_ref[rows, :].astype(F32) * mixed_ref[rows, :].astype(F32)
        gq = None
        for h in range(2):
            mine = (lane < HEAD_DIM) if h == 0 else (lane >= HEAD_DIM)
            query = jnp.where(mine, q_ref[rows, :], 0)
            grad = jnp.where(mine, grad_ref[rows, :], 0)
            ones = jnp.where(mine, jnp.ones((8, LANES), F32), 0.0)
            delta = lax.dot_general(
                ones,
                product,
                (((1,), (1,)), ((), ())),
                precision=lax.Precision.HIGHEST,
                preferred_element_type=F32,
            )[0:1, :]
            lse = lse_ref[0, h : h + 1, rows]
            for j in range(i + 1):
                keys = pl.ds(j * block, block)
                key_rows = k_ref[keys, :]
                probs = jnp.exp(dot(key_rows, query, 1, 1) - lse)
                if j == i:
                    probs = jnp.where(causal, probs, 0.0)
                gprobs = dot(v_ref[keys, :], grad, 1, 1)
                gscores = (probs * (gprobs - delta)).astype(BF16)
                gv, gk = dot(probs.astype(BF16), grad, 1, 0), dot(gscores, query, 1, 0)
                if i == count - 1 and h == 0:
                    gv_sum[keys, :] = gv
                    gk_sum[keys, :] = gk
                else:
                    gv_sum[keys, :] += gv
                    gk_sum[keys, :] += gk
                part = dot(gscores, jnp.where(mine, key_rows, 0), 0, 0)
                gq = part if gq is None else gq + part
        put(gq_ref, 0, rows, unrotated(gq * HEAD_DIM**-0.5, rows))
    for i in range(count):
        rows = pl.ds(i * block, block)
        put(gk_ref, 1, rows, unrotated(gk_sum[rows, :], rows))
        put(gv_ref, 2, rows, gv_sum[rows, :])


def attend_back(sequence, qkv, grad, mixed, lse, tables, length, block, deps):
    width = qkv.shape[1] // 3
    pairs = width // LANES
    at = lambda off: pl.BlockSpec((length, LANES), lambda g: (sequence, off * pairs + g))
    out = pl.BlockSpec((length, LANES), lambda g: (0, g))
    table = pl.BlockSpec((length, LANES), lambda g: (0, 0))
    small = pl.BlockSpec((1, 8, length), lambda g: (sequence * pairs + g, 0, 0))
    return call(
        functools.partial(attend_back_kernel, block),
        "attend_back",
        [qkv, qkv, qkv, grad, mixed, lse, *tables],
        deps,
        grid=(pairs,),
        in_specs=[at(0), at(1), at(2), at(0), at(0), small, table, table, table],
        out_specs=[out] * 3 + [pl.BlockSpec((1, 8, LANES), lambda g: (g, 0, 0))],
        out_shape=[jax.ShapeDtypeStruct((length, width), BF16)] * 3
        + [jax.ShapeDtypeStruct((pairs, 8, LANES), F32)],
        scratch_shapes=[pltpu.VMEM((length, LANES), F32)] * 2,
    )


def by_sequence(tile, width, steps):
    return [
        pl.BlockSpec((tile, width), lambda i: (jnp.minimum(i, steps - 1), 0)),
        pl.BlockSpec((tile, width), lambda i: (jnp.maximum(i - steps, 0), 0)),
    ]


def other_first(tile, width, steps):
    return pl.BlockSpec((tile, width), lambda i: ((i + steps) % (2 * steps), 0))


def put_by_sequence(step, steps, value, other_ref, own_ref):
    @pl.when(step < steps)
    def _():
        other_ref[...] = value

    @pl.when(step >= steps)
    def _():
        own_ref[...] = value


def branch_kernel(count, steps, mixed_ref, act_ref, *rest):
    blocks, (other_ref, own_ref, held, sems) = rest[:count], rest[count:]
    step = pl.program_id(0)

    @pl.when(step == 0)
    def _():
        loads = block_copies(blocks, columns_at(held, blocks[0].shape[1]), sems)
        for copy in loads:
            copy.start()
        for copy in loads:
            copy.wait()

    x = jnp.concatenate([mixed_ref[...], act_ref[...]], axis=1)
    put_by_sequence(step, steps, dot(x, held[...], 1, 0).astype(BF16), other_ref, own_ref)


def branch_sums(mixed, act, blocks, tile, deps):
    length, count = mixed.shape[0] // 2, len(blocks)
    inner, model, steps = blocks[0].shape[0], count * blocks[0].shape[1], length // tile
    return call(
        functools.partial(branch_kernel, count, steps),
        "branch_sums",
        [mixed, act, *blocks],
        deps,
        grid=(2 * steps,),
        in_specs=[other_first(tile, a.shape[1], steps) for a in (mixed, act)] + [HBM] * count,
        out_specs=by_sequence(tile, model, steps),
        out_shape=[jax.ShapeDtypeStruct((length, model), BF16)] * 2,
        scratch_shapes=[pltpu.VMEM((inner, model), BF16), pltpu.SemaphoreType.DMA((count,))],
    )


def grad_in_kernel(setup, dy_ref, slope_ref, *rest):
    count, width, hidden = setup
    blocks = rest[:count]
    gmixed_ref, gpre_ref, gsum_ref, dsum_ref, held, sems = rest[-6:]

    @pl.when(pl.program_id(0) == 0)
    def _():
        loads = block_copies(blocks, columns_at(held, blocks[0].shape[1]), sems)
        for copy in loads:
            copy.start()
        gsum_ref[...] = jnp.zeros_like(gsum_ref)
        dsum_ref[...] = jnp.zeros_like(dsum_ref)
        for copy in loads:
            copy.wait()

    dy = dy_ref[...]
    gmixed_ref[...] = dot(dy, held[:width, :], 1, 1).astype(BF16)
    for start in range(0, hidden, width):
        part = slice(start, start + width)
        gact = dot(dy, held[width + start : 2 * width + start, :], 1, 1)
        gpre = (gact * slope_ref[:, part].astype(F32)).astype(BF16)
        gpre_ref[:, part] = gpre
        gsum_ref[0:1, part] += jnp.sum(gpre.astype(F32), axis=0, keepdims=True)
    dsum_ref[0:1, :] += jnp.sum(dy.astype(F32), axis=0, keepdims=True)


def grad_in(sequence, dy, slope, blocks, width, tile, earlier, deps):
    (length, model), hidden, count = dy.shape, slope.shape[1], len(blocks)
    steps = length // tile
    at = lambda w: pl.BlockSpec((tile, w), lambda i: (sequence * steps + i, 0))
    total = lambda w: pl.BlockSpec((8, w), lambda i: (0, 0))
    operands = [dy, slope, *blocks]
    return call(
        functools.partial(grad_in_kernel, (count, width, hidden)),
        "grad_in",
        operands + list(earlier),
        deps,
        grid=(steps,),
        in_specs=[pl.BlockSpec((tile, model), lambda i: (i, 0)), at(hidden)]
        + [HBM] * (count + len(earlier)),
        out_specs=[
            at(width),
            pl.BlockSpec((tile, hidden), lambda i: (i, 0)),
            total(hidden),
            total(model),
        ],
        out_shape=[
            jax.ShapeDtypeStruct((2 * length, width), BF16),
            jax.ShapeDtypeStruct((length, hidden), BF16),
            jax.ShapeDtypeStruct((8, hidden), F32),
            jax.ShapeDtypeStruct((8, model), F32),
        ],
        input_output_aliases={len(operands) + n: n for n in range(len(earlier))},
        scratch_shapes=[
            pltpu.VMEM((width + hidden, model), BF16),
            pltpu.SemaphoreType.DMA((count,)),
        ],
    )


def add_kernel(a_ref, b_ref, out_ref):
    out_ref[...] = (a_ref[...].astype(F32) + b_ref[...].astype(F32)).astype(BF16)


def add_rows(a, b):
    rows = pl.BlockSpec((a.shape[0] // 2, a.shape[1]), lambda i: (i, 0))
    return call(
        add_kernel,
        "add_rows",
        [a, b],
        grid=(2,),
        in_specs=[rows, rows],
        out_specs=rows,
        out_shape=jax.ShapeDtypeStruct(a.shape, BF16),
    )


def grad_normed_kernel(count, half, x_ref, *rest):
    grads, blocks, (out_ref, sum_ref, held, sems) = rest[:8], rest[8 : 8 + 2 * count], rest[-4:]
    (size, total), few, me = blocks[0].shape, count // 2, lax.axis_index("dp")

    @pl.when(pl.program_id(0) == 0)
    def _():
        for start in (True, False):
            for n, block in enumerate(blocks):
                core, j = n // count, n % count
                owner = lax.bitwise_xor(me, j ^ core) - half * few
                columns = slice(core * total, (core + 1) * total)

                @pl.when((owner >= 0) & (owner < few))
                def _(start=start, n=n, block=block, owner=owner, columns=columns):
                    target = held.at[span(owner, size), columns]
                    copy = pltpu.make_async_copy(block, target, sems.at[n])
                    if start:
                        copy.start()
                    else:
                        copy.wait()

        sum_ref[...] = jnp.zeros_like(sum_ref)

    columns = slice(half * few * size, (half + 1) * few * size)
    normal = normalized(x_ref[...])[:, columns]
    g = jnp.concatenate([ref[...] for ref in grads], axis=1)
    result = dot(g, held[...], 1, 1)
    sum_ref[0:1, :] += jnp.sum(result * normal, axis=0, keepdims=True)
    sum_ref[1:2, :] += jnp.sum(result, axis=0, keepdims=True)
    out_ref[...] = result.astype(BF16)


def grad_normed_sums(half, grads, x, blocks, tile, deps, adds=()):
    (length, model), count, total = x.shape, len(blocks) // 2, blocks[0].shape[1]
    part = model // 2
    rows = lambda w: pl.BlockSpec((tile, w), lambda i: (i, 0))
    return call(
        functools.partial(grad_normed_kernel, count, half),
        "grad_normed_sums",
        [x, *grads, *blocks],
        deps,
        adds=adds,
        grid=(length // tile,),
        in_specs=[rows(model)] + [rows(g.shape[1]) for g in grads] + [HBM] * (2 * count),
        out_specs=[rows(part), pl.BlockSpec((8, part), lambda i: (0, 0))],
        out_shape=[
            jax.ShapeDtypeStruct((length, part), BF16),
            jax.ShapeDtypeStruct((8, part), F32),
        ],
        scratch_shapes=[
            pltpu.VMEM((part, 2 * total), BF16),
            pltpu.SemaphoreType.DMA((2 * count,)),
        ],
    )


def weight_grad_kernel(writes, left, rows, many, groups, at_ref, *refs):
    cuts, (*refs, held, grad, sems) = refs[:many], refs[many:]
    whole, outs = refs[: len(refs) - len(writes)], refs[len(refs) - len(writes) :]
    step, core, loads, first = pl.program_id(0), lax.rem(lax.axis_index("dp"), 2), [], 0
    for group in groups:
        below = 0
        for ref in whole[:group]:
            columns = pl.ds(first, ref.shape[1])
            for start in range(0, ref.shape[0], rows):
                target = held.at[pl.ds(below + start, rows), columns]
                loads.append((ref.at[pl.ds(start, rows)], target))
            below += ref.shape[0]
        first += whole[0].shape[1]
        whole = whole[group:]
    loads = [pltpu.make_async_copy(*pair, sems.at[n]) for n, pair in enumerate(loads)]

    @pl.when(step == 0)
    def _():
        for copy in loads:
            copy.start()
        for copy in loads:
            copy.wait()

    cut = jnp.concatenate([ref[...] for ref in cuts], axis=0)
    pair = (cut, held[...]) if left else (held[...], cut)
    grad[...] = dot(*pair, 0, 0).astype(BF16)
    size = cut.shape[1] // 2
    for half, steps, out_ref in writes_of(writes, outs):
        here = functools.reduce(jnp.logical_or, [step == s for s in steps])

        @pl.when(here)
        def _(half=half, out_ref=out_ref):
            mine = span(core if half == 0 else 1 - core, size)
            out_ref[0] = grad[mine, :] if left else grad[:, mine]


def writes_of(writes, outs):
    return [(half, steps, out) for (half, steps), out in zip(writes, outs)]


def weight_grads(me, xs, gs, count, deps, left, adds=()):
    plan, chips = scatter_plan(count), count // 2
    order = [j // 2 for s in plan[0] for j in s]
    sets = [(half, s) for s in range(len(plan[0])) for half in range(2)]
    writes = [(half, [order.index(j // 2) for j in plan[half][s]]) for half, s in sets]
    table = []
    for _, steps in writes:
        for i in range(chips):
            later = [w for w in steps if w >= i]
            table.append(steps.index(min(later) if later else max(steps)))
    owners = lax.bitwise_xor(me // 2, jnp.array(order, jnp.int32))
    at = jnp.concatenate([owners, jnp.array(table, jnp.int32)])
    cut, whole = (xs, gs) if left else (gs, xs)
    groups, length = [len(g) for g in whole], sum(a.shape[0] for a in whole[0])
    size, full = cut[0].shape[1] // count, sum(g[0].shape[1] for g in whole)
    shape, whole = (size, full) if left else (full, size), [a for g in whole for a in g]
    rows = length // 4
    pieces = 4 * len(groups)

    def out(n):
        return pl.BlockSpec((1, *shape), lambda i, at: (at[chips * (n + 1) + i], 0, 0))

    outs = call(
        functools.partial(weight_grad_kernel, writes, left, rows, len(cut), groups),
        "weight_grads",
        [*cut, *whole],
        deps,
        (at,),
        adds,
        grid=(chips,),
        in_specs=[pl.BlockSpec((a.shape[0], 2 * size), lambda i, at: (0, at[i])) for a in cut]
        + [HBM] * len(whole),
        out_specs=[out(n) for n in range(len(sets))],
        out_shape=[
            jax.ShapeDtypeStruct((len(plan[half][s]), *shape), BF16) for half, s in sets
        ],
        scratch_shapes=[
            pltpu.VMEM((length, full), BF16),
            pltpu.VMEM((2 * size, full) if left else (full, 2 * size), BF16),
            pltpu.SemaphoreType.DMA((pieces,)),
        ],
    )
    blocks = [[o for o, (half, _) in zip(outs, sets) if half == h] for h in range(2)]
    return (blocks, *outs[len(sets) :]) if adds else blocks


def finish_kernel(sizes, width, *refs):
    ins, (up_ref, qkv_ref, dense_ref, down_ref) = refs[:-4], refs[-4:]
    core = lax.rem(lax.axis_index("dp"), 2)
    pairs = []
    for size in sizes:
        mine = sum(ref[0].astype(F32) for ref in ins[: size - 1])
        pairs.append(((core, mine), (1 - core, ins[size - 1][0].astype(F32))))
        ins = ins[size:]
    for where, value in pairs[0]:
        up_ref[:, span(where, value.shape[1])] = value
    for where, value in pairs[1]:
        for c in range(3):
            qkv_ref[c, :, span(where, width)] = value[:, c * width : (c + 1) * width]
    for out_ref, pair in ((dense_ref, pairs[2]), (down_ref, pairs[3])):
        for where, value in pair:
            out_ref[where] = value


def finish(up, qkv, columns):
    (size, hidden), width = up[1].shape, qkv[1].shape[1] // 3
    steps = hidden // width
    operands, specs, sizes = [], [], []

    def take(parts, rows, base):
        addends, theirs = parts
        for array, first in [*addends, (theirs[None], 0)]:
            operands.append(array)
            specs.append(
                pl.BlockSpec(
                    (1, rows, array.shape[2]), lambda i, first=first: (first, base + i, 0)
                )
            )
        sizes.append(len(addends) + 1)

    take(up, size // steps, 0)
    take(qkv, size // steps, 0)
    take(columns, width // steps, 0)
    take(columns, width, 1)
    owned_up, owned_qkv, owned_dense, owned_down = call(
        lambda *refs: finish_kernel(sizes, width, *refs),
        "finish",
        operands,
        grid=(steps,),
        in_specs=specs,
        out_specs=[
            pl.BlockSpec((size // steps, 2 * hidden), lambda i: (i, 0)),
            pl.BlockSpec((3, size // steps, 2 * width), lambda i: (0, i, 0)),
            pl.BlockSpec((2, width // steps, size), lambda i: (0, i, 0)),
            pl.BlockSpec((2, width, size), lambda i: (0, i, 0)),
        ],
        out_shape=[
            jax.ShapeDtypeStruct((size, 2 * hidden), F32),
            jax.ShapeDtypeStruct((3, size, 2 * width), F32),
            jax.ShapeDtypeStruct((2, width, size), F32),
            jax.ShapeDtypeStruct((2, hidden, size), F32),
        ],
    )
    return (
        owned_up,
        owned_qkv,
        owned_dense.reshape(2 * width, size),
        owned_down.reshape(2 * hidden, size),
    )


def norm_back_kernel(tokens_ref, dy_ref, gain_ref, left_ref, right_ref, out_ref):
    x = tokens_ref[...].astype(F32)
    centered = x - jnp.mean(x, axis=1, keepdims=True)
    inverse_std = lax.rsqrt(jnp.mean(centered * centered, axis=1, keepdims=True) + EPS)
    normal = centered * inverse_std
    grad = jnp.concatenate([left_ref[...], right_ref[...]], axis=1).astype(F32)
    scaled = grad * gain_ref[...]
    first_mean = jnp.mean(scaled, axis=1, keepdims=True)
    second_mean = jnp.mean(scaled * normal, axis=1, keepdims=True)
    back = (scaled - first_mean - normal * second_mean) * inverse_std
    out_ref[...] = (dy_ref[...].astype(F32) + back).astype(BF16)


def norm_back(tokens, dy, gain, halves, deps):
    rows, model = tokens.shape
    tile = min(128, rows)
    part = lambda w: pl.BlockSpec((tile, w), lambda i: (i, 0))
    return call(
        norm_back_kernel,
        "norm_back",
        [tokens, dy, gain, *halves],
        deps,
        grid=(rows // tile,),
        in_specs=[part(model), part(model), pl.BlockSpec((1, model), lambda i: (0, 0))]
        + [part(model // 2)] * 2,
        out_specs=part(model),
        out_shape=jax.ShapeDtypeStruct((rows, model), BF16),
    )


def across(value, bit, count):
    return lax.ppermute(value, "dp", [(i, i ^ bit) for i in range(count)])


def added(addends):
    return sum(a.astype(F32) for a in addends).astype(BF16)


def pair_sum(parts):
    while len(parts) > 1:
        parts = [a + b for a, b in zip(parts[::2], parts[1::2])]
    return parts[0]


def chip_bits(count):
    bits, bit = [], 2
    while bit < count:
        bits.append(bit)
        bit *= 2
    return bits


class BlockGather:
    def __init__(self, own, sibling, count):
        self.held, self.count = {0: own, 1: sibling}, count
        self.orders = (chip_bits(count), chip_bits(count)[::-1])

    def own_to(self, s):
        if s < len(self.orders[0]):
            for half in range(2):
                bit = self.orders[half][s]
                self.held[half ^ bit] = across(self.held[half], bit, self.count)

    def rest(self):
        for s in range(1, len(self.orders[0])):
            for half in range(2):
                order = self.orders[half]
                for j in [j for j in self.held if j % 2 == half]:
                    if j ^ order[s] not in self.held and not any(j & b for b in order[s:]):
                        self.held[j ^ order[s]] = across(self.held[j], order[s], self.count)

    def fenced(self, others=(), deps=()):
        keys = sorted(self.held)
        values = fence([self.held[j] for j in keys] + list(others), deps)
        self.held = dict(zip(keys, values))
        return values[len(keys) :]

    def blocks(self):
        return [self.held[j] for j in range(self.count)]


def scatter_orders(count):
    return (chip_bits(count)[::-1], chip_bits(count))


def scatter_plan(count):
    plan = []
    for half, order in enumerate(scatter_orders(count)):
        sets, rest = [[half]], [half]
        for bit in reversed(order):
            sets.insert(0, [j ^ bit for j in rest])
            rest = sets[0] + rest
        plan.append(sets)
    return plan


class BlockScatter:
    def __init__(self, halves, count):
        self.count, self.orders, self.plan = count, scatter_orders(count), scatter_plan(count)
        self.held = [[[(a, 0)] for a in arrays] for arrays in halves]
        self.steps = len(self.orders[0])

    def parts(self, half, s):
        many = len(self.plan[half][s])
        return [a[first : first + many] for a, first in self.held[half][s]]

    def total(self, half, s):
        if len(self.held[half][s]) > 1:
            self.held[half][s] = [(added(self.parts(half, s)), 0)]
        return self.parts(half, s)[0]

    def ready(self, s):
        return [self.total(half, s) for half in range(2)]

    def adds(self, s):
        return [(len(self.plan[half][s]), self.held[half][s]) for half in range(2)]

    def settle(self, s, sums):
        for half in range(2):
            self.held[half][s] = [(sums[half], 0)]

    def send(self, s):
        return [across(self.total(h, s), self.orders[h][s], self.count) for h in range(2)]

    def arrive(self, s, came):
        for half in range(2):
            first = 0
            for t in range(s + 1, len(self.plan[half])):
                self.held[half][t].append((came[half], first))
                first += len(self.plan[half][t])

    def between(self):
        for s in range(1, self.steps - 1):
            self.arrive(s, self.send(s))

    def last(self):
        return self.total(1, -1)[0]

    def kept(self):
        return self.held[0][-1]


def on_device(
    tokens,
    norm_gain,
    norm_bias,
    qkv_weight,
    qkv_bias,
    dense_weight,
    dense_bias,
    up_weight,
    up_bias,
    down_weight,
    down_bias,
    cotangent,
    *,
    ndp,
    nmp,
):
    me = lax.axis_index("dp")
    core = me % 2
    length, model = tokens.shape[0] * nmp, tokens.shape[1]
    tile, block = min(256, length), min(512, length)
    width, hidden = qkv_weight.shape[2] // 2, up_weight.shape[1] // 2
    chip_steps = len(chip_bits(ndp))
    rank = lambda array, axis, which, size: lax.dynamic_slice_in_dim(
        array, which * size, size, axis
    )

    def row_pack(which):
        qkv = rank(qkv_weight, 2, which, width)
        return jnp.concatenate([qkv[0], qkv[1], qkv[2], rank(up_weight, 1, which, hidden)], axis=1)

    def column_pack(which):
        return jnp.concatenate(
            [rank(dense_weight, 0, which, width), rank(down_weight, 0, which, hidden)], axis=0
        )

    pairs = width // LANES
    swap = lambda array: across(array, 1, ndp)
    line_gather = lambda array: lax.all_gather(array, "mp", axis=0, tiled=True)
    line_scatter = lambda array: lax.psum_scatter(array, "mp", scatter_dimension=0, tiled=True)
    x_own, dy_own = line_gather(tokens), line_gather(cotangent)
    rows = BlockGather(row_pack(core), swap(row_pack(1 - core)), ndp)
    columns = BlockGather(column_pack(core), swap(column_pack(1 - core)), ndp)
    rows.own_to(0)
    rows.fenced(deps=columns.held.values())
    rows.own_to(1)
    rows.fenced()
    rows.rest()
    x_own, *held = fence([x_own, columns.held[0], columns.held[1]], rows.blocks())
    columns.held = dict(enumerate(held))

    tables = rotary_tables(length)
    bias = jnp.concatenate(
        [
            rank(qkv_bias, 1, core, width).astype(F32).reshape(1, 3 * width),
            rank(up_bias[None, :], 1, core, hidden).astype(F32),
        ],
        axis=1,
    )
    gain, shift = norm_gain.astype(F32)[None, :], norm_bias.astype(F32)[None, :]
    x_other = swap(x_own)
    columns.own_to(0)
    common = (rows.blocks(), bias, gain, shift, tables, width, tile)
    first = project(0, x_own, *common, (), [columns.held[0]])
    (x_other,) = columns.fenced([x_other], [first[0]])
    columns.own_to(1)
    qkv, act, slope, normed = project(1, x_other, *common, first, [columns.held[0]])
    held = columns.fenced(rows.blocks(), [qkv])
    columns.rest()
    row_blocks, row_others = held, [swap(a) for a in held[:3]]
    mixed, lse = attend(qkv, length, block, [columns.held[0]])
    row_others = columns.fenced(row_others, [mixed])
    row_blocks[3:] = fence(row_blocks[3:], [row_others[0]])
    row_others += [swap(a) for a in row_blocks[3:]]
    other_sums, own_sums = branch_sums(mixed, act, columns.blocks(), tile, [row_blocks[3]])
    other_sums, dy_own, *row_others[3:] = fence([other_sums, dy_own, *row_others[3:]], [own_sums])
    theirs = swap(other_sums)
    dy_other = swap(dy_own)

    grads = (slope, columns.blocks(), width, tile)
    gmixed, gpre_own, *grad_a = grad_in(0, dy_own, *grads, (), [own_sums])
    theirs, dy_other = fence([theirs, dy_other], [grad_a[0]])
    total = add_rows(own_sums, theirs)
    branches = line_scatter(total)
    gmixed, gpre_other, *grad_b = grad_in(1, dy_other, *grads, [gmixed], [total])
    (gpre_sent,) = fence([gpre_other])
    gpre_came = swap(gpre_sent)
    column_grads = BlockScatter(
        weight_grads(me, [[mixed], [act]], [dy_own, dy_other], ndp, [gpre_sent], left=False), ndp
    )
    (gpre_came,) = fence([gpre_came], [column_grads.held[0][0][0][0]])
    column_came = column_grads.send(0)
    back = lambda sequence, deps: attend_back(
        sequence, qkv, gmixed, mixed, lse, tables, length, block, deps
    )
    *other, qkv_sums_b = back(1, [gpre_came])
    came = [swap(a) for a in other]
    *own, qkv_sums_a = back(0, [other[0]])
    came = fence([*came, *column_came], [own[0]])
    column_came, came = came[3:], came[:3]
    column_grads.arrive(0, column_came)
    column_grads.between()
    all_grads = [*own, gpre_own, *came, gpre_came]

    def normed_half(half, deps, adds=()):
        return grad_normed_sums(
            half, all_grads, x_own, [*row_blocks, *row_others], tile, deps, adds
        )

    total_a, sums_a, *settled = normed_half(0, [], column_grads.adds(chip_steps - 1))
    column_grads.settle(chip_steps - 1, settled)
    half_a = line_scatter(total_a)
    column_came = column_grads.send(chip_steps - 1)
    up_grads = BlockScatter(
        weight_grads(me, [normed], [[gpre_own, gpre_sent]], ndp, [sums_a], left=True), ndp
    )
    c0, c1, branches, u0, u1 = fence(
        [*column_came, branches, *(up_grads.held[h][0][0][0] for h in range(2))]
    )
    up_grads.held[0][0], up_grads.held[1][0] = [(u0, 0)], [(u1, 0)]
    up_came = up_grads.send(0)
    column_grads.arrive(chip_steps - 1, [c0, c1])
    blocks, column_last = weight_grads(
        me,
        [normed],
        [[a, b] for a, b in zip(own, other)],
        ndp,
        [c0],
        True,
        [column_grads.adds(len(column_grads.plan[1]) - 1)[1]],
    )
    qkv_grads = BlockScatter(blocks, ndp)
    qkv_came = qkv_grads.send(0)
    column_theirs = swap(column_last[0])
    total_b, sums_b = normed_half(1, [qkv_grads.held[0][0][0][0]])
    half_b = line_scatter(total_b)
    u0, u1, q0, q1, half_a = fence([*up_came, *qkv_came, half_a], [sums_b, column_theirs])
    up_grads.arrive(0, [u0, u1])
    qkv_grads.arrive(0, [q0, q1])
    up_grads.between()
    qkv_grads.between()
    up_came, qkv_came = up_grads.send(chip_steps - 1), qkv_grads.send(chip_steps - 1)
    u0, u1, q0, q1, branches, sums_b, column_theirs = fence(
        [*up_came, *qkv_came, branches, sums_b, column_theirs]
    )
    up_grads.arrive(chip_steps - 1, [u0, u1])
    qkv_grads.arrive(chip_steps - 1, [q0, q1])
    up_theirs = swap(up_grads.last())
    qkv_theirs = swap(qkv_grads.last())
    qkv_sum = (qkv_sums_a + qkv_sums_b)[:, :3, :].transpose(1, 0, 2).reshape(3 * width)
    norm_sums = jnp.concatenate([sums_a[:2], sums_b[:2]], axis=1)
    small = jnp.concatenate(
        [
            norm_sums.reshape(2 * model),
            qkv_sum,
            grad_a[0][0] + grad_b[0][0],
            grad_a[1][0] + grad_b[1][0],
        ]
    )
    small = pair_sum([small] + [across(small, j, ndp) for j in range(2, ndp, 2)])
    small_other = swap(small)
    owned_up, owned_qkv, owned_dense, owned_down = finish(
        (up_grads.kept(), up_theirs),
        (qkv_grads.kept(), qkv_theirs),
        (column_grads.kept(), column_theirs),
    )
    grad_tokens = norm_back(tokens, cotangent, gain, [half_a, half_b], [small_other, owned_up])
    norm_sums = small[: 2 * model] + small_other[: 2 * model]
    norm_sums = [norm_sums] + [
        lax.ppermute(norm_sums, "mp", [(i, i ^ j) for i in range(nmp)]) for j in range(1, nmp)
    ]
    while len(norm_sums) > 1:
        norm_sums = [a + b for a, b in zip(norm_sums[::2], norm_sums[1::2])]
    norm_sums = norm_sums[0]

    output = (
        tokens.astype(F32)
        + branches.astype(F32)
        + (dense_bias.astype(F32) + down_bias.astype(F32))[None, :]
    ).astype(BF16)

    inner = 3 * width + hidden
    grad_out_bias = small[2 * model + inner :]
    here, there = (a[2 * model : 2 * model + inner] for a in (small, small_other))
    even, odd = jnp.where(core == 0, here, there), jnp.where(core == 0, there, here)
    grad_qkv_bias = jnp.concatenate(
        [a[: 3 * width].reshape(3, width) for a in (even, odd)], axis=1
    )
    grad_up_bias = jnp.concatenate([even[3 * width :], odd[3 * width :]])

    return (
        output,
        grad_tokens,
        norm_sums[:model],
        norm_sums[model:],
        owned_qkv,
        grad_qkv_bias,
        owned_dense,
        grad_out_bias,
        owned_up,
        grad_up_bias,
        owned_down,
        grad_out_bias,
    )


def solution(mesh):
    return jax.shard_map(
        functools.partial(on_device, ndp=mesh.shape["dp"], nmp=mesh.shape["mp"]),
        mesh=mesh,
        in_specs=(
            P(("dp", "mp"), None),
            P(),
            P(),
            P(None, "dp", "mp"),
            P(None, "mp"),
            P("mp", "dp"),
            P(),
            P("dp", "mp"),
            P("mp"),
            P("mp", "dp"),
            P(),
            P(("dp", "mp"), None),
        ),
        out_specs=(
            P(("dp", "mp"), None),
            P(("dp", "mp"), None),
            P(),
            P(),
            P(None, "dp", "mp"),
            P(None, "mp"),
            P("mp", "dp"),
            P(),
            P("dp", "mp"),
            P("mp"),
            P("mp", "dp"),
            P(),
        ),
        check_vma=False,
    )
```

```python
import functools

import jax
import jax.numpy as jnp
import numpy as np
from jax import lax
from jax.experimental import pallas as pl
from jax.experimental.pallas import tpu as pltpu
from jax.sharding import PartitionSpec as P

HEAD_DIM = 64
ROT = 32
EPS = 1e-05
LANES = 128
F32 = jnp.float32
BF16 = jnp.bfloat16
HBM = pl.BlockSpec(memory_space=pltpu.HBM)


def dot(lhs, rhs, lhs_dim, rhs_dim):
    return lax.dot_general(
        lhs, rhs, (((lhs_dim,), (rhs_dim,)), ((), ())), preferred_element_type=F32
    )


def call(kernel, name, operands, deps=(), scalars=(), adds=(), vmem=64, **spec):
    deps, out_shape = tuple(deps), spec.pop("out_shape")
    single = not isinstance(out_shape, list)
    out_shape = [out_shape] if single else out_shape
    out_specs = spec.pop("out_specs")
    out_specs = [out_specs] if single else list(out_specs)
    extra, extra_specs, sizes = [], [], []
    steps = spec["grid"][0] if adds else 1
    for many, addends in adds:
        _, rows, columns = addends[0][0].shape
        block = (many, rows // steps, columns)
        for array, first in addends:
            extra.append(array)
            extra_specs.append(
                pl.BlockSpec(block, lambda i, *at, first=first, many=many: (first // many, i, 0))
            )
        out_shape = out_shape + [jax.ShapeDtypeStruct((many, rows, columns), BF16)]
        out_specs = out_specs + [pl.BlockSpec(block, lambda i, *at: (0, i, 0))]
        sizes.append(len(addends))
    lead, outs = len(scalars) + len(operands), len(out_shape) - len(adds)

    def body(*refs):
        first = lead + len(extra) + len(deps)
        kernel(*refs[:lead], *refs[first : first + outs], *refs[first + outs + len(adds) :])
        sources = refs[lead : lead + len(extra)]
        for n, out in zip(sizes, refs[first + outs : first + outs + len(adds)]):
            out[...] = sum(ref[...].astype(F32) for ref in sources[:n]).astype(BF16)
            sources = sources[n:]

    in_specs = list(spec.pop("in_specs")) + extra_specs + [HBM] * len(deps)
    aliases = spec.pop("input_output_aliases", {})
    if scalars:
        grid_spec = pltpu.PrefetchScalarGridSpec(
            num_scalar_prefetch=len(scalars), in_specs=in_specs, out_specs=out_specs, **spec
        )
        spec = {"grid_spec": grid_spec}
    else:
        spec.update(in_specs=in_specs, out_specs=out_specs)
    results = pl.pallas_call(
        body,
        out_shape=out_shape,
        input_output_aliases=aliases,
        compiler_params=pltpu.CompilerParams(vmem_limit_bytes=vmem << 20),
        cost_estimate=pl.CostEstimate(flops=0, transcendentals=0, bytes_accessed=0),
        name=name,
        **spec,
    )(*scalars, *operands, *extra, *deps)
    return results[0] if single and not adds else results


def fence(values, deps=()):
    return list(
        call(
            lambda *refs: None,
            "fence",
            values,
            deps,
            in_specs=[HBM] * len(values),
            out_specs=[HBM] * len(values),
            out_shape=[jax.ShapeDtypeStruct(v.shape, v.dtype) for v in values],
            input_output_aliases={n: n for n in range(len(values))},
        )
    )


def rotary_tables(length):
    positions = np.arange(length, dtype=np.float32)
    frequency = 10000.0 ** (-np.arange(ROT // 2, dtype=np.float64) * 2.0 / ROT)
    angles = positions[:, None] * frequency.astype(np.float32)[None, :]
    cosine, sine = np.cos(angles.astype(np.float64)), np.sin(angles.astype(np.float64))
    rest = HEAD_DIM - ROT
    none = np.zeros((length, ROT // 2))
    ones, zeros = np.ones((length, rest)), np.zeros((length, rest))
    straight = np.concatenate([cosine, cosine, ones], axis=1)
    left = np.concatenate([-sine, none, zeros], axis=1)
    right = np.concatenate([none, sine, zeros], axis=1)
    return [
        jnp.asarray(np.concatenate([t, t], axis=1).astype(np.float32))
        for t in (straight, left, right)
    ]


def rotated(u, straight, left, right, sign):
    half = ROT // 2
    turned = pltpu.roll(u, LANES - half, 1) * left + pltpu.roll(u, half, 1) * right
    return u * straight + sign * turned


def normalized(x):
    x = x.astype(F32)
    centered = x - jnp.mean(x, axis=1, keepdims=True)
    variance = jnp.mean(centered * centered, axis=1, keepdims=True)
    return centered * lax.rsqrt(variance + EPS)


def block_copies(blocks, place, sems):
    me = lax.axis_index("dp")
    return [
        pltpu.make_async_copy(block, place(lax.bitwise_xor(me, j)), sems.at[j])
        for j, block in enumerate(blocks)
    ]


def span(owner, size):
    return pl.ds(pl.multiple_of(owner * size, size), size)


def rows_at(ref, size):
    return lambda owner: ref.at[pl.ds(pl.multiple_of(owner * size, size), size)]


def columns_at(ref, size):
    return lambda owner: ref.at[:, pl.ds(pl.multiple_of(owner * size, size), size)]


def project_kernel(setup, x_ref, bias_ref, gain_ref, shift_ref, cos_ref, left_ref, right_ref, *rest):
    count, width, hidden = setup
    blocks = rest[:count]
    qkv_ref, act_ref, slope_ref, normed_ref, held, sems = rest[-6:]

    @pl.when(pl.program_id(0) == 0)
    def _():
        loads = block_copies(blocks, rows_at(held, blocks[0].shape[0]), sems)
        for copy in loads:
            copy.start()
        for copy in loads:
            copy.wait()

    x = (normalized(x_ref[...]) * gain_ref[...] + shift_ref[...]).astype(BF16)
    normed_ref[...] = x
    root = 0.7978845608028654
    for t in range((3 * width + hidden) // width):
        columns = slice(t * width, (t + 1) * width)
        y = dot(x, held[:, columns], 1, 0) + bias_ref[:, columns]
        if t < 3:
            for g in range(width // LANES):
                part = y[:, g * LANES : (g + 1) * LANES]
                if t < 2:
                    part = rotated(part, cos_ref[...], left_ref[...], right_ref[...], 1.0)
                if t == 0:
                    part = part * HEAD_DIM**-0.5
                start = t * width + g * LANES
                qkv_ref[:, start : start + LANES] = part.astype(BF16)
        else:
            columns = slice((t - 3) * width, (t - 2) * width)
            square = y * y
            turn = jnp.tanh(root * y * (1.0 + 0.044715 * square))
            half = 0.5 * (1.0 + turn)
            act_ref[:, columns] = (y * half).astype(BF16)
            slope = half * (1.0 + y * (1.0 - turn) * (root + (3.0 * 0.044715 * root) * square))
            slope_ref[:, columns] = slope.astype(BF16)


def project(sequence, x, blocks, bias, gain, shift, tables, width, tile, earlier, deps):
    (length, model), total, count = x.shape, blocks[0].shape[1], len(blocks)
    hidden, steps = total - 3 * width, length // tile
    rows = lambda w: pl.BlockSpec((tile, w), lambda i: (i, 0))
    out = lambda w: pl.BlockSpec((tile, w), lambda i: (sequence * steps + i, 0))
    line = lambda a: pl.BlockSpec(a.shape, lambda i: (0, 0))
    widths = (3 * width, hidden, hidden, model)
    operands = [x, bias, gain, shift, *tables, *blocks]
    return call(
        functools.partial(project_kernel, (count, width, hidden)),
        "project",
        operands + list(earlier),
        deps,
        grid=(steps,),
        in_specs=[rows(model), line(bias), line(gain), line(shift)]
        + [rows(LANES)] * 3
        + [HBM] * (count + len(earlier)),
        out_specs=[out(w) for w in widths],
        out_shape=[jax.ShapeDtypeStruct((2 * length, w), BF16) for w in widths],
        input_output_aliases={len(operands) + n: n for n in range(len(earlier))},
        scratch_shapes=[pltpu.VMEM((model, total), BF16), pltpu.SemaphoreType.DMA((count,))],
    )


def attend_kernel(block, q_ref, k_ref, v_ref, out_ref, lse_ref):
    length = q_ref.shape[0]
    lane = lax.broadcasted_iota(jnp.int32, (1, LANES), 1)
    key = lax.broadcasted_iota(jnp.int32, (block, block), 0)
    causal = key <= lax.broadcasted_iota(jnp.int32, (block, block), 1)
    for i in range(length // block):
        rows, before = pl.ds(i * block, block), pl.ds(0, i * block)
        results = []
        for h in range(2):
            mine = (lane < HEAD_DIM) if h == 0 else (lane >= HEAD_DIM)
            query = jnp.where(mine, q_ref[rows, :], 0)
            near = jnp.where(causal, dot(k_ref[rows, :], query, 1, 1), -1e30)
            highest = jnp.max(near, axis=0, keepdims=True)
            if i:
                far = dot(k_ref[before, :], query, 1, 1)
                highest = jnp.maximum(highest, jnp.max(far, axis=0, keepdims=True))
            near = jnp.exp(near - highest)
            total = jnp.sum(near, axis=0, keepdims=True)
            if i:
                far = jnp.exp(far - highest)
                total = total + jnp.sum(far, axis=0, keepdims=True)
            inverse = 1.0 / total
            result = dot((near * inverse).astype(BF16), v_ref[rows, :], 0, 0)
            if i:
                result = result + dot((far * inverse).astype(BF16), v_ref[before, :], 0, 0)
            results.append(result)
            lse_ref[0, h : h + 1, rows] = highest + jnp.log(total)
        out_ref[rows, :] = jnp.where(lane < HEAD_DIM, results[0], results[1]).astype(BF16)


def pair_specs(length, pairs):
    return lambda off: pl.BlockSpec(
        (length, LANES), lambda g: (g // pairs, off * pairs + g % pairs)
    )


def attend(qkv, length, block, deps):
    width, sequences = qkv.shape[1] // 3, qkv.shape[0] // length
    pairs = width // LANES
    at = pair_specs(length, pairs)
    return call(
        functools.partial(attend_kernel, block),
        "attend",
        [qkv, qkv, qkv],
        deps,
        grid=(sequences * pairs,),
        in_specs=[at(0), at(1), at(2)],
        out_specs=[at(0), pl.BlockSpec((1, 8, length), lambda g: (g, 0, 0))],
        out_shape=[
            jax.ShapeDtypeStruct((qkv.shape[0], width), BF16),
            jax.ShapeDtypeStruct((sequences * pairs, 8, length), F32),
        ],
    )


def attend_back_kernel(
    block,
    q_ref,
    k_ref,
    v_ref,
    grad_ref,
    mixed_ref,
    lse_ref,
    cos_ref,
    left_ref,
    right_ref,
    gq_ref,
    gk_ref,
    gv_ref,
    sum_ref,
    gk_sum,
    gv_sum,
):
    length = q_ref.shape[0]
    lane = lax.broadcasted_iota(jnp.int32, (1, LANES), 1)
    key = lax.broadcasted_iota(jnp.int32, (block, block), 0)
    causal = key <= lax.broadcasted_iota(jnp.int32, (block, block), 1)
    count = length // block
    sum_ref[...] = jnp.zeros_like(sum_ref)

    def put(ref, which, rows, value):
        value = value.astype(BF16)
        ref[rows, :] = value
        sum_ref[0, which : which + 1, :] += jnp.sum(value.astype(F32), axis=0, keepdims=True)

    def unrotated(value, rows):
        return rotated(value, cos_ref[rows, :], left_ref[rows, :], right_ref[rows, :], -1.0)

    for i in reversed(range(count)):
        rows = pl.ds(i * block, block)
        product = grad_ref[rows, :].astype(F32) * mixed_ref[rows, :].astype(F32)
        gq = None
        for h in range(2):
            mine = (lane < HEAD_DIM) if h == 0 else (lane >= HEAD_DIM)
            query = jnp.where(mine, q_ref[rows, :], 0)
            grad = jnp.where(mine, grad_ref[rows, :], 0)
            ones = jnp.where(mine, jnp.ones((8, LANES), F32), 0.0)
            delta = lax.dot_general(
                ones,
                product,
                (((1,), (1,)), ((), ())),
                precision=lax.Precision.HIGHEST,
                preferred_element_type=F32,
            )[0:1, :]
            lse = lse_ref[0, h : h + 1, rows]
            for j in range(i + 1):
                keys = pl.ds(j * block, block)
                key_rows = k_ref[keys, :]
                probs = jnp.exp(dot(key_rows, query, 1, 1) - lse)
                if j == i:
                    probs = jnp.where(causal, probs, 0.0)
                gprobs = dot(v_ref[keys, :], grad, 1, 1)
                gscores = (probs * (gprobs - delta)).astype(BF16)
                gv, gk = dot(probs.astype(BF16), grad, 1, 0), dot(gscores, query, 1, 0)
                if i == count - 1 and h == 0:
                    gv_sum[keys, :] = gv
                    gk_sum[keys, :] = gk
                else:
                    gv_sum[keys, :] += gv
                    gk_sum[keys, :] += gk
                part = dot(gscores, jnp.where(mine, key_rows, 0), 0, 0)
                gq = part if gq is None else gq + part
        put(gq_ref, 0, rows, unrotated(gq * HEAD_DIM**-0.5, rows))
    for i in range(count):
        rows = pl.ds(i * block, block)
        put(gk_ref, 1, rows, unrotated(gk_sum[rows, :], rows))
        put(gv_ref, 2, rows, gv_sum[rows, :])


def attend_back(sequence, qkv, grad, mixed, lse, tables, length, block, deps):
    width = qkv.shape[1] // 3
    pairs = width // LANES
    at = lambda off: pl.BlockSpec((length, LANES), lambda g: (sequence, off * pairs + g))
    out = pl.BlockSpec((length, LANES), lambda g: (0, g))
    table = pl.BlockSpec((length, LANES), lambda g: (0, 0))
    small = pl.BlockSpec((1, 8, length), lambda g: (sequence * pairs + g, 0, 0))
    return call(
        functools.partial(attend_back_kernel, block),
        "attend_back",
        [qkv, qkv, qkv, grad, mixed, lse, *tables],
        deps,
        grid=(pairs,),
        in_specs=[at(0), at(1), at(2), at(0), at(0), small, table, table, table],
        out_specs=[out] * 3 + [pl.BlockSpec((1, 8, LANES), lambda g: (g, 0, 0))],
        out_shape=[jax.ShapeDtypeStruct((length, width), BF16)] * 3
        + [jax.ShapeDtypeStruct((pairs, 8, LANES), F32)],
        scratch_shapes=[pltpu.VMEM((length, LANES), F32)] * 2,
    )


def by_sequence(tile, width, steps):
    return [
        pl.BlockSpec((tile, width), lambda i: (jnp.minimum(i, steps - 1), 0)),
        pl.BlockSpec((tile, width), lambda i: (jnp.maximum(i - steps, 0), 0)),
    ]


def other_first(tile, width, steps):
    return pl.BlockSpec((tile, width), lambda i: ((i + steps) % (2 * steps), 0))


def put_by_sequence(step, steps, value, other_ref, own_ref):
    @pl.when(step < steps)
    def _():
        other_ref[...] = value

    @pl.when(step >= steps)
    def _():
        own_ref[...] = value


def branch_kernel(count, steps, mixed_ref, act_ref, *rest):
    blocks, (other_ref, own_ref, held, sems) = rest[:count], rest[count:]
    step = pl.program_id(0)

    @pl.when(step == 0)
    def _():
        loads = block_copies(blocks, columns_at(held, blocks[0].shape[1]), sems)
        for copy in loads:
            copy.start()
        for copy in loads:
            copy.wait()

    x = jnp.concatenate([mixed_ref[...], act_ref[...]], axis=1)
    put_by_sequence(step, steps, dot(x, held[...], 1, 0).astype(BF16), other_ref, own_ref)


def branch_sums(mixed, act, blocks, tile, deps):
    length, count = mixed.shape[0] // 2, len(blocks)
    inner, model, steps = blocks[0].shape[0], count * blocks[0].shape[1], length // tile
    return call(
        functools.partial(branch_kernel, count, steps),
        "branch_sums",
        [mixed, act, *blocks],
        deps,
        grid=(2 * steps,),
        in_specs=[other_first(tile, a.shape[1], steps) for a in (mixed, act)] + [HBM] * count,
        out_specs=by_sequence(tile, model, steps),
        out_shape=[jax.ShapeDtypeStruct((length, model), BF16)] * 2,
        scratch_shapes=[pltpu.VMEM((inner, model), BF16), pltpu.SemaphoreType.DMA((count,))],
    )


def grad_in_kernel(setup, dy_ref, slope_ref, *rest):
    count, width, hidden = setup
    blocks = rest[:count]
    gmixed_ref, gpre_ref, gsum_ref, dsum_ref, held, sems = rest[-6:]

    @pl.when(pl.program_id(0) == 0)
    def _():
        loads = block_copies(blocks, columns_at(held, blocks[0].shape[1]), sems)
        for copy in loads:
            copy.start()
        gsum_ref[...] = jnp.zeros_like(gsum_ref)
        dsum_ref[...] = jnp.zeros_like(dsum_ref)
        for copy in loads:
            copy.wait()

    dy = dy_ref[...]
    gmixed_ref[...] = dot(dy, held[:width, :], 1, 1).astype(BF16)
    for start in range(0, hidden, width):
        part = slice(start, start + width)
        gact = dot(dy, held[width + start : 2 * width + start, :], 1, 1)
        gpre = (gact * slope_ref[:, part].astype(F32)).astype(BF16)
        gpre_ref[:, part] = gpre
        gsum_ref[0:1, part] += jnp.sum(gpre.astype(F32), axis=0, keepdims=True)
    dsum_ref[0:1, :] += jnp.sum(dy.astype(F32), axis=0, keepdims=True)


def grad_in(sequence, dy, slope, blocks, width, tile, earlier, deps):
    (length, model), hidden, count = dy.shape, slope.shape[1], len(blocks)
    steps = length // tile
    at = lambda w: pl.BlockSpec((tile, w), lambda i: (sequence * steps + i, 0))
    total = lambda w: pl.BlockSpec((8, w), lambda i: (0, 0))
    operands = [dy, slope, *blocks]
    return call(
        functools.partial(grad_in_kernel, (count, width, hidden)),
        "grad_in",
        operands + list(earlier),
        deps,
        grid=(steps,),
        in_specs=[pl.BlockSpec((tile, model), lambda i: (i, 0)), at(hidden)]
        + [HBM] * (count + len(earlier)),
        out_specs=[
            at(width),
            pl.BlockSpec((tile, hidden), lambda i: (i, 0)),
            total(hidden),
            total(model),
        ],
        out_shape=[
            jax.ShapeDtypeStruct((2 * length, width), BF16),
            jax.ShapeDtypeStruct((length, hidden), BF16),
            jax.ShapeDtypeStruct((8, hidden), F32),
            jax.ShapeDtypeStruct((8, model), F32),
        ],
        input_output_aliases={len(operands) + n: n for n in range(len(earlier))},
        scratch_shapes=[
            pltpu.VMEM((width + hidden, model), BF16),
            pltpu.SemaphoreType.DMA((count,)),
        ],
    )


def add_kernel(a_ref, b_ref, out_ref):
    out_ref[...] = (a_ref[...].astype(F32) + b_ref[...].astype(F32)).astype(BF16)


def add_rows(a, b):
    rows = pl.BlockSpec((a.shape[0] // 2, a.shape[1]), lambda i: (i, 0))
    return call(
        add_kernel,
        "add_rows",
        [a, b],
        grid=(2,),
        in_specs=[rows, rows],
        out_specs=rows,
        out_shape=jax.ShapeDtypeStruct(a.shape, BF16),
    )


def grad_normed_kernel(count, half, x_ref, *rest):
    grads, blocks, (out_ref, sum_ref, held, sems) = rest[:8], rest[8 : 8 + 2 * count], rest[-4:]
    (size, total), few, me = blocks[0].shape, count // 2, lax.axis_index("dp")

    @pl.when(pl.program_id(0) == 0)
    def _():
        for start in (True, False):
            for n, block in enumerate(blocks):
                core, j = n // count, n % count
                owner = lax.bitwise_xor(me, j ^ core) - half * few
                columns = slice(core * total, (core + 1) * total)

                @pl.when((owner >= 0) & (owner < few))
                def _(start=start, n=n, block=block, owner=owner, columns=columns):
                    target = held.at[span(owner, size), columns]
                    copy = pltpu.make_async_copy(block, target, sems.at[n])
                    if start:
                        copy.start()
                    else:
                        copy.wait()

        sum_ref[...] = jnp.zeros_like(sum_ref)

    columns = slice(half * few * size, (half + 1) * few * size)
    normal = normalized(x_ref[...])[:, columns]
    g = jnp.concatenate([ref[...] for ref in grads], axis=1)
    result = dot(g, held[...], 1, 1)
    sum_ref[0:1, :] += jnp.sum(result * normal, axis=0, keepdims=True)
    sum_ref[1:2, :] += jnp.sum(result, axis=0, keepdims=True)
    out_ref[...] = result.astype(BF16)


def grad_normed_sums(half, grads, x, blocks, tile, deps, adds=()):
    (length, model), count, total = x.shape, len(blocks) // 2, blocks[0].shape[1]
    part = model // 2
    rows = lambda w: pl.BlockSpec((tile, w), lambda i: (i, 0))
    return call(
        functools.partial(grad_normed_kernel, count, half),
        "grad_normed_sums",
        [x, *grads, *blocks],
        deps,
        adds=adds,
        grid=(length // tile,),
        in_specs=[rows(model)] + [rows(g.shape[1]) for g in grads] + [HBM] * (2 * count),
        out_specs=[rows(part), pl.BlockSpec((8, part), lambda i: (0, 0))],
        out_shape=[
            jax.ShapeDtypeStruct((length, part), BF16),
            jax.ShapeDtypeStruct((8, part), F32),
        ],
        scratch_shapes=[
            pltpu.VMEM((part, 2 * total), BF16),
            pltpu.SemaphoreType.DMA((2 * count,)),
        ],
    )


def weight_grad_kernel(writes, left, rows, many, groups, at_ref, *refs):
    cuts, (*refs, held, grad, sems) = refs[:many], refs[many:]
    whole, outs = refs[: len(refs) - len(writes)], refs[len(refs) - len(writes) :]
    step, core, loads, first = pl.program_id(0), lax.rem(lax.axis_index("dp"), 2), [], 0
    for group in groups:
        below = 0
        for ref in whole[:group]:
            columns = pl.ds(first, ref.shape[1])
            for start in range(0, ref.shape[0], rows):
                target = held.at[pl.ds(below + start, rows), columns]
                loads.append((ref.at[pl.ds(start, rows)], target))
            below += ref.shape[0]
        first += whole[0].shape[1]
        whole = whole[group:]
    loads = [pltpu.make_async_copy(*pair, sems.at[n]) for n, pair in enumerate(loads)]

    @pl.when(step == 0)
    def _():
        for copy in loads:
            copy.start()
        for copy in loads:
            copy.wait()

    cut = jnp.concatenate([ref[...] for ref in cuts], axis=0)
    pair = (cut, held[...]) if left else (held[...], cut)
    grad[...] = dot(*pair, 0, 0).astype(BF16)
    size = cut.shape[1] // 2
    for half, steps, out_ref in writes_of(writes, outs):
        here = functools.reduce(jnp.logical_or, [step == s for s in steps])

        @pl.when(here)
        def _(half=half, out_ref=out_ref):
            mine = span(core if half == 0 else 1 - core, size)
            out_ref[0] = grad[mine, :] if left else grad[:, mine]


def writes_of(writes, outs):
    return [(half, steps, out) for (half, steps), out in zip(writes, outs)]


def weight_grads(me, xs, gs, count, deps, left, adds=()):
    plan, chips = scatter_plan(count), count // 2
    order = [j // 2 for s in plan[0] for j in s]
    sets = [(half, s) for s in range(len(plan[0])) for half in range(2)]
    writes = [(half, [order.index(j // 2) for j in plan[half][s]]) for half, s in sets]
    table = []
    for _, steps in writes:
        for i in range(chips):
            later = [w for w in steps if w >= i]
            table.append(steps.index(min(later) if later else max(steps)))
    owners = lax.bitwise_xor(me // 2, jnp.array(order, jnp.int32))
    at = jnp.concatenate([owners, jnp.array(table, jnp.int32)])
    cut, whole = (xs, gs) if left else (gs, xs)
    groups, length = [len(g) for g in whole], sum(a.shape[0] for a in whole[0])
    size, full = cut[0].shape[1] // count, sum(g[0].shape[1] for g in whole)
    shape, whole = (size, full) if left else (full, size), [a for g in whole for a in g]
    rows = length // 4
    pieces = 4 * len(groups)

    def out(n):
        return pl.BlockSpec((1, *shape), lambda i, at: (at[chips * (n + 1) + i], 0, 0))

    outs = call(
        functools.partial(weight_grad_kernel, writes, left, rows, len(cut), groups),
        "weight_grads",
        [*cut, *whole],
        deps,
        (at,),
        adds,
        grid=(chips,),
        in_specs=[pl.BlockSpec((a.shape[0], 2 * size), lambda i, at: (0, at[i])) for a in cut]
        + [HBM] * len(whole),
        out_specs=[out(n) for n in range(len(sets))],
        out_shape=[
            jax.ShapeDtypeStruct((len(plan[half][s]), *shape), BF16) for half, s in sets
        ],
        scratch_shapes=[
            pltpu.VMEM((length, full), BF16),
            pltpu.VMEM((2 * size, full) if left else (full, 2 * size), BF16),
            pltpu.SemaphoreType.DMA((pieces,)),
        ],
    )
    blocks = [[o for o, (half, _) in zip(outs, sets) if half == h] for h in range(2)]
    return (blocks, *outs[len(sets) :]) if adds else blocks


def finish_kernel(sizes, width, *refs):
    ins, (up_ref, qkv_ref, dense_ref, down_ref) = refs[:-4], refs[-4:]
    core = lax.rem(lax.axis_index("dp"), 2)
    pairs = []
    for size in sizes:
        mine = sum(ref[0].astype(F32) for ref in ins[: size - 1])
        pairs.append(((core, mine), (1 - core, ins[size - 1][0].astype(F32))))
        ins = ins[size:]
    for where, value in pairs[0]:
        up_ref[:, span(where, value.shape[1])] = value
    for where, value in pairs[1]:
        for c in range(3):
            qkv_ref[c, :, span(where, width)] = value[:, c * width : (c + 1) * width]
    for out_ref, pair in ((dense_ref, pairs[2]), (down_ref, pairs[3])):
        for where, value in pair:
            out_ref[where] = value


def finish(up, qkv, columns):
    (size, hidden), width = up[1].shape, qkv[1].shape[1] // 3
    steps = hidden // width
    operands, specs, sizes = [], [], []

    def take(parts, rows, base):
        addends, theirs = parts
        for array, first in [*addends, (theirs[None], 0)]:
            operands.append(array)
            specs.append(
                pl.BlockSpec(
                    (1, rows, array.shape[2]), lambda i, first=first: (first, base + i, 0)
                )
            )
        sizes.append(len(addends) + 1)

    take(up, size // steps, 0)
    take(qkv, size // steps, 0)
    take(columns, width // steps, 0)
    take(columns, width, 1)
    owned_up, owned_qkv, owned_dense, owned_down = call(
        lambda *refs: finish_kernel(sizes, width, *refs),
        "finish",
        operands,
        grid=(steps,),
        in_specs=specs,
        out_specs=[
            pl.BlockSpec((size // steps, 2 * hidden), lambda i: (i, 0)),
            pl.BlockSpec((3, size // steps, 2 * width), lambda i: (0, i, 0)),
            pl.BlockSpec((2, width // steps, size), lambda i: (0, i, 0)),
            pl.BlockSpec((2, width, size), lambda i: (0, i, 0)),
        ],
        out_shape=[
            jax.ShapeDtypeStruct((size, 2 * hidden), F32),
            jax.ShapeDtypeStruct((3, size, 2 * width), F32),
            jax.ShapeDtypeStruct((2, width, size), F32),
            jax.ShapeDtypeStruct((2, hidden, size), F32),
        ],
    )
    return (
        owned_up,
        owned_qkv,
        owned_dense.reshape(2 * width, size),
        owned_down.reshape(2 * hidden, size),
    )


def norm_back_kernel(tokens_ref, dy_ref, gain_ref, left_ref, right_ref, out_ref):
    x = tokens_ref[...].astype(F32)
    centered = x - jnp.mean(x, axis=1, keepdims=True)
    inverse_std = lax.rsqrt(jnp.mean(centered * centered, axis=1, keepdims=True) + EPS)
    normal = centered * inverse_std
    grad = jnp.concatenate([left_ref[...], right_ref[...]], axis=1).astype(F32)
    scaled = grad * gain_ref[...]
    first_mean = jnp.mean(scaled, axis=1, keepdims=True)
    second_mean = jnp.mean(scaled * normal, axis=1, keepdims=True)
    back = (scaled - first_mean - normal * second_mean) * inverse_std
    out_ref[...] = (dy_ref[...].astype(F32) + back).astype(BF16)


def norm_back(tokens, dy, gain, halves, deps):
    rows, model = tokens.shape
    tile = min(128, rows)
    part = lambda w: pl.BlockSpec((tile, w), lambda i: (i, 0))
    return call(
        norm_back_kernel,
        "norm_back",
        [tokens, dy, gain, *halves],
        deps,
        grid=(rows // tile,),
        in_specs=[part(model), part(model), pl.BlockSpec((1, model), lambda i: (0, 0))]
        + [part(model // 2)] * 2,
        out_specs=part(model),
        out_shape=jax.ShapeDtypeStruct((rows, model), BF16),
    )


def across(value, bit, count):
    return lax.ppermute(value, "dp", [(i, i ^ bit) for i in range(count)])


def added(addends):
    return sum(a.astype(F32) for a in addends).astype(BF16)


def pair_sum(parts):
    while len(parts) > 1:
        parts = [a + b for a, b in zip(parts[::2], parts[1::2])]
    return parts[0]


def chip_bits(count):
    bits, bit = [], 2
    while bit < count:
        bits.append(bit)
        bit *= 2
    return bits


class BlockGather:
    def __init__(self, own, sibling, count):
        self.held, self.count = {0: own, 1: sibling}, count
        self.orders = (chip_bits(count), chip_bits(count)[::-1])

    def own_to(self, s):
        if s < len(self.orders[0]):
            for half in range(2):
                bit = self.orders[half][s]
                self.held[half ^ bit] = across(self.held[half], bit, self.count)

    def rest(self):
        for s in range(1, len(self.orders[0])):
            for half in range(2):
                order = self.orders[half]
                for j in [j for j in self.held if j % 2 == half]:
                    if j ^ order[s] not in self.held and not any(j & b for b in order[s:]):
                        self.held[j ^ order[s]] = across(self.held[j], order[s], self.count)

    def fenced(self, others=(), deps=()):
        keys = sorted(self.held)
        values = fence([self.held[j] for j in keys] + list(others), deps)
        self.held = dict(zip(keys, values))
        return values[len(keys) :]

    def blocks(self):
        return [self.held[j] for j in range(self.count)]


def scatter_orders(count):
    return (chip_bits(count)[::-1], chip_bits(count))


def scatter_plan(count):
    plan = []
    for half, order in enumerate(scatter_orders(count)):
        sets, rest = [[half]], [half]
        for bit in reversed(order):
            sets.insert(0, [j ^ bit for j in rest])
            rest = sets[0] + rest
        plan.append(sets)
    return plan


class BlockScatter:
    def __init__(self, halves, count):
        self.count, self.orders, self.plan = count, scatter_orders(count), scatter_plan(count)
        self.held = [[[(a, 0)] for a in arrays] for arrays in halves]
        self.steps = len(self.orders[0])

    def parts(self, half, s):
        many = len(self.plan[half][s])
        return [a[first : first + many] for a, first in self.held[half][s]]

    def total(self, half, s):
        if len(self.held[half][s]) > 1:
            self.held[half][s] = [(added(self.parts(half, s)), 0)]
        return self.parts(half, s)[0]

    def ready(self, s):
        return [self.total(half, s) for half in range(2)]

    def adds(self, s):
        return [(len(self.plan[half][s]), self.held[half][s]) for half in range(2)]

    def settle(self, s, sums):
        for half in range(2):
            self.held[half][s] = [(sums[half], 0)]

    def send(self, s):
        return [across(self.total(h, s), self.orders[h][s], self.count) for h in range(2)]

    def arrive(self, s, came):
        for half in range(2):
            first = 0
            for t in range(s + 1, len(self.plan[half])):
                self.held[half][t].append((came[half], first))
                first += len(self.plan[half][t])

    def between(self):
        for s in range(1, self.steps - 1):
            self.arrive(s, self.send(s))

    def last(self):
        return self.total(1, -1)[0]

    def kept(self):
        return self.held[0][-1]


def on_device(
    tokens,
    norm_gain,
    norm_bias,
    qkv_weight,
    qkv_bias,
    dense_weight,
    dense_bias,
    up_weight,
    up_bias,
    down_weight,
    down_bias,
    cotangent,
    *,
    ndp,
    nmp,
):
    me = lax.axis_index("dp")
    core = me % 2
    length, model = tokens.shape[0] * nmp, tokens.shape[1]
    tile, block = min(256, length), min(512, length)
    width, hidden = qkv_weight.shape[2] // 2, up_weight.shape[1] // 2
    chip_steps = len(chip_bits(ndp))
    rank = lambda array, axis, which, size: lax.dynamic_slice_in_dim(
        array, which * size, size, axis
    )

    def row_pack(which):
        qkv = rank(qkv_weight, 2, which, width)
        return jnp.concatenate([qkv[0], qkv[1], qkv[2], rank(up_weight, 1, which, hidden)], axis=1)

    def column_pack(which):
        return jnp.concatenate(
            [rank(dense_weight, 0, which, width), rank(down_weight, 0, which, hidden)], axis=0
        )

    pairs = width // LANES
    swap = lambda array: across(array, 1, ndp)
    line_gather = lambda array: lax.all_gather(array, "mp", axis=0, tiled=True)
    line_scatter = lambda array: lax.psum_scatter(array, "mp", scatter_dimension=0, tiled=True)
    x_own, dy_own = line_gather(tokens), line_gather(cotangent)
    rows = BlockGather(row_pack(core), swap(row_pack(1 - core)), ndp)
    columns = BlockGather(column_pack(core), swap(column_pack(1 - core)), ndp)
    rows.own_to(0)
    rows.fenced(deps=columns.held.values())
    rows.own_to(1)
    rows.fenced()
    rows.rest()
    x_own, *held = fence([x_own, columns.held[0], columns.held[1]], rows.blocks())
    columns.held = dict(enumerate(held))

    tables = rotary_tables(length)
    bias = jnp.concatenate(
        [
            rank(qkv_bias, 1, core, width).astype(F32).reshape(1, 3 * width),
            rank(up_bias[None, :], 1, core, hidden).astype(F32),
        ],
        axis=1,
    )
    gain, shift = norm_gain.astype(F32)[None, :], norm_bias.astype(F32)[None, :]
    x_other = swap(x_own)
    columns.own_to(0)
    common = (rows.blocks(), bias, gain, shift, tables, width, tile)
    first = project(0, x_own, *common, (), [columns.held[0]])
    (x_other,) = columns.fenced([x_other], [first[0]])
    columns.own_to(1)
    qkv, act, slope, normed = project(1, x_other, *common, first, [columns.held[0]])
    held = columns.fenced(rows.blocks(), [qkv])
    columns.rest()
    row_blocks, row_others = held, [swap(a) for a in held[:3]]
    mixed, lse = attend(qkv, length, block, [columns.held[0]])
    row_others = columns.fenced(row_others, [mixed])
    row_blocks[3:] = fence(row_blocks[3:], [row_others[0]])
    row_others += [swap(a) for a in row_blocks[3:]]
    other_sums, own_sums = branch_sums(mixed, act, columns.blocks(), tile, [row_blocks[3]])
    other_sums, dy_own, *row_others[3:] = fence([other_sums, dy_own, *row_others[3:]], [own_sums])
    theirs = swap(other_sums)
    dy_other = swap(dy_own)

    grads = (slope, columns.blocks(), width, tile)
    gmixed, gpre_own, *grad_a = grad_in(0, dy_own, *grads, (), [own_sums])
    theirs, dy_other = fence([theirs, dy_other], [grad_a[0]])
    total = add_rows(own_sums, theirs)
    branches = line_scatter(total)
    gmixed, gpre_other, *grad_b = grad_in(1, dy_other, *grads, [gmixed], [total])
    (gpre_sent,) = fence([gpre_other])
    gpre_came = swap(gpre_sent)
    column_grads = BlockScatter(
        weight_grads(me, [[mixed], [act]], [dy_own, dy_other], ndp, [gpre_sent], left=False), ndp
    )
    (gpre_came,) = fence([gpre_came], [column_grads.held[0][0][0][0]])
    column_came = column_grads.send(0)
    back = lambda sequence, deps: attend_back(
        sequence, qkv, gmixed, mixed, lse, tables, length, block, deps
    )
    *other, qkv_sums_b = back(1, [gpre_came])
    came = [swap(a) for a in other]
    *own, qkv_sums_a = back(0, [other[0]])
    came = fence([*came, *column_came], [own[0]])
    column_came, came = came[3:], came[:3]
    column_grads.arrive(0, column_came)
    column_grads.between()
    all_grads = [*own, gpre_own, *came, gpre_came]

    def normed_half(half, deps, adds=()):
        return grad_normed_sums(
            half, all_grads, x_own, [*row_blocks, *row_others], tile, deps, adds
        )

    total_a, sums_a, *settled = normed_half(0, [], column_grads.adds(chip_steps - 1))
    column_grads.settle(chip_steps - 1, settled)
    half_a = line_scatter(total_a)
    column_came = column_grads.send(chip_steps - 1)
    up_grads = BlockScatter(
        weight_grads(me, [normed], [[gpre_own, gpre_sent]], ndp, [sums_a], left=True), ndp
    )
    c0, c1, branches, u0, u1 = fence(
        [*column_came, branches, *(up_grads.held[h][0][0][0] for h in range(2))]
    )
    up_grads.held[0][0], up_grads.held[1][0] = [(u0, 0)], [(u1, 0)]
    up_came = up_grads.send(0)
    column_grads.arrive(chip_steps - 1, [c0, c1])
    blocks, column_last = weight_grads(
        me,
        [normed],
        [[a, b] for a, b in zip(own, other)],
        ndp,
        [c0],
        True,
        [column_grads.adds(len(column_grads.plan[1]) - 1)[1]],
    )
    qkv_grads = BlockScatter(blocks, ndp)
    qkv_came = qkv_grads.send(0)
    column_theirs = swap(column_last[0])
    total_b, sums_b = normed_half(1, [qkv_grads.held[0][0][0][0]])
    half_b = line_scatter(total_b)
    u0, u1, q0, q1, half_a = fence([*up_came, *qkv_came, half_a], [sums_b, column_theirs])
    up_grads.arrive(0, [u0, u1])
    qkv_grads.arrive(0, [q0, q1])
    up_grads.between()
    qkv_grads.between()
    up_came, qkv_came = up_grads.send(chip_steps - 1), qkv_grads.send(chip_steps - 1)
    u0, u1, q0, q1, branches, sums_b, column_theirs = fence(
        [*up_came, *qkv_came, branches, sums_b, column_theirs]
    )
    up_grads.arrive(chip_steps - 1, [u0, u1])
    qkv_grads.arrive(chip_steps - 1, [q0, q1])
    up_theirs = swap(up_grads.last())
    qkv_theirs = swap(qkv_grads.last())
    qkv_sum = (qkv_sums_a + qkv_sums_b)[:, :3, :].transpose(1, 0, 2).reshape(3 * width)
    norm_sums = jnp.concatenate([sums_a[:2], sums_b[:2]], axis=1)
    small = jnp.concatenate(
        [
            norm_sums.reshape(2 * model),
            qkv_sum,
            grad_a[0][0] + grad_b[0][0],
            grad_a[1][0] + grad_b[1][0],
        ]
    )
    small = pair_sum([small] + [across(small, j, ndp) for j in range(2, ndp, 2)])
    small_other = swap(small)
    owned_up, owned_qkv, owned_dense, owned_down = finish(
        (up_grads.kept(), up_theirs),
        (qkv_grads.kept(), qkv_theirs),
        (column_grads.kept(), column_theirs),
    )
    grad_tokens = norm_back(tokens, cotangent, gain, [half_a, half_b], [small_other, owned_up])
    norm_sums = small[: 2 * model] + small_other[: 2 * model]
    norm_sums = [norm_sums] + fence(
        [
            lax.ppermute(norm_sums, "mp", [(i, i ^ j) for i in range(nmp)])
            for j in range(1, nmp)
        ],
        [grad_tokens],
    )
    while len(norm_sums) > 1:
        norm_sums = [a + b for a, b in zip(norm_sums[::2], norm_sums[1::2])]
    norm_sums = norm_sums[0]

    output = (
        tokens.astype(F32)
        + branches.astype(F32)
        + (dense_bias.astype(F32) + down_bias.astype(F32))[None, :]
    ).astype(BF16)

    inner = 3 * width + hidden
    grad_out_bias = small[2 * model + inner :]
    here, there = (a[2 * model : 2 * model + inner] for a in (small, small_other))
    even, odd = jnp.where(core == 0, here, there), jnp.where(core == 0, there, here)
    grad_qkv_bias = jnp.concatenate(
        [a[: 3 * width].reshape(3, width) for a in (even, odd)], axis=1
    )
    grad_up_bias = jnp.concatenate([even[3 * width :], odd[3 * width :]])

    return (
        output,
        grad_tokens,
        norm_sums[:model],
        norm_sums[model:],
        owned_qkv,
        grad_qkv_bias,
        owned_dense,
        grad_out_bias,
        owned_up,
        grad_up_bias,
        owned_down,
        grad_out_bias,
    )


def solution(mesh):
    return jax.shard_map(
        functools.partial(on_device, ndp=mesh.shape["dp"], nmp=mesh.shape["mp"]),
        mesh=mesh,
        in_specs=(
            P(("dp", "mp"), None),
            P(),
            P(),
            P(None, "dp", "mp"),
            P(None, "mp"),
            P("mp", "dp"),
            P(),
            P("dp", "mp"),
            P("mp"),
            P("mp", "dp"),
            P(),
            P(("dp", "mp"), None),
        ),
        out_specs=(
            P(("dp", "mp"), None),
            P(("dp", "mp"), None),
            P(),
            P(),
            P(None, "dp", "mp"),
            P(None, "mp"),
            P("mp", "dp"),
            P(),
            P("dp", "mp"),
            P("mp"),
            P("mp", "dp"),
            P(),
        ),
        check_vma=False,
    )
```

```python
import functools

import jax
import jax.numpy as jnp
import numpy as np
from jax import lax
from jax.experimental import pallas as pl
from jax.experimental.pallas import tpu as pltpu
from jax.sharding import PartitionSpec as P

HEAD_DIM = 64
ROT = 32
EPS = 1e-05
LANES = 128
F32 = jnp.float32
BF16 = jnp.bfloat16
HBM = pl.BlockSpec(memory_space=pltpu.HBM)


def dot(lhs, rhs, lhs_dim, rhs_dim):
    return lax.dot_general(
        lhs, rhs, (((lhs_dim,), (rhs_dim,)), ((), ())), preferred_element_type=F32
    )


def call(kernel, name, operands, deps=(), scalars=(), adds=(), vmem=64, **spec):
    deps, out_shape = tuple(deps), spec.pop("out_shape")
    single = not isinstance(out_shape, list)
    out_shape = [out_shape] if single else out_shape
    out_specs = spec.pop("out_specs")
    out_specs = [out_specs] if single else list(out_specs)
    extra, extra_specs, sizes = [], [], []
    steps = spec["grid"][0] if adds else 1
    for many, addends in adds:
        _, rows, columns = addends[0][0].shape
        block = (many, rows // steps, columns)
        for array, first in addends:
            extra.append(array)
            extra_specs.append(
                pl.BlockSpec(block, lambda i, *at, first=first, many=many: (first // many, i, 0))
            )
        out_shape = out_shape + [jax.ShapeDtypeStruct((many, rows, columns), BF16)]
        out_specs = out_specs + [pl.BlockSpec(block, lambda i, *at: (0, i, 0))]
        sizes.append(len(addends))
    lead, outs = len(scalars) + len(operands), len(out_shape) - len(adds)

    def body(*refs):
        first = lead + len(extra) + len(deps)
        kernel(*refs[:lead], *refs[first : first + outs], *refs[first + outs + len(adds) :])
        sources = refs[lead : lead + len(extra)]
        for n, out in zip(sizes, refs[first + outs : first + outs + len(adds)]):
            out[...] = sum(ref[...].astype(F32) for ref in sources[:n]).astype(BF16)
            sources = sources[n:]

    in_specs = list(spec.pop("in_specs")) + extra_specs + [HBM] * len(deps)
    aliases = spec.pop("input_output_aliases", {})
    if scalars:
        grid_spec = pltpu.PrefetchScalarGridSpec(
            num_scalar_prefetch=len(scalars), in_specs=in_specs, out_specs=out_specs, **spec
        )
        spec = {"grid_spec": grid_spec}
    else:
        spec.update(in_specs=in_specs, out_specs=out_specs)
    results = pl.pallas_call(
        body,
        out_shape=out_shape,
        input_output_aliases=aliases,
        compiler_params=pltpu.CompilerParams(vmem_limit_bytes=vmem << 20),
        cost_estimate=pl.CostEstimate(flops=0, transcendentals=0, bytes_accessed=0),
        name=name,
        **spec,
    )(*scalars, *operands, *extra, *deps)
    return results[0] if single and not adds else results


def fence(values, deps=()):
    return list(
        call(
            lambda *refs: None,
            "fence",
            values,
            deps,
            in_specs=[HBM] * len(values),
            out_specs=[HBM] * len(values),
            out_shape=[jax.ShapeDtypeStruct(v.shape, v.dtype) for v in values],
            input_output_aliases={n: n for n in range(len(values))},
        )
    )


def rotary_tables(length):
    positions = np.arange(length, dtype=np.float32)
    frequency = 10000.0 ** (-np.arange(ROT // 2, dtype=np.float64) * 2.0 / ROT)
    angles = positions[:, None] * frequency.astype(np.float32)[None, :]
    cosine, sine = np.cos(angles.astype(np.float64)), np.sin(angles.astype(np.float64))
    rest = HEAD_DIM - ROT
    none = np.zeros((length, ROT // 2))
    ones, zeros = np.ones((length, rest)), np.zeros((length, rest))
    straight = np.concatenate([cosine, cosine, ones], axis=1)
    left = np.concatenate([-sine, none, zeros], axis=1)
    right = np.concatenate([none, sine, zeros], axis=1)
    return [
        jnp.asarray(np.concatenate([t, t], axis=1).astype(np.float32))
        for t in (straight, left, right)
    ]


def rotated(u, straight, left, right, sign):
    half = ROT // 2
    turned = pltpu.roll(u, LANES - half, 1) * left + pltpu.roll(u, half, 1) * right
    return u * straight + sign * turned


def normalized(x):
    x = x.astype(F32)
    centered = x - jnp.mean(x, axis=1, keepdims=True)
    variance = jnp.mean(centered * centered, axis=1, keepdims=True)
    return centered * lax.rsqrt(variance + EPS)


def block_copies(blocks, place, sems):
    me = lax.axis_index("dp")
    return [
        pltpu.make_async_copy(block, place(lax.bitwise_xor(me, j)), sems.at[j])
        for j, block in enumerate(blocks)
    ]


def span(owner, size):
    return pl.ds(pl.multiple_of(owner * size, size), size)


def rows_at(ref, size):
    return lambda owner: ref.at[pl.ds(pl.multiple_of(owner * size, size), size)]


def columns_at(ref, size):
    return lambda owner: ref.at[:, pl.ds(pl.multiple_of(owner * size, size), size)]


def project_kernel(setup, x_ref, bias_ref, gain_ref, shift_ref, cos_ref, left_ref, right_ref, *rest):
    count, width, hidden = setup
    blocks = rest[:count]
    qkv_ref, act_ref, slope_ref, normed_ref, held, sems = rest[-6:]

    @pl.when(pl.program_id(0) == 0)
    def _():
        loads = block_copies(blocks, rows_at(held, blocks[0].shape[0]), sems)
        for copy in loads:
            copy.start()
        for copy in loads:
            copy.wait()

    x = (normalized(x_ref[...]) * gain_ref[...] + shift_ref[...]).astype(BF16)
    normed_ref[...] = x
    root = 0.7978845608028654
    for t in range((3 * width + hidden) // width):
        columns = slice(t * width, (t + 1) * width)
        y = dot(x, held[:, columns], 1, 0) + bias_ref[:, columns]
        if t < 3:
            for g in range(width // LANES):
                part = y[:, g * LANES : (g + 1) * LANES]
                if t < 2:
                    part = rotated(part, cos_ref[...], left_ref[...], right_ref[...], 1.0)
                if t == 0:
                    part = part * HEAD_DIM**-0.5
                start = t * width + g * LANES
                qkv_ref[:, start : start + LANES] = part.astype(BF16)
        else:
            columns = slice((t - 3) * width, (t - 2) * width)
            square = y * y
            turn = jnp.tanh(root * y * (1.0 + 0.044715 * square))
            half = 0.5 * (1.0 + turn)
            act_ref[:, columns] = (y * half).astype(BF16)
            slope = half * (1.0 + y * (1.0 - turn) * (root + (3.0 * 0.044715 * root) * square))
            slope_ref[:, columns] = slope.astype(BF16)


def project(sequence, x, blocks, bias, gain, shift, tables, width, tile, earlier, deps):
    (length, model), total, count = x.shape, blocks[0].shape[1], len(blocks)
    hidden, steps = total - 3 * width, length // tile
    rows = lambda w: pl.BlockSpec((tile, w), lambda i: (i, 0))
    out = lambda w: pl.BlockSpec((tile, w), lambda i: (sequence * steps + i, 0))
    line = lambda a: pl.BlockSpec(a.shape, lambda i: (0, 0))
    widths = (3 * width, hidden, hidden, model)
    operands = [x, bias, gain, shift, *tables, *blocks]
    return call(
        functools.partial(project_kernel, (count, width, hidden)),
        "project",
        operands + list(earlier),
        deps,
        grid=(steps,),
        in_specs=[rows(model), line(bias), line(gain), line(shift)]
        + [rows(LANES)] * 3
        + [HBM] * (count + len(earlier)),
        out_specs=[out(w) for w in widths],
        out_shape=[jax.ShapeDtypeStruct((2 * length, w), BF16) for w in widths],
        input_output_aliases={len(operands) + n: n for n in range(len(earlier))},
        scratch_shapes=[pltpu.VMEM((model, total), BF16), pltpu.SemaphoreType.DMA((count,))],
    )


def attend_kernel(block, q_ref, k_ref, v_ref, out_ref, lse_ref):
    length = q_ref.shape[0]
    lane = lax.broadcasted_iota(jnp.int32, (1, LANES), 1)
    key = lax.broadcasted_iota(jnp.int32, (block, block), 0)
    causal = key <= lax.broadcasted_iota(jnp.int32, (block, block), 1)
    for i in range(length // block):
        rows, before = pl.ds(i * block, block), pl.ds(0, i * block)
        results = []
        for h in range(2):
            mine = (lane < HEAD_DIM) if h == 0 else (lane >= HEAD_DIM)
            query = jnp.where(mine, q_ref[rows, :], 0)
            near = jnp.where(causal, dot(k_ref[rows, :], query, 1, 1), -1e30)
            highest = jnp.max(near, axis=0, keepdims=True)
            if i:
                far = dot(k_ref[before, :], query, 1, 1)
                highest = jnp.maximum(highest, jnp.max(far, axis=0, keepdims=True))
            near = jnp.exp(near - highest)
            total = jnp.sum(near, axis=0, keepdims=True)
            if i:
                far = jnp.exp(far - highest)
                total = total + jnp.sum(far, axis=0, keepdims=True)
            inverse = 1.0 / total
            result = dot((near * inverse).astype(BF16), v_ref[rows, :], 0, 0)
            if i:
                result = result + dot((far * inverse).astype(BF16), v_ref[before, :], 0, 0)
            results.append(result)
            lse_ref[0, h : h + 1, rows] = highest + jnp.log(total)
        out_ref[rows, :] = jnp.where(lane < HEAD_DIM, results[0], results[1]).astype(BF16)


def pair_specs(length, pairs):
    return lambda off: pl.BlockSpec(
        (length, LANES), lambda g: (g // pairs, off * pairs + g % pairs)
    )


def attend(qkv, length, block, deps):
    width, sequences = qkv.shape[1] // 3, qkv.shape[0] // length
    pairs = width // LANES
    at = pair_specs(length, pairs)
    return call(
        functools.partial(attend_kernel, block),
        "attend",
        [qkv, qkv, qkv],
        deps,
        grid=(sequences * pairs,),
        in_specs=[at(0), at(1), at(2)],
        out_specs=[at(0), pl.BlockSpec((1, 8, length), lambda g: (g, 0, 0))],
        out_shape=[
            jax.ShapeDtypeStruct((qkv.shape[0], width), BF16),
            jax.ShapeDtypeStruct((sequences * pairs, 8, length), F32),
        ],
    )


def attend_back_kernel(
    block,
    q_ref,
    k_ref,
    v_ref,
    grad_ref,
    mixed_ref,
    lse_ref,
    cos_ref,
    left_ref,
    right_ref,
    gq_ref,
    gk_ref,
    gv_ref,
    sum_ref,
    gk_sum,
    gv_sum,
):
    length = q_ref.shape[0]
    lane = lax.broadcasted_iota(jnp.int32, (1, LANES), 1)
    key = lax.broadcasted_iota(jnp.int32, (block, block), 0)
    causal = key <= lax.broadcasted_iota(jnp.int32, (block, block), 1)
    count = length // block
    sum_ref[...] = jnp.zeros_like(sum_ref)

    def put(ref, which, rows, value):
        value = value.astype(BF16)
        ref[rows, :] = value
        sum_ref[0, which : which + 1, :] += jnp.sum(value.astype(F32), axis=0, keepdims=True)

    def unrotated(value, rows):
        return rotated(value, cos_ref[rows, :], left_ref[rows, :], right_ref[rows, :], -1.0)

    for i in reversed(range(count)):
        rows = pl.ds(i * block, block)
        product = grad_ref[rows, :].astype(F32) * mixed_ref[rows, :].astype(F32)
        gq = None
        for h in range(2):
            mine = (lane < HEAD_DIM) if h == 0 else (lane >= HEAD_DIM)
            query = jnp.where(mine, q_ref[rows, :], 0)
            grad = jnp.where(mine, grad_ref[rows, :], 0)
            ones = jnp.where(mine, jnp.ones((8, LANES), F32), 0.0)
            delta = lax.dot_general(
                ones,
                product,
                (((1,), (1,)), ((), ())),
                precision=lax.Precision.HIGHEST,
                preferred_element_type=F32,
            )[0:1, :]
            lse = lse_ref[0, h : h + 1, rows]
            for j in range(i + 1):
                keys = pl.ds(j * block, block)
                key_rows = k_ref[keys, :]
                probs = jnp.exp(dot(key_rows, query, 1, 1) - lse)
                if j == i:
                    probs = jnp.where(causal, probs, 0.0)
                gprobs = dot(v_ref[keys, :], grad, 1, 1)
                gscores = (probs * (gprobs - delta)).astype(BF16)
                gv, gk = dot(probs.astype(BF16), grad, 1, 0), dot(gscores, query, 1, 0)
                if i == count - 1 and h == 0:
                    gv_sum[keys, :] = gv
                    gk_sum[keys, :] = gk
                else:
                    gv_sum[keys, :] += gv
                    gk_sum[keys, :] += gk
                part = dot(gscores, jnp.where(mine, key_rows, 0), 0, 0)
                gq = part if gq is None else gq + part
        put(gq_ref, 0, rows, unrotated(gq * HEAD_DIM**-0.5, rows))
    for i in range(count):
        rows = pl.ds(i * block, block)
        put(gk_ref, 1, rows, unrotated(gk_sum[rows, :], rows))
        put(gv_ref, 2, rows, gv_sum[rows, :])


def attend_back(sequence, qkv, grad, mixed, lse, tables, length, block, deps):
    width = qkv.shape[1] // 3
    pairs = width // LANES
    at = lambda off: pl.BlockSpec((length, LANES), lambda g: (sequence, off * pairs + g))
    out = pl.BlockSpec((length, LANES), lambda g: (0, g))
    table = pl.BlockSpec((length, LANES), lambda g: (0, 0))
    small = pl.BlockSpec((1, 8, length), lambda g: (sequence * pairs + g, 0, 0))
    return call(
        functools.partial(attend_back_kernel, block),
        "attend_back",
        [qkv, qkv, qkv, grad, mixed, lse, *tables],
        deps,
        grid=(pairs,),
        in_specs=[at(0), at(1), at(2), at(0), at(0), small, table, table, table],
        out_specs=[out] * 3 + [pl.BlockSpec((1, 8, LANES), lambda g: (g, 0, 0))],
        out_shape=[jax.ShapeDtypeStruct((length, width), BF16)] * 3
        + [jax.ShapeDtypeStruct((pairs, 8, LANES), F32)],
        scratch_shapes=[pltpu.VMEM((length, LANES), F32)] * 2,
    )


def by_sequence(tile, width, steps):
    return [
        pl.BlockSpec((tile, width), lambda i: (jnp.minimum(i, steps - 1), 0)),
        pl.BlockSpec((tile, width), lambda i: (jnp.maximum(i - steps, 0), 0)),
    ]


def other_first(tile, width, steps):
    return pl.BlockSpec((tile, width), lambda i: ((i + steps) % (2 * steps), 0))


def put_by_sequence(step, steps, value, other_ref, own_ref):
    @pl.when(step < steps)
    def _():
        other_ref[...] = value

    @pl.when(step >= steps)
    def _():
        own_ref[...] = value


def branch_kernel(count, steps, mixed_ref, act_ref, *rest):
    blocks, (other_ref, own_ref, held, sems) = rest[:count], rest[count:]
    step = pl.program_id(0)

    @pl.when(step == 0)
    def _():
        loads = block_copies(blocks, columns_at(held, blocks[0].shape[1]), sems)
        for copy in loads:
            copy.start()
        for copy in loads:
            copy.wait()

    x = jnp.concatenate([mixed_ref[...], act_ref[...]], axis=1)
    put_by_sequence(step, steps, dot(x, held[...], 1, 0).astype(BF16), other_ref, own_ref)


def branch_sums(mixed, act, blocks, tile, deps):
    length, count = mixed.shape[0] // 2, len(blocks)
    inner, model, steps = blocks[0].shape[0], count * blocks[0].shape[1], length // tile
    return call(
        functools.partial(branch_kernel, count, steps),
        "branch_sums",
        [mixed, act, *blocks],
        deps,
        grid=(2 * steps,),
        in_specs=[other_first(tile, a.shape[1], steps) for a in (mixed, act)] + [HBM] * count,
        out_specs=by_sequence(tile, model, steps),
        out_shape=[jax.ShapeDtypeStruct((length, model), BF16)] * 2,
        scratch_shapes=[pltpu.VMEM((inner, model), BF16), pltpu.SemaphoreType.DMA((count,))],
    )


def grad_in_kernel(setup, dy_ref, slope_ref, *rest):
    count, width, hidden = setup
    blocks = rest[:count]
    gmixed_ref, gpre_ref, gsum_ref, dsum_ref, held, sems = rest[-6:]

    @pl.when(pl.program_id(0) == 0)
    def _():
        loads = block_copies(blocks, columns_at(held, blocks[0].shape[1]), sems)
        for copy in loads:
            copy.start()
        gsum_ref[...] = jnp.zeros_like(gsum_ref)
        dsum_ref[...] = jnp.zeros_like(dsum_ref)
        for copy in loads:
            copy.wait()

    dy = dy_ref[...]
    gmixed_ref[...] = dot(dy, held[:width, :], 1, 1).astype(BF16)
    for start in range(0, hidden, width):
        part = slice(start, start + width)
        gact = dot(dy, held[width + start : 2 * width + start, :], 1, 1)
        gpre = (gact * slope_ref[:, part].astype(F32)).astype(BF16)
        gpre_ref[:, part] = gpre
        gsum_ref[0:1, part] += jnp.sum(gpre.astype(F32), axis=0, keepdims=True)
    dsum_ref[0:1, :] += jnp.sum(dy.astype(F32), axis=0, keepdims=True)


def grad_in(sequence, dy, slope, blocks, width, tile, earlier, deps):
    (length, model), hidden, count = dy.shape, slope.shape[1], len(blocks)
    steps = length // tile
    at = lambda w: pl.BlockSpec((tile, w), lambda i: (sequence * steps + i, 0))
    total = lambda w: pl.BlockSpec((8, w), lambda i: (0, 0))
    operands = [dy, slope, *blocks]
    return call(
        functools.partial(grad_in_kernel, (count, width, hidden)),
        "grad_in",
        operands + list(earlier),
        deps,
        grid=(steps,),
        in_specs=[pl.BlockSpec((tile, model), lambda i: (i, 0)), at(hidden)]
        + [HBM] * (count + len(earlier)),
        out_specs=[
            at(width),
            pl.BlockSpec((tile, hidden), lambda i: (i, 0)),
            total(hidden),
            total(model),
        ],
        out_shape=[
            jax.ShapeDtypeStruct((2 * length, width), BF16),
            jax.ShapeDtypeStruct((length, hidden), BF16),
            jax.ShapeDtypeStruct((8, hidden), F32),
            jax.ShapeDtypeStruct((8, model), F32),
        ],
        input_output_aliases={len(operands) + n: n for n in range(len(earlier))},
        scratch_shapes=[
            pltpu.VMEM((width + hidden, model), BF16),
            pltpu.SemaphoreType.DMA((count,)),
        ],
    )


def add_kernel(a_ref, b_ref, out_ref):
    out_ref[...] = (a_ref[...].astype(F32) + b_ref[...].astype(F32)).astype(BF16)


def add_rows(a, b):
    rows = pl.BlockSpec((a.shape[0] // 2, a.shape[1]), lambda i: (i, 0))
    return call(
        add_kernel,
        "add_rows",
        [a, b],
        grid=(2,),
        in_specs=[rows, rows],
        out_specs=rows,
        out_shape=jax.ShapeDtypeStruct(a.shape, BF16),
    )


def grad_normed_kernel(count, half, x_ref, *rest):
    grads, blocks, (out_ref, sum_ref, held, sems) = rest[:8], rest[8 : 8 + 2 * count], rest[-4:]
    (size, total), few, me = blocks[0].shape, count // 2, lax.axis_index("dp")

    @pl.when(pl.program_id(0) == 0)
    def _():
        for start in (True, False):
            for n, block in enumerate(blocks):
                core, j = n // count, n % count
                owner = lax.bitwise_xor(me, j ^ core) - half * few
                columns = slice(core * total, (core + 1) * total)

                @pl.when((owner >= 0) & (owner < few))
                def _(start=start, n=n, block=block, owner=owner, columns=columns):
                    target = held.at[span(owner, size), columns]
                    copy = pltpu.make_async_copy(block, target, sems.at[n])
                    if start:
                        copy.start()
                    else:
                        copy.wait()

        sum_ref[...] = jnp.zeros_like(sum_ref)

    columns = slice(half * few * size, (half + 1) * few * size)
    normal = normalized(x_ref[...])[:, columns]
    g = jnp.concatenate([ref[...] for ref in grads], axis=1)
    result = dot(g, held[...], 1, 1)
    sum_ref[0:1, :] += jnp.sum(result * normal, axis=0, keepdims=True)
    sum_ref[1:2, :] += jnp.sum(result, axis=0, keepdims=True)
    out_ref[...] = result.astype(BF16)


def grad_normed_sums(half, grads, x, blocks, tile, deps, adds=()):
    (length, model), count, total = x.shape, len(blocks) // 2, blocks[0].shape[1]
    part = model // 2
    rows = lambda w: pl.BlockSpec((tile, w), lambda i: (i, 0))
    return call(
        functools.partial(grad_normed_kernel, count, half),
        "grad_normed_sums",
        [x, *grads, *blocks],
        deps,
        adds=adds,
        grid=(length // tile,),
        in_specs=[rows(model)] + [rows(g.shape[1]) for g in grads] + [HBM] * (2 * count),
        out_specs=[rows(part), pl.BlockSpec((8, part), lambda i: (0, 0))],
        out_shape=[
            jax.ShapeDtypeStruct((length, part), BF16),
            jax.ShapeDtypeStruct((8, part), F32),
        ],
        scratch_shapes=[
            pltpu.VMEM((part, 2 * total), BF16),
            pltpu.SemaphoreType.DMA((2 * count,)),
        ],
    )


def weight_grad_kernel(writes, left, rows, many, groups, at_ref, *refs):
    cuts, (*refs, held, grad, sems) = refs[:many], refs[many:]
    whole, outs = refs[: len(refs) - len(writes)], refs[len(refs) - len(writes) :]
    step, core, loads, first = pl.program_id(0), lax.rem(lax.axis_index("dp"), 2), [], 0
    for group in groups:
        below = 0
        for ref in whole[:group]:
            columns = pl.ds(first, ref.shape[1])
            for start in range(0, ref.shape[0], rows):
                target = held.at[pl.ds(below + start, rows), columns]
                loads.append((ref.at[pl.ds(start, rows)], target))
            below += ref.shape[0]
        first += whole[0].shape[1]
        whole = whole[group:]
    loads = [pltpu.make_async_copy(*pair, sems.at[n]) for n, pair in enumerate(loads)]

    @pl.when(step == 0)
    def _():
        for copy in loads:
            copy.start()
        for copy in loads:
            copy.wait()

    cut = jnp.concatenate([ref[...] for ref in cuts], axis=0)
    pair = (cut, held[...]) if left else (held[...], cut)
    grad[...] = dot(*pair, 0, 0).astype(BF16)
    size = cut.shape[1] // 2
    for half, steps, out_ref in writes_of(writes, outs):
        here = functools.reduce(jnp.logical_or, [step == s for s in steps])

        @pl.when(here)
        def _(half=half, out_ref=out_ref):
            mine = span(core if half == 0 else 1 - core, size)
            out_ref[0] = grad[mine, :] if left else grad[:, mine]


def writes_of(writes, outs):
    return [(half, steps, out) for (half, steps), out in zip(writes, outs)]


def block_table(me, count):
    plan, chips = scatter_plan(count), count // 2
    order = [j // 2 for s in plan[0] for j in s]
    sets = [(half, s) for s in range(len(plan[0])) for half in range(2)]
    writes = [(half, [order.index(j // 2) for j in plan[half][s]]) for half, s in sets]
    table = []
    for _, steps in writes:
        for i in range(chips):
            later = [w for w in steps if w >= i]
            table.append(steps.index(min(later) if later else max(steps)))
    owners = lax.bitwise_xor(me // 2, jnp.array(order, jnp.int32))
    return sets, writes, jnp.concatenate([owners, jnp.array(table, jnp.int32)])


def weight_grads(at, xs, gs, count, deps, left, adds=()):
    plan, chips = scatter_plan(count), count // 2
    sets, writes, _ = block_table(0, count)
    cut, whole = (xs, gs) if left else (gs, xs)
    groups, length = [len(g) for g in whole], sum(a.shape[0] for a in whole[0])
    size, full = cut[0].shape[1] // count, sum(g[0].shape[1] for g in whole)
    shape, whole = (size, full) if left else (full, size), [a for g in whole for a in g]
    rows = length // 4
    pieces = 4 * len(groups)

    def out(n):
        return pl.BlockSpec((1, *shape), lambda i, at: (at[chips * (n + 1) + i], 0, 0))

    outs = call(
        functools.partial(weight_grad_kernel, writes, left, rows, len(cut), groups),
        "weight_grads",
        [*cut, *whole],
        deps,
        (at,),
        adds,
        grid=(chips,),
        in_specs=[pl.BlockSpec((a.shape[0], 2 * size), lambda i, at: (0, at[i])) for a in cut]
        + [HBM] * len(whole),
        out_specs=[out(n) for n in range(len(sets))],
        out_shape=[
            jax.ShapeDtypeStruct((len(plan[half][s]), *shape), BF16) for half, s in sets
        ],
        scratch_shapes=[
            pltpu.VMEM((length, full), BF16),
            pltpu.VMEM((2 * size, full) if left else (full, 2 * size), BF16),
            pltpu.SemaphoreType.DMA((pieces,)),
        ],
    )
    blocks = [[o for o, (half, _) in zip(outs, sets) if half == h] for h in range(2)]
    return (blocks, *outs[len(sets) :]) if adds else blocks


def finish_kernel(sizes, width, *refs):
    ins, (up_ref, qkv_ref, dense_ref, down_ref) = refs[:-4], refs[-4:]
    core = lax.rem(lax.axis_index("dp"), 2)
    pairs = []
    for size in sizes:
        mine = sum(ref[0].astype(F32) for ref in ins[: size - 1])
        pairs.append(((core, mine), (1 - core, ins[size - 1][0].astype(F32))))
        ins = ins[size:]
    for where, value in pairs[0]:
        up_ref[:, span(where, value.shape[1])] = value
    for where, value in pairs[1]:
        for c in range(3):
            qkv_ref[c, :, span(where, width)] = value[:, c * width : (c + 1) * width]
    for out_ref, pair in ((dense_ref, pairs[2]), (down_ref, pairs[3])):
        for where, value in pair:
            out_ref[where] = value


def finish(up, qkv, columns):
    (size, hidden), width = up[1].shape, qkv[1].shape[1] // 3
    steps = hidden // width
    operands, specs, sizes = [], [], []

    def take(parts, rows, base):
        addends, theirs = parts
        for array, first in [*addends, (theirs[None], 0)]:
            operands.append(array)
            specs.append(
                pl.BlockSpec(
                    (1, rows, array.shape[2]), lambda i, first=first: (first, base + i, 0)
                )
            )
        sizes.append(len(addends) + 1)

    take(up, size // steps, 0)
    take(qkv, size // steps, 0)
    take(columns, width // steps, 0)
    take(columns, width, 1)
    owned_up, owned_qkv, owned_dense, owned_down = call(
        lambda *refs: finish_kernel(sizes, width, *refs),
        "finish",
        operands,
        grid=(steps,),
        in_specs=specs,
        out_specs=[
            pl.BlockSpec((size // steps, 2 * hidden), lambda i: (i, 0)),
            pl.BlockSpec((3, size // steps, 2 * width), lambda i: (0, i, 0)),
            pl.BlockSpec((2, width // steps, size), lambda i: (0, i, 0)),
            pl.BlockSpec((2, width, size), lambda i: (0, i, 0)),
        ],
        out_shape=[
            jax.ShapeDtypeStruct((size, 2 * hidden), F32),
            jax.ShapeDtypeStruct((3, size, 2 * width), F32),
            jax.ShapeDtypeStruct((2, width, size), F32),
            jax.ShapeDtypeStruct((2, hidden, size), F32),
        ],
    )
    return (
        owned_up,
        owned_qkv,
        owned_dense.reshape(2 * width, size),
        owned_down.reshape(2 * hidden, size),
    )


def norm_back_kernel(tokens_ref, dy_ref, gain_ref, left_ref, right_ref, out_ref):
    x = tokens_ref[...].astype(F32)
    centered = x - jnp.mean(x, axis=1, keepdims=True)
    inverse_std = lax.rsqrt(jnp.mean(centered * centered, axis=1, keepdims=True) + EPS)
    normal = centered * inverse_std
    grad = jnp.concatenate([left_ref[...], right_ref[...]], axis=1).astype(F32)
    scaled = grad * gain_ref[...]
    first_mean = jnp.mean(scaled, axis=1, keepdims=True)
    second_mean = jnp.mean(scaled * normal, axis=1, keepdims=True)
    back = (scaled - first_mean - normal * second_mean) * inverse_std
    out_ref[...] = (dy_ref[...].astype(F32) + back).astype(BF16)


def norm_back(tokens, dy, gain, halves, deps):
    rows, model = tokens.shape
    tile = min(128, rows)
    part = lambda w: pl.BlockSpec((tile, w), lambda i: (i, 0))
    return call(
        norm_back_kernel,
        "norm_back",
        [tokens, dy, gain, *halves],
        deps,
        grid=(rows // tile,),
        in_specs=[part(model), part(model), pl.BlockSpec((1, model), lambda i: (0, 0))]
        + [part(model // 2)] * 2,
        out_specs=part(model),
        out_shape=jax.ShapeDtypeStruct((rows, model), BF16),
    )


def across(value, bit, count):
    return lax.ppermute(value, "dp", [(i, i ^ bit) for i in range(count)])


def added(addends):
    return sum(a.astype(F32) for a in addends).astype(BF16)


def pair_sum(parts):
    while len(parts) > 1:
        parts = [a + b for a, b in zip(parts[::2], parts[1::2])]
    return parts[0]


def chip_bits(count):
    bits, bit = [], 2
    while bit < count:
        bits.append(bit)
        bit *= 2
    return bits


class BlockGather:
    def __init__(self, own, sibling, count):
        self.held, self.count = {0: own, 1: sibling}, count
        self.orders = (chip_bits(count), chip_bits(count)[::-1])

    def own_to(self, s):
        if s < len(self.orders[0]):
            for half in range(2):
                bit = self.orders[half][s]
                self.held[half ^ bit] = across(self.held[half], bit, self.count)

    def rest(self):
        for s in range(1, len(self.orders[0])):
            for half in range(2):
                order = self.orders[half]
                for j in [j for j in self.held if j % 2 == half]:
                    if j ^ order[s] not in self.held and not any(j & b for b in order[s:]):
                        self.held[j ^ order[s]] = across(self.held[j], order[s], self.count)

    def fenced(self, others=(), deps=()):
        keys = sorted(self.held)
        values = fence([self.held[j] for j in keys] + list(others), deps)
        self.held = dict(zip(keys, values))
        return values[len(keys) :]

    def blocks(self):
        return [self.held[j] for j in range(self.count)]


def scatter_orders(count):
    return (chip_bits(count)[::-1], chip_bits(count))


def scatter_plan(count):
    plan = []
    for half, order in enumerate(scatter_orders(count)):
        sets, rest = [[half]], [half]
        for bit in reversed(order):
            sets.insert(0, [j ^ bit for j in rest])
            rest = sets[0] + rest
        plan.append(sets)
    return plan


class BlockScatter:
    def __init__(self, halves, count):
        self.count, self.orders, self.plan = count, scatter_orders(count), scatter_plan(count)
        self.held = [[[(a, 0)] for a in arrays] for arrays in halves]
        self.steps = len(self.orders[0])

    def parts(self, half, s):
        many = len(self.plan[half][s])
        return [a[first : first + many] for a, first in self.held[half][s]]

    def total(self, half, s):
        if len(self.held[half][s]) > 1:
            self.held[half][s] = [(added(self.parts(half, s)), 0)]
        return self.parts(half, s)[0]

    def ready(self, s):
        return [self.total(half, s) for half in range(2)]

    def adds(self, s):
        return [(len(self.plan[half][s]), self.held[half][s]) for half in range(2)]

    def settle(self, s, sums):
        for half in range(2):
            self.held[half][s] = [(sums[half], 0)]

    def send(self, s):
        return [across(self.total(h, s), self.orders[h][s], self.count) for h in range(2)]

    def arrive(self, s, came):
        for half in range(2):
            first = 0
            for t in range(s + 1, len(self.plan[half])):
                self.held[half][t].append((came[half], first))
                first += len(self.plan[half][t])

    def between(self):
        for s in range(1, self.steps - 1):
            self.arrive(s, self.send(s))

    def last(self):
        return self.total(1, -1)[0]

    def kept(self):
        return self.held[0][-1]


def on_device(
    tokens,
    norm_gain,
    norm_bias,
    qkv_weight,
    qkv_bias,
    dense_weight,
    dense_bias,
    up_weight,
    up_bias,
    down_weight,
    down_bias,
    cotangent,
    *,
    ndp,
    nmp,
):
    me = lax.axis_index("dp")
    core = me % 2
    length, model = tokens.shape[0] * nmp, tokens.shape[1]
    tile, block = min(256, length), min(512, length)
    width, hidden = qkv_weight.shape[2] // 2, up_weight.shape[1] // 2
    chip_steps = len(chip_bits(ndp))
    rank = lambda array, axis, which, size: lax.dynamic_slice_in_dim(
        array, which * size, size, axis
    )

    def row_pack(which):
        qkv = rank(qkv_weight, 2, which, width)
        return jnp.concatenate([qkv[0], qkv[1], qkv[2], rank(up_weight, 1, which, hidden)], axis=1)

    def column_pack(which):
        return jnp.concatenate(
            [rank(dense_weight, 0, which, width), rank(down_weight, 0, which, hidden)], axis=0
        )

    pairs = width // LANES
    swap = lambda array: across(array, 1, ndp)
    line_gather = lambda array: lax.all_gather(array, "mp", axis=0, tiled=True)
    line_scatter = lambda array: lax.psum_scatter(array, "mp", scatter_dimension=0, tiled=True)
    x_own, dy_own = line_gather(tokens), line_gather(cotangent)
    bias = jnp.concatenate(
        [
            rank(qkv_bias, 1, core, width).astype(F32).reshape(1, 3 * width),
            rank(up_bias[None, :], 1, core, hidden).astype(F32),
        ],
        axis=1,
    )
    gain, shift = norm_gain.astype(F32)[None, :], norm_bias.astype(F32)[None, :]
    rows = BlockGather(row_pack(core), swap(row_pack(1 - core)), ndp)
    columns = BlockGather(column_pack(core), swap(column_pack(1 - core)), ndp)
    rows.own_to(0)
    _, _, at = block_table(me, ndp)
    at, bias, gain, shift = rows.fenced([at, bias, gain, shift], columns.held.values())
    rows.own_to(1)
    rows.fenced()
    rows.rest()
    x_own, *held = fence([x_own, columns.held[0], columns.held[1]], rows.blocks())
    columns.held = dict(enumerate(held))

    tables = rotary_tables(length)
    x_other = swap(x_own)
    columns.own_to(0)
    common = (rows.blocks(), bias, gain, shift, tables, width, tile)
    first = project(0, x_own, *common, (), [columns.held[0]])
    (x_other,) = columns.fenced([x_other], [first[0]])
    columns.own_to(1)
    qkv, act, slope, normed = project(1, x_other, *common, first, [columns.held[0]])
    held = columns.fenced(rows.blocks(), [qkv])
    columns.rest()
    row_blocks, row_others = held, [swap(a) for a in held[:3]]
    mixed, lse = attend(qkv, length, block, [columns.held[0]])
    row_others = columns.fenced(row_others, [mixed])
    row_blocks[3:] = fence(row_blocks[3:], [row_others[0]])
    row_others += [swap(a) for a in row_blocks[3:]]
    other_sums, own_sums = branch_sums(mixed, act, columns.blocks(), tile, [row_blocks[3]])
    other_sums, dy_own, *row_others[3:] = fence([other_sums, dy_own, *row_others[3:]], [own_sums])
    theirs = swap(other_sums)
    dy_other = swap(dy_own)

    grads = (slope, columns.blocks(), width, tile)
    gmixed, gpre_own, *grad_a = grad_in(0, dy_own, *grads, (), [own_sums])
    theirs, dy_other = fence([theirs, dy_other], [grad_a[0]])
    total = add_rows(own_sums, theirs)
    branches = line_scatter(total)
    gmixed, gpre_other, *grad_b = grad_in(1, dy_other, *grads, [gmixed], [total])
    (gpre_sent,) = fence([gpre_other])
    gpre_came = swap(gpre_sent)
    column_grads = BlockScatter(
        weight_grads(at, [[mixed], [act]], [dy_own, dy_other], ndp, [gpre_sent], left=False), ndp
    )
    (gpre_came,) = fence([gpre_came], [column_grads.held[0][0][0][0]])
    column_came = column_grads.send(0)
    back = lambda sequence, deps: attend_back(
        sequence, qkv, gmixed, mixed, lse, tables, length, block, deps
    )
    *other, qkv_sums_b = back(1, [gpre_came])
    came = [swap(a) for a in other]
    *own, qkv_sums_a = back(0, [other[0]])
    came = fence([*came, *column_came], [own[0]])
    column_came, came = came[3:], came[:3]
    column_grads.arrive(0, column_came)
    column_grads.between()
    all_grads = [*own, gpre_own, *came, gpre_came]

    def normed_half(half, deps, adds=()):
        return grad_normed_sums(
            half, all_grads, x_own, [*row_blocks, *row_others], tile, deps, adds
        )

    total_a, sums_a, *settled = normed_half(0, [], column_grads.adds(chip_steps - 1))
    column_grads.settle(chip_steps - 1, settled)
    half_a = line_scatter(total_a)
    column_came = column_grads.send(chip_steps - 1)
    up_grads = BlockScatter(
        weight_grads(at, [normed], [[gpre_own, gpre_sent]], ndp, [sums_a], left=True), ndp
    )
    c0, c1, branches, u0, u1 = fence(
        [*column_came, branches, *(up_grads.held[h][0][0][0] for h in range(2))]
    )
    up_grads.held[0][0], up_grads.held[1][0] = [(u0, 0)], [(u1, 0)]
    up_came = up_grads.send(0)
    column_grads.arrive(chip_steps - 1, [c0, c1])
    blocks, column_last = weight_grads(
        at,
        [normed],
        [[a, b] for a, b in zip(own, other)],
        ndp,
        [c0],
        True,
        [column_grads.adds(len(column_grads.plan[1]) - 1)[1]],
    )
    qkv_grads = BlockScatter(blocks, ndp)
    qkv_came = qkv_grads.send(0)
    column_theirs = swap(column_last[0])
    total_b, sums_b = normed_half(1, [qkv_grads.held[0][0][0][0]])
    half_b = line_scatter(total_b)
    u0, u1, q0, q1, half_a = fence([*up_came, *qkv_came, half_a], [sums_b, column_theirs])
    up_grads.arrive(0, [u0, u1])
    qkv_grads.arrive(0, [q0, q1])
    up_grads.between()
    qkv_grads.between()
    up_came, qkv_came = up_grads.send(chip_steps - 1), qkv_grads.send(chip_steps - 1)
    u0, u1, q0, q1, branches, sums_b, column_theirs = fence(
        [*up_came, *qkv_came, branches, sums_b, column_theirs]
    )
    up_grads.arrive(chip_steps - 1, [u0, u1])
    qkv_grads.arrive(chip_steps - 1, [q0, q1])
    up_theirs = swap(up_grads.last())
    qkv_theirs = swap(qkv_grads.last())
    qkv_sum = (qkv_sums_a + qkv_sums_b)[:, :3, :].transpose(1, 0, 2).reshape(3 * width)
    norm_sums = jnp.concatenate([sums_a[:2], sums_b[:2]], axis=1)
    small = jnp.concatenate(
        [
            norm_sums.reshape(2 * model),
            qkv_sum,
            grad_a[0][0] + grad_b[0][0],
            grad_a[1][0] + grad_b[1][0],
        ]
    )
    small = pair_sum([small] + [across(small, j, ndp) for j in range(2, ndp, 2)])
    small_other = swap(small)
    owned_up, owned_qkv, owned_dense, owned_down = finish(
        (up_grads.kept(), up_theirs),
        (qkv_grads.kept(), qkv_theirs),
        (column_grads.kept(), column_theirs),
    )
    grad_tokens = norm_back(tokens, cotangent, gain, [half_a, half_b], [small_other, owned_up])
    norm_sums = small[: 2 * model] + small_other[: 2 * model]
    norm_sums = [norm_sums] + fence(
        [
            lax.ppermute(norm_sums, "mp", [(i, i ^ j) for i in range(nmp)])
            for j in range(1, nmp)
        ],
        [grad_tokens],
    )
    while len(norm_sums) > 1:
        norm_sums = [a + b for a, b in zip(norm_sums[::2], norm_sums[1::2])]
    norm_sums = norm_sums[0]

    output = (
        tokens.astype(F32)
        + branches.astype(F32)
        + (dense_bias.astype(F32) + down_bias.astype(F32))[None, :]
    ).astype(BF16)

    inner = 3 * width + hidden
    grad_out_bias = small[2 * model + inner :]
    here, there = (a[2 * model : 2 * model + inner] for a in (small, small_other))
    even, odd = jnp.where(core == 0, here, there), jnp.where(core == 0, there, here)
    grad_qkv_bias = jnp.concatenate(
        [a[: 3 * width].reshape(3, width) for a in (even, odd)], axis=1
    )
    grad_up_bias = jnp.concatenate([even[3 * width :], odd[3 * width :]])

    return (
        output,
        grad_tokens,
        norm_sums[:model],
        norm_sums[model:],
        owned_qkv,
        grad_qkv_bias,
        owned_dense,
        grad_out_bias,
        owned_up,
        grad_up_bias,
        owned_down,
        grad_out_bias,
    )


def solution(mesh):
    return jax.shard_map(
        functools.partial(on_device, ndp=mesh.shape["dp"], nmp=mesh.shape["mp"]),
        mesh=mesh,
        in_specs=(
            P(("dp", "mp"), None),
            P(),
            P(),
            P(None, "dp", "mp"),
            P(None, "mp"),
            P("mp", "dp"),
            P(),
            P("dp", "mp"),
            P("mp"),
            P("mp", "dp"),
            P(),
            P(("dp", "mp"), None),
        ),
        out_specs=(
            P(("dp", "mp"), None),
            P(("dp", "mp"), None),
            P(),
            P(),
            P(None, "dp", "mp"),
            P(None, "mp"),
            P("mp", "dp"),
            P(),
            P("dp", "mp"),
            P("mp"),
            P("mp", "dp"),
            P(),
        ),
        check_vma=False,
    )
```

```python
import functools

import jax
import jax.numpy as jnp
import numpy as np
from jax import lax
from jax.experimental import pallas as pl
from jax.experimental.pallas import tpu as pltpu
from jax.sharding import PartitionSpec as P

HEAD_DIM = 64
ROT = 32
EPS = 1e-05
LANES = 128
F32 = jnp.float32
BF16 = jnp.bfloat16
HBM = pl.BlockSpec(memory_space=pltpu.HBM)


def dot(lhs, rhs, lhs_dim, rhs_dim):
    return lax.dot_general(
        lhs, rhs, (((lhs_dim,), (rhs_dim,)), ((), ())), preferred_element_type=F32
    )


def call(kernel, name, operands, deps=(), scalars=(), adds=(), vmem=64, **spec):
    deps, out_shape = tuple(deps), spec.pop("out_shape")
    single = not isinstance(out_shape, list)
    out_shape = [out_shape] if single else out_shape
    out_specs = spec.pop("out_specs")
    out_specs = [out_specs] if single else list(out_specs)
    extra, extra_specs, sizes = [], [], []
    steps = spec["grid"][0] if adds else 1
    for many, addends in adds:
        _, rows, columns = addends[0][0].shape
        block = (many, rows // steps, columns)
        for array, first in addends:
            extra.append(array)
            extra_specs.append(
                pl.BlockSpec(block, lambda i, *at, first=first, many=many: (first // many, i, 0))
            )
        out_shape = out_shape + [jax.ShapeDtypeStruct((many, rows, columns), BF16)]
        out_specs = out_specs + [pl.BlockSpec(block, lambda i, *at: (0, i, 0))]
        sizes.append(len(addends))
    lead, outs = len(scalars) + len(operands), len(out_shape) - len(adds)

    def body(*refs):
        first = lead + len(extra) + len(deps)
        kernel(*refs[:lead], *refs[first : first + outs], *refs[first + outs + len(adds) :])
        sources = refs[lead : lead + len(extra)]
        for n, out in zip(sizes, refs[first + outs : first + outs + len(adds)]):
            out[...] = sum(ref[...].astype(F32) for ref in sources[:n]).astype(BF16)
            sources = sources[n:]

    in_specs = list(spec.pop("in_specs")) + extra_specs + [HBM] * len(deps)
    aliases = spec.pop("input_output_aliases", {})
    if scalars:
        grid_spec = pltpu.PrefetchScalarGridSpec(
            num_scalar_prefetch=len(scalars), in_specs=in_specs, out_specs=out_specs, **spec
        )
        spec = {"grid_spec": grid_spec}
    else:
        spec.update(in_specs=in_specs, out_specs=out_specs)
    results = pl.pallas_call(
        body,
        out_shape=out_shape,
        input_output_aliases=aliases,
        compiler_params=pltpu.CompilerParams(vmem_limit_bytes=vmem << 20),
        cost_estimate=pl.CostEstimate(flops=0, transcendentals=0, bytes_accessed=0),
        name=name,
        **spec,
    )(*scalars, *operands, *extra, *deps)
    return results[0] if single and not adds else results


def fence(values, deps=()):
    return list(
        call(
            lambda *refs: None,
            "fence",
            values,
            deps,
            in_specs=[HBM] * len(values),
            out_specs=[HBM] * len(values),
            out_shape=[jax.ShapeDtypeStruct(v.shape, v.dtype) for v in values],
            input_output_aliases={n: n for n in range(len(values))},
        )
    )


def rotary_tables(length):
    positions = np.arange(length, dtype=np.float32)
    frequency = 10000.0 ** (-np.arange(ROT // 2, dtype=np.float64) * 2.0 / ROT)
    angles = positions[:, None] * frequency.astype(np.float32)[None, :]
    cosine, sine = np.cos(angles.astype(np.float64)), np.sin(angles.astype(np.float64))
    rest = HEAD_DIM - ROT
    none = np.zeros((length, ROT // 2))
    ones, zeros = np.ones((length, rest)), np.zeros((length, rest))
    straight = np.concatenate([cosine, cosine, ones], axis=1)
    left = np.concatenate([-sine, none, zeros], axis=1)
    right = np.concatenate([none, sine, zeros], axis=1)
    return [
        jnp.asarray(np.concatenate([t, t], axis=1).astype(np.float32))
        for t in (straight, left, right)
    ]


def rotated(u, straight, left, right, sign):
    half = ROT // 2
    turned = pltpu.roll(u, LANES - half, 1) * left + pltpu.roll(u, half, 1) * right
    return u * straight + sign * turned


def normalized(x):
    x = x.astype(F32)
    centered = x - jnp.mean(x, axis=1, keepdims=True)
    variance = jnp.mean(centered * centered, axis=1, keepdims=True)
    return centered * lax.rsqrt(variance + EPS)


def block_copies(blocks, place, sems):
    me = lax.axis_index("dp")
    return [
        pltpu.make_async_copy(block, place(lax.bitwise_xor(me, j)), sems.at[j])
        for j, block in enumerate(blocks)
    ]


def span(owner, size):
    return pl.ds(pl.multiple_of(owner * size, size), size)


def rows_at(ref, size):
    return lambda owner: ref.at[pl.ds(pl.multiple_of(owner * size, size), size)]


def columns_at(ref, size):
    return lambda owner: ref.at[:, pl.ds(pl.multiple_of(owner * size, size), size)]


def project_kernel(setup, x_ref, bias_ref, gain_ref, shift_ref, cos_ref, left_ref, right_ref, *rest):
    count, width, hidden = setup
    blocks = rest[:count]
    qkv_ref, act_ref, slope_ref, normed_ref, held, sems = rest[-6:]

    @pl.when(pl.program_id(0) == 0)
    def _():
        loads = block_copies(blocks, rows_at(held, blocks[0].shape[0]), sems)
        for copy in loads:
            copy.start()
        for copy in loads:
            copy.wait()

    x = (normalized(x_ref[...]) * gain_ref[...] + shift_ref[...]).astype(BF16)
    normed_ref[...] = x
    root = 0.7978845608028654
    for t in range((3 * width + hidden) // width):
        columns = slice(t * width, (t + 1) * width)
        y = dot(x, held[:, columns], 1, 0) + bias_ref[:, columns]
        if t < 3:
            for g in range(width // LANES):
                part = y[:, g * LANES : (g + 1) * LANES]
                if t < 2:
                    part = rotated(part, cos_ref[...], left_ref[...], right_ref[...], 1.0)
                if t == 0:
                    part = part * HEAD_DIM**-0.5
                start = t * width + g * LANES
                qkv_ref[:, start : start + LANES] = part.astype(BF16)
        else:
            columns = slice((t - 3) * width, (t - 2) * width)
            square = y * y
            turn = jnp.tanh(root * y * (1.0 + 0.044715 * square))
            half = 0.5 * (1.0 + turn)
            act_ref[:, columns] = (y * half).astype(BF16)
            slope = half * (1.0 + y * (1.0 - turn) * (root + (3.0 * 0.044715 * root) * square))
            slope_ref[:, columns] = slope.astype(BF16)


def project(sequence, x, blocks, bias, gain, shift, tables, width, tile, earlier, deps):
    (length, model), total, count = x.shape, blocks[0].shape[1], len(blocks)
    hidden, steps = total - 3 * width, length // tile
    rows = lambda w: pl.BlockSpec((tile, w), lambda i: (i, 0))
    out = lambda w: pl.BlockSpec((tile, w), lambda i: (sequence * steps + i, 0))
    line = lambda a: pl.BlockSpec(a.shape, lambda i: (0, 0))
    widths = (3 * width, hidden, hidden, model)
    operands = [x, bias, gain, shift, *tables, *blocks]
    return call(
        functools.partial(project_kernel, (count, width, hidden)),
        "project",
        operands + list(earlier),
        deps,
        grid=(steps,),
        in_specs=[rows(model), line(bias), line(gain), line(shift)]
        + [rows(LANES)] * 3
        + [HBM] * (count + len(earlier)),
        out_specs=[out(w) for w in widths],
        out_shape=[jax.ShapeDtypeStruct((2 * length, w), BF16) for w in widths],
        input_output_aliases={len(operands) + n: n for n in range(len(earlier))},
        scratch_shapes=[pltpu.VMEM((model, total), BF16), pltpu.SemaphoreType.DMA((count,))],
    )


def attend_kernel(block, q_ref, k_ref, v_ref, out_ref, lse_ref):
    length = q_ref.shape[0]
    lane = lax.broadcasted_iota(jnp.int32, (1, LANES), 1)
    key = lax.broadcasted_iota(jnp.int32, (block, block), 0)
    causal = key <= lax.broadcasted_iota(jnp.int32, (block, block), 1)
    for i in range(length // block):
        rows, before = pl.ds(i * block, block), pl.ds(0, i * block)
        results = []
        for h in range(2):
            mine = (lane < HEAD_DIM) if h == 0 else (lane >= HEAD_DIM)
            query = jnp.where(mine, q_ref[rows, :], 0)
            near = jnp.where(causal, dot(k_ref[rows, :], query, 1, 1), -1e30)
            highest = jnp.max(near, axis=0, keepdims=True)
            if i:
                far = dot(k_ref[before, :], query, 1, 1)
                highest = jnp.maximum(highest, jnp.max(far, axis=0, keepdims=True))
            near = jnp.exp(near - highest)
            total = jnp.sum(near, axis=0, keepdims=True)
            if i:
                far = jnp.exp(far - highest)
                total = total + jnp.sum(far, axis=0, keepdims=True)
            inverse = 1.0 / total
            result = dot((near * inverse).astype(BF16), v_ref[rows, :], 0, 0)
            if i:
                result = result + dot((far * inverse).astype(BF16), v_ref[before, :], 0, 0)
            results.append(result)
            lse_ref[0, h : h + 1, rows] = highest + jnp.log(total)
        out_ref[rows, :] = jnp.where(lane < HEAD_DIM, results[0], results[1]).astype(BF16)


def pair_specs(length, pairs):
    return lambda off: pl.BlockSpec(
        (length, LANES), lambda g: (g // pairs, off * pairs + g % pairs)
    )


def attend(qkv, length, block, deps):
    width, sequences = qkv.shape[1] // 3, qkv.shape[0] // length
    pairs = width // LANES
    at = pair_specs(length, pairs)
    return call(
        functools.partial(attend_kernel, block),
        "attend",
        [qkv, qkv, qkv],
        deps,
        grid=(sequences * pairs,),
        in_specs=[at(0), at(1), at(2)],
        out_specs=[at(0), pl.BlockSpec((1, 8, length), lambda g: (g, 0, 0))],
        out_shape=[
            jax.ShapeDtypeStruct((qkv.shape[0], width), BF16),
            jax.ShapeDtypeStruct((sequences * pairs, 8, length), F32),
        ],
    )


def attend_back_kernel(
    block,
    q_ref,
    k_ref,
    v_ref,
    grad_ref,
    mixed_ref,
    lse_ref,
    cos_ref,
    left_ref,
    right_ref,
    gq_ref,
    gk_ref,
    gv_ref,
    sum_ref,
    gk_sum,
    gv_sum,
):
    length = q_ref.shape[0]
    lane = lax.broadcasted_iota(jnp.int32, (1, LANES), 1)
    key = lax.broadcasted_iota(jnp.int32, (block, block), 0)
    causal = key <= lax.broadcasted_iota(jnp.int32, (block, block), 1)
    count = length // block
    sum_ref[...] = jnp.zeros_like(sum_ref)

    def put(ref, which, rows, value):
        value = value.astype(BF16)
        ref[rows, :] = value
        sum_ref[0, which : which + 1, :] += jnp.sum(value.astype(F32), axis=0, keepdims=True)

    def unrotated(value, rows):
        return rotated(value, cos_ref[rows, :], left_ref[rows, :], right_ref[rows, :], -1.0)

    for i in reversed(range(count)):
        rows = pl.ds(i * block, block)
        product = grad_ref[rows, :].astype(F32) * mixed_ref[rows, :].astype(F32)
        gq = None
        for h in range(2):
            mine = (lane < HEAD_DIM) if h == 0 else (lane >= HEAD_DIM)
            query = jnp.where(mine, q_ref[rows, :], 0)
            grad = jnp.where(mine, grad_ref[rows, :], 0)
            ones = jnp.where(mine, jnp.ones((8, LANES), F32), 0.0)
            delta = lax.dot_general(
                ones,
                product,
                (((1,), (1,)), ((), ())),
                precision=lax.Precision.HIGHEST,
                preferred_element_type=F32,
            )[0:1, :]
            lse = lse_ref[0, h : h + 1, rows]
            for j in range(i + 1):
                keys = pl.ds(j * block, block)
                key_rows = k_ref[keys, :]
                probs = jnp.exp(dot(key_rows, query, 1, 1) - lse)
                if j == i:
                    probs = jnp.where(causal, probs, 0.0)
                gprobs = dot(v_ref[keys, :], grad, 1, 1)
                gscores = (probs * (gprobs - delta)).astype(BF16)
                gv, gk = dot(probs.astype(BF16), grad, 1, 0), dot(gscores, query, 1, 0)
                if i == count - 1 and h == 0:
                    gv_sum[keys, :] = gv
                    gk_sum[keys, :] = gk
                else:
                    gv_sum[keys, :] += gv
                    gk_sum[keys, :] += gk
                part = dot(gscores, jnp.where(mine, key_rows, 0), 0, 0)
                gq = part if gq is None else gq + part
        put(gq_ref, 0, rows, unrotated(gq * HEAD_DIM**-0.5, rows))
    for i in range(count):
        rows = pl.ds(i * block, block)
        put(gk_ref, 1, rows, unrotated(gk_sum[rows, :], rows))
        put(gv_ref, 2, rows, gv_sum[rows, :])


def attend_back(sequence, qkv, grad, mixed, lse, tables, length, block, deps):
    width = qkv.shape[1] // 3
    pairs = width // LANES
    at = lambda off: pl.BlockSpec((length, LANES), lambda g: (sequence, off * pairs + g))
    out = pl.BlockSpec((length, LANES), lambda g: (0, g))
    table = pl.BlockSpec((length, LANES), lambda g: (0, 0))
    small = pl.BlockSpec((1, 8, length), lambda g: (sequence * pairs + g, 0, 0))
    return call(
        functools.partial(attend_back_kernel, block),
        "attend_back",
        [qkv, qkv, qkv, grad, mixed, lse, *tables],
        deps,
        grid=(pairs,),
        in_specs=[at(0), at(1), at(2), at(0), at(0), small, table, table, table],
        out_specs=[out] * 3 + [pl.BlockSpec((1, 8, LANES), lambda g: (g, 0, 0))],
        out_shape=[jax.ShapeDtypeStruct((length, width), BF16)] * 3
        + [jax.ShapeDtypeStruct((pairs, 8, LANES), F32)],
        scratch_shapes=[pltpu.VMEM((length, LANES), F32)] * 2,
    )


def by_sequence(tile, width, steps):
    return [
        pl.BlockSpec((tile, width), lambda i: (jnp.minimum(i, steps - 1), 0)),
        pl.BlockSpec((tile, width), lambda i: (jnp.maximum(i - steps, 0), 0)),
    ]


def other_first(tile, width, steps):
    return pl.BlockSpec((tile, width), lambda i: ((i + steps) % (2 * steps), 0))


def put_by_sequence(step, steps, value, other_ref, own_ref):
    @pl.when(step < steps)
    def _():
        other_ref[...] = value

    @pl.when(step >= steps)
    def _():
        own_ref[...] = value


def branch_kernel(count, steps, mixed_ref, act_ref, *rest):
    blocks, (other_ref, own_ref, held, sems) = rest[:count], rest[count:]
    step = pl.program_id(0)

    @pl.when(step == 0)
    def _():
        loads = block_copies(blocks, columns_at(held, blocks[0].shape[1]), sems)
        for copy in loads:
            copy.start()
        for copy in loads:
            copy.wait()

    x = jnp.concatenate([mixed_ref[...], act_ref[...]], axis=1)
    put_by_sequence(step, steps, dot(x, held[...], 1, 0).astype(BF16), other_ref, own_ref)


def branch_sums(mixed, act, blocks, tile, deps):
    length, count = mixed.shape[0] // 2, len(blocks)
    inner, model, steps = blocks[0].shape[0], count * blocks[0].shape[1], length // tile
    return call(
        functools.partial(branch_kernel, count, steps),
        "branch_sums",
        [mixed, act, *blocks],
        deps,
        grid=(2 * steps,),
        in_specs=[other_first(tile, a.shape[1], steps) for a in (mixed, act)] + [HBM] * count,
        out_specs=by_sequence(tile, model, steps),
        out_shape=[jax.ShapeDtypeStruct((length, model), BF16)] * 2,
        scratch_shapes=[pltpu.VMEM((inner, model), BF16), pltpu.SemaphoreType.DMA((count,))],
    )


def grad_in_kernel(setup, dy_ref, slope_ref, *rest):
    count, width, hidden = setup
    blocks = rest[:count]
    gmixed_ref, gpre_ref, gsum_ref, dsum_ref, held, sems = rest[-6:]

    @pl.when(pl.program_id(0) == 0)
    def _():
        loads = block_copies(blocks, columns_at(held, blocks[0].shape[1]), sems)
        for copy in loads:
            copy.start()
        gsum_ref[...] = jnp.zeros_like(gsum_ref)
        dsum_ref[...] = jnp.zeros_like(dsum_ref)
        for copy in loads:
            copy.wait()

    dy = dy_ref[...]
    gmixed_ref[...] = dot(dy, held[:width, :], 1, 1).astype(BF16)
    for start in range(0, hidden, width):
        part = slice(start, start + width)
        gact = dot(dy, held[width + start : 2 * width + start, :], 1, 1)
        gpre = (gact * slope_ref[:, part].astype(F32)).astype(BF16)
        gpre_ref[:, part] = gpre
        gsum_ref[0:1, part] += jnp.sum(gpre.astype(F32), axis=0, keepdims=True)
    dsum_ref[0:1, :] += jnp.sum(dy.astype(F32), axis=0, keepdims=True)


def grad_in(sequence, dy, slope, blocks, width, tile, earlier, deps):
    (length, model), hidden, count = dy.shape, slope.shape[1], len(blocks)
    steps = length // tile
    at = lambda w: pl.BlockSpec((tile, w), lambda i: (sequence * steps + i, 0))
    total = lambda w: pl.BlockSpec((8, w), lambda i: (0, 0))
    operands = [dy, slope, *blocks]
    return call(
        functools.partial(grad_in_kernel, (count, width, hidden)),
        "grad_in",
        operands + list(earlier),
        deps,
        grid=(steps,),
        in_specs=[pl.BlockSpec((tile, model), lambda i: (i, 0)), at(hidden)]
        + [HBM] * (count + len(earlier)),
        out_specs=[
            at(width),
            pl.BlockSpec((tile, hidden), lambda i: (i, 0)),
            total(hidden),
            total(model),
        ],
        out_shape=[
            jax.ShapeDtypeStruct((2 * length, width), BF16),
            jax.ShapeDtypeStruct((length, hidden), BF16),
            jax.ShapeDtypeStruct((8, hidden), F32),
            jax.ShapeDtypeStruct((8, model), F32),
        ],
        input_output_aliases={len(operands) + n: n for n in range(len(earlier))},
        scratch_shapes=[
            pltpu.VMEM((width + hidden, model), BF16),
            pltpu.SemaphoreType.DMA((count,)),
        ],
    )


def add_kernel(a_ref, b_ref, out_ref):
    out_ref[...] = (a_ref[...].astype(F32) + b_ref[...].astype(F32)).astype(BF16)


def add_rows(a, b):
    rows = pl.BlockSpec((a.shape[0] // 2, a.shape[1]), lambda i: (i, 0))
    return call(
        add_kernel,
        "add_rows",
        [a, b],
        grid=(2,),
        in_specs=[rows, rows],
        out_specs=rows,
        out_shape=jax.ShapeDtypeStruct(a.shape, BF16),
    )


def grad_normed_kernel(count, half, x_ref, *rest):
    grads, blocks, (out_ref, sum_ref, held, sems) = rest[:8], rest[8 : 8 + 2 * count], rest[-4:]
    (size, total), few, me = blocks[0].shape, count // 2, lax.axis_index("dp")

    @pl.when(pl.program_id(0) == 0)
    def _():
        for start in (True, False):
            for n, block in enumerate(blocks):
                core, j = n // count, n % count
                owner = lax.bitwise_xor(me, j ^ core) - half * few
                columns = slice(core * total, (core + 1) * total)

                @pl.when((owner >= 0) & (owner < few))
                def _(start=start, n=n, block=block, owner=owner, columns=columns):
                    target = held.at[span(owner, size), columns]
                    copy = pltpu.make_async_copy(block, target, sems.at[n])
                    if start:
                        copy.start()
                    else:
                        copy.wait()

        sum_ref[...] = jnp.zeros_like(sum_ref)

    columns = slice(half * few * size, (half + 1) * few * size)
    normal = normalized(x_ref[...])[:, columns]
    g = jnp.concatenate([ref[...] for ref in grads], axis=1)
    result = dot(g, held[...], 1, 1)
    sum_ref[0:1, :] += jnp.sum(result * normal, axis=0, keepdims=True)
    sum_ref[1:2, :] += jnp.sum(result, axis=0, keepdims=True)
    out_ref[...] = result.astype(BF16)


def grad_normed_sums(half, grads, x, blocks, tile, deps, adds=()):
    (length, model), count, total = x.shape, len(blocks) // 2, blocks[0].shape[1]
    part = model // 2
    rows = lambda w: pl.BlockSpec((tile, w), lambda i: (i, 0))
    return call(
        functools.partial(grad_normed_kernel, count, half),
        "grad_normed_sums",
        [x, *grads, *blocks],
        deps,
        adds=adds,
        grid=(length // tile,),
        in_specs=[rows(model)] + [rows(g.shape[1]) for g in grads] + [HBM] * (2 * count),
        out_specs=[rows(part), pl.BlockSpec((8, part), lambda i: (0, 0))],
        out_shape=[
            jax.ShapeDtypeStruct((length, part), BF16),
            jax.ShapeDtypeStruct((8, part), F32),
        ],
        scratch_shapes=[
            pltpu.VMEM((part, 2 * total), BF16),
            pltpu.SemaphoreType.DMA((2 * count,)),
        ],
    )


def weight_grad_kernel(writes, left, rows, many, groups, at_ref, *refs):
    cuts, (*refs, held, grad, sems) = refs[:many], refs[many:]
    whole, outs = refs[: len(refs) - len(writes)], refs[len(refs) - len(writes) :]
    step, core, loads, first = pl.program_id(0), lax.rem(lax.axis_index("dp"), 2), [], 0
    for group in groups:
        below = 0
        for ref in whole[:group]:
            columns = pl.ds(first, ref.shape[1])
            for start in range(0, ref.shape[0], rows):
                target = held.at[pl.ds(below + start, rows), columns]
                loads.append((ref.at[pl.ds(start, rows)], target))
            below += ref.shape[0]
        first += whole[0].shape[1]
        whole = whole[group:]
    loads = [pltpu.make_async_copy(*pair, sems.at[n]) for n, pair in enumerate(loads)]

    @pl.when(step == 0)
    def _():
        for copy in loads:
            copy.start()
        for copy in loads:
            copy.wait()

    cut = jnp.concatenate([ref[...] for ref in cuts], axis=0)
    pair = (cut, held[...]) if left else (held[...], cut)
    grad[...] = dot(*pair, 0, 0).astype(BF16)
    size = cut.shape[1] // 2
    for half, steps, out_ref in writes_of(writes, outs):
        here = functools.reduce(jnp.logical_or, [step == s for s in steps])

        @pl.when(here)
        def _(half=half, out_ref=out_ref):
            mine = span(core if half == 0 else 1 - core, size)
            out_ref[0] = grad[mine, :] if left else grad[:, mine]


def writes_of(writes, outs):
    return [(half, steps, out) for (half, steps), out in zip(writes, outs)]


def block_table(me, count):
    plan, chips = scatter_plan(count), count // 2
    order = [j // 2 for s in plan[0] for j in s]
    sets = [(half, s) for s in range(len(plan[0])) for half in range(2)]
    writes = [(half, [order.index(j // 2) for j in plan[half][s]]) for half, s in sets]
    table = []
    for _, steps in writes:
        for i in range(chips):
            later = [w for w in steps if w >= i]
            table.append(steps.index(min(later) if later else max(steps)))
    owners = lax.bitwise_xor(me // 2, jnp.array(order, jnp.int32))
    return sets, writes, jnp.concatenate([owners, jnp.array(table, jnp.int32)])


def weight_grads(at, xs, gs, count, deps, left, adds=()):
    plan, chips = scatter_plan(count), count // 2
    sets, writes, _ = block_table(0, count)
    cut, whole = (xs, gs) if left else (gs, xs)
    groups, length = [len(g) for g in whole], sum(a.shape[0] for a in whole[0])
    size, full = cut[0].shape[1] // count, sum(g[0].shape[1] for g in whole)
    shape, whole = (size, full) if left else (full, size), [a for g in whole for a in g]
    rows = length // 4
    pieces = 4 * len(groups)

    def out(n):
        return pl.BlockSpec((1, *shape), lambda i, at: (at[chips * (n + 1) + i], 0, 0))

    outs = call(
        functools.partial(weight_grad_kernel, writes, left, rows, len(cut), groups),
        "weight_grads",
        [*cut, *whole],
        deps,
        (at,),
        adds,
        grid=(chips,),
        in_specs=[pl.BlockSpec((a.shape[0], 2 * size), lambda i, at: (0, at[i])) for a in cut]
        + [HBM] * len(whole),
        out_specs=[out(n) for n in range(len(sets))],
        out_shape=[
            jax.ShapeDtypeStruct((len(plan[half][s]), *shape), BF16) for half, s in sets
        ],
        scratch_shapes=[
            pltpu.VMEM((length, full), BF16),
            pltpu.VMEM((2 * size, full) if left else (full, 2 * size), BF16),
            pltpu.SemaphoreType.DMA((pieces,)),
        ],
    )
    blocks = [[o for o, (half, _) in zip(outs, sets) if half == h] for h in range(2)]
    return (blocks, *outs[len(sets) :]) if adds else blocks


def finish_kernel(sizes, width, *refs):
    ins, (up_ref, qkv_ref, dense_ref, down_ref) = refs[:-4], refs[-4:]
    core = lax.rem(lax.axis_index("dp"), 2)
    pairs = []
    for size in sizes:
        mine = sum(ref[0].astype(F32) for ref in ins[: size - 1])
        pairs.append(((core, mine), (1 - core, ins[size - 1][0].astype(F32))))
        ins = ins[size:]
    for where, value in pairs[0]:
        up_ref[:, span(where, value.shape[1])] = value
    for where, value in pairs[1]:
        for c in range(3):
            qkv_ref[c, :, span(where, width)] = value[:, c * width : (c + 1) * width]
    for out_ref, pair in ((dense_ref, pairs[2]), (down_ref, pairs[3])):
        for where, value in pair:
            out_ref[where] = value


def finish(up, qkv, columns):
    (size, hidden), width = up[1].shape, qkv[1].shape[1] // 3
    steps = hidden // width
    operands, specs, sizes = [], [], []

    def take(parts, rows, base):
        addends, theirs = parts
        for array, first in [*addends, (theirs[None], 0)]:
            operands.append(array)
            specs.append(
                pl.BlockSpec(
                    (1, rows, array.shape[2]), lambda i, first=first: (first, base + i, 0)
                )
            )
        sizes.append(len(addends) + 1)

    take(up, size // steps, 0)
    take(qkv, size // steps, 0)
    take(columns, width // steps, 0)
    take(columns, width, 1)
    owned_up, owned_qkv, owned_dense, owned_down = call(
        lambda *refs: finish_kernel(sizes, width, *refs),
        "finish",
        operands,
        grid=(steps,),
        in_specs=specs,
        out_specs=[
            pl.BlockSpec((size // steps, 2 * hidden), lambda i: (i, 0)),
            pl.BlockSpec((3, size // steps, 2 * width), lambda i: (0, i, 0)),
            pl.BlockSpec((2, width // steps, size), lambda i: (0, i, 0)),
            pl.BlockSpec((2, width, size), lambda i: (0, i, 0)),
        ],
        out_shape=[
            jax.ShapeDtypeStruct((size, 2 * hidden), F32),
            jax.ShapeDtypeStruct((3, size, 2 * width), F32),
            jax.ShapeDtypeStruct((2, width, size), F32),
            jax.ShapeDtypeStruct((2, hidden, size), F32),
        ],
    )
    return (
        owned_up,
        owned_qkv,
        owned_dense.reshape(2 * width, size),
        owned_down.reshape(2 * hidden, size),
    )


def norm_back_kernel(tokens_ref, dy_ref, gain_ref, left_ref, right_ref, out_ref):
    x = tokens_ref[...].astype(F32)
    centered = x - jnp.mean(x, axis=1, keepdims=True)
    inverse_std = lax.rsqrt(jnp.mean(centered * centered, axis=1, keepdims=True) + EPS)
    normal = centered * inverse_std
    grad = jnp.concatenate([left_ref[...], right_ref[...]], axis=1).astype(F32)
    scaled = grad * gain_ref[...]
    first_mean = jnp.mean(scaled, axis=1, keepdims=True)
    second_mean = jnp.mean(scaled * normal, axis=1, keepdims=True)
    back = (scaled - first_mean - normal * second_mean) * inverse_std
    out_ref[...] = (dy_ref[...].astype(F32) + back).astype(BF16)


def norm_back(tokens, dy, gain, halves, deps):
    rows, model = tokens.shape
    tile = min(128, rows)
    part = lambda w: pl.BlockSpec((tile, w), lambda i: (i, 0))
    return call(
        norm_back_kernel,
        "norm_back",
        [tokens, dy, gain, *halves],
        deps,
        grid=(rows // tile,),
        in_specs=[part(model), part(model), pl.BlockSpec((1, model), lambda i: (0, 0))]
        + [part(model // 2)] * 2,
        out_specs=part(model),
        out_shape=jax.ShapeDtypeStruct((rows, model), BF16),
    )


def across(value, bit, count):
    return lax.ppermute(value, "dp", [(i, i ^ bit) for i in range(count)])


def added(addends):
    return sum(a.astype(F32) for a in addends).astype(BF16)


def pair_sum(parts):
    while len(parts) > 1:
        parts = [a + b for a, b in zip(parts[::2], parts[1::2])]
    return parts[0]


def chip_bits(count):
    bits, bit = [], 2
    while bit < count:
        bits.append(bit)
        bit *= 2
    return bits


class BlockGather:
    def __init__(self, own, sibling, count):
        self.held, self.count = {0: own, 1: sibling}, count
        self.orders = (chip_bits(count), chip_bits(count)[::-1])

    def own_to(self, s):
        if s < len(self.orders[0]):
            for half in range(2):
                bit = self.orders[half][s]
                self.held[half ^ bit] = across(self.held[half], bit, self.count)

    def rest(self):
        for s in range(1, len(self.orders[0])):
            for half in range(2):
                order = self.orders[half]
                for j in [j for j in self.held if j % 2 == half]:
                    if j ^ order[s] not in self.held and not any(j & b for b in order[s:]):
                        self.held[j ^ order[s]] = across(self.held[j], order[s], self.count)

    def fenced(self, others=(), deps=()):
        keys = sorted(self.held)
        values = fence([self.held[j] for j in keys] + list(others), deps)
        self.held = dict(zip(keys, values))
        return values[len(keys) :]

    def blocks(self):
        return [self.held[j] for j in range(self.count)]


def scatter_orders(count):
    return (chip_bits(count)[::-1], chip_bits(count))


def scatter_plan(count):
    plan = []
    for half, order in enumerate(scatter_orders(count)):
        sets, rest = [[half]], [half]
        for bit in reversed(order):
            sets.insert(0, [j ^ bit for j in rest])
            rest = sets[0] + rest
        plan.append(sets)
    return plan


class BlockScatter:
    def __init__(self, halves, count):
        self.count, self.orders, self.plan = count, scatter_orders(count), scatter_plan(count)
        self.held = [[[(a, 0)] for a in arrays] for arrays in halves]
        self.steps = len(self.orders[0])

    def parts(self, half, s):
        many = len(self.plan[half][s])
        return [a[first : first + many] for a, first in self.held[half][s]]

    def total(self, half, s):
        if len(self.held[half][s]) > 1:
            self.held[half][s] = [(added(self.parts(half, s)), 0)]
        return self.parts(half, s)[0]

    def ready(self, s):
        return [self.total(half, s) for half in range(2)]

    def adds(self, s):
        return [(len(self.plan[half][s]), self.held[half][s]) for half in range(2)]

    def settle(self, s, sums):
        for half in range(2):
            self.held[half][s] = [(sums[half], 0)]

    def send(self, s):
        return [across(self.total(h, s), self.orders[h][s], self.count) for h in range(2)]

    def arrive(self, s, came):
        for half in range(2):
            first = 0
            for t in range(s + 1, len(self.plan[half])):
                self.held[half][t].append((came[half], first))
                first += len(self.plan[half][t])

    def between(self):
        for s in range(1, self.steps - 1):
            self.arrive(s, self.send(s))

    def last(self):
        return self.total(1, -1)[0]

    def kept(self):
        return self.held[0][-1]


def on_device(
    tokens,
    norm_gain,
    norm_bias,
    qkv_weight,
    qkv_bias,
    dense_weight,
    dense_bias,
    up_weight,
    up_bias,
    down_weight,
    down_bias,
    cotangent,
    *,
    ndp,
    nmp,
):
    me = lax.axis_index("dp")
    core = me % 2
    length, model = tokens.shape[0] * nmp, tokens.shape[1]
    tile, block = min(256, length), min(512, length)
    width, hidden = qkv_weight.shape[2] // 2, up_weight.shape[1] // 2
    chip_steps = len(chip_bits(ndp))
    rank = lambda array, axis, which, size: lax.dynamic_slice_in_dim(
        array, which * size, size, axis
    )

    def row_pack(which):
        qkv = rank(qkv_weight, 2, which, width)
        return jnp.concatenate([qkv[0], qkv[1], qkv[2], rank(up_weight, 1, which, hidden)], axis=1)

    def column_pack(which):
        return jnp.concatenate(
            [rank(dense_weight, 0, which, width), rank(down_weight, 0, which, hidden)], axis=0
        )

    pairs = width // LANES
    swap = lambda array: across(array, 1, ndp)
    line_gather = lambda array: lax.all_gather(array, "mp", axis=0, tiled=True)
    line_scatter = lambda array: lax.psum_scatter(array, "mp", scatter_dimension=0, tiled=True)
    x_own, dy_own = line_gather(tokens), line_gather(cotangent)
    bias = jnp.concatenate(
        [
            rank(qkv_bias, 1, core, width).astype(F32).reshape(1, 3 * width),
            rank(up_bias[None, :], 1, core, hidden).astype(F32),
        ],
        axis=1,
    )
    gain, shift = norm_gain.astype(F32)[None, :], norm_bias.astype(F32)[None, :]
    rows = BlockGather(row_pack(core), swap(row_pack(1 - core)), ndp)
    columns = BlockGather(column_pack(core), swap(column_pack(1 - core)), ndp)
    rows.own_to(0)
    _, _, at = block_table(me, ndp)
    at, bias, gain, shift = rows.fenced([at, bias, gain, shift], columns.held.values())
    rows.own_to(1)
    rows.fenced()
    rows.rest()
    x_own, *held = fence([x_own, columns.held[0], columns.held[1]], rows.blocks())
    columns.held = dict(enumerate(held))

    tables = rotary_tables(length)
    x_other = swap(x_own)
    columns.own_to(0)
    common = (rows.blocks(), bias, gain, shift, tables, width, tile)
    first = project(0, x_own, *common, (), [columns.held[0]])
    (x_other,) = columns.fenced([x_other], [first[0]])
    columns.own_to(1)
    qkv, act, slope, normed = project(1, x_other, *common, first, [columns.held[0]])
    held = columns.fenced(rows.blocks(), [qkv])
    columns.rest()
    row_blocks, row_others = held, [swap(a) for a in held[:3]]
    mixed, lse = attend(qkv, length, block, [columns.held[0]])
    row_others = columns.fenced(row_others, [mixed])
    row_blocks[3:] = fence(row_blocks[3:], [row_others[0]])
    row_others += [swap(a) for a in row_blocks[3:]]
    other_sums, own_sums = branch_sums(mixed, act, columns.blocks(), tile, [row_blocks[3]])
    other_sums, dy_own, *row_others[3:] = fence([other_sums, dy_own, *row_others[3:]], [own_sums])
    theirs = swap(other_sums)
    dy_other = swap(dy_own)

    grads = (slope, columns.blocks(), width, tile)
    gmixed, gpre_own, *grad_a = grad_in(0, dy_own, *grads, (), [own_sums])
    theirs, dy_other = fence([theirs, dy_other], [grad_a[0]])
    total = add_rows(own_sums, theirs)
    branches = line_scatter(total)
    gmixed, gpre_other, *grad_b = grad_in(1, dy_other, *grads, [gmixed], [total])
    (gpre_sent,) = fence([gpre_other])
    gpre_came = swap(gpre_sent)
    column_grads = BlockScatter(
        weight_grads(at, [[mixed], [act]], [dy_own, dy_other], ndp, [gpre_sent], left=False), ndp
    )
    (gpre_came,) = fence([gpre_came], [column_grads.held[0][0][0][0]])
    column_came = column_grads.send(0)
    back = lambda sequence, deps: attend_back(
        sequence, qkv, gmixed, mixed, lse, tables, length, block, deps
    )
    *other, qkv_sums_b = back(1, [gpre_came])
    came = [swap(a) for a in other]
    *own, qkv_sums_a = back(0, [other[0]])
    came = fence([*came, *column_came], [own[0]])
    column_came, came = came[3:], came[:3]
    column_grads.arrive(0, column_came)
    column_grads.between()
    all_grads = [*own, gpre_own, *came, gpre_came]

    def normed_half(half, deps, adds=()):
        return grad_normed_sums(
            half, all_grads, x_own, [*row_blocks, *row_others], tile, deps, adds
        )

    total_a, sums_a, *settled = normed_half(0, [], column_grads.adds(chip_steps - 1))
    column_grads.settle(chip_steps - 1, settled)
    half_a = line_scatter(total_a)
    column_came = column_grads.send(chip_steps - 1)
    up_grads = BlockScatter(
        weight_grads(at, [normed], [[gpre_own, gpre_sent]], ndp, [sums_a], left=True), ndp
    )
    c0, c1, branches, u0, u1 = fence(
        [*column_came, branches, *(up_grads.held[h][0][0][0] for h in range(2))]
    )
    up_grads.held[0][0], up_grads.held[1][0] = [(u0, 0)], [(u1, 0)]
    up_came = up_grads.send(0)
    column_grads.arrive(chip_steps - 1, [c0, c1])
    blocks, column_last = weight_grads(
        at,
        [normed],
        [[a, b] for a, b in zip(own, other)],
        ndp,
        [c0],
        True,
        [column_grads.adds(len(column_grads.plan[1]) - 1)[1]],
    )
    qkv_grads = BlockScatter(blocks, ndp)
    qkv_came = qkv_grads.send(0)
    column_theirs = swap(column_last[0])
    total_b, sums_b = normed_half(1, [qkv_grads.held[0][0][0][0]])
    half_b = line_scatter(total_b)
    u0, u1, q0, q1, half_a = fence([*up_came, *qkv_came, half_a], [sums_b, column_theirs])
    up_grads.arrive(0, [u0, u1])
    qkv_grads.arrive(0, [q0, q1])
    up_grads.between()
    qkv_grads.between()
    up_came, qkv_came = up_grads.send(chip_steps - 1), qkv_grads.send(chip_steps - 1)
    u0, u1, q0, q1, branches, sums_b, column_theirs = fence(
        [*up_came, *qkv_came, branches, sums_b, column_theirs]
    )
    up_grads.arrive(chip_steps - 1, [u0, u1])
    qkv_grads.arrive(chip_steps - 1, [q0, q1])
    up_theirs = swap(up_grads.last())
    qkv_theirs = swap(qkv_grads.last())
    qkv_sum = (qkv_sums_a + qkv_sums_b)[:, :3, :].transpose(1, 0, 2).reshape(3 * width)
    norm_sums = jnp.concatenate([sums_a[:2], sums_b[:2]], axis=1)
    small = jnp.concatenate(
        [
            norm_sums.reshape(2 * model),
            qkv_sum,
            grad_a[0][0] + grad_b[0][0],
            grad_a[1][0] + grad_b[1][0],
        ]
    )
    small = pair_sum([small] + [across(small, j, ndp) for j in range(2, ndp, 2)])
    small_other = swap(small)
    owned_up, owned_qkv, owned_dense, owned_down = finish(
        (up_grads.kept(), up_theirs),
        (qkv_grads.kept(), qkv_theirs),
        (column_grads.kept(), column_theirs),
    )
    grad_tokens = norm_back(tokens, cotangent, gain, [half_a, half_b], [small_other, owned_up])
    (norm_sums,) = fence([small[: 2 * model] + small_other[: 2 * model]], [owned_up])
    norm_sums = [norm_sums] + fence(
        [
            lax.ppermute(norm_sums, "mp", [(i, i ^ j) for i in range(nmp)])
            for j in range(1, nmp)
        ],
        [grad_tokens],
    )
    while len(norm_sums) > 1:
        norm_sums = [a + b for a, b in zip(norm_sums[::2], norm_sums[1::2])]
    norm_sums = norm_sums[0]

    output = (
        tokens.astype(F32)
        + branches.astype(F32)
        + (dense_bias.astype(F32) + down_bias.astype(F32))[None, :]
    ).astype(BF16)

    inner = 3 * width + hidden
    grad_out_bias = small[2 * model + inner :]
    here, there = (a[2 * model : 2 * model + inner] for a in (small, small_other))
    even, odd = jnp.where(core == 0, here, there), jnp.where(core == 0, there, here)
    grad_qkv_bias = jnp.concatenate(
        [a[: 3 * width].reshape(3, width) for a in (even, odd)], axis=1
    )
    grad_up_bias = jnp.concatenate([even[3 * width :], odd[3 * width :]])

    return (
        output,
        grad_tokens,
        norm_sums[:model],
        norm_sums[model:],
        owned_qkv,
        grad_qkv_bias,
        owned_dense,
        grad_out_bias,
        owned_up,
        grad_up_bias,
        owned_down,
        grad_out_bias,
    )


def solution(mesh):
    return jax.shard_map(
        functools.partial(on_device, ndp=mesh.shape["dp"], nmp=mesh.shape["mp"]),
        mesh=mesh,
        in_specs=(
            P(("dp", "mp"), None),
            P(),
            P(),
            P(None, "dp", "mp"),
            P(None, "mp"),
            P("mp", "dp"),
            P(),
            P("dp", "mp"),
            P("mp"),
            P("mp", "dp"),
            P(),
            P(("dp", "mp"), None),
        ),
        out_specs=(
            P(("dp", "mp"), None),
            P(("dp", "mp"), None),
            P(),
            P(),
            P(None, "dp", "mp"),
            P(None, "mp"),
            P("mp", "dp"),
            P(),
            P("dp", "mp"),
            P("mp"),
            P("mp", "dp"),
            P(),
        ),
        check_vma=False,
    )
```

```python
import functools

import jax
import jax.numpy as jnp
import numpy as np
from jax import lax
from jax.experimental import pallas as pl
from jax.experimental.pallas import tpu as pltpu
from jax.sharding import PartitionSpec as P

HEAD_DIM = 64
ROT = 32
EPS = 1e-05
LANES = 128
F32 = jnp.float32
BF16 = jnp.bfloat16
HBM = pl.BlockSpec(memory_space=pltpu.HBM)


def dot(lhs, rhs, lhs_dim, rhs_dim):
    return lax.dot_general(
        lhs, rhs, (((lhs_dim,), (rhs_dim,)), ((), ())), preferred_element_type=F32
    )


def call(kernel, name, operands, deps=(), scalars=(), adds=(), vmem=64, **spec):
    deps, out_shape = tuple(deps), spec.pop("out_shape")
    single = not isinstance(out_shape, list)
    out_shape = [out_shape] if single else out_shape
    out_specs = spec.pop("out_specs")
    out_specs = [out_specs] if single else list(out_specs)
    extra, extra_specs, sizes = [], [], []
    steps = spec["grid"][0] if adds else 1
    for many, addends in adds:
        _, rows, columns = addends[0][0].shape
        block = (many, rows // steps, columns)
        for array, first in addends:
            extra.append(array)
            extra_specs.append(
                pl.BlockSpec(block, lambda i, *at, first=first, many=many: (first // many, i, 0))
            )
        out_shape = out_shape + [jax.ShapeDtypeStruct((many, rows, columns), BF16)]
        out_specs = out_specs + [pl.BlockSpec(block, lambda i, *at: (0, i, 0))]
        sizes.append(len(addends))
    lead, outs = len(scalars) + len(operands), len(out_shape) - len(adds)

    def body(*refs):
        first = lead + len(extra) + len(deps)
        kernel(*refs[:lead], *refs[first : first + outs], *refs[first + outs + len(adds) :])
        sources = refs[lead : lead + len(extra)]
        for n, out in zip(sizes, refs[first + outs : first + outs + len(adds)]):
            out[...] = sum(ref[...].astype(F32) for ref in sources[:n]).astype(BF16)
            sources = sources[n:]

    in_specs = list(spec.pop("in_specs")) + extra_specs + [HBM] * len(deps)
    aliases = spec.pop("input_output_aliases", {})
    if scalars:
        grid_spec = pltpu.PrefetchScalarGridSpec(
            num_scalar_prefetch=len(scalars), in_specs=in_specs, out_specs=out_specs, **spec
        )
        spec = {"grid_spec": grid_spec}
    else:
        spec.update(in_specs=in_specs, out_specs=out_specs)
    results = pl.pallas_call(
        body,
        out_shape=out_shape,
        input_output_aliases=aliases,
        compiler_params=pltpu.CompilerParams(vmem_limit_bytes=vmem << 20),
        cost_estimate=pl.CostEstimate(flops=0, transcendentals=0, bytes_accessed=0),
        name=name,
        **spec,
    )(*scalars, *operands, *extra, *deps)
    return results[0] if single and not adds else results


def fence(values, deps=()):
    return list(
        call(
            lambda *refs: None,
            "fence",
            values,
            deps,
            in_specs=[HBM] * len(values),
            out_specs=[HBM] * len(values),
            out_shape=[jax.ShapeDtypeStruct(v.shape, v.dtype) for v in values],
            input_output_aliases={n: n for n in range(len(values))},
        )
    )


def rotary_tables(length):
    positions = np.arange(length, dtype=np.float32)
    frequency = 10000.0 ** (-np.arange(ROT // 2, dtype=np.float64) * 2.0 / ROT)
    angles = positions[:, None] * frequency.astype(np.float32)[None, :]
    cosine, sine = np.cos(angles.astype(np.float64)), np.sin(angles.astype(np.float64))
    rest = HEAD_DIM - ROT
    none = np.zeros((length, ROT // 2))
    ones, zeros = np.ones((length, rest)), np.zeros((length, rest))
    straight = np.concatenate([cosine, cosine, ones], axis=1)
    left = np.concatenate([-sine, none, zeros], axis=1)
    right = np.concatenate([none, sine, zeros], axis=1)
    return [
        jnp.asarray(np.concatenate([t, t], axis=1).astype(np.float32))
        for t in (straight, left, right)
    ]


def rotated(u, straight, left, right, sign):
    half = ROT // 2
    turned = pltpu.roll(u, LANES - half, 1) * left + pltpu.roll(u, half, 1) * right
    return u * straight + sign * turned


def normalized(x):
    x = x.astype(F32)
    centered = x - jnp.mean(x, axis=1, keepdims=True)
    variance = jnp.mean(centered * centered, axis=1, keepdims=True)
    return centered * lax.rsqrt(variance + EPS)


def block_copies(blocks, place, sems):
    me = lax.axis_index("dp")
    return [
        pltpu.make_async_copy(block, place(lax.bitwise_xor(me, j)), sems.at[j])
        for j, block in enumerate(blocks)
    ]


def span(owner, size):
    return pl.ds(pl.multiple_of(owner * size, size), size)


def rows_at(ref, size):
    return lambda owner: ref.at[pl.ds(pl.multiple_of(owner * size, size), size)]


def columns_at(ref, size):
    return lambda owner: ref.at[:, pl.ds(pl.multiple_of(owner * size, size), size)]


def project_kernel(setup, x_ref, bias_ref, gain_ref, shift_ref, cos_ref, left_ref, right_ref, *rest):
    count, width, hidden = setup
    blocks = rest[:count]
    qkv_ref, act_ref, slope_ref, normed_ref, held, sems = rest[-6:]

    @pl.when(pl.program_id(0) == 0)
    def _():
        loads = block_copies(blocks, rows_at(held, blocks[0].shape[0]), sems)
        for copy in loads:
            copy.start()
        for copy in loads:
            copy.wait()

    x = (normalized(x_ref[...]) * gain_ref[...] + shift_ref[...]).astype(BF16)
    normed_ref[...] = x
    root = 0.7978845608028654
    for t in range((3 * width + hidden) // width):
        columns = slice(t * width, (t + 1) * width)
        y = dot(x, held[:, columns], 1, 0) + bias_ref[:, columns]
        if t < 3:
            for g in range(width // LANES):
                part = y[:, g * LANES : (g + 1) * LANES]
                if t < 2:
                    part = rotated(part, cos_ref[...], left_ref[...], right_ref[...], 1.0)
                if t == 0:
                    part = part * HEAD_DIM**-0.5
                start = t * width + g * LANES
                qkv_ref[:, start : start + LANES] = part.astype(BF16)
        else:
            columns = slice((t - 3) * width, (t - 2) * width)
            square = y * y
            turn = jnp.tanh(root * y * (1.0 + 0.044715 * square))
            half = 0.5 * (1.0 + turn)
            act_ref[:, columns] = (y * half).astype(BF16)
            slope = half * (1.0 + y * (1.0 - turn) * (root + (3.0 * 0.044715 * root) * square))
            slope_ref[:, columns] = slope.astype(BF16)


def project(sequence, x, blocks, bias, gain, shift, tables, width, tile, earlier, deps):
    (length, model), total, count = x.shape, blocks[0].shape[1], len(blocks)
    hidden, steps = total - 3 * width, length // tile
    rows = lambda w: pl.BlockSpec((tile, w), lambda i: (i, 0))
    out = lambda w: pl.BlockSpec((tile, w), lambda i: (sequence * steps + i, 0))
    line = lambda a: pl.BlockSpec(a.shape, lambda i: (0, 0))
    widths = (3 * width, hidden, hidden, model)
    operands = [x, bias, gain, shift, *tables, *blocks]
    return call(
        functools.partial(project_kernel, (count, width, hidden)),
        "project",
        operands + list(earlier),
        deps,
        grid=(steps,),
        in_specs=[rows(model), line(bias), line(gain), line(shift)]
        + [rows(LANES)] * 3
        + [HBM] * (count + len(earlier)),
        out_specs=[out(w) for w in widths],
        out_shape=[jax.ShapeDtypeStruct((2 * length, w), BF16) for w in widths],
        input_output_aliases={len(operands) + n: n for n in range(len(earlier))},
        scratch_shapes=[pltpu.VMEM((model, total), BF16), pltpu.SemaphoreType.DMA((count,))],
    )


def attend_kernel(block, q_ref, k_ref, v_ref, out_ref, lse_ref):
    length = q_ref.shape[0]
    lane = lax.broadcasted_iota(jnp.int32, (1, LANES), 1)
    key = lax.broadcasted_iota(jnp.int32, (block, block), 0)
    causal = key <= lax.broadcasted_iota(jnp.int32, (block, block), 1)
    for i in range(length // block):
        rows, before = pl.ds(i * block, block), pl.ds(0, i * block)
        results = []
        for h in range(2):
            mine = (lane < HEAD_DIM) if h == 0 else (lane >= HEAD_DIM)
            query = jnp.where(mine, q_ref[rows, :], 0)
            near = jnp.where(causal, dot(k_ref[rows, :], query, 1, 1), -1e30)
            highest = jnp.max(near, axis=0, keepdims=True)
            if i:
                far = dot(k_ref[before, :], query, 1, 1)
                highest = jnp.maximum(highest, jnp.max(far, axis=0, keepdims=True))
            near = jnp.exp(near - highest)
            total = jnp.sum(near, axis=0, keepdims=True)
            if i:
                far = jnp.exp(far - highest)
                total = total + jnp.sum(far, axis=0, keepdims=True)
            inverse = 1.0 / total
            result = dot((near * inverse).astype(BF16), v_ref[rows, :], 0, 0)
            if i:
                result = result + dot((far * inverse).astype(BF16), v_ref[before, :], 0, 0)
            results.append(result)
            lse_ref[0, h : h + 1, rows] = highest + jnp.log(total)
        out_ref[rows, :] = jnp.where(lane < HEAD_DIM, results[0], results[1]).astype(BF16)


def pair_specs(length, pairs):
    return lambda off: pl.BlockSpec(
        (length, LANES), lambda g: (g // pairs, off * pairs + g % pairs)
    )


def attend(qkv, length, block, deps):
    width, sequences = qkv.shape[1] // 3, qkv.shape[0] // length
    pairs = width // LANES
    at = pair_specs(length, pairs)
    return call(
        functools.partial(attend_kernel, block),
        "attend",
        [qkv, qkv, qkv],
        deps,
        grid=(sequences * pairs,),
        in_specs=[at(0), at(1), at(2)],
        out_specs=[at(0), pl.BlockSpec((1, 8, length), lambda g: (g, 0, 0))],
        out_shape=[
            jax.ShapeDtypeStruct((qkv.shape[0], width), BF16),
            jax.ShapeDtypeStruct((sequences * pairs, 8, length), F32),
        ],
    )


def attend_back_kernel(
    block,
    q_ref,
    k_ref,
    v_ref,
    grad_ref,
    mixed_ref,
    lse_ref,
    cos_ref,
    left_ref,
    right_ref,
    gq_ref,
    gk_ref,
    gv_ref,
    sum_ref,
    gk_sum,
    gv_sum,
):
    length = q_ref.shape[0]
    lane = lax.broadcasted_iota(jnp.int32, (1, LANES), 1)
    key = lax.broadcasted_iota(jnp.int32, (block, block), 0)
    causal = key <= lax.broadcasted_iota(jnp.int32, (block, block), 1)
    count = length // block
    sum_ref[...] = jnp.zeros_like(sum_ref)

    def put(ref, which, rows, value):
        value = value.astype(BF16)
        ref[rows, :] = value
        sum_ref[0, which : which + 1, :] += jnp.sum(value.astype(F32), axis=0, keepdims=True)

    def unrotated(value, rows):
        return rotated(value, cos_ref[rows, :], left_ref[rows, :], right_ref[rows, :], -1.0)

    for i in reversed(range(count)):
        rows = pl.ds(i * block, block)
        product = grad_ref[rows, :].astype(F32) * mixed_ref[rows, :].astype(F32)
        gq = None
        for h in range(2):
            mine = (lane < HEAD_DIM) if h == 0 else (lane >= HEAD_DIM)
            query = jnp.where(mine, q_ref[rows, :], 0)
            grad = jnp.where(mine, grad_ref[rows, :], 0)
            ones = jnp.where(mine, jnp.ones((8, LANES), F32), 0.0)
            delta = lax.dot_general(
                ones,
                product,
                (((1,), (1,)), ((), ())),
                precision=lax.Precision.HIGHEST,
                preferred_element_type=F32,
            )[0:1, :]
            lse = lse_ref[0, h : h + 1, rows]
            for j in range(i + 1):
                keys = pl.ds(j * block, block)
                key_rows = k_ref[keys, :]
                probs = jnp.exp(dot(key_rows, query, 1, 1) - lse)
                if j == i:
                    probs = jnp.where(causal, probs, 0.0)
                gprobs = dot(v_ref[keys, :], grad, 1, 1)
                gscores = (probs * (gprobs - delta)).astype(BF16)
                gv, gk = dot(probs.astype(BF16), grad, 1, 0), dot(gscores, query, 1, 0)
                if i == count - 1 and h == 0:
                    gv_sum[keys, :] = gv
                    gk_sum[keys, :] = gk
                else:
                    gv_sum[keys, :] += gv
                    gk_sum[keys, :] += gk
                part = dot(gscores, jnp.where(mine, key_rows, 0), 0, 0)
                gq = part if gq is None else gq + part
        put(gq_ref, 0, rows, unrotated(gq * HEAD_DIM**-0.5, rows))
    for i in range(count):
        rows = pl.ds(i * block, block)
        put(gk_ref, 1, rows, unrotated(gk_sum[rows, :], rows))
        put(gv_ref, 2, rows, gv_sum[rows, :])


def attend_back(sequence, qkv, grad, mixed, lse, tables, length, block, deps):
    width = qkv.shape[1] // 3
    pairs = width // LANES
    at = lambda off: pl.BlockSpec((length, LANES), lambda g: (sequence, off * pairs + g))
    out = pl.BlockSpec((length, LANES), lambda g: (0, g))
    table = pl.BlockSpec((length, LANES), lambda g: (0, 0))
    small = pl.BlockSpec((1, 8, length), lambda g: (sequence * pairs + g, 0, 0))
    return call(
        functools.partial(attend_back_kernel, block),
        "attend_back",
        [qkv, qkv, qkv, grad, mixed, lse, *tables],
        deps,
        grid=(pairs,),
        in_specs=[at(0), at(1), at(2), at(0), at(0), small, table, table, table],
        out_specs=[out] * 3 + [pl.BlockSpec((1, 8, LANES), lambda g: (g, 0, 0))],
        out_shape=[jax.ShapeDtypeStruct((length, width), BF16)] * 3
        + [jax.ShapeDtypeStruct((pairs, 8, LANES), F32)],
        scratch_shapes=[pltpu.VMEM((length, LANES), F32)] * 2,
    )


def by_sequence(tile, width, steps):
    return [
        pl.BlockSpec((tile, width), lambda i: (jnp.minimum(i, steps - 1), 0)),
        pl.BlockSpec((tile, width), lambda i: (jnp.maximum(i - steps, 0), 0)),
    ]


def other_first(tile, width, steps):
    return pl.BlockSpec((tile, width), lambda i: ((i + steps) % (2 * steps), 0))


def put_by_sequence(step, steps, value, other_ref, own_ref):
    @pl.when(step < steps)
    def _():
        other_ref[...] = value

    @pl.when(step >= steps)
    def _():
        own_ref[...] = value


def branch_kernel(count, steps, mixed_ref, act_ref, *rest):
    blocks, (other_ref, own_ref, held, sems) = rest[:count], rest[count:]
    step = pl.program_id(0)

    @pl.when(step == 0)
    def _():
        loads = block_copies(blocks, columns_at(held, blocks[0].shape[1]), sems)
        for copy in loads:
            copy.start()
        for copy in loads:
            copy.wait()

    x = jnp.concatenate([mixed_ref[...], act_ref[...]], axis=1)
    put_by_sequence(step, steps, dot(x, held[...], 1, 0).astype(BF16), other_ref, own_ref)


def branch_sums(mixed, act, blocks, tile, deps):
    length, count = mixed.shape[0] // 2, len(blocks)
    inner, model, steps = blocks[0].shape[0], count * blocks[0].shape[1], length // tile
    return call(
        functools.partial(branch_kernel, count, steps),
        "branch_sums",
        [mixed, act, *blocks],
        deps,
        grid=(2 * steps,),
        in_specs=[other_first(tile, a.shape[1], steps) for a in (mixed, act)] + [HBM] * count,
        out_specs=by_sequence(tile, model, steps),
        out_shape=[jax.ShapeDtypeStruct((length, model), BF16)] * 2,
        scratch_shapes=[pltpu.VMEM((inner, model), BF16), pltpu.SemaphoreType.DMA((count,))],
    )


def grad_in_kernel(setup, dy_ref, slope_ref, *rest):
    count, width, hidden = setup
    blocks = rest[:count]
    gmixed_ref, gpre_ref, gsum_ref, dsum_ref, held, sems = rest[-6:]

    @pl.when(pl.program_id(0) == 0)
    def _():
        loads = block_copies(blocks, columns_at(held, blocks[0].shape[1]), sems)
        for copy in loads:
            copy.start()
        gsum_ref[...] = jnp.zeros_like(gsum_ref)
        dsum_ref[...] = jnp.zeros_like(dsum_ref)
        for copy in loads:
            copy.wait()

    dy = dy_ref[...]
    gmixed_ref[...] = dot(dy, held[:width, :], 1, 1).astype(BF16)
    for start in range(0, hidden, width):
        part = slice(start, start + width)
        gact = dot(dy, held[width + start : 2 * width + start, :], 1, 1)
        gpre = (gact * slope_ref[:, part].astype(F32)).astype(BF16)
        gpre_ref[:, part] = gpre
        gsum_ref[0:1, part] += jnp.sum(gpre.astype(F32), axis=0, keepdims=True)
    dsum_ref[0:1, :] += jnp.sum(dy.astype(F32), axis=0, keepdims=True)


def grad_in(sequence, dy, slope, blocks, width, tile, earlier, deps):
    (length, model), hidden, count = dy.shape, slope.shape[1], len(blocks)
    steps = length // tile
    at = lambda w: pl.BlockSpec((tile, w), lambda i: (sequence * steps + i, 0))
    total = lambda w: pl.BlockSpec((8, w), lambda i: (0, 0))
    operands = [dy, slope, *blocks]
    return call(
        functools.partial(grad_in_kernel, (count, width, hidden)),
        "grad_in",
        operands + list(earlier),
        deps,
        grid=(steps,),
        in_specs=[pl.BlockSpec((tile, model), lambda i: (i, 0)), at(hidden)]
        + [HBM] * (count + len(earlier)),
        out_specs=[
            at(width),
            pl.BlockSpec((tile, hidden), lambda i: (i, 0)),
            total(hidden),
            total(model),
        ],
        out_shape=[
            jax.ShapeDtypeStruct((2 * length, width), BF16),
            jax.ShapeDtypeStruct((length, hidden), BF16),
            jax.ShapeDtypeStruct((8, hidden), F32),
            jax.ShapeDtypeStruct((8, model), F32),
        ],
        input_output_aliases={len(operands) + n: n for n in range(len(earlier))},
        scratch_shapes=[
            pltpu.VMEM((width + hidden, model), BF16),
            pltpu.SemaphoreType.DMA((count,)),
        ],
    )


def add_kernel(a_ref, b_ref, out_ref):
    out_ref[...] = (a_ref[...].astype(F32) + b_ref[...].astype(F32)).astype(BF16)


def add_rows(a, b):
    rows = pl.BlockSpec((a.shape[0] // 2, a.shape[1]), lambda i: (i, 0))
    return call(
        add_kernel,
        "add_rows",
        [a, b],
        grid=(2,),
        in_specs=[rows, rows],
        out_specs=rows,
        out_shape=jax.ShapeDtypeStruct(a.shape, BF16),
    )


def grad_normed_kernel(count, half, x_ref, *rest):
    grads, blocks, (out_ref, sum_ref, held, sems) = rest[:8], rest[8 : 8 + 2 * count], rest[-4:]
    (size, total), few, me = blocks[0].shape, count // 2, lax.axis_index("dp")

    @pl.when(pl.program_id(0) == 0)
    def _():
        for start in (True, False):
            for n, block in enumerate(blocks):
                core, j = n // count, n % count
                owner = lax.bitwise_xor(me, j ^ core) - half * few
                columns = slice(core * total, (core + 1) * total)

                @pl.when((owner >= 0) & (owner < few))
                def _(start=start, n=n, block=block, owner=owner, columns=columns):
                    target = held.at[span(owner, size), columns]
                    copy = pltpu.make_async_copy(block, target, sems.at[n])
                    if start:
                        copy.start()
                    else:
                        copy.wait()

        sum_ref[...] = jnp.zeros_like(sum_ref)

    columns = slice(half * few * size, (half + 1) * few * size)
    normal = normalized(x_ref[...])[:, columns]
    g = jnp.concatenate([ref[...] for ref in grads], axis=1)
    result = dot(g, held[...], 1, 1)
    sum_ref[0:1, :] += jnp.sum(result * normal, axis=0, keepdims=True)
    sum_ref[1:2, :] += jnp.sum(result, axis=0, keepdims=True)
    out_ref[...] = result.astype(BF16)


def grad_normed_sums(half, grads, x, blocks, tile, deps, adds=()):
    (length, model), count, total = x.shape, len(blocks) // 2, blocks[0].shape[1]
    part = model // 2
    rows = lambda w: pl.BlockSpec((tile, w), lambda i: (i, 0))
    return call(
        functools.partial(grad_normed_kernel, count, half),
        "grad_normed_sums",
        [x, *grads, *blocks],
        deps,
        adds=adds,
        grid=(length // tile,),
        in_specs=[rows(model)] + [rows(g.shape[1]) for g in grads] + [HBM] * (2 * count),
        out_specs=[rows(part), pl.BlockSpec((8, part), lambda i: (0, 0))],
        out_shape=[
            jax.ShapeDtypeStruct((length, part), BF16),
            jax.ShapeDtypeStruct((8, part), F32),
        ],
        scratch_shapes=[
            pltpu.VMEM((part, 2 * total), BF16),
            pltpu.SemaphoreType.DMA((2 * count,)),
        ],
    )


def weight_grad_kernel(writes, left, rows, many, groups, at_ref, *refs):
    cuts, (*refs, held, grad, sems) = refs[:many], refs[many:]
    whole, outs = refs[: len(refs) - len(writes)], refs[len(refs) - len(writes) :]
    step, core, loads, first = pl.program_id(0), lax.rem(lax.axis_index("dp"), 2), [], 0
    for group in groups:
        below = 0
        for ref in whole[:group]:
            columns = pl.ds(first, ref.shape[1])
            for start in range(0, ref.shape[0], rows):
                target = held.at[pl.ds(below + start, rows), columns]
                loads.append((ref.at[pl.ds(start, rows)], target))
            below += ref.shape[0]
        first += whole[0].shape[1]
        whole = whole[group:]
    loads = [pltpu.make_async_copy(*pair, sems.at[n]) for n, pair in enumerate(loads)]

    @pl.when(step == 0)
    def _():
        for copy in loads:
            copy.start()
        for copy in loads:
            copy.wait()

    cut = jnp.concatenate([ref[...] for ref in cuts], axis=0)
    pair = (cut, held[...]) if left else (held[...], cut)
    grad[...] = dot(*pair, 0, 0).astype(BF16)
    size = cut.shape[1] // 2
    for half, steps, out_ref in writes_of(writes, outs):
        here = functools.reduce(jnp.logical_or, [step == s for s in steps])

        @pl.when(here)
        def _(half=half, out_ref=out_ref):
            mine = span(core if half == 0 else 1 - core, size)
            out_ref[0] = grad[mine, :] if left else grad[:, mine]


def writes_of(writes, outs):
    return [(half, steps, out) for (half, steps), out in zip(writes, outs)]


def block_table(me, count):
    plan, chips = scatter_plan(count), count // 2
    order = [j // 2 for s in plan[0] for j in s]
    sets = [(half, s) for s in range(len(plan[0])) for half in range(2)]
    writes = [(half, [order.index(j // 2) for j in plan[half][s]]) for half, s in sets]
    table = []
    for _, steps in writes:
        for i in range(chips):
            later = [w for w in steps if w >= i]
            table.append(steps.index(min(later) if later else max(steps)))
    owners = lax.bitwise_xor(me // 2, jnp.array(order, jnp.int32))
    return sets, writes, jnp.concatenate([owners, jnp.array(table, jnp.int32)])


def weight_grads(at, xs, gs, count, deps, left, adds=()):
    plan, chips = scatter_plan(count), count // 2
    sets, writes, _ = block_table(0, count)
    cut, whole = (xs, gs) if left else (gs, xs)
    groups, length = [len(g) for g in whole], sum(a.shape[0] for a in whole[0])
    size, full = cut[0].shape[1] // count, sum(g[0].shape[1] for g in whole)
    shape, whole = (size, full) if left else (full, size), [a for g in whole for a in g]
    rows = length // 4
    pieces = 4 * len(groups)

    def out(n):
        return pl.BlockSpec((1, *shape), lambda i, at: (at[chips * (n + 1) + i], 0, 0))

    outs = call(
        functools.partial(weight_grad_kernel, writes, left, rows, len(cut), groups),
        "weight_grads",
        [*cut, *whole],
        deps,
        (at,),
        adds,
        grid=(chips,),
        in_specs=[pl.BlockSpec((a.shape[0], 2 * size), lambda i, at: (0, at[i])) for a in cut]
        + [HBM] * len(whole),
        out_specs=[out(n) for n in range(len(sets))],
        out_shape=[
            jax.ShapeDtypeStruct((len(plan[half][s]), *shape), BF16) for half, s in sets
        ],
        scratch_shapes=[
            pltpu.VMEM((length, full), BF16),
            pltpu.VMEM((2 * size, full) if left else (full, 2 * size), BF16),
            pltpu.SemaphoreType.DMA((pieces,)),
        ],
    )
    blocks = [[o for o, (half, _) in zip(outs, sets) if half == h] for h in range(2)]
    return (blocks, *outs[len(sets) :]) if adds else blocks


def finish_kernel(sizes, width, *refs):
    ins, (up_ref, qkv_ref, dense_ref, down_ref) = refs[:-4], refs[-4:]
    core = lax.rem(lax.axis_index("dp"), 2)
    pairs = []
    for size in sizes:
        mine = sum(ref[0].astype(F32) for ref in ins[: size - 1])
        pairs.append(((core, mine), (1 - core, ins[size - 1][0].astype(F32))))
        ins = ins[size:]
    for where, value in pairs[0]:
        up_ref[:, span(where, value.shape[1])] = value
    for where, value in pairs[1]:
        for c in range(3):
            qkv_ref[c, :, span(where, width)] = value[:, c * width : (c + 1) * width]
    for out_ref, pair in ((dense_ref, pairs[2]), (down_ref, pairs[3])):
        for where, value in pair:
            out_ref[where] = value


def finish(up, qkv, columns):
    (size, hidden), width = up[1].shape, qkv[1].shape[1] // 3
    steps = hidden // width
    operands, specs, sizes = [], [], []

    def take(parts, rows, base):
        addends, theirs = parts
        for array, first in [*addends, (theirs[None], 0)]:
            operands.append(array)
            specs.append(
                pl.BlockSpec(
                    (1, rows, array.shape[2]), lambda i, first=first: (first, base + i, 0)
                )
            )
        sizes.append(len(addends) + 1)

    take(up, size // steps, 0)
    take(qkv, size // steps, 0)
    take(columns, width // steps, 0)
    take(columns, width, 1)
    owned_up, owned_qkv, owned_dense, owned_down = call(
        lambda *refs: finish_kernel(sizes, width, *refs),
        "finish",
        operands,
        grid=(steps,),
        in_specs=specs,
        out_specs=[
            pl.BlockSpec((size // steps, 2 * hidden), lambda i: (i, 0)),
            pl.BlockSpec((3, size // steps, 2 * width), lambda i: (0, i, 0)),
            pl.BlockSpec((2, width // steps, size), lambda i: (0, i, 0)),
            pl.BlockSpec((2, width, size), lambda i: (0, i, 0)),
        ],
        out_shape=[
            jax.ShapeDtypeStruct((size, 2 * hidden), F32),
            jax.ShapeDtypeStruct((3, size, 2 * width), F32),
            jax.ShapeDtypeStruct((2, width, size), F32),
            jax.ShapeDtypeStruct((2, hidden, size), F32),
        ],
    )
    return (
        owned_up,
        owned_qkv,
        owned_dense.reshape(2 * width, size),
        owned_down.reshape(2 * hidden, size),
    )


def norm_back_kernel(tokens_ref, dy_ref, gain_ref, left_ref, right_ref, out_ref):
    x = tokens_ref[...].astype(F32)
    centered = x - jnp.mean(x, axis=1, keepdims=True)
    inverse_std = lax.rsqrt(jnp.mean(centered * centered, axis=1, keepdims=True) + EPS)
    normal = centered * inverse_std
    grad = jnp.concatenate([left_ref[...], right_ref[...]], axis=1).astype(F32)
    scaled = grad * gain_ref[...]
    first_mean = jnp.mean(scaled, axis=1, keepdims=True)
    second_mean = jnp.mean(scaled * normal, axis=1, keepdims=True)
    back = (scaled - first_mean - normal * second_mean) * inverse_std
    out_ref[...] = (dy_ref[...].astype(F32) + back).astype(BF16)


def norm_back(tokens, dy, gain, halves, deps):
    rows, model = tokens.shape
    tile = min(128, rows)
    part = lambda w: pl.BlockSpec((tile, w), lambda i: (i, 0))
    return call(
        norm_back_kernel,
        "norm_back",
        [tokens, dy, gain, *halves],
        deps,
        grid=(rows // tile,),
        in_specs=[part(model), part(model), pl.BlockSpec((1, model), lambda i: (0, 0))]
        + [part(model // 2)] * 2,
        out_specs=part(model),
        out_shape=jax.ShapeDtypeStruct((rows, model), BF16),
    )


def across(value, bit, count):
    return lax.ppermute(value, "dp", [(i, i ^ bit) for i in range(count)])


def added(addends):
    return sum(a.astype(F32) for a in addends).astype(BF16)


def pair_sum(parts):
    while len(parts) > 1:
        parts = [a + b for a, b in zip(parts[::2], parts[1::2])]
    return parts[0]


def chip_bits(count):
    bits, bit = [], 2
    while bit < count:
        bits.append(bit)
        bit *= 2
    return bits


class BlockGather:
    def __init__(self, own, sibling, count):
        self.held, self.count = {0: own, 1: sibling}, count
        self.orders = (chip_bits(count), chip_bits(count)[::-1])

    def own_to(self, s):
        if s < len(self.orders[0]):
            for half in range(2):
                bit = self.orders[half][s]
                self.held[half ^ bit] = across(self.held[half], bit, self.count)

    def rest(self):
        for s in range(1, len(self.orders[0])):
            for half in range(2):
                order = self.orders[half]
                for j in [j for j in self.held if j % 2 == half]:
                    if j ^ order[s] not in self.held and not any(j & b for b in order[s:]):
                        self.held[j ^ order[s]] = across(self.held[j], order[s], self.count)

    def fenced(self, others=(), deps=()):
        keys = sorted(self.held)
        values = fence([self.held[j] for j in keys] + list(others), deps)
        self.held = dict(zip(keys, values))
        return values[len(keys) :]

    def blocks(self):
        return [self.held[j] for j in range(self.count)]


def scatter_orders(count):
    return (chip_bits(count)[::-1], chip_bits(count))


def scatter_plan(count):
    plan = []
    for half, order in enumerate(scatter_orders(count)):
        sets, rest = [[half]], [half]
        for bit in reversed(order):
            sets.insert(0, [j ^ bit for j in rest])
            rest = sets[0] + rest
        plan.append(sets)
    return plan


class BlockScatter:
    def __init__(self, halves, count):
        self.count, self.orders, self.plan = count, scatter_orders(count), scatter_plan(count)
        self.held = [[[(a, 0)] for a in arrays] for arrays in halves]
        self.steps = len(self.orders[0])

    def parts(self, half, s):
        many = len(self.plan[half][s])
        return [a[first : first + many] for a, first in self.held[half][s]]

    def total(self, half, s):
        if len(self.held[half][s]) > 1:
            self.held[half][s] = [(added(self.parts(half, s)), 0)]
        return self.parts(half, s)[0]

    def ready(self, s):
        return [self.total(half, s) for half in range(2)]

    def adds(self, s):
        return [(len(self.plan[half][s]), self.held[half][s]) for half in range(2)]

    def settle(self, s, sums):
        for half in range(2):
            self.held[half][s] = [(sums[half], 0)]

    def send(self, s):
        return [across(self.total(h, s), self.orders[h][s], self.count) for h in range(2)]

    def arrive(self, s, came):
        for half in range(2):
            first = 0
            for t in range(s + 1, len(self.plan[half])):
                self.held[half][t].append((came[half], first))
                first += len(self.plan[half][t])

    def between(self):
        for s in range(1, self.steps - 1):
            self.arrive(s, self.send(s))

    def last(self):
        return self.total(1, -1)[0]

    def kept(self):
        return self.held[0][-1]


def on_device(
    tokens,
    norm_gain,
    norm_bias,
    qkv_weight,
    qkv_bias,
    dense_weight,
    dense_bias,
    up_weight,
    up_bias,
    down_weight,
    down_bias,
    cotangent,
    *,
    ndp,
    nmp,
):
    me = lax.axis_index("dp")
    core = me % 2
    length, model = tokens.shape[0] * nmp, tokens.shape[1]
    tile, block = min(256, length), min(512, length)
    width, hidden = qkv_weight.shape[2] // 2, up_weight.shape[1] // 2
    chip_steps = len(chip_bits(ndp))
    rank = lambda array, axis, which, size: lax.dynamic_slice_in_dim(
        array, which * size, size, axis
    )

    def row_pack(which):
        qkv = rank(qkv_weight, 2, which, width)
        return jnp.concatenate([qkv[0], qkv[1], qkv[2], rank(up_weight, 1, which, hidden)], axis=1)

    def column_pack(which):
        return jnp.concatenate(
            [rank(dense_weight, 0, which, width), rank(down_weight, 0, which, hidden)], axis=0
        )

    pairs = width // LANES
    swap = lambda array: across(array, 1, ndp)
    line_gather = lambda array: lax.all_gather(array, "mp", axis=0, tiled=True)
    line_scatter = lambda array: lax.psum_scatter(array, "mp", scatter_dimension=0, tiled=True)
    x_own, dy_own = line_gather(tokens), line_gather(cotangent)
    bias = jnp.concatenate(
        [
            rank(qkv_bias, 1, core, width).astype(F32).reshape(1, 3 * width),
            rank(up_bias[None, :], 1, core, hidden).astype(F32),
        ],
        axis=1,
    )
    gain, shift = norm_gain.astype(F32)[None, :], norm_bias.astype(F32)[None, :]
    rows = BlockGather(row_pack(core), swap(row_pack(1 - core)), ndp)
    columns = BlockGather(column_pack(core), swap(column_pack(1 - core)), ndp)
    rows.own_to(0)
    _, _, at = block_table(me, ndp)
    at, bias, gain, shift = rows.fenced([at, bias, gain, shift], columns.held.values())
    rows.own_to(1)
    rows.fenced()
    rows.rest()
    x_own, *held = fence([x_own, columns.held[0], columns.held[1]], rows.blocks())
    columns.held = dict(enumerate(held))

    tables = rotary_tables(length)
    x_other = swap(x_own)
    columns.own_to(0)
    common = (rows.blocks(), bias, gain, shift, tables, width, tile)
    first = project(0, x_own, *common, (), [columns.held[0]])
    (x_other,) = columns.fenced([x_other], [first[0]])
    columns.own_to(1)
    qkv, act, slope, normed = project(1, x_other, *common, first, [columns.held[0]])
    held = columns.fenced(rows.blocks(), [qkv])
    columns.rest()
    row_blocks, row_others = held, [swap(a) for a in held[:3]]
    mixed, lse = attend(qkv, length, block, [columns.held[0]])
    row_others = columns.fenced(row_others, [mixed])
    row_blocks[3:] = fence(row_blocks[3:], [row_others[0]])
    row_others += [swap(a) for a in row_blocks[3:]]
    other_sums, own_sums = branch_sums(mixed, act, columns.blocks(), tile, [row_blocks[3]])
    other_sums, dy_own, *row_others[3:] = fence([other_sums, dy_own, *row_others[3:]], [own_sums])
    theirs = swap(other_sums)
    dy_other = swap(dy_own)

    grads = (slope, columns.blocks(), width, tile)
    gmixed, gpre_own, *grad_a = grad_in(0, dy_own, *grads, (), [own_sums])
    theirs, dy_other = fence([theirs, dy_other], [grad_a[0]])
    total = add_rows(own_sums, theirs)
    branches = line_scatter(total)
    gmixed, gpre_other, *grad_b = grad_in(1, dy_other, *grads, [gmixed], [total])
    (gpre_sent,) = fence([gpre_other])
    gpre_came = swap(gpre_sent)
    column_grads = BlockScatter(
        weight_grads(at, [[mixed], [act]], [dy_own, dy_other], ndp, [gpre_sent], left=False), ndp
    )
    (gpre_came,) = fence([gpre_came], [column_grads.held[0][0][0][0]])
    column_came = column_grads.send(0)
    back = lambda sequence, deps: attend_back(
        sequence, qkv, gmixed, mixed, lse, tables, length, block, deps
    )
    *other, qkv_sums_b = back(1, [gpre_came])
    came = [swap(a) for a in other]
    *own, qkv_sums_a = back(0, [other[0]])
    came = fence([*came, *column_came], [own[0]])
    column_came, came = came[3:], came[:3]
    column_grads.arrive(0, column_came)
    column_grads.between()
    all_grads = [*own, gpre_own, *came, gpre_came]

    def normed_half(half, deps, adds=()):
        return grad_normed_sums(
            half, all_grads, x_own, [*row_blocks, *row_others], tile, deps, adds
        )

    total_a, sums_a, *settled = normed_half(0, [], column_grads.adds(chip_steps - 1))
    column_grads.settle(chip_steps - 1, settled)
    half_a = line_scatter(total_a)
    column_came = column_grads.send(chip_steps - 1)
    up_grads = BlockScatter(
        weight_grads(at, [normed], [[gpre_own, gpre_sent]], ndp, [sums_a], left=True), ndp
    )
    c0, c1, branches, u0, u1 = fence(
        [*column_came, branches, *(up_grads.held[h][0][0][0] for h in range(2))]
    )
    up_grads.held[0][0], up_grads.held[1][0] = [(u0, 0)], [(u1, 0)]
    up_came = up_grads.send(0)
    column_grads.arrive(chip_steps - 1, [c0, c1])
    blocks, column_last = weight_grads(
        at,
        [normed],
        [[a, b] for a, b in zip(own, other)],
        ndp,
        [c0],
        True,
        [column_grads.adds(len(column_grads.plan[1]) - 1)[1]],
    )
    qkv_grads = BlockScatter(blocks, ndp)
    qkv_came = qkv_grads.send(0)
    column_theirs = swap(column_last[0])
    total_b, sums_b = normed_half(1, [qkv_grads.held[0][0][0][0]])
    half_b = line_scatter(total_b)
    u0, u1, q0, q1, half_a = fence([*up_came, *qkv_came, half_a], [sums_b, column_theirs])
    up_grads.arrive(0, [u0, u1])
    qkv_grads.arrive(0, [q0, q1])
    up_grads.between()
    qkv_grads.between()
    up_came, qkv_came = up_grads.send(chip_steps - 1), qkv_grads.send(chip_steps - 1)
    u0, u1, q0, q1, branches, sums_b, column_theirs = fence(
        [*up_came, *qkv_came, branches, sums_b, column_theirs]
    )
    up_grads.arrive(chip_steps - 1, [u0, u1])
    qkv_grads.arrive(chip_steps - 1, [q0, q1])
    up_theirs = swap(up_grads.last())
    qkv_theirs = swap(qkv_grads.last())
    qkv_sum = (qkv_sums_a + qkv_sums_b)[:, :3, :].transpose(1, 0, 2).reshape(3 * width)
    norm_sums = jnp.concatenate([sums_a[:2], sums_b[:2]], axis=1)
    small = jnp.concatenate(
        [
            norm_sums.reshape(2 * model),
            qkv_sum,
            grad_a[0][0] + grad_b[0][0],
            grad_a[1][0] + grad_b[1][0],
        ]
    )
    small = pair_sum([small] + [across(small, j, ndp) for j in range(2, ndp, 2)])
    small_other = swap(small)
    owned_up, owned_qkv, owned_dense, owned_down = finish(
        (up_grads.kept(), up_theirs),
        (qkv_grads.kept(), qkv_theirs),
        (column_grads.kept(), column_theirs),
    )
    grad_tokens = norm_back(tokens, cotangent, gain, [half_a, half_b], [small_other, owned_up])
    norm_sums = small[: 2 * model] + small_other[: 2 * model]
    norm_sums = [norm_sums] + fence(
        [
            lax.ppermute(norm_sums, "mp", [(i, i ^ j) for i in range(nmp)])
            for j in range(1, nmp)
        ],
        [grad_tokens],
    )
    while len(norm_sums) > 1:
        norm_sums = [a + b for a, b in zip(norm_sums[::2], norm_sums[1::2])]
    norm_sums = norm_sums[0]

    output = (
        tokens.astype(F32)
        + branches.astype(F32)
        + (dense_bias.astype(F32) + down_bias.astype(F32))[None, :]
    ).astype(BF16)

    inner = 3 * width + hidden
    grad_out_bias = small[2 * model + inner :]
    here, there = (a[2 * model : 2 * model + inner] for a in (small, small_other))
    even, odd = jnp.where(core == 0, here, there), jnp.where(core == 0, there, here)
    grad_qkv_bias = jnp.concatenate(
        [a[: 3 * width].reshape(3, width) for a in (even, odd)], axis=1
    )
    grad_up_bias = jnp.concatenate([even[3 * width :], odd[3 * width :]])

    return (
        output,
        grad_tokens,
        norm_sums[:model],
        norm_sums[model:],
        owned_qkv,
        grad_qkv_bias,
        owned_dense,
        grad_out_bias,
        owned_up,
        grad_up_bias,
        owned_down,
        small_other[2 * model + inner :],
    )


def solution(mesh):
    return jax.shard_map(
        functools.partial(on_device, ndp=mesh.shape["dp"], nmp=mesh.shape["mp"]),
        mesh=mesh,
        in_specs=(
            P(("dp", "mp"), None),
            P(),
            P(),
            P(None, "dp", "mp"),
            P(None, "mp"),
            P("mp", "dp"),
            P(),
            P("dp", "mp"),
            P("mp"),
            P("mp", "dp"),
            P(),
            P(("dp", "mp"), None),
        ),
        out_specs=(
            P(("dp", "mp"), None),
            P(("dp", "mp"), None),
            P(),
            P(),
            P(None, "dp", "mp"),
            P(None, "mp"),
            P("mp", "dp"),
            P(),
            P("dp", "mp"),
            P("mp"),
            P("mp", "dp"),
            P(),
        ),
        check_vma=False,
    )
```
